32 devices in a mesh: groups: 2 (over x), slab: 16 (over z, y, core).
Axes of the slice: x: 2, y: 2, z: 4, core: 2. Of those that a mesh axis runs over, the one named last changes fastest.
Arguments:
- particles: bfloat16 [32, 1048576], P(('groups', 'slab')), parts along dimension 0, may hold values from -8 to 8
- observed: bfloat16 [2097152], P('groups'), parts along dimension 0, may hold values from -1 to 1
- precision: bfloat16 [2097152], P('groups'), parts along dimension 0, may hold values from 0.099609375 to 10
- spread: float32 [2], P('groups'), parts along dimension 0, may hold values from 1 to 4
- anneal: float32 [2], P('groups'), parts along dimension 0, may hold values from 0.06 to 0.6
- step_size: float32 [2], P('groups'), parts along dimension 0, may hold values from 2 to 8
Outputs:
- updated: bfloat16 [32, 1048576], P(('groups', 'slab')), parts along dimension 0
The draws below stay inside these ranges and needn't reach their ends.
There are 2 independent parts, one for each index of `groups`. The reference program is written for one: setup_inputs(seed, part) draws one part's arguments, and reference() takes and returns one part's arrays. A program takes and returns all parts, laid end to end along the dimension named above; each array names one. Nothing has to cross between parts.
All inputs are finite; a program needn't handle non-finite values.
Results may differ from the reference program's by a relative error of at most 0.0014.
The reference program's roundings to bfloat16 on the way (of `grads` and `kernel`) count: a program that leaves them out, or rounds other values in their place, can miss the bound.
Values may be sent and summed in bfloat16 or wider, within the bound.
No kernel may reach another device: no remote copies, remote signals or barrier semaphores. Data moves between devices by JAX's collectives and lax.ppermute only.
A program may use at most 128 MiB of HBM per device.

```python
import math
import jax
import jax.numpy as jnp
from jax import lax

GRID_X = 1024
GRID_Y = 1024
NCELL = 1048576
P_SIZE = 16


def draw_particles(key, part):
    key = jax.random.fold_in(key, 7)
    keys = jax.random.split(key, 5)
    families = 16
    scales = jnp.exp(jax.random.uniform(keys[0], (P_SIZE, 1), jnp.float32, math.log(0.5), math.log(1.5)))
    member = jax.random.randint(keys[1], (P_SIZE,), 0, families)
    share = jax.random.uniform(keys[2], (P_SIZE, 1), jnp.float32, 0.5, 1.0)
    common = jax.random.normal(keys[3], (families, NCELL), jnp.float32)
    grid_row = (jnp.arange(NCELL, dtype=jnp.int32) // GRID_Y).astype(jnp.float32)
    position = grid_row / (GRID_X - 1.0)
    own = jax.random.normal(keys[4], (P_SIZE, NCELL), jnp.float32)
    ramp = 0.5 + position
    values = ramp[None, :] * (scales * (own + share * common[member]))
    return jnp.clip(values, -8.0, 8.0).astype(jnp.bfloat16)


def setup_inputs(seed: int = 0, part: int = 0) -> dict:
    seeds = jax.random.split(jax.random.key(seed), 7)
    part_keys = jax.random.split(jax.random.fold_in(seeds[6], part), 7)
    return {
        "particles": draw_particles(jax.random.fold_in(jax.random.fold_in(seeds[6], part), 71), part),
        "observed": jnp.clip(jax.random.uniform(part_keys[1], (NCELL,), jnp.float32, -1.0, 1.0), -1.0, 1.0).astype(jnp.bfloat16),
        "precision": jnp.clip(jnp.exp(jax.random.uniform(part_keys[2], (NCELL,), jnp.float32, math.log(0.099609375), math.log(10.0))), 0.099609375, 10.0).astype(jnp.bfloat16),
        "spread": jnp.clip(jnp.exp(jax.random.uniform(part_keys[3], (1,), jnp.float32, math.log(1.0), math.log(4.0))), 1.0, 4.0),
        "anneal": jnp.clip(jnp.exp(jax.random.uniform(part_keys[4], (1,), jnp.float32, math.log(0.06), math.log(0.6))), 0.06, 0.6),
        "step_size": jnp.clip(jnp.exp(jax.random.uniform(part_keys[5], (1,), jnp.float32, math.log(2.0), math.log(8.0))), 2.0, 8.0),
    }


prior_scale = 0.25
mass_term = 1.0


def gradient_row(particle, observed, precision):
    field = particle.astype(jnp.float32).reshape(GRID_X, GRID_Y)
    padded = jnp.pad(field, 1)
    beside_all = padded[2:, 1:-1] + padded[:-2, 1:-1] + padded[1:-1, 2:] + padded[1:-1, :-2]
    laplace = (4.0 + mass_term) * field - beside_all
    squash = jnp.tanh(field)
    obs = observed.astype(jnp.float32).reshape(GRID_X, GRID_Y)
    prec = precision.astype(jnp.float32).reshape(GRID_X, GRID_Y)
    result = prec * (obs - squash) * (1.0 - squash * squash) - prior_scale * laplace
    return result.reshape(-1).astype(jnp.bfloat16)


def reference(particles, observed, precision, spread, anneal, step_size):
    grads = lax.map(lambda particle: gradient_row(particle, observed, precision), particles)
    gram = jnp.dot(particles, particles.T, preferred_element_type=jnp.float32)
    norms = jnp.diagonal(gram)
    kernel = jnp.exp(-(norms[:, None] + norms[None, :] - 2.0 * gram) / (spread[0] * NCELL)).astype(jnp.bfloat16)
    ksum = jnp.sum(kernel.astype(jnp.float32), axis=1)
    drive = jnp.dot(kernel, grads, preferred_element_type=jnp.float32)
    pulled = jnp.dot(kernel, particles, preferred_element_type=jnp.float32)
    states = particles.astype(jnp.float32)
    repel = states * ksum[:, None] - pulled
    coeff = 2.0 * anneal[0] / spread[0]
    return (states + (step_size[0] / P_SIZE) * (drive + coeff * repel)).astype(jnp.bfloat16)
```

```python
import functools

import jax
import jax.numpy as jnp
from jax import lax
from jax.experimental import pallas as pl
from jax.experimental.pallas import tpu as pltpu
from jax.sharding import PartitionSpec as P

GRID_X = 1024
GRID_Y = 1024
NCELL = 1048576
LANES = 128
LINE = GRID_Y // LANES
TILE = 16

prior_scale = 0.25
mass_term = 1.0

F32 = jnp.float32
BF16 = jnp.bfloat16
VMEM_LIMIT = 32 * 1024 * 1024


def call(body, name, flops=0, moved=0, **kwargs):
    return pl.pallas_call(
        body,
        name=name,
        compiler_params=pltpu.CompilerParams(vmem_limit_bytes=VMEM_LIMIT),
        cost_estimate=pl.CostEstimate(flops=flops, bytes_accessed=moved, transcendentals=0),
        **kwargs,
    )


def split_body(row_ref, above_ref, below_ref, out_ref):
    slab = pl.program_id(0)
    lines = out_ref.shape[1] - TILE
    out_ref[0, :lines, :] = row_ref[...].reshape(lines, LANES)
    below = below_ref[...].astype(F32).reshape(LINE, LANES)
    above = above_ref[...].astype(F32).reshape(LINE, LANES)
    below = jnp.where(slab == pl.num_programs(0) - 1, 0.0, below)
    above = jnp.where(slab == 0, 0.0, above)
    out_ref[0, lines:, :] = jnp.concatenate([below, above], axis=0).astype(BF16)


def split_row(row, slabs):
    cells = row.shape[1] // slabs
    rows = cells // GRID_Y
    lines = cells // LANES
    last = GRID_X - 1
    return call(
        split_body,
        "split_row",
        moved=6 * row.shape[1],
        grid=(slabs,),
        in_specs=[
            pl.BlockSpec((1, cells), lambda i: (0, i)),
            pl.BlockSpec((1, GRID_Y), lambda i: (0, jnp.maximum(i * rows - 1, 0))),
            pl.BlockSpec((1, GRID_Y), lambda i: (0, jnp.minimum(i * rows + rows, last))),
        ],
        out_specs=pl.BlockSpec((1, lines + TILE, LANES), lambda i: (i, 0, 0)),
        out_shape=jax.ShapeDtypeStruct((slabs, lines + TILE, LANES), BF16),
    )(row, row, row)


def join_body(slab_ref, row_ref):
    row_ref[...] = slab_ref[...].reshape(row_ref.shape)


def join_row(slabs):
    count, lines, _ = slabs.shape
    cells = lines * LANES
    return call(
        join_body,
        "join_row",
        moved=6 * count * cells,
        grid=(count,),
        in_specs=[pl.BlockSpec((1, lines, LANES), lambda i: (i, 0, 0))],
        out_specs=pl.BlockSpec((1, cells), lambda i: (0, i)),
        out_shape=jax.ShapeDtypeStruct((1, count * cells), BF16),
    )(slabs)


def same_line(total):
    wide = total * TILE
    row = lax.broadcasted_iota(jnp.int32, (wide, wide), 0)
    col = lax.broadcasted_iota(jnp.int32, (wide, wide), 1)
    return row % TILE == col % TILE


def members(total, dtype):
    wide = total * TILE
    row = lax.broadcasted_iota(jnp.int32, (wide, total), 0)
    col = lax.broadcasted_iota(jnp.int32, (wide, total), 1)
    return (row // TILE == col).astype(dtype)


def gram_body(states_ref, out_ref, pairs):
    total = states_ref.shape[0]
    wide = total * TILE
    tiles = 4
    steps = (states_ref.shape[1] - TILE) // (tiles * TILE)
    pairs[...] = jnp.zeros_like(pairs)

    def step(i, carry):
        parts = [
            states_ref[:, pl.ds(pl.multiple_of((i * tiles + t) * TILE, TILE), TILE), :].reshape(wide, LANES)
            for t in range(tiles)
        ]
        block = jnp.concatenate(parts, axis=1)
        pairs[...] += lax.dot_general(block, block, (((1,), (1,)), ((), ())), preferred_element_type=F32)
        return carry

    lax.fori_loop(0, steps, step, 0)
    equal = jnp.where(same_line(total), pairs[...], 0.0)
    rows = jnp.sum(equal.reshape(total, TILE, wide), axis=1)
    gram = jnp.dot(rows, members(total, F32), precision=lax.Precision.HIGHEST, preferred_element_type=F32)
    gram = jnp.concatenate([gram, jnp.zeros((total, LANES - total), F32)], axis=1)
    out_ref[...] = jnp.broadcast_to(gram[None], out_ref.shape)


def slab_gram(states, copies):
    total, lines, _ = states.shape
    wide = total * TILE
    return call(
        gram_body,
        "slab_gram",
        flops=2 * wide * wide * LANES * (lines // TILE),
        moved=2 * states.size,
        in_specs=[pl.BlockSpec(memory_space=pltpu.VMEM)],
        out_specs=pl.BlockSpec(memory_space=pltpu.VMEM),
        out_shape=jax.ShapeDtypeStruct((copies, total, LANES), F32),
        scratch_shapes=[pltpu.VMEM((wide, wide), F32)],
    )(states)


def gradient_body(states_ref, observed_ref, precision_ref, out_ref):
    total = states_ref.shape[0]
    tiles = (states_ref.shape[1] - TILE) // TILE
    lane = lax.broadcasted_iota(jnp.int32, (2, LINE, LANES), 2)
    line = lax.broadcasted_iota(jnp.int32, (2, LINE, LANES), 1)
    group = 4

    def load(particle, tile):
        start = pl.multiple_of(tile * TILE, TILE)
        return states_ref[particle, pl.ds(start, TILE), :].astype(F32)

    def step(i, carry):
        tile = i // (total // group)
        first = (i % (total // group)) * group
        start = pl.multiple_of(tile * TILE, TILE)
        obs = observed_ref[pl.ds(start, TILE), :].astype(F32).reshape(2, LINE, LANES)
        prec = precision_ref[pl.ds(start, TILE), :].astype(F32).reshape(2, LINE, LANES)
        for p in range(group):
            particle = first + p
            here = load(particle, tile)
            before = load(particle, jnp.where(tile == 0, tiles, tile - 1))
            after = load(particle, tile + 1)
            above = jnp.concatenate([before[LINE:], here[:LINE]], axis=0).reshape(2, LINE, LANES)
            below = jnp.concatenate([here[LINE:], after[:LINE]], axis=0).reshape(2, LINE, LANES)
            field = here.reshape(2, LINE, LANES)
            turned = pltpu.roll(field, 1, 2)
            carried = jnp.where(line == 0, 0.0, pltpu.roll(turned, 1, 1))
            left = jnp.where(lane == 0, carried, turned)
            turned = pltpu.roll(field, LANES - 1, 2)
            carried = jnp.where(line == LINE - 1, 0.0, pltpu.roll(turned, LINE - 1, 1))
            right = jnp.where(lane == LANES - 1, carried, turned)
            laplace = (4.0 + mass_term) * field - (below + above + right + left)
            squash = jnp.tanh(field)
            result = prec * (obs - squash) * (1.0 - squash * squash) - prior_scale * laplace
            out_ref[particle, pl.ds(start, TILE), :] = result.reshape(TILE, LANES).astype(BF16)
        return carry

    lax.fori_loop(0, tiles * (total // group), step, 0)


def slab_gradient(states, observed, precision):
    total, lines, _ = states.shape
    return call(
        gradient_body,
        "slab_gradient",
        flops=30 * states.size,
        moved=4 * states.size,
        in_specs=[pl.BlockSpec(memory_space=pltpu.VMEM)] * 3,
        out_specs=pl.BlockSpec(memory_space=pltpu.VMEM),
        out_shape=jax.ShapeDtypeStruct((total, lines - TILE, LANES), BF16),
    )(states, observed, precision)


def update_body(spread_ref, anneal_ref, step_ref, grams_ref, states_ref, grads_ref, out_ref, mixer, own):
    total = states_ref.shape[0]
    wide = total * TILE
    rate = step_ref[0] / total
    coeff = 2.0 * anneal_ref[0] / spread_ref[0]

    @pl.when(pl.program_id(0) == 0)
    def _():
        gram = jnp.sum(grams_ref[...], axis=0)[:, :total]
        row = lax.broadcasted_iota(jnp.int32, (total, total), 0)
        col = lax.broadcasted_iota(jnp.int32, (total, total), 1)
        diagonal = jnp.where(row == col, gram, 0.0)
        down = jnp.sum(diagonal, axis=1, keepdims=True)
        across = jnp.sum(diagonal, axis=0, keepdims=True)
        kernel = jnp.exp(-(down + across - 2.0 * gram) / (spread_ref[0] * NCELL)).astype(BF16)
        ksum = jnp.sum(kernel.astype(F32), axis=1, keepdims=True)
        member = members(total, BF16)
        half = jnp.dot(member, kernel, preferred_element_type=F32).astype(BF16)
        full = lax.dot_general(half, member, (((1,), (1,)), ((), ())), preferred_element_type=F32)
        mixer[...] = jnp.where(same_line(total), full, 0.0).astype(BF16)
        gain = 1.0 + rate * coeff * ksum
        own[...] = jnp.broadcast_to(gain[:, :, None], (total, TILE, LANES)).reshape(wide, LANES)

    for t in range(states_ref.shape[1] // TILE):
        lines = slice(t * TILE, (t + 1) * TILE)
        states = states_ref[:, lines, :].reshape(wide, LANES)
        grads = grads_ref[:, lines, :].reshape(wide, LANES)
        mixed = jnp.dot(mixer[...], jnp.concatenate([grads, states], axis=1), preferred_element_type=F32)
        drive, pulled = mixed[:, :LANES], mixed[:, LANES:]
        new = states.astype(F32) * own[...] + rate * (drive - coeff * pulled)
        out_ref[:, lines, :] = new.astype(BF16).reshape(total, TILE, LANES)


def slab_update(spread, anneal, step_size, grams, states, grads):
    total, lines, _ = grads.shape
    wide = total * TILE
    block = min(lines, 4 * TILE)
    return call(
        update_body,
        "slab_update",
        flops=4 * wide * wide * LANES * (lines // TILE),
        moved=6 * grads.size,
        grid=(lines // block,),
        in_specs=[pl.BlockSpec(memory_space=pltpu.SMEM)] * 3
        + [
            pl.BlockSpec(grams.shape, lambda i: (0, 0, 0)),
            pl.BlockSpec((total, block, LANES), lambda i: (0, i, 0)),
            pl.BlockSpec((total, block, LANES), lambda i: (0, i, 0)),
        ],
        out_specs=pl.BlockSpec((total, block, LANES), lambda i: (0, i, 0)),
        out_shape=jax.ShapeDtypeStruct(grads.shape, BF16),
        scratch_shapes=[pltpu.VMEM((wide, wide), BF16), pltpu.VMEM((wide, LANES), F32)],
    )(spread, anneal, step_size, grams, states, grads)


def plain_update(spread, anneal, step_size, states, grads):
    total, lines, _ = grads.shape
    flat = states[:, :lines].reshape(total, -1)
    gram = lax.dot_general(flat, flat, (((1,), (1,)), ((), ())), preferred_element_type=F32)
    gram = lax.psum(gram, "slab")
    norms = jnp.diagonal(gram)
    kernel = jnp.exp(-(norms[:, None] + norms[None, :] - 2.0 * gram) / (spread[0] * NCELL)).astype(BF16)
    ksum = jnp.sum(kernel.astype(F32), axis=1)
    drive = jnp.dot(kernel, grads.reshape(total, -1), preferred_element_type=F32)
    pulled = jnp.dot(kernel, flat, preferred_element_type=F32)
    values = flat.astype(F32)
    repel = values * ksum[:, None] - pulled
    coeff = 2.0 * anneal[0] / spread[0]
    new = values + step_size[0] / total * (drive + coeff * repel)
    return new.astype(BF16).reshape(grads.shape)


def on_device(particles, observed, precision, spread, anneal, step_size):
    slabs = lax.axis_size("slab")
    total = particles.shape[0] * slabs
    cells = NCELL // slabs
    lines = cells // LANES
    states = split_row(particles, slabs)
    states = lax.all_to_all(states, "slab", split_axis=0, concat_axis=0, tiled=True)
    start = lax.axis_index("slab") * lines
    obs = lax.dynamic_slice_in_dim(observed.reshape(-1, LANES), start, lines)
    prec = lax.dynamic_slice_in_dim(precision.reshape(-1, LANES), start, lines)
    if total * TILE <= 256:
        grams = slab_gram(states, slabs)
        grams = lax.all_to_all(grams, "slab", split_axis=0, concat_axis=0, tiled=True)
        grads = slab_gradient(states, obs, prec)
        new = slab_update(spread, anneal, step_size, grams, states, grads)
    else:
        grads = slab_gradient(states, obs, prec)
        new = plain_update(spread, anneal, step_size, states, grads)
    new = lax.all_to_all(new, "slab", split_axis=0, concat_axis=0, tiled=True)
    return join_row(new)


def solution(mesh):
    in_specs = (
        P(("groups", "slab"), None),
        P("groups"),
        P("groups"),
        P("groups"),
        P("groups"),
        P("groups"),
    )
    out_specs = P(("groups", "slab"), None)
    return jax.shard_map(
        on_device, mesh=mesh, in_specs=in_specs, out_specs=out_specs, check_vma=False
    )
```

```python
import functools

import jax
import jax.numpy as jnp
from jax import lax
from jax.experimental import pallas as pl
from jax.experimental.pallas import tpu as pltpu
from jax.sharding import PartitionSpec as P

GRID_X = 1024
GRID_Y = 1024
NCELL = 1048576
LANES = 128
LINE = GRID_Y // LANES
TILE = 16

prior_scale = 0.25
mass_term = 1.0

F32 = jnp.float32
BF16 = jnp.bfloat16
VMEM_LIMIT = 32 * 1024 * 1024


def call(body, name, flops=0, moved=0, **kwargs):
    return pl.pallas_call(
        body,
        name=name,
        compiler_params=pltpu.CompilerParams(vmem_limit_bytes=VMEM_LIMIT),
        cost_estimate=pl.CostEstimate(flops=flops, bytes_accessed=moved, transcendentals=0),
        **kwargs,
    )


def split_body(row_ref, above_ref, below_ref, out_ref):
    slab = pl.program_id(0)
    lines = out_ref.shape[1] - TILE
    out_ref[0, :lines, :] = row_ref[...].reshape(lines, LANES)
    below = below_ref[...].astype(F32).reshape(LINE, LANES)
    above = above_ref[...].astype(F32).reshape(LINE, LANES)
    below = jnp.where(slab == pl.num_programs(0) - 1, 0.0, below)
    above = jnp.where(slab == 0, 0.0, above)
    out_ref[0, lines:, :] = jnp.concatenate([below, above], axis=0).astype(BF16)


def split_row(row, slabs):
    cells = row.shape[1] // slabs
    rows = cells // GRID_Y
    lines = cells // LANES
    last = GRID_X - 1
    return call(
        split_body,
        "split_row",
        moved=6 * row.shape[1],
        grid=(slabs,),
        in_specs=[
            pl.BlockSpec((1, cells), lambda i: (0, i)),
            pl.BlockSpec((1, GRID_Y), lambda i: (0, jnp.maximum(i * rows - 1, 0))),
            pl.BlockSpec((1, GRID_Y), lambda i: (0, jnp.minimum(i * rows + rows, last))),
        ],
        out_specs=pl.BlockSpec((1, lines + TILE, LANES), lambda i: (i, 0, 0)),
        out_shape=jax.ShapeDtypeStruct((slabs, lines + TILE, LANES), BF16),
    )(row, row, row)


def join_body(slab_ref, row_ref):
    row_ref[...] = slab_ref[...].reshape(row_ref.shape)


def join_row(slabs):
    count, lines, _ = slabs.shape
    cells = lines * LANES
    return call(
        join_body,
        "join_row",
        moved=6 * count * cells,
        grid=(count,),
        in_specs=[pl.BlockSpec((1, lines, LANES), lambda i: (i, 0, 0))],
        out_specs=pl.BlockSpec((1, cells), lambda i: (0, i)),
        out_shape=jax.ShapeDtypeStruct((1, count * cells), BF16),
    )(slabs)


def same_line(total):
    wide = total * TILE
    row = lax.broadcasted_iota(jnp.int32, (wide, wide), 0)
    col = lax.broadcasted_iota(jnp.int32, (wide, wide), 1)
    return row % TILE == col % TILE


def members(total, dtype):
    wide = total * TILE
    row = lax.broadcasted_iota(jnp.int32, (wide, total), 0)
    col = lax.broadcasted_iota(jnp.int32, (wide, total), 1)
    return (row // TILE == col).astype(dtype)


def gram_body(states_ref, out_ref, pairs):
    total = states_ref.shape[0]
    wide = total * TILE
    tiles = 4
    steps = (states_ref.shape[1] - TILE) // (tiles * TILE)
    pairs[...] = jnp.zeros_like(pairs)

    def step(i, carry):
        parts = [
            states_ref[:, pl.ds(pl.multiple_of((i * tiles + t) * TILE, TILE), TILE), :].reshape(wide, LANES)
            for t in range(tiles)
        ]
        block = jnp.concatenate(parts, axis=1)
        pairs[...] += lax.dot_general(block, block, (((1,), (1,)), ((), ())), preferred_element_type=F32)
        return carry

    lax.fori_loop(0, steps, step, 0)
    equal = jnp.where(same_line(total), pairs[...], 0.0)
    rows = jnp.sum(equal.reshape(total, TILE, wide), axis=1)
    gram = jnp.dot(rows, members(total, F32), precision=lax.Precision.HIGHEST, preferred_element_type=F32)
    gram = jnp.concatenate([gram, jnp.zeros((total, LANES - total), F32)], axis=1)
    out_ref[...] = jnp.broadcast_to(gram[None], out_ref.shape)


def slab_gram(states, copies):
    total, lines, _ = states.shape
    wide = total * TILE
    return call(
        gram_body,
        "slab_gram",
        flops=2 * wide * wide * LANES * (lines // TILE),
        moved=2 * states.size,
        in_specs=[pl.BlockSpec(memory_space=pltpu.VMEM)],
        out_specs=pl.BlockSpec(memory_space=pltpu.VMEM),
        out_shape=jax.ShapeDtypeStruct((copies, total, LANES), F32),
        scratch_shapes=[pltpu.VMEM((wide, wide), F32)],
    )(states)


def gradient_body(states_ref, observed_ref, precision_ref, out_ref):
    total = states_ref.shape[0]
    tiles = (states_ref.shape[1] - TILE) // TILE
    lane = lax.broadcasted_iota(jnp.int32, (2, LINE, LANES), 2)
    line = lax.broadcasted_iota(jnp.int32, (2, LINE, LANES), 1)
    group = 4

    def load(particle, tile):
        start = pl.multiple_of(tile * TILE, TILE)
        return states_ref[particle, pl.ds(start, TILE), :].astype(F32)

    def step(i, carry):
        tile = i // (total // group)
        first = (i % (total // group)) * group
        start = pl.multiple_of(tile * TILE, TILE)
        obs = observed_ref[pl.ds(start, TILE), :].astype(F32).reshape(2, LINE, LANES)
        prec = precision_ref[pl.ds(start, TILE), :].astype(F32).reshape(2, LINE, LANES)
        for p in range(group):
            particle = first + p
            here = load(particle, tile)
            before = load(particle, jnp.where(tile == 0, tiles, tile - 1))
            after = load(particle, tile + 1)
            above = jnp.concatenate([before[LINE:], here[:LINE]], axis=0).reshape(2, LINE, LANES)
            below = jnp.concatenate([here[LINE:], after[:LINE]], axis=0).reshape(2, LINE, LANES)
            field = here.reshape(2, LINE, LANES)
            turned = pltpu.roll(field, 1, 2)
            carried = jnp.where(line == 0, 0.0, pltpu.roll(turned, 1, 1))
            left = jnp.where(lane == 0, carried, turned)
            turned = pltpu.roll(field, LANES - 1, 2)
            carried = jnp.where(line == LINE - 1, 0.0, pltpu.roll(turned, LINE - 1, 1))
            right = jnp.where(lane == LANES - 1, carried, turned)
            laplace = (4.0 + mass_term) * field - (below + above + right + left)
            squash = jnp.tanh(field)
            result = prec * (obs - squash) * (1.0 - squash * squash) - prior_scale * laplace
            out_ref[particle, pl.ds(start, TILE), :] = result.reshape(TILE, LANES).astype(BF16)
        return carry

    lax.fori_loop(0, tiles * (total // group), step, 0)


def slab_gradient(states, observed, precision):
    total, lines, _ = states.shape
    return call(
        gradient_body,
        "slab_gradient",
        flops=30 * states.size,
        moved=4 * states.size,
        in_specs=[pl.BlockSpec(memory_space=pltpu.VMEM)] * 3,
        out_specs=pl.BlockSpec(memory_space=pltpu.VMEM),
        out_shape=jax.ShapeDtypeStruct((total, lines - TILE, LANES), BF16),
    )(states, observed, precision)


def update_body(spread_ref, anneal_ref, step_ref, grams_ref, states_ref, grads_ref, out_ref, mixer, own):
    total = states_ref.shape[0]
    wide = total * TILE
    rate = step_ref[0] / total
    coeff = 2.0 * anneal_ref[0] / spread_ref[0]

    @pl.when(pl.program_id(0) == 0)
    def _():
        gram = jnp.sum(grams_ref[...], axis=0)[:, :total]
        row = lax.broadcasted_iota(jnp.int32, (total, total), 0)
        col = lax.broadcasted_iota(jnp.int32, (total, total), 1)
        diagonal = jnp.where(row == col, gram, 0.0)
        down = jnp.sum(diagonal, axis=1, keepdims=True)
        across = jnp.sum(diagonal, axis=0, keepdims=True)
        kernel = jnp.exp(-(down + across - 2.0 * gram) / (spread_ref[0] * NCELL)).astype(BF16)
        ksum = jnp.sum(kernel.astype(F32), axis=1, keepdims=True)
        member = members(total, BF16)
        half = jnp.dot(member, kernel, preferred_element_type=F32).astype(BF16)
        full = lax.dot_general(half, member, (((1,), (1,)), ((), ())), preferred_element_type=F32)
        mixer[...] = jnp.where(same_line(total), full, 0.0).astype(BF16)
        gain = 1.0 + rate * coeff * ksum
        own[...] = jnp.broadcast_to(gain[:, :, None], (total, TILE, LANES)).reshape(wide, LANES)

    for t in range(states_ref.shape[1] // TILE):
        lines = slice(t * TILE, (t + 1) * TILE)
        states = states_ref[:, lines, :].reshape(wide, LANES)
        grads = grads_ref[:, lines, :].reshape(wide, LANES)
        mixed = jnp.dot(mixer[...], jnp.concatenate([grads, states], axis=1), preferred_element_type=F32)
        drive, pulled = mixed[:, :LANES], mixed[:, LANES:]
        new = states.astype(F32) * own[...] + rate * (drive - coeff * pulled)
        out_ref[:, lines, :] = new.astype(BF16).reshape(total, TILE, LANES)


def slab_update(spread, anneal, step_size, grams, states, grads):
    total, lines, _ = grads.shape
    wide = total * TILE
    block = min(lines, 4 * TILE)
    return call(
        update_body,
        "slab_update",
        flops=4 * wide * wide * LANES * (lines // TILE),
        moved=6 * grads.size,
        grid=(lines // block,),
        in_specs=[pl.BlockSpec(memory_space=pltpu.SMEM)] * 3
        + [
            pl.BlockSpec(grams.shape, lambda i: (0, 0, 0)),
            pl.BlockSpec((total, block, LANES), lambda i: (0, i, 0)),
            pl.BlockSpec((total, block, LANES), lambda i: (0, i, 0)),
        ],
        out_specs=pl.BlockSpec((total, block, LANES), lambda i: (0, i, 0)),
        out_shape=jax.ShapeDtypeStruct(grads.shape, BF16),
        scratch_shapes=[pltpu.VMEM((wide, wide), BF16), pltpu.VMEM((wide, LANES), F32)],
    )(spread, anneal, step_size, grams, states, grads)


def plain_update(spread, anneal, step_size, states, grads):
    total, lines, _ = grads.shape
    flat = states[:, :lines].reshape(total, -1)
    gram = lax.dot_general(flat, flat, (((1,), (1,)), ((), ())), preferred_element_type=F32)
    gram = lax.psum(gram, "slab")
    norms = jnp.diagonal(gram)
    kernel = jnp.exp(-(norms[:, None] + norms[None, :] - 2.0 * gram) / (spread[0] * NCELL)).astype(BF16)
    ksum = jnp.sum(kernel.astype(F32), axis=1)
    drive = jnp.dot(kernel, grads.reshape(total, -1), preferred_element_type=F32)
    pulled = jnp.dot(kernel, flat, preferred_element_type=F32)
    values = flat.astype(F32)
    repel = values * ksum[:, None] - pulled
    coeff = 2.0 * anneal[0] / spread[0]
    new = values + step_size[0] / total * (drive + coeff * repel)
    return new.astype(BF16).reshape(grads.shape)


def split_pieces_body(first, me_ref, row_ref, above_ref, below_ref, *out_refs):
    step = pl.program_id(0)
    slab = me_ref[0] ^ (first + step)
    slabs = GRID_X * GRID_Y // row_ref.shape[1]
    lines = out_refs[0].shape[0] - TILE
    for k, out_ref in enumerate(out_refs):

        @pl.when(step == k)
        def _():
            out_ref[:lines, :] = row_ref[...].reshape(lines, LANES)
            below = below_ref[...].astype(F32).reshape(LINE, LANES)
            above = above_ref[...].astype(F32).reshape(LINE, LANES)
            below = jnp.where(slab == slabs - 1, 0.0, below)
            above = jnp.where(slab == 0, 0.0, above)
            out_ref[lines:, :] = jnp.concatenate([below, above], axis=0).astype(BF16)


def split_pieces(me, row, slabs, first, count):
    cells = row.shape[1] // slabs
    rows = cells // GRID_Y
    lines = cells // LANES
    last = GRID_X - 1

    def slab(i, me_ref):
        return me_ref[0] ^ (first + i)

    return call(
        functools.partial(split_pieces_body, first),
        "split_pieces",
        moved=6 * cells * count,
        grid_spec=pltpu.PrefetchScalarGridSpec(
            num_scalar_prefetch=1,
            grid=(count,),
            in_specs=[
                pl.BlockSpec((1, cells), lambda i, m: (0, slab(i, m))),
                pl.BlockSpec((1, GRID_Y), lambda i, m: (0, jnp.maximum(slab(i, m) * rows - 1, 0))),
                pl.BlockSpec((1, GRID_Y), lambda i, m: (0, jnp.minimum(slab(i, m) * rows + rows, last))),
            ],
            out_specs=[pl.BlockSpec((lines + TILE, LANES), lambda i, m: (0, 0))] * count,
        ),
        out_shape=[jax.ShapeDtypeStruct((lines + TILE, LANES), BF16)] * count,
    )(me, row, row, row)


def join_pieces_body(me_ref, *refs):
    row_ref = refs[-1]
    pieces = refs[:-1] if refs[0].shape[-1] == LANES else refs[1:-1]
    for k, piece_ref in enumerate(pieces):

        @pl.when(pl.program_id(0) == k)
        def _():
            row_ref[...] = piece_ref[...].reshape(row_ref.shape)


def join_pieces(me, row, pieces, group):
    count = len(pieces)
    lines = pieces[0].shape[0]
    cells = lines * LANES
    whole = pl.BlockSpec((lines, LANES), lambda i, m: (0, 0))
    begun = [] if row is None else [row]

    def slab(i, me_ref):
        k = jnp.int32(group[0])
        for at in range(1, count):
            k = jnp.where(i == at, group[at], k)
        return me_ref[0] ^ k

    return call(
        join_pieces_body,
        "join_pieces",
        moved=6 * count * cells,
        grid_spec=pltpu.PrefetchScalarGridSpec(
            num_scalar_prefetch=1,
            grid=(count,),
            in_specs=[pl.BlockSpec(memory_space=pl.ANY)] * len(begun) + [whole] * count,
            out_specs=pl.BlockSpec((1, cells), lambda i, m: (0, slab(i, m))),
        ),
        out_shape=jax.ShapeDtypeStruct((1, NCELL), BF16),
        input_output_aliases={1: 0} if begun else {},
    )(me, *begun, *pieces)


def swap(me, total):
    row = lax.broadcasted_iota(jnp.int32, (total, total), 0)
    col = lax.broadcasted_iota(jnp.int32, (total, total), 1)
    return (row == col ^ me).astype(F32)


def reorder(me, gram):
    order = swap(me, gram.shape[0])
    half = jnp.dot(order, gram, precision=lax.Precision.HIGHEST, preferred_element_type=F32)
    return jnp.dot(half, order, precision=lax.Precision.HIGHEST, preferred_element_type=F32)


def gram_pieces_body(total, me_ref, *refs):
    pieces, out_ref, pairs = refs[:total], refs[-2], refs[-1]
    wide = total * TILE
    tiles = 4
    steps = (pieces[0].shape[0] - TILE) // (tiles * TILE)
    pairs[...] = jnp.zeros_like(pairs)

    def step(i, carry):
        parts = []
        for t in range(tiles):
            lines = pl.ds(pl.multiple_of((i * tiles + t) * TILE, TILE), TILE)
            parts.append(jnp.concatenate([piece[lines, :] for piece in pieces], axis=0))
        block = jnp.concatenate(parts, axis=1)
        pairs[...] += lax.dot_general(block, block, (((1,), (1,)), ((), ())), preferred_element_type=F32)
        return carry

    lax.fori_loop(0, steps, step, 0)
    equal = jnp.where(same_line(total), pairs[...], 0.0)
    rows = jnp.sum(equal.reshape(total, TILE, wide), axis=1)
    gram = jnp.dot(rows, members(total, F32), precision=lax.Precision.HIGHEST, preferred_element_type=F32)
    gram = reorder(me_ref[0], gram)
    gram = jnp.concatenate([gram, jnp.zeros((total, LANES - total), F32)], axis=1)
    out_ref[...] = jnp.broadcast_to(gram[None], out_ref.shape)


def gram_pieces(me, pieces, earlier):
    total = len(pieces)
    wide = total * TILE
    lines = pieces[0].shape[0]
    return call(
        functools.partial(gram_pieces_body, total),
        "gram_pieces",
        flops=2 * wide * wide * LANES * (lines // TILE),
        moved=2 * total * pieces[0].size,
        in_specs=[pl.BlockSpec(memory_space=pltpu.SMEM)]
        + [pl.BlockSpec(memory_space=pltpu.VMEM)] * total
        + [pl.BlockSpec(memory_space=pl.ANY)] * len(earlier),
        out_specs=pl.BlockSpec(memory_space=pltpu.VMEM),
        out_shape=jax.ShapeDtypeStruct((total, total, LANES), F32),
        scratch_shapes=[pltpu.VMEM((wide, wide), F32)],
    )(me, *pieces, *earlier)


def gradient_pieces_body(count, observed_ref, precision_ref, *refs):
    pieces, out_refs = refs[:count], refs[count:]
    tiles = 4
    block = tiles * TILE
    rows = block // LINE
    steps = (pieces[0].shape[0] - TILE) // block
    shape = (rows, LINE, LANES)
    lane = lax.broadcasted_iota(jnp.int32, (1, LINE, LANES), 2)
    line = lax.broadcasted_iota(jnp.int32, (1, LINE, LANES), 1)

    def step(i, carry):
        start = pl.multiple_of(i * block, block)
        before = pl.multiple_of(jnp.where(i == 0, steps * block, start - TILE), TILE)
        after = pl.multiple_of(start + block, TILE)
        obs = observed_ref[pl.ds(start, block), :].astype(F32).reshape(shape)
        prec = precision_ref[pl.ds(start, block), :].astype(F32).reshape(shape)
        for piece, out_ref in zip(pieces, out_refs):
            here = piece[pl.ds(start, block), :].astype(F32)
            first = piece[pl.ds(before, TILE), :].astype(F32)[LINE:]
            last = piece[pl.ds(after, TILE), :].astype(F32)[:LINE]
            above = jnp.concatenate([first, here[:-LINE]], axis=0).reshape(shape)
            below = jnp.concatenate([here[LINE:], last], axis=0).reshape(shape)
            field = here.reshape(shape)
            turned = pltpu.roll(field, 1, 2)
            carried = jnp.where(line == 0, 0.0, pltpu.roll(turned, 1, 1))
            left = jnp.where(lane == 0, carried, turned)
            turned = pltpu.roll(field, LANES - 1, 2)
            carried = jnp.where(line == LINE - 1, 0.0, pltpu.roll(turned, LINE - 1, 1))
            right = jnp.where(lane == LANES - 1, carried, turned)
            laplace = (4.0 + mass_term) * field - (below + above + right + left)
            squash = jnp.tanh(field)
            result = prec * (obs - squash) * (1.0 - squash * squash) - prior_scale * laplace
            out_ref[pl.ds(start, block), :] = result.reshape(block, LANES).astype(BF16)
        return carry

    lax.fori_loop(0, steps, step, 0)


def gradient_pieces(pieces, observed, precision):
    count = len(pieces)
    lines = pieces[0].shape[0] - TILE
    return call(
        functools.partial(gradient_pieces_body, count),
        "gradient_pieces",
        flops=30 * count * lines * LANES,
        moved=4 * count * lines * LANES,
        in_specs=[pl.BlockSpec(memory_space=pltpu.VMEM)] * (2 + count),
        out_specs=[pl.BlockSpec(memory_space=pltpu.VMEM)] * count,
        out_shape=[jax.ShapeDtypeStruct((lines, LANES), BF16)] * count,
    )(observed, precision, *pieces)


def update_pieces_body(total, first, count, me_ref, spread_ref, anneal_ref, step_ref, grams_ref, *refs):
    states_refs, grads_refs = refs[:total], refs[total : 2 * total]
    out_refs, mixer, own = refs[2 * total : 2 * total + count], refs[-2], refs[-1]
    wide = total * TILE
    high = count * TILE
    rate = step_ref[0] / total
    coeff = 2.0 * anneal_ref[0] / spread_ref[0]

    @pl.when(pl.program_id(0) == 0)
    def _():
        gram = reorder(me_ref[0], jnp.sum(grams_ref[...], axis=0)[:, :total])
        row = lax.broadcasted_iota(jnp.int32, (total, total), 0)
        col = lax.broadcasted_iota(jnp.int32, (total, total), 1)
        diagonal = jnp.where(row == col, gram, 0.0)
        down = jnp.sum(diagonal, axis=1, keepdims=True)
        across = jnp.sum(diagonal, axis=0, keepdims=True)
        kernel = jnp.exp(-(down + across - 2.0 * gram) / (spread_ref[0] * NCELL)).astype(BF16)
        ksum = jnp.sum(kernel.astype(F32), axis=1, keepdims=True)[first : first + count]
        member = members(total, BF16)
        half = jnp.dot(member, kernel, preferred_element_type=F32).astype(BF16)
        full = lax.dot_general(half, member, (((1,), (1,)), ((), ())), preferred_element_type=F32)
        full = jnp.where(same_line(total), full, 0.0)
        mixer[...] = full[first * TILE : first * TILE + high].astype(BF16)
        gain = 1.0 + rate * coeff * ksum
        own[...] = jnp.broadcast_to(gain[:, :, None], (count, TILE, LANES)).reshape(high, LANES)

    for t in range(out_refs[0].shape[0] // TILE):
        lines = slice(t * TILE, (t + 1) * TILE)
        states = jnp.concatenate([ref[lines, :] for ref in states_refs], axis=0)
        grads = jnp.concatenate([ref[lines, :] for ref in grads_refs], axis=0)
        mixed = jnp.dot(mixer[...], jnp.concatenate([grads, states], axis=1), preferred_element_type=F32)
        drive, pulled = mixed[:, :LANES], mixed[:, LANES:]
        kept = states[first * TILE : first * TILE + high].astype(F32)
        new = (kept * own[...] + rate * (drive - coeff * pulled)).astype(BF16)
        for k, out_ref in enumerate(out_refs):
            out_ref[lines, :] = new[k * TILE : (k + 1) * TILE]


def update_pieces(me, spread, anneal, step_size, grams, states, grads, first, count):
    total = len(states)
    lines = grads[0].shape[0]
    wide = total * TILE
    block = min(lines, 4 * TILE)
    part = pl.BlockSpec((block, LANES), lambda i: (i, 0))
    return call(
        functools.partial(update_pieces_body, total, first, count),
        "update_pieces",
        flops=4 * count * TILE * wide * LANES * (lines // TILE),
        moved=2 * (2 * total + count) * grads[0].size,
        grid=(lines // block,),
        in_specs=[pl.BlockSpec(memory_space=pltpu.SMEM)] * 4
        + [pl.BlockSpec(grams.shape, lambda i: (0, 0, 0))]
        + [part] * (2 * total),
        out_specs=[part] * count,
        out_shape=[jax.ShapeDtypeStruct((lines, LANES), BF16)] * count,
        scratch_shapes=[pltpu.VMEM((count * TILE, wide), BF16), pltpu.VMEM((count * TILE, LANES), F32)],
    )(me, spread, anneal, step_size, grams, *states, *grads)


def exchange(piece, k, slabs):
    return lax.ppermute(piece, "slab", [(i, i ^ k) for i in range(slabs)])


ORDER = (8, 9, 4, 10, 11, 5, 12, 13, 6, 14, 15, 7, 1, 2, 3)
GROUPS = ((0, 8, 9, 4), (10, 11, 5, 12), (13, 6, 14, 15), (7, 1, 2, 3))


def by_pieces(particles, observed, precision, spread, anneal, step_size):
    slabs = lax.axis_size("slab")
    half = slabs // 2
    me = lax.axis_index("slab").astype(jnp.int32).reshape(1)
    far = split_pieces(me, particles, slabs, half, half)
    near = split_pieces(me, particles, slabs, 0, half)
    mine = near + far
    states = [mine[0]] + [None] * (slabs - 1)
    for k in ORDER:
        states[k] = exchange(mine[k], k, slabs)
    lines = NCELL // slabs // LANES
    start = me[0] * lines
    obs = lax.dynamic_slice_in_dim(observed.reshape(-1, LANES), start, lines)
    prec = lax.dynamic_slice_in_dim(precision.reshape(-1, LANES), start, lines)
    grads = [None] * slabs
    for group in GROUPS[:-1]:
        for k, grad in zip(group, gradient_pieces([states[k] for k in group], obs, prec)):
            grads[k] = grad
    grams = gram_pieces(me, states, [grads[group[0]] for group in GROUPS[:-1]])
    grams = lax.all_to_all(grams, "slab", split_axis=0, concat_axis=0, tiled=True)
    for group in GROUPS[-1:]:
        for k, grad in zip(group, gradient_pieces([states[k] for k in group], obs, prec)):
            grads[k] = grad
    far = update_pieces(me, spread, anneal, step_size, grams, states, grads, half, half)
    near = update_pieces(me, spread, anneal, step_size, grams, states, grads, 0, half)
    mine = near + far
    new = [mine[0]] + [None] * (slabs - 1)
    for k in ORDER:
        new[k] = exchange(mine[k], k, slabs)
    row = None
    for group in GROUPS:
        row = join_pieces(me, row, [new[k] for k in group], group)
    return row


def on_device(particles, observed, precision, spread, anneal, step_size):
    slabs = lax.axis_size("slab")
    total = particles.shape[0] * slabs
    if slabs == 16:
        return by_pieces(particles, observed, precision, spread, anneal, step_size)
    cells = NCELL // slabs
    lines = cells // LANES
    states = split_row(particles, slabs)
    states = lax.all_to_all(states, "slab", split_axis=0, concat_axis=0, tiled=True)
    start = lax.axis_index("slab") * lines
    obs = lax.dynamic_slice_in_dim(observed.reshape(-1, LANES), start, lines)
    prec = lax.dynamic_slice_in_dim(precision.reshape(-1, LANES), start, lines)
    if total * TILE <= 256:
        grams = slab_gram(states, slabs)
        grams = lax.all_to_all(grams, "slab", split_axis=0, concat_axis=0, tiled=True)
        grads = slab_gradient(states, obs, prec)
        new = slab_update(spread, anneal, step_size, grams, states, grads)
    else:
        grads = slab_gradient(states, obs, prec)
        new = plain_update(spread, anneal, step_size, states, grads)
    new = lax.all_to_all(new, "slab", split_axis=0, concat_axis=0, tiled=True)
    return join_row(new)


def solution(mesh):
    in_specs = (
        P(("groups", "slab"), None),
        P("groups"),
        P("groups"),
        P("groups"),
        P("groups"),
        P("groups"),
    )
    out_specs = P(("groups", "slab"), None)
    return jax.shard_map(
        on_device, mesh=mesh, in_specs=in_specs, out_specs=out_specs, check_vma=False
    )
```

```python
import jax
import jax.numpy as jnp
from jax import lax
from jax.experimental import pallas as pl
from jax.experimental.pallas import tpu as pltpu
from jax.sharding import PartitionSpec as P

GRID_X = 1024
GRID_Y = 1024
NCELL = 1048576
LANES = 128
LINE = GRID_Y // LANES
TILE = 16

prior_scale = 0.25
mass_term = 1.0

F32 = jnp.float32
BF16 = jnp.bfloat16
MIB = 1024 * 1024


def call(body, name, flops=0, moved=0, limit=16, **kwargs):
    return pl.pallas_call(
        body,
        name=name,
        compiler_params=pltpu.CompilerParams(vmem_limit_bytes=limit * MIB),
        cost_estimate=pl.CostEstimate(flops=flops, bytes_accessed=moved, transcendentals=0),
        **kwargs,
    )


IN_VMEM = pl.BlockSpec(memory_space=pltpu.VMEM)
ANYWHERE = pl.BlockSpec(memory_space=pl.ANY)


def split_body(row_ref, out_ref, held, sems):
    slabs, lines, _ = out_ref.shape
    lines -= TILE
    cells = lines * LANES

    def part(slab):
        at = pl.ds(slab * cells, cells)
        return pltpu.make_async_copy(row_ref.at[:, at], held.at[:, at], sems.at[slab])

    def edge(start):
        return held[:, pl.ds(start, GRID_Y)].astype(F32).reshape(LINE, LANES)

    for slab in range(slabs):
        part(slab).start()
    part(0).wait()
    outside = jnp.zeros((LINE, LANES), F32)
    for slab in range(slabs):
        if slab + 1 < slabs:
            part(slab + 1).wait()
        out_ref[slab, :lines, :] = held[:, pl.ds(slab * cells, cells)].reshape(lines, LANES)
        below = edge((slab + 1) * cells) if slab + 1 < slabs else outside
        above = edge(slab * cells - GRID_Y) if slab else outside
        out_ref[slab, lines:, :] = jnp.concatenate([below, above], axis=0).astype(BF16)


def split_row(row, slabs):
    lines = row.shape[1] // slabs // LANES
    return call(
        split_body,
        "split_row",
        moved=6 * row.shape[1],
        limit=60,
        in_specs=[ANYWHERE],
        out_specs=IN_VMEM,
        out_shape=jax.ShapeDtypeStruct((slabs, lines + TILE, LANES), BF16),
        scratch_shapes=[pltpu.VMEM(row.shape, BF16), pltpu.SemaphoreType.DMA((slabs,))],
    )(row)


def join_body(slabs_ref, row_ref, held, sems):
    slabs, lines, _ = slabs_ref.shape
    cells = lines * LANES
    copies = []
    for slab in range(slabs):
        at = pl.ds(slab * cells, cells)
        held[:, at] = slabs_ref[slab].reshape(1, cells)
        copies.append(pltpu.make_async_copy(held.at[:, at], row_ref.at[:, at], sems.at[slab]))
        copies[-1].start()
    for copy in copies:
        copy.wait()


def join_row(slabs):
    count, lines, _ = slabs.shape
    row = jax.ShapeDtypeStruct((1, count * lines * LANES), BF16)
    return call(
        join_body,
        "join_row",
        moved=6 * row.size,
        in_specs=[IN_VMEM],
        out_specs=ANYWHERE,
        out_shape=row,
        scratch_shapes=[pltpu.VMEM(row.shape, BF16), pltpu.SemaphoreType.DMA((count,))],
    )(slabs)


def same_line(total):
    wide = total * TILE
    row = lax.broadcasted_iota(jnp.int32, (wide, wide), 0)
    col = lax.broadcasted_iota(jnp.int32, (wide, wide), 1)
    return row % TILE == col % TILE


def members(total, dtype):
    wide = total * TILE
    row = lax.broadcasted_iota(jnp.int32, (wide, total), 0)
    col = lax.broadcasted_iota(jnp.int32, (wide, total), 1)
    return (row // TILE == col).astype(dtype)


def gram_body(states_ref, out_ref, pairs):
    total = states_ref.shape[0]
    wide = total * TILE
    tiles = min(8, states_ref.shape[1] // TILE - 1)
    steps = (states_ref.shape[1] - TILE) // (tiles * TILE)
    pairs[...] = jnp.zeros_like(pairs)

    def step(i, carry):
        parts = [
            states_ref[:, pl.ds(pl.multiple_of((i * tiles + t) * TILE, TILE), TILE), :].reshape(wide, LANES)
            for t in range(tiles)
        ]
        block = jnp.concatenate(parts, axis=1)
        pairs[...] += lax.dot_general(block, block, (((1,), (1,)), ((), ())), preferred_element_type=F32)
        return carry

    lax.fori_loop(0, steps, step, 0)
    equal = jnp.where(same_line(total), pairs[...], 0.0)
    rows = jnp.sum(equal.reshape(total, TILE, wide), axis=1)
    gram = jnp.dot(rows, members(total, F32), precision=lax.Precision.HIGHEST, preferred_element_type=F32)
    gram = jnp.concatenate([gram, jnp.zeros((total, LANES - total), F32)], axis=1)
    out_ref[...] = jnp.broadcast_to(gram[None], out_ref.shape)


def slab_gram(states, copies):
    total, lines, _ = states.shape
    wide = total * TILE
    return call(
        gram_body,
        "slab_gram",
        flops=2 * wide * wide * LANES * (lines // TILE),
        moved=2 * states.size,
        in_specs=[IN_VMEM],
        out_specs=IN_VMEM,
        out_shape=jax.ShapeDtypeStruct((copies, total, LANES), F32),
        scratch_shapes=[pltpu.VMEM((wide, wide), F32)],
    )(states)


def gradient_body(states_ref, observed_ref, precision_ref, out_ref, observed, precision, sems):
    total, lines, _ = out_ref.shape
    tiles = min(4, lines // TILE)
    block = tiles * TILE
    rows = block // LINE
    steps = lines // block
    group = 4
    shape = (rows, LINE, LANES)
    lane = lax.broadcasted_iota(jnp.int32, (1, LINE, LANES), 2)
    line = lax.broadcasted_iota(jnp.int32, (1, LINE, LANES), 1)
    slab = pl.ds(pl.multiple_of(lax.axis_index("slab") * lines, TILE), lines)
    fetches = [
        pltpu.make_async_copy(observed_ref.at[slab, :], observed, sems.at[0]),
        pltpu.make_async_copy(precision_ref.at[slab, :], precision, sems.at[1]),
    ]
    for fetch in fetches:
        fetch.start()
    for fetch in fetches:
        fetch.wait()

    def step(i, carry):
        at = i // (total // group)
        start = pl.multiple_of(at * block, block)
        before = pl.multiple_of(jnp.where(at == 0, lines, start - TILE), TILE)
        after = pl.multiple_of(start + block, TILE)
        obs = observed[pl.ds(start, block), :].astype(F32).reshape(shape)
        prec = precision[pl.ds(start, block), :].astype(F32).reshape(shape)
        for p in range(group):
            particle = (i % (total // group)) * group + p
            here = states_ref[particle, pl.ds(start, block), :].astype(F32)
            first = states_ref[particle, pl.ds(before, TILE), :].astype(F32)[LINE:]
            last = states_ref[particle, pl.ds(after, TILE), :].astype(F32)[:LINE]
            above = jnp.concatenate([first, here[:-LINE]], axis=0).reshape(shape)
            below = jnp.concatenate([here[LINE:], last], axis=0).reshape(shape)
            field = here.reshape(shape)
            turned = pltpu.roll(field, 1, 2)
            carried = jnp.where(line == 0, 0.0, pltpu.roll(turned, 1, 1))
            left = jnp.where(lane == 0, carried, turned)
            turned = pltpu.roll(field, LANES - 1, 2)
            carried = jnp.where(line == LINE - 1, 0.0, pltpu.roll(turned, LINE - 1, 1))
            right = jnp.where(lane == LANES - 1, carried, turned)
            laplace = (4.0 + mass_term) * field - (below + above + right + left)
            squash = jnp.tanh(field)
            result = prec * (obs - squash) * (1.0 - squash * squash) - prior_scale * laplace
            out_ref[particle, pl.ds(start, block), :] = result.reshape(block, LANES).astype(BF16)
        return carry

    lax.fori_loop(0, steps * (total // group), step, 0)


def slab_gradient(states, observed, precision):
    total, lines, _ = states.shape
    lines -= TILE
    return call(
        gradient_body,
        "slab_gradient",
        flops=30 * states.size,
        moved=4 * states.size,
        in_specs=[IN_VMEM, ANYWHERE, ANYWHERE],
        out_specs=IN_VMEM,
        out_shape=jax.ShapeDtypeStruct((total, lines, LANES), BF16),
        scratch_shapes=[pltpu.VMEM((lines, LANES), BF16)] * 2 + [pltpu.SemaphoreType.DMA((2,))],
    )(states, observed, precision)


def update_body(spread_ref, anneal_ref, step_ref, grams_ref, states_ref, grads_ref, out_ref, mixer, own):
    total, lines, _ = grads_ref.shape
    wide = total * TILE
    spread = spread_ref[...]
    rate = step_ref[...] / total
    coeff = 2.0 * anneal_ref[...] / spread

    gram = jnp.sum(grams_ref[...], axis=0)[:, :total]
    row = lax.broadcasted_iota(jnp.int32, (total, total), 0)
    col = lax.broadcasted_iota(jnp.int32, (total, total), 1)
    diagonal = jnp.where(row == col, gram, 0.0)
    down = jnp.sum(diagonal, axis=1, keepdims=True)
    across = jnp.sum(diagonal, axis=0, keepdims=True)
    kernel = jnp.exp(-(down + across - 2.0 * gram) / (spread * NCELL)).astype(BF16)
    ksum = jnp.sum(kernel.astype(F32), axis=1, keepdims=True)
    member = members(total, BF16)
    half = jnp.dot(member, kernel, preferred_element_type=F32).astype(BF16)
    full = lax.dot_general(half, member, (((1,), (1,)), ((), ())), preferred_element_type=F32)
    mixer[...] = jnp.where(same_line(total), full, 0.0).astype(BF16)
    gain = 1.0 + rate * coeff * ksum
    own[...] = jnp.broadcast_to(gain[:, :, None], (total, TILE, LANES)).reshape(wide, LANES)
    tiles = min(4, lines // TILE)

    def step(i, carry):
        for t in range(tiles):
            at = pl.ds(pl.multiple_of((i * tiles + t) * TILE, TILE), TILE)
            states = states_ref[:, at, :].reshape(wide, LANES)
            grads = grads_ref[:, at, :].reshape(wide, LANES)
            mixed = jnp.dot(mixer[...], jnp.concatenate([grads, states], axis=1), preferred_element_type=F32)
            drive, pulled = mixed[:, :LANES], mixed[:, LANES:]
            new = states.astype(F32) * own[...] + rate * (drive - coeff * pulled)
            out_ref[:, at, :] = new.astype(BF16).reshape(total, TILE, LANES)
        return carry

    lax.fori_loop(0, lines // TILE // tiles, step, 0)


def slab_update(spread, anneal, step_size, grams, states, grads):
    total, lines, _ = grads.shape
    wide = total * TILE
    return call(
        update_body,
        "slab_update",
        flops=4 * wide * wide * LANES * (lines // TILE),
        moved=6 * grads.size,
        in_specs=[IN_VMEM] * 6,
        out_specs=IN_VMEM,
        out_shape=jax.ShapeDtypeStruct(grads.shape, BF16),
        scratch_shapes=[pltpu.VMEM((wide, wide), BF16), pltpu.VMEM((wide, LANES), F32)],
    )(spread.reshape(1, 1), anneal.reshape(1, 1), step_size.reshape(1, 1), grams, states, grads)


def plain_update(spread, anneal, step_size, states, grads):
    total, lines, _ = grads.shape
    flat = states[:, :lines].reshape(total, -1)
    gram = lax.dot_general(flat, flat, (((1,), (1,)), ((), ())), preferred_element_type=F32)
    gram = lax.psum(gram, "slab")
    norms = jnp.diagonal(gram)
    kernel = jnp.exp(-(norms[:, None] + norms[None, :] - 2.0 * gram) / (spread[0] * NCELL)).astype(BF16)
    ksum = jnp.sum(kernel.astype(F32), axis=1)
    drive = jnp.dot(kernel, grads.reshape(total, -1), preferred_element_type=F32)
    pulled = jnp.dot(kernel, flat, preferred_element_type=F32)
    values = flat.astype(F32)
    repel = values * ksum[:, None] - pulled
    coeff = 2.0 * anneal[0] / spread[0]
    new = values + step_size[0] / total * (drive + coeff * repel)
    return new.astype(BF16).reshape(grads.shape)


def on_device(particles, observed, precision, spread, anneal, step_size):
    slabs = lax.axis_size("slab")
    total = particles.shape[0] * slabs
    states = split_row(particles, slabs)
    states = lax.all_to_all(states, "slab", split_axis=0, concat_axis=0, tiled=True)
    obs = observed.reshape(-1, LANES)
    prec = precision.reshape(-1, LANES)
    if total * TILE <= 256:
        grams = slab_gram(states, slabs)
        grams = lax.all_to_all(grams, "slab", split_axis=0, concat_axis=0, tiled=True)
        grads = slab_gradient(states, obs, prec)
        new = slab_update(spread, anneal, step_size, grams, states, grads)
    else:
        grads = slab_gradient(states, obs, prec)
        new = plain_update(spread, anneal, step_size, states, grads)
    new = lax.all_to_all(new, "slab", split_axis=0, concat_axis=0, tiled=True)
    return join_row(new)


def solution(mesh):
    in_specs = (
        P(("groups", "slab"), None),
        P("groups"),
        P("groups"),
        P("groups"),
        P("groups"),
        P("groups"),
    )
    out_specs = P(("groups", "slab"), None)
    return jax.shard_map(
        on_device, mesh=mesh, in_specs=in_specs, out_specs=out_specs, check_vma=False
    )
```

```python
import functools

import jax
import jax.numpy as jnp
from jax import lax
from jax.experimental import pallas as pl
from jax.experimental.pallas import tpu as pltpu
from jax.sharding import PartitionSpec as P

GRID_X = 1024
GRID_Y = 1024
NCELL = 1048576
LANES = 128
LINE = GRID_Y // LANES
TILE = 16

prior_scale = 0.25
mass_term = 1.0

F32 = jnp.float32
BF16 = jnp.bfloat16
MIB = 1024 * 1024


def call(body, name, flops=0, moved=0, limit=16, **kwargs):
    return pl.pallas_call(
        body,
        name=name,
        compiler_params=pltpu.CompilerParams(vmem_limit_bytes=limit * MIB),
        cost_estimate=pl.CostEstimate(flops=flops, bytes_accessed=moved, transcendentals=0),
        **kwargs,
    )


IN_VMEM = pl.BlockSpec(memory_space=pltpu.VMEM)
IN_HBM = pl.BlockSpec(memory_space=pltpu.HBM)
BLOCK = 4 * TILE


def cuts(lines):
    if lines % (8 * BLOCK):
        return lines, lines
    return lines * 3 // 4, lines * 3 // 4 - BLOCK


def split_body(lines, begin, rim, fields, numbers, row_ref, *refs):
    field_refs, number_refs = refs[:fields], refs[fields : fields + numbers]
    out_ref, *slab_refs, rows_ref = refs[-7 - fields : -5]
    held, edges, sems, edge_sems, field_sems = refs[-5:]
    for k, number_ref in enumerate(number_refs):
        rows_ref[k : k + 1, :] = jnp.broadcast_to(number_ref[...].reshape(1, 1), (1, LANES))
    slabs, count, _ = out_ref.shape
    count -= TILE * rim
    size = count * LANES
    cells = lines * LANES

    def part(slab):
        source = row_ref.at[:, pl.ds(slab * cells + begin * LANES, size)]
        return pltpu.make_async_copy(source, held.at[:, pl.ds(slab * size, size)], sems.at[slab])

    def edge(slab):
        source = row_ref.at[:, pl.ds(slab * cells - GRID_Y, GRID_Y)]
        return pltpu.make_async_copy(source, edges.at[:, pl.ds(slab * GRID_Y, GRID_Y)], edge_sems.at[slab])

    def grid_row(ref, start):
        return ref[:, pl.ds(start, GRID_Y)].astype(F32).reshape(LINE, LANES)

    for slab in range(slabs):
        part(slab).start()
        if rim and slab:
            edge(slab).start()
    mine = pl.ds(pl.multiple_of(lax.axis_index("slab") * lines, TILE), lines)
    fetches = [
        pltpu.make_async_copy(source.at[mine, :], target, field_sems.at[k])
        for k, (source, target) in enumerate(zip(field_refs, slab_refs))
    ]
    for fetch in fetches:
        fetch.start()
    part(0).wait()
    outside = jnp.zeros((LINE, LANES), F32)
    for slab in range(slabs):
        if slab + 1 < slabs:
            part(slab + 1).wait()
        out_ref[slab, :count, :] = held[:, pl.ds(slab * size, size)].reshape(count, LANES)
        if rim:
            if slab:
                edge(slab).wait()
            below = grid_row(held, (slab + 1) * size) if slab + 1 < slabs else outside
            above = grid_row(edges, slab * GRID_Y) if slab else outside
            out_ref[slab, count:, :] = jnp.concatenate([below, above], axis=0).astype(BF16)
    for fetch in fetches:
        fetch.wait()


def split_row(row, slabs, begin, end, rim, fields, numbers, earlier):
    lines = row.shape[1] // slabs // LANES
    count = end - begin
    return call(
        functools.partial(split_body, lines, begin, rim, len(fields), len(numbers)),
        "split_row",
        moved=6 * slabs * count * LANES,
        limit=60,
        in_specs=[IN_HBM] * (1 + len(fields)) + [IN_VMEM] * len(numbers) + [IN_HBM] * len(earlier),
        out_specs=[IN_VMEM] * (2 + len(fields)),
        out_shape=[jax.ShapeDtypeStruct((slabs, count + TILE * rim, LANES), BF16)]
        + [jax.ShapeDtypeStruct((lines, LANES), BF16)] * len(fields)
        + [jax.ShapeDtypeStruct((8, LANES), F32)],
        scratch_shapes=[
            pltpu.VMEM((1, slabs * count * LANES), BF16),
            pltpu.VMEM((1, slabs * GRID_Y), BF16),
            pltpu.SemaphoreType.DMA((slabs,)),
            pltpu.SemaphoreType.DMA((slabs,)),
            pltpu.SemaphoreType.DMA((2,)),
        ],
    )(row, *fields, *numbers, *earlier)


def join_body(lines, begin, slabs_ref, *refs):
    row_ref, held, sems = refs[-3:]
    slabs, count, _ = slabs_ref.shape
    size = count * LANES
    copies = []
    for slab in range(slabs):
        at = pl.ds(slab * size, size)
        held[:, at] = slabs_ref[slab].reshape(1, size)
        target = row_ref.at[:, pl.ds((slab * lines + begin) * LANES, size)]
        copies.append(pltpu.make_async_copy(held.at[:, at], target, sems.at[slab]))
        copies[-1].start()
    for copy in copies:
        copy.wait()


def join_row(slabs, lines, begin, row):
    total, count, _ = slabs.shape
    begun = [] if row is None else [row]
    return call(
        functools.partial(join_body, lines, begin),
        "join_row",
        moved=6 * slabs.size,
        in_specs=[IN_VMEM] + [IN_HBM] * len(begun),
        out_specs=IN_HBM,
        out_shape=jax.ShapeDtypeStruct((1, total * lines * LANES), BF16),
        input_output_aliases={1: 0} if begun else {},
        scratch_shapes=[pltpu.VMEM((1, slabs.size), BF16), pltpu.SemaphoreType.DMA((total,))],
    )(slabs, *begun)


def same_line(total):
    wide = total * TILE
    row = lax.broadcasted_iota(jnp.int32, (wide, wide), 0)
    col = lax.broadcasted_iota(jnp.int32, (wide, wide), 1)
    return row % TILE == col % TILE


def members(total, dtype):
    wide = total * TILE
    row = lax.broadcasted_iota(jnp.int32, (wide, total), 0)
    col = lax.broadcasted_iota(jnp.int32, (wide, total), 1)
    return (row // TILE == col).astype(dtype)


def gram_body(steps, tiles, parts, states_ref, *refs):
    out_ref, pairs = refs[-2:]
    total = states_ref.shape[0]
    wide = total * TILE
    pairs[...] = jnp.zeros_like(pairs)

    def step(i, carry):
        parts = [
            states_ref[:, pl.ds(pl.multiple_of((i * tiles + t) * TILE, TILE), TILE), :].reshape(wide, LANES)
            for t in range(tiles)
        ]
        block = jnp.concatenate(parts, axis=1)
        pairs[...] += lax.dot_general(block, block, (((1,), (1,)), ((), ())), preferred_element_type=F32)
        return carry

    lax.fori_loop(0, steps, step, 0)
    equal = jnp.where(same_line(total), pairs[...], 0.0)
    rows = jnp.sum(equal.reshape(total, TILE, wide), axis=1)
    gram = jnp.dot(rows, members(total, F32), precision=lax.Precision.HIGHEST, preferred_element_type=F32)
    gram = jnp.concatenate([gram, jnp.zeros((total, LANES - total), F32)], axis=1)
    for part_ref in refs[:parts]:
        gram += part_ref[0]
    out_ref[...] = jnp.broadcast_to(gram[None], out_ref.shape)


def slab_gram(states, lines, copies, parts, earlier):
    total = states.shape[0]
    wide = total * TILE
    tiles = min(8, lines // TILE)
    return call(
        functools.partial(gram_body, lines // TILE // tiles, tiles, len(parts)),
        "slab_gram",
        flops=2 * wide * wide * LANES * (lines // TILE),
        moved=2 * states.size,
        in_specs=[IN_VMEM] * (1 + len(parts)) + [IN_HBM] * len(earlier),
        out_specs=IN_VMEM,
        out_shape=jax.ShapeDtypeStruct((copies, total, LANES), F32),
        scratch_shapes=[pltpu.VMEM((wide, wide), F32)],
    )(states, *parts, *earlier)


def gradient_body(lines, begin, end, parts, *refs):
    observed, precision, out_ref, grads, sems = refs[parts:]
    total = grads.shape[0]
    first = refs[0].shape[1] - TILE
    rows = BLOCK // LINE
    group = 4
    shape = (rows, LINE, LANES)
    lane = lax.broadcasted_iota(jnp.int32, (1, LINE, LANES), 2)
    line = lax.broadcasted_iota(jnp.int32, (1, LINE, LANES), 1)

    def load(particle, at, count):
        ref, at = (refs[0], at) if at < first else (refs[1], at - first)
        return ref[particle, at : at + count, :].astype(F32)

    def rim(particle):
        return refs[0][particle, first:, :].astype(F32)

    stores = []
    for k, at in enumerate(range(begin, end, BLOCK)):
        mine = slice(at - begin, at - begin + BLOCK)
        obs = observed[at : at + BLOCK, :].astype(F32).reshape(shape)
        prec = precision[at : at + BLOCK, :].astype(F32).reshape(shape)

        def step(i, carry):
            for p in range(group):
                particle = i * group + p
                here = load(particle, at, BLOCK)
                before = load(particle, at - TILE, TILE) if at else rim(particle)
                after = load(particle, at + BLOCK, TILE) if at + BLOCK < lines else rim(particle)
                above = jnp.concatenate([before[LINE:], here[:-LINE]], axis=0).reshape(shape)
                below = jnp.concatenate([here[LINE:], after[:LINE]], axis=0).reshape(shape)
                field = here.reshape(shape)
                turned = pltpu.roll(field, 1, 2)
                carried = jnp.where(line == 0, 0.0, pltpu.roll(turned, 1, 1))
                left = jnp.where(lane == 0, carried, turned)
                turned = pltpu.roll(field, LANES - 1, 2)
                carried = jnp.where(line == LINE - 1, 0.0, pltpu.roll(turned, LINE - 1, 1))
                right = jnp.where(lane == LANES - 1, carried, turned)
                laplace = (4.0 + mass_term) * field - (below + above + right + left)
                squash = jnp.tanh(field)
                result = prec * (obs - squash) * (1.0 - squash * squash) - prior_scale * laplace
                grads[particle, mine, :] = result.reshape(BLOCK, LANES).astype(BF16)
            return carry

        lax.fori_loop(0, total // group, step, 0)
        stores.append(pltpu.make_async_copy(grads.at[:, mine, :], out_ref.at[:, mine, :], sems.at[k]))
        stores[-1].start()
    for store in stores:
        store.wait()


def slab_gradient(parts, observed, precision, lines, begin, end):
    total = parts[0].shape[0]
    count = end - begin
    out = jax.ShapeDtypeStruct((total, count, LANES), BF16)
    return call(
        functools.partial(gradient_body, lines, begin, end, len(parts)),
        "slab_gradient",
        flops=30 * out.size,
        moved=8 * out.size,
        in_specs=[IN_VMEM] * (len(parts) + 2),
        out_specs=IN_HBM,
        out_shape=out,
        scratch_shapes=[pltpu.VMEM(out.shape, BF16), pltpu.SemaphoreType.DMA((count // BLOCK,))],
    )(*parts, observed, precision)


def update_body(begin, end, parts, *refs):
    states_refs, refs = refs[:parts], refs[parts:]
    scalars_ref, grams_ref, grads_ref = refs[:3]
    out_ref, grads, mixer, own, sem = refs[-5:]
    total = out_ref.shape[0]
    wide = total * TILE
    fetch = pltpu.make_async_copy(grads_ref, grads, sem)
    fetch.start()
    gram = jnp.sum(grams_ref[...], axis=0)[:, :total]
    row = lax.broadcasted_iota(jnp.int32, (total, total), 0)
    col = lax.broadcasted_iota(jnp.int32, (total, total), 1)
    diagonal = jnp.where(row == col, gram, 0.0)
    down = jnp.sum(diagonal, axis=1, keepdims=True)
    across = jnp.sum(diagonal, axis=0, keepdims=True)
    member = members(total, BF16)
    spread, anneal, step_size = (scalars_ref[k : k + 1, :1] for k in range(3))
    rate = step_size / total
    coeff = 2.0 * anneal / spread
    kernel = jnp.exp(-(down + across - 2.0 * gram) / (spread * NCELL)).astype(BF16)
    ksum = jnp.sum(kernel.astype(F32), axis=1, keepdims=True)
    half = jnp.dot(member, kernel, preferred_element_type=F32).astype(BF16)
    full = lax.dot_general(half, member, (((1,), (1,)), ((), ())), preferred_element_type=F32)
    mixer[...] = jnp.where(same_line(total), full, 0.0).astype(BF16)
    gain = 1.0 + rate * coeff * ksum
    own[...] = jnp.broadcast_to(gain[:, :, None], (total, TILE, LANES)).reshape(wide, LANES)
    fetch.wait()

    done = 0
    for part, states_ref in enumerate(states_refs):
        have = states_ref.shape[1] - (0 if part else TILE)
        low = max(begin - done, 0)
        high = min(end - done, have)
        into = done - begin
        done += have

        def step(i, carry):
            for t in range(BLOCK // TILE):
                at = pl.multiple_of(i * BLOCK + t * TILE, TILE)
                there = pl.ds(pl.multiple_of(at + into, TILE), TILE)
                states = states_ref[:, pl.ds(at, TILE), :].reshape(wide, LANES)
                both = jnp.concatenate([grads[:, there, :].reshape(wide, LANES), states], axis=1)
                mixed = jnp.dot(mixer[...], both, preferred_element_type=F32)
                drive, pulled = mixed[:, :LANES], mixed[:, LANES:]
                new = states.astype(F32) * own[...] + rate * (drive - coeff * pulled)
                out_ref[:, there, :] = new.astype(BF16).reshape(total, TILE, LANES)
            return carry

        lax.fori_loop(low // BLOCK, high // BLOCK, step, 0)


def slab_update(scalars, grams, parts, grads, begin, end, earlier):
    total, count, _ = grads.shape
    wide = total * TILE
    return call(
        functools.partial(update_body, begin, end, len(parts)),
        "slab_update",
        flops=4 * wide * wide * LANES * (count // TILE),
        moved=6 * grads.size,
        in_specs=[IN_VMEM] * len(parts)
        + [IN_VMEM, IN_VMEM, IN_HBM]
        + [IN_HBM] * len(earlier),
        out_specs=IN_VMEM,
        out_shape=jax.ShapeDtypeStruct(grads.shape, BF16),
        scratch_shapes=[
            pltpu.VMEM(grads.shape, BF16),
            pltpu.VMEM((wide, wide), BF16),
            pltpu.VMEM((wide, LANES), F32),
            pltpu.SemaphoreType.DMA,
        ],
    )(*parts, scalars, grams, grads, *earlier)


def plain_update(spread, anneal, step_size, states, grads):
    total, lines, _ = grads.shape
    flat = states[:, :lines].reshape(total, -1)
    gram = lax.dot_general(flat, flat, (((1,), (1,)), ((), ())), preferred_element_type=F32)
    gram = lax.psum(gram, "slab")
    norms = jnp.diagonal(gram)
    kernel = jnp.exp(-(norms[:, None] + norms[None, :] - 2.0 * gram) / (spread[0] * NCELL)).astype(BF16)
    ksum = jnp.sum(kernel.astype(F32), axis=1)
    drive = jnp.dot(kernel, grads.reshape(total, -1), preferred_element_type=F32)
    pulled = jnp.dot(kernel, flat, preferred_element_type=F32)
    values = flat.astype(F32)
    repel = values * ksum[:, None] - pulled
    coeff = 2.0 * anneal[0] / spread[0]
    new = values + step_size[0] / total * (drive + coeff * repel)
    return new.astype(BF16).reshape(grads.shape)


def swap(slabs):
    return lax.all_to_all(slabs, "slab", split_axis=0, concat_axis=0, tiled=True)


def on_device(particles, observed, precision, spread, anneal, step_size):
    slabs = lax.axis_size("slab")
    total = particles.shape[0] * slabs
    lines = NCELL // slabs // LANES
    sent, begun = cuts(lines)
    fields = [observed.reshape(-1, LANES), precision.reshape(-1, LANES)]
    numbers = [spread, anneal, step_size]
    first, obs, prec, scalars = split_row(particles, slabs, 0, sent, True, fields, numbers, [])
    parts = [swap(first)]
    if sent < lines:
        parts += [swap(split_row(particles, slabs, sent, lines, False, [], [], [scalars])[0])]
    if total * TILE > 256:
        grads = slab_gradient(parts, obs, prec, lines, 0, lines)
        states = jnp.concatenate([parts[0][:, :sent]] + parts[1:], axis=1)
        new = plain_update(spread, anneal, step_size, states, grads)
        return join_row(swap(new), lines, 0, None)
    if sent == lines:
        grads = slab_gradient(parts, obs, prec, lines, 0, lines)
        grams = swap(slab_gram(parts[0], lines, slabs, [], []))
        new = slab_update(scalars, grams, parts, grads, 0, lines, [])
        return join_row(swap(new), lines, 0, None)
    gram = slab_gram(parts[0], sent, 1, [], [])
    early = slab_gradient(parts[:1], obs, prec, lines, 0, begun)
    grams = swap(slab_gram(parts[1], lines - sent, slabs, [gram], [early]))
    late = slab_gradient(parts, obs, prec, lines, begun, lines)
    new = slab_update(scalars, grams, parts[:1], early, 0, begun, [])
    rest = slab_update(scalars, grams, parts, late, begun, lines, [new])
    row = join_row(swap(new), lines, 0, None)
    return join_row(swap(rest), lines, begun, row)


def solution(mesh):
    in_specs = (
        P(("groups", "slab"), None),
        P("groups"),
        P("groups"),
        P("groups"),
        P("groups"),
        P("groups"),
    )
    out_specs = P(("groups", "slab"), None)
    return jax.shard_map(
        on_device, mesh=mesh, in_specs=in_specs, out_specs=out_specs, check_vma=False
    )
```

```python
import functools

import jax
import jax.numpy as jnp
from jax import lax
from jax.experimental import pallas as pl
from jax.experimental.pallas import tpu as pltpu
from jax.sharding import PartitionSpec as P

GRID_X = 1024
GRID_Y = 1024
NCELL = 1048576
LANES = 128
LINE = GRID_Y // LANES
TILE = 16

prior_scale = 0.25
mass_term = 1.0

F32 = jnp.float32
BF16 = jnp.bfloat16
MIB = 1024 * 1024


def call(body, name, flops=0, moved=0, limit=16, **kwargs):
    return pl.pallas_call(
        body,
        name=name,
        compiler_params=pltpu.CompilerParams(vmem_limit_bytes=limit * MIB),
        cost_estimate=pl.CostEstimate(flops=flops, bytes_accessed=moved, transcendentals=0),
        **kwargs,
    )


IN_VMEM = pl.BlockSpec(memory_space=pltpu.VMEM)
IN_HBM = pl.BlockSpec(memory_space=pltpu.HBM)
BLOCK = 4 * TILE


def cuts(lines):
    if lines % (8 * BLOCK):
        return lines, lines
    return lines * 3 // 4, lines * 3 // 4 - BLOCK


def split_body(lines, begin, rim, fields, numbers, row_ref, *refs):
    field_refs, number_refs = refs[:fields], refs[fields : fields + numbers]
    out_ref, *slab_refs, rows_ref = refs[-7 - fields : -5]
    held, edges, sems, edge_sems, field_sems = refs[-5:]
    for k, number_ref in enumerate(number_refs):
        rows_ref[k : k + 1, :] = jnp.broadcast_to(number_ref[...].reshape(1, 1), (1, LANES))
    slabs, count, _ = out_ref.shape
    count -= TILE * rim
    size = count * LANES
    cells = lines * LANES

    def part(slab):
        source = row_ref.at[:, pl.ds(slab * cells + begin * LANES, size)]
        return pltpu.make_async_copy(source, held.at[:, pl.ds(slab * size, size)], sems.at[slab])

    def edge(slab):
        source = row_ref.at[:, pl.ds(slab * cells - GRID_Y, GRID_Y)]
        return pltpu.make_async_copy(source, edges.at[:, pl.ds(slab * GRID_Y, GRID_Y)], edge_sems.at[slab])

    def grid_row(ref, start):
        return ref[:, pl.ds(start, GRID_Y)].astype(F32).reshape(LINE, LANES)

    for slab in range(slabs):
        part(slab).start()
        if rim and slab:
            edge(slab).start()
    mine = pl.ds(pl.multiple_of(lax.axis_index("slab") * lines, TILE), lines)
    fetches = [
        pltpu.make_async_copy(source.at[mine, :], target, field_sems.at[k])
        for k, (source, target) in enumerate(zip(field_refs, slab_refs))
    ]
    for fetch in fetches:
        fetch.start()
    part(0).wait()
    outside = jnp.zeros((LINE, LANES), F32)
    for slab in range(slabs):
        if slab + 1 < slabs:
            part(slab + 1).wait()
        out_ref[slab, :count, :] = held[:, pl.ds(slab * size, size)].reshape(count, LANES)
        if rim:
            if slab:
                edge(slab).wait()
            below = grid_row(held, (slab + 1) * size) if slab + 1 < slabs else outside
            above = grid_row(edges, slab * GRID_Y) if slab else outside
            out_ref[slab, count:, :] = jnp.concatenate([below, above], axis=0).astype(BF16)
    for fetch in fetches:
        fetch.wait()


def split_row(row, slabs, begin, end, rim, fields, numbers, earlier):
    lines = row.shape[1] // slabs // LANES
    count = end - begin
    return call(
        functools.partial(split_body, lines, begin, rim, len(fields), len(numbers)),
        "split_row",
        moved=6 * slabs * count * LANES,
        limit=60,
        in_specs=[IN_HBM] * (1 + len(fields)) + [IN_VMEM] * len(numbers) + [IN_HBM] * len(earlier),
        out_specs=[IN_VMEM] * (2 + len(fields)),
        out_shape=[jax.ShapeDtypeStruct((slabs, count + TILE * rim, LANES), BF16)]
        + [jax.ShapeDtypeStruct((lines, LANES), BF16)] * len(fields)
        + [jax.ShapeDtypeStruct((8, LANES), F32)],
        scratch_shapes=[
            pltpu.VMEM((1, slabs * count * LANES), BF16),
            pltpu.VMEM((1, slabs * GRID_Y), BF16),
            pltpu.SemaphoreType.DMA((slabs,)),
            pltpu.SemaphoreType.DMA((slabs,)),
            pltpu.SemaphoreType.DMA((2,)),
        ],
    )(row, *fields, *numbers, *earlier)


def join_body(lines, begin, slabs_ref, *refs):
    row_ref, held, sems = refs[-3:]
    slabs, count, _ = slabs_ref.shape
    size = count * LANES
    copies = []
    for slab in range(slabs):
        at = pl.ds(slab * size, size)
        held[:, at] = slabs_ref[slab].reshape(1, size)
        target = row_ref.at[:, pl.ds((slab * lines + begin) * LANES, size)]
        copies.append(pltpu.make_async_copy(held.at[:, at], target, sems.at[slab]))
        copies[-1].start()
    for copy in copies:
        copy.wait()


def join_row(slabs, lines, begin, row):
    total, count, _ = slabs.shape
    begun = [] if row is None else [row]
    return call(
        functools.partial(join_body, lines, begin),
        "join_row",
        moved=6 * slabs.size,
        in_specs=[IN_VMEM] + [IN_HBM] * len(begun),
        out_specs=IN_HBM,
        out_shape=jax.ShapeDtypeStruct((1, total * lines * LANES), BF16),
        input_output_aliases={1: 0} if begun else {},
        scratch_shapes=[pltpu.VMEM((1, slabs.size), BF16), pltpu.SemaphoreType.DMA((total,))],
    )(slabs, *begun)


def same_line(total):
    wide = total * TILE
    row = lax.broadcasted_iota(jnp.int32, (wide, wide), 0)
    col = lax.broadcasted_iota(jnp.int32, (wide, wide), 1)
    return row % TILE == col % TILE


def members(total, dtype):
    wide = total * TILE
    row = lax.broadcasted_iota(jnp.int32, (wide, total), 0)
    col = lax.broadcasted_iota(jnp.int32, (wide, total), 1)
    return (row // TILE == col).astype(dtype)


def gram_body(steps, tiles, parts, states_ref, *refs):
    out_ref, pairs = refs[-2:]
    total = states_ref.shape[0]
    wide = total * TILE
    pairs[...] = jnp.zeros_like(pairs)

    def step(i, carry):
        parts = [
            states_ref[:, pl.ds(pl.multiple_of((i * tiles + t) * TILE, TILE), TILE), :].reshape(wide, LANES)
            for t in range(tiles)
        ]
        block = jnp.concatenate(parts, axis=1)
        pairs[...] += lax.dot_general(block, block, (((1,), (1,)), ((), ())), preferred_element_type=F32)
        return carry

    lax.fori_loop(0, steps, step, 0)
    equal = jnp.where(same_line(total), pairs[...], 0.0)
    rows = jnp.sum(equal.reshape(total, TILE, wide), axis=1)
    gram = jnp.dot(rows, members(total, F32), precision=lax.Precision.HIGHEST, preferred_element_type=F32)
    gram = jnp.concatenate([gram, jnp.zeros((total, LANES - total), F32)], axis=1)
    for part_ref in refs[:parts]:
        gram += part_ref[0]
    out_ref[...] = jnp.broadcast_to(gram[None], out_ref.shape)


def slab_gram(states, lines, copies, parts, earlier):
    total = states.shape[0]
    wide = total * TILE
    tiles = min(8, lines // TILE)
    return call(
        functools.partial(gram_body, lines // TILE // tiles, tiles, len(parts)),
        "slab_gram",
        flops=2 * wide * wide * LANES * (lines // TILE),
        moved=2 * states.size,
        in_specs=[IN_VMEM] * (1 + len(parts)) + [IN_HBM] * len(earlier),
        out_specs=IN_VMEM,
        out_shape=jax.ShapeDtypeStruct((copies, total, LANES), F32),
        scratch_shapes=[pltpu.VMEM((wide, wide), F32)],
    )(states, *parts, *earlier)


def gradient_body(lines, begin, end, parts, *refs):
    observed, precision, out_ref, grads, sems = refs[parts:]
    total = grads.shape[0]
    first = refs[0].shape[1] - TILE
    rows = BLOCK // LINE
    group = 4
    shape = (rows, LINE, LANES)
    lane = lax.broadcasted_iota(jnp.int32, (1, LINE, LANES), 2)
    line = lax.broadcasted_iota(jnp.int32, (1, LINE, LANES), 1)

    def load(particle, at, count):
        ref, at = (refs[0], at) if at < first else (refs[1], at - first)
        return ref[particle, at : at + count, :].astype(F32)

    def rim(particle):
        return refs[0][particle, first:, :].astype(F32)

    stores = []
    for k, at in enumerate(range(begin, end, BLOCK)):
        mine = slice(at - begin, at - begin + BLOCK)
        obs = observed[at : at + BLOCK, :].astype(F32).reshape(shape)
        prec = precision[at : at + BLOCK, :].astype(F32).reshape(shape)

        def step(i, carry):
            for p in range(group):
                particle = i * group + p
                here = load(particle, at, BLOCK)
                before = load(particle, at - TILE, TILE) if at else rim(particle)
                after = load(particle, at + BLOCK, TILE) if at + BLOCK < lines else rim(particle)
                above = jnp.concatenate([before[LINE:], here[:-LINE]], axis=0).reshape(shape)
                below = jnp.concatenate([here[LINE:], after[:LINE]], axis=0).reshape(shape)
                field = here.reshape(shape)
                turned = pltpu.roll(field, 1, 2)
                carried = jnp.where(line == 0, 0.0, pltpu.roll(turned, 1, 1))
                left = jnp.where(lane == 0, carried, turned)
                turned = pltpu.roll(field, LANES - 1, 2)
                carried = jnp.where(line == LINE - 1, 0.0, pltpu.roll(turned, LINE - 1, 1))
                right = jnp.where(lane == LANES - 1, carried, turned)
                laplace = (4.0 + mass_term) * field - (below + above + right + left)
                squash = jnp.tanh(field)
                result = prec * (obs - squash) * (1.0 - squash * squash) - prior_scale * laplace
                grads[particle, mine, :] = result.reshape(BLOCK, LANES).astype(BF16)
            return carry

        lax.fori_loop(0, total // group, step, 0)
        stores.append(pltpu.make_async_copy(grads.at[:, mine, :], out_ref.at[:, mine, :], sems.at[k]))
        stores[-1].start()
    for store in stores:
        store.wait()


def slab_gradient(parts, observed, precision, lines, begin, end):
    total = parts[0].shape[0]
    count = end - begin
    out = jax.ShapeDtypeStruct((total, count, LANES), BF16)
    return call(
        functools.partial(gradient_body, lines, begin, end, len(parts)),
        "slab_gradient",
        flops=30 * out.size,
        moved=8 * out.size,
        in_specs=[IN_VMEM] * (len(parts) + 2),
        out_specs=IN_HBM,
        out_shape=out,
        scratch_shapes=[pltpu.VMEM(out.shape, BF16), pltpu.SemaphoreType.DMA((count // BLOCK,))],
    )(*parts, observed, precision)


def update_body(begin, end, parts, *refs):
    states_refs, refs = refs[:parts], refs[parts:]
    scalars_ref, grams_ref, grads_ref = refs[:3]
    out_ref, grads, mixer, own, sem = refs[-5:]
    total = out_ref.shape[0]
    wide = total * TILE
    fetch = pltpu.make_async_copy(grads_ref, grads, sem)
    fetch.start()
    gram = jnp.sum(grams_ref[...], axis=0)[:, :total]
    row = lax.broadcasted_iota(jnp.int32, (total, total), 0)
    col = lax.broadcasted_iota(jnp.int32, (total, total), 1)
    diagonal = jnp.where(row == col, gram, 0.0)
    down = jnp.sum(diagonal, axis=1, keepdims=True)
    across = jnp.sum(diagonal, axis=0, keepdims=True)
    member = members(total, BF16)
    spread, anneal, step_size = (scalars_ref[k : k + 1, :1] for k in range(3))
    rate = step_size / total
    coeff = 2.0 * anneal / spread
    kernel = jnp.exp(-(down + across - 2.0 * gram) / (spread * NCELL)).astype(BF16)
    ksum = jnp.sum(kernel.astype(F32), axis=1, keepdims=True)
    half = jnp.dot(member, kernel, preferred_element_type=F32).astype(BF16)
    full = lax.dot_general(half, member, (((1,), (1,)), ((), ())), preferred_element_type=F32)
    mixer[...] = jnp.where(same_line(total), full, 0.0).astype(BF16)
    gain = 1.0 + rate * coeff * ksum
    own[...] = jnp.broadcast_to(gain[:, :, None], (total, TILE, LANES)).reshape(wide, LANES)
    fetch.wait()

    done = 0
    for part, states_ref in enumerate(states_refs):
        have = states_ref.shape[1] - (0 if part else TILE)
        low = max(begin - done, 0)
        high = min(end - done, have)
        into = done - begin
        done += have

        def step(i, carry):
            for t in range(BLOCK // TILE):
                at = pl.multiple_of(i * BLOCK + t * TILE, TILE)
                there = pl.ds(pl.multiple_of(at + into, TILE), TILE)
                states = states_ref[:, pl.ds(at, TILE), :].reshape(wide, LANES)
                both = jnp.concatenate([grads[:, there, :].reshape(wide, LANES), states], axis=1)
                mixed = jnp.dot(mixer[...], both, preferred_element_type=F32)
                drive, pulled = mixed[:, :LANES], mixed[:, LANES:]
                new = states.astype(F32) * own[...] + rate * (drive - coeff * pulled)
                out_ref[:, there, :] = new.astype(BF16).reshape(total, TILE, LANES)
            return carry

        lax.fori_loop(low // BLOCK, high // BLOCK, step, 0)


def slab_update(scalars, grams, parts, grads, begin, end, earlier):
    total, count, _ = grads.shape
    wide = total * TILE
    return call(
        functools.partial(update_body, begin, end, len(parts)),
        "slab_update",
        flops=4 * wide * wide * LANES * (count // TILE),
        moved=6 * grads.size,
        in_specs=[IN_VMEM] * len(parts)
        + [IN_VMEM, IN_VMEM, IN_HBM]
        + [IN_HBM] * len(earlier),
        out_specs=IN_VMEM,
        out_shape=jax.ShapeDtypeStruct(grads.shape, BF16),
        scratch_shapes=[
            pltpu.VMEM(grads.shape, BF16),
            pltpu.VMEM((wide, wide), BF16),
            pltpu.VMEM((wide, LANES), F32),
            pltpu.SemaphoreType.DMA,
        ],
    )(*parts, scalars, grams, grads, *earlier)


def plain_update(spread, anneal, step_size, states, grads):
    total, lines, _ = grads.shape
    flat = states[:, :lines].reshape(total, -1)
    gram = lax.dot_general(flat, flat, (((1,), (1,)), ((), ())), preferred_element_type=F32)
    gram = lax.psum(gram, "slab")
    norms = jnp.diagonal(gram)
    kernel = jnp.exp(-(norms[:, None] + norms[None, :] - 2.0 * gram) / (spread[0] * NCELL)).astype(BF16)
    ksum = jnp.sum(kernel.astype(F32), axis=1)
    drive = jnp.dot(kernel, grads.reshape(total, -1), preferred_element_type=F32)
    pulled = jnp.dot(kernel, flat, preferred_element_type=F32)
    values = flat.astype(F32)
    repel = values * ksum[:, None] - pulled
    coeff = 2.0 * anneal[0] / spread[0]
    new = values + step_size[0] / total * (drive + coeff * repel)
    return new.astype(BF16).reshape(grads.shape)


def swap(slabs):
    return lax.all_to_all(slabs, "slab", split_axis=0, concat_axis=0, tiled=True)


def partner(k):
    return lax.axis_index("slab").astype(jnp.int32) ^ k


def lines_of(start, count):
    return pl.ds(pl.multiple_of(start, TILE), count)


def split_pieces_body(ks, half, raw, lines, gates, row_ref, *refs):
    refs = refs[gates:]
    count = len(ks)
    out_refs, helds, sems = refs[:count], refs[count : 2 * count], refs[2 * count]
    cells = lines * LANES
    end = row_ref.shape[1]
    copies = []
    for k, held in zip(ks, helds):
        mine = []

        def fetch(start, size, to):
            source = row_ref.at[:, pl.ds(pl.multiple_of(start, GRID_Y), size)]
            at = sems.at[len(copies) * 5 + len(mine)]
            mine.append(pltpu.make_async_copy(source, held.at[:, pl.ds(to, size)], at))
            mine[-1].start()

        slab = partner(k)
        fetch(slab * cells, cells, 0)
        fetch(jnp.minimum((slab + 1) * cells, end - GRID_Y), GRID_Y, cells)
        fetch(jnp.maximum(slab * cells - GRID_Y, 0), GRID_Y, cells + GRID_Y)
        if raw and k < half:
            other = partner(k ^ half)
            fetch(other * cells, raw * LANES + GRID_Y, cells + 2 * GRID_Y)
            fetch(jnp.maximum(other * cells - GRID_Y, 0), GRID_Y, cells + 3 * GRID_Y + raw * LANES)
        copies.append(mine)

    def grid_row(held, at):
        return held[:, pl.ds(at, GRID_Y)].astype(F32).reshape(LINE, LANES)

    for k, held, out_ref, mine in zip(ks, helds, out_refs, copies):
        for copy in mine:
            copy.wait()
        slab = partner(k)
        out_ref[:lines, :] = held[:, :cells].reshape(lines, LANES)
        below = jnp.where(slab == end // cells - 1, 0.0, grid_row(held, cells))
        above = jnp.where(slab == 0, 0.0, grid_row(held, cells + GRID_Y))
        out_ref[lines : lines + TILE, :] = jnp.concatenate([below, above], axis=0).astype(BF16)
        if raw and k < half:
            at = cells + 2 * GRID_Y
            to = lines + TILE
            out_ref[to : to + raw, :] = held[:, at : at + raw * LANES].reshape(raw, LANES)
            below = grid_row(held, at + raw * LANES)
            above = jnp.where(partner(k ^ half) == 0, 0.0, grid_row(held, at + raw * LANES + GRID_Y))
            out_ref[to + raw :, :] = jnp.concatenate([below, above], axis=0).astype(BF16)


def split_pieces(row, slabs, raw, ks, gates):
    lines = row.shape[1] // slabs // LANES
    half = slabs // 2
    extra = [raw if k < half else 0 for k in ks]
    sizes = [lines + TILE + (more + TILE if more else 0) for more in extra]
    return call(
        functools.partial(split_pieces_body, ks, half, raw, lines, len(gates)),
        "split_pieces",
        moved=6 * sum(sizes) * LANES,
        limit=16 if gates else 60,
        in_specs=[IN_HBM] + [IN_VMEM] * len(gates),
        out_specs=[IN_VMEM] * len(ks),
        out_shape=[jax.ShapeDtypeStruct((size, LANES), BF16) for size in sizes],
        scratch_shapes=[pltpu.VMEM((1, (size + TILE) * LANES), BF16) for size in sizes]
        + [pltpu.SemaphoreType.DMA((5 * len(ks),))],
    )(row, *gates)


def join_pieces_body(ks, half, raw, lines, row_ref, *refs):
    count = len(ks)
    pieces = refs[:count]
    row_ref, token_ref, *helds, sems = refs[count:]
    cells = lines * LANES
    skip = raw * LANES
    copies = []
    for k, piece, held in zip(ks, pieces, helds):
        near = k < half
        held[...] = piece[...].reshape(held.shape)

        def store(at, size, start):
            target = row_ref.at[:, pl.ds(pl.multiple_of(start, GRID_Y), size)]
            copies.append(pltpu.make_async_copy(held.at[:, pl.ds(at, size)], target, sems.at[len(copies)]))
            copies[-1].start()

        if near:
            store(0, cells, partner(k) * cells)
            if raw:
                store(cells, skip, partner(k ^ half) * cells)
        else:
            store(0, cells - skip, partner(k) * cells + skip)
    for copy in copies:
        copy.wait()
    token_ref[...] = jnp.zeros_like(token_ref)


def join_pieces(row, slabs, raw, pieces, ks):
    cells = NCELL // slabs
    out = jax.ShapeDtypeStruct((1, NCELL), BF16)
    token = jax.ShapeDtypeStruct((8, LANES), F32)
    body = functools.partial(join_pieces_body, ks, slabs // 2, raw, cells // LANES)
    return call(
        body if row is not None else functools.partial(body, None),
        "join_pieces",
        moved=6 * sum(piece.size for piece in pieces),
        in_specs=([] if row is None else [IN_HBM]) + [IN_VMEM] * len(ks),
        out_specs=[IN_HBM, IN_VMEM],
        out_shape=[out, token],
        input_output_aliases={} if row is None else {0: 0},
        scratch_shapes=[pltpu.VMEM((1, piece.size), BF16) for piece in pieces]
        + [pltpu.SemaphoreType.DMA((2 * len(ks),))],
    )(*([] if row is None else [row]), *pieces)


def swap_order(total):
    row = lax.broadcasted_iota(jnp.int32, (total, total), 0)
    col = lax.broadcasted_iota(jnp.int32, (total, total), 1)
    return (row == partner(col)).astype(F32)


def reorder(gram):
    order = swap_order(gram.shape[0])
    half = jnp.dot(order, gram, precision=lax.Precision.HIGHEST, preferred_element_type=F32)
    return jnp.dot(half, order, precision=lax.Precision.HIGHEST, preferred_element_type=F32)


def gram_pieces_body(lines, *refs):
    pieces, out_ref, pairs = refs[:-2], refs[-2], refs[-1]
    total = len(pieces)
    wide = total * TILE
    tiles = 4
    pairs[...] = jnp.zeros_like(pairs)

    def step(i, carry):
        parts = []
        for t in range(tiles):
            at = lines_of((i * tiles + t) * TILE, TILE)
            parts.append(jnp.concatenate([piece[at, :] for piece in pieces], axis=0))
        block = jnp.concatenate(parts, axis=1)
        pairs[...] += lax.dot_general(block, block, (((1,), (1,)), ((), ())), preferred_element_type=F32)
        return carry

    lax.fori_loop(0, lines // TILE // tiles, step, 0)
    equal = jnp.where(same_line(total), pairs[...], 0.0)
    rows = jnp.sum(equal.reshape(total, TILE, wide), axis=1)
    gram = jnp.dot(rows, members(total, F32), precision=lax.Precision.HIGHEST, preferred_element_type=F32)
    gram = jnp.concatenate([reorder(gram), jnp.zeros((total, LANES - total), F32)], axis=1)
    out_ref[...] = jnp.broadcast_to(gram[None], out_ref.shape)


def gram_pieces(pieces, lines):
    total = len(pieces)
    wide = total * TILE
    return call(
        functools.partial(gram_pieces_body, lines),
        "gram_pieces",
        flops=2 * wide * wide * LANES * (lines // TILE),
        moved=2 * total * lines * LANES,
        in_specs=[IN_VMEM] * total,
        out_specs=IN_VMEM,
        out_shape=jax.ShapeDtypeStruct((total, total, LANES), F32),
        scratch_shapes=[pltpu.VMEM((wide, wide), F32)],
    )(*pieces)


def gradient_pieces_body(k, lines, count, views, arrays, *refs):
    observed_ref, precision_ref, out_ref, observed, precision, grads, sems = refs[arrays:]
    rows = BLOCK // LINE
    shape = (rows, LINE, LANES)
    lane = lax.broadcasted_iota(jnp.int32, (1, LINE, LANES), 2)
    line = lax.broadcasted_iota(jnp.int32, (1, LINE, LANES), 1)
    steps = count // BLOCK
    mine = lines_of(partner(k) * lines, count)
    fetches = [
        pltpu.make_async_copy(observed_ref.at[mine, :], observed, sems.at[steps]),
        pltpu.make_async_copy(precision_ref.at[mine, :], precision, sems.at[steps + 1]),
    ]
    for fetch in fetches:
        fetch.start()
    for fetch in fetches:
        fetch.wait()

    def store(i):
        at = lines_of(i * BLOCK, BLOCK)
        return pltpu.make_async_copy(grads.at[:, at, :], out_ref.at[:, at, :], sems.at[i])

    def step(i, carry):
        start = i * BLOCK
        at = lines_of(start, BLOCK)
        obs = observed[at, :].astype(F32).reshape(shape)
        prec = precision[at, :].astype(F32).reshape(shape)
        for p, (array, lead, base) in enumerate(views):

            def load(begin, size):
                part = lines_of(base + begin, size)
                value = refs[array][part, :] if lead is None else refs[array][lead, part, :]
                return value.astype(F32)

            here = load(start, BLOCK)
            before = load(jnp.where(i == 0, count, start - TILE), TILE)
            after = load(start + BLOCK, TILE)
            above = jnp.concatenate([before[LINE:], here[:-LINE]], axis=0).reshape(shape)
            below = jnp.concatenate([here[LINE:], after[:LINE]], axis=0).reshape(shape)
            field = here.reshape(shape)
            turned = pltpu.roll(field, 1, 2)
            carried = jnp.where(line == 0, 0.0, pltpu.roll(turned, 1, 1))
            left = jnp.where(lane == 0, carried, turned)
            turned = pltpu.roll(field, LANES - 1, 2)
            carried = jnp.where(line == LINE - 1, 0.0, pltpu.roll(turned, LINE - 1, 1))
            right = jnp.where(lane == LANES - 1, carried, turned)
            laplace = (4.0 + mass_term) * field - (below + above + right + left)
            squash = jnp.tanh(field)
            result = prec * (obs - squash) * (1.0 - squash * squash) - prior_scale * laplace
            grads[p, at, :] = result.reshape(BLOCK, LANES).astype(BF16)
        store(i).start()
        return carry

    def finish(i, carry):
        store(i).wait()
        return carry

    lax.fori_loop(0, steps, step, 0)
    lax.fori_loop(0, steps, finish, 0)


def gradient_pieces(arrays, views, observed, precision, lines, count, k):
    out = jax.ShapeDtypeStruct((len(views), count, LANES), BF16)
    return call(
        functools.partial(gradient_pieces_body, k, lines, count, views, len(arrays)),
        "gradient_pieces",
        flops=30 * out.size,
        moved=8 * out.size,
        in_specs=[IN_VMEM] * len(arrays) + [IN_HBM, IN_HBM],
        out_specs=IN_HBM,
        out_shape=out,
        scratch_shapes=[
            pltpu.VMEM((count, LANES), BF16),
            pltpu.VMEM((count, LANES), BF16),
            pltpu.VMEM(out.shape, BF16),
            pltpu.SemaphoreType.DMA((count // BLOCK + 2,)),
        ],
    )(*arrays, observed, precision)


def raw_body(raw, lines, *refs):
    out_ref = refs[-1]
    for k, piece in enumerate(refs[:-1]):
        out_ref[k, :raw, :] = piece[:raw, :]
        below = piece[raw : raw + TILE, :].astype(F32)[:LINE]
        above = piece[lines : lines + TILE, :].astype(F32)[LINE:]
        out_ref[k, raw:, :] = jnp.concatenate([below, above], axis=0).astype(BF16)


def raw_states(pieces, raw, lines):
    out = jax.ShapeDtypeStruct((len(pieces), raw + TILE, LANES), BF16)
    return call(
        functools.partial(raw_body, raw, lines),
        "raw_states",
        moved=4 * out.size,
        in_specs=[IN_VMEM] * len(pieces),
        out_specs=IN_VMEM,
        out_shape=out,
    )(*pieces)


def update_pieces_body(ks, half, raw, lines, groups, extra, *refs):
    total = 2 * half
    pieces, refs = refs[:total], refs[total:]
    scalars_ref, grams_ref, *refs = refs
    group_refs, refs = refs[: len(groups)], refs[len(groups) :]
    raw_refs, refs = refs[:extra], refs[extra:]
    out_refs = refs[-len(ks) - 5 : -5]
    grads, raw_grads, mixer, own, sems = refs[-5:]
    wide = total * TILE
    high = len(ks) * TILE
    fetches = []
    for group, group_ref in zip(groups, group_refs):
        for j, k in enumerate(group):
            fetches.append(pltpu.make_async_copy(group_ref.at[j], grads.at[k], sems.at[len(fetches)]))
    if extra:
        fetches.append(pltpu.make_async_copy(raw_refs[1], raw_grads, sems.at[len(fetches)]))
    for fetch in fetches:
        fetch.start()
    spread, anneal, step_size = (scalars_ref[k : k + 1, :1] for k in range(3))
    rate = step_size / total
    coeff = 2.0 * anneal / spread
    gram = reorder(jnp.sum(grams_ref[...], axis=0)[:, :total])
    row = lax.broadcasted_iota(jnp.int32, (total, total), 0)
    col = lax.broadcasted_iota(jnp.int32, (total, total), 1)
    diagonal = jnp.where(row == col, gram, 0.0)
    down = jnp.sum(diagonal, axis=1, keepdims=True)
    across = jnp.sum(diagonal, axis=0, keepdims=True)
    kernel = jnp.exp(-(down + across - 2.0 * gram) / (spread * NCELL)).astype(BF16)
    ksum = jnp.sum(kernel.astype(F32), axis=1, keepdims=True)
    member = members(total, BF16)
    half_way = jnp.dot(member, kernel, preferred_element_type=F32).astype(BF16)
    full = lax.dot_general(half_way, member, (((1,), (1,)), ((), ())), preferred_element_type=F32)
    full = jnp.where(same_line(total), full, 0.0)
    gain = jnp.broadcast_to((1.0 + rate * coeff * ksum)[:, :, None], (total, TILE, LANES)).reshape(wide, LANES)
    for j, k in enumerate(ks):
        mixer[j * TILE : (j + 1) * TILE, :] = full[k * TILE : (k + 1) * TILE].astype(BF16)
        own[j * TILE : (j + 1) * TILE, :] = gain[k * TILE : (k + 1) * TILE]
    for fetch in fetches:
        fetch.wait()

    def mix(states, slopes, who, stores):
        size = len(who) * TILE
        states = jnp.concatenate(states, axis=0)
        both = jnp.concatenate([slopes.reshape(wide, LANES), states], axis=1)
        mixed = jnp.dot(mixer[:size, :], both, preferred_element_type=F32)
        drive, pulled = mixed[:, :LANES], mixed[:, LANES:]
        kept = jnp.concatenate([states[k * TILE : (k + 1) * TILE] for k in who], axis=0).astype(F32)
        new = (kept * own[:size, :] + rate * (drive - coeff * pulled)).astype(BF16)
        for j, (out_ref, to) in enumerate(stores):
            out_ref[lines_of(to, TILE), :] = new[j * TILE : (j + 1) * TILE]

    near = [k for k in ks if k < half]

    def slab_step(who, i, carry):
        for t in range(BLOCK // TILE):
            at = i * BLOCK + t * TILE
            stores = [(out_ref, at if k < half else at - raw) for k, out_ref in zip(who, out_refs)]
            mix([ref[lines_of(at, TILE), :] for ref in pieces], grads[:, lines_of(at, TILE), :], who, stores)
        return carry

    def raw_step(i, carry):
        for t in range(BLOCK // TILE):
            at = i * BLOCK + t * TILE
            states = [ref[lines_of(lines + TILE + at, TILE), :] for ref in pieces[:half]]
            states += [raw_refs[0][j, lines_of(at, TILE), :] for j in range(half)]
            stores = [(out_ref, lines + at) for out_ref in out_refs[: len(near)]]
            mix(states, raw_grads[:, lines_of(at, TILE), :], near, stores)
        return carry

    if near and raw:
        lax.fori_loop(0, raw // BLOCK, functools.partial(slab_step, near), 0)
    lax.fori_loop(raw // BLOCK, lines // BLOCK, functools.partial(slab_step, ks), 0)
    if near and raw:
        lax.fori_loop(0, raw // BLOCK, raw_step, 0)


def update_pieces(scalars, grams, pieces, grads, groups, raw_parts, gates, raw, lines, ks):
    total = len(pieces)
    half = total // 2
    wide = total * TILE
    ks = tuple(sorted(ks))
    sizes = [lines + raw if k < half else lines - raw for k in ks]
    results = call(
        functools.partial(update_pieces_body, ks, half, raw, lines, groups, len(raw_parts)),
        "update_pieces",
        flops=4 * len(ks) * TILE * wide * LANES * (lines // TILE),
        moved=2 * (2 * total + len(ks)) * lines * LANES,
        in_specs=[IN_VMEM] * (total + 2)
        + [IN_HBM] * len(groups)
        + [IN_VMEM, IN_HBM][: len(raw_parts)]
        + [IN_VMEM] * len(gates),
        out_specs=[IN_VMEM] * len(ks),
        out_shape=[jax.ShapeDtypeStruct((size, LANES), BF16) for size in sizes],
        scratch_shapes=[
            pltpu.VMEM((total, lines, LANES), BF16),
            pltpu.VMEM((total, max(raw, TILE), LANES), BF16),
            pltpu.VMEM((len(ks) * TILE, wide), BF16),
            pltpu.VMEM((len(ks) * TILE, LANES), F32),
            pltpu.SemaphoreType.DMA((total + 1,)),
        ],
    )(*pieces, scalars, grams, *grads, *raw_parts, *gates)
    return dict(zip(ks, results))


def exchange(piece, k, slabs):
    return lax.ppermute(piece, "slab", [(i, i ^ k) for i in range(slabs)])


RAW = 0
SENDS = ((8, 9, 10, 4, 11), (5, 12, 6, 13, 7), (14, 1, 15, 2, 3, 0))
GROUPS = ((8, 9, 10, 4), (11, 5, 12, 6), (13, 7, 14, 0), (1, 15, 2, 3))


def by_pieces(particles, observed, precision, spread, anneal, step_size):
    slabs = lax.axis_size("slab")
    half = slabs // 2
    lines = NCELL // slabs // LANES
    obs = observed.reshape(-1, LANES)
    prec = precision.reshape(-1, LANES)
    states = [None] * slabs
    for n, ks in enumerate(SENDS):
        gates = [states[SENDS[n - 1][0]]] if n else []
        for k, piece in zip(ks, split_pieces(particles, slabs, RAW, ks, gates)):
            states[k] = exchange(piece, k, slabs) if k else piece
    grads = []
    for group in GROUPS:
        arrays = [states[k] for k in group]
        views = tuple((j, None, 0) for j in range(len(group)))
        grads.append(gradient_pieces(arrays, views, obs, prec, lines, lines, 0))
    grams = swap(gram_pieces(states, lines))
    scalars = jnp.concatenate([spread, anneal, step_size])
    scalars = jnp.broadcast_to(scalars[:, None], (3, LANES))
    extra = []
    if RAW:
        far = exchange(raw_states(states[:half], RAW, lines), half, slabs)
        views = [(k, None, lines + TILE) for k in range(half)] + [(half, k, 0) for k in range(half)]
        slopes = gradient_pieces(states[:half] + [far], tuple(views), obs, prec, lines, RAW, half)
        extra = [far, slopes]
    new = [None] * slabs
    row = None
    gates = []
    for n, ks in enumerate(SENDS):
        more = extra if min(ks) < half else []
        results = update_pieces(scalars, grams, states, grads, GROUPS, more, gates, RAW, lines, ks)
        for k in ks:
            new[k] = exchange(results[k], k, slabs) if k else results[k]
        gates = [new[ks[0]]]
    for group in GROUPS:
        row, _ = join_pieces(row, slabs, RAW, [new[k] for k in group], group)
    return row


def on_device(particles, observed, precision, spread, anneal, step_size):
    slabs = lax.axis_size("slab")
    total = particles.shape[0] * slabs
    lines = NCELL // slabs // LANES
    if slabs == 16:
        return by_pieces(particles, observed, precision, spread, anneal, step_size)
    sent, begun = cuts(lines)
    fields = [observed.reshape(-1, LANES), precision.reshape(-1, LANES)]
    numbers = [spread, anneal, step_size]
    first, obs, prec, scalars = split_row(particles, slabs, 0, sent, True, fields, numbers, [])
    parts = [swap(first)]
    if sent < lines:
        parts += [swap(split_row(particles, slabs, sent, lines, False, [], [], [scalars])[0])]
    if total * TILE > 256:
        grads = slab_gradient(parts, obs, prec, lines, 0, lines)
        states = jnp.concatenate([parts[0][:, :sent]] + parts[1:], axis=1)
        new = plain_update(spread, anneal, step_size, states, grads)
        return join_row(swap(new), lines, 0, None)
    if sent == lines:
        grads = slab_gradient(parts, obs, prec, lines, 0, lines)
        grams = swap(slab_gram(parts[0], lines, slabs, [], []))
        new = slab_update(scalars, grams, parts, grads, 0, lines, [])
        return join_row(swap(new), lines, 0, None)
    gram = slab_gram(parts[0], sent, 1, [], [])
    early = slab_gradient(parts[:1], obs, prec, lines, 0, begun)
    grams = swap(slab_gram(parts[1], lines - sent, slabs, [gram], [early]))
    late = slab_gradient(parts, obs, prec, lines, begun, lines)
    new = slab_update(scalars, grams, parts[:1], early, 0, begun, [])
    rest = slab_update(scalars, grams, parts, late, begun, lines, [new])
    row = join_row(swap(new), lines, 0, None)
    return join_row(swap(rest), lines, begun, row)


def solution(mesh):
    in_specs = (
        P(("groups", "slab"), None),
        P("groups"),
        P("groups"),
        P("groups"),
        P("groups"),
        P("groups"),
    )
    out_specs = P(("groups", "slab"), None)
    return jax.shard_map(
        on_device, mesh=mesh, in_specs=in_specs, out_specs=out_specs, check_vma=False
    )
```

```python
import functools

import jax
import jax.numpy as jnp
from jax import lax
from jax.experimental import pallas as pl
from jax.experimental.pallas import tpu as pltpu
from jax.sharding import PartitionSpec as P

GRID_X = 1024
GRID_Y = 1024
NCELL = 1048576
LANES = 128
LINE = GRID_Y // LANES
TILE = 16

prior_scale = 0.25
mass_term = 1.0

F32 = jnp.float32
BF16 = jnp.bfloat16
MIB = 1024 * 1024


def call(body, name, flops=0, moved=0, limit=16, **kwargs):
    return pl.pallas_call(
        body,
        name=name,
        compiler_params=pltpu.CompilerParams(vmem_limit_bytes=limit * MIB),
        cost_estimate=pl.CostEstimate(flops=flops, bytes_accessed=moved, transcendentals=0),
        **kwargs,
    )


IN_VMEM = pl.BlockSpec(memory_space=pltpu.VMEM)
IN_HBM = pl.BlockSpec(memory_space=pltpu.HBM)


def in_hbm(array):
    return pltpu.with_memory_space_constraint(array, pltpu.HBM)


BLOCK = 4 * TILE


def cuts(lines):
    if lines % (8 * BLOCK):
        return lines, lines
    return lines * 3 // 4, lines * 3 // 4 - BLOCK


def split_body(lines, begin, rim, fields, numbers, row_ref, *refs):
    field_refs, number_refs = refs[:fields], refs[fields : fields + numbers]
    out_ref, *slab_refs, rows_ref = refs[-7 - fields : -5]
    held, edges, sems, edge_sems, field_sems = refs[-5:]
    for k, number_ref in enumerate(number_refs):
        rows_ref[k : k + 1, :] = jnp.broadcast_to(number_ref[...].reshape(1, 1), (1, LANES))
    slabs, count, _ = out_ref.shape
    count -= TILE * rim
    size = count * LANES
    cells = lines * LANES

    def part(slab):
        source = row_ref.at[:, pl.ds(slab * cells + begin * LANES, size)]
        return pltpu.make_async_copy(source, held.at[:, pl.ds(slab * size, size)], sems.at[slab])

    def edge(slab):
        source = row_ref.at[:, pl.ds(slab * cells - GRID_Y, GRID_Y)]
        return pltpu.make_async_copy(source, edges.at[:, pl.ds(slab * GRID_Y, GRID_Y)], edge_sems.at[slab])

    def grid_row(ref, start):
        return ref[:, pl.ds(start, GRID_Y)].astype(F32).reshape(LINE, LANES)

    for slab in range(slabs):
        part(slab).start()
        if rim and slab:
            edge(slab).start()
    mine = pl.ds(pl.multiple_of(lax.axis_index("slab") * lines, TILE), lines)
    fetches = [
        pltpu.make_async_copy(source.at[mine, :], target, field_sems.at[k])
        for k, (source, target) in enumerate(zip(field_refs, slab_refs))
    ]
    for fetch in fetches:
        fetch.start()
    part(0).wait()
    outside = jnp.zeros((LINE, LANES), F32)
    for slab in range(slabs):
        if slab + 1 < slabs:
            part(slab + 1).wait()
        out_ref[slab, :count, :] = held[:, pl.ds(slab * size, size)].reshape(count, LANES)
        if rim:
            if slab:
                edge(slab).wait()
            below = grid_row(held, (slab + 1) * size) if slab + 1 < slabs else outside
            above = grid_row(edges, slab * GRID_Y) if slab else outside
            out_ref[slab, count:, :] = jnp.concatenate([below, above], axis=0).astype(BF16)
    for fetch in fetches:
        fetch.wait()


def split_row(row, slabs, begin, end, rim, fields, numbers, earlier):
    lines = row.shape[1] // slabs // LANES
    count = end - begin
    return call(
        functools.partial(split_body, lines, begin, rim, len(fields), len(numbers)),
        "split_row",
        moved=6 * slabs * count * LANES,
        in_specs=[IN_HBM] * (1 + len(fields)) + [IN_VMEM] * len(numbers) + [IN_HBM] * len(earlier),
        out_specs=[IN_VMEM] * (2 + len(fields)),
        out_shape=[jax.ShapeDtypeStruct((slabs, count + TILE * rim, LANES), BF16)]
        + [jax.ShapeDtypeStruct((lines, LANES), BF16)] * len(fields)
        + [jax.ShapeDtypeStruct((8, LANES), F32)],
        scratch_shapes=[
            pltpu.VMEM((1, slabs * count * LANES), BF16),
            pltpu.VMEM((1, slabs * GRID_Y), BF16),
            pltpu.SemaphoreType.DMA((slabs,)),
            pltpu.SemaphoreType.DMA((slabs,)),
            pltpu.SemaphoreType.DMA((2,)),
        ],
    )(row, *fields, *numbers, *earlier)


def join_body(lines, begin, slabs_ref, *refs):
    row_ref, held, sems = refs[-3:]
    slabs, count, _ = slabs_ref.shape
    size = count * LANES
    copies = []
    for slab in range(slabs):
        at = pl.ds(slab * size, size)
        held[:, at] = slabs_ref[slab].reshape(1, size)
        target = row_ref.at[:, pl.ds((slab * lines + begin) * LANES, size)]
        copies.append(pltpu.make_async_copy(held.at[:, at], target, sems.at[slab]))
        copies[-1].start()
    for copy in copies:
        copy.wait()


def join_row(slabs, lines, begin, row):
    total, count, _ = slabs.shape
    begun = [] if row is None else [row]
    return call(
        functools.partial(join_body, lines, begin),
        "join_row",
        moved=6 * slabs.size,
        in_specs=[IN_VMEM] + [IN_HBM] * len(begun),
        out_specs=IN_HBM,
        out_shape=jax.ShapeDtypeStruct((1, total * lines * LANES), BF16),
        input_output_aliases={1: 0} if begun else {},
        scratch_shapes=[pltpu.VMEM((1, slabs.size), BF16), pltpu.SemaphoreType.DMA((total,))],
    )(slabs, *begun)


def same_line(total):
    wide = total * TILE
    row = lax.broadcasted_iota(jnp.int32, (wide, wide), 0)
    col = lax.broadcasted_iota(jnp.int32, (wide, wide), 1)
    return row % TILE == col % TILE


def members(total, dtype):
    wide = total * TILE
    row = lax.broadcasted_iota(jnp.int32, (wide, total), 0)
    col = lax.broadcasted_iota(jnp.int32, (wide, total), 1)
    return (row // TILE == col).astype(dtype)


def gram_body(steps, tiles, parts, states_ref, *refs):
    out_ref, pairs = refs[-2:]
    total = states_ref.shape[0]
    wide = total * TILE
    pairs[...] = jnp.zeros_like(pairs)

    def step(i, carry):
        parts = [
            states_ref[:, pl.ds(pl.multiple_of((i * tiles + t) * TILE, TILE), TILE), :].reshape(wide, LANES)
            for t in range(tiles)
        ]
        block = jnp.concatenate(parts, axis=1)
        pairs[...] += lax.dot_general(block, block, (((1,), (1,)), ((), ())), preferred_element_type=F32)
        return carry

    lax.fori_loop(0, steps, step, 0)
    equal = jnp.where(same_line(total), pairs[...], 0.0)
    rows = jnp.sum(equal.reshape(total, TILE, wide), axis=1)
    gram = jnp.dot(rows, members(total, F32), precision=lax.Precision.HIGHEST, preferred_element_type=F32)
    gram = jnp.concatenate([gram, jnp.zeros((total, LANES - total), F32)], axis=1)
    for part_ref in refs[:parts]:
        gram += part_ref[0]
    out_ref[...] = jnp.broadcast_to(gram[None], out_ref.shape)


def slab_gram(states, lines, copies, parts, earlier):
    total = states.shape[0]
    wide = total * TILE
    tiles = min(8, lines // TILE)
    return call(
        functools.partial(gram_body, lines // TILE // tiles, tiles, len(parts)),
        "slab_gram",
        flops=2 * wide * wide * LANES * (lines // TILE),
        moved=2 * states.size,
        in_specs=[IN_VMEM] * (1 + len(parts)) + [IN_HBM] * len(earlier),
        out_specs=IN_VMEM,
        out_shape=jax.ShapeDtypeStruct((copies, total, LANES), F32),
        scratch_shapes=[pltpu.VMEM((wide, wide), F32)],
    )(states, *parts, *earlier)


def gradient_body(lines, begin, end, parts, *refs):
    observed, precision, out_ref, grads, sems = refs[parts:]
    total = grads.shape[0]
    first = refs[0].shape[1] - TILE
    rows = BLOCK // LINE
    group = 4
    shape = (rows, LINE, LANES)
    lane = lax.broadcasted_iota(jnp.int32, (1, LINE, LANES), 2)
    line = lax.broadcasted_iota(jnp.int32, (1, LINE, LANES), 1)

    def load(particle, at, count):
        ref, at = (refs[0], at) if at < first else (refs[1], at - first)
        return ref[particle, at : at + count, :].astype(F32)

    def rim(particle):
        return refs[0][particle, first:, :].astype(F32)

    stores = []
    for k, at in enumerate(range(begin, end, BLOCK)):
        mine = slice(at - begin, at - begin + BLOCK)
        obs = observed[at : at + BLOCK, :].astype(F32).reshape(shape)
        prec = precision[at : at + BLOCK, :].astype(F32).reshape(shape)

        def step(i, carry):
            for p in range(group):
                particle = i * group + p
                here = load(particle, at, BLOCK)
                before = load(particle, at - TILE, TILE) if at else rim(particle)
                after = load(particle, at + BLOCK, TILE) if at + BLOCK < lines else rim(particle)
                above = jnp.concatenate([before[LINE:], here[:-LINE]], axis=0).reshape(shape)
                below = jnp.concatenate([here[LINE:], after[:LINE]], axis=0).reshape(shape)
                field = here.reshape(shape)
                turned = pltpu.roll(field, 1, 2)
                carried = jnp.where(line == 0, 0.0, pltpu.roll(turned, 1, 1))
                left = jnp.where(lane == 0, carried, turned)
                turned = pltpu.roll(field, LANES - 1, 2)
                carried = jnp.where(line == LINE - 1, 0.0, pltpu.roll(turned, LINE - 1, 1))
                right = jnp.where(lane == LANES - 1, carried, turned)
                laplace = (4.0 + mass_term) * field - (below + above + right + left)
                squash = jnp.tanh(field)
                result = prec * (obs - squash) * (1.0 - squash * squash) - prior_scale * laplace
                grads[particle, mine, :] = result.reshape(BLOCK, LANES).astype(BF16)
            return carry

        lax.fori_loop(0, total // group, step, 0)
        stores.append(pltpu.make_async_copy(grads.at[:, mine, :], out_ref.at[:, mine, :], sems.at[k]))
        stores[-1].start()
    for store in stores:
        store.wait()


def slab_gradient(parts, observed, precision, lines, begin, end):
    total = parts[0].shape[0]
    count = end - begin
    out = jax.ShapeDtypeStruct((total, count, LANES), BF16)
    return call(
        functools.partial(gradient_body, lines, begin, end, len(parts)),
        "slab_gradient",
        flops=30 * out.size,
        moved=8 * out.size,
        in_specs=[IN_VMEM] * (len(parts) + 2),
        out_specs=IN_HBM,
        out_shape=out,
        scratch_shapes=[pltpu.VMEM(out.shape, BF16), pltpu.SemaphoreType.DMA((count // BLOCK,))],
    )(*parts, observed, precision)


def update_body(begin, end, parts, *refs):
    states_refs, refs = refs[:parts], refs[parts:]
    scalars_ref, grams_ref, grads_ref = refs[:3]
    out_ref, grads, mixer, own, sem = refs[-5:]
    total = out_ref.shape[0]
    wide = total * TILE
    fetch = pltpu.make_async_copy(grads_ref, grads, sem)
    fetch.start()
    gram = jnp.sum(grams_ref[...], axis=0)[:, :total]
    row = lax.broadcasted_iota(jnp.int32, (total, total), 0)
    col = lax.broadcasted_iota(jnp.int32, (total, total), 1)
    diagonal = jnp.where(row == col, gram, 0.0)
    down = jnp.sum(diagonal, axis=1, keepdims=True)
    across = jnp.sum(diagonal, axis=0, keepdims=True)
    member = members(total, BF16)
    spread, anneal, step_size = (scalars_ref[k : k + 1, :1] for k in range(3))
    rate = step_size / total
    coeff = 2.0 * anneal / spread
    kernel = jnp.exp(-(down + across - 2.0 * gram) / (spread * NCELL)).astype(BF16)
    ksum = jnp.sum(kernel.astype(F32), axis=1, keepdims=True)
    half = jnp.dot(member, kernel, preferred_element_type=F32).astype(BF16)
    full = lax.dot_general(half, member, (((1,), (1,)), ((), ())), preferred_element_type=F32)
    mixer[...] = jnp.where(same_line(total), full, 0.0).astype(BF16)
    gain = 1.0 + rate * coeff * ksum
    own[...] = jnp.broadcast_to(gain[:, :, None], (total, TILE, LANES)).reshape(wide, LANES)
    fetch.wait()

    done = 0
    for part, states_ref in enumerate(states_refs):
        have = states_ref.shape[1] - (0 if part else TILE)
        low = max(begin - done, 0)
        high = min(end - done, have)
        into = done - begin
        done += have

        def step(i, carry):
            for t in range(BLOCK // TILE):
                at = pl.multiple_of(i * BLOCK + t * TILE, TILE)
                there = pl.ds(pl.multiple_of(at + into, TILE), TILE)
                states = states_ref[:, pl.ds(at, TILE), :].reshape(wide, LANES)
                both = jnp.concatenate([grads[:, there, :].reshape(wide, LANES), states], axis=1)
                mixed = jnp.dot(mixer[...], both, preferred_element_type=F32)
                drive, pulled = mixed[:, :LANES], mixed[:, LANES:]
                new = states.astype(F32) * own[...] + rate * (drive - coeff * pulled)
                out_ref[:, there, :] = new.astype(BF16).reshape(total, TILE, LANES)
            return carry

        lax.fori_loop(low // BLOCK, high // BLOCK, step, 0)


def slab_update(scalars, grams, parts, grads, begin, end, earlier):
    total, count, _ = grads.shape
    wide = total * TILE
    return call(
        functools.partial(update_body, begin, end, len(parts)),
        "slab_update",
        flops=4 * wide * wide * LANES * (count // TILE),
        moved=6 * grads.size,
        in_specs=[IN_VMEM] * len(parts)
        + [IN_VMEM, IN_VMEM, IN_HBM]
        + [IN_HBM] * len(earlier),
        out_specs=IN_VMEM,
        out_shape=jax.ShapeDtypeStruct(grads.shape, BF16),
        scratch_shapes=[
            pltpu.VMEM(grads.shape, BF16),
            pltpu.VMEM((wide, wide), BF16),
            pltpu.VMEM((wide, LANES), F32),
            pltpu.SemaphoreType.DMA,
        ],
    )(*parts, scalars, grams, grads, *earlier)


def plain_update(spread, anneal, step_size, states, grads):
    total, lines, _ = grads.shape
    flat = states[:, :lines].reshape(total, -1)
    gram = lax.dot_general(flat, flat, (((1,), (1,)), ((), ())), preferred_element_type=F32)
    gram = lax.psum(gram, "slab")
    norms = jnp.diagonal(gram)
    kernel = jnp.exp(-(norms[:, None] + norms[None, :] - 2.0 * gram) / (spread[0] * NCELL)).astype(BF16)
    ksum = jnp.sum(kernel.astype(F32), axis=1)
    drive = jnp.dot(kernel, grads.reshape(total, -1), preferred_element_type=F32)
    pulled = jnp.dot(kernel, flat, preferred_element_type=F32)
    values = flat.astype(F32)
    repel = values * ksum[:, None] - pulled
    coeff = 2.0 * anneal[0] / spread[0]
    new = values + step_size[0] / total * (drive + coeff * repel)
    return new.astype(BF16).reshape(grads.shape)


def swap(slabs):
    return lax.all_to_all(slabs, "slab", split_axis=0, concat_axis=0, tiled=True)


def device_at(at, half):
    me = lax.axis_index("slab").astype(jnp.int32)
    return jnp.where(at < half, me - me % half + at, me ^ at)


def lines_of(start, count):
    return pl.ds(pl.multiple_of(start, TILE), count)


def split_pieces_body(positions, half, raw, lines, gates, row_ref, *refs):
    refs = refs[gates:]
    count = len(positions)
    out_refs, helds, sems = refs[: -count - 1], refs[-count - 1 : -1], refs[-1]
    cells = lines * LANES
    end = row_ref.shape[1]
    copies = []
    for at, held in zip(positions, helds):
        mine = []

        def fetch(start, size, to):
            source = row_ref.at[:, pl.ds(pl.multiple_of(start, GRID_Y), size)]
            sem = sems.at[len(copies) * 5 + len(mine)]
            mine.append(pltpu.make_async_copy(source, held.at[:, pl.ds(to, size)], sem))
            mine[-1].start()

        slab = device_at(at, half)
        fetch(slab * cells, cells, 0)
        fetch(jnp.minimum((slab + 1) * cells, end - GRID_Y), GRID_Y, cells)
        fetch(jnp.maximum(slab * cells - GRID_Y, 0), GRID_Y, cells + GRID_Y)
        if raw and at < half:
            other = slab ^ half
            fetch(other * cells, raw * LANES + GRID_Y, cells + 2 * GRID_Y)
            fetch(jnp.maximum(other * cells - GRID_Y, 0), GRID_Y, cells + 3 * GRID_Y + raw * LANES)
        copies.append(mine)

    def grid_row(held, at):
        return held[:, pl.ds(at, GRID_Y)].astype(F32).reshape(LINE, LANES)

    for n, (at, held, mine) in enumerate(zip(positions, helds, copies)):
        out_ref = out_refs[n] if at >= half else out_refs[0].at[n]
        for copy in mine:
            copy.wait()
        slab = device_at(at, half)
        out_ref[:lines, :] = held[:, :cells].reshape(lines, LANES)
        below = jnp.where(slab == end // cells - 1, 0.0, grid_row(held, cells))
        above = jnp.where(slab == 0, 0.0, grid_row(held, cells + GRID_Y))
        out_ref[lines : lines + TILE, :] = jnp.concatenate([below, above], axis=0).astype(BF16)
        if raw and at < half:
            start = cells + 2 * GRID_Y
            to = lines + TILE
            out_ref[to : to + raw, :] = held[:, start : start + raw * LANES].reshape(raw, LANES)
            below = grid_row(held, start + raw * LANES)
            above = jnp.where(slab ^ half == 0, 0.0, grid_row(held, start + raw * LANES + GRID_Y))
            out_ref[to + raw :, :] = jnp.concatenate([below, above], axis=0).astype(BF16)


def split_pieces(row, slabs, raw, near, gates):
    lines = row.shape[1] // slabs // LANES
    half = slabs // 2
    count = half
    size = lines + TILE + (raw + TILE if near and raw else 0)
    if near:
        out_shape = [jax.ShapeDtypeStruct((count, size, LANES), BF16)]
    else:
        out_shape = [jax.ShapeDtypeStruct((size, LANES), BF16)] * count
    positions = range(half) if near else range(half, slabs)
    return call(
        functools.partial(split_pieces_body, positions, half, raw, lines, len(gates)),
        "split_pieces",
        moved=6 * count * size * LANES,
        in_specs=[IN_HBM] + [IN_VMEM] * len(gates),
        out_specs=[IN_VMEM] * len(out_shape),
        out_shape=out_shape,
        scratch_shapes=[pltpu.VMEM((1, (size + TILE) * LANES), BF16)] * count + [pltpu.SemaphoreType.DMA((5 * count,))],
    )(row, *gates)


def join_pieces_body(positions, half, raw, lines, begun, *refs):
    count = len(positions)
    pieces, row_ref, helds, sems = refs[begun : -count - 2], refs[-count - 2], refs[-count - 1 : -1], refs[-1]
    cells = lines * LANES
    skip = raw * LANES
    copies = []
    for n, (at, held) in enumerate(zip(positions, helds)):
        piece = pieces[n][...] if at >= half else pieces[0][n]
        held[...] = piece.reshape(held.shape)

        def store(begin, size, start):
            target = row_ref.at[:, pl.ds(pl.multiple_of(start, GRID_Y), size)]
            copies.append(pltpu.make_async_copy(held.at[:, pl.ds(begin, size)], target, sems.at[len(copies)]))
            copies[-1].start()

        slab = device_at(at, half)
        if at >= half:
            store(0, cells - skip, slab * cells + skip)
        else:
            store(0, cells, slab * cells)
            if raw:
                store(cells, skip, (slab ^ half) * cells)
    for copy in copies:
        copy.wait()


def join_pieces(row, slabs, raw, pieces, positions):
    cells = NCELL // slabs
    size = pieces[0].shape[-2] * LANES
    begun = [] if row is None else [row]
    return call(
        functools.partial(join_pieces_body, positions, slabs // 2, raw, cells // LANES, len(begun)),
        "join_pieces",
        moved=6 * size * len(positions),
        in_specs=[IN_HBM] * len(begun) + [IN_VMEM] * len(pieces),
        out_specs=IN_HBM,
        out_shape=jax.ShapeDtypeStruct((1, NCELL), BF16),
        input_output_aliases={0: 0} if begun else {},
        scratch_shapes=[pltpu.VMEM((1, size), BF16)] * len(positions)
        + [pltpu.SemaphoreType.DMA((2 * len(positions),))],
    )(*begun, *pieces)


def reorder(gram, back):
    total = gram.shape[0]
    row = lax.broadcasted_iota(jnp.int32, (total, total), 0)
    col = lax.broadcasted_iota(jnp.int32, (total, total), 1)
    left = (col == device_at(row, total // 2) if back else row == device_at(col, total // 2)).astype(F32)
    right = (row == device_at(col, total // 2) if back else col == device_at(row, total // 2)).astype(F32)
    exact = {"precision": lax.Precision.HIGHEST, "preferred_element_type": F32}
    return jnp.dot(jnp.dot(left, gram, **exact), right, **exact)


def gram_pieces_body(lines, total, near_ref, *refs):
    half = total // 2
    pieces, out_ref, pairs = refs[:half], refs[-2], refs[-1]
    wide = total * TILE
    tiles = 4
    pairs[...] = jnp.zeros_like(pairs)

    def step(i, carry):
        parts = []
        for t in range(tiles):
            at = lines_of((i * tiles + t) * TILE, TILE)
            near = near_ref[:, at, :].reshape(wide // 2, LANES)
            parts.append(jnp.concatenate([near] + [piece[at, :] for piece in pieces], axis=0))
        block = jnp.concatenate(parts, axis=1)
        pairs[...] += lax.dot_general(block, block, (((1,), (1,)), ((), ())), preferred_element_type=F32)
        return carry

    lax.fori_loop(0, lines // TILE // tiles, step, 0)
    equal = jnp.where(same_line(total), pairs[...], 0.0)
    rows = jnp.sum(equal.reshape(total, TILE, wide), axis=1)
    gram = jnp.dot(rows, members(total, F32), precision=lax.Precision.HIGHEST, preferred_element_type=F32)
    gram = jnp.concatenate([reorder(gram, False), jnp.zeros((total, LANES - total), F32)], axis=1)
    out_ref[...] = jnp.broadcast_to(gram[None], out_ref.shape)


def gram_pieces(near, far, lines, gates):
    total = 2 * len(far)
    wide = total * TILE
    return call(
        functools.partial(gram_pieces_body, lines, total),
        "gram_pieces",
        flops=2 * wide * wide * LANES * (lines // TILE),
        moved=2 * total * lines * LANES,
        in_specs=[IN_VMEM] * (1 + len(far)) + [IN_HBM] * len(gates),
        out_specs=IN_VMEM,
        out_shape=jax.ShapeDtypeStruct((total, total, LANES), F32),
        scratch_shapes=[pltpu.VMEM((wide, wide), F32)],
    )(near, *far, *gates)


def gradient_pieces_body(k, lines, count, views, arrays, numbers, *refs):
    observed_ref, precision_ref, *number_refs = refs[arrays : arrays + 2 + numbers]
    out_ref, rows_ref, observed, precision, grads, sems = refs[-6:]
    for n, number_ref in enumerate(number_refs):
        rows_ref[n : n + 1, :] = jnp.full((1, LANES), number_ref[0], F32)
    rows = BLOCK // LINE
    shape = (rows, LINE, LANES)
    lane = lax.broadcasted_iota(jnp.int32, (1, LINE, LANES), 2)
    line = lax.broadcasted_iota(jnp.int32, (1, LINE, LANES), 1)
    steps = count // BLOCK
    mine = lines_of((lax.axis_index("slab").astype(jnp.int32) ^ k) * lines, count)
    fetches = [
        pltpu.make_async_copy(observed_ref.at[mine, :], observed, sems.at[steps]),
        pltpu.make_async_copy(precision_ref.at[mine, :], precision, sems.at[steps + 1]),
    ]
    for fetch in fetches:
        fetch.start()
    for fetch in fetches:
        fetch.wait()

    def store(i):
        at = lines_of(i * BLOCK, BLOCK)
        return pltpu.make_async_copy(grads.at[:, at, :], out_ref.at[:, at, :], sems.at[i])

    def step(i, carry):
        start = i * BLOCK
        at = lines_of(start, BLOCK)
        obs = observed[at, :].astype(F32).reshape(shape)
        prec = precision[at, :].astype(F32).reshape(shape)
        for p, (array, lead, base) in enumerate(views):

            def load(begin, size):
                part = lines_of(base + begin, size)
                value = refs[array][part, :] if lead is None else refs[array][lead, part, :]
                return value.astype(F32)

            here = load(start, BLOCK)
            before = load(jnp.where(i == 0, count, start - TILE), TILE)
            after = load(start + BLOCK, TILE)
            above = jnp.concatenate([before[LINE:], here[:-LINE]], axis=0).reshape(shape)
            below = jnp.concatenate([here[LINE:], after[:LINE]], axis=0).reshape(shape)
            field = here.reshape(shape)
            turned = pltpu.roll(field, 1, 2)
            carried = jnp.where(line == 0, 0.0, pltpu.roll(turned, 1, 1))
            left = jnp.where(lane == 0, carried, turned)
            turned = pltpu.roll(field, LANES - 1, 2)
            carried = jnp.where(line == LINE - 1, 0.0, pltpu.roll(turned, LINE - 1, 1))
            right = jnp.where(lane == LANES - 1, carried, turned)
            laplace = (4.0 + mass_term) * field - (below + above + right + left)
            squash = jnp.tanh(field)
            result = prec * (obs - squash) * (1.0 - squash * squash) - prior_scale * laplace
            grads[p, at, :] = result.reshape(BLOCK, LANES).astype(BF16)
        store(i).start()
        return carry

    def finish(i, carry):
        store(i).wait()
        return carry

    lax.fori_loop(0, steps, step, 0)
    lax.fori_loop(0, steps, finish, 0)


def gradient_pieces(arrays, views, observed, precision, lines, count, k, numbers):
    out = pltpu.HBM((len(views), count, LANES), BF16)
    size = len(views) * count * LANES
    return call(
        functools.partial(gradient_pieces_body, k, lines, count, views, len(arrays), len(numbers)),
        "gradient_pieces",
        flops=30 * size,
        moved=8 * size,
        in_specs=[IN_VMEM] * len(arrays)
        + [IN_HBM, IN_HBM]
        + [pl.BlockSpec(memory_space=pltpu.SMEM)] * len(numbers),
        out_specs=[IN_HBM, IN_VMEM],
        out_shape=[out, jax.ShapeDtypeStruct((8, LANES), F32)],
        scratch_shapes=[
            pltpu.VMEM((count, LANES), BF16),
            pltpu.VMEM((count, LANES), BF16),
            pltpu.VMEM(out.shape, BF16),
            pltpu.SemaphoreType.DMA((count // BLOCK + 2,)),
        ],
    )(*arrays, observed, precision, *numbers)


def raw_body(raw, lines, near_ref, out_ref):
    for k in range(near_ref.shape[0]):
        out_ref[k, :raw, :] = near_ref[k, :raw, :]
        below = near_ref[k, raw : raw + TILE, :].astype(F32)[:LINE]
        above = near_ref[k, lines : lines + TILE, :].astype(F32)[LINE:]
        out_ref[k, raw:, :] = jnp.concatenate([below, above], axis=0).astype(BF16)


def raw_states(near, raw, lines):
    out = jax.ShapeDtypeStruct((near.shape[0], raw + TILE, LANES), BF16)
    return call(
        functools.partial(raw_body, raw, lines),
        "raw_states",
        moved=4 * out.size,
        in_specs=[IN_VMEM],
        out_specs=IN_VMEM,
        out_shape=out,
    )(near)


def update_pieces_body(near, half, raw, lines, groups, extra, near_ref, *refs):
    total = 2 * half
    far_refs, numbers_ref, grams_ref, refs = refs[:half], refs[half], refs[half + 1], refs[half + 2 :]
    group_refs, refs = refs[: len(groups)], refs[len(groups) :]
    raw_refs, out_refs, (grads, raw_grads, mixer, own, sems) = refs[:extra], refs[extra:-5], refs[-5:]
    wide = total * TILE
    high = half * TILE
    first = 0 if near else high
    fetches = []
    for group, group_ref in zip(groups, group_refs):
        for j, at in enumerate(group):
            fetches.append(pltpu.make_async_copy(group_ref.at[j], grads.at[at], sems.at[len(fetches)]))
    if extra:
        fetches.append(pltpu.make_async_copy(raw_refs[1], raw_grads, sems.at[len(fetches)]))
    for fetch in fetches:
        fetch.start()
    gram = reorder(jnp.sum(grams_ref[...], axis=0)[:, :total], True)
    spread, anneal, step_size = (numbers_ref[k : k + 1, :1] for k in range(3))
    rate = step_size / total
    coeff = 2.0 * anneal / spread
    row = lax.broadcasted_iota(jnp.int32, (total, total), 0)
    col = lax.broadcasted_iota(jnp.int32, (total, total), 1)
    diagonal = jnp.where(row == col, gram, 0.0)
    down = jnp.sum(diagonal, axis=1, keepdims=True)
    across = jnp.sum(diagonal, axis=0, keepdims=True)
    kernel = jnp.exp(-(down + across - 2.0 * gram) / (spread * NCELL)).astype(BF16)
    ksum = jnp.sum(kernel.astype(F32), axis=1, keepdims=True)
    member = members(total, BF16)
    half_way = jnp.dot(member, kernel, preferred_element_type=F32).astype(BF16)
    full = lax.dot_general(half_way, member, (((1,), (1,)), ((), ())), preferred_element_type=F32)
    full = jnp.where(same_line(total), full, 0.0)
    gain = jnp.broadcast_to((1.0 + rate * coeff * ksum)[:, :, None], (total, TILE, LANES)).reshape(wide, LANES)
    mixer[...] = full[first : first + high].astype(BF16)
    own[...] = gain[first : first + high]
    for fetch in fetches:
        fetch.wait()

    def mix(states, slopes):
        both = jnp.concatenate([slopes, states], axis=1)
        mixed = jnp.dot(mixer[...], both, preferred_element_type=F32)
        drive, pulled = mixed[:, :LANES], mixed[:, LANES:]
        kept = states[first : first + high].astype(F32)
        return (kept * own[...] + rate * (drive - coeff * pulled)).astype(BF16)

    def put(to, new):
        if near:
            out_refs[0][:, lines_of(to, TILE), :] = new.reshape(half, TILE, LANES)
        else:
            for j, out_ref in enumerate(out_refs):
                out_ref[lines_of(to, TILE), :] = new[j * TILE : (j + 1) * TILE]

    def slab_step(i, carry):
        for t in range(BLOCK // TILE):
            at = i * BLOCK + t * TILE
            states = [near_ref[:, lines_of(at, TILE), :].reshape(high, LANES)]
            states += [ref[lines_of(at, TILE), :] for ref in far_refs]
            slopes = grads[:, lines_of(at, TILE), :].reshape(wide, LANES)
            put(at if near else at - raw, mix(jnp.concatenate(states, axis=0), slopes))
        return carry

    def raw_step(i, carry):
        here = lax.axis_index("slab").astype(jnp.int32) % half
        for t in range(BLOCK // TILE):
            at = i * BLOCK + t * TILE
            part = lines_of(at, TILE)
            states = [near_ref[:, lines_of(lines + TILE + at, TILE), :].reshape(high, LANES)]
            slopes = [raw_grads[:half, part, :].reshape(high, LANES)]
            for x in range(half):
                states += [raw_refs[0][here ^ x, part, :]]
                slopes += [raw_grads[half + (here ^ x), part, :]]
            put(lines + at, mix(jnp.concatenate(states, axis=0), jnp.concatenate(slopes, axis=0)))
        return carry

    lax.fori_loop(0 if near else raw // BLOCK, lines // BLOCK, slab_step, 0)
    if near and raw:
        lax.fori_loop(0, raw // BLOCK, raw_step, 0)


def update_pieces(numbers, grams, near_states, far_states, grads, groups, raw_parts, raw, lines, near):
    half = len(far_states)
    total = 2 * half
    wide = total * TILE
    if near:
        out_shape = [jax.ShapeDtypeStruct((half, lines + raw, LANES), BF16)]
    else:
        out_shape = [jax.ShapeDtypeStruct((lines - raw, LANES), BF16)] * half
    return call(
        functools.partial(update_pieces_body, near, half, raw, lines, groups, len(raw_parts)),
        "update_pieces",
        flops=4 * half * TILE * wide * LANES * (lines // TILE),
        moved=2 * (2 * total + half) * lines * LANES,
        in_specs=[IN_VMEM] * (half + 3) + [IN_HBM] * len(groups) + [IN_VMEM, IN_HBM][: len(raw_parts)],
        out_specs=[IN_VMEM] * len(out_shape),
        out_shape=out_shape,
        scratch_shapes=[
            pltpu.VMEM((total, lines, LANES), BF16),
            pltpu.VMEM((total, max(raw, TILE), LANES), BF16),
            pltpu.VMEM((half * TILE, wide), BF16),
            pltpu.VMEM((half * TILE, LANES), F32),
            pltpu.SemaphoreType.DMA((total + 1,)),
        ],
    )(near_states, *far_states, numbers, grams, *grads, *raw_parts)


def exchange(piece, k, slabs):
    return lax.ppermute(piece, "slab", [(i, i ^ k) for i in range(slabs)])


def swap_near(pieces, slabs):
    groups = [list(range(slabs // 2)), list(range(slabs // 2, slabs))]
    return lax.all_to_all(pieces, "slab", 0, 0, axis_index_groups=groups, tiled=True)


RAW = 0
GRADIENTS = ((8, 9, 10, 11), (0, 1, 2, 3), (4, 5, 6, 7), (12, 13), (14, 15))
JOINS = ((0, 1, 2, 3, 4, 5, 6, 7), (8, 9, 10, 11), (12, 13), (14, 15))


def by_halves(particles, observed, precision, spread, anneal, step_size):
    slabs = lax.axis_size("slab")
    half = slabs // 2
    lines = NCELL // slabs // LANES
    row = in_hbm(particles)
    obs = in_hbm(observed.reshape(-1, LANES))
    prec = in_hbm(precision.reshape(-1, LANES))
    far = split_pieces(row, slabs, RAW, False, [])
    near = split_pieces(row, slabs, RAW, True, far[:1])[0]
    near = swap_near(near, slabs)
    far = [exchange(piece, half + x, slabs) for x, piece in enumerate(far)]
    extra = []
    if RAW:
        extra = [exchange(raw_states(near, RAW, lines), half, slabs)]
    grads = []
    numbers = [spread, anneal, step_size]
    for group in GRADIENTS:
        if group[0] < half:
            arrays, views = [near], [(0, k, 0) for k in group]
        else:
            arrays, views = [far[k - half] for k in group], [(j, None, 0) for j in range(len(group))]
        slopes, rows = gradient_pieces(arrays, tuple(views), obs, prec, lines, lines, 0, [] if grads else numbers)
        grads.append(in_hbm(slopes))
        numbers = numbers if len(grads) > 1 else rows
    grams = swap(gram_pieces(near, far, lines, grads[:-1]))
    if RAW:
        views = [(0, k, lines + TILE) for k in range(half)] + [(1, k, 0) for k in range(half)]
        slopes, _ = gradient_pieces([near] + extra, tuple(views), obs, prec, lines, RAW, half, [])
        extra += [in_hbm(slopes)]
    new_far = update_pieces(numbers, grams, near, far, grads, GRADIENTS, [], RAW, lines, False)
    new_near = update_pieces(numbers, grams, near, far, grads, GRADIENTS, extra, RAW, lines, True)[0]
    new_near = swap_near(new_near, slabs)
    new_far = [exchange(piece, half + x, slabs) for x, piece in enumerate(new_far)]
    row = None
    for group in JOINS:
        pieces = [new_near] if group[0] < half else [new_far[k - half] for k in group]
        row = join_pieces(row, slabs, RAW, pieces, group)
    return row


def on_device(particles, observed, precision, spread, anneal, step_size):
    slabs = lax.axis_size("slab")
    total = particles.shape[0] * slabs
    lines = NCELL // slabs // LANES
    if slabs == 16:
        return by_halves(particles, observed, precision, spread, anneal, step_size)
    sent, begun = cuts(lines)
    fields = [observed.reshape(-1, LANES), precision.reshape(-1, LANES)]
    numbers = [spread, anneal, step_size]
    first, obs, prec, scalars = split_row(particles, slabs, 0, sent, True, fields, numbers, [])
    parts = [swap(first)]
    if sent < lines:
        parts += [swap(split_row(particles, slabs, sent, lines, False, [], [], [scalars])[0])]
    if total * TILE > 256:
        grads = slab_gradient(parts, obs, prec, lines, 0, lines)
        states = jnp.concatenate([parts[0][:, :sent]] + parts[1:], axis=1)
        new = plain_update(spread, anneal, step_size, states, grads)
        return join_row(swap(new), lines, 0, None)
    if sent == lines:
        grads = slab_gradient(parts, obs, prec, lines, 0, lines)
        grams = swap(slab_gram(parts[0], lines, slabs, [], []))
        new = slab_update(scalars, grams, parts, grads, 0, lines, [])
        return join_row(swap(new), lines, 0, None)
    gram = slab_gram(parts[0], sent, 1, [], [])
    early = slab_gradient(parts[:1], obs, prec, lines, 0, begun)
    grams = swap(slab_gram(parts[1], lines - sent, slabs, [gram], [early]))
    late = slab_gradient(parts, obs, prec, lines, begun, lines)
    new = slab_update(scalars, grams, parts[:1], early, 0, begun, [])
    rest = slab_update(scalars, grams, parts, late, begun, lines, [new])
    row = join_row(swap(new), lines, 0, None)
    return join_row(swap(rest), lines, begun, row)


def solution(mesh):
    in_specs = (
        P(("groups", "slab"), None),
        P("groups"),
        P("groups"),
        P("groups"),
        P("groups"),
        P("groups"),
    )
    out_specs = P(("groups", "slab"), None)
    return jax.shard_map(
        on_device, mesh=mesh, in_specs=in_specs, out_specs=out_specs, check_vma=False
    )
```

```python
import functools

import jax
import jax.numpy as jnp
from jax import lax
from jax.experimental import pallas as pl
from jax.experimental.pallas import tpu as pltpu
from jax.sharding import PartitionSpec as P

GRID_X = 1024
GRID_Y = 1024
NCELL = 1048576
LANES = 128
LINE = GRID_Y // LANES
TILE = 16

prior_scale = 0.25
mass_term = 1.0

F32 = jnp.float32
BF16 = jnp.bfloat16
MIB = 1024 * 1024


def call(body, name, flops=0, moved=0, limit=16, **kwargs):
    return pl.pallas_call(
        body,
        name=name,
        compiler_params=pltpu.CompilerParams(vmem_limit_bytes=limit * MIB),
        cost_estimate=pl.CostEstimate(flops=flops, bytes_accessed=moved, transcendentals=0),
        **kwargs,
    )


IN_VMEM = pl.BlockSpec(memory_space=pltpu.VMEM)
IN_HBM = pl.BlockSpec(memory_space=pltpu.HBM)


def in_hbm(array):
    return pltpu.with_memory_space_constraint(array, pltpu.HBM)


BLOCK = 4 * TILE


def cuts(lines):
    if lines % (8 * BLOCK):
        return lines, lines
    return lines * 3 // 4, lines * 3 // 4 - BLOCK


def split_body(lines, begin, rim, fields, numbers, row_ref, *refs):
    field_refs, number_refs = refs[:fields], refs[fields : fields + numbers]
    out_ref, *slab_refs, rows_ref = refs[-7 - fields : -5]
    held, edges, sems, edge_sems, field_sems = refs[-5:]
    for k, number_ref in enumerate(number_refs):
        rows_ref[k : k + 1, :] = jnp.broadcast_to(number_ref[...].reshape(1, 1), (1, LANES))
    slabs, count, _ = out_ref.shape
    count -= TILE * rim
    size = count * LANES
    cells = lines * LANES

    def part(slab):
        source = row_ref.at[:, pl.ds(slab * cells + begin * LANES, size)]
        return pltpu.make_async_copy(source, held.at[:, pl.ds(slab * size, size)], sems.at[slab])

    def edge(slab):
        source = row_ref.at[:, pl.ds(slab * cells - GRID_Y, GRID_Y)]
        return pltpu.make_async_copy(source, edges.at[:, pl.ds(slab * GRID_Y, GRID_Y)], edge_sems.at[slab])

    def grid_row(ref, start):
        return ref[:, pl.ds(start, GRID_Y)].astype(F32).reshape(LINE, LANES)

    for slab in range(slabs):
        part(slab).start()
        if rim and slab:
            edge(slab).start()
    mine = pl.ds(pl.multiple_of(lax.axis_index("slab") * lines, TILE), lines)
    fetches = [
        pltpu.make_async_copy(source.at[mine, :], target, field_sems.at[k])
        for k, (source, target) in enumerate(zip(field_refs, slab_refs))
    ]
    for fetch in fetches:
        fetch.start()
    part(0).wait()
    outside = jnp.zeros((LINE, LANES), F32)
    for slab in range(slabs):
        if slab + 1 < slabs:
            part(slab + 1).wait()
        out_ref[slab, :count, :] = held[:, pl.ds(slab * size, size)].reshape(count, LANES)
        if rim:
            if slab:
                edge(slab).wait()
            below = grid_row(held, (slab + 1) * size) if slab + 1 < slabs else outside
            above = grid_row(edges, slab * GRID_Y) if slab else outside
            out_ref[slab, count:, :] = jnp.concatenate([below, above], axis=0).astype(BF16)
    for fetch in fetches:
        fetch.wait()


def split_row(row, slabs, begin, end, rim, fields, numbers, earlier):
    lines = row.shape[1] // slabs // LANES
    count = end - begin
    return call(
        functools.partial(split_body, lines, begin, rim, len(fields), len(numbers)),
        "split_row",
        moved=6 * slabs * count * LANES,
        in_specs=[IN_HBM] * (1 + len(fields)) + [IN_VMEM] * len(numbers) + [IN_HBM] * len(earlier),
        out_specs=[IN_VMEM] * (2 + len(fields)),
        out_shape=[jax.ShapeDtypeStruct((slabs, count + TILE * rim, LANES), BF16)]
        + [jax.ShapeDtypeStruct((lines, LANES), BF16)] * len(fields)
        + [jax.ShapeDtypeStruct((8, LANES), F32)],
        scratch_shapes=[
            pltpu.VMEM((1, slabs * count * LANES), BF16),
            pltpu.VMEM((1, slabs * GRID_Y), BF16),
            pltpu.SemaphoreType.DMA((slabs,)),
            pltpu.SemaphoreType.DMA((slabs,)),
            pltpu.SemaphoreType.DMA((2,)),
        ],
    )(row, *fields, *numbers, *earlier)


def join_body(lines, begin, slabs_ref, *refs):
    row_ref, held, sems = refs[-3:]
    slabs, count, _ = slabs_ref.shape
    size = count * LANES
    copies = []
    for slab in range(slabs):
        at = pl.ds(slab * size, size)
        held[:, at] = slabs_ref[slab].reshape(1, size)
        target = row_ref.at[:, pl.ds((slab * lines + begin) * LANES, size)]
        copies.append(pltpu.make_async_copy(held.at[:, at], target, sems.at[slab]))
        copies[-1].start()
    for copy in copies:
        copy.wait()


def join_row(slabs, lines, begin, row):
    total, count, _ = slabs.shape
    begun = [] if row is None else [row]
    return call(
        functools.partial(join_body, lines, begin),
        "join_row",
        moved=6 * slabs.size,
        in_specs=[IN_VMEM] + [IN_HBM] * len(begun),
        out_specs=IN_HBM,
        out_shape=jax.ShapeDtypeStruct((1, total * lines * LANES), BF16),
        input_output_aliases={1: 0} if begun else {},
        scratch_shapes=[pltpu.VMEM((1, slabs.size), BF16), pltpu.SemaphoreType.DMA((total,))],
    )(slabs, *begun)


def same_line(total):
    wide = total * TILE
    row = lax.broadcasted_iota(jnp.int32, (wide, wide), 0)
    col = lax.broadcasted_iota(jnp.int32, (wide, wide), 1)
    return row % TILE == col % TILE


def members(total, dtype):
    wide = total * TILE
    row = lax.broadcasted_iota(jnp.int32, (wide, total), 0)
    col = lax.broadcasted_iota(jnp.int32, (wide, total), 1)
    return (row // TILE == col).astype(dtype)


def gram_body(steps, tiles, parts, states_ref, *refs):
    out_ref, pairs = refs[-2:]
    total = states_ref.shape[0]
    wide = total * TILE
    pairs[...] = jnp.zeros_like(pairs)

    def step(i, carry):
        parts = [
            states_ref[:, pl.ds(pl.multiple_of((i * tiles + t) * TILE, TILE), TILE), :].reshape(wide, LANES)
            for t in range(tiles)
        ]
        block = jnp.concatenate(parts, axis=1)
        pairs[...] += lax.dot_general(block, block, (((1,), (1,)), ((), ())), preferred_element_type=F32)
        return carry

    lax.fori_loop(0, steps, step, 0)
    equal = jnp.where(same_line(total), pairs[...], 0.0)
    rows = jnp.sum(equal.reshape(total, TILE, wide), axis=1)
    gram = jnp.dot(rows, members(total, F32), precision=lax.Precision.HIGHEST, preferred_element_type=F32)
    gram = jnp.concatenate([gram, jnp.zeros((total, LANES - total), F32)], axis=1)
    for part_ref in refs[:parts]:
        gram += part_ref[0]
    out_ref[...] = jnp.broadcast_to(gram[None], out_ref.shape)


def slab_gram(states, lines, copies, parts, earlier):
    total = states.shape[0]
    wide = total * TILE
    tiles = min(8, lines // TILE)
    return call(
        functools.partial(gram_body, lines // TILE // tiles, tiles, len(parts)),
        "slab_gram",
        flops=2 * wide * wide * LANES * (lines // TILE),
        moved=2 * states.size,
        in_specs=[IN_VMEM] * (1 + len(parts)) + [IN_HBM] * len(earlier),
        out_specs=IN_VMEM,
        out_shape=jax.ShapeDtypeStruct((copies, total, LANES), F32),
        scratch_shapes=[pltpu.VMEM((wide, wide), F32)],
    )(states, *parts, *earlier)


def gradient_body(lines, begin, end, parts, *refs):
    observed, precision, out_ref, grads, sems = refs[parts:]
    total = grads.shape[0]
    first = refs[0].shape[1] - TILE
    rows = BLOCK // LINE
    group = 4
    shape = (rows, LINE, LANES)
    lane = lax.broadcasted_iota(jnp.int32, (1, LINE, LANES), 2)
    line = lax.broadcasted_iota(jnp.int32, (1, LINE, LANES), 1)

    def load(particle, at, count):
        ref, at = (refs[0], at) if at < first else (refs[1], at - first)
        return ref[particle, at : at + count, :].astype(F32)

    def rim(particle):
        return refs[0][particle, first:, :].astype(F32)

    stores = []
    for k, at in enumerate(range(begin, end, BLOCK)):
        mine = slice(at - begin, at - begin + BLOCK)
        obs = observed[at : at + BLOCK, :].astype(F32).reshape(shape)
        prec = precision[at : at + BLOCK, :].astype(F32).reshape(shape)

        def step(i, carry):
            for p in range(group):
                particle = i * group + p
                here = load(particle, at, BLOCK)
                before = load(particle, at - TILE, TILE) if at else rim(particle)
                after = load(particle, at + BLOCK, TILE) if at + BLOCK < lines else rim(particle)
                above = jnp.concatenate([before[LINE:], here[:-LINE]], axis=0).reshape(shape)
                below = jnp.concatenate([here[LINE:], after[:LINE]], axis=0).reshape(shape)
                field = here.reshape(shape)
                turned = pltpu.roll(field, 1, 2)
                carried = jnp.where(line == 0, 0.0, pltpu.roll(turned, 1, 1))
                left = jnp.where(lane == 0, carried, turned)
                turned = pltpu.roll(field, LANES - 1, 2)
                carried = jnp.where(line == LINE - 1, 0.0, pltpu.roll(turned, LINE - 1, 1))
                right = jnp.where(lane == LANES - 1, carried, turned)
                laplace = (4.0 + mass_term) * field - (below + above + right + left)
                squash = jnp.tanh(field)
                result = prec * (obs - squash) * (1.0 - squash * squash) - prior_scale * laplace
                grads[particle, mine, :] = result.reshape(BLOCK, LANES).astype(BF16)
            return carry

        lax.fori_loop(0, total // group, step, 0)
        stores.append(pltpu.make_async_copy(grads.at[:, mine, :], out_ref.at[:, mine, :], sems.at[k]))
        stores[-1].start()
    for store in stores:
        store.wait()


def slab_gradient(parts, observed, precision, lines, begin, end):
    total = parts[0].shape[0]
    count = end - begin
    out = jax.ShapeDtypeStruct((total, count, LANES), BF16)
    return call(
        functools.partial(gradient_body, lines, begin, end, len(parts)),
        "slab_gradient",
        flops=30 * out.size,
        moved=8 * out.size,
        in_specs=[IN_VMEM] * (len(parts) + 2),
        out_specs=IN_HBM,
        out_shape=out,
        scratch_shapes=[pltpu.VMEM(out.shape, BF16), pltpu.SemaphoreType.DMA((count // BLOCK,))],
    )(*parts, observed, precision)


def update_body(begin, end, parts, *refs):
    states_refs, refs = refs[:parts], refs[parts:]
    scalars_ref, grams_ref, grads_ref = refs[:3]
    out_ref, grads, mixer, own, sem = refs[-5:]
    total = out_ref.shape[0]
    wide = total * TILE
    fetch = pltpu.make_async_copy(grads_ref, grads, sem)
    fetch.start()
    gram = jnp.sum(grams_ref[...], axis=0)[:, :total]
    row = lax.broadcasted_iota(jnp.int32, (total, total), 0)
    col = lax.broadcasted_iota(jnp.int32, (total, total), 1)
    diagonal = jnp.where(row == col, gram, 0.0)
    down = jnp.sum(diagonal, axis=1, keepdims=True)
    across = jnp.sum(diagonal, axis=0, keepdims=True)
    member = members(total, BF16)
    spread, anneal, step_size = (scalars_ref[k : k + 1, :1] for k in range(3))
    rate = step_size / total
    coeff = 2.0 * anneal / spread
    kernel = jnp.exp(-(down + across - 2.0 * gram) / (spread * NCELL)).astype(BF16)
    ksum = jnp.sum(kernel.astype(F32), axis=1, keepdims=True)
    half = jnp.dot(member, kernel, preferred_element_type=F32).astype(BF16)
    full = lax.dot_general(half, member, (((1,), (1,)), ((), ())), preferred_element_type=F32)
    mixer[...] = jnp.where(same_line(total), full, 0.0).astype(BF16)
    gain = 1.0 + rate * coeff * ksum
    own[...] = jnp.broadcast_to(gain[:, :, None], (total, TILE, LANES)).reshape(wide, LANES)
    fetch.wait()

    done = 0
    for part, states_ref in enumerate(states_refs):
        have = states_ref.shape[1] - (0 if part else TILE)
        low = max(begin - done, 0)
        high = min(end - done, have)
        into = done - begin
        done += have

        def step(i, carry):
            for t in range(BLOCK // TILE):
                at = pl.multiple_of(i * BLOCK + t * TILE, TILE)
                there = pl.ds(pl.multiple_of(at + into, TILE), TILE)
                states = states_ref[:, pl.ds(at, TILE), :].reshape(wide, LANES)
                both = jnp.concatenate([grads[:, there, :].reshape(wide, LANES), states], axis=1)
                mixed = jnp.dot(mixer[...], both, preferred_element_type=F32)
                drive, pulled = mixed[:, :LANES], mixed[:, LANES:]
                new = states.astype(F32) * own[...] + rate * (drive - coeff * pulled)
                out_ref[:, there, :] = new.astype(BF16).reshape(total, TILE, LANES)
            return carry

        lax.fori_loop(low // BLOCK, high // BLOCK, step, 0)


def slab_update(scalars, grams, parts, grads, begin, end, earlier):
    total, count, _ = grads.shape
    wide = total * TILE
    return call(
        functools.partial(update_body, begin, end, len(parts)),
        "slab_update",
        flops=4 * wide * wide * LANES * (count // TILE),
        moved=6 * grads.size,
        in_specs=[IN_VMEM] * len(parts)
        + [IN_VMEM, IN_VMEM, IN_HBM]
        + [IN_HBM] * len(earlier),
        out_specs=IN_VMEM,
        out_shape=jax.ShapeDtypeStruct(grads.shape, BF16),
        scratch_shapes=[
            pltpu.VMEM(grads.shape, BF16),
            pltpu.VMEM((wide, wide), BF16),
            pltpu.VMEM((wide, LANES), F32),
            pltpu.SemaphoreType.DMA,
        ],
    )(*parts, scalars, grams, grads, *earlier)


def plain_update(spread, anneal, step_size, states, grads):
    total, lines, _ = grads.shape
    flat = states[:, :lines].reshape(total, -1)
    gram = lax.dot_general(flat, flat, (((1,), (1,)), ((), ())), preferred_element_type=F32)
    gram = lax.psum(gram, "slab")
    norms = jnp.diagonal(gram)
    kernel = jnp.exp(-(norms[:, None] + norms[None, :] - 2.0 * gram) / (spread[0] * NCELL)).astype(BF16)
    ksum = jnp.sum(kernel.astype(F32), axis=1)
    drive = jnp.dot(kernel, grads.reshape(total, -1), preferred_element_type=F32)
    pulled = jnp.dot(kernel, flat, preferred_element_type=F32)
    values = flat.astype(F32)
    repel = values * ksum[:, None] - pulled
    coeff = 2.0 * anneal[0] / spread[0]
    new = values + step_size[0] / total * (drive + coeff * repel)
    return new.astype(BF16).reshape(grads.shape)


def swap(slabs):
    return lax.all_to_all(slabs, "slab", split_axis=0, concat_axis=0, tiled=True)


def device_at(at, half):
    me = lax.axis_index("slab").astype(jnp.int32)
    return jnp.where(at < half, me - me % half + at, me ^ at)


def lines_of(start, count):
    return pl.ds(pl.multiple_of(start, TILE), count)


def split_pieces_body(positions, half, raw, lines, gates, fields, row_ref, *refs):
    field_refs, refs = refs[:fields], refs[fields + gates :]
    count = len(positions)
    out_refs, helds, sems = refs[: -count - 1], refs[-count - 1 : -1], refs[-1]
    me = lax.axis_index("slab").astype(jnp.int32)
    slab_refs = out_refs[len(out_refs) - 2 * fields :]
    fetches = []
    for n, target in enumerate(slab_refs):
        start = (me if n < fields else me ^ half) * lines
        source = field_refs[n % fields].at[lines_of(start, target.shape[0]), :]
        fetches.append(pltpu.make_async_copy(source, target, sems.at[5 * count + n]))
    cells = lines * LANES
    end = row_ref.shape[1]
    copies = []
    for at, held in zip(positions, helds):
        mine = []

        def fetch(start, size, to):
            source = row_ref.at[:, pl.ds(pl.multiple_of(start, GRID_Y), size)]
            sem = sems.at[len(copies) * 5 + len(mine)]
            mine.append(pltpu.make_async_copy(source, held.at[:, pl.ds(to, size)], sem))
            mine[-1].start()

        slab = device_at(at, half)
        fetch(slab * cells, cells, 0)
        fetch(jnp.minimum((slab + 1) * cells, end - GRID_Y), GRID_Y, cells)
        fetch(jnp.maximum(slab * cells - GRID_Y, 0), GRID_Y, cells + GRID_Y)
        if raw and at < half:
            other = slab ^ half
            fetch(other * cells, raw * LANES + GRID_Y, cells + 2 * GRID_Y)
            fetch(jnp.maximum(other * cells - GRID_Y, 0), GRID_Y, cells + 3 * GRID_Y + raw * LANES)
        copies.append(mine)

    def grid_row(held, at):
        return held[:, pl.ds(at, GRID_Y)].astype(F32).reshape(LINE, LANES)

    for fetch in fetches:
        fetch.start()
    for n, (at, held, mine) in enumerate(zip(positions, helds, copies)):
        out_ref = out_refs[n] if at >= half else out_refs[0].at[n]
        for copy in mine:
            copy.wait()
        slab = device_at(at, half)
        out_ref[:lines, :] = held[:, :cells].reshape(lines, LANES)
        below = jnp.where(slab == end // cells - 1, 0.0, grid_row(held, cells))
        above = jnp.where(slab == 0, 0.0, grid_row(held, cells + GRID_Y))
        out_ref[lines : lines + TILE, :] = jnp.concatenate([below, above], axis=0).astype(BF16)
        if raw and at < half:
            start = cells + 2 * GRID_Y
            to = lines + TILE
            out_ref[to : to + raw, :] = held[:, start : start + raw * LANES].reshape(raw, LANES)
            below = grid_row(held, start + raw * LANES)
            above = jnp.where(slab ^ half == 0, 0.0, grid_row(held, start + raw * LANES + GRID_Y))
            out_ref[to + raw :, :] = jnp.concatenate([below, above], axis=0).astype(BF16)
    for fetch in fetches:
        fetch.wait()


def split_pieces(row, slabs, raw, near, gates, fields):
    lines = row.shape[1] // slabs // LANES
    half = slabs // 2
    count = half
    size = lines + TILE + (raw + TILE if near and raw else 0)
    if near:
        out_shape = [jax.ShapeDtypeStruct((count, size, LANES), BF16)]
    else:
        out_shape = [jax.ShapeDtypeStruct((size, LANES), BF16)] * count
    out_shape += [jax.ShapeDtypeStruct((lines, LANES), BF16)] * len(fields)
    out_shape += [jax.ShapeDtypeStruct((max(raw, TILE), LANES), BF16)] * len(fields)
    positions = range(half) if near else range(half, slabs)
    return call(
        functools.partial(split_pieces_body, positions, half, raw, lines, len(gates), len(fields)),
        "split_pieces",
        moved=6 * count * size * LANES,
        in_specs=[IN_HBM] * (1 + len(fields)) + [IN_VMEM] * len(gates),
        out_specs=[IN_VMEM] * len(out_shape),
        out_shape=out_shape,
        scratch_shapes=[pltpu.VMEM((1, (size + TILE) * LANES), BF16)] * count
        + [pltpu.SemaphoreType.DMA((5 * count + 2 * len(fields),))],
    )(row, *fields, *gates)


def join_pieces_body(positions, half, raw, lines, begun, *refs):
    count = len(positions)
    pieces, row_ref, helds, sems = refs[begun : -count - 2], refs[-count - 2], refs[-count - 1 : -1], refs[-1]
    cells = lines * LANES
    skip = raw * LANES
    copies = []
    for n, (at, held) in enumerate(zip(positions, helds)):
        piece = pieces[n][...] if at >= half else pieces[0][n]
        held[...] = piece.reshape(held.shape)

        def store(begin, size, start):
            target = row_ref.at[:, pl.ds(pl.multiple_of(start, GRID_Y), size)]
            copies.append(pltpu.make_async_copy(held.at[:, pl.ds(begin, size)], target, sems.at[len(copies)]))
            copies[-1].start()

        slab = device_at(at, half)
        if at >= half:
            store(0, cells - skip, slab * cells + skip)
        else:
            store(0, cells, slab * cells)
            if raw:
                store(cells, skip, (slab ^ half) * cells)
    for copy in copies:
        copy.wait()


def join_pieces(row, slabs, raw, pieces, positions):
    cells = NCELL // slabs
    size = pieces[0].shape[-2] * LANES
    begun = [] if row is None else [row]
    return call(
        functools.partial(join_pieces_body, positions, slabs // 2, raw, cells // LANES, len(begun)),
        "join_pieces",
        moved=6 * size * len(positions),
        in_specs=[IN_HBM] * len(begun) + [IN_VMEM] * len(pieces),
        out_specs=IN_HBM,
        out_shape=jax.ShapeDtypeStruct((1, NCELL), BF16),
        input_output_aliases={0: 0} if begun else {},
        scratch_shapes=[pltpu.VMEM((1, size), BF16)] * len(positions)
        + [pltpu.SemaphoreType.DMA((2 * len(positions),))],
    )(*begun, *pieces)


def owners(total, dtype):
    wide = total * TILE
    row = lax.broadcasted_iota(jnp.int32, (wide, total), 0)
    col = lax.broadcasted_iota(jnp.int32, (wide, total), 1)
    return (device_at(row // TILE, total // 2) == col).astype(dtype)


def gram_pieces_body(lines, total, near_ref, *refs):
    half = total // 2
    pieces, out_ref, pairs = refs[:half], refs[-2], refs[-1]
    wide = total * TILE
    tiles = 4
    pairs[...] = jnp.zeros_like(pairs)

    def step(i, carry):
        parts = []
        for t in range(tiles):
            at = lines_of((i * tiles + t) * TILE, TILE)
            near = near_ref[:, at, :].reshape(wide // 2, LANES)
            parts.append(jnp.concatenate([near] + [piece[at, :] for piece in pieces], axis=0))
        block = jnp.concatenate(parts, axis=1)
        pairs[...] += lax.dot_general(block, block, (((1,), (1,)), ((), ())), preferred_element_type=F32)
        return carry

    lax.fori_loop(0, lines // TILE // tiles, step, 0)
    equal = jnp.where(same_line(total), pairs[...], 0.0)
    exact = {"precision": lax.Precision.HIGHEST, "preferred_element_type": F32}
    owner = owners(total, F32)
    half_way = jnp.dot(equal, owner, **exact)
    gram = lax.dot_general(owner, half_way, (((0,), (0,)), ((), ())), **exact)
    out_ref[...] = jnp.concatenate([gram, jnp.zeros((total, LANES - total), F32)], axis=1)


def gram_pieces(near, far, lines, gates):
    total = 2 * len(far)
    wide = total * TILE
    return call(
        functools.partial(gram_pieces_body, lines, total),
        "gram_pieces",
        flops=2 * wide * wide * LANES * (lines // TILE),
        moved=2 * total * lines * LANES,
        in_specs=[IN_VMEM] * (1 + len(far)) + [IN_HBM] * len(gates),
        out_specs=IN_VMEM,
        out_shape=jax.ShapeDtypeStruct((total, LANES), F32),
        scratch_shapes=[pltpu.VMEM((wide, wide), F32)],
    )(near, *far, *gates)


def gradient_pieces_body(views, arrays, numbers, *refs):
    observed, precision, *number_refs = refs[arrays : arrays + 2 + numbers]
    out_ref, rows_ref, grads, sems = refs[-4:]
    for n, number_ref in enumerate(number_refs):
        rows_ref[n : n + 1, :] = jnp.full((1, LANES), number_ref[0], F32)
    count = observed.shape[0]
    rows = BLOCK // LINE
    shape = (rows, LINE, LANES)
    lane = lax.broadcasted_iota(jnp.int32, (1, LINE, LANES), 2)
    line = lax.broadcasted_iota(jnp.int32, (1, LINE, LANES), 1)
    steps = count // BLOCK

    def store(i):
        at = lines_of(i * BLOCK, BLOCK)
        return pltpu.make_async_copy(grads.at[:, at, :], out_ref.at[:, at, :], sems.at[i])

    def step(i, carry):
        start = i * BLOCK
        at = lines_of(start, BLOCK)
        obs = observed[at, :].astype(F32).reshape(shape)
        prec = precision[at, :].astype(F32).reshape(shape)
        for p, (array, lead, base) in enumerate(views):

            def load(begin, size):
                part = lines_of(base + begin, size)
                value = refs[array][part, :] if lead is None else refs[array][lead, part, :]
                return value.astype(F32)

            here = load(start, BLOCK)
            before = load(jnp.where(i == 0, count, start - TILE), TILE)
            after = load(start + BLOCK, TILE)
            above = jnp.concatenate([before[LINE:], here[:-LINE]], axis=0).reshape(shape)
            below = jnp.concatenate([here[LINE:], after[:LINE]], axis=0).reshape(shape)
            field = here.reshape(shape)
            turned = pltpu.roll(field, 1, 2)
            carried = jnp.where(line == 0, 0.0, pltpu.roll(turned, 1, 1))
            left = jnp.where(lane == 0, carried, turned)
            turned = pltpu.roll(field, LANES - 1, 2)
            carried = jnp.where(line == LINE - 1, 0.0, pltpu.roll(turned, LINE - 1, 1))
            right = jnp.where(lane == LANES - 1, carried, turned)
            laplace = (4.0 + mass_term) * field - (below + above + right + left)
            squash = jnp.tanh(field)
            result = prec * (obs - squash) * (1.0 - squash * squash) - prior_scale * laplace
            grads[p, at, :] = result.reshape(BLOCK, LANES).astype(BF16)
        store(i).start()
        return carry

    def finish(i, carry):
        store(i).wait()
        return carry

    lax.fori_loop(0, steps, step, 0)
    lax.fori_loop(0, steps, finish, 0)


def gradient_pieces(arrays, views, observed, precision, numbers):
    count = observed.shape[0]
    out = pltpu.HBM((len(views), count, LANES), BF16)
    size = len(views) * count * LANES
    return call(
        functools.partial(gradient_pieces_body, views, len(arrays), len(numbers)),
        "gradient_pieces",
        flops=30 * size,
        moved=8 * size,
        in_specs=[IN_VMEM] * (len(arrays) + 2)
        + [pl.BlockSpec(memory_space=pltpu.SMEM)] * len(numbers),
        out_specs=[IN_HBM, IN_VMEM],
        out_shape=[out, jax.ShapeDtypeStruct((8, LANES), F32)],
        scratch_shapes=[pltpu.VMEM(out.shape, BF16), pltpu.SemaphoreType.DMA((count // BLOCK,))],
    )(*arrays, observed, precision, *numbers)


def raw_body(raw, lines, near_ref, out_ref):
    for k in range(near_ref.shape[0]):
        out_ref[k, :raw, :] = near_ref[k, :raw, :]
        below = near_ref[k, raw : raw + TILE, :].astype(F32)[:LINE]
        above = near_ref[k, lines : lines + TILE, :].astype(F32)[LINE:]
        out_ref[k, raw:, :] = jnp.concatenate([below, above], axis=0).astype(BF16)


def raw_states(near, raw, lines):
    out = jax.ShapeDtypeStruct((near.shape[0], raw + TILE, LANES), BF16)
    return call(
        functools.partial(raw_body, raw, lines),
        "raw_states",
        moved=4 * out.size,
        in_specs=[IN_VMEM],
        out_specs=IN_VMEM,
        out_shape=out,
    )(near)


def update_pieces_body(near, half, raw, lines, groups, extra, gates, near_ref, *refs):
    total = 2 * half
    refs = refs[gates:]
    far_refs, numbers_ref, grams_ref, refs = refs[:half], refs[half], refs[half + 1], refs[half + 2 :]
    group_refs, refs = refs[: len(groups)], refs[len(groups) :]
    raw_refs, out_refs, (grads, raw_grads, mixer, own, sems) = refs[:extra], refs[extra:-5], refs[-5:]
    wide = total * TILE
    high = half * TILE
    first = 0 if near else high
    fetches = []
    for group, group_ref in zip(groups, group_refs):
        for j, at in enumerate(group):
            fetches.append(pltpu.make_async_copy(group_ref.at[j], grads.at[at], sems.at[len(fetches)]))
    if extra:
        fetches.append(pltpu.make_async_copy(raw_refs[1], raw_grads, sems.at[len(fetches)]))
    for fetch in fetches:
        fetch.start()
    gram = jnp.sum(grams_ref[...], axis=0)[:, :total]
    spread, anneal, step_size = (numbers_ref[k : k + 1, :1] for k in range(3))
    rate = step_size / total
    coeff = 2.0 * anneal / spread
    row = lax.broadcasted_iota(jnp.int32, (total, total), 0)
    col = lax.broadcasted_iota(jnp.int32, (total, total), 1)
    diagonal = jnp.where(row == col, gram, 0.0)
    down = jnp.sum(diagonal, axis=1, keepdims=True)
    across = jnp.sum(diagonal, axis=0, keepdims=True)
    kernel = jnp.exp(-(down + across - 2.0 * gram) / (spread * NCELL)).astype(BF16)
    owner = owners(total, BF16)
    half_way = jnp.dot(owner[first : first + high], kernel, preferred_element_type=F32).astype(BF16)
    full = lax.dot_general(half_way, owner, (((1,), (1,)), ((), ())), preferred_element_type=F32)
    full = jnp.where(same_line(total)[first : first + high], full, 0.0)
    mixer[...] = full.astype(BF16)
    ksum = jnp.sum(full, axis=1, keepdims=True)
    own[...] = jnp.broadcast_to(1.0 + rate * coeff * ksum, (high, LANES))
    for fetch in fetches:
        fetch.wait()

    def mix(states, slopes):
        both = jnp.concatenate([slopes, states], axis=1)
        mixed = jnp.dot(mixer[...], both, preferred_element_type=F32)
        drive, pulled = mixed[:, :LANES], mixed[:, LANES:]
        kept = states[first : first + high].astype(F32)
        return (kept * own[...] + rate * (drive - coeff * pulled)).astype(BF16)

    def put(to, new):
        if near:
            out_refs[0][:, lines_of(to, TILE), :] = new.reshape(half, TILE, LANES)
        else:
            for j, out_ref in enumerate(out_refs):
                out_ref[lines_of(to, TILE), :] = new[j * TILE : (j + 1) * TILE]

    def slab_step(i, carry):
        for t in range(BLOCK // TILE):
            at = i * BLOCK + t * TILE
            states = [near_ref[:, lines_of(at, TILE), :].reshape(high, LANES)]
            states += [ref[lines_of(at, TILE), :] for ref in far_refs]
            slopes = grads[:, lines_of(at, TILE), :].reshape(wide, LANES)
            put(at if near else at - raw, mix(jnp.concatenate(states, axis=0), slopes))
        return carry

    def raw_step(i, carry):
        here = lax.axis_index("slab").astype(jnp.int32) % half
        for t in range(BLOCK // TILE):
            at = i * BLOCK + t * TILE
            part = lines_of(at, TILE)
            states = [near_ref[:, lines_of(lines + TILE + at, TILE), :].reshape(high, LANES)]
            slopes = [raw_grads[:half, part, :].reshape(high, LANES)]
            for x in range(half):
                states += [raw_refs[0][here ^ x, part, :]]
                slopes += [raw_grads[half + (here ^ x), part, :]]
            put(lines + at, mix(jnp.concatenate(states, axis=0), jnp.concatenate(slopes, axis=0)))
        return carry

    lax.fori_loop(0 if near else raw // BLOCK, lines // BLOCK, slab_step, 0)
    if near and raw:
        lax.fori_loop(0, raw // BLOCK, raw_step, 0)


def update_pieces(numbers, grams, near_states, far_states, grads, groups, raw_parts, gates, raw, lines, near):
    half = len(far_states)
    total = 2 * half
    wide = total * TILE
    if near:
        out_shape = [jax.ShapeDtypeStruct((half, lines + raw, LANES), BF16)]
    else:
        out_shape = [jax.ShapeDtypeStruct((lines - raw, LANES), BF16)] * half
    return call(
        functools.partial(update_pieces_body, near, half, raw, lines, groups, len(raw_parts), len(gates)),
        "update_pieces",
        flops=4 * half * TILE * wide * LANES * (lines // TILE),
        moved=2 * (2 * total + half) * lines * LANES,
        in_specs=[IN_VMEM] * (half + 3 + len(gates)) + [IN_HBM] * len(groups) + [IN_VMEM, IN_HBM][: len(raw_parts)],
        out_specs=[IN_VMEM] * len(out_shape),
        out_shape=out_shape,
        scratch_shapes=[
            pltpu.VMEM((total, lines, LANES), BF16),
            pltpu.VMEM((total, max(raw, TILE), LANES), BF16),
            pltpu.VMEM((half * TILE, wide), BF16),
            pltpu.VMEM((half * TILE, LANES), F32),
            pltpu.SemaphoreType.DMA((total + 1,)),
        ],
    )(near_states, *gates, *far_states, numbers, grams, *grads, *raw_parts)


def exchange(piece, k, slabs):
    return lax.ppermute(piece, "slab", [(i, i ^ k) for i in range(slabs)])


def swap_near(pieces, slabs):
    groups = [list(range(slabs // 2)), list(range(slabs // 2, slabs))]
    return lax.all_to_all(pieces, "slab", 0, 0, axis_index_groups=groups, tiled=True)


RAW = 0
GRADIENTS = ((8, 9, 10, 11), (0, 1, 2, 3, 4, 5, 6, 7), (12, 13, 14, 15))
JOINS = ((0, 1, 2, 3, 4, 5, 6, 7), (8, 9, 10, 11), (12, 13), (14, 15))


def by_halves(particles, observed, precision, spread, anneal, step_size):
    slabs = lax.axis_size("slab")
    half = slabs // 2
    lines = NCELL // slabs // LANES
    row = in_hbm(particles)
    fields = [in_hbm(field.reshape(-1, LANES)) for field in (observed, precision)]
    *far, obs, prec, raw_obs, raw_prec = split_pieces(row, slabs, RAW, False, [], fields)
    far = [exchange(piece, half + x, slabs) for x, piece in enumerate(far)]
    near = swap_near(split_pieces(row, slabs, RAW, True, far[:1], [])[0], slabs)
    extra = []
    if RAW:
        extra = [exchange(raw_states(near, RAW, lines), half, slabs)]
    grads = []
    numbers = [spread, anneal, step_size]
    for group in GRADIENTS:
        if group[0] < half:
            arrays, views = [near], [(0, k, 0) for k in group]
        else:
            arrays, views = [far[k - half] for k in group], [(j, None, 0) for j in range(len(group))]
        slopes, rows = gradient_pieces(arrays, tuple(views), obs, prec, [] if grads else numbers)
        grads.append(in_hbm(slopes))
        numbers = numbers if len(grads) > 1 else rows
    grams = lax.all_gather(gram_pieces(near, far, lines, grads[:1]), "slab")
    if RAW:
        views = [(0, k, lines + TILE) for k in range(half)] + [(1, k, 0) for k in range(half)]
        slopes, _ = gradient_pieces([near] + extra, tuple(views), raw_obs, raw_prec, [])
        extra += [in_hbm(slopes)]
    new_far = update_pieces(numbers, grams, near, far, grads, GRADIENTS, [], [], RAW, lines, False)
    new_far = [exchange(piece, half + x, slabs) for x, piece in enumerate(new_far)]
    gates = new_far[:1]
    new_near = update_pieces(numbers, grams, near, far, grads, GRADIENTS, extra, gates, RAW, lines, True)[0]
    new_near = swap_near(new_near, slabs)
    row = None
    for group in JOINS:
        pieces = [new_near] if group[0] < half else [new_far[k - half] for k in group]
        row = join_pieces(row, slabs, RAW, pieces, group)
    return row


def on_device(particles, observed, precision, spread, anneal, step_size):
    slabs = lax.axis_size("slab")
    total = particles.shape[0] * slabs
    lines = NCELL // slabs // LANES
    if slabs == 16:
        return by_halves(particles, observed, precision, spread, anneal, step_size)
    sent, begun = cuts(lines)
    fields = [observed.reshape(-1, LANES), precision.reshape(-1, LANES)]
    numbers = [spread, anneal, step_size]
    first, obs, prec, scalars = split_row(particles, slabs, 0, sent, True, fields, numbers, [])
    parts = [swap(first)]
    if sent < lines:
        parts += [swap(split_row(particles, slabs, sent, lines, False, [], [], [scalars])[0])]
    if total * TILE > 256:
        grads = slab_gradient(parts, obs, prec, lines, 0, lines)
        states = jnp.concatenate([parts[0][:, :sent]] + parts[1:], axis=1)
        new = plain_update(spread, anneal, step_size, states, grads)
        return join_row(swap(new), lines, 0, None)
    if sent == lines:
        grads = slab_gradient(parts, obs, prec, lines, 0, lines)
        grams = swap(slab_gram(parts[0], lines, slabs, [], []))
        new = slab_update(scalars, grams, parts, grads, 0, lines, [])
        return join_row(swap(new), lines, 0, None)
    gram = slab_gram(parts[0], sent, 1, [], [])
    early = slab_gradient(parts[:1], obs, prec, lines, 0, begun)
    grams = swap(slab_gram(parts[1], lines - sent, slabs, [gram], [early]))
    late = slab_gradient(parts, obs, prec, lines, begun, lines)
    new = slab_update(scalars, grams, parts[:1], early, 0, begun, [])
    rest = slab_update(scalars, grams, parts, late, begun, lines, [new])
    row = join_row(swap(new), lines, 0, None)
    return join_row(swap(rest), lines, begun, row)


def solution(mesh):
    in_specs = (
        P(("groups", "slab"), None),
        P("groups"),
        P("groups"),
        P("groups"),
        P("groups"),
        P("groups"),
    )
    out_specs = P(("groups", "slab"), None)
    return jax.shard_map(
        on_device, mesh=mesh, in_specs=in_specs, out_specs=out_specs, check_vma=False
    )
```

```python
import functools

import jax
import jax.numpy as jnp
from jax import lax
from jax.experimental import pallas as pl
from jax.experimental.pallas import tpu as pltpu
from jax.sharding import PartitionSpec as P

GRID_X = 1024
GRID_Y = 1024
NCELL = 1048576
LANES = 128
LINE = GRID_Y // LANES
TILE = 16

prior_scale = 0.25
mass_term = 1.0

F32 = jnp.float32
BF16 = jnp.bfloat16
MIB = 1024 * 1024


def call(body, name, flops=0, moved=0, limit=16, **kwargs):
    return pl.pallas_call(
        body,
        name=name,
        compiler_params=pltpu.CompilerParams(vmem_limit_bytes=limit * MIB),
        cost_estimate=pl.CostEstimate(flops=flops, bytes_accessed=moved, transcendentals=0),
        **kwargs,
    )


IN_VMEM = pl.BlockSpec(memory_space=pltpu.VMEM)
IN_HBM = pl.BlockSpec(memory_space=pltpu.HBM)


def in_hbm(array):
    return pltpu.with_memory_space_constraint(array, pltpu.HBM)


BLOCK = 4 * TILE


def cuts(lines):
    if lines % (8 * BLOCK):
        return lines, lines
    return lines * 3 // 4, lines * 3 // 4 - BLOCK


def split_body(lines, begin, rim, fields, numbers, row_ref, *refs):
    field_refs, number_refs = refs[:fields], refs[fields : fields + numbers]
    out_ref, *slab_refs, rows_ref = refs[-7 - fields : -5]
    held, edges, sems, edge_sems, field_sems = refs[-5:]
    for k, number_ref in enumerate(number_refs):
        rows_ref[k : k + 1, :] = jnp.broadcast_to(number_ref[...].reshape(1, 1), (1, LANES))
    slabs, count, _ = out_ref.shape
    count -= TILE * rim
    size = count * LANES
    cells = lines * LANES

    def part(slab):
        source = row_ref.at[:, pl.ds(slab * cells + begin * LANES, size)]
        return pltpu.make_async_copy(source, held.at[:, pl.ds(slab * size, size)], sems.at[slab])

    def edge(slab):
        source = row_ref.at[:, pl.ds(slab * cells - GRID_Y, GRID_Y)]
        return pltpu.make_async_copy(source, edges.at[:, pl.ds(slab * GRID_Y, GRID_Y)], edge_sems.at[slab])

    def grid_row(ref, start):
        return ref[:, pl.ds(start, GRID_Y)].astype(F32).reshape(LINE, LANES)

    for slab in range(slabs):
        part(slab).start()
        if rim and slab:
            edge(slab).start()
    mine = pl.ds(pl.multiple_of(lax.axis_index("slab") * lines, TILE), lines)
    fetches = [
        pltpu.make_async_copy(source.at[mine, :], target, field_sems.at[k])
        for k, (source, target) in enumerate(zip(field_refs, slab_refs))
    ]
    for fetch in fetches:
        fetch.start()
    part(0).wait()
    outside = jnp.zeros((LINE, LANES), F32)
    for slab in range(slabs):
        if slab + 1 < slabs:
            part(slab + 1).wait()
        out_ref[slab, :count, :] = held[:, pl.ds(slab * size, size)].reshape(count, LANES)
        if rim:
            if slab:
                edge(slab).wait()
            below = grid_row(held, (slab + 1) * size) if slab + 1 < slabs else outside
            above = grid_row(edges, slab * GRID_Y) if slab else outside
            out_ref[slab, count:, :] = jnp.concatenate([below, above], axis=0).astype(BF16)
    for fetch in fetches:
        fetch.wait()


def split_row(row, slabs, begin, end, rim, fields, numbers, earlier):
    lines = row.shape[1] // slabs // LANES
    count = end - begin
    return call(
        functools.partial(split_body, lines, begin, rim, len(fields), len(numbers)),
        "split_row",
        moved=6 * slabs * count * LANES,
        in_specs=[IN_HBM] * (1 + len(fields)) + [IN_VMEM] * len(numbers) + [IN_HBM] * len(earlier),
        out_specs=[IN_VMEM] * (2 + len(fields)),
        out_shape=[jax.ShapeDtypeStruct((slabs, count + TILE * rim, LANES), BF16)]
        + [jax.ShapeDtypeStruct((lines, LANES), BF16)] * len(fields)
        + [jax.ShapeDtypeStruct((8, LANES), F32)],
        scratch_shapes=[
            pltpu.VMEM((1, slabs * count * LANES), BF16),
            pltpu.VMEM((1, slabs * GRID_Y), BF16),
            pltpu.SemaphoreType.DMA((slabs,)),
            pltpu.SemaphoreType.DMA((slabs,)),
            pltpu.SemaphoreType.DMA((2,)),
        ],
    )(row, *fields, *numbers, *earlier)


def join_body(lines, begin, slabs_ref, *refs):
    row_ref, held, sems = refs[-3:]
    slabs, count, _ = slabs_ref.shape
    size = count * LANES
    copies = []
    for slab in range(slabs):
        at = pl.ds(slab * size, size)
        held[:, at] = slabs_ref[slab].reshape(1, size)
        target = row_ref.at[:, pl.ds((slab * lines + begin) * LANES, size)]
        copies.append(pltpu.make_async_copy(held.at[:, at], target, sems.at[slab]))
        copies[-1].start()
    for copy in copies:
        copy.wait()


def join_row(slabs, lines, begin, row):
    total, count, _ = slabs.shape
    begun = [] if row is None else [row]
    return call(
        functools.partial(join_body, lines, begin),
        "join_row",
        moved=6 * slabs.size,
        in_specs=[IN_VMEM] + [IN_HBM] * len(begun),
        out_specs=IN_HBM,
        out_shape=jax.ShapeDtypeStruct((1, total * lines * LANES), BF16),
        input_output_aliases={1: 0} if begun else {},
        scratch_shapes=[pltpu.VMEM((1, slabs.size), BF16), pltpu.SemaphoreType.DMA((total,))],
    )(slabs, *begun)


def same_line(total):
    wide = total * TILE
    row = lax.broadcasted_iota(jnp.int32, (wide, wide), 0)
    col = lax.broadcasted_iota(jnp.int32, (wide, wide), 1)
    return row % TILE == col % TILE


def members(total, dtype):
    wide = total * TILE
    row = lax.broadcasted_iota(jnp.int32, (wide, total), 0)
    col = lax.broadcasted_iota(jnp.int32, (wide, total), 1)
    return (row // TILE == col).astype(dtype)


def gram_body(steps, tiles, parts, states_ref, *refs):
    out_ref, pairs = refs[-2:]
    total = states_ref.shape[0]
    wide = total * TILE
    pairs[...] = jnp.zeros_like(pairs)

    def step(i, carry):
        parts = [
            states_ref[:, pl.ds(pl.multiple_of((i * tiles + t) * TILE, TILE), TILE), :].reshape(wide, LANES)
            for t in range(tiles)
        ]
        block = jnp.concatenate(parts, axis=1)
        pairs[...] += lax.dot_general(block, block, (((1,), (1,)), ((), ())), preferred_element_type=F32)
        return carry

    lax.fori_loop(0, steps, step, 0)
    equal = jnp.where(same_line(total), pairs[...], 0.0)
    rows = jnp.sum(equal.reshape(total, TILE, wide), axis=1)
    gram = jnp.dot(rows, members(total, F32), precision=lax.Precision.HIGHEST, preferred_element_type=F32)
    gram = jnp.concatenate([gram, jnp.zeros((total, LANES - total), F32)], axis=1)
    for part_ref in refs[:parts]:
        gram += part_ref[0]
    out_ref[...] = jnp.broadcast_to(gram[None], out_ref.shape)


def slab_gram(states, lines, copies, parts, earlier):
    total = states.shape[0]
    wide = total * TILE
    tiles = min(8, lines // TILE)
    return call(
        functools.partial(gram_body, lines // TILE // tiles, tiles, len(parts)),
        "slab_gram",
        flops=2 * wide * wide * LANES * (lines // TILE),
        moved=2 * states.size,
        in_specs=[IN_VMEM] * (1 + len(parts)) + [IN_HBM] * len(earlier),
        out_specs=IN_VMEM,
        out_shape=jax.ShapeDtypeStruct((copies, total, LANES), F32),
        scratch_shapes=[pltpu.VMEM((wide, wide), F32)],
    )(states, *parts, *earlier)


def gradient_body(lines, begin, end, parts, *refs):
    observed, precision, out_ref, grads, sems = refs[parts:]
    total = grads.shape[0]
    first = refs[0].shape[1] - TILE
    rows = BLOCK // LINE
    group = 4
    shape = (rows, LINE, LANES)
    lane = lax.broadcasted_iota(jnp.int32, (1, LINE, LANES), 2)
    line = lax.broadcasted_iota(jnp.int32, (1, LINE, LANES), 1)

    def load(particle, at, count):
        ref, at = (refs[0], at) if at < first else (refs[1], at - first)
        return ref[particle, at : at + count, :].astype(F32)

    def rim(particle):
        return refs[0][particle, first:, :].astype(F32)

    stores = []
    for k, at in enumerate(range(begin, end, BLOCK)):
        mine = slice(at - begin, at - begin + BLOCK)
        obs = observed[at : at + BLOCK, :].astype(F32).reshape(shape)
        prec = precision[at : at + BLOCK, :].astype(F32).reshape(shape)

        def step(i, carry):
            for p in range(group):
                particle = i * group + p
                here = load(particle, at, BLOCK)
                before = load(particle, at - TILE, TILE) if at else rim(particle)
                after = load(particle, at + BLOCK, TILE) if at + BLOCK < lines else rim(particle)
                above = jnp.concatenate([before[LINE:], here[:-LINE]], axis=0).reshape(shape)
                below = jnp.concatenate([here[LINE:], after[:LINE]], axis=0).reshape(shape)
                field = here.reshape(shape)
                turned = pltpu.roll(field, 1, 2)
                carried = jnp.where(line == 0, 0.0, pltpu.roll(turned, 1, 1))
                left = jnp.where(lane == 0, carried, turned)
                turned = pltpu.roll(field, LANES - 1, 2)
                carried = jnp.where(line == LINE - 1, 0.0, pltpu.roll(turned, LINE - 1, 1))
                right = jnp.where(lane == LANES - 1, carried, turned)
                laplace = (4.0 + mass_term) * field - (below + above + right + left)
                squash = jnp.tanh(field)
                result = prec * (obs - squash) * (1.0 - squash * squash) - prior_scale * laplace
                grads[particle, mine, :] = result.reshape(BLOCK, LANES).astype(BF16)
            return carry

        lax.fori_loop(0, total // group, step, 0)
        stores.append(pltpu.make_async_copy(grads.at[:, mine, :], out_ref.at[:, mine, :], sems.at[k]))
        stores[-1].start()
    for store in stores:
        store.wait()


def slab_gradient(parts, observed, precision, lines, begin, end):
    total = parts[0].shape[0]
    count = end - begin
    out = jax.ShapeDtypeStruct((total, count, LANES), BF16)
    return call(
        functools.partial(gradient_body, lines, begin, end, len(parts)),
        "slab_gradient",
        flops=30 * out.size,
        moved=8 * out.size,
        in_specs=[IN_VMEM] * (len(parts) + 2),
        out_specs=IN_HBM,
        out_shape=out,
        scratch_shapes=[pltpu.VMEM(out.shape, BF16), pltpu.SemaphoreType.DMA((count // BLOCK,))],
    )(*parts, observed, precision)


def update_body(begin, end, parts, *refs):
    states_refs, refs = refs[:parts], refs[parts:]
    scalars_ref, grams_ref, grads_ref = refs[:3]
    out_ref, grads, mixer, own, sem = refs[-5:]
    total = out_ref.shape[0]
    wide = total * TILE
    fetch = pltpu.make_async_copy(grads_ref, grads, sem)
    fetch.start()
    gram = jnp.sum(grams_ref[...], axis=0)[:, :total]
    row = lax.broadcasted_iota(jnp.int32, (total, total), 0)
    col = lax.broadcasted_iota(jnp.int32, (total, total), 1)
    diagonal = jnp.where(row == col, gram, 0.0)
    down = jnp.sum(diagonal, axis=1, keepdims=True)
    across = jnp.sum(diagonal, axis=0, keepdims=True)
    member = members(total, BF16)
    spread, anneal, step_size = (scalars_ref[k : k + 1, :1] for k in range(3))
    rate = step_size / total
    coeff = 2.0 * anneal / spread
    kernel = jnp.exp(-(down + across - 2.0 * gram) / (spread * NCELL)).astype(BF16)
    ksum = jnp.sum(kernel.astype(F32), axis=1, keepdims=True)
    half = jnp.dot(member, kernel, preferred_element_type=F32).astype(BF16)
    full = lax.dot_general(half, member, (((1,), (1,)), ((), ())), preferred_element_type=F32)
    mixer[...] = jnp.where(same_line(total), full, 0.0).astype(BF16)
    gain = 1.0 + rate * coeff * ksum
    own[...] = jnp.broadcast_to(gain[:, :, None], (total, TILE, LANES)).reshape(wide, LANES)
    fetch.wait()

    done = 0
    for part, states_ref in enumerate(states_refs):
        have = states_ref.shape[1] - (0 if part else TILE)
        low = max(begin - done, 0)
        high = min(end - done, have)
        into = done - begin
        done += have

        def step(i, carry):
            for t in range(BLOCK // TILE):
                at = pl.multiple_of(i * BLOCK + t * TILE, TILE)
                there = pl.ds(pl.multiple_of(at + into, TILE), TILE)
                states = states_ref[:, pl.ds(at, TILE), :].reshape(wide, LANES)
                both = jnp.concatenate([grads[:, there, :].reshape(wide, LANES), states], axis=1)
                mixed = jnp.dot(mixer[...], both, preferred_element_type=F32)
                drive, pulled = mixed[:, :LANES], mixed[:, LANES:]
                new = states.astype(F32) * own[...] + rate * (drive - coeff * pulled)
                out_ref[:, there, :] = new.astype(BF16).reshape(total, TILE, LANES)
            return carry

        lax.fori_loop(low // BLOCK, high // BLOCK, step, 0)


def slab_update(scalars, grams, parts, grads, begin, end, earlier):
    total, count, _ = grads.shape
    wide = total * TILE
    return call(
        functools.partial(update_body, begin, end, len(parts)),
        "slab_update",
        flops=4 * wide * wide * LANES * (count // TILE),
        moved=6 * grads.size,
        in_specs=[IN_VMEM] * len(parts)
        + [IN_VMEM, IN_VMEM, IN_HBM]
        + [IN_HBM] * len(earlier),
        out_specs=IN_VMEM,
        out_shape=jax.ShapeDtypeStruct(grads.shape, BF16),
        scratch_shapes=[
            pltpu.VMEM(grads.shape, BF16),
            pltpu.VMEM((wide, wide), BF16),
            pltpu.VMEM((wide, LANES), F32),
            pltpu.SemaphoreType.DMA,
        ],
    )(*parts, scalars, grams, grads, *earlier)


def plain_update(spread, anneal, step_size, states, grads):
    total, lines, _ = grads.shape
    flat = states[:, :lines].reshape(total, -1)
    gram = lax.dot_general(flat, flat, (((1,), (1,)), ((), ())), preferred_element_type=F32)
    gram = lax.psum(gram, "slab")
    norms = jnp.diagonal(gram)
    kernel = jnp.exp(-(norms[:, None] + norms[None, :] - 2.0 * gram) / (spread[0] * NCELL)).astype(BF16)
    ksum = jnp.sum(kernel.astype(F32), axis=1)
    drive = jnp.dot(kernel, grads.reshape(total, -1), preferred_element_type=F32)
    pulled = jnp.dot(kernel, flat, preferred_element_type=F32)
    values = flat.astype(F32)
    repel = values * ksum[:, None] - pulled
    coeff = 2.0 * anneal[0] / spread[0]
    new = values + step_size[0] / total * (drive + coeff * repel)
    return new.astype(BF16).reshape(grads.shape)


def swap(slabs):
    return lax.all_to_all(slabs, "slab", split_axis=0, concat_axis=0, tiled=True)


def device_at(at, half):
    me = lax.axis_index("slab").astype(jnp.int32)
    return jnp.where(at < half, me - me % half + at, me ^ at)


def lines_of(start, count):
    return pl.ds(pl.multiple_of(start, TILE), count)


def split_pieces_body(positions, half, raw, lines, gates, fields, row_ref, *refs):
    field_refs, refs = refs[:fields], refs[fields + gates :]
    count = len(positions)
    out_refs, helds, sems = refs[: -count - 1], refs[-count - 1 : -1], refs[-1]
    me = lax.axis_index("slab").astype(jnp.int32)
    slab_refs = out_refs[len(out_refs) - 2 * fields :]
    fetches = []
    for n, target in enumerate(slab_refs):
        start = (me if n < fields else me ^ half) * lines
        source = field_refs[n % fields].at[lines_of(start, target.shape[0]), :]
        fetches.append(pltpu.make_async_copy(source, target, sems.at[5 * count + n]))
    cells = lines * LANES
    end = row_ref.shape[1]
    copies = []
    for at, held in zip(positions, helds):
        mine = []

        def fetch(start, size, to):
            source = row_ref.at[:, pl.ds(pl.multiple_of(start, GRID_Y), size)]
            sem = sems.at[len(copies) * 5 + len(mine)]
            mine.append(pltpu.make_async_copy(source, held.at[:, pl.ds(to, size)], sem))
            mine[-1].start()

        slab = device_at(at, half)
        fetch(slab * cells, cells, 0)
        fetch(jnp.minimum((slab + 1) * cells, end - GRID_Y), GRID_Y, cells)
        fetch(jnp.maximum(slab * cells - GRID_Y, 0), GRID_Y, cells + GRID_Y)
        if raw and at < half:
            other = slab ^ half
            fetch(other * cells, raw * LANES + GRID_Y, cells + 2 * GRID_Y)
            fetch(jnp.maximum(other * cells - GRID_Y, 0), GRID_Y, cells + 3 * GRID_Y + raw * LANES)
        copies.append(mine)

    def grid_row(held, at):
        return held[:, pl.ds(at, GRID_Y)].astype(F32).reshape(LINE, LANES)

    for fetch in fetches:
        fetch.start()
    for n, (at, held, mine) in enumerate(zip(positions, helds, copies)):
        out_ref = out_refs[1 + at - half] if at >= half else out_refs[0].at[at]
        for copy in mine:
            copy.wait()
        slab = device_at(at, half)
        out_ref[:lines, :] = held[:, :cells].reshape(lines, LANES)
        below = jnp.where(slab == end // cells - 1, 0.0, grid_row(held, cells))
        above = jnp.where(slab == 0, 0.0, grid_row(held, cells + GRID_Y))
        out_ref[lines : lines + TILE, :] = jnp.concatenate([below, above], axis=0).astype(BF16)
        if raw and at < half:
            start = cells + 2 * GRID_Y
            to = lines + TILE
            out_ref[to : to + raw, :] = held[:, start : start + raw * LANES].reshape(raw, LANES)
            below = grid_row(held, start + raw * LANES)
            above = jnp.where(slab ^ half == 0, 0.0, grid_row(held, start + raw * LANES + GRID_Y))
            out_ref[to + raw :, :] = jnp.concatenate([below, above], axis=0).astype(BF16)
    for fetch in fetches:
        fetch.wait()


def split_pieces(row, slabs, raw, fields):
    lines = row.shape[1] // slabs // LANES
    half = slabs // 2
    rim = lines + TILE
    size = rim + (raw + TILE if raw else 0)
    out_shape = [jax.ShapeDtypeStruct((half, size, LANES), BF16)]
    out_shape += [jax.ShapeDtypeStruct((rim, LANES), BF16)] * half
    out_shape += [jax.ShapeDtypeStruct((lines, LANES), BF16)] * len(fields)
    out_shape += [jax.ShapeDtypeStruct((max(raw, TILE), LANES), BF16)] * len(fields)
    return call(
        functools.partial(split_pieces_body, range(slabs), half, raw, lines, 0, len(fields)),
        "split_pieces",
        moved=6 * half * (size + rim) * LANES,
        in_specs=[IN_HBM] * (1 + len(fields)),
        out_specs=[IN_VMEM] * len(out_shape),
        out_shape=out_shape,
        scratch_shapes=[pltpu.VMEM((1, (size + TILE) * LANES), BF16)] * half
        + [pltpu.VMEM((1, (rim + TILE) * LANES), BF16)] * half
        + [pltpu.SemaphoreType.DMA((5 * slabs + 2 * len(fields),))],
    )(row, *fields)


def join_pieces_body(pieces, half, lines, begun, arrays, *refs):
    row_ref, helds, sems = refs[begun + arrays], refs[begun + arrays + 1 : -1], refs[-1]
    copies = []
    for (array, lead, at, across, begin), held in zip(pieces, helds):
        ref = refs[begun + array]
        piece = ref[...] if lead is None else ref[lead]
        held[...] = piece.reshape(held.shape)
        slab = device_at(at, half)
        start = ((slab ^ half if across else slab) * lines + begin) * LANES
        target = row_ref.at[:, pl.ds(pl.multiple_of(start, GRID_Y), held.shape[1])]
        copies.append(pltpu.make_async_copy(held, target, sems.at[len(copies)]))
        copies[-1].start()
    for copy in copies:
        copy.wait()


def join_pieces(row, slabs, arrays, pieces):
    sizes = [arrays[piece[0]].shape[-2] * LANES for piece in pieces]
    begun = [] if row is None else [row]
    return call(
        functools.partial(join_pieces_body, pieces, slabs // 2, NCELL // slabs // LANES, len(begun), len(arrays)),
        "join_pieces",
        moved=6 * sum(sizes),
        in_specs=[IN_HBM] * len(begun) + [IN_VMEM] * len(arrays),
        out_specs=IN_HBM,
        out_shape=jax.ShapeDtypeStruct((1, NCELL), BF16),
        input_output_aliases={0: 0} if begun else {},
        scratch_shapes=[pltpu.VMEM((1, size), BF16) for size in sizes] + [pltpu.SemaphoreType.DMA((len(sizes),))],
    )(*begun, *arrays)


def owners(total, dtype):
    wide = total * TILE
    row = lax.broadcasted_iota(jnp.int32, (wide, total), 0)
    col = lax.broadcasted_iota(jnp.int32, (wide, total), 1)
    return (device_at(row // TILE, total // 2) == col).astype(dtype)


def gram_pieces_body(lines, total, near_ref, *refs):
    half = total // 2
    pieces, out_ref, pairs = refs[:half], refs[-2], refs[-1]
    wide = total * TILE
    tiles = 4
    pairs[...] = jnp.zeros_like(pairs)

    def step(i, carry):
        parts = []
        for t in range(tiles):
            at = lines_of((i * tiles + t) * TILE, TILE)
            near = near_ref[:, at, :].reshape(wide // 2, LANES)
            parts.append(jnp.concatenate([near] + [piece[at, :] for piece in pieces], axis=0))
        block = jnp.concatenate(parts, axis=1)
        pairs[...] += lax.dot_general(block, block, (((1,), (1,)), ((), ())), preferred_element_type=F32)
        return carry

    lax.fori_loop(0, lines // TILE // tiles, step, 0)
    equal = jnp.where(same_line(total), pairs[...], 0.0)
    exact = {"precision": lax.Precision.HIGHEST, "preferred_element_type": F32}
    owner = owners(total, F32)
    half_way = jnp.dot(equal, owner, **exact)
    gram = lax.dot_general(owner, half_way, (((0,), (0,)), ((), ())), **exact)
    gram = jnp.concatenate([gram, jnp.zeros((total, LANES - total), F32)], axis=1)
    out_ref[...] = jnp.broadcast_to(gram[None], out_ref.shape)


def gram_pieces(near, far, lines, gates, early):
    total = 2 * len(far)
    wide = total * TILE
    return call(
        functools.partial(gram_pieces_body, lines, total),
        "gram_pieces",
        flops=2 * wide * wide * LANES * (lines // TILE),
        moved=2 * total * lines * LANES,
        in_specs=[IN_VMEM] * (1 + len(far)) + [IN_HBM] * len(gates) + [IN_VMEM] * len(early),
        out_specs=IN_VMEM,
        out_shape=jax.ShapeDtypeStruct((total, total, LANES), F32),
        scratch_shapes=[pltpu.VMEM((wide, wide), F32)],
    )(near, *far, *gates, *early)


def gradient_pieces_body(views, arrays, numbers, *refs):
    observed, precision, *number_refs = refs[arrays : arrays + 2 + numbers]
    out_ref, rows_ref, grads, sems = refs[-4:]
    for n, number_ref in enumerate(number_refs):
        rows_ref[n : n + 1, :] = jnp.full((1, LANES), number_ref[0], F32)
    count = observed.shape[0]
    rows = BLOCK // LINE
    shape = (rows, LINE, LANES)
    lane = lax.broadcasted_iota(jnp.int32, (1, LINE, LANES), 2)
    line = lax.broadcasted_iota(jnp.int32, (1, LINE, LANES), 1)
    steps = count // BLOCK

    def store(i):
        at = lines_of(i * BLOCK, BLOCK)
        return pltpu.make_async_copy(grads.at[:, at, :], out_ref.at[:, at, :], sems.at[i])

    def step(i, carry):
        start = i * BLOCK
        at = lines_of(start, BLOCK)
        obs = observed[at, :].astype(F32).reshape(shape)
        prec = precision[at, :].astype(F32).reshape(shape)
        for p, (array, lead, base) in enumerate(views):

            def load(begin, size):
                part = lines_of(base + begin, size)
                value = refs[array][part, :] if lead is None else refs[array][lead, part, :]
                return value.astype(F32)

            here = load(start, BLOCK)
            before = load(jnp.where(i == 0, count, start - TILE), TILE)
            after = load(start + BLOCK, TILE)
            above = jnp.concatenate([before[LINE:], here[:-LINE]], axis=0).reshape(shape)
            below = jnp.concatenate([here[LINE:], after[:LINE]], axis=0).reshape(shape)
            field = here.reshape(shape)
            turned = pltpu.roll(field, 1, 2)
            carried = jnp.where(line == 0, 0.0, pltpu.roll(turned, 1, 1))
            left = jnp.where(lane == 0, carried, turned)
            turned = pltpu.roll(field, LANES - 1, 2)
            carried = jnp.where(line == LINE - 1, 0.0, pltpu.roll(turned, LINE - 1, 1))
            right = jnp.where(lane == LANES - 1, carried, turned)
            laplace = (4.0 + mass_term) * field - (below + above + right + left)
            squash = jnp.tanh(field)
            result = prec * (obs - squash) * (1.0 - squash * squash) - prior_scale * laplace
            grads[p, at, :] = result.reshape(BLOCK, LANES).astype(BF16)
        store(i).start()
        return carry

    def finish(i, carry):
        store(i).wait()
        return carry

    lax.fori_loop(0, steps, step, 0)
    lax.fori_loop(0, steps, finish, 0)


def gradient_pieces(arrays, views, observed, precision, numbers):
    count = observed.shape[0]
    out = pltpu.HBM((len(views), count, LANES), BF16)
    size = len(views) * count * LANES
    return call(
        functools.partial(gradient_pieces_body, views, len(arrays), len(numbers)),
        "gradient_pieces",
        flops=30 * size,
        moved=8 * size,
        in_specs=[IN_VMEM] * (len(arrays) + 2)
        + [pl.BlockSpec(memory_space=pltpu.SMEM)] * len(numbers),
        out_specs=[IN_HBM, IN_VMEM],
        out_shape=[out, jax.ShapeDtypeStruct((8, LANES), F32)],
        scratch_shapes=[pltpu.VMEM(out.shape, BF16), pltpu.SemaphoreType.DMA((count // BLOCK,))],
    )(*arrays, observed, precision, *numbers)


def raw_body(raw, lines, near_ref, out_ref):
    for k in range(near_ref.shape[0]):
        out_ref[k, :raw, :] = near_ref[k, :raw, :]
        below = near_ref[k, raw : raw + TILE, :].astype(F32)[:LINE]
        above = near_ref[k, lines : lines + TILE, :].astype(F32)[LINE:]
        out_ref[k, raw:, :] = jnp.concatenate([below, above], axis=0).astype(BF16)


def raw_states(near, raw, lines):
    out = jax.ShapeDtypeStruct((near.shape[0], raw + TILE, LANES), BF16)
    return call(
        functools.partial(raw_body, raw, lines),
        "raw_states",
        moved=4 * out.size,
        in_specs=[IN_VMEM],
        out_specs=IN_VMEM,
        out_shape=out,
    )(near)


def mix(mixer, own, numbers_ref, total, states, slopes):
    high = mixer.shape[0]
    rate = numbers_ref[2:3, :1] / total
    coeff = 2.0 * numbers_ref[1:2, :1] / numbers_ref[:1, :1]
    both = jnp.concatenate([slopes, states], axis=1)
    mixed = jnp.dot(mixer[...], both, preferred_element_type=F32)
    drive, pulled = mixed[:, :LANES], mixed[:, LANES:]
    return (states[:high].astype(F32) * own[...] + rate * (drive - coeff * pulled)).astype(BF16)


def update_pieces_body(half, raw, lines, groups, near_ref, *refs):
    total = 2 * half
    far_refs, numbers_ref, grams_ref, refs = refs[:half], refs[half], refs[half + 1], refs[half + 2 :]
    group_refs, near_out, far_outs = refs[: len(groups)], refs[-5 - half], refs[-4 - half : -4]
    mixer, own, grads, sems = refs[-4:]
    wide = total * TILE
    high = half * TILE
    fetches = []
    for group, group_ref in zip(groups, group_refs):
        for j, at in enumerate(group):
            fetches.append(pltpu.make_async_copy(group_ref.at[j], grads.at[at], sems.at[len(fetches)]))
    for fetch in fetches:
        fetch.start()
    gram = jnp.sum(grams_ref[...], axis=0)[:, :total]
    spread, anneal, step_size = (numbers_ref[k : k + 1, :1] for k in range(3))
    rate = step_size / total
    coeff = 2.0 * anneal / spread
    row = lax.broadcasted_iota(jnp.int32, (total, total), 0)
    col = lax.broadcasted_iota(jnp.int32, (total, total), 1)
    diagonal = jnp.where(row == col, gram, 0.0)
    down = jnp.sum(diagonal, axis=1, keepdims=True)
    across = jnp.sum(diagonal, axis=0, keepdims=True)
    kernel = jnp.exp(-(down + across - 2.0 * gram) / (spread * NCELL)).astype(BF16)
    owner = owners(total, BF16)
    half_way = jnp.dot(owner, kernel, preferred_element_type=F32).astype(BF16)
    full = lax.dot_general(half_way, owner, (((1,), (1,)), ((), ())), preferred_element_type=F32)
    full = jnp.where(same_line(total), full, 0.0)
    mixer[...] = full.astype(BF16)
    ksum = jnp.sum(full, axis=1, keepdims=True)
    own[...] = jnp.broadcast_to(1.0 + rate * coeff * ksum, (wide, LANES))
    for fetch in fetches:
        fetch.wait()

    def step(with_far, i, carry):
        for t in range(BLOCK // TILE):
            at = i * BLOCK + t * TILE
            part = lines_of(at, TILE)
            states = [near_ref[:, part, :].reshape(high, LANES)] + [ref[part, :] for ref in far_refs]
            slopes = grads[:, part, :].reshape(wide, LANES)
            new = mix(mixer, own, numbers_ref, total, jnp.concatenate(states, axis=0), slopes)
            near_out[:, part, :] = new[:high].reshape(half, TILE, LANES)
            if with_far:
                for x, far_out in enumerate(far_outs):
                    far_out[lines_of(at - raw, TILE), :] = new[high + x * TILE : high + (x + 1) * TILE]
        return carry

    lax.fori_loop(0, raw // BLOCK, functools.partial(step, False), 0)
    lax.fori_loop(raw // BLOCK, lines // BLOCK, functools.partial(step, True), 0)


def update_pieces(numbers, grams, near, far, grads, groups, gates, raw, lines):
    half = len(far)
    total = 2 * half
    wide = total * TILE
    out_shape = [jax.ShapeDtypeStruct((half, lines, LANES), BF16)]
    out_shape += [jax.ShapeDtypeStruct((lines - raw, LANES), BF16)] * half
    out_shape += [jax.ShapeDtypeStruct((wide, wide), BF16), jax.ShapeDtypeStruct((wide, LANES), F32)]
    return call(
        functools.partial(update_pieces_body, half, raw, lines, groups),
        "update_pieces",
        flops=4 * wide * wide * LANES * (lines // TILE),
        moved=6 * total * lines * LANES,
        in_specs=[IN_VMEM] * (half + 3) + [IN_HBM] * len(groups) + [IN_VMEM] * len(gates),
        out_specs=[IN_VMEM] * len(out_shape),
        out_shape=out_shape,
        scratch_shapes=[pltpu.VMEM((total, lines, LANES), BF16), pltpu.SemaphoreType.DMA((total,))],
    )(near, *far, numbers, grams, *grads, *gates)


def update_raw_body(lines, near_ref, across_ref, mixer, own, numbers_ref, grads_ref, out_ref, grads, sem):
    half, raw, _ = out_ref.shape
    high = half * TILE
    fetch = pltpu.make_async_copy(grads_ref, grads, sem)
    fetch.start()
    fetch.wait()
    here = lax.axis_index("slab").astype(jnp.int32) % half

    def step(i, carry):
        for t in range(BLOCK // TILE):
            at = i * BLOCK + t * TILE
            part = lines_of(at, TILE)
            states = [near_ref[:, lines_of(lines + TILE + at, TILE), :].reshape(high, LANES)]
            slopes = [grads[:half, part, :].reshape(high, LANES)]
            for x in range(half):
                states += [across_ref[here ^ x, part, :]]
                slopes += [grads[half + (here ^ x), part, :]]
            states, slopes = jnp.concatenate(states, axis=0), jnp.concatenate(slopes, axis=0)
            new = mix(mixer.at[:high, :], own.at[:high, :], numbers_ref, 2 * half, states, slopes)
            out_ref[:, part, :] = new.reshape(half, TILE, LANES)
        return carry

    lax.fori_loop(0, raw // BLOCK, step, 0)


def update_raw(near, across, mixer, own, numbers, grads, raw, lines):
    half = near.shape[0]
    return call(
        functools.partial(update_raw_body, lines),
        "update_raw",
        flops=2 * mixer.size * LANES * (raw // TILE),
        moved=12 * half * raw * LANES,
        in_specs=[IN_VMEM] * 5 + [IN_HBM],
        out_specs=IN_VMEM,
        out_shape=jax.ShapeDtypeStruct((half, raw, LANES), BF16),
        scratch_shapes=[pltpu.VMEM((2 * half, raw, LANES), BF16), pltpu.SemaphoreType.DMA],
    )(near, across, mixer, own, numbers, grads)


def exchange(piece, k, slabs):
    return lax.ppermute(piece, "slab", [(i, i ^ k) for i in range(slabs)])


def swap_near(pieces, slabs):
    groups = [list(range(slabs // 2)), list(range(slabs // 2, slabs))]
    return lax.all_to_all(pieces, "slab", 0, 0, axis_index_groups=groups, tiled=True)


RAW = 128
GRADIENTS = ((8, 9, 10, 11), (12, 13, 14, 15), (0, 1, 2, 3, 4, 5, 6, 7))


def by_halves(particles, observed, precision, spread, anneal, step_size):
    slabs = lax.axis_size("slab")
    half = slabs // 2
    lines = NCELL // slabs // LANES
    row = in_hbm(particles)
    fields = [in_hbm(field.reshape(-1, LANES)) for field in (observed, precision)]
    near, *far = split_pieces(row, slabs, RAW, fields)
    far, (obs, prec, raw_obs, raw_prec) = far[:half], far[half:]
    near = swap_near(near, slabs)
    far = [exchange(piece, half + x, slabs) for x, piece in enumerate(far)]
    early, gates = [], []
    if RAW:
        early = [raw_states(near, RAW, lines)]
        gates = [exchange(early[0], half, slabs)]
    grads = []
    numbers = [spread, anneal, step_size]
    for group in GRADIENTS:
        if group[0] < half:
            arrays, views = [near], [(0, k, 0) for k in group]
        else:
            arrays, views = [far[k - half] for k in group], [(j, None, 0) for j in range(len(group))]
        slopes, rows = gradient_pieces(arrays, tuple(views), obs, prec, [] if grads else numbers)
        grads.append(in_hbm(slopes))
        numbers = numbers if len(grads) > 1 else rows
    grams = swap(gram_pieces(near, far, lines, grads[:1], early))
    new_near, *new_far = update_pieces(numbers, grams, near, far, grads, GRADIENTS, gates, RAW, lines)
    new_far, (mixer, own) = new_far[:half], new_far[half:]
    new_near = swap_near(new_near, slabs)
    new_far = [exchange(piece, half + x, slabs) for x, piece in enumerate(new_far)]
    if RAW:
        views = [(0, k, lines + TILE) for k in range(half)] + [(1, k, 0) for k in range(half)]
        slopes, _ = gradient_pieces([near] + gates, tuple(views), raw_obs, raw_prec, [])
        new_raw = swap_near(update_raw(near, gates[0], mixer, own, numbers, in_hbm(slopes), RAW, lines), slabs)
    row = join_pieces(None, slabs, [new_near], [(0, k, k, False, 0) for k in range(half)])
    for group in ((0, 1, 2, 3), (4, 5)):
        pieces = [(n, None, half + x, False, RAW) for n, x in enumerate(group)]
        row = join_pieces(row, slabs, [new_far[x] for x in group], pieces)
    if RAW:
        row = join_pieces(row, slabs, [new_raw], [(0, k, k, True, 0) for k in range(half)])
    return join_pieces(row, slabs, new_far[6:], [(n, None, half + 6 + n, False, RAW) for n in range(half - 6)])


def on_device(particles, observed, precision, spread, anneal, step_size):
    slabs = lax.axis_size("slab")
    total = particles.shape[0] * slabs
    lines = NCELL // slabs // LANES
    if slabs == 16:
        return by_halves(particles, observed, precision, spread, anneal, step_size)
    sent, begun = cuts(lines)
    fields = [observed.reshape(-1, LANES), precision.reshape(-1, LANES)]
    numbers = [spread, anneal, step_size]
    first, obs, prec, scalars = split_row(particles, slabs, 0, sent, True, fields, numbers, [])
    parts = [swap(first)]
    if sent < lines:
        parts += [swap(split_row(particles, slabs, sent, lines, False, [], [], [scalars])[0])]
    if total * TILE > 256:
        grads = slab_gradient(parts, obs, prec, lines, 0, lines)
        states = jnp.concatenate([parts[0][:, :sent]] + parts[1:], axis=1)
        new = plain_update(spread, anneal, step_size, states, grads)
        return join_row(swap(new), lines, 0, None)
    if sent == lines:
        grads = slab_gradient(parts, obs, prec, lines, 0, lines)
        grams = swap(slab_gram(parts[0], lines, slabs, [], []))
        new = slab_update(scalars, grams, parts, grads, 0, lines, [])
        return join_row(swap(new), lines, 0, None)
    gram = slab_gram(parts[0], sent, 1, [], [])
    early = slab_gradient(parts[:1], obs, prec, lines, 0, begun)
    grams = swap(slab_gram(parts[1], lines - sent, slabs, [gram], [early]))
    late = slab_gradient(parts, obs, prec, lines, begun, lines)
    new = slab_update(scalars, grams, parts[:1], early, 0, begun, [])
    rest = slab_update(scalars, grams, parts, late, begun, lines, [new])
    row = join_row(swap(new), lines, 0, None)
    return join_row(swap(rest), lines, begun, row)


def solution(mesh):
    in_specs = (
        P(("groups", "slab"), None),
        P("groups"),
        P("groups"),
        P("groups"),
        P("groups"),
        P("groups"),
    )
    out_specs = P(("groups", "slab"), None)
    return jax.shard_map(
        on_device, mesh=mesh, in_specs=in_specs, out_specs=out_specs, check_vma=False
    )
```

```python
import functools

import jax
import jax.numpy as jnp
from jax import lax
from jax.experimental import pallas as pl
from jax.experimental.pallas import tpu as pltpu
from jax.sharding import PartitionSpec as P

GRID_X = 1024
GRID_Y = 1024
NCELL = 1048576
LANES = 128
LINE = GRID_Y // LANES
TILE = 16

prior_scale = 0.25
mass_term = 1.0

F32 = jnp.float32
BF16 = jnp.bfloat16
MIB = 1024 * 1024


def call(body, name, flops=0, moved=0, limit=16, **kwargs):
    return pl.pallas_call(
        body,
        name=name,
        compiler_params=pltpu.CompilerParams(vmem_limit_bytes=limit * MIB),
        cost_estimate=pl.CostEstimate(flops=flops, bytes_accessed=moved, transcendentals=0),
        **kwargs,
    )


IN_VMEM = pl.BlockSpec(memory_space=pltpu.VMEM)
IN_HBM = pl.BlockSpec(memory_space=pltpu.HBM)


def in_hbm(array):
    return pltpu.with_memory_space_constraint(array, pltpu.HBM)


BLOCK = 4 * TILE


def cuts(lines):
    if lines % (8 * BLOCK):
        return lines, lines
    return lines * 3 // 4, lines * 3 // 4 - BLOCK


def split_body(lines, begin, rim, fields, numbers, row_ref, *refs):
    field_refs, number_refs = refs[:fields], refs[fields : fields + numbers]
    out_ref, *slab_refs, rows_ref = refs[-7 - fields : -5]
    held, edges, sems, edge_sems, field_sems = refs[-5:]
    for k, number_ref in enumerate(number_refs):
        rows_ref[k : k + 1, :] = jnp.broadcast_to(number_ref[...].reshape(1, 1), (1, LANES))
    slabs, count, _ = out_ref.shape
    count -= TILE * rim
    size = count * LANES
    cells = lines * LANES

    def part(slab):
        source = row_ref.at[:, pl.ds(slab * cells + begin * LANES, size)]
        return pltpu.make_async_copy(source, held.at[:, pl.ds(slab * size, size)], sems.at[slab])

    def edge(slab):
        source = row_ref.at[:, pl.ds(slab * cells - GRID_Y, GRID_Y)]
        return pltpu.make_async_copy(source, edges.at[:, pl.ds(slab * GRID_Y, GRID_Y)], edge_sems.at[slab])

    def grid_row(ref, start):
        return ref[:, pl.ds(start, GRID_Y)].astype(F32).reshape(LINE, LANES)

    for slab in range(slabs):
        part(slab).start()
        if rim and slab:
            edge(slab).start()
    mine = pl.ds(pl.multiple_of(lax.axis_index("slab") * lines, TILE), lines)
    fetches = [
        pltpu.make_async_copy(source.at[mine, :], target, field_sems.at[k])
        for k, (source, target) in enumerate(zip(field_refs, slab_refs))
    ]
    for fetch in fetches:
        fetch.start()
    part(0).wait()
    outside = jnp.zeros((LINE, LANES), F32)
    for slab in range(slabs):
        if slab + 1 < slabs:
            part(slab + 1).wait()
        out_ref[slab, :count, :] = held[:, pl.ds(slab * size, size)].reshape(count, LANES)
        if rim:
            if slab:
                edge(slab).wait()
            below = grid_row(held, (slab + 1) * size) if slab + 1 < slabs else outside
            above = grid_row(edges, slab * GRID_Y) if slab else outside
            out_ref[slab, count:, :] = jnp.concatenate([below, above], axis=0).astype(BF16)
    for fetch in fetches:
        fetch.wait()


def split_row(row, slabs, begin, end, rim, fields, numbers, earlier):
    lines = row.shape[1] // slabs // LANES
    count = end - begin
    return call(
        functools.partial(split_body, lines, begin, rim, len(fields), len(numbers)),
        "split_row",
        moved=6 * slabs * count * LANES,
        in_specs=[IN_HBM] * (1 + len(fields)) + [IN_VMEM] * len(numbers) + [IN_HBM] * len(earlier),
        out_specs=[IN_VMEM] * (2 + len(fields)),
        out_shape=[jax.ShapeDtypeStruct((slabs, count + TILE * rim, LANES), BF16)]
        + [jax.ShapeDtypeStruct((lines, LANES), BF16)] * len(fields)
        + [jax.ShapeDtypeStruct((8, LANES), F32)],
        scratch_shapes=[
            pltpu.VMEM((1, slabs * count * LANES), BF16),
            pltpu.VMEM((1, slabs * GRID_Y), BF16),
            pltpu.SemaphoreType.DMA((slabs,)),
            pltpu.SemaphoreType.DMA((slabs,)),
            pltpu.SemaphoreType.DMA((2,)),
        ],
    )(row, *fields, *numbers, *earlier)


def join_body(lines, begin, slabs_ref, *refs):
    row_ref, held, sems = refs[-3:]
    slabs, count, _ = slabs_ref.shape
    size = count * LANES
    copies = []
    for slab in range(slabs):
        at = pl.ds(slab * size, size)
        held[:, at] = slabs_ref[slab].reshape(1, size)
        target = row_ref.at[:, pl.ds((slab * lines + begin) * LANES, size)]
        copies.append(pltpu.make_async_copy(held.at[:, at], target, sems.at[slab]))
        copies[-1].start()
    for copy in copies:
        copy.wait()


def join_row(slabs, lines, begin, row):
    total, count, _ = slabs.shape
    begun = [] if row is None else [row]
    return call(
        functools.partial(join_body, lines, begin),
        "join_row",
        moved=6 * slabs.size,
        in_specs=[IN_VMEM] + [IN_HBM] * len(begun),
        out_specs=IN_HBM,
        out_shape=jax.ShapeDtypeStruct((1, total * lines * LANES), BF16),
        input_output_aliases={1: 0} if begun else {},
        scratch_shapes=[pltpu.VMEM((1, slabs.size), BF16), pltpu.SemaphoreType.DMA((total,))],
    )(slabs, *begun)


def same_line(total):
    wide = total * TILE
    row = lax.broadcasted_iota(jnp.int32, (wide, wide), 0)
    col = lax.broadcasted_iota(jnp.int32, (wide, wide), 1)
    return row % TILE == col % TILE


def members(total, dtype):
    wide = total * TILE
    row = lax.broadcasted_iota(jnp.int32, (wide, total), 0)
    col = lax.broadcasted_iota(jnp.int32, (wide, total), 1)
    return (row // TILE == col).astype(dtype)


def gram_body(steps, tiles, parts, states_ref, *refs):
    out_ref, pairs = refs[-2:]
    total = states_ref.shape[0]
    wide = total * TILE
    pairs[...] = jnp.zeros_like(pairs)

    def step(i, carry):
        parts = [
            states_ref[:, pl.ds(pl.multiple_of((i * tiles + t) * TILE, TILE), TILE), :].reshape(wide, LANES)
            for t in range(tiles)
        ]
        block = jnp.concatenate(parts, axis=1)
        pairs[...] += lax.dot_general(block, block, (((1,), (1,)), ((), ())), preferred_element_type=F32)
        return carry

    lax.fori_loop(0, steps, step, 0)
    equal = jnp.where(same_line(total), pairs[...], 0.0)
    rows = jnp.sum(equal.reshape(total, TILE, wide), axis=1)
    gram = jnp.dot(rows, members(total, F32), precision=lax.Precision.HIGHEST, preferred_element_type=F32)
    gram = jnp.concatenate([gram, jnp.zeros((total, LANES - total), F32)], axis=1)
    for part_ref in refs[:parts]:
        gram += part_ref[0]
    out_ref[...] = jnp.broadcast_to(gram[None], out_ref.shape)


def slab_gram(states, lines, copies, parts, earlier):
    total = states.shape[0]
    wide = total * TILE
    tiles = min(8, lines // TILE)
    return call(
        functools.partial(gram_body, lines // TILE // tiles, tiles, len(parts)),
        "slab_gram",
        flops=2 * wide * wide * LANES * (lines // TILE),
        moved=2 * states.size,
        in_specs=[IN_VMEM] * (1 + len(parts)) + [IN_HBM] * len(earlier),
        out_specs=IN_VMEM,
        out_shape=jax.ShapeDtypeStruct((copies, total, LANES), F32),
        scratch_shapes=[pltpu.VMEM((wide, wide), F32)],
    )(states, *parts, *earlier)


def gradient_body(lines, begin, end, parts, *refs):
    observed, precision, out_ref, grads, sems = refs[parts:]
    total = grads.shape[0]
    first = refs[0].shape[1] - TILE
    rows = BLOCK // LINE
    group = 4
    shape = (rows, LINE, LANES)
    lane = lax.broadcasted_iota(jnp.int32, (1, LINE, LANES), 2)
    line = lax.broadcasted_iota(jnp.int32, (1, LINE, LANES), 1)

    def load(particle, at, count):
        ref, at = (refs[0], at) if at < first else (refs[1], at - first)
        return ref[particle, at : at + count, :].astype(F32)

    def rim(particle):
        return refs[0][particle, first:, :].astype(F32)

    stores = []
    for k, at in enumerate(range(begin, end, BLOCK)):
        mine = slice(at - begin, at - begin + BLOCK)
        obs = observed[at : at + BLOCK, :].astype(F32).reshape(shape)
        prec = precision[at : at + BLOCK, :].astype(F32).reshape(shape)

        def step(i, carry):
            for p in range(group):
                particle = i * group + p
                here = load(particle, at, BLOCK)
                before = load(particle, at - TILE, TILE) if at else rim(particle)
                after = load(particle, at + BLOCK, TILE) if at + BLOCK < lines else rim(particle)
                above = jnp.concatenate([before[LINE:], here[:-LINE]], axis=0).reshape(shape)
                below = jnp.concatenate([here[LINE:], after[:LINE]], axis=0).reshape(shape)
                field = here.reshape(shape)
                turned = pltpu.roll(field, 1, 2)
                carried = jnp.where(line == 0, 0.0, pltpu.roll(turned, 1, 1))
                left = jnp.where(lane == 0, carried, turned)
                turned = pltpu.roll(field, LANES - 1, 2)
                carried = jnp.where(line == LINE - 1, 0.0, pltpu.roll(turned, LINE - 1, 1))
                right = jnp.where(lane == LANES - 1, carried, turned)
                laplace = (4.0 + mass_term) * field - (below + above + right + left)
                squash = jnp.tanh(field)
                result = prec * (obs - squash) * (1.0 - squash * squash) - prior_scale * laplace
                grads[particle, mine, :] = result.reshape(BLOCK, LANES).astype(BF16)
            return carry

        lax.fori_loop(0, total // group, step, 0)
        stores.append(pltpu.make_async_copy(grads.at[:, mine, :], out_ref.at[:, mine, :], sems.at[k]))
        stores[-1].start()
    for store in stores:
        store.wait()


def slab_gradient(parts, observed, precision, lines, begin, end):
    total = parts[0].shape[0]
    count = end - begin
    out = jax.ShapeDtypeStruct((total, count, LANES), BF16)
    return call(
        functools.partial(gradient_body, lines, begin, end, len(parts)),
        "slab_gradient",
        flops=30 * out.size,
        moved=8 * out.size,
        in_specs=[IN_VMEM] * (len(parts) + 2),
        out_specs=IN_HBM,
        out_shape=out,
        scratch_shapes=[pltpu.VMEM(out.shape, BF16), pltpu.SemaphoreType.DMA((count // BLOCK,))],
    )(*parts, observed, precision)


def update_body(begin, end, parts, *refs):
    states_refs, refs = refs[:parts], refs[parts:]
    scalars_ref, grams_ref, grads_ref = refs[:3]
    out_ref, grads, mixer, own, sem = refs[-5:]
    total = out_ref.shape[0]
    wide = total * TILE
    fetch = pltpu.make_async_copy(grads_ref, grads, sem)
    fetch.start()
    gram = jnp.sum(grams_ref[...], axis=0)[:, :total]
    row = lax.broadcasted_iota(jnp.int32, (total, total), 0)
    col = lax.broadcasted_iota(jnp.int32, (total, total), 1)
    diagonal = jnp.where(row == col, gram, 0.0)
    down = jnp.sum(diagonal, axis=1, keepdims=True)
    across = jnp.sum(diagonal, axis=0, keepdims=True)
    member = members(total, BF16)
    spread, anneal, step_size = (scalars_ref[k : k + 1, :1] for k in range(3))
    rate = step_size / total
    coeff = 2.0 * anneal / spread
    kernel = jnp.exp(-(down + across - 2.0 * gram) / (spread * NCELL)).astype(BF16)
    ksum = jnp.sum(kernel.astype(F32), axis=1, keepdims=True)
    half = jnp.dot(member, kernel, preferred_element_type=F32).astype(BF16)
    full = lax.dot_general(half, member, (((1,), (1,)), ((), ())), preferred_element_type=F32)
    mixer[...] = jnp.where(same_line(total), full, 0.0).astype(BF16)
    gain = 1.0 + rate * coeff * ksum
    own[...] = jnp.broadcast_to(gain[:, :, None], (total, TILE, LANES)).reshape(wide, LANES)
    fetch.wait()

    done = 0
    for part, states_ref in enumerate(states_refs):
        have = states_ref.shape[1] - (0 if part else TILE)
        low = max(begin - done, 0)
        high = min(end - done, have)
        into = done - begin
        done += have

        def step(i, carry):
            for t in range(BLOCK // TILE):
                at = pl.multiple_of(i * BLOCK + t * TILE, TILE)
                there = pl.ds(pl.multiple_of(at + into, TILE), TILE)
                states = states_ref[:, pl.ds(at, TILE), :].reshape(wide, LANES)
                both = jnp.concatenate([grads[:, there, :].reshape(wide, LANES), states], axis=1)
                mixed = jnp.dot(mixer[...], both, preferred_element_type=F32)
                drive, pulled = mixed[:, :LANES], mixed[:, LANES:]
                new = states.astype(F32) * own[...] + rate * (drive - coeff * pulled)
                out_ref[:, there, :] = new.astype(BF16).reshape(total, TILE, LANES)
            return carry

        lax.fori_loop(low // BLOCK, high // BLOCK, step, 0)


def slab_update(scalars, grams, parts, grads, begin, end, earlier):
    total, count, _ = grads.shape
    wide = total * TILE
    return call(
        functools.partial(update_body, begin, end, len(parts)),
        "slab_update",
        flops=4 * wide * wide * LANES * (count // TILE),
        moved=6 * grads.size,
        in_specs=[IN_VMEM] * len(parts)
        + [IN_VMEM, IN_VMEM, IN_HBM]
        + [IN_HBM] * len(earlier),
        out_specs=IN_VMEM,
        out_shape=jax.ShapeDtypeStruct(grads.shape, BF16),
        scratch_shapes=[
            pltpu.VMEM(grads.shape, BF16),
            pltpu.VMEM((wide, wide), BF16),
            pltpu.VMEM((wide, LANES), F32),
            pltpu.SemaphoreType.DMA,
        ],
    )(*parts, scalars, grams, grads, *earlier)


def plain_update(spread, anneal, step_size, states, grads):
    total, lines, _ = grads.shape
    flat = states[:, :lines].reshape(total, -1)
    gram = lax.dot_general(flat, flat, (((1,), (1,)), ((), ())), preferred_element_type=F32)
    gram = lax.psum(gram, "slab")
    norms = jnp.diagonal(gram)
    kernel = jnp.exp(-(norms[:, None] + norms[None, :] - 2.0 * gram) / (spread[0] * NCELL)).astype(BF16)
    ksum = jnp.sum(kernel.astype(F32), axis=1)
    drive = jnp.dot(kernel, grads.reshape(total, -1), preferred_element_type=F32)
    pulled = jnp.dot(kernel, flat, preferred_element_type=F32)
    values = flat.astype(F32)
    repel = values * ksum[:, None] - pulled
    coeff = 2.0 * anneal[0] / spread[0]
    new = values + step_size[0] / total * (drive + coeff * repel)
    return new.astype(BF16).reshape(grads.shape)


def swap(slabs):
    return lax.all_to_all(slabs, "slab", split_axis=0, concat_axis=0, tiled=True)


def device_at(at, half):
    me = lax.axis_index("slab").astype(jnp.int32)
    return jnp.where(at < half, me - me % half + at, me ^ at)


def lines_of(start, count):
    return pl.ds(pl.multiple_of(start, TILE), count)


def split_pieces_body(slabs, lines, fields, row_ref, *refs):
    half = slabs // 2
    field_refs, near_out, far_outs = refs[:fields], refs[fields], refs[fields + 1 : fields + 1 + half]
    slab_refs, helds, sems = refs[fields + 1 + half : -slabs - 1], refs[-slabs - 1 : -1], refs[-1]
    cells = lines * LANES
    end = row_ref.shape[1]
    copies = []
    for at, held in enumerate(helds):
        slab = device_at(at, half)
        parts = (
            (slab * cells, cells, 0),
            (jnp.minimum((slab + 1) * cells, end - GRID_Y), GRID_Y, cells),
            (jnp.maximum(slab * cells - GRID_Y, 0), GRID_Y, cells + GRID_Y),
        )
        for n, (start, size, to) in enumerate(parts):
            source = row_ref.at[:, pl.ds(pl.multiple_of(start, GRID_Y), size)]
            copies.append(pltpu.make_async_copy(source, held.at[:, pl.ds(to, size)], sems.at[3 * at + n]))
            copies[-1].start()
    start = lax.axis_index("slab").astype(jnp.int32) * lines
    for n, (field_ref, slab_ref) in enumerate(zip(field_refs, slab_refs)):
        copies.append(pltpu.make_async_copy(field_ref.at[lines_of(start, lines), :], slab_ref, sems.at[3 * slabs + n]))
        copies[-1].start()

    for at, held in enumerate(helds):
        out_ref = near_out.at[at] if at < half else far_outs[at - half]
        for copy in copies[3 * at : 3 * at + 3]:
            copy.wait()
        slab = device_at(at, half)
        out_ref[:lines, :] = held[:, :cells].reshape(lines, LANES)
        below = held[:, cells : cells + GRID_Y].astype(F32).reshape(LINE, LANES)
        above = held[:, cells + GRID_Y :].astype(F32).reshape(LINE, LANES)
        below = jnp.where(slab == slabs - 1, 0.0, below)
        above = jnp.where(slab == 0, 0.0, above)
        out_ref[lines:, :] = jnp.concatenate([below, above], axis=0).astype(BF16)
    for copy in copies[3 * slabs :]:
        copy.wait()


def split_pieces(row, slabs, fields):
    lines = row.shape[1] // slabs // LANES
    half = slabs // 2
    rim = lines + TILE
    out_shape = [jax.ShapeDtypeStruct((half, rim, LANES), BF16)]
    out_shape += [jax.ShapeDtypeStruct((rim, LANES), BF16)] * half
    out_shape += [jax.ShapeDtypeStruct((lines, LANES), BF16)] * len(fields)
    return call(
        functools.partial(split_pieces_body, slabs, lines, len(fields)),
        "split_pieces",
        moved=6 * slabs * rim * LANES,
        in_specs=[IN_HBM] * (1 + len(fields)),
        out_specs=[IN_VMEM] * len(out_shape),
        out_shape=out_shape,
        scratch_shapes=[pltpu.VMEM((1, rim * LANES), BF16)] * slabs
        + [pltpu.SemaphoreType.DMA((3 * slabs + len(fields),))],
    )(row, *fields)


def join_pieces_body(pieces, half, lines, begun, arrays, *refs):
    row_ref, helds, sems = refs[begun + arrays], refs[begun + arrays + 1 : -1], refs[-1]
    copies = []
    for (array, lead, at), held in zip(pieces, helds):
        ref = refs[begun + array]
        piece = ref[...] if lead is None else ref[lead]
        held[...] = piece.reshape(held.shape)
        start = device_at(at, half) * lines * LANES
        target = row_ref.at[:, pl.ds(pl.multiple_of(start, GRID_Y), held.shape[1])]
        copies.append(pltpu.make_async_copy(held, target, sems.at[len(copies)]))
        copies[-1].start()
    for copy in copies:
        copy.wait()


def join_pieces(row, slabs, arrays, pieces):
    sizes = [arrays[piece[0]].shape[-2] * LANES for piece in pieces]
    begun = [] if row is None else [row]
    return call(
        functools.partial(join_pieces_body, pieces, slabs // 2, NCELL // slabs // LANES, len(begun), len(arrays)),
        "join_pieces",
        moved=6 * sum(sizes),
        in_specs=[IN_HBM] * len(begun) + [IN_VMEM] * len(arrays),
        out_specs=IN_HBM,
        out_shape=jax.ShapeDtypeStruct((1, NCELL), BF16),
        input_output_aliases={0: 0} if begun else {},
        scratch_shapes=[pltpu.VMEM((1, size), BF16) for size in sizes] + [pltpu.SemaphoreType.DMA((len(sizes),))],
    )(*begun, *arrays)


def owners(total, dtype):
    wide = total * TILE
    row = lax.broadcasted_iota(jnp.int32, (wide, total), 0)
    col = lax.broadcasted_iota(jnp.int32, (wide, total), 1)
    return (device_at(row // TILE, total // 2) == col).astype(dtype)


def gram_pieces_body(lines, total, near_ref, *refs):
    half = total // 2
    pieces, out_ref, pairs = refs[:half], refs[-2], refs[-1]
    wide = total * TILE
    tiles = 4
    pairs[...] = jnp.zeros_like(pairs)

    def step(i, carry):
        parts = []
        for t in range(tiles):
            at = lines_of((i * tiles + t) * TILE, TILE)
            near = near_ref[:, at, :].reshape(wide // 2, LANES)
            parts.append(jnp.concatenate([near] + [piece[at, :] for piece in pieces], axis=0))
        block = jnp.concatenate(parts, axis=1)
        pairs[...] += lax.dot_general(block, block, (((1,), (1,)), ((), ())), preferred_element_type=F32)
        return carry

    lax.fori_loop(0, lines // TILE // tiles, step, 0)
    equal = jnp.where(same_line(total), pairs[...], 0.0)
    exact = {"precision": lax.Precision.HIGHEST, "preferred_element_type": F32}
    owner = owners(total, F32)
    half_way = jnp.dot(equal, owner, **exact)
    gram = lax.dot_general(owner, half_way, (((0,), (0,)), ((), ())), **exact)
    gram = jnp.concatenate([gram, jnp.zeros((total, LANES - total), F32)], axis=1)
    out_ref[...] = jnp.broadcast_to(gram[None], out_ref.shape)


def gram_pieces(near, far, lines, gates):
    total = 2 * len(far)
    wide = total * TILE
    return call(
        functools.partial(gram_pieces_body, lines, total),
        "gram_pieces",
        flops=2 * wide * wide * LANES * (lines // TILE),
        moved=2 * total * lines * LANES,
        in_specs=[IN_VMEM] * (1 + len(far)) + [IN_HBM] * len(gates),
        out_specs=IN_VMEM,
        out_shape=jax.ShapeDtypeStruct((total, total, LANES), F32),
        scratch_shapes=[pltpu.VMEM((wide, wide), F32)],
    )(near, *far, *gates)


def gradient_pieces_body(views, arrays, numbers, *refs):
    observed, precision, *number_refs = refs[arrays : arrays + 2 + numbers]
    out_ref, rows_ref, grads, sems = refs[-4:]
    for n, number_ref in enumerate(number_refs):
        rows_ref[n : n + 1, :] = jnp.full((1, LANES), number_ref[0], F32)
    count = observed.shape[0]
    rows = BLOCK // LINE
    shape = (rows, LINE, LANES)
    lane = lax.broadcasted_iota(jnp.int32, (1, LINE, LANES), 2)
    line = lax.broadcasted_iota(jnp.int32, (1, LINE, LANES), 1)
    steps = count // BLOCK

    def store(i):
        at = lines_of(i * BLOCK, BLOCK)
        return pltpu.make_async_copy(grads.at[:, at, :], out_ref.at[:, at, :], sems.at[i])

    def step(i, carry):
        start = i * BLOCK
        at = lines_of(start, BLOCK)
        obs = observed[at, :].astype(F32).reshape(shape)
        prec = precision[at, :].astype(F32).reshape(shape)
        for p, (array, lead, base) in enumerate(views):

            def load(begin, size):
                part = lines_of(base + begin, size)
                value = refs[array][part, :] if lead is None else refs[array][lead, part, :]
                return value.astype(F32)

            here = load(start, BLOCK)
            before = load(jnp.where(i == 0, count, start - TILE), TILE)
            after = load(start + BLOCK, TILE)
            above = jnp.concatenate([before[LINE:], here[:-LINE]], axis=0).reshape(shape)
            below = jnp.concatenate([here[LINE:], after[:LINE]], axis=0).reshape(shape)
            field = here.reshape(shape)
            turned = pltpu.roll(field, 1, 2)
            carried = jnp.where(line == 0, 0.0, pltpu.roll(turned, 1, 1))
            left = jnp.where(lane == 0, carried, turned)
            turned = pltpu.roll(field, LANES - 1, 2)
            carried = jnp.where(line == LINE - 1, 0.0, pltpu.roll(turned, LINE - 1, 1))
            right = jnp.where(lane == LANES - 1, carried, turned)
            laplace = (4.0 + mass_term) * field - (below + above + right + left)
            squash = jnp.tanh(field)
            result = prec * (obs - squash) * (1.0 - squash * squash) - prior_scale * laplace
            grads[p, at, :] = result.reshape(BLOCK, LANES).astype(BF16)
        store(i).start()
        return carry

    def finish(i, carry):
        store(i).wait()
        return carry

    lax.fori_loop(0, steps, step, 0)
    lax.fori_loop(0, steps, finish, 0)


def gradient_pieces(arrays, views, observed, precision, numbers):
    count = observed.shape[0]
    out = pltpu.HBM((len(views), count, LANES), BF16)
    size = len(views) * count * LANES
    return call(
        functools.partial(gradient_pieces_body, views, len(arrays), len(numbers)),
        "gradient_pieces",
        flops=30 * size,
        moved=8 * size,
        in_specs=[IN_VMEM] * (len(arrays) + 2)
        + [pl.BlockSpec(memory_space=pltpu.SMEM)] * len(numbers),
        out_specs=[IN_HBM, IN_VMEM],
        out_shape=[out, jax.ShapeDtypeStruct((8, LANES), F32)],
        scratch_shapes=[pltpu.VMEM(out.shape, BF16), pltpu.SemaphoreType.DMA((count // BLOCK,))],
    )(*arrays, observed, precision, *numbers)


def mix(mixer, own, numbers_ref, total, states, slopes):
    high = mixer.shape[0]
    rate = numbers_ref[2:3, :1] / total
    coeff = 2.0 * numbers_ref[1:2, :1] / numbers_ref[:1, :1]
    both = jnp.concatenate([slopes, states], axis=1)
    mixed = jnp.dot(mixer[...], both, preferred_element_type=F32)
    drive, pulled = mixed[:, :LANES], mixed[:, LANES:]
    return (states[:high].astype(F32) * own[...] + rate * (drive - coeff * pulled)).astype(BF16)


def update_pieces_body(half, lines, groups, near_ref, *refs):
    total = 2 * half
    far_refs, numbers_ref, grams_ref, refs = refs[:half], refs[half], refs[half + 1], refs[half + 2 :]
    group_refs, near_out, far_outs = refs[: len(groups)], refs[-5 - half], refs[-4 - half : -4]
    mixer, own, grads, sems = refs[-4:]
    wide = total * TILE
    high = half * TILE
    fetches = []
    for group, group_ref in zip(groups, group_refs):
        for j, at in enumerate(group):
            fetches.append(pltpu.make_async_copy(group_ref.at[j], grads.at[at], sems.at[len(fetches)]))
    for fetch in fetches:
        fetch.start()
    gram = jnp.sum(grams_ref[...], axis=0)[:, :total]
    spread, anneal, step_size = (numbers_ref[k : k + 1, :1] for k in range(3))
    rate = step_size / total
    coeff = 2.0 * anneal / spread
    row = lax.broadcasted_iota(jnp.int32, (total, total), 0)
    col = lax.broadcasted_iota(jnp.int32, (total, total), 1)
    diagonal = jnp.where(row == col, gram, 0.0)
    down = jnp.sum(diagonal, axis=1, keepdims=True)
    across = jnp.sum(diagonal, axis=0, keepdims=True)
    kernel = jnp.exp(-(down + across - 2.0 * gram) / (spread * NCELL)).astype(BF16)
    owner = owners(total, BF16)
    half_way = jnp.dot(owner, kernel, preferred_element_type=F32).astype(BF16)
    full = lax.dot_general(half_way, owner, (((1,), (1,)), ((), ())), preferred_element_type=F32)
    full = jnp.where(same_line(total), full, 0.0)
    mixer[...] = full.astype(BF16)
    ksum = jnp.sum(full, axis=1, keepdims=True)
    own[...] = jnp.broadcast_to(1.0 + rate * coeff * ksum, (wide, LANES))
    for fetch in fetches:
        fetch.wait()

    def step(i, carry):
        for t in range(BLOCK // TILE):
            at = i * BLOCK + t * TILE
            part = lines_of(at, TILE)
            states = [near_ref[:, part, :].reshape(high, LANES)] + [ref[part, :] for ref in far_refs]
            slopes = grads[:, part, :].reshape(wide, LANES)
            new = mix(mixer, own, numbers_ref, total, jnp.concatenate(states, axis=0), slopes)
            near_out[:, part, :] = new[:high].reshape(half, TILE, LANES)
            for x, far_out in enumerate(far_outs):
                far_out[part, :] = new[high + x * TILE : high + (x + 1) * TILE]
        return carry

    lax.fori_loop(0, lines // BLOCK, step, 0)


def update_pieces(numbers, grams, near, far, grads, groups, lines):
    half = len(far)
    total = 2 * half
    wide = total * TILE
    out_shape = [jax.ShapeDtypeStruct((half, lines, LANES), BF16)]
    out_shape += [jax.ShapeDtypeStruct((lines, LANES), BF16)] * half
    return call(
        functools.partial(update_pieces_body, half, lines, groups),
        "update_pieces",
        flops=4 * wide * wide * LANES * (lines // TILE),
        moved=6 * total * lines * LANES,
        in_specs=[IN_VMEM] * (half + 3) + [IN_HBM] * len(groups),
        out_specs=[IN_VMEM] * len(out_shape),
        out_shape=out_shape,
        scratch_shapes=[
            pltpu.VMEM((wide, wide), BF16),
            pltpu.VMEM((wide, LANES), F32),
            pltpu.VMEM((total, lines, LANES), BF16),
            pltpu.SemaphoreType.DMA((total,)),
        ],
    )(near, *far, numbers, grams, *grads)


def exchange(piece, k, slabs):
    return lax.ppermute(piece, "slab", [(i, i ^ k) for i in range(slabs)])


def swap_near(pieces, slabs):
    groups = [list(range(slabs // 2)), list(range(slabs // 2, slabs))]
    return lax.all_to_all(pieces, "slab", 0, 0, axis_index_groups=groups, tiled=True)


GRADIENTS = ((8, 9, 10, 11), (12, 13, 14, 15), (0, 1, 2, 3, 4, 5, 6, 7))


def by_halves(particles, observed, precision, spread, anneal, step_size):
    slabs = lax.axis_size("slab")
    half = slabs // 2
    lines = NCELL // slabs // LANES
    row = in_hbm(particles)
    fields = [in_hbm(field.reshape(-1, LANES)) for field in (observed, precision)]
    near, *far = split_pieces(row, slabs, fields)
    far, (obs, prec) = far[:half], far[half:]
    near = swap_near(near, slabs)
    far = [exchange(piece, half + x, slabs) for x, piece in enumerate(far)]
    grads = []
    numbers = [spread, anneal, step_size]
    for group in GRADIENTS:
        if group[0] < half:
            arrays, views = [near], [(0, k, 0) for k in group]
        else:
            arrays, views = [far[k - half] for k in group], [(j, None, 0) for j in range(len(group))]
        slopes, rows = gradient_pieces(arrays, tuple(views), obs, prec, [] if grads else numbers)
        grads.append(in_hbm(slopes))
        numbers = numbers if len(grads) > 1 else rows
    grams = swap(gram_pieces(near, far, lines, grads[:1]))
    new_near, *new_far = update_pieces(numbers, grams, near, far, grads, GRADIENTS, lines)
    new_near = swap_near(new_near, slabs)
    new_far = [exchange(piece, half + x, slabs) for x, piece in enumerate(new_far)]
    row = join_pieces(None, slabs, [new_near], [(0, k, k) for k in range(half)])
    for group in ((0, 1, 2, 3), (4, 5)):
        pieces = [(n, None, half + x) for n, x in enumerate(group)]
        row = join_pieces(row, slabs, [new_far[x] for x in group], pieces)
    return join_pieces(row, slabs, new_far[6:], [(n, None, half + 6 + n) for n in range(half - 6)])


def on_device(particles, observed, precision, spread, anneal, step_size):
    slabs = lax.axis_size("slab")
    total = particles.shape[0] * slabs
    lines = NCELL // slabs // LANES
    if slabs == 16:
        return by_halves(particles, observed, precision, spread, anneal, step_size)
    sent, begun = cuts(lines)
    fields = [observed.reshape(-1, LANES), precision.reshape(-1, LANES)]
    numbers = [spread, anneal, step_size]
    first, obs, prec, scalars = split_row(particles, slabs, 0, sent, True, fields, numbers, [])
    parts = [swap(first)]
    if sent < lines:
        parts += [swap(split_row(particles, slabs, sent, lines, False, [], [], [scalars])[0])]
    if total * TILE > 256:
        grads = slab_gradient(parts, obs, prec, lines, 0, lines)
        states = jnp.concatenate([parts[0][:, :sent]] + parts[1:], axis=1)
        new = plain_update(spread, anneal, step_size, states, grads)
        return join_row(swap(new), lines, 0, None)
    if sent == lines:
        grads = slab_gradient(parts, obs, prec, lines, 0, lines)
        grams = swap(slab_gram(parts[0], lines, slabs, [], []))
        new = slab_update(scalars, grams, parts, grads, 0, lines, [])
        return join_row(swap(new), lines, 0, None)
    gram = slab_gram(parts[0], sent, 1, [], [])
    early = slab_gradient(parts[:1], obs, prec, lines, 0, begun)
    grams = swap(slab_gram(parts[1], lines - sent, slabs, [gram], [early]))
    late = slab_gradient(parts, obs, prec, lines, begun, lines)
    new = slab_update(scalars, grams, parts[:1], early, 0, begun, [])
    rest = slab_update(scalars, grams, parts, late, begun, lines, [new])
    row = join_row(swap(new), lines, 0, None)
    return join_row(swap(rest), lines, begun, row)


def solution(mesh):
    in_specs = (
        P(("groups", "slab"), None),
        P("groups"),
        P("groups"),
        P("groups"),
        P("groups"),
        P("groups"),
    )
    out_specs = P(("groups", "slab"), None)
    return jax.shard_map(
        on_device, mesh=mesh, in_specs=in_specs, out_specs=out_specs, check_vma=False
    )
```

```python
import functools

import jax
import jax.numpy as jnp
from jax import lax
from jax.experimental import pallas as pl
from jax.experimental.pallas import tpu as pltpu
from jax.sharding import PartitionSpec as P

GRID_X = 1024
GRID_Y = 1024
NCELL = 1048576
LANES = 128
LINE = GRID_Y // LANES
TILE = 16

prior_scale = 0.25
mass_term = 1.0

F32 = jnp.float32
BF16 = jnp.bfloat16
MIB = 1024 * 1024


def call(body, name, flops=0, moved=0, limit=16, **kwargs):
    return pl.pallas_call(
        body,
        name=name,
        compiler_params=pltpu.CompilerParams(vmem_limit_bytes=limit * MIB),
        cost_estimate=pl.CostEstimate(flops=flops, bytes_accessed=moved, transcendentals=0),
        **kwargs,
    )


IN_VMEM = pl.BlockSpec(memory_space=pltpu.VMEM)
IN_HBM = pl.BlockSpec(memory_space=pltpu.HBM)


def in_hbm(array):
    return pltpu.with_memory_space_constraint(array, pltpu.HBM)


BLOCK = 4 * TILE


def cuts(lines):
    if lines % (8 * BLOCK):
        return lines, lines
    return lines * 3 // 4, lines * 3 // 4 - BLOCK


def split_body(lines, begin, rim, fields, numbers, row_ref, *refs):
    field_refs, number_refs = refs[:fields], refs[fields : fields + numbers]
    out_ref, *slab_refs, rows_ref = refs[-7 - fields : -5]
    held, edges, sems, edge_sems, field_sems = refs[-5:]
    for k, number_ref in enumerate(number_refs):
        rows_ref[k : k + 1, :] = jnp.broadcast_to(number_ref[...].reshape(1, 1), (1, LANES))
    slabs, count, _ = out_ref.shape
    count -= TILE * rim
    size = count * LANES
    cells = lines * LANES

    def part(slab):
        source = row_ref.at[:, pl.ds(slab * cells + begin * LANES, size)]
        return pltpu.make_async_copy(source, held.at[:, pl.ds(slab * size, size)], sems.at[slab])

    def edge(slab):
        source = row_ref.at[:, pl.ds(slab * cells - GRID_Y, GRID_Y)]
        return pltpu.make_async_copy(source, edges.at[:, pl.ds(slab * GRID_Y, GRID_Y)], edge_sems.at[slab])

    def grid_row(ref, start):
        return ref[:, pl.ds(start, GRID_Y)].astype(F32).reshape(LINE, LANES)

    for slab in range(slabs):
        part(slab).start()
        if rim and slab:
            edge(slab).start()
    mine = pl.ds(pl.multiple_of(lax.axis_index("slab") * lines, TILE), lines)
    fetches = [
        pltpu.make_async_copy(source.at[mine, :], target, field_sems.at[k])
        for k, (source, target) in enumerate(zip(field_refs, slab_refs))
    ]
    for fetch in fetches:
        fetch.start()
    part(0).wait()
    outside = jnp.zeros((LINE, LANES), F32)
    for slab in range(slabs):
        if slab + 1 < slabs:
            part(slab + 1).wait()
        out_ref[slab, :count, :] = held[:, pl.ds(slab * size, size)].reshape(count, LANES)
        if rim:
            if slab:
                edge(slab).wait()
            below = grid_row(held, (slab + 1) * size) if slab + 1 < slabs else outside
            above = grid_row(edges, slab * GRID_Y) if slab else outside
            out_ref[slab, count:, :] = jnp.concatenate([below, above], axis=0).astype(BF16)
    for fetch in fetches:
        fetch.wait()


def split_row(row, slabs, begin, end, rim, fields, numbers, earlier):
    lines = row.shape[1] // slabs // LANES
    count = end - begin
    return call(
        functools.partial(split_body, lines, begin, rim, len(fields), len(numbers)),
        "split_row",
        moved=6 * slabs * count * LANES,
        in_specs=[IN_HBM] * (1 + len(fields)) + [IN_VMEM] * len(numbers) + [IN_HBM] * len(earlier),
        out_specs=[IN_VMEM] * (2 + len(fields)),
        out_shape=[jax.ShapeDtypeStruct((slabs, count + TILE * rim, LANES), BF16)]
        + [jax.ShapeDtypeStruct((lines, LANES), BF16)] * len(fields)
        + [jax.ShapeDtypeStruct((8, LANES), F32)],
        scratch_shapes=[
            pltpu.VMEM((1, slabs * count * LANES), BF16),
            pltpu.VMEM((1, slabs * GRID_Y), BF16),
            pltpu.SemaphoreType.DMA((slabs,)),
            pltpu.SemaphoreType.DMA((slabs,)),
            pltpu.SemaphoreType.DMA((2,)),
        ],
    )(row, *fields, *numbers, *earlier)


def join_body(lines, begin, slabs_ref, *refs):
    row_ref, held, sems = refs[-3:]
    slabs, count, _ = slabs_ref.shape
    size = count * LANES
    copies = []
    for slab in range(slabs):
        at = pl.ds(slab * size, size)
        held[:, at] = slabs_ref[slab].reshape(1, size)
        target = row_ref.at[:, pl.ds((slab * lines + begin) * LANES, size)]
        copies.append(pltpu.make_async_copy(held.at[:, at], target, sems.at[slab]))
        copies[-1].start()
    for copy in copies:
        copy.wait()


def join_row(slabs, lines, begin, row):
    total, count, _ = slabs.shape
    begun = [] if row is None else [row]
    return call(
        functools.partial(join_body, lines, begin),
        "join_row",
        moved=6 * slabs.size,
        in_specs=[IN_VMEM] + [IN_HBM] * len(begun),
        out_specs=IN_HBM,
        out_shape=jax.ShapeDtypeStruct((1, total * lines * LANES), BF16),
        input_output_aliases={1: 0} if begun else {},
        scratch_shapes=[pltpu.VMEM((1, slabs.size), BF16), pltpu.SemaphoreType.DMA((total,))],
    )(slabs, *begun)


def same_line(total):
    wide = total * TILE
    row = lax.broadcasted_iota(jnp.int32, (wide, wide), 0)
    col = lax.broadcasted_iota(jnp.int32, (wide, wide), 1)
    return row % TILE == col % TILE


def members(total, dtype):
    wide = total * TILE
    row = lax.broadcasted_iota(jnp.int32, (wide, total), 0)
    col = lax.broadcasted_iota(jnp.int32, (wide, total), 1)
    return (row // TILE == col).astype(dtype)


def gram_body(steps, tiles, parts, states_ref, *refs):
    out_ref, pairs = refs[-2:]
    total = states_ref.shape[0]
    wide = total * TILE
    pairs[...] = jnp.zeros_like(pairs)

    def step(i, carry):
        parts = [
            states_ref[:, pl.ds(pl.multiple_of((i * tiles + t) * TILE, TILE), TILE), :].reshape(wide, LANES)
            for t in range(tiles)
        ]
        block = jnp.concatenate(parts, axis=1)
        pairs[...] += lax.dot_general(block, block, (((1,), (1,)), ((), ())), preferred_element_type=F32)
        return carry

    lax.fori_loop(0, steps, step, 0)
    equal = jnp.where(same_line(total), pairs[...], 0.0)
    rows = jnp.sum(equal.reshape(total, TILE, wide), axis=1)
    gram = jnp.dot(rows, members(total, F32), precision=lax.Precision.HIGHEST, preferred_element_type=F32)
    gram = jnp.concatenate([gram, jnp.zeros((total, LANES - total), F32)], axis=1)
    for part_ref in refs[:parts]:
        gram += part_ref[0]
    out_ref[...] = jnp.broadcast_to(gram[None], out_ref.shape)


def slab_gram(states, lines, copies, parts, earlier):
    total = states.shape[0]
    wide = total * TILE
    tiles = min(8, lines // TILE)
    return call(
        functools.partial(gram_body, lines // TILE // tiles, tiles, len(parts)),
        "slab_gram",
        flops=2 * wide * wide * LANES * (lines // TILE),
        moved=2 * states.size,
        in_specs=[IN_VMEM] * (1 + len(parts)) + [IN_HBM] * len(earlier),
        out_specs=IN_VMEM,
        out_shape=jax.ShapeDtypeStruct((copies, total, LANES), F32),
        scratch_shapes=[pltpu.VMEM((wide, wide), F32)],
    )(states, *parts, *earlier)


def gradient_body(lines, begin, end, parts, *refs):
    observed, precision, out_ref, grads, sems = refs[parts:]
    total = grads.shape[0]
    first = refs[0].shape[1] - TILE
    rows = BLOCK // LINE
    group = 4
    shape = (rows, LINE, LANES)
    lane = lax.broadcasted_iota(jnp.int32, (1, LINE, LANES), 2)
    line = lax.broadcasted_iota(jnp.int32, (1, LINE, LANES), 1)

    def load(particle, at, count):
        ref, at = (refs[0], at) if at < first else (refs[1], at - first)
        return ref[particle, at : at + count, :].astype(F32)

    def rim(particle):
        return refs[0][particle, first:, :].astype(F32)

    stores = []
    for k, at in enumerate(range(begin, end, BLOCK)):
        mine = slice(at - begin, at - begin + BLOCK)
        obs = observed[at : at + BLOCK, :].astype(F32).reshape(shape)
        prec = precision[at : at + BLOCK, :].astype(F32).reshape(shape)

        def step(i, carry):
            for p in range(group):
                particle = i * group + p
                here = load(particle, at, BLOCK)
                before = load(particle, at - TILE, TILE) if at else rim(particle)
                after = load(particle, at + BLOCK, TILE) if at + BLOCK < lines else rim(particle)
                above = jnp.concatenate([before[LINE:], here[:-LINE]], axis=0).reshape(shape)
                below = jnp.concatenate([here[LINE:], after[:LINE]], axis=0).reshape(shape)
                field = here.reshape(shape)
                turned = pltpu.roll(field, 1, 2)
                carried = jnp.where(line == 0, 0.0, pltpu.roll(turned, 1, 1))
                left = jnp.where(lane == 0, carried, turned)
                turned = pltpu.roll(field, LANES - 1, 2)
                carried = jnp.where(line == LINE - 1, 0.0, pltpu.roll(turned, LINE - 1, 1))
                right = jnp.where(lane == LANES - 1, carried, turned)
                laplace = (4.0 + mass_term) * field - (below + above + right + left)
                squash = jnp.tanh(field)
                result = prec * (obs - squash) * (1.0 - squash * squash) - prior_scale * laplace
                grads[particle, mine, :] = result.reshape(BLOCK, LANES).astype(BF16)
            return carry

        lax.fori_loop(0, total // group, step, 0)
        stores.append(pltpu.make_async_copy(grads.at[:, mine, :], out_ref.at[:, mine, :], sems.at[k]))
        stores[-1].start()
    for store in stores:
        store.wait()


def slab_gradient(parts, observed, precision, lines, begin, end):
    total = parts[0].shape[0]
    count = end - begin
    out = jax.ShapeDtypeStruct((total, count, LANES), BF16)
    return call(
        functools.partial(gradient_body, lines, begin, end, len(parts)),
        "slab_gradient",
        flops=30 * out.size,
        moved=8 * out.size,
        in_specs=[IN_VMEM] * (len(parts) + 2),
        out_specs=IN_HBM,
        out_shape=out,
        scratch_shapes=[pltpu.VMEM(out.shape, BF16), pltpu.SemaphoreType.DMA((count // BLOCK,))],
    )(*parts, observed, precision)


def update_body(begin, end, parts, *refs):
    states_refs, refs = refs[:parts], refs[parts:]
    scalars_ref, grams_ref, grads_ref = refs[:3]
    out_ref, grads, mixer, own, sem = refs[-5:]
    total = out_ref.shape[0]
    wide = total * TILE
    fetch = pltpu.make_async_copy(grads_ref, grads, sem)
    fetch.start()
    gram = jnp.sum(grams_ref[...], axis=0)[:, :total]
    row = lax.broadcasted_iota(jnp.int32, (total, total), 0)
    col = lax.broadcasted_iota(jnp.int32, (total, total), 1)
    diagonal = jnp.where(row == col, gram, 0.0)
    down = jnp.sum(diagonal, axis=1, keepdims=True)
    across = jnp.sum(diagonal, axis=0, keepdims=True)
    member = members(total, BF16)
    spread, anneal, step_size = (scalars_ref[k : k + 1, :1] for k in range(3))
    rate = step_size / total
    coeff = 2.0 * anneal / spread
    kernel = jnp.exp(-(down + across - 2.0 * gram) / (spread * NCELL)).astype(BF16)
    ksum = jnp.sum(kernel.astype(F32), axis=1, keepdims=True)
    half = jnp.dot(member, kernel, preferred_element_type=F32).astype(BF16)
    full = lax.dot_general(half, member, (((1,), (1,)), ((), ())), preferred_element_type=F32)
    mixer[...] = jnp.where(same_line(total), full, 0.0).astype(BF16)
    gain = 1.0 + rate * coeff * ksum
    own[...] = jnp.broadcast_to(gain[:, :, None], (total, TILE, LANES)).reshape(wide, LANES)
    fetch.wait()

    done = 0
    for part, states_ref in enumerate(states_refs):
        have = states_ref.shape[1] - (0 if part else TILE)
        low = max(begin - done, 0)
        high = min(end - done, have)
        into = done - begin
        done += have

        def step(i, carry):
            for t in range(BLOCK // TILE):
                at = pl.multiple_of(i * BLOCK + t * TILE, TILE)
                there = pl.ds(pl.multiple_of(at + into, TILE), TILE)
                states = states_ref[:, pl.ds(at, TILE), :].reshape(wide, LANES)
                both = jnp.concatenate([grads[:, there, :].reshape(wide, LANES), states], axis=1)
                mixed = jnp.dot(mixer[...], both, preferred_element_type=F32)
                drive, pulled = mixed[:, :LANES], mixed[:, LANES:]
                new = states.astype(F32) * own[...] + rate * (drive - coeff * pulled)
                out_ref[:, there, :] = new.astype(BF16).reshape(total, TILE, LANES)
            return carry

        lax.fori_loop(low // BLOCK, high // BLOCK, step, 0)


def slab_update(scalars, grams, parts, grads, begin, end, earlier):
    total, count, _ = grads.shape
    wide = total * TILE
    return call(
        functools.partial(update_body, begin, end, len(parts)),
        "slab_update",
        flops=4 * wide * wide * LANES * (count // TILE),
        moved=6 * grads.size,
        in_specs=[IN_VMEM] * len(parts)
        + [IN_VMEM, IN_VMEM, IN_HBM]
        + [IN_HBM] * len(earlier),
        out_specs=IN_VMEM,
        out_shape=jax.ShapeDtypeStruct(grads.shape, BF16),
        scratch_shapes=[
            pltpu.VMEM(grads.shape, BF16),
            pltpu.VMEM((wide, wide), BF16),
            pltpu.VMEM((wide, LANES), F32),
            pltpu.SemaphoreType.DMA,
        ],
    )(*parts, scalars, grams, grads, *earlier)


def plain_update(spread, anneal, step_size, states, grads):
    total, lines, _ = grads.shape
    flat = states[:, :lines].reshape(total, -1)
    gram = lax.dot_general(flat, flat, (((1,), (1,)), ((), ())), preferred_element_type=F32)
    gram = lax.psum(gram, "slab")
    norms = jnp.diagonal(gram)
    kernel = jnp.exp(-(norms[:, None] + norms[None, :] - 2.0 * gram) / (spread[0] * NCELL)).astype(BF16)
    ksum = jnp.sum(kernel.astype(F32), axis=1)
    drive = jnp.dot(kernel, grads.reshape(total, -1), preferred_element_type=F32)
    pulled = jnp.dot(kernel, flat, preferred_element_type=F32)
    values = flat.astype(F32)
    repel = values * ksum[:, None] - pulled
    coeff = 2.0 * anneal[0] / spread[0]
    new = values + step_size[0] / total * (drive + coeff * repel)
    return new.astype(BF16).reshape(grads.shape)


def swap(slabs):
    return lax.all_to_all(slabs, "slab", split_axis=0, concat_axis=0, tiled=True)


def device_at(at, half):
    me = lax.axis_index("slab").astype(jnp.int32)
    return jnp.where(at < half, me - me % half + at, me ^ at)


def lines_of(start, count):
    return pl.ds(pl.multiple_of(start, TILE), count)


def split_pieces_body(positions, half, raw, lines, gates, fields, row_ref, *refs):
    field_refs, refs = refs[:fields], refs[fields + gates :]
    count = len(positions)
    out_refs, helds, sems = refs[: -count - 1], refs[-count - 1 : -1], refs[-1]
    me = lax.axis_index("slab").astype(jnp.int32)
    slab_refs = out_refs[len(out_refs) - 2 * fields :]
    fetches = []
    for n, target in enumerate(slab_refs):
        start = (me if n < fields else me ^ half) * lines
        source = field_refs[n % fields].at[lines_of(start, target.shape[0]), :]
        fetches.append(pltpu.make_async_copy(source, target, sems.at[5 * count + n]))
    cells = lines * LANES
    end = row_ref.shape[1]
    copies = []
    for at, held in zip(positions, helds):
        mine = []

        def fetch(start, size, to):
            source = row_ref.at[:, pl.ds(pl.multiple_of(start, GRID_Y), size)]
            sem = sems.at[len(copies) * 5 + len(mine)]
            mine.append(pltpu.make_async_copy(source, held.at[:, pl.ds(to, size)], sem))
            mine[-1].start()

        slab = device_at(at, half)
        fetch(slab * cells, cells, 0)
        fetch(jnp.minimum((slab + 1) * cells, end - GRID_Y), GRID_Y, cells)
        fetch(jnp.maximum(slab * cells - GRID_Y, 0), GRID_Y, cells + GRID_Y)
        if raw and at < half:
            other = slab ^ half
            fetch(other * cells, raw * LANES + GRID_Y, cells + 2 * GRID_Y)
            fetch(jnp.maximum(other * cells - GRID_Y, 0), GRID_Y, cells + 3 * GRID_Y + raw * LANES)
        copies.append(mine)

    def grid_row(held, at):
        return held[:, pl.ds(at, GRID_Y)].astype(F32).reshape(LINE, LANES)

    for fetch in fetches:
        fetch.start()
    for n, (at, held, mine) in enumerate(zip(positions, helds, copies)):
        out_ref = out_refs[1 + at - half] if at >= half else out_refs[0].at[at]
        for copy in mine:
            copy.wait()
        slab = device_at(at, half)
        out_ref[:lines, :] = held[:, :cells].reshape(lines, LANES)
        below = jnp.where(slab == end // cells - 1, 0.0, grid_row(held, cells))
        above = jnp.where(slab == 0, 0.0, grid_row(held, cells + GRID_Y))
        out_ref[lines : lines + TILE, :] = jnp.concatenate([below, above], axis=0).astype(BF16)
        if raw and at < half:
            start = cells + 2 * GRID_Y
            to = lines + TILE
            out_ref[to : to + raw, :] = held[:, start : start + raw * LANES].reshape(raw, LANES)
            below = grid_row(held, start + raw * LANES)
            above = jnp.where(slab ^ half == 0, 0.0, grid_row(held, start + raw * LANES + GRID_Y))
            out_ref[to + raw :, :] = jnp.concatenate([below, above], axis=0).astype(BF16)
    for fetch in fetches:
        fetch.wait()


def split_pieces(row, slabs, raw, fields):
    lines = row.shape[1] // slabs // LANES
    half = slabs // 2
    rim = lines + TILE
    size = rim + (raw + TILE if raw else 0)
    out_shape = [jax.ShapeDtypeStruct((half, size, LANES), BF16)]
    out_shape += [jax.ShapeDtypeStruct((rim, LANES), BF16)] * half
    out_shape += [jax.ShapeDtypeStruct((lines, LANES), BF16)] * len(fields)
    out_shape += [jax.ShapeDtypeStruct((max(raw, TILE), LANES), BF16)] * len(fields)
    return call(
        functools.partial(split_pieces_body, range(slabs), half, raw, lines, 0, len(fields)),
        "split_pieces",
        moved=6 * half * (size + rim) * LANES,
        in_specs=[IN_HBM] * (1 + len(fields)),
        out_specs=[IN_VMEM] * len(out_shape),
        out_shape=out_shape,
        scratch_shapes=[pltpu.VMEM((1, (size + TILE) * LANES), BF16)] * half
        + [pltpu.VMEM((1, (rim + TILE) * LANES), BF16)] * half
        + [pltpu.SemaphoreType.DMA((5 * slabs + 2 * len(fields),))],
    )(row, *fields)


def join_pieces_body(pieces, half, lines, begun, arrays, *refs):
    row_ref, helds, sems = refs[begun + arrays], refs[begun + arrays + 1 : -1], refs[-1]
    copies = []
    for (array, lead, at, across, begin), held in zip(pieces, helds):
        ref = refs[begun + array]
        piece = ref[...] if lead is None else ref[lead]
        held[...] = piece.reshape(held.shape)
        me = lax.axis_index("slab").astype(jnp.int32)
        slab = me ^ half ^ at if across else device_at(at, half)
        start = (slab * lines + begin) * LANES
        target = row_ref.at[:, pl.ds(pl.multiple_of(start, GRID_Y), held.shape[1])]
        copies.append(pltpu.make_async_copy(held, target, sems.at[len(copies)]))
        copies[-1].start()
    for copy in copies:
        copy.wait()


def join_pieces(row, slabs, arrays, pieces):
    sizes = [arrays[piece[0]].shape[-2] * LANES for piece in pieces]
    begun = [] if row is None else [row]
    return call(
        functools.partial(join_pieces_body, pieces, slabs // 2, NCELL // slabs // LANES, len(begun), len(arrays)),
        "join_pieces",
        moved=6 * sum(sizes),
        in_specs=[IN_HBM] * len(begun) + [IN_VMEM] * len(arrays),
        out_specs=IN_HBM,
        out_shape=jax.ShapeDtypeStruct((1, NCELL), BF16),
        input_output_aliases={0: 0} if begun else {},
        scratch_shapes=[pltpu.VMEM((1, size), BF16) for size in sizes] + [pltpu.SemaphoreType.DMA((len(sizes),))],
    )(*begun, *arrays)


def owners(total, dtype):
    wide = total * TILE
    row = lax.broadcasted_iota(jnp.int32, (wide, total), 0)
    col = lax.broadcasted_iota(jnp.int32, (wide, total), 1)
    return (device_at(row // TILE, total // 2) == col).astype(dtype)


def gram_pieces_body(lines, total, near_ref, *refs):
    half = total // 2
    pieces, out_ref, pairs = refs[:half], refs[-2], refs[-1]
    wide = total * TILE
    tiles = 4
    pairs[...] = jnp.zeros_like(pairs)

    def step(i, carry):
        parts = []
        for t in range(tiles):
            at = lines_of((i * tiles + t) * TILE, TILE)
            near = near_ref[:, at, :].reshape(wide // 2, LANES)
            parts.append(jnp.concatenate([near] + [piece[at, :] for piece in pieces], axis=0))
        block = jnp.concatenate(parts, axis=1)
        pairs[...] += lax.dot_general(block, block, (((1,), (1,)), ((), ())), preferred_element_type=F32)
        return carry

    lax.fori_loop(0, lines // TILE // tiles, step, 0)
    equal = jnp.where(same_line(total), pairs[...], 0.0)
    exact = {"precision": lax.Precision.HIGHEST, "preferred_element_type": F32}
    owner = owners(total, F32)
    half_way = jnp.dot(equal, owner, **exact)
    gram = lax.dot_general(owner, half_way, (((0,), (0,)), ((), ())), **exact)
    gram = jnp.concatenate([gram, jnp.zeros((total, LANES - total), F32)], axis=1)
    out_ref[...] = jnp.broadcast_to(gram[None], out_ref.shape)


def gram_pieces(near, far, lines, gates, early):
    total = 2 * len(far)
    wide = total * TILE
    return call(
        functools.partial(gram_pieces_body, lines, total),
        "gram_pieces",
        flops=2 * wide * wide * LANES * (lines // TILE),
        moved=2 * total * lines * LANES,
        in_specs=[IN_VMEM] * (1 + len(far)) + [IN_HBM] * len(gates) + [IN_VMEM] * len(early),
        out_specs=IN_VMEM,
        out_shape=jax.ShapeDtypeStruct((total, total, LANES), F32),
        scratch_shapes=[pltpu.VMEM((wide, wide), F32)],
    )(near, *far, *gates, *early)


def gradient_pieces_body(views, arrays, numbers, *refs):
    observed, precision, *number_refs = refs[arrays : arrays + 2 + numbers]
    out_ref, rows_ref, grads, sems = refs[-4:]
    for n, number_ref in enumerate(number_refs):
        rows_ref[n : n + 1, :] = jnp.full((1, LANES), number_ref[0], F32)
    count = observed.shape[0]
    rows = BLOCK // LINE
    shape = (rows, LINE, LANES)
    lane = lax.broadcasted_iota(jnp.int32, (1, LINE, LANES), 2)
    line = lax.broadcasted_iota(jnp.int32, (1, LINE, LANES), 1)
    steps = count // BLOCK

    def store(i):
        at = lines_of(i * BLOCK, BLOCK)
        return pltpu.make_async_copy(grads.at[:, at, :], out_ref.at[:, at, :], sems.at[i])

    def step(i, carry):
        start = i * BLOCK
        at = lines_of(start, BLOCK)
        obs = observed[at, :].astype(F32).reshape(shape)
        prec = precision[at, :].astype(F32).reshape(shape)
        for p, (array, lead, base) in enumerate(views):

            def load(begin, size):
                part = lines_of(base + begin, size)
                value = refs[array][part, :] if lead is None else refs[array][lead, part, :]
                return value.astype(F32)

            here = load(start, BLOCK)
            before = load(jnp.where(i == 0, count, start - TILE), TILE)
            after = load(start + BLOCK, TILE)
            above = jnp.concatenate([before[LINE:], here[:-LINE]], axis=0).reshape(shape)
            below = jnp.concatenate([here[LINE:], after[:LINE]], axis=0).reshape(shape)
            field = here.reshape(shape)
            turned = pltpu.roll(field, 1, 2)
            carried = jnp.where(line == 0, 0.0, pltpu.roll(turned, 1, 1))
            left = jnp.where(lane == 0, carried, turned)
            turned = pltpu.roll(field, LANES - 1, 2)
            carried = jnp.where(line == LINE - 1, 0.0, pltpu.roll(turned, LINE - 1, 1))
            right = jnp.where(lane == LANES - 1, carried, turned)
            laplace = (4.0 + mass_term) * field - (below + above + right + left)
            squash = jnp.tanh(field)
            result = prec * (obs - squash) * (1.0 - squash * squash) - prior_scale * laplace
            grads[p, at, :] = result.reshape(BLOCK, LANES).astype(BF16)
        store(i).start()
        return carry

    def finish(i, carry):
        store(i).wait()
        return carry

    lax.fori_loop(0, steps, step, 0)
    lax.fori_loop(0, steps, finish, 0)


def gradient_pieces(arrays, views, observed, precision, numbers):
    count = observed.shape[0]
    out = pltpu.HBM((len(views), count, LANES), BF16)
    size = len(views) * count * LANES
    return call(
        functools.partial(gradient_pieces_body, views, len(arrays), len(numbers)),
        "gradient_pieces",
        flops=30 * size,
        moved=8 * size,
        in_specs=[IN_VMEM] * (len(arrays) + 2)
        + [pl.BlockSpec(memory_space=pltpu.SMEM)] * len(numbers),
        out_specs=[IN_HBM, IN_VMEM],
        out_shape=[out, jax.ShapeDtypeStruct((8, LANES), F32)],
        scratch_shapes=[pltpu.VMEM(out.shape, BF16), pltpu.SemaphoreType.DMA((count // BLOCK,))],
    )(*arrays, observed, precision, *numbers)


def raw_body(raw, lines, near_ref, *refs):
    out_ref, here_ref = refs[-2:]
    for k in range(near_ref.shape[0]):
        out_ref[k, :raw, :] = near_ref[k, :raw, :]
        below = near_ref[k, raw : raw + TILE, :].astype(F32)[:LINE]
        above = near_ref[k, lines : lines + TILE, :].astype(F32)[LINE:]
        out_ref[k, raw:, :] = jnp.concatenate([below, above], axis=0).astype(BF16)
        here_ref[k, :, :] = near_ref[k, lines + TILE :, :]


def raw_states(near, raw, lines, gates):
    out = jax.ShapeDtypeStruct((near.shape[0], raw + TILE, LANES), BF16)
    return call(
        functools.partial(raw_body, raw, lines),
        "raw_states",
        moved=8 * out.size,
        in_specs=[IN_VMEM] * (1 + len(gates)),
        out_specs=[IN_VMEM] * 2,
        out_shape=[out] * 2,
    )(near, *gates)


def mix(mixer, own, numbers_ref, total, states, slopes):
    high = mixer.shape[0]
    rate = numbers_ref[2:3, :1] / total
    coeff = 2.0 * numbers_ref[1:2, :1] / numbers_ref[:1, :1]
    both = jnp.concatenate([slopes, states], axis=1)
    mixed = jnp.dot(mixer[...], both, preferred_element_type=F32)
    drive, pulled = mixed[:, :LANES], mixed[:, LANES:]
    return (states[:high].astype(F32) * own[...] + rate * (drive - coeff * pulled)).astype(BF16)


def update_pieces_body(half, raw, lines, groups, near_ref, *refs):
    total = 2 * half
    far_refs, numbers_ref, grams_ref, refs = refs[:half], refs[half], refs[half + 1], refs[half + 2 :]
    group_refs, refs = refs[: len(groups)], refs[-half - 11 :]
    near_to, far_tos, mixer_to, own_to = refs[0], refs[1 : 1 + half], refs[1 + half], refs[2 + half]
    near_out, far_out, mixer, own, grads, sems, out_sems, last_sems = refs[3 + half :]
    wide = total * TILE
    high = half * TILE
    fetches = []
    for group, group_ref in zip(groups, group_refs):
        for j, at in enumerate(group):
            fetches.append(pltpu.make_async_copy(group_ref.at[j], grads.at[at], sems.at[len(fetches)]))
    for fetch in fetches:
        fetch.start()
    gram = jnp.sum(grams_ref[...], axis=0)[:, :total]
    spread, anneal, step_size = (numbers_ref[k : k + 1, :1] for k in range(3))
    rate = step_size / total
    coeff = 2.0 * anneal / spread
    row = lax.broadcasted_iota(jnp.int32, (total, total), 0)
    col = lax.broadcasted_iota(jnp.int32, (total, total), 1)
    diagonal = jnp.where(row == col, gram, 0.0)
    down = jnp.sum(diagonal, axis=1, keepdims=True)
    across = jnp.sum(diagonal, axis=0, keepdims=True)
    kernel = jnp.exp(-(down + across - 2.0 * gram) / (spread * NCELL)).astype(BF16)
    owner = owners(total, BF16)
    half_way = jnp.dot(owner, kernel, preferred_element_type=F32).astype(BF16)
    full = lax.dot_general(half_way, owner, (((1,), (1,)), ((), ())), preferred_element_type=F32)
    full = jnp.where(same_line(total), full, 0.0)
    mixer[...] = full.astype(BF16)
    ksum = jnp.sum(full, axis=1, keepdims=True)
    own[...] = jnp.broadcast_to(1.0 + rate * coeff * ksum, (wide, LANES))
    stores = [
        pltpu.make_async_copy(mixer, mixer_to, last_sems.at[0]),
        pltpu.make_async_copy(own, own_to, last_sems.at[1]),
    ]
    for store in stores:
        store.start()
    for fetch in fetches:
        fetch.wait()

    def sent(i, with_far):
        here = lines_of(i * BLOCK, BLOCK)
        copies = [pltpu.make_async_copy(near_out.at[:, here, :], near_to.at[:, here, :], out_sems.at[i, 0])]
        if with_far:
            there = lines_of(i * BLOCK - raw, BLOCK)
            for x, far_to in enumerate(far_tos):
                copies.append(pltpu.make_async_copy(far_out.at[x, there, :], far_to.at[there, :], out_sems.at[i, 1 + x]))
        return copies

    def step(with_far, i, carry):
        for t in range(BLOCK // TILE):
            at = i * BLOCK + t * TILE
            part = lines_of(at, TILE)
            states = [near_ref[:, part, :].reshape(high, LANES)] + [ref[part, :] for ref in far_refs]
            slopes = grads[:, part, :].reshape(wide, LANES)
            new = mix(mixer, own, numbers_ref, total, jnp.concatenate(states, axis=0), slopes)
            near_out[:, part, :] = new[:high].reshape(half, TILE, LANES)
            if with_far:
                far_out[:, lines_of(at - raw, TILE), :] = new[high:].reshape(half, TILE, LANES)
        for copy in sent(i, with_far):
            copy.start()
        return carry

    def finish(with_far, i, carry):
        for copy in sent(i, with_far):
            copy.wait()
        return carry

    first, last = raw // BLOCK, lines // BLOCK
    lax.fori_loop(0, first, functools.partial(step, False), 0)
    lax.fori_loop(first, last, functools.partial(step, True), 0)
    lax.fori_loop(0, first, functools.partial(finish, False), 0)
    lax.fori_loop(first, last, functools.partial(finish, True), 0)
    for store in stores:
        store.wait()


def update_pieces(numbers, grams, near, far, grads, groups, gates, raw, lines):
    half = len(far)
    total = 2 * half
    wide = total * TILE
    out_shape = [jax.ShapeDtypeStruct((half, lines, LANES), BF16)]
    out_shape += [jax.ShapeDtypeStruct((lines - raw, LANES), BF16)] * half
    out_shape += [jax.ShapeDtypeStruct((wide, wide), BF16), jax.ShapeDtypeStruct((wide, LANES), F32)]
    return call(
        functools.partial(update_pieces_body, half, raw, lines, groups),
        "update_pieces",
        flops=4 * wide * wide * LANES * (lines // TILE),
        moved=6 * total * lines * LANES,
        in_specs=[IN_VMEM] * (half + 3) + [IN_HBM] * len(groups) + [IN_VMEM] * len(gates),
        out_specs=[IN_HBM] * len(out_shape),
        out_shape=out_shape,
        scratch_shapes=[
            pltpu.VMEM((half, lines, LANES), BF16),
            pltpu.VMEM((half, lines - raw, LANES), BF16),
            pltpu.VMEM((wide, wide), BF16),
            pltpu.VMEM((wide, LANES), F32),
            pltpu.VMEM((total, lines, LANES), BF16),
            pltpu.SemaphoreType.DMA((total,)),
            pltpu.SemaphoreType.DMA((lines // BLOCK, 1 + half)),
            pltpu.SemaphoreType.DMA((2,)),
        ],
    )(near, *far, numbers, grams, *grads, *gates)


def update_raw_body(here_ref, across_ref, numbers_ref, mixer_ref, own_ref, grads_ref, *refs):
    out_refs, (news, mixer, own, grads, sems) = refs[:-5], refs[-5:]
    half, raw, _ = news.shape
    high = half * TILE
    fetches = [
        pltpu.make_async_copy(mixer_ref.at[pl.ds(0, high), :], mixer, sems.at[0]),
        pltpu.make_async_copy(own_ref.at[pl.ds(0, high), :], own, sems.at[1]),
        pltpu.make_async_copy(grads_ref, grads, sems.at[2]),
    ]
    for fetch in fetches:
        fetch.start()
    for fetch in fetches:
        fetch.wait()
    me = lax.axis_index("slab").astype(jnp.int32) % half

    def step(i, carry):
        for t in range(BLOCK // TILE):
            part = lines_of(i * BLOCK + t * TILE, TILE)
            states = [here_ref[:, part, :].reshape(high, LANES)]
            slopes = [grads[:half, part, :].reshape(high, LANES)]
            for x in range(half):
                states += [across_ref[me ^ x, part, :]]
                slopes += [grads[half + (me ^ x), part, :]]
            states, slopes = jnp.concatenate(states, axis=0), jnp.concatenate(slopes, axis=0)
            new = mix(mixer, own, numbers_ref, 2 * half, states, slopes)
            news[:, part, :] = new.reshape(half, TILE, LANES)
        return carry

    lax.fori_loop(0, raw // BLOCK, step, 0)
    for k, out_ref in enumerate(out_refs):
        out_ref[...] = news[me ^ k]


def update_raw(here, across, mixer, own, numbers, grads, raw):
    half = here.shape[0]
    wide = mixer.shape[0]
    return call(
        update_raw_body,
        "update_raw",
        flops=2 * mixer.size * LANES * (raw // TILE),
        moved=12 * half * raw * LANES,
        in_specs=[IN_VMEM] * 3 + [IN_HBM] * 3,
        out_specs=[IN_VMEM] * half,
        out_shape=[jax.ShapeDtypeStruct((raw, LANES), BF16)] * half,
        scratch_shapes=[
            pltpu.VMEM((half, raw, LANES), BF16),
            pltpu.VMEM((half * TILE, wide), BF16),
            pltpu.VMEM((half * TILE, LANES), F32),
            pltpu.VMEM((2 * half, raw, LANES), BF16),
            pltpu.SemaphoreType.DMA((3,)),
        ],
    )(here, across, numbers, mixer, own, grads)


def exchange(piece, k, slabs):
    return lax.ppermute(piece, "slab", [(i, i ^ k) for i in range(slabs)])


def swap_near(pieces, slabs):
    groups = [list(range(slabs // 2)), list(range(slabs // 2, slabs))]
    return lax.all_to_all(pieces, "slab", 0, 0, axis_index_groups=groups, tiled=True)


RAW = 128
GRADIENTS = ((8, 9, 10, 11), (12, 13, 14, 15), (0, 1, 2, 3, 4, 5, 6, 7))


def by_halves(particles, observed, precision, spread, anneal, step_size):
    slabs = lax.axis_size("slab")
    half = slabs // 2
    lines = NCELL // slabs // LANES
    row = in_hbm(particles)
    fields = [in_hbm(field.reshape(-1, LANES)) for field in (observed, precision)]
    near, *far = split_pieces(row, slabs, RAW, fields)
    far, (obs, prec, raw_obs, raw_prec) = far[:half], far[half:]
    near = swap_near(near, slabs)
    far = [exchange(piece, half + x, slabs) for x, piece in enumerate(far)]
    raw_near, here = raw_states(near, RAW, lines, far)
    across = exchange(raw_near, half, slabs)
    grads = []
    numbers = [spread, anneal, step_size]
    for group in GRADIENTS:
        if group[0] < half:
            arrays, views = [near], [(0, k, 0) for k in group]
        else:
            arrays, views = [far[k - half] for k in group], [(j, None, 0) for j in range(len(group))]
        slopes, rows = gradient_pieces(arrays, tuple(views), obs, prec, [] if grads else numbers)
        grads.append(in_hbm(slopes))
        numbers = numbers if len(grads) > 1 else rows
    grams = swap(gram_pieces(near, far, lines, grads[:1], [here]))
    new_near, *new_far = update_pieces(numbers, grams, near, far, grads, GRADIENTS, [across], RAW, lines)
    new_far, (mixer, own) = new_far[:half], new_far[half:]
    new_near = swap_near(new_near, slabs)
    new_far = [exchange(piece, half + x, slabs) for x, piece in enumerate(new_far)]
    views = [(0, k, 0) for k in range(half)] + [(1, k, 0) for k in range(half)]
    slopes, _ = gradient_pieces([here, across, new_far[2]], tuple(views), raw_obs, raw_prec, [])
    new_raw = update_raw(here, across, in_hbm(mixer), in_hbm(own), numbers, in_hbm(slopes), RAW)
    new_raw = [exchange(piece, k, slabs) if k else piece for k, piece in enumerate(new_raw)]
    row = join_pieces(None, slabs, [new_near], [(0, k, k, False, 0) for k in range(half)])
    for group in ((0, 1, 2, 3), (4, 5)):
        pieces = [(n, None, half + x, False, RAW) for n, x in enumerate(group)]
        row = join_pieces(row, slabs, [new_far[x] for x in group], pieces)
    row = join_pieces(row, slabs, new_raw, [(k, None, k, True, 0) for k in range(half)])
    return join_pieces(row, slabs, new_far[6:], [(n, None, half + 6 + n, False, RAW) for n in range(half - 6)])


def on_device(particles, observed, precision, spread, anneal, step_size):
    slabs = lax.axis_size("slab")
    total = particles.shape[0] * slabs
    lines = NCELL // slabs // LANES
    if slabs == 16:
        return by_halves(particles, observed, precision, spread, anneal, step_size)
    sent, begun = cuts(lines)
    fields = [observed.reshape(-1, LANES), precision.reshape(-1, LANES)]
    numbers = [spread, anneal, step_size]
    first, obs, prec, scalars = split_row(particles, slabs, 0, sent, True, fields, numbers, [])
    parts = [swap(first)]
    if sent < lines:
        parts += [swap(split_row(particles, slabs, sent, lines, False, [], [], [scalars])[0])]
    if total * TILE > 256:
        grads = slab_gradient(parts, obs, prec, lines, 0, lines)
        states = jnp.concatenate([parts[0][:, :sent]] + parts[1:], axis=1)
        new = plain_update(spread, anneal, step_size, states, grads)
        return join_row(swap(new), lines, 0, None)
    if sent == lines:
        grads = slab_gradient(parts, obs, prec, lines, 0, lines)
        grams = swap(slab_gram(parts[0], lines, slabs, [], []))
        new = slab_update(scalars, grams, parts, grads, 0, lines, [])
        return join_row(swap(new), lines, 0, None)
    gram = slab_gram(parts[0], sent, 1, [], [])
    early = slab_gradient(parts[:1], obs, prec, lines, 0, begun)
    grams = swap(slab_gram(parts[1], lines - sent, slabs, [gram], [early]))
    late = slab_gradient(parts, obs, prec, lines, begun, lines)
    new = slab_update(scalars, grams, parts[:1], early, 0, begun, [])
    rest = slab_update(scalars, grams, parts, late, begun, lines, [new])
    row = join_row(swap(new), lines, 0, None)
    return join_row(swap(rest), lines, begun, row)


def solution(mesh):
    in_specs = (
        P(("groups", "slab"), None),
        P("groups"),
        P("groups"),
        P("groups"),
        P("groups"),
        P("groups"),
    )
    out_specs = P(("groups", "slab"), None)
    return jax.shard_map(
        on_device, mesh=mesh, in_specs=in_specs, out_specs=out_specs, check_vma=False
    )
```

```python
import functools

import jax
import jax.numpy as jnp
from jax import lax
from jax.experimental import pallas as pl
from jax.experimental.pallas import tpu as pltpu
from jax.sharding import PartitionSpec as P

GRID_X = 1024
GRID_Y = 1024
NCELL = 1048576
LANES = 128
LINE = GRID_Y // LANES
TILE = 16

prior_scale = 0.25
mass_term = 1.0

F32 = jnp.float32
BF16 = jnp.bfloat16
MIB = 1024 * 1024


def call(body, name, flops=0, moved=0, limit=16, **kwargs):
    return pl.pallas_call(
        body,
        name=name,
        compiler_params=pltpu.CompilerParams(vmem_limit_bytes=limit * MIB),
        cost_estimate=pl.CostEstimate(flops=flops, bytes_accessed=moved, transcendentals=0),
        **kwargs,
    )


IN_VMEM = pl.BlockSpec(memory_space=pltpu.VMEM)
IN_HBM = pl.BlockSpec(memory_space=pltpu.HBM)


def in_hbm(array):
    return pltpu.with_memory_space_constraint(array, pltpu.HBM)


BLOCK = 4 * TILE


def cuts(lines):
    if lines % (8 * BLOCK):
        return lines, lines
    return lines * 3 // 4, lines * 3 // 4 - BLOCK


def split_body(lines, begin, rim, fields, numbers, row_ref, *refs):
    field_refs, number_refs = refs[:fields], refs[fields : fields + numbers]
    out_ref, *slab_refs, rows_ref = refs[-7 - fields : -5]
    held, edges, sems, edge_sems, field_sems = refs[-5:]
    for k, number_ref in enumerate(number_refs):
        rows_ref[k : k + 1, :] = jnp.broadcast_to(number_ref[...].reshape(1, 1), (1, LANES))
    slabs, count, _ = out_ref.shape
    count -= TILE * rim
    size = count * LANES
    cells = lines * LANES

    def part(slab):
        source = row_ref.at[:, pl.ds(slab * cells + begin * LANES, size)]
        return pltpu.make_async_copy(source, held.at[:, pl.ds(slab * size, size)], sems.at[slab])

    def edge(slab):
        source = row_ref.at[:, pl.ds(slab * cells - GRID_Y, GRID_Y)]
        return pltpu.make_async_copy(source, edges.at[:, pl.ds(slab * GRID_Y, GRID_Y)], edge_sems.at[slab])

    def grid_row(ref, start):
        return ref[:, pl.ds(start, GRID_Y)].astype(F32).reshape(LINE, LANES)

    for slab in range(slabs):
        part(slab).start()
        if rim and slab:
            edge(slab).start()
    mine = pl.ds(pl.multiple_of(lax.axis_index("slab") * lines, TILE), lines)
    fetches = [
        pltpu.make_async_copy(source.at[mine, :], target, field_sems.at[k])
        for k, (source, target) in enumerate(zip(field_refs, slab_refs))
    ]
    for fetch in fetches:
        fetch.start()
    part(0).wait()
    outside = jnp.zeros((LINE, LANES), F32)
    for slab in range(slabs):
        if slab + 1 < slabs:
            part(slab + 1).wait()
        out_ref[slab, :count, :] = held[:, pl.ds(slab * size, size)].reshape(count, LANES)
        if rim:
            if slab:
                edge(slab).wait()
            below = grid_row(held, (slab + 1) * size) if slab + 1 < slabs else outside
            above = grid_row(edges, slab * GRID_Y) if slab else outside
            out_ref[slab, count:, :] = jnp.concatenate([below, above], axis=0).astype(BF16)
    for fetch in fetches:
        fetch.wait()


def split_row(row, slabs, begin, end, rim, fields, numbers, earlier):
    lines = row.shape[1] // slabs // LANES
    count = end - begin
    return call(
        functools.partial(split_body, lines, begin, rim, len(fields), len(numbers)),
        "split_row",
        moved=6 * slabs * count * LANES,
        in_specs=[IN_HBM] * (1 + len(fields)) + [IN_VMEM] * len(numbers) + [IN_HBM] * len(earlier),
        out_specs=[IN_VMEM] * (2 + len(fields)),
        out_shape=[jax.ShapeDtypeStruct((slabs, count + TILE * rim, LANES), BF16)]
        + [jax.ShapeDtypeStruct((lines, LANES), BF16)] * len(fields)
        + [jax.ShapeDtypeStruct((8, LANES), F32)],
        scratch_shapes=[
            pltpu.VMEM((1, slabs * count * LANES), BF16),
            pltpu.VMEM((1, slabs * GRID_Y), BF16),
            pltpu.SemaphoreType.DMA((slabs,)),
            pltpu.SemaphoreType.DMA((slabs,)),
            pltpu.SemaphoreType.DMA((2,)),
        ],
    )(row, *fields, *numbers, *earlier)


def join_body(lines, begin, slabs_ref, *refs):
    row_ref, held, sems = refs[-3:]
    slabs, count, _ = slabs_ref.shape
    size = count * LANES
    copies = []
    for slab in range(slabs):
        at = pl.ds(slab * size, size)
        held[:, at] = slabs_ref[slab].reshape(1, size)
        target = row_ref.at[:, pl.ds((slab * lines + begin) * LANES, size)]
        copies.append(pltpu.make_async_copy(held.at[:, at], target, sems.at[slab]))
        copies[-1].start()
    for copy in copies:
        copy.wait()


def join_row(slabs, lines, begin, row):
    total, count, _ = slabs.shape
    begun = [] if row is None else [row]
    return call(
        functools.partial(join_body, lines, begin),
        "join_row",
        moved=6 * slabs.size,
        in_specs=[IN_VMEM] + [IN_HBM] * len(begun),
        out_specs=IN_HBM,
        out_shape=jax.ShapeDtypeStruct((1, total * lines * LANES), BF16),
        input_output_aliases={1: 0} if begun else {},
        scratch_shapes=[pltpu.VMEM((1, slabs.size), BF16), pltpu.SemaphoreType.DMA((total,))],
    )(slabs, *begun)


def same_line(total):
    wide = total * TILE
    row = lax.broadcasted_iota(jnp.int32, (wide, wide), 0)
    col = lax.broadcasted_iota(jnp.int32, (wide, wide), 1)
    return row % TILE == col % TILE


def members(total, dtype):
    wide = total * TILE
    row = lax.broadcasted_iota(jnp.int32, (wide, total), 0)
    col = lax.broadcasted_iota(jnp.int32, (wide, total), 1)
    return (row // TILE == col).astype(dtype)


def gram_body(steps, tiles, parts, states_ref, *refs):
    out_ref, pairs = refs[-2:]
    total = states_ref.shape[0]
    wide = total * TILE
    pairs[...] = jnp.zeros_like(pairs)

    def step(i, carry):
        parts = [
            states_ref[:, pl.ds(pl.multiple_of((i * tiles + t) * TILE, TILE), TILE), :].reshape(wide, LANES)
            for t in range(tiles)
        ]
        block = jnp.concatenate(parts, axis=1)
        pairs[...] += lax.dot_general(block, block, (((1,), (1,)), ((), ())), preferred_element_type=F32)
        return carry

    lax.fori_loop(0, steps, step, 0)
    equal = jnp.where(same_line(total), pairs[...], 0.0)
    rows = jnp.sum(equal.reshape(total, TILE, wide), axis=1)
    gram = jnp.dot(rows, members(total, F32), precision=lax.Precision.HIGHEST, preferred_element_type=F32)
    gram = jnp.concatenate([gram, jnp.zeros((total, LANES - total), F32)], axis=1)
    for part_ref in refs[:parts]:
        gram += part_ref[0]
    out_ref[...] = jnp.broadcast_to(gram[None], out_ref.shape)


def slab_gram(states, lines, copies, parts, earlier):
    total = states.shape[0]
    wide = total * TILE
    tiles = min(8, lines // TILE)
    return call(
        functools.partial(gram_body, lines // TILE // tiles, tiles, len(parts)),
        "slab_gram",
        flops=2 * wide * wide * LANES * (lines // TILE),
        moved=2 * states.size,
        in_specs=[IN_VMEM] * (1 + len(parts)) + [IN_HBM] * len(earlier),
        out_specs=IN_VMEM,
        out_shape=jax.ShapeDtypeStruct((copies, total, LANES), F32),
        scratch_shapes=[pltpu.VMEM((wide, wide), F32)],
    )(states, *parts, *earlier)


def gradient_body(lines, begin, end, parts, *refs):
    observed, precision, out_ref, grads, sems = refs[parts:]
    total = grads.shape[0]
    first = refs[0].shape[1] - TILE
    rows = BLOCK // LINE
    group = 4
    shape = (rows, LINE, LANES)
    lane = lax.broadcasted_iota(jnp.int32, (1, LINE, LANES), 2)
    line = lax.broadcasted_iota(jnp.int32, (1, LINE, LANES), 1)

    def load(particle, at, count):
        ref, at = (refs[0], at) if at < first else (refs[1], at - first)
        return ref[particle, at : at + count, :].astype(F32)

    def rim(particle):
        return refs[0][particle, first:, :].astype(F32)

    stores = []
    for k, at in enumerate(range(begin, end, BLOCK)):
        mine = slice(at - begin, at - begin + BLOCK)
        obs = observed[at : at + BLOCK, :].astype(F32).reshape(shape)
        prec = precision[at : at + BLOCK, :].astype(F32).reshape(shape)

        def step(i, carry):
            for p in range(group):
                particle = i * group + p
                here = load(particle, at, BLOCK)
                before = load(particle, at - TILE, TILE) if at else rim(particle)
                after = load(particle, at + BLOCK, TILE) if at + BLOCK < lines else rim(particle)
                above = jnp.concatenate([before[LINE:], here[:-LINE]], axis=0).reshape(shape)
                below = jnp.concatenate([here[LINE:], after[:LINE]], axis=0).reshape(shape)
                field = here.reshape(shape)
                turned = pltpu.roll(field, 1, 2)
                carried = jnp.where(line == 0, 0.0, pltpu.roll(turned, 1, 1))
                left = jnp.where(lane == 0, carried, turned)
                turned = pltpu.roll(field, LANES - 1, 2)
                carried = jnp.where(line == LINE - 1, 0.0, pltpu.roll(turned, LINE - 1, 1))
                right = jnp.where(lane == LANES - 1, carried, turned)
                laplace = (4.0 + mass_term) * field - (below + above + right + left)
                squash = jnp.tanh(field)
                result = prec * (obs - squash) * (1.0 - squash * squash) - prior_scale * laplace
                grads[particle, mine, :] = result.reshape(BLOCK, LANES).astype(BF16)
            return carry

        lax.fori_loop(0, total // group, step, 0)
        stores.append(pltpu.make_async_copy(grads.at[:, mine, :], out_ref.at[:, mine, :], sems.at[k]))
        stores[-1].start()
    for store in stores:
        store.wait()


def slab_gradient(parts, observed, precision, lines, begin, end):
    total = parts[0].shape[0]
    count = end - begin
    out = jax.ShapeDtypeStruct((total, count, LANES), BF16)
    return call(
        functools.partial(gradient_body, lines, begin, end, len(parts)),
        "slab_gradient",
        flops=30 * out.size,
        moved=8 * out.size,
        in_specs=[IN_VMEM] * (len(parts) + 2),
        out_specs=IN_HBM,
        out_shape=out,
        scratch_shapes=[pltpu.VMEM(out.shape, BF16), pltpu.SemaphoreType.DMA((count // BLOCK,))],
    )(*parts, observed, precision)


def update_body(begin, end, parts, *refs):
    states_refs, refs = refs[:parts], refs[parts:]
    scalars_ref, grams_ref, grads_ref = refs[:3]
    out_ref, grads, mixer, own, sem = refs[-5:]
    total = out_ref.shape[0]
    wide = total * TILE
    fetch = pltpu.make_async_copy(grads_ref, grads, sem)
    fetch.start()
    gram = jnp.sum(grams_ref[...], axis=0)[:, :total]
    row = lax.broadcasted_iota(jnp.int32, (total, total), 0)
    col = lax.broadcasted_iota(jnp.int32, (total, total), 1)
    diagonal = jnp.where(row == col, gram, 0.0)
    down = jnp.sum(diagonal, axis=1, keepdims=True)
    across = jnp.sum(diagonal, axis=0, keepdims=True)
    member = members(total, BF16)
    spread, anneal, step_size = (scalars_ref[k : k + 1, :1] for k in range(3))
    rate = step_size / total
    coeff = 2.0 * anneal / spread
    kernel = jnp.exp(-(down + across - 2.0 * gram) / (spread * NCELL)).astype(BF16)
    ksum = jnp.sum(kernel.astype(F32), axis=1, keepdims=True)
    half = jnp.dot(member, kernel, preferred_element_type=F32).astype(BF16)
    full = lax.dot_general(half, member, (((1,), (1,)), ((), ())), preferred_element_type=F32)
    mixer[...] = jnp.where(same_line(total), full, 0.0).astype(BF16)
    gain = 1.0 + rate * coeff * ksum
    own[...] = jnp.broadcast_to(gain[:, :, None], (total, TILE, LANES)).reshape(wide, LANES)
    fetch.wait()

    done = 0
    for part, states_ref in enumerate(states_refs):
        have = states_ref.shape[1] - (0 if part else TILE)
        low = max(begin - done, 0)
        high = min(end - done, have)
        into = done - begin
        done += have

        def step(i, carry):
            for t in range(BLOCK // TILE):
                at = pl.multiple_of(i * BLOCK + t * TILE, TILE)
                there = pl.ds(pl.multiple_of(at + into, TILE), TILE)
                states = states_ref[:, pl.ds(at, TILE), :].reshape(wide, LANES)
                both = jnp.concatenate([grads[:, there, :].reshape(wide, LANES), states], axis=1)
                mixed = jnp.dot(mixer[...], both, preferred_element_type=F32)
                drive, pulled = mixed[:, :LANES], mixed[:, LANES:]
                new = states.astype(F32) * own[...] + rate * (drive - coeff * pulled)
                out_ref[:, there, :] = new.astype(BF16).reshape(total, TILE, LANES)
            return carry

        lax.fori_loop(low // BLOCK, high // BLOCK, step, 0)


def slab_update(scalars, grams, parts, grads, begin, end, earlier):
    total, count, _ = grads.shape
    wide = total * TILE
    return call(
        functools.partial(update_body, begin, end, len(parts)),
        "slab_update",
        flops=4 * wide * wide * LANES * (count // TILE),
        moved=6 * grads.size,
        in_specs=[IN_VMEM] * len(parts)
        + [IN_VMEM, IN_VMEM, IN_HBM]
        + [IN_HBM] * len(earlier),
        out_specs=IN_VMEM,
        out_shape=jax.ShapeDtypeStruct(grads.shape, BF16),
        scratch_shapes=[
            pltpu.VMEM(grads.shape, BF16),
            pltpu.VMEM((wide, wide), BF16),
            pltpu.VMEM((wide, LANES), F32),
            pltpu.SemaphoreType.DMA,
        ],
    )(*parts, scalars, grams, grads, *earlier)


def plain_update(spread, anneal, step_size, states, grads):
    total, lines, _ = grads.shape
    flat = states[:, :lines].reshape(total, -1)
    gram = lax.dot_general(flat, flat, (((1,), (1,)), ((), ())), preferred_element_type=F32)
    gram = lax.psum(gram, "slab")
    norms = jnp.diagonal(gram)
    kernel = jnp.exp(-(norms[:, None] + norms[None, :] - 2.0 * gram) / (spread[0] * NCELL)).astype(BF16)
    ksum = jnp.sum(kernel.astype(F32), axis=1)
    drive = jnp.dot(kernel, grads.reshape(total, -1), preferred_element_type=F32)
    pulled = jnp.dot(kernel, flat, preferred_element_type=F32)
    values = flat.astype(F32)
    repel = values * ksum[:, None] - pulled
    coeff = 2.0 * anneal[0] / spread[0]
    new = values + step_size[0] / total * (drive + coeff * repel)
    return new.astype(BF16).reshape(grads.shape)


def swap(slabs):
    return lax.all_to_all(slabs, "slab", split_axis=0, concat_axis=0, tiled=True)


def partner(k):
    return lax.axis_index("slab").astype(jnp.int32) ^ k


def lines_of(start, count):
    return pl.ds(pl.multiple_of(start, TILE), count)


def split_pieces_body(ks, half, raw, lines, gates, fields, row_ref, *refs):
    field_refs, refs = refs[:fields], refs[fields + gates :]
    count = len(ks)
    out_refs, slab_refs, helds, sems = refs[:count], refs[count : -count - 1], refs[-count - 1 : -1], refs[-1]
    cells = lines * LANES
    end = row_ref.shape[1]
    started = []

    def fetch(source, target):
        started.append(pltpu.make_async_copy(source, target, sems.at[len(started)]))
        started[-1].start()
        return started[-1]

    def part(start, size):
        return row_ref.at[:, pl.ds(pl.multiple_of(start, GRID_Y), size)]

    copies = []
    for k, held in zip(ks, helds):
        slab = partner(k)
        mine = [
            fetch(part(slab * cells, cells), held.at[:, pl.ds(0, cells)]),
            fetch(part(jnp.minimum((slab + 1) * cells, end - GRID_Y), GRID_Y), held.at[:, pl.ds(cells, GRID_Y)]),
            fetch(part(jnp.maximum(slab * cells - GRID_Y, 0), GRID_Y), held.at[:, pl.ds(cells + GRID_Y, GRID_Y)]),
        ]
        if k < half:
            other = partner(k ^ half)
            at = cells + 2 * GRID_Y
            size = raw * LANES + GRID_Y
            mine += [
                fetch(part(other * cells, size), held.at[:, pl.ds(at, size)]),
                fetch(part(jnp.maximum(other * cells - GRID_Y, 0), GRID_Y), held.at[:, pl.ds(at + size, GRID_Y)]),
            ]
        copies.append(mine)
    fetches = []
    for n, target in enumerate(slab_refs):
        start = partner(0 if n < fields else half) * lines
        fetches.append(fetch(field_refs[n % fields].at[lines_of(start, target.shape[0]), :], target))

    def grid_row(held, at):
        return held[:, pl.ds(at, GRID_Y)].astype(F32).reshape(LINE, LANES)

    for k, held, out_ref, mine in zip(ks, helds, out_refs, copies):
        for copy in mine:
            copy.wait()
        slab = partner(k)
        out_ref[:lines, :] = held[:, :cells].reshape(lines, LANES)
        below = jnp.where(slab == end // cells - 1, 0.0, grid_row(held, cells))
        above = jnp.where(slab == 0, 0.0, grid_row(held, cells + GRID_Y))
        out_ref[lines : lines + TILE, :] = jnp.concatenate([below, above], axis=0).astype(BF16)
        if k < half:
            at = cells + 2 * GRID_Y
            to = lines + TILE
            out_ref[to : to + raw, :] = held[:, at : at + raw * LANES].reshape(raw, LANES)
            below = grid_row(held, at + raw * LANES)
            above = jnp.where(partner(k ^ half) == 0, 0.0, grid_row(held, at + raw * LANES + GRID_Y))
            out_ref[to + raw :, :] = jnp.concatenate([below, above], axis=0).astype(BF16)
    for copy in fetches:
        copy.wait()


def split_pieces(row, slabs, raw, ks, gates, fields):
    lines = row.shape[1] // slabs // LANES
    half = slabs // 2
    sizes = [lines + TILE + (raw + TILE if k < half else 0) for k in ks]
    shapes = sizes + [lines] * len(fields) + [raw] * len(fields)
    return call(
        functools.partial(split_pieces_body, ks, half, raw, lines, len(gates), len(fields)),
        "split_pieces",
        moved=6 * sum(sizes) * LANES,
        in_specs=[IN_HBM] * (1 + len(fields)) + [IN_VMEM] * len(gates),
        out_specs=[IN_VMEM] * len(shapes),
        out_shape=[jax.ShapeDtypeStruct((size, LANES), BF16) for size in shapes],
        scratch_shapes=[pltpu.VMEM((1, size * LANES), BF16) for size in sizes]
        + [pltpu.SemaphoreType.DMA((5 * len(ks) + 2 * len(fields),))],
    )(row, *fields, *gates)


def join_pieces_body(ks, half, raw, lines, begun, *refs):
    count = len(ks)
    pieces, row_ref, helds, sems = refs[begun : begun + count], refs[begun + count], refs[begun + count + 1 : -1], refs[-1]
    cells = lines * LANES
    skip = raw * LANES
    copies = []
    for k, piece, held in zip(ks, pieces, helds):
        held[...] = piece[...].reshape(held.shape)
        if k < half:
            parts = [(0, cells, partner(k) * cells), (cells, skip, partner(k ^ half) * cells)]
        else:
            parts = [(0, cells - skip, partner(k) * cells + skip)]
        for at, size, start in parts:
            target = row_ref.at[:, pl.ds(pl.multiple_of(start, GRID_Y), size)]
            copies.append(pltpu.make_async_copy(held.at[:, pl.ds(at, size)], target, sems.at[len(copies)]))
            copies[-1].start()
    for copy in copies:
        copy.wait()


def join_pieces(row, slabs, raw, pieces, ks):
    sizes = [piece.size for piece in pieces]
    begun = [] if row is None else [row]
    return call(
        functools.partial(join_pieces_body, ks, slabs // 2, raw, NCELL // slabs // LANES, len(begun)),
        "join_pieces",
        moved=6 * sum(sizes),
        in_specs=[IN_HBM] * len(begun) + [IN_VMEM] * len(pieces),
        out_specs=IN_HBM,
        out_shape=jax.ShapeDtypeStruct((1, NCELL), BF16),
        input_output_aliases={0: 0} if begun else {},
        scratch_shapes=[pltpu.VMEM((1, size), BF16) for size in sizes] + [pltpu.SemaphoreType.DMA((2 * len(sizes),))],
    )(*begun, *pieces)


def owners(total, dtype):
    wide = total * TILE
    row = lax.broadcasted_iota(jnp.int32, (wide, total), 0)
    col = lax.broadcasted_iota(jnp.int32, (wide, total), 1)
    return (partner(row // TILE) == col).astype(dtype)


def gram_pieces_body(lines, total, *refs):
    pieces, out_ref, pairs = refs[:total], refs[-2], refs[-1]
    wide = total * TILE
    tiles = 4
    pairs[...] = jnp.zeros_like(pairs)

    def step(i, carry):
        parts = []
        for t in range(tiles):
            at = lines_of((i * tiles + t) * TILE, TILE)
            parts.append(jnp.concatenate([piece[at, :] for piece in pieces], axis=0))
        block = jnp.concatenate(parts, axis=1)
        pairs[...] += lax.dot_general(block, block, (((1,), (1,)), ((), ())), preferred_element_type=F32)
        return carry

    lax.fori_loop(0, lines // TILE // tiles, step, 0)
    exact = {"precision": lax.Precision.HIGHEST, "preferred_element_type": F32}
    equal = jnp.where(same_line(total), pairs[...], 0.0)
    rows = jnp.sum(equal.reshape(total, TILE, wide), axis=1)
    gram = jnp.dot(rows, owners(total, F32), **exact)
    row = lax.broadcasted_iota(jnp.int32, (total, total), 0)
    col = lax.broadcasted_iota(jnp.int32, (total, total), 1)
    gram = jnp.dot((row == partner(col)).astype(F32), gram, **exact)
    gram = jnp.concatenate([gram, jnp.zeros((total, LANES - total), F32)], axis=1)
    out_ref[...] = jnp.broadcast_to(gram[None], out_ref.shape)


def gram_pieces(pieces, lines, gates):
    total = len(pieces)
    wide = total * TILE
    return call(
        functools.partial(gram_pieces_body, lines, total),
        "gram_pieces",
        flops=2 * wide * wide * LANES * (lines // TILE),
        moved=2 * total * lines * LANES,
        in_specs=[IN_VMEM] * total + [IN_HBM] * len(gates),
        out_specs=IN_VMEM,
        out_shape=jax.ShapeDtypeStruct((total, total, LANES), F32),
        scratch_shapes=[pltpu.VMEM((wide, wide), F32)],
    )(*pieces, *gates)


def gradient_pieces_body(views, arrays, numbers, *refs):
    observed, precision, *number_refs = refs[arrays : arrays + 2 + numbers]
    out_ref, rows_ref, grads, sems = refs[-4:]
    for n, number_ref in enumerate(number_refs):
        rows_ref[n : n + 1, :] = jnp.full((1, LANES), number_ref[0], F32)
    count = observed.shape[0]
    rows = BLOCK // LINE
    shape = (rows, LINE, LANES)
    lane = lax.broadcasted_iota(jnp.int32, (1, LINE, LANES), 2)
    line = lax.broadcasted_iota(jnp.int32, (1, LINE, LANES), 1)
    steps = count // BLOCK

    def store(i):
        at = lines_of(i * BLOCK, BLOCK)
        return pltpu.make_async_copy(grads.at[:, at, :], out_ref.at[:, at, :], sems.at[i])

    def step(i, carry):
        start = i * BLOCK
        at = lines_of(start, BLOCK)
        obs = observed[at, :].astype(F32).reshape(shape)
        prec = precision[at, :].astype(F32).reshape(shape)
        for p, (array, lead, base) in enumerate(views):

            def load(begin, size):
                part = lines_of(base + begin, size)
                value = refs[array][part, :] if lead is None else refs[array][lead, part, :]
                return value.astype(F32)

            here = load(start, BLOCK)
            before = load(jnp.where(i == 0, count, start - TILE), TILE)
            after = load(start + BLOCK, TILE)
            above = jnp.concatenate([before[LINE:], here[:-LINE]], axis=0).reshape(shape)
            below = jnp.concatenate([here[LINE:], after[:LINE]], axis=0).reshape(shape)
            field = here.reshape(shape)
            turned = pltpu.roll(field, 1, 2)
            carried = jnp.where(line == 0, 0.0, pltpu.roll(turned, 1, 1))
            left = jnp.where(lane == 0, carried, turned)
            turned = pltpu.roll(field, LANES - 1, 2)
            carried = jnp.where(line == LINE - 1, 0.0, pltpu.roll(turned, LINE - 1, 1))
            right = jnp.where(lane == LANES - 1, carried, turned)
            laplace = (4.0 + mass_term) * field - (below + above + right + left)
            squash = jnp.tanh(field)
            result = prec * (obs - squash) * (1.0 - squash * squash) - prior_scale * laplace
            grads[p, at, :] = result.reshape(BLOCK, LANES).astype(BF16)
        store(i).start()
        return carry

    def finish(i, carry):
        store(i).wait()
        return carry

    lax.fori_loop(0, steps, step, 0)
    lax.fori_loop(0, steps, finish, 0)


def gradient_pieces(arrays, views, observed, precision, numbers, gates):
    count = observed.shape[0]
    size = len(views) * count * LANES
    return call(
        functools.partial(gradient_pieces_body, views, len(arrays), len(numbers)),
        "gradient_pieces",
        flops=30 * size,
        moved=8 * size,
        in_specs=[IN_VMEM] * (len(arrays) + 2)
        + [pl.BlockSpec(memory_space=pltpu.SMEM)] * len(numbers)
        + [IN_VMEM] * len(gates),
        out_specs=[IN_HBM, IN_VMEM],
        out_shape=[pltpu.HBM((len(views), count, LANES), BF16), jax.ShapeDtypeStruct((8, LANES), F32)],
        scratch_shapes=[
            pltpu.VMEM((len(views), count, LANES), BF16),
            pltpu.SemaphoreType.DMA((count // BLOCK,)),
        ],
    )(*arrays, observed, precision, *numbers, *gates)


def raw_body(raw, lines, half, *refs):
    out_ref = refs[-1]
    for k, piece in enumerate(refs[:half]):
        out_ref[k, :raw, :] = piece[:raw, :]
        below = piece[raw : raw + TILE, :].astype(F32)[:LINE]
        above = piece[lines : lines + TILE, :].astype(F32)[LINE:]
        out_ref[k, raw:, :] = jnp.concatenate([below, above], axis=0).astype(BF16)


def raw_states(near, raw, lines, gates):
    half = len(near)
    return call(
        functools.partial(raw_body, raw, lines, half),
        "raw_states",
        moved=4 * half * raw * LANES,
        in_specs=[IN_VMEM] * (half + len(gates)),
        out_specs=IN_VMEM,
        out_shape=jax.ShapeDtypeStruct((half, raw + TILE, LANES), BF16),
    )(*near, *gates)


def update_pieces_body(near, half, raw, lines, groups, extra, gates, *refs):
    total = 2 * half
    pieces, numbers_ref, grams_ref, refs = refs[:total], refs[total], refs[total + 1], refs[total + 2 :]
    group_refs, refs = refs[: len(groups)], refs[len(groups) :]
    raw_refs, refs = refs[:extra], refs[extra + gates :]
    targets, (news, grads, raw_grads, mixer, own, sems, out_sems) = refs[:half], refs[half:]
    wide = total * TILE
    high = half * TILE
    first = 0 if near else high
    fetches = []
    for group, group_ref in zip(groups, group_refs):
        for j, k in enumerate(group):
            fetches.append(pltpu.make_async_copy(group_ref.at[j], grads.at[k], sems.at[len(fetches)]))
    if extra:
        fetches.append(pltpu.make_async_copy(raw_refs[1], raw_grads, sems.at[len(fetches)]))
    for fetch in fetches:
        fetch.start()
    gram = jnp.sum(grams_ref[...], axis=0)[:, :total]
    spread, anneal, step_size = (numbers_ref[k : k + 1, :1] for k in range(3))
    rate = step_size / total
    coeff = 2.0 * anneal / spread
    row = lax.broadcasted_iota(jnp.int32, (total, total), 0)
    col = lax.broadcasted_iota(jnp.int32, (total, total), 1)
    diagonal = jnp.where(row == col, gram, 0.0)
    down = jnp.sum(diagonal, axis=1, keepdims=True)
    across = jnp.sum(diagonal, axis=0, keepdims=True)
    kernel = jnp.exp(-(down + across - 2.0 * gram) / (spread * NCELL)).astype(BF16)
    owner = owners(total, BF16)
    half_way = jnp.dot(owner[first : first + high], kernel, preferred_element_type=F32).astype(BF16)
    full = lax.dot_general(half_way, owner, (((1,), (1,)), ((), ())), preferred_element_type=F32)
    full = jnp.where(same_line(total)[first : first + high], full, 0.0)
    mixer[...] = full.astype(BF16)
    ksum = jnp.sum(full, axis=1, keepdims=True)
    own[...] = jnp.broadcast_to(1.0 + rate * coeff * ksum, (high, LANES))
    for fetch in fetches:
        fetch.wait()

    def mix(to, states, slopes):
        states = jnp.concatenate(states, axis=0)
        both = jnp.concatenate([slopes.reshape(wide, LANES), states], axis=1)
        mixed = jnp.dot(mixer[...], both, preferred_element_type=F32)
        drive, pulled = mixed[:, :LANES], mixed[:, LANES:]
        new = states[first : first + high].astype(F32) * own[...] + rate * (drive - coeff * pulled)
        news[:, lines_of(to, TILE), :] = new.astype(BF16).reshape(half, TILE, LANES)

    def sent(i):
        part = lines_of(i * BLOCK, BLOCK)
        return [
            pltpu.make_async_copy(news.at[k, part, :], target.at[part, :], out_sems.at[i, k])
            for k, target in enumerate(targets)
        ]

    begin = 0 if near else raw // BLOCK
    steps = lines // BLOCK - begin

    def slab_step(i, carry):
        for t in range(BLOCK // TILE):
            to = i * BLOCK + t * TILE
            at = lines_of(begin * BLOCK + to, TILE)
            mix(to, [piece[at, :] for piece in pieces], grads[:, at, :])
        for copy in sent(i):
            copy.start()
        return carry

    def raw_step(i, carry):
        for t in range(BLOCK // TILE):
            to = i * BLOCK + t * TILE
            at = lines_of(to - lines, TILE)
            states = [piece[lines_of(to + TILE, TILE), :] for piece in pieces[:half]]
            states += [raw_refs[0][k, at, :] for k in range(half)]
            mix(to, states, raw_grads[:, at, :])
        for copy in sent(i):
            copy.start()
        return carry

    def finish(i, carry):
        for copy in sent(i):
            copy.wait()
        return carry

    lax.fori_loop(0, steps, slab_step, 0)
    if near:
        lax.fori_loop(steps, steps + raw // BLOCK, raw_step, 0)
        steps += raw // BLOCK
    lax.fori_loop(0, steps, finish, 0)


def update_pieces(numbers, grams, pieces, grads, groups, raw_parts, gates, raw, lines, near):
    total = len(pieces)
    half = total // 2
    wide = total * TILE
    size = lines + raw if near else lines - raw
    return call(
        functools.partial(update_pieces_body, near, half, raw, lines, groups, len(raw_parts), len(gates)),
        "update_pieces",
        flops=4 * half * TILE * wide * LANES * (lines // TILE),
        moved=6 * total * lines * LANES,
        in_specs=[IN_VMEM] * (total + 2)
        + [IN_HBM] * len(groups)
        + [IN_VMEM, IN_HBM][: len(raw_parts)]
        + [IN_VMEM] * len(gates),
        out_specs=[IN_HBM] * half,
        out_shape=[pltpu.HBM((size, LANES), BF16)] * half,
        scratch_shapes=[
            pltpu.VMEM((half, size, LANES), BF16),
            pltpu.VMEM((total, lines, LANES), BF16),
            pltpu.VMEM((total, raw, LANES), BF16),
            pltpu.VMEM((half * TILE, wide), BF16),
            pltpu.VMEM((half * TILE, LANES), F32),
            pltpu.SemaphoreType.DMA((total + 1,)),
            pltpu.SemaphoreType.DMA((size // BLOCK, half)),
        ],
    )(*pieces, numbers, grams, *grads, *raw_parts, *gates)


def exchange(piece, k, slabs):
    return lax.ppermute(piece, "slab", [(i, i ^ k) for i in range(slabs)]) if k else piece


def swap(slabs):
    return lax.all_to_all(slabs, "slab", split_axis=0, concat_axis=0, tiled=True)


RAW = 128
GRADIENTS = ((8, 9, 10, 11), (0, 1, 2, 3), (4, 5, 6, 7), (12, 13, 14, 15))
JOINS = ((8, 9, 10, 11), (4, 5, 6, 7), (12, 13), (0, 1, 2, 3), (14, 15))


def by_pieces(particles, observed, precision, spread, anneal, step_size):
    slabs = lax.axis_size("slab")
    half = slabs // 2
    lines = NCELL // slabs // LANES
    row = in_hbm(particles)
    fields = [in_hbm(field.reshape(-1, LANES)) for field in (observed, precision)]
    nears, fars = tuple(range(half)), tuple(range(half, slabs))
    *pieces, obs, prec, raw_obs, raw_prec = split_pieces(row, slabs, RAW, fars, [], fields)
    far = [exchange(piece, k, slabs) for k, piece in zip(fars, pieces)]
    pieces = split_pieces(row, slabs, RAW, nears, far[:1], [])
    near = [exchange(piece, k, slabs) for k, piece in zip(nears, pieces)]
    states = near + far
    raw_near = raw_states(near, RAW, lines, far)
    across = exchange(raw_near, half, slabs)
    grads = []
    numbers = [spread, anneal, step_size]
    for group in GRADIENTS:
        views = tuple((j, None, 0) for j in range(len(group)))
        arrays = [states[k] for k in group]
        slopes, rows = gradient_pieces(arrays, views, obs, prec, [] if grads else numbers, [])
        grads.append(in_hbm(slopes))
        numbers = numbers if len(grads) > 1 else rows
    grams = swap(gram_pieces(states, lines, grads[:-1]))
    pieces = update_pieces(numbers, grams, states, grads, GRADIENTS, [], [], RAW, lines, False)
    new_far = [exchange(piece, k, slabs) for k, piece in zip(fars, pieces)]
    views = [(k, None, lines + TILE) for k in range(half)] + [(half, k, 0) for k in range(half)]
    slopes, _ = gradient_pieces(near + [across], tuple(views), raw_obs, raw_prec, [], new_far[:1])
    raw_parts = [across, in_hbm(slopes)]
    pieces = update_pieces(numbers, grams, states, grads, GRADIENTS, raw_parts, new_far[1:2], RAW, lines, True)
    new = [exchange(piece, k, slabs) for k, piece in zip(nears, pieces)] + new_far
    row = None
    for group in JOINS:
        row = join_pieces(row, slabs, RAW, [new[k] for k in group], group)
    return row


def on_device(particles, observed, precision, spread, anneal, step_size):
    slabs = lax.axis_size("slab")
    total = particles.shape[0] * slabs
    lines = NCELL // slabs // LANES
    if slabs == 16:
        return by_pieces(particles, observed, precision, spread, anneal, step_size)
    sent, begun = cuts(lines)
    fields = [observed.reshape(-1, LANES), precision.reshape(-1, LANES)]
    numbers = [spread, anneal, step_size]
    first, obs, prec, scalars = split_row(particles, slabs, 0, sent, True, fields, numbers, [])
    parts = [swap(first)]
    if sent < lines:
        parts += [swap(split_row(particles, slabs, sent, lines, False, [], [], [scalars])[0])]
    if total * TILE > 256:
        grads = slab_gradient(parts, obs, prec, lines, 0, lines)
        states = jnp.concatenate([parts[0][:, :sent]] + parts[1:], axis=1)
        new = plain_update(spread, anneal, step_size, states, grads)
        return join_row(swap(new), lines, 0, None)
    if sent == lines:
        grads = slab_gradient(parts, obs, prec, lines, 0, lines)
        grams = swap(slab_gram(parts[0], lines, slabs, [], []))
        new = slab_update(scalars, grams, parts, grads, 0, lines, [])
        return join_row(swap(new), lines, 0, None)
    gram = slab_gram(parts[0], sent, 1, [], [])
    early = slab_gradient(parts[:1], obs, prec, lines, 0, begun)
    grams = swap(slab_gram(parts[1], lines - sent, slabs, [gram], [early]))
    late = slab_gradient(parts, obs, prec, lines, begun, lines)
    new = slab_update(scalars, grams, parts[:1], early, 0, begun, [])
    rest = slab_update(scalars, grams, parts, late, begun, lines, [new])
    row = join_row(swap(new), lines, 0, None)
    return join_row(swap(rest), lines, begun, row)


def solution(mesh):
    in_specs = (
        P(("groups", "slab"), None),
        P("groups"),
        P("groups"),
        P("groups"),
        P("groups"),
        P("groups"),
    )
    out_specs = P(("groups", "slab"), None)
    return jax.shard_map(
        on_device, mesh=mesh, in_specs=in_specs, out_specs=out_specs, check_vma=False
    )
```

```python
import functools

import jax
import jax.numpy as jnp
from jax import lax
from jax.experimental import pallas as pl
from jax.experimental.pallas import tpu as pltpu
from jax.sharding import PartitionSpec as P

GRID_X = 1024
GRID_Y = 1024
NCELL = 1048576
LANES = 128
LINE = GRID_Y // LANES
TILE = 16

prior_scale = 0.25
mass_term = 1.0

F32 = jnp.float32
BF16 = jnp.bfloat16
MIB = 1024 * 1024


LATE = 400 * 1000 * 1000


def call(body, name, flops=0, moved=0, limit=16, **kwargs):
    return pl.pallas_call(
        body,
        name=name,
        compiler_params=pltpu.CompilerParams(vmem_limit_bytes=limit * MIB),
        cost_estimate=pl.CostEstimate(flops=flops, bytes_accessed=moved, transcendentals=0),
        **kwargs,
    )


IN_VMEM = pl.BlockSpec(memory_space=pltpu.VMEM)
IN_HBM = pl.BlockSpec(memory_space=pltpu.HBM)


def in_hbm(array):
    return pltpu.with_memory_space_constraint(array, pltpu.HBM)


BLOCK = 4 * TILE


def cuts(lines):
    if lines % (8 * BLOCK):
        return lines, lines
    return lines * 3 // 4, lines * 3 // 4 - BLOCK


def split_body(lines, begin, rim, fields, numbers, row_ref, *refs):
    field_refs, number_refs = refs[:fields], refs[fields : fields + numbers]
    out_ref, *slab_refs, rows_ref = refs[-7 - fields : -5]
    held, edges, sems, edge_sems, field_sems = refs[-5:]
    for k, number_ref in enumerate(number_refs):
        rows_ref[k : k + 1, :] = jnp.broadcast_to(number_ref[...].reshape(1, 1), (1, LANES))
    slabs, count, _ = out_ref.shape
    count -= TILE * rim
    size = count * LANES
    cells = lines * LANES

    def part(slab):
        source = row_ref.at[:, pl.ds(slab * cells + begin * LANES, size)]
        return pltpu.make_async_copy(source, held.at[:, pl.ds(slab * size, size)], sems.at[slab])

    def edge(slab):
        source = row_ref.at[:, pl.ds(slab * cells - GRID_Y, GRID_Y)]
        return pltpu.make_async_copy(source, edges.at[:, pl.ds(slab * GRID_Y, GRID_Y)], edge_sems.at[slab])

    def grid_row(ref, start):
        return ref[:, pl.ds(start, GRID_Y)].astype(F32).reshape(LINE, LANES)

    for slab in range(slabs):
        part(slab).start()
        if rim and slab:
            edge(slab).start()
    mine = pl.ds(pl.multiple_of(lax.axis_index("slab") * lines, TILE), lines)
    fetches = [
        pltpu.make_async_copy(source.at[mine, :], target, field_sems.at[k])
        for k, (source, target) in enumerate(zip(field_refs, slab_refs))
    ]
    for fetch in fetches:
        fetch.start()
    part(0).wait()
    outside = jnp.zeros((LINE, LANES), F32)
    for slab in range(slabs):
        if slab + 1 < slabs:
            part(slab + 1).wait()
        out_ref[slab, :count, :] = held[:, pl.ds(slab * size, size)].reshape(count, LANES)
        if rim:
            if slab:
                edge(slab).wait()
            below = grid_row(held, (slab + 1) * size) if slab + 1 < slabs else outside
            above = grid_row(edges, slab * GRID_Y) if slab else outside
            out_ref[slab, count:, :] = jnp.concatenate([below, above], axis=0).astype(BF16)
    for fetch in fetches:
        fetch.wait()


def split_row(row, slabs, begin, end, rim, fields, numbers, earlier):
    lines = row.shape[1] // slabs // LANES
    count = end - begin
    return call(
        functools.partial(split_body, lines, begin, rim, len(fields), len(numbers)),
        "split_row",
        moved=6 * slabs * count * LANES,
        in_specs=[IN_HBM] * (1 + len(fields)) + [IN_VMEM] * len(numbers) + [IN_HBM] * len(earlier),
        out_specs=[IN_VMEM] * (2 + len(fields)),
        out_shape=[jax.ShapeDtypeStruct((slabs, count + TILE * rim, LANES), BF16)]
        + [jax.ShapeDtypeStruct((lines, LANES), BF16)] * len(fields)
        + [jax.ShapeDtypeStruct((8, LANES), F32)],
        scratch_shapes=[
            pltpu.VMEM((1, slabs * count * LANES), BF16),
            pltpu.VMEM((1, slabs * GRID_Y), BF16),
            pltpu.SemaphoreType.DMA((slabs,)),
            pltpu.SemaphoreType.DMA((slabs,)),
            pltpu.SemaphoreType.DMA((2,)),
        ],
    )(row, *fields, *numbers, *earlier)


def join_body(lines, begin, slabs_ref, *refs):
    row_ref, held, sems = refs[-3:]
    slabs, count, _ = slabs_ref.shape
    size = count * LANES
    copies = []
    for slab in range(slabs):
        at = pl.ds(slab * size, size)
        held[:, at] = slabs_ref[slab].reshape(1, size)
        target = row_ref.at[:, pl.ds((slab * lines + begin) * LANES, size)]
        copies.append(pltpu.make_async_copy(held.at[:, at], target, sems.at[slab]))
        copies[-1].start()
    for copy in copies:
        copy.wait()


def join_row(slabs, lines, begin, row):
    total, count, _ = slabs.shape
    begun = [] if row is None else [row]
    return call(
        functools.partial(join_body, lines, begin),
        "join_row",
        moved=6 * slabs.size,
        in_specs=[IN_VMEM] + [IN_HBM] * len(begun),
        out_specs=IN_HBM,
        out_shape=jax.ShapeDtypeStruct((1, total * lines * LANES), BF16),
        input_output_aliases={1: 0} if begun else {},
        scratch_shapes=[pltpu.VMEM((1, slabs.size), BF16), pltpu.SemaphoreType.DMA((total,))],
    )(slabs, *begun)


def same_line(total):
    wide = total * TILE
    row = lax.broadcasted_iota(jnp.int32, (wide, wide), 0)
    col = lax.broadcasted_iota(jnp.int32, (wide, wide), 1)
    return row % TILE == col % TILE


def members(total, dtype):
    wide = total * TILE
    row = lax.broadcasted_iota(jnp.int32, (wide, total), 0)
    col = lax.broadcasted_iota(jnp.int32, (wide, total), 1)
    return (row // TILE == col).astype(dtype)


def gram_body(steps, tiles, parts, states_ref, *refs):
    out_ref, pairs = refs[-2:]
    total = states_ref.shape[0]
    wide = total * TILE
    pairs[...] = jnp.zeros_like(pairs)

    def step(i, carry):
        parts = [
            states_ref[:, pl.ds(pl.multiple_of((i * tiles + t) * TILE, TILE), TILE), :].reshape(wide, LANES)
            for t in range(tiles)
        ]
        block = jnp.concatenate(parts, axis=1)
        pairs[...] += lax.dot_general(block, block, (((1,), (1,)), ((), ())), preferred_element_type=F32)
        return carry

    lax.fori_loop(0, steps, step, 0)
    equal = jnp.where(same_line(total), pairs[...], 0.0)
    rows = jnp.sum(equal.reshape(total, TILE, wide), axis=1)
    gram = jnp.dot(rows, members(total, F32), precision=lax.Precision.HIGHEST, preferred_element_type=F32)
    gram = jnp.concatenate([gram, jnp.zeros((total, LANES - total), F32)], axis=1)
    for part_ref in refs[:parts]:
        gram += part_ref[0]
    out_ref[...] = jnp.broadcast_to(gram[None], out_ref.shape)


def slab_gram(states, lines, copies, parts, earlier):
    total = states.shape[0]
    wide = total * TILE
    tiles = min(8, lines // TILE)
    return call(
        functools.partial(gram_body, lines // TILE // tiles, tiles, len(parts)),
        "slab_gram",
        flops=2 * wide * wide * LANES * (lines // TILE),
        moved=2 * states.size,
        in_specs=[IN_VMEM] * (1 + len(parts)) + [IN_HBM] * len(earlier),
        out_specs=IN_VMEM,
        out_shape=jax.ShapeDtypeStruct((copies, total, LANES), F32),
        scratch_shapes=[pltpu.VMEM((wide, wide), F32)],
    )(states, *parts, *earlier)


def gradient_body(lines, begin, end, parts, *refs):
    observed, precision, out_ref, grads, sems = refs[parts:]
    total = grads.shape[0]
    first = refs[0].shape[1] - TILE
    rows = BLOCK // LINE
    group = 4
    shape = (rows, LINE, LANES)
    lane = lax.broadcasted_iota(jnp.int32, (1, LINE, LANES), 2)
    line = lax.broadcasted_iota(jnp.int32, (1, LINE, LANES), 1)

    def load(particle, at, count):
        ref, at = (refs[0], at) if at < first else (refs[1], at - first)
        return ref[particle, at : at + count, :].astype(F32)

    def rim(particle):
        return refs[0][particle, first:, :].astype(F32)

    stores = []
    for k, at in enumerate(range(begin, end, BLOCK)):
        mine = slice(at - begin, at - begin + BLOCK)
        obs = observed[at : at + BLOCK, :].astype(F32).reshape(shape)
        prec = precision[at : at + BLOCK, :].astype(F32).reshape(shape)

        def step(i, carry):
            for p in range(group):
                particle = i * group + p
                here = load(particle, at, BLOCK)
                before = load(particle, at - TILE, TILE) if at else rim(particle)
                after = load(particle, at + BLOCK, TILE) if at + BLOCK < lines else rim(particle)
                above = jnp.concatenate([before[LINE:], here[:-LINE]], axis=0).reshape(shape)
                below = jnp.concatenate([here[LINE:], after[:LINE]], axis=0).reshape(shape)
                field = here.reshape(shape)
                turned = pltpu.roll(field, 1, 2)
                carried = jnp.where(line == 0, 0.0, pltpu.roll(turned, 1, 1))
                left = jnp.where(lane == 0, carried, turned)
                turned = pltpu.roll(field, LANES - 1, 2)
                carried = jnp.where(line == LINE - 1, 0.0, pltpu.roll(turned, LINE - 1, 1))
                right = jnp.where(lane == LANES - 1, carried, turned)
                laplace = (4.0 + mass_term) * field - (below + above + right + left)
                squash = jnp.tanh(field)
                result = prec * (obs - squash) * (1.0 - squash * squash) - prior_scale * laplace
                grads[particle, mine, :] = result.reshape(BLOCK, LANES).astype(BF16)
            return carry

        lax.fori_loop(0, total // group, step, 0)
        stores.append(pltpu.make_async_copy(grads.at[:, mine, :], out_ref.at[:, mine, :], sems.at[k]))
        stores[-1].start()
    for store in stores:
        store.wait()


def slab_gradient(parts, observed, precision, lines, begin, end):
    total = parts[0].shape[0]
    count = end - begin
    out = jax.ShapeDtypeStruct((total, count, LANES), BF16)
    return call(
        functools.partial(gradient_body, lines, begin, end, len(parts)),
        "slab_gradient",
        flops=30 * out.size,
        moved=8 * out.size,
        in_specs=[IN_VMEM] * (len(parts) + 2),
        out_specs=IN_HBM,
        out_shape=out,
        scratch_shapes=[pltpu.VMEM(out.shape, BF16), pltpu.SemaphoreType.DMA((count // BLOCK,))],
    )(*parts, observed, precision)


def update_body(begin, end, parts, *refs):
    states_refs, refs = refs[:parts], refs[parts:]
    scalars_ref, grams_ref, grads_ref = refs[:3]
    out_ref, grads, mixer, own, sem = refs[-5:]
    total = out_ref.shape[0]
    wide = total * TILE
    fetch = pltpu.make_async_copy(grads_ref, grads, sem)
    fetch.start()
    gram = jnp.sum(grams_ref[...], axis=0)[:, :total]
    row = lax.broadcasted_iota(jnp.int32, (total, total), 0)
    col = lax.broadcasted_iota(jnp.int32, (total, total), 1)
    diagonal = jnp.where(row == col, gram, 0.0)
    down = jnp.sum(diagonal, axis=1, keepdims=True)
    across = jnp.sum(diagonal, axis=0, keepdims=True)
    member = members(total, BF16)
    spread, anneal, step_size = (scalars_ref[k : k + 1, :1] for k in range(3))
    rate = step_size / total
    coeff = 2.0 * anneal / spread
    kernel = jnp.exp(-(down + across - 2.0 * gram) / (spread * NCELL)).astype(BF16)
    ksum = jnp.sum(kernel.astype(F32), axis=1, keepdims=True)
    half = jnp.dot(member, kernel, preferred_element_type=F32).astype(BF16)
    full = lax.dot_general(half, member, (((1,), (1,)), ((), ())), preferred_element_type=F32)
    mixer[...] = jnp.where(same_line(total), full, 0.0).astype(BF16)
    gain = 1.0 + rate * coeff * ksum
    own[...] = jnp.broadcast_to(gain[:, :, None], (total, TILE, LANES)).reshape(wide, LANES)
    fetch.wait()

    done = 0
    for part, states_ref in enumerate(states_refs):
        have = states_ref.shape[1] - (0 if part else TILE)
        low = max(begin - done, 0)
        high = min(end - done, have)
        into = done - begin
        done += have

        def step(i, carry):
            for t in range(BLOCK // TILE):
                at = pl.multiple_of(i * BLOCK + t * TILE, TILE)
                there = pl.ds(pl.multiple_of(at + into, TILE), TILE)
                states = states_ref[:, pl.ds(at, TILE), :].reshape(wide, LANES)
                both = jnp.concatenate([grads[:, there, :].reshape(wide, LANES), states], axis=1)
                mixed = jnp.dot(mixer[...], both, preferred_element_type=F32)
                drive, pulled = mixed[:, :LANES], mixed[:, LANES:]
                new = states.astype(F32) * own[...] + rate * (drive - coeff * pulled)
                out_ref[:, there, :] = new.astype(BF16).reshape(total, TILE, LANES)
            return carry

        lax.fori_loop(low // BLOCK, high // BLOCK, step, 0)


def slab_update(scalars, grams, parts, grads, begin, end, earlier):
    total, count, _ = grads.shape
    wide = total * TILE
    return call(
        functools.partial(update_body, begin, end, len(parts)),
        "slab_update",
        flops=4 * wide * wide * LANES * (count // TILE),
        moved=6 * grads.size,
        in_specs=[IN_VMEM] * len(parts)
        + [IN_VMEM, IN_VMEM, IN_HBM]
        + [IN_HBM] * len(earlier),
        out_specs=IN_VMEM,
        out_shape=jax.ShapeDtypeStruct(grads.shape, BF16),
        scratch_shapes=[
            pltpu.VMEM(grads.shape, BF16),
            pltpu.VMEM((wide, wide), BF16),
            pltpu.VMEM((wide, LANES), F32),
            pltpu.SemaphoreType.DMA,
        ],
    )(*parts, scalars, grams, grads, *earlier)


def plain_update(spread, anneal, step_size, states, grads):
    total, lines, _ = grads.shape
    flat = states[:, :lines].reshape(total, -1)
    gram = lax.dot_general(flat, flat, (((1,), (1,)), ((), ())), preferred_element_type=F32)
    gram = lax.psum(gram, "slab")
    norms = jnp.diagonal(gram)
    kernel = jnp.exp(-(norms[:, None] + norms[None, :] - 2.0 * gram) / (spread[0] * NCELL)).astype(BF16)
    ksum = jnp.sum(kernel.astype(F32), axis=1)
    drive = jnp.dot(kernel, grads.reshape(total, -1), preferred_element_type=F32)
    pulled = jnp.dot(kernel, flat, preferred_element_type=F32)
    values = flat.astype(F32)
    repel = values * ksum[:, None] - pulled
    coeff = 2.0 * anneal[0] / spread[0]
    new = values + step_size[0] / total * (drive + coeff * repel)
    return new.astype(BF16).reshape(grads.shape)


def swap(slabs):
    return lax.all_to_all(slabs, "slab", split_axis=0, concat_axis=0, tiled=True)


def device_at(at, half):
    me = lax.axis_index("slab").astype(jnp.int32)
    return jnp.where(at < half, me - me % half + at, me ^ at)


def lines_of(start, count):
    return pl.ds(pl.multiple_of(start, TILE), count)


def split_pieces_body(positions, half, lines, fields, row_ref, *refs):
    slabs = 2 * half
    count = len(positions)
    field_refs, out_refs = refs[:fields], refs[fields : -count - 1]
    helds, sems = refs[-count - 1 : -1], refs[-1]
    slab_refs = out_refs[len(out_refs) - fields :]
    cells = lines * LANES
    end = row_ref.shape[1]
    copies = []
    for at, held in zip(positions, helds):
        slab = device_at(at, half)
        parts = (
            (slab * cells, cells, 0),
            (jnp.minimum((slab + 1) * cells, end - GRID_Y), GRID_Y, cells),
            (jnp.maximum(slab * cells - GRID_Y, 0), GRID_Y, cells + GRID_Y),
        )
        for n, (start, size, to) in enumerate(parts):
            source = row_ref.at[:, pl.ds(pl.multiple_of(start, GRID_Y), size)]
            copies.append(pltpu.make_async_copy(source, held.at[:, pl.ds(to, size)], sems.at[len(copies)]))
            copies[-1].start()
    start = lax.axis_index("slab").astype(jnp.int32) * lines
    for field_ref, slab_ref in zip(field_refs, slab_refs):
        copies.append(pltpu.make_async_copy(field_ref.at[lines_of(start, lines), :], slab_ref, sems.at[len(copies)]))
        copies[-1].start()

    for n, (at, held) in enumerate(zip(positions, helds)):
        out_ref = out_refs[0].at[n] if at < half else out_refs[n]
        for copy in copies[3 * n : 3 * n + 3]:
            copy.wait()
        slab = device_at(at, half)
        out_ref[:lines, :] = held[:, :cells].reshape(lines, LANES)
        below = held[:, cells : cells + GRID_Y].astype(F32).reshape(LINE, LANES)
        above = held[:, cells + GRID_Y :].astype(F32).reshape(LINE, LANES)
        below = jnp.where(slab == slabs - 1, 0.0, below)
        above = jnp.where(slab == 0, 0.0, above)
        out_ref[lines:, :] = jnp.concatenate([below, above], axis=0).astype(BF16)
    for copy in copies[3 * count :]:
        copy.wait()


def split_pieces(row, slabs, near, fields):
    lines = row.shape[1] // slabs // LANES
    half = slabs // 2
    rim = lines + TILE
    out_shape = [jax.ShapeDtypeStruct((half, rim, LANES), BF16)] if near else []
    out_shape += [] if near else [jax.ShapeDtypeStruct((rim, LANES), BF16)] * half
    out_shape += [jax.ShapeDtypeStruct((lines, LANES), BF16)] * len(fields)
    positions = range(half) if near else range(half, slabs)
    return call(
        functools.partial(split_pieces_body, positions, half, lines, len(fields)),
        "split_pieces",
        moved=6 * half * rim * LANES,
        in_specs=[IN_HBM] * (1 + len(fields)),
        out_specs=[IN_VMEM] * len(out_shape),
        out_shape=out_shape,
        scratch_shapes=[pltpu.VMEM((1, rim * LANES), BF16)] * half
        + [pltpu.SemaphoreType.DMA((3 * half + len(fields),))],
    )(row, *fields)


def join_pieces_body(pieces, half, lines, begun, arrays, *refs):
    row_ref, helds, sems = refs[begun + arrays], refs[begun + arrays + 1 : -1], refs[-1]
    copies = []
    for (array, lead, at), held in zip(pieces, helds):
        ref = refs[begun + array]
        piece = ref[...] if lead is None else ref[lead]
        held[...] = piece.reshape(held.shape)
        start = device_at(at, half) * lines * LANES
        target = row_ref.at[:, pl.ds(pl.multiple_of(start, GRID_Y), held.shape[1])]
        copies.append(pltpu.make_async_copy(held, target, sems.at[len(copies)]))
        copies[-1].start()
    for copy in copies:
        copy.wait()


def join_pieces(row, slabs, arrays, pieces, late=0):
    sizes = [arrays[piece[0]].shape[-2] * LANES for piece in pieces]
    begun = [] if row is None else [row]
    return call(
        functools.partial(join_pieces_body, pieces, slabs // 2, NCELL // slabs // LANES, len(begun), len(arrays)),
        "join_pieces",
        moved=6 * sum(sizes) + late,
        in_specs=[IN_HBM] * len(begun) + [IN_VMEM] * len(arrays),
        out_specs=IN_HBM,
        out_shape=jax.ShapeDtypeStruct((1, NCELL), BF16),
        input_output_aliases={0: 0} if begun else {},
        scratch_shapes=[pltpu.VMEM((1, size), BF16) for size in sizes] + [pltpu.SemaphoreType.DMA((len(sizes),))],
    )(*begun, *arrays)


def owners(total, dtype):
    wide = total * TILE
    row = lax.broadcasted_iota(jnp.int32, (wide, total), 0)
    col = lax.broadcasted_iota(jnp.int32, (wide, total), 1)
    return (device_at(row // TILE, total // 2) == col).astype(dtype)


def gram_pieces_body(lines, total, near_ref, *refs):
    half = total // 2
    pieces, out_ref, pairs = refs[:half], refs[-2], refs[-1]
    wide = total * TILE
    tiles = 4
    pairs[...] = jnp.zeros_like(pairs)

    def step(i, carry):
        parts = []
        for t in range(tiles):
            at = lines_of((i * tiles + t) * TILE, TILE)
            near = near_ref[:, at, :].reshape(wide // 2, LANES)
            parts.append(jnp.concatenate([near] + [piece[at, :] for piece in pieces], axis=0))
        block = jnp.concatenate(parts, axis=1)
        pairs[...] += lax.dot_general(block, block, (((1,), (1,)), ((), ())), preferred_element_type=F32)
        return carry

    lax.fori_loop(0, lines // TILE // tiles, step, 0)
    equal = jnp.where(same_line(total), pairs[...], 0.0)
    exact = {"precision": lax.Precision.HIGHEST, "preferred_element_type": F32}
    owner = owners(total, F32)
    half_way = jnp.dot(equal, owner, **exact)
    gram = lax.dot_general(owner, half_way, (((0,), (0,)), ((), ())), **exact)
    gram = jnp.concatenate([gram, jnp.zeros((total, LANES - total), F32)], axis=1)
    out_ref[...] = jnp.broadcast_to(gram[None], out_ref.shape)


def gram_pieces(near, far, lines, gates):
    total = 2 * len(far)
    wide = total * TILE
    return call(
        functools.partial(gram_pieces_body, lines, total),
        "gram_pieces",
        flops=2 * wide * wide * LANES * (lines // TILE),
        moved=2 * total * lines * LANES,
        in_specs=[IN_VMEM] * (1 + len(far)) + [IN_HBM] * len(gates),
        out_specs=IN_VMEM,
        out_shape=jax.ShapeDtypeStruct((total, total, LANES), F32),
        scratch_shapes=[pltpu.VMEM((wide, wide), F32)],
    )(near, *far, *gates)


def gradient_pieces_body(views, arrays, numbers, *refs):
    observed, precision, *number_refs = refs[arrays : arrays + 2 + numbers]
    out_ref, rows_ref, grads, sems = refs[-4:]
    for n, number_ref in enumerate(number_refs):
        rows_ref[n : n + 1, :] = jnp.full((1, LANES), number_ref[0], F32)
    count = observed.shape[0]
    rows = BLOCK // LINE
    shape = (rows, LINE, LANES)
    lane = lax.broadcasted_iota(jnp.int32, (1, LINE, LANES), 2)
    line = lax.broadcasted_iota(jnp.int32, (1, LINE, LANES), 1)
    steps = count // BLOCK

    def store(i):
        at = lines_of(i * BLOCK, BLOCK)
        return pltpu.make_async_copy(grads.at[:, at, :], out_ref.at[:, at, :], sems.at[i])

    def step(i, carry):
        start = i * BLOCK
        at = lines_of(start, BLOCK)
        obs = observed[at, :].astype(F32).reshape(shape)
        prec = precision[at, :].astype(F32).reshape(shape)
        for p, (array, lead, base) in enumerate(views):

            def load(begin, size):
                part = lines_of(base + begin, size)
                value = refs[array][part, :] if lead is None else refs[array][lead, part, :]
                return value.astype(F32)

            here = load(start, BLOCK)
            before = load(jnp.where(i == 0, count, start - TILE), TILE)
            after = load(start + BLOCK, TILE)
            above = jnp.concatenate([before[LINE:], here[:-LINE]], axis=0).reshape(shape)
            below = jnp.concatenate([here[LINE:], after[:LINE]], axis=0).reshape(shape)
            field = here.reshape(shape)
            turned = pltpu.roll(field, 1, 2)
            carried = jnp.where(line == 0, 0.0, pltpu.roll(turned, 1, 1))
            left = jnp.where(lane == 0, carried, turned)
            turned = pltpu.roll(field, LANES - 1, 2)
            carried = jnp.where(line == LINE - 1, 0.0, pltpu.roll(turned, LINE - 1, 1))
            right = jnp.where(lane == LANES - 1, carried, turned)
            laplace = (4.0 + mass_term) * field - (below + above + right + left)
            squash = jnp.tanh(field)
            result = prec * (obs - squash) * (1.0 - squash * squash) - prior_scale * laplace
            grads[p, at, :] = result.reshape(BLOCK, LANES).astype(BF16)
        store(i).start()
        return carry

    def finish(i, carry):
        store(i).wait()
        return carry

    lax.fori_loop(0, steps, step, 0)
    lax.fori_loop(0, steps, finish, 0)


def gradient_pieces(arrays, views, observed, precision, numbers, gates, late=0):
    count = observed.shape[0]
    out = pltpu.HBM((len(views), count, LANES), BF16)
    size = len(views) * count * LANES
    return call(
        functools.partial(gradient_pieces_body, views, len(arrays), len(numbers)),
        "gradient_pieces",
        flops=30 * size,
        moved=8 * size + late,
        in_specs=[IN_VMEM] * (len(arrays) + 2)
        + [pl.BlockSpec(memory_space=pltpu.SMEM)] * len(numbers)
        + [IN_VMEM] * len(gates),
        out_specs=[IN_HBM, IN_VMEM],
        out_shape=[out, jax.ShapeDtypeStruct((8, LANES), F32)],
        scratch_shapes=[pltpu.VMEM(out.shape, BF16), pltpu.SemaphoreType.DMA((count // BLOCK,))],
    )(*arrays, observed, precision, *numbers, *gates)


def mix(mixer, own, numbers_ref, total, states, slopes):
    high = mixer.shape[0]
    rate = numbers_ref[2:3, :1] / total
    coeff = 2.0 * numbers_ref[1:2, :1] / numbers_ref[:1, :1]
    both = jnp.concatenate([slopes, states], axis=1)
    mixed = jnp.dot(mixer[...], both, preferred_element_type=F32)
    drive, pulled = mixed[:, :LANES], mixed[:, LANES:]
    return (states[:high].astype(F32) * own[...] + rate * (drive - coeff * pulled)).astype(BF16)


def update_pieces_body(half, lines, groups, near_ref, *refs):
    total = 2 * half
    far_refs, numbers_ref, grams_ref, refs = refs[:half], refs[half], refs[half + 1], refs[half + 2 :]
    group_refs, near_out, far_outs = refs[: len(groups)], refs[-5 - half], refs[-4 - half : -4]
    mixer, own, grads, sems = refs[-4:]
    wide = total * TILE
    high = half * TILE
    fetches = []
    for group, group_ref in zip(groups, group_refs):
        for j, at in enumerate(group):
            fetches.append(pltpu.make_async_copy(group_ref.at[j], grads.at[at], sems.at[len(fetches)]))
    for fetch in fetches:
        fetch.start()
    gram = jnp.sum(grams_ref[...], axis=0)[:, :total]
    spread, anneal, step_size = (numbers_ref[k : k + 1, :1] for k in range(3))
    rate = step_size / total
    coeff = 2.0 * anneal / spread
    row = lax.broadcasted_iota(jnp.int32, (total, total), 0)
    col = lax.broadcasted_iota(jnp.int32, (total, total), 1)
    diagonal = jnp.where(row == col, gram, 0.0)
    down = jnp.sum(diagonal, axis=1, keepdims=True)
    across = jnp.sum(diagonal, axis=0, keepdims=True)
    kernel = jnp.exp(-(down + across - 2.0 * gram) / (spread * NCELL)).astype(BF16)
    owner = owners(total, BF16)
    half_way = jnp.dot(owner, kernel, preferred_element_type=F32).astype(BF16)
    full = lax.dot_general(half_way, owner, (((1,), (1,)), ((), ())), preferred_element_type=F32)
    full = jnp.where(same_line(total), full, 0.0)
    mixer[...] = full.astype(BF16)
    ksum = jnp.sum(full, axis=1, keepdims=True)
    own[...] = jnp.broadcast_to(1.0 + rate * coeff * ksum, (wide, LANES))
    for fetch in fetches:
        fetch.wait()

    def step(i, carry):
        for t in range(BLOCK // TILE):
            at = i * BLOCK + t * TILE
            part = lines_of(at, TILE)
            states = [near_ref[:, part, :].reshape(high, LANES)] + [ref[part, :] for ref in far_refs]
            slopes = grads[:, part, :].reshape(wide, LANES)
            new = mix(mixer, own, numbers_ref, total, jnp.concatenate(states, axis=0), slopes)
            near_out[:, part, :] = new[:high].reshape(half, TILE, LANES)
            for x, far_out in enumerate(far_outs):
                far_out[part, :] = new[high + x * TILE : high + (x + 1) * TILE]
        return carry

    lax.fori_loop(0, lines // BLOCK, step, 0)


def update_pieces(numbers, grams, near, far, grads, groups, lines):
    half = len(far)
    total = 2 * half
    wide = total * TILE
    out_shape = [jax.ShapeDtypeStruct((half, lines, LANES), BF16)]
    out_shape += [jax.ShapeDtypeStruct((lines, LANES), BF16)] * half
    return call(
        functools.partial(update_pieces_body, half, lines, groups),
        "update_pieces",
        flops=4 * wide * wide * LANES * (lines // TILE),
        moved=6 * total * lines * LANES,
        in_specs=[IN_VMEM] * (half + 3) + [IN_HBM] * len(groups),
        out_specs=[IN_VMEM] * len(out_shape),
        out_shape=out_shape,
        scratch_shapes=[
            pltpu.VMEM((wide, wide), BF16),
            pltpu.VMEM((wide, LANES), F32),
            pltpu.VMEM((total, lines, LANES), BF16),
            pltpu.SemaphoreType.DMA((total,)),
        ],
    )(near, *far, numbers, grams, *grads)


def exchange(piece, k, slabs):
    return lax.ppermute(piece, "slab", [(i, i ^ k) for i in range(slabs)])


def swap_near(pieces, slabs):
    groups = [list(range(slabs // 2)), list(range(slabs // 2, slabs))]
    return lax.all_to_all(pieces, "slab", 0, 0, axis_index_groups=groups, tiled=True)


GRADIENTS = ((8,), (9, 10, 11), (0, 1, 2, 3, 4, 5, 6, 7), (12, 13, 14, 15))


def by_halves(particles, observed, precision, spread, anneal, step_size):
    slabs = lax.axis_size("slab")
    half = slabs // 2
    lines = NCELL // slabs // LANES
    row = in_hbm(particles)
    fields = [in_hbm(field.reshape(-1, LANES)) for field in (observed, precision)]
    *far, obs, prec = split_pieces(row, slabs, False, fields)
    far = [exchange(piece, half + x, slabs) for x, piece in enumerate(far)]
    near = swap_near(split_pieces(row, slabs, True, [])[0], slabs)
    grads = []
    numbers = [spread, anneal, step_size]
    for n, group in enumerate(GRADIENTS):
        if group[0] < half:
            arrays, views = [near], [(0, k, 0) for k in group]
        else:
            arrays, views = [far[k - half] for k in group], [(j, None, 0) for j in range(len(group))]
        gates = [numbers] if n else []
        given = [] if n else numbers
        slopes, rows = gradient_pieces(arrays, tuple(views), obs, prec, given, gates, 0 if n else LATE)
        grads.append(in_hbm(slopes))
        numbers = numbers if n else rows
    grams = swap(gram_pieces(near, far, lines, grads[:2]))
    new_near, *new_far = update_pieces(numbers, grams, near, far, grads, GRADIENTS, lines)
    new_near = swap_near(new_near, slabs)
    new_far = [exchange(piece, half + x, slabs) for x, piece in enumerate(new_far)]
    row = join_pieces(None, slabs, new_far[:1], [(0, None, half)], LATE)
    row = join_pieces(row, slabs, [new_near], [(0, k, k) for k in range(half)])
    for group in ((1, 2, 3), (4, 5), (6, 7)):
        pieces = [(n, None, half + x) for n, x in enumerate(group)]
        row = join_pieces(row, slabs, [new_far[x] for x in group], pieces)
    return row


def on_device(particles, observed, precision, spread, anneal, step_size):
    slabs = lax.axis_size("slab")
    total = particles.shape[0] * slabs
    lines = NCELL // slabs // LANES
    if slabs == 16:
        return by_halves(particles, observed, precision, spread, anneal, step_size)
    sent, begun = cuts(lines)
    fields = [observed.reshape(-1, LANES), precision.reshape(-1, LANES)]
    numbers = [spread, anneal, step_size]
    first, obs, prec, scalars = split_row(particles, slabs, 0, sent, True, fields, numbers, [])
    parts = [swap(first)]
    if sent < lines:
        parts += [swap(split_row(particles, slabs, sent, lines, False, [], [], [scalars])[0])]
    if total * TILE > 256:
        grads = slab_gradient(parts, obs, prec, lines, 0, lines)
        states = jnp.concatenate([parts[0][:, :sent]] + parts[1:], axis=1)
        new = plain_update(spread, anneal, step_size, states, grads)
        return join_row(swap(new), lines, 0, None)
    if sent == lines:
        grads = slab_gradient(parts, obs, prec, lines, 0, lines)
        grams = swap(slab_gram(parts[0], lines, slabs, [], []))
        new = slab_update(scalars, grams, parts, grads, 0, lines, [])
        return join_row(swap(new), lines, 0, None)
    gram = slab_gram(parts[0], sent, 1, [], [])
    early = slab_gradient(parts[:1], obs, prec, lines, 0, begun)
    grams = swap(slab_gram(parts[1], lines - sent, slabs, [gram], [early]))
    late = slab_gradient(parts, obs, prec, lines, begun, lines)
    new = slab_update(scalars, grams, parts[:1], early, 0, begun, [])
    rest = slab_update(scalars, grams, parts, late, begun, lines, [new])
    row = join_row(swap(new), lines, 0, None)
    return join_row(swap(rest), lines, begun, row)


def solution(mesh):
    in_specs = (
        P(("groups", "slab"), None),
        P("groups"),
        P("groups"),
        P("groups"),
        P("groups"),
        P("groups"),
    )
    out_specs = P(("groups", "slab"), None)
    return jax.shard_map(
        on_device, mesh=mesh, in_specs=in_specs, out_specs=out_specs, check_vma=False
    )
```

```python
import functools

import jax
import jax.numpy as jnp
from jax import lax
from jax.experimental import pallas as pl
from jax.experimental.pallas import tpu as pltpu
from jax.sharding import PartitionSpec as P

GRID_X = 1024
GRID_Y = 1024
NCELL = 1048576
LANES = 128
LINE = GRID_Y // LANES
TILE = 16

prior_scale = 0.25
mass_term = 1.0

F32 = jnp.float32
BF16 = jnp.bfloat16
MIB = 1024 * 1024


def call(body, name, flops=0, moved=0, limit=16, **kwargs):
    return pl.pallas_call(
        body,
        name=name,
        compiler_params=pltpu.CompilerParams(vmem_limit_bytes=limit * MIB),
        cost_estimate=pl.CostEstimate(flops=flops, bytes_accessed=moved, transcendentals=0),
        **kwargs,
    )


IN_VMEM = pl.BlockSpec(memory_space=pltpu.VMEM)
IN_HBM = pl.BlockSpec(memory_space=pltpu.HBM)


def in_hbm(array):
    return pltpu.with_memory_space_constraint(array, pltpu.HBM)


BLOCK = 4 * TILE


def cuts(lines):
    if lines % (8 * BLOCK):
        return lines, lines
    return lines * 3 // 4, lines * 3 // 4 - BLOCK


def split_body(lines, begin, rim, fields, numbers, row_ref, *refs):
    field_refs, number_refs = refs[:fields], refs[fields : fields + numbers]
    out_ref, *slab_refs, rows_ref = refs[-7 - fields : -5]
    held, edges, sems, edge_sems, field_sems = refs[-5:]
    for k, number_ref in enumerate(number_refs):
        rows_ref[k : k + 1, :] = jnp.broadcast_to(number_ref[...].reshape(1, 1), (1, LANES))
    slabs, count, _ = out_ref.shape
    count -= TILE * rim
    size = count * LANES
    cells = lines * LANES

    def part(slab):
        source = row_ref.at[:, pl.ds(slab * cells + begin * LANES, size)]
        return pltpu.make_async_copy(source, held.at[:, pl.ds(slab * size, size)], sems.at[slab])

    def edge(slab):
        source = row_ref.at[:, pl.ds(slab * cells - GRID_Y, GRID_Y)]
        return pltpu.make_async_copy(source, edges.at[:, pl.ds(slab * GRID_Y, GRID_Y)], edge_sems.at[slab])

    def grid_row(ref, start):
        return ref[:, pl.ds(start, GRID_Y)].astype(F32).reshape(LINE, LANES)

    for slab in range(slabs):
        part(slab).start()
        if rim and slab:
            edge(slab).start()
    mine = pl.ds(pl.multiple_of(lax.axis_index("slab") * lines, TILE), lines)
    fetches = [
        pltpu.make_async_copy(source.at[mine, :], target, field_sems.at[k])
        for k, (source, target) in enumerate(zip(field_refs, slab_refs))
    ]
    for fetch in fetches:
        fetch.start()
    part(0).wait()
    outside = jnp.zeros((LINE, LANES), F32)
    for slab in range(slabs):
        if slab + 1 < slabs:
            part(slab + 1).wait()
        out_ref[slab, :count, :] = held[:, pl.ds(slab * size, size)].reshape(count, LANES)
        if rim:
            if slab:
                edge(slab).wait()
            below = grid_row(held, (slab + 1) * size) if slab + 1 < slabs else outside
            above = grid_row(edges, slab * GRID_Y) if slab else outside
            out_ref[slab, count:, :] = jnp.concatenate([below, above], axis=0).astype(BF16)
    for fetch in fetches:
        fetch.wait()


def split_row(row, slabs, begin, end, rim, fields, numbers, earlier):
    lines = row.shape[1] // slabs // LANES
    count = end - begin
    return call(
        functools.partial(split_body, lines, begin, rim, len(fields), len(numbers)),
        "split_row",
        moved=6 * slabs * count * LANES,
        in_specs=[IN_HBM] * (1 + len(fields)) + [IN_VMEM] * len(numbers) + [IN_HBM] * len(earlier),
        out_specs=[IN_VMEM] * (2 + len(fields)),
        out_shape=[jax.ShapeDtypeStruct((slabs, count + TILE * rim, LANES), BF16)]
        + [jax.ShapeDtypeStruct((lines, LANES), BF16)] * len(fields)
        + [jax.ShapeDtypeStruct((8, LANES), F32)],
        scratch_shapes=[
            pltpu.VMEM((1, slabs * count * LANES), BF16),
            pltpu.VMEM((1, slabs * GRID_Y), BF16),
            pltpu.SemaphoreType.DMA((slabs,)),
            pltpu.SemaphoreType.DMA((slabs,)),
            pltpu.SemaphoreType.DMA((2,)),
        ],
    )(row, *fields, *numbers, *earlier)


def join_body(lines, begin, slabs_ref, *refs):
    row_ref, held, sems = refs[-3:]
    slabs, count, _ = slabs_ref.shape
    size = count * LANES
    copies = []
    for slab in range(slabs):
        at = pl.ds(slab * size, size)
        held[:, at] = slabs_ref[slab].reshape(1, size)
        target = row_ref.at[:, pl.ds((slab * lines + begin) * LANES, size)]
        copies.append(pltpu.make_async_copy(held.at[:, at], target, sems.at[slab]))
        copies[-1].start()
    for copy in copies:
        copy.wait()


def join_row(slabs, lines, begin, row):
    total, count, _ = slabs.shape
    begun = [] if row is None else [row]
    return call(
        functools.partial(join_body, lines, begin),
        "join_row",
        moved=6 * slabs.size,
        in_specs=[IN_VMEM] + [IN_HBM] * len(begun),
        out_specs=IN_HBM,
        out_shape=jax.ShapeDtypeStruct((1, total * lines * LANES), BF16),
        input_output_aliases={1: 0} if begun else {},
        scratch_shapes=[pltpu.VMEM((1, slabs.size), BF16), pltpu.SemaphoreType.DMA((total,))],
    )(slabs, *begun)


def same_line(total):
    wide = total * TILE
    row = lax.broadcasted_iota(jnp.int32, (wide, wide), 0)
    col = lax.broadcasted_iota(jnp.int32, (wide, wide), 1)
    return row % TILE == col % TILE


def members(total, dtype):
    wide = total * TILE
    row = lax.broadcasted_iota(jnp.int32, (wide, total), 0)
    col = lax.broadcasted_iota(jnp.int32, (wide, total), 1)
    return (row // TILE == col).astype(dtype)


def gram_body(steps, tiles, parts, states_ref, *refs):
    out_ref, pairs = refs[-2:]
    total = states_ref.shape[0]
    wide = total * TILE
    pairs[...] = jnp.zeros_like(pairs)

    def step(i, carry):
        parts = [
            states_ref[:, pl.ds(pl.multiple_of((i * tiles + t) * TILE, TILE), TILE), :].reshape(wide, LANES)
            for t in range(tiles)
        ]
        block = jnp.concatenate(parts, axis=1)
        pairs[...] += lax.dot_general(block, block, (((1,), (1,)), ((), ())), preferred_element_type=F32)
        return carry

    lax.fori_loop(0, steps, step, 0)
    equal = jnp.where(same_line(total), pairs[...], 0.0)
    rows = jnp.sum(equal.reshape(total, TILE, wide), axis=1)
    gram = jnp.dot(rows, members(total, F32), precision=lax.Precision.HIGHEST, preferred_element_type=F32)
    gram = jnp.concatenate([gram, jnp.zeros((total, LANES - total), F32)], axis=1)
    for part_ref in refs[:parts]:
        gram += part_ref[0]
    out_ref[...] = jnp.broadcast_to(gram[None], out_ref.shape)


def slab_gram(states, lines, copies, parts, earlier):
    total = states.shape[0]
    wide = total * TILE
    tiles = min(8, lines // TILE)
    return call(
        functools.partial(gram_body, lines // TILE // tiles, tiles, len(parts)),
        "slab_gram",
        flops=2 * wide * wide * LANES * (lines // TILE),
        moved=2 * states.size,
        in_specs=[IN_VMEM] * (1 + len(parts)) + [IN_HBM] * len(earlier),
        out_specs=IN_VMEM,
        out_shape=jax.ShapeDtypeStruct((copies, total, LANES), F32),
        scratch_shapes=[pltpu.VMEM((wide, wide), F32)],
    )(states, *parts, *earlier)


def gradient_body(lines, begin, end, parts, *refs):
    observed, precision, out_ref, grads, sems = refs[parts:]
    total = grads.shape[0]
    first = refs[0].shape[1] - TILE
    rows = BLOCK // LINE
    group = 4
    shape = (rows, LINE, LANES)
    lane = lax.broadcasted_iota(jnp.int32, (1, LINE, LANES), 2)
    line = lax.broadcasted_iota(jnp.int32, (1, LINE, LANES), 1)

    def load(particle, at, count):
        ref, at = (refs[0], at) if at < first else (refs[1], at - first)
        return ref[particle, at : at + count, :].astype(F32)

    def rim(particle):
        return refs[0][particle, first:, :].astype(F32)

    stores = []
    for k, at in enumerate(range(begin, end, BLOCK)):
        mine = slice(at - begin, at - begin + BLOCK)
        obs = observed[at : at + BLOCK, :].astype(F32).reshape(shape)
        prec = precision[at : at + BLOCK, :].astype(F32).reshape(shape)

        def step(i, carry):
            for p in range(group):
                particle = i * group + p
                here = load(particle, at, BLOCK)
                before = load(particle, at - TILE, TILE) if at else rim(particle)
                after = load(particle, at + BLOCK, TILE) if at + BLOCK < lines else rim(particle)
                above = jnp.concatenate([before[LINE:], here[:-LINE]], axis=0).reshape(shape)
                below = jnp.concatenate([here[LINE:], after[:LINE]], axis=0).reshape(shape)
                field = here.reshape(shape)
                turned = pltpu.roll(field, 1, 2)
                carried = jnp.where(line == 0, 0.0, pltpu.roll(turned, 1, 1))
                left = jnp.where(lane == 0, carried, turned)
                turned = pltpu.roll(field, LANES - 1, 2)
                carried = jnp.where(line == LINE - 1, 0.0, pltpu.roll(turned, LINE - 1, 1))
                right = jnp.where(lane == LANES - 1, carried, turned)
                laplace = (4.0 + mass_term) * field - (below + above + right + left)
                squash = jnp.tanh(field)
                result = prec * (obs - squash) * (1.0 - squash * squash) - prior_scale * laplace
                grads[particle, mine, :] = result.reshape(BLOCK, LANES).astype(BF16)
            return carry

        lax.fori_loop(0, total // group, step, 0)
        stores.append(pltpu.make_async_copy(grads.at[:, mine, :], out_ref.at[:, mine, :], sems.at[k]))
        stores[-1].start()
    for store in stores:
        store.wait()


def slab_gradient(parts, observed, precision, lines, begin, end):
    total = parts[0].shape[0]
    count = end - begin
    out = jax.ShapeDtypeStruct((total, count, LANES), BF16)
    return call(
        functools.partial(gradient_body, lines, begin, end, len(parts)),
        "slab_gradient",
        flops=30 * out.size,
        moved=8 * out.size,
        in_specs=[IN_VMEM] * (len(parts) + 2),
        out_specs=IN_HBM,
        out_shape=out,
        scratch_shapes=[pltpu.VMEM(out.shape, BF16), pltpu.SemaphoreType.DMA((count // BLOCK,))],
    )(*parts, observed, precision)


def update_body(begin, end, parts, *refs):
    states_refs, refs = refs[:parts], refs[parts:]
    scalars_ref, grams_ref, grads_ref = refs[:3]
    out_ref, grads, mixer, own, sem = refs[-5:]
    total = out_ref.shape[0]
    wide = total * TILE
    fetch = pltpu.make_async_copy(grads_ref, grads, sem)
    fetch.start()
    gram = jnp.sum(grams_ref[...], axis=0)[:, :total]
    row = lax.broadcasted_iota(jnp.int32, (total, total), 0)
    col = lax.broadcasted_iota(jnp.int32, (total, total), 1)
    diagonal = jnp.where(row == col, gram, 0.0)
    down = jnp.sum(diagonal, axis=1, keepdims=True)
    across = jnp.sum(diagonal, axis=0, keepdims=True)
    member = members(total, BF16)
    spread, anneal, step_size = (scalars_ref[k : k + 1, :1] for k in range(3))
    rate = step_size / total
    coeff = 2.0 * anneal / spread
    kernel = jnp.exp(-(down + across - 2.0 * gram) / (spread * NCELL)).astype(BF16)
    ksum = jnp.sum(kernel.astype(F32), axis=1, keepdims=True)
    half = jnp.dot(member, kernel, preferred_element_type=F32).astype(BF16)
    full = lax.dot_general(half, member, (((1,), (1,)), ((), ())), preferred_element_type=F32)
    mixer[...] = jnp.where(same_line(total), full, 0.0).astype(BF16)
    gain = 1.0 + rate * coeff * ksum
    own[...] = jnp.broadcast_to(gain[:, :, None], (total, TILE, LANES)).reshape(wide, LANES)
    fetch.wait()

    done = 0
    for part, states_ref in enumerate(states_refs):
        have = states_ref.shape[1] - (0 if part else TILE)
        low = max(begin - done, 0)
        high = min(end - done, have)
        into = done - begin
        done += have

        def step(i, carry):
            for t in range(BLOCK // TILE):
                at = pl.multiple_of(i * BLOCK + t * TILE, TILE)
                there = pl.ds(pl.multiple_of(at + into, TILE), TILE)
                states = states_ref[:, pl.ds(at, TILE), :].reshape(wide, LANES)
                both = jnp.concatenate([grads[:, there, :].reshape(wide, LANES), states], axis=1)
                mixed = jnp.dot(mixer[...], both, preferred_element_type=F32)
                drive, pulled = mixed[:, :LANES], mixed[:, LANES:]
                new = states.astype(F32) * own[...] + rate * (drive - coeff * pulled)
                out_ref[:, there, :] = new.astype(BF16).reshape(total, TILE, LANES)
            return carry

        lax.fori_loop(low // BLOCK, high // BLOCK, step, 0)


def slab_update(scalars, grams, parts, grads, begin, end, earlier):
    total, count, _ = grads.shape
    wide = total * TILE
    return call(
        functools.partial(update_body, begin, end, len(parts)),
        "slab_update",
        flops=4 * wide * wide * LANES * (count // TILE),
        moved=6 * grads.size,
        in_specs=[IN_VMEM] * len(parts)
        + [IN_VMEM, IN_VMEM, IN_HBM]
        + [IN_HBM] * len(earlier),
        out_specs=IN_VMEM,
        out_shape=jax.ShapeDtypeStruct(grads.shape, BF16),
        scratch_shapes=[
            pltpu.VMEM(grads.shape, BF16),
            pltpu.VMEM((wide, wide), BF16),
            pltpu.VMEM((wide, LANES), F32),
            pltpu.SemaphoreType.DMA,
        ],
    )(*parts, scalars, grams, grads, *earlier)


def plain_update(spread, anneal, step_size, states, grads):
    total, lines, _ = grads.shape
    flat = states[:, :lines].reshape(total, -1)
    gram = lax.dot_general(flat, flat, (((1,), (1,)), ((), ())), preferred_element_type=F32)
    gram = lax.psum(gram, "slab")
    norms = jnp.diagonal(gram)
    kernel = jnp.exp(-(norms[:, None] + norms[None, :] - 2.0 * gram) / (spread[0] * NCELL)).astype(BF16)
    ksum = jnp.sum(kernel.astype(F32), axis=1)
    drive = jnp.dot(kernel, grads.reshape(total, -1), preferred_element_type=F32)
    pulled = jnp.dot(kernel, flat, preferred_element_type=F32)
    values = flat.astype(F32)
    repel = values * ksum[:, None] - pulled
    coeff = 2.0 * anneal[0] / spread[0]
    new = values + step_size[0] / total * (drive + coeff * repel)
    return new.astype(BF16).reshape(grads.shape)


def swap(slabs):
    return lax.all_to_all(slabs, "slab", split_axis=0, concat_axis=0, tiled=True)


def device_at(at, half):
    me = lax.axis_index("slab").astype(jnp.int32)
    return jnp.where(at < half, me - me % half + at, me ^ at)


def lines_of(start, count):
    return pl.ds(pl.multiple_of(start, TILE), count)


def split_pieces_body(slabs, raw, lines, fields, row_ref, *refs):
    half = slabs // 2
    field_refs, near_out, far_outs = refs[:fields], refs[fields], refs[fields + 1 : fields + 1 + half]
    slab_refs, helds, sems = refs[fields + 1 + half : -slabs - 1], refs[-slabs - 1 : -1], refs[-1]
    cells = lines * LANES
    end = row_ref.shape[1]
    started = []

    def fetch(source, target):
        started.append(pltpu.make_async_copy(source, target, sems.at[len(started)]))
        started[-1].start()
        return started[-1]

    copies = []
    for at, held in enumerate(helds):
        slab = device_at(at, half)
        parts = [
            (slab * cells, cells),
            (jnp.minimum((slab + 1) * cells, end - GRID_Y), GRID_Y),
            (jnp.maximum(slab * cells - GRID_Y, 0), GRID_Y),
        ]
        if at < half:
            other = slab ^ half
            parts += [(other * cells, raw * LANES + GRID_Y), (jnp.maximum(other * cells - GRID_Y, 0), GRID_Y)]
        mine, to = [], 0
        for start, size in parts:
            source = row_ref.at[:, pl.ds(pl.multiple_of(start, GRID_Y), size)]
            mine.append(fetch(source, held.at[:, pl.ds(to, size)]))
            to += size
        copies.append(mine)
    me = lax.axis_index("slab").astype(jnp.int32)
    fetches = []
    for n, target in enumerate(slab_refs):
        start = (me if n < fields else me ^ half) * lines
        fetches.append(fetch(field_refs[n % fields].at[lines_of(start, target.shape[0]), :], target))

    def grid_row(held, at):
        return held[:, pl.ds(at, GRID_Y)].astype(F32).reshape(LINE, LANES)

    for at, held in enumerate(helds):
        out_ref = near_out.at[at] if at < half else far_outs[at - half]
        for copy in copies[at]:
            copy.wait()
        slab = device_at(at, half)
        out_ref[:lines, :] = held[:, :cells].reshape(lines, LANES)
        below = jnp.where(slab == slabs - 1, 0.0, grid_row(held, cells))
        above = jnp.where(slab == 0, 0.0, grid_row(held, cells + GRID_Y))
        out_ref[lines : lines + TILE, :] = jnp.concatenate([below, above], axis=0).astype(BF16)
        if at < half:
            start = cells + 2 * GRID_Y
            to = lines + TILE
            out_ref[to : to + raw, :] = held[:, start : start + raw * LANES].reshape(raw, LANES)
            below = grid_row(held, start + raw * LANES)
            above = jnp.where(slab ^ half == 0, 0.0, grid_row(held, start + raw * LANES + GRID_Y))
            out_ref[to + raw :, :] = jnp.concatenate([below, above], axis=0).astype(BF16)
    for copy in fetches:
        copy.wait()


def split_pieces(row, slabs, raw, fields):
    lines = row.shape[1] // slabs // LANES
    half = slabs // 2
    rim = lines + TILE
    size = rim + raw + TILE
    out_shape = [jax.ShapeDtypeStruct((half, size, LANES), BF16)]
    out_shape += [jax.ShapeDtypeStruct((rim, LANES), BF16)] * half
    out_shape += [jax.ShapeDtypeStruct((lines, LANES), BF16)] * len(fields)
    out_shape += [jax.ShapeDtypeStruct((raw, LANES), BF16)] * len(fields)
    return call(
        functools.partial(split_pieces_body, slabs, raw, lines, len(fields)),
        "split_pieces",
        moved=6 * half * (rim + size) * LANES,
        in_specs=[IN_HBM] * (1 + len(fields)),
        out_specs=[IN_VMEM] * len(out_shape),
        out_shape=out_shape,
        scratch_shapes=[pltpu.VMEM((1, size * LANES), BF16)] * half
        + [pltpu.VMEM((1, rim * LANES), BF16)] * half
        + [pltpu.SemaphoreType.DMA((8 * slabs + 2 * len(fields),))],
    )(row, *fields)


def join_pieces_body(pieces, half, raw, lines, begun, arrays, *refs):
    row_ref, helds, sems = refs[begun + arrays], refs[begun + arrays + 1 : -1], refs[-1]
    cells = lines * LANES
    skip = raw * LANES
    copies = []
    for (array, lead, at), held in zip(pieces, helds):
        ref = refs[begun + array]
        piece = ref[...] if lead is None else ref[lead]
        held[...] = piece.reshape(held.shape)
        slab = device_at(at, half)
        if at < half:
            parts = [(0, cells, slab * cells), (cells, skip, (slab ^ half) * cells)]
        else:
            parts = [(0, cells - skip, slab * cells + skip)]
        for begin, size, start in parts:
            target = row_ref.at[:, pl.ds(pl.multiple_of(start, GRID_Y), size)]
            copies.append(pltpu.make_async_copy(held.at[:, pl.ds(begin, size)], target, sems.at[len(copies)]))
            copies[-1].start()
    for copy in copies:
        copy.wait()


def join_pieces(row, slabs, raw, arrays, pieces):
    sizes = [arrays[piece[0]].shape[-2] * LANES for piece in pieces]
    begun = [] if row is None else [row]
    return call(
        functools.partial(
            join_pieces_body, pieces, slabs // 2, raw, NCELL // slabs // LANES, len(begun), len(arrays)
        ),
        "join_pieces",
        moved=6 * sum(sizes),
        in_specs=[IN_HBM] * len(begun) + [IN_VMEM] * len(arrays),
        out_specs=IN_HBM,
        out_shape=jax.ShapeDtypeStruct((1, NCELL), BF16),
        input_output_aliases={0: 0} if begun else {},
        scratch_shapes=[pltpu.VMEM((1, size), BF16) for size in sizes]
        + [pltpu.SemaphoreType.DMA((2 * len(sizes),))],
    )(*begun, *arrays)


def owners(total, dtype):
    wide = total * TILE
    row = lax.broadcasted_iota(jnp.int32, (wide, total), 0)
    col = lax.broadcasted_iota(jnp.int32, (wide, total), 1)
    return (device_at(row // TILE, total // 2) == col).astype(dtype)


def gram_pieces_body(lines, total, near_ref, *refs):
    half = total // 2
    pieces, out_ref, pairs = refs[:half], refs[-2], refs[-1]
    wide = total * TILE
    tiles = 4
    pairs[...] = jnp.zeros_like(pairs)

    def step(i, carry):
        parts = []
        for t in range(tiles):
            at = lines_of((i * tiles + t) * TILE, TILE)
            near = near_ref[:, at, :].reshape(wide // 2, LANES)
            parts.append(jnp.concatenate([near] + [piece[at, :] for piece in pieces], axis=0))
        block = jnp.concatenate(parts, axis=1)
        pairs[...] += lax.dot_general(block, block, (((1,), (1,)), ((), ())), preferred_element_type=F32)
        return carry

    lax.fori_loop(0, lines // TILE // tiles, step, 0)
    equal = jnp.where(same_line(total), pairs[...], 0.0)
    exact = {"precision": lax.Precision.HIGHEST, "preferred_element_type": F32}
    owner = owners(total, F32)
    half_way = jnp.dot(equal, owner, **exact)
    gram = lax.dot_general(owner, half_way, (((0,), (0,)), ((), ())), **exact)
    gram = jnp.concatenate([gram, jnp.zeros((total, LANES - total), F32)], axis=1)
    out_ref[...] = jnp.broadcast_to(gram[None], out_ref.shape)


def gram_pieces(near, far, lines, gates, early):
    total = 2 * len(far)
    wide = total * TILE
    return call(
        functools.partial(gram_pieces_body, lines, total),
        "gram_pieces",
        flops=2 * wide * wide * LANES * (lines // TILE),
        moved=2 * total * lines * LANES,
        in_specs=[IN_VMEM] * (1 + len(far)) + [IN_HBM] * len(gates) + [IN_VMEM] * len(early),
        out_specs=IN_VMEM,
        out_shape=jax.ShapeDtypeStruct((total, total, LANES), F32),
        scratch_shapes=[pltpu.VMEM((wide, wide), F32)],
    )(near, *far, *gates, *early)


def block_gradient(load, i, count, observed, precision):
    start = i * BLOCK
    at = lines_of(start, BLOCK)
    shape = (BLOCK // LINE, LINE, LANES)
    lane = lax.broadcasted_iota(jnp.int32, (1, LINE, LANES), 2)
    line = lax.broadcasted_iota(jnp.int32, (1, LINE, LANES), 1)
    obs = observed[at, :].astype(F32).reshape(shape)
    prec = precision[at, :].astype(F32).reshape(shape)
    here = load(start, BLOCK).astype(F32)
    before = load(jnp.where(i == 0, count, start - TILE), TILE).astype(F32)
    after = load(start + BLOCK, TILE).astype(F32)
    above = jnp.concatenate([before[LINE:], here[:-LINE]], axis=0).reshape(shape)
    below = jnp.concatenate([here[LINE:], after[:LINE]], axis=0).reshape(shape)
    field = here.reshape(shape)
    turned = pltpu.roll(field, 1, 2)
    carried = jnp.where(line == 0, 0.0, pltpu.roll(turned, 1, 1))
    left = jnp.where(lane == 0, carried, turned)
    turned = pltpu.roll(field, LANES - 1, 2)
    carried = jnp.where(line == LINE - 1, 0.0, pltpu.roll(turned, LINE - 1, 1))
    right = jnp.where(lane == LANES - 1, carried, turned)
    laplace = (4.0 + mass_term) * field - (below + above + right + left)
    squash = jnp.tanh(field)
    result = prec * (obs - squash) * (1.0 - squash * squash) - prior_scale * laplace
    return result.reshape(BLOCK, LANES).astype(BF16)


def gradient_pieces_body(views, arrays, numbers, *refs):
    observed, precision, *number_refs = refs[arrays : arrays + 2 + numbers]
    out_ref, rows_ref, grads, sems = refs[-4:]
    for n, number_ref in enumerate(number_refs):
        rows_ref[n : n + 1, :] = jnp.full((1, LANES), number_ref[0], F32)
    count = observed.shape[0]
    steps = count // BLOCK

    def store(i):
        at = lines_of(i * BLOCK, BLOCK)
        return pltpu.make_async_copy(grads.at[:, at, :], out_ref.at[:, at, :], sems.at[i])

    def step(i, carry):
        for p, (array, lead) in enumerate(views):

            def load(start, size):
                part = lines_of(start, size)
                return refs[array][part, :] if lead is None else refs[array][lead, part, :]

            grads[p, lines_of(i * BLOCK, BLOCK), :] = block_gradient(load, i, count, observed, precision)
        store(i).start()
        return carry

    def finish(i, carry):
        store(i).wait()
        return carry

    lax.fori_loop(0, steps, step, 0)
    lax.fori_loop(0, steps, finish, 0)


def gradient_pieces(arrays, views, observed, precision, numbers):
    count = observed.shape[0]
    out = pltpu.HBM((len(views), count, LANES), BF16)
    size = len(views) * count * LANES
    return call(
        functools.partial(gradient_pieces_body, views, len(arrays), len(numbers)),
        "gradient_pieces",
        flops=30 * size,
        moved=8 * size,
        in_specs=[IN_VMEM] * (len(arrays) + 2)
        + [pl.BlockSpec(memory_space=pltpu.SMEM)] * len(numbers),
        out_specs=[IN_HBM, IN_VMEM],
        out_shape=[out, jax.ShapeDtypeStruct((8, LANES), F32)],
        scratch_shapes=[pltpu.VMEM(out.shape, BF16), pltpu.SemaphoreType.DMA((count // BLOCK,))],
    )(*arrays, observed, precision, *numbers)


def raw_body(raw, lines, near_ref, *refs):
    out_ref = refs[-1]
    for k in range(near_ref.shape[0]):
        out_ref[k, :raw, :] = near_ref[k, :raw, :]
        below = near_ref[k, raw : raw + TILE, :].astype(F32)[:LINE]
        above = near_ref[k, lines : lines + TILE, :].astype(F32)[LINE:]
        out_ref[k, raw:, :] = jnp.concatenate([below, above], axis=0).astype(BF16)


def raw_states(near, raw, lines, gates):
    out = jax.ShapeDtypeStruct((near.shape[0], raw + TILE, LANES), BF16)
    return call(
        functools.partial(raw_body, raw, lines),
        "raw_states",
        moved=4 * out.size,
        in_specs=[IN_VMEM] * (1 + len(gates)),
        out_specs=IN_VMEM,
        out_shape=out,
    )(near, *gates)


def mix(mixer, own, numbers_ref, total, states, slopes):
    high = mixer.shape[0]
    rate = numbers_ref[2:3, :1] / total
    coeff = 2.0 * numbers_ref[1:2, :1] / numbers_ref[:1, :1]
    both = jnp.concatenate([slopes, states], axis=1)
    mixed = jnp.dot(mixer[...], both, preferred_element_type=F32)
    drive, pulled = mixed[:, :LANES], mixed[:, LANES:]
    return (states[:high].astype(F32) * own[...] + rate * (drive - coeff * pulled)).astype(BF16)


def update_pieces_body(half, raw, lines, groups, near_ref, *refs):
    total = 2 * half
    far_refs, refs = refs[:half], refs[half:]
    across_ref, raw_observed, raw_precision, numbers_ref, grams_ref, *refs = refs
    group_refs, near_out, far_outs = refs[: len(groups)], refs[len(groups)], refs[len(groups) + 1 : -5]
    mixer, own, grads, raw_grads, sems = refs[-5:]
    wide = total * TILE
    high = half * TILE
    fetches = []
    for group, group_ref in zip(groups, group_refs):
        for j, at in enumerate(group):
            fetches.append(pltpu.make_async_copy(group_ref.at[j], grads.at[at], sems.at[len(fetches)]))
    for fetch in fetches:
        fetch.start()

    def raw_gradient(i, carry):
        for k in range(total):

            def load(start, size):
                if k < half:
                    return near_ref[k, lines_of(lines + TILE + start, size), :]
                return across_ref[k - half, lines_of(start, size), :]

            part = lines_of(i * BLOCK, BLOCK)
            raw_grads[k, part, :] = block_gradient(load, i, raw, raw_observed, raw_precision)
        return carry

    lax.fori_loop(0, raw // BLOCK, raw_gradient, 0)
    gram = jnp.sum(grams_ref[...], axis=0)[:, :total]
    spread, anneal, step_size = (numbers_ref[k : k + 1, :1] for k in range(3))
    rate = step_size / total
    coeff = 2.0 * anneal / spread
    row = lax.broadcasted_iota(jnp.int32, (total, total), 0)
    col = lax.broadcasted_iota(jnp.int32, (total, total), 1)
    diagonal = jnp.where(row == col, gram, 0.0)
    down = jnp.sum(diagonal, axis=1, keepdims=True)
    across = jnp.sum(diagonal, axis=0, keepdims=True)
    kernel = jnp.exp(-(down + across - 2.0 * gram) / (spread * NCELL)).astype(BF16)
    owner = owners(total, BF16)
    half_way = jnp.dot(owner, kernel, preferred_element_type=F32).astype(BF16)
    full = lax.dot_general(half_way, owner, (((1,), (1,)), ((), ())), preferred_element_type=F32)
    full = jnp.where(same_line(total), full, 0.0)
    mixer[...] = full.astype(BF16)
    ksum = jnp.sum(full, axis=1, keepdims=True)
    own[...] = jnp.broadcast_to(1.0 + rate * coeff * ksum, (wide, LANES))
    for fetch in fetches:
        fetch.wait()

    def slab_step(with_far, i, carry):
        rows = wide if with_far else high
        for t in range(BLOCK // TILE):
            at = i * BLOCK + t * TILE
            part = lines_of(at, TILE)
            states = [near_ref[:, part, :].reshape(high, LANES)] + [ref[part, :] for ref in far_refs]
            slopes = grads[:, part, :].reshape(wide, LANES)
            states = jnp.concatenate(states, axis=0)
            new = mix(mixer.at[:rows, :], own.at[:rows, :], numbers_ref, total, states, slopes)
            near_out[:, part, :] = new[:high].reshape(half, TILE, LANES)
            if with_far:
                for x, far_out in enumerate(far_outs):
                    far_out[lines_of(at - raw, TILE), :] = new[high + x * TILE : high + (x + 1) * TILE]
        return carry

    here = lax.axis_index("slab").astype(jnp.int32) % half

    def raw_step(i, carry):
        for t in range(BLOCK // TILE):
            at = i * BLOCK + t * TILE
            part = lines_of(at, TILE)
            states = [near_ref[:, lines_of(lines + TILE + at, TILE), :].reshape(high, LANES)]
            slopes = [raw_grads[:half, part, :].reshape(high, LANES)]
            for x in range(half):
                states += [across_ref[here ^ x, part, :]]
                slopes += [raw_grads[half + (here ^ x), part, :]]
            states, slopes = jnp.concatenate(states, axis=0), jnp.concatenate(slopes, axis=0)
            new = mix(mixer.at[:high, :], own.at[:high, :], numbers_ref, total, states, slopes)
            near_out[:, lines_of(lines + at, TILE), :] = new.reshape(half, TILE, LANES)
        return carry

    lax.fori_loop(0, raw // BLOCK, raw_step, 0)
    lax.fori_loop(0, raw // BLOCK, functools.partial(slab_step, False), 0)
    lax.fori_loop(raw // BLOCK, lines // BLOCK, functools.partial(slab_step, True), 0)


def update_pieces(numbers, grams, near, far, across, raw_fields, grads, groups, raw, lines):
    half = len(far)
    total = 2 * half
    wide = total * TILE
    out_shape = [jax.ShapeDtypeStruct((half, lines + raw, LANES), BF16)]
    out_shape += [jax.ShapeDtypeStruct((lines - raw, LANES), BF16)] * half
    return call(
        functools.partial(update_pieces_body, half, raw, lines, groups),
        "update_pieces",
        flops=4 * wide * wide * LANES * (lines // TILE),
        moved=6 * total * lines * LANES,
        in_specs=[IN_VMEM] * (half + 6) + [IN_HBM] * len(groups),
        out_specs=[IN_VMEM] * len(out_shape),
        out_shape=out_shape,
        scratch_shapes=[
            pltpu.VMEM((wide, wide), BF16),
            pltpu.VMEM((wide, LANES), F32),
            pltpu.VMEM((total, lines, LANES), BF16),
            pltpu.VMEM((total, raw, LANES), BF16),
            pltpu.SemaphoreType.DMA((total,)),
        ],
    )(near, *far, across, *raw_fields, numbers, grams, *grads)


def exchange(piece, k, slabs):
    return lax.ppermute(piece, "slab", [(i, i ^ k) for i in range(slabs)])


def swap_near(pieces, slabs):
    groups = [list(range(slabs // 2)), list(range(slabs // 2, slabs))]
    return lax.all_to_all(pieces, "slab", 0, 0, axis_index_groups=groups, tiled=True)


RAW = 128
GRADIENTS = ((8, 9, 10, 11), (12, 13, 14, 15), (0, 1, 2, 3, 4, 5, 6, 7))


def by_halves(particles, observed, precision, spread, anneal, step_size):
    slabs = lax.axis_size("slab")
    half = slabs // 2
    lines = NCELL // slabs // LANES
    row = in_hbm(particles)
    fields = [in_hbm(field.reshape(-1, LANES)) for field in (observed, precision)]
    near, *far = split_pieces(row, slabs, RAW, fields)
    far, (obs, prec, *raw_fields) = far[:half], far[half:]
    near = swap_near(near, slabs)
    far = [exchange(piece, half + x, slabs) for x, piece in enumerate(far)]
    raw_near = raw_states(near, RAW, lines, far)
    across = exchange(raw_near, half, slabs)
    grads = []
    numbers = [spread, anneal, step_size]
    for group in GRADIENTS:
        if group[0] < half:
            arrays, views = [near], [(0, k) for k in group]
        else:
            arrays, views = [far[k - half] for k in group], [(j, None) for j in range(len(group))]
        slopes, rows = gradient_pieces(arrays, tuple(views), obs, prec, [] if grads else numbers)
        grads.append(in_hbm(slopes))
        numbers = numbers if len(grads) > 1 else rows
    grams = swap(gram_pieces(near, far, lines, grads[:1], [raw_near]))
    new_near, *new_far = update_pieces(
        numbers, grams, near, far, across, raw_fields, grads, GRADIENTS, RAW, lines
    )
    new_near = swap_near(new_near, slabs)
    new_far = [exchange(piece, half + x, slabs) for x, piece in enumerate(new_far)]
    row = join_pieces(None, slabs, RAW, [new_near], [(0, k, k) for k in range(half)])
    for group in ((0, 1, 2, 3), (4, 5)):
        pieces = [(n, None, half + x) for n, x in enumerate(group)]
        row = join_pieces(row, slabs, RAW, [new_far[x] for x in group], pieces)
    return join_pieces(row, slabs, RAW, new_far[6:], [(n, None, half + 6 + n) for n in range(half - 6)])


def on_device(particles, observed, precision, spread, anneal, step_size):
    slabs = lax.axis_size("slab")
    total = particles.shape[0] * slabs
    lines = NCELL // slabs // LANES
    if slabs == 16:
        return by_halves(particles, observed, precision, spread, anneal, step_size)
    sent, begun = cuts(lines)
    fields = [observed.reshape(-1, LANES), precision.reshape(-1, LANES)]
    numbers = [spread, anneal, step_size]
    first, obs, prec, scalars = split_row(particles, slabs, 0, sent, True, fields, numbers, [])
    parts = [swap(first)]
    if sent < lines:
        parts += [swap(split_row(particles, slabs, sent, lines, False, [], [], [scalars])[0])]
    if total * TILE > 256:
        grads = slab_gradient(parts, obs, prec, lines, 0, lines)
        states = jnp.concatenate([parts[0][:, :sent]] + parts[1:], axis=1)
        new = plain_update(spread, anneal, step_size, states, grads)
        return join_row(swap(new), lines, 0, None)
    if sent == lines:
        grads = slab_gradient(parts, obs, prec, lines, 0, lines)
        grams = swap(slab_gram(parts[0], lines, slabs, [], []))
        new = slab_update(scalars, grams, parts, grads, 0, lines, [])
        return join_row(swap(new), lines, 0, None)
    gram = slab_gram(parts[0], sent, 1, [], [])
    early = slab_gradient(parts[:1], obs, prec, lines, 0, begun)
    grams = swap(slab_gram(parts[1], lines - sent, slabs, [gram], [early]))
    late = slab_gradient(parts, obs, prec, lines, begun, lines)
    new = slab_update(scalars, grams, parts[:1], early, 0, begun, [])
    rest = slab_update(scalars, grams, parts, late, begun, lines, [new])
    row = join_row(swap(new), lines, 0, None)
    return join_row(swap(rest), lines, begun, row)


def solution(mesh):
    in_specs = (
        P(("groups", "slab"), None),
        P("groups"),
        P("groups"),
        P("groups"),
        P("groups"),
        P("groups"),
    )
    out_specs = P(("groups", "slab"), None)
    return jax.shard_map(
        on_device, mesh=mesh, in_specs=in_specs, out_specs=out_specs, check_vma=False
    )
```

```python
import functools

import jax
import jax.numpy as jnp
from jax import lax
from jax.experimental import pallas as pl
from jax.experimental.pallas import tpu as pltpu
from jax.sharding import PartitionSpec as P

GRID_X = 1024
GRID_Y = 1024
NCELL = 1048576
LANES = 128
LINE = GRID_Y // LANES
TILE = 16

prior_scale = 0.25
mass_term = 1.0

F32 = jnp.float32
BF16 = jnp.bfloat16
MIB = 1024 * 1024


def call(body, name, flops=0, moved=0, limit=16, **kwargs):
    return pl.pallas_call(
        body,
        name=name,
        compiler_params=pltpu.CompilerParams(vmem_limit_bytes=limit * MIB),
        cost_estimate=pl.CostEstimate(flops=flops, bytes_accessed=moved, transcendentals=0),
        **kwargs,
    )


IN_VMEM = pl.BlockSpec(memory_space=pltpu.VMEM)
IN_HBM = pl.BlockSpec(memory_space=pltpu.HBM)


def in_hbm(array):
    return pltpu.with_memory_space_constraint(array, pltpu.HBM)


BLOCK = 4 * TILE


def cuts(lines):
    if lines % (8 * BLOCK):
        return lines, lines
    return lines * 3 // 4, lines * 3 // 4 - BLOCK


def split_body(lines, begin, rim, fields, numbers, row_ref, *refs):
    field_refs, number_refs = refs[:fields], refs[fields : fields + numbers]
    out_ref, *slab_refs, rows_ref = refs[-7 - fields : -5]
    held, edges, sems, edge_sems, field_sems = refs[-5:]
    for k, number_ref in enumerate(number_refs):
        rows_ref[k : k + 1, :] = jnp.broadcast_to(number_ref[...].reshape(1, 1), (1, LANES))
    slabs, count, _ = out_ref.shape
    count -= TILE * rim
    size = count * LANES
    cells = lines * LANES

    def part(slab):
        source = row_ref.at[:, pl.ds(slab * cells + begin * LANES, size)]
        return pltpu.make_async_copy(source, held.at[:, pl.ds(slab * size, size)], sems.at[slab])

    def edge(slab):
        source = row_ref.at[:, pl.ds(slab * cells - GRID_Y, GRID_Y)]
        return pltpu.make_async_copy(source, edges.at[:, pl.ds(slab * GRID_Y, GRID_Y)], edge_sems.at[slab])

    def grid_row(ref, start):
        return ref[:, pl.ds(start, GRID_Y)].astype(F32).reshape(LINE, LANES)

    for slab in range(slabs):
        part(slab).start()
        if rim and slab:
            edge(slab).start()
    mine = pl.ds(pl.multiple_of(lax.axis_index("slab") * lines, TILE), lines)
    fetches = [
        pltpu.make_async_copy(source.at[mine, :], target, field_sems.at[k])
        for k, (source, target) in enumerate(zip(field_refs, slab_refs))
    ]
    for fetch in fetches:
        fetch.start()
    part(0).wait()
    outside = jnp.zeros((LINE, LANES), F32)
    for slab in range(slabs):
        if slab + 1 < slabs:
            part(slab + 1).wait()
        out_ref[slab, :count, :] = held[:, pl.ds(slab * size, size)].reshape(count, LANES)
        if rim:
            if slab:
                edge(slab).wait()
            below = grid_row(held, (slab + 1) * size) if slab + 1 < slabs else outside
            above = grid_row(edges, slab * GRID_Y) if slab else outside
            out_ref[slab, count:, :] = jnp.concatenate([below, above], axis=0).astype(BF16)
    for fetch in fetches:
        fetch.wait()


def split_row(row, slabs, begin, end, rim, fields, numbers, earlier):
    lines = row.shape[1] // slabs // LANES
    count = end - begin
    return call(
        functools.partial(split_body, lines, begin, rim, len(fields), len(numbers)),
        "split_row",
        moved=6 * slabs * count * LANES,
        in_specs=[IN_HBM] * (1 + len(fields)) + [IN_VMEM] * len(numbers) + [IN_HBM] * len(earlier),
        out_specs=[IN_VMEM] * (2 + len(fields)),
        out_shape=[jax.ShapeDtypeStruct((slabs, count + TILE * rim, LANES), BF16)]
        + [jax.ShapeDtypeStruct((lines, LANES), BF16)] * len(fields)
        + [jax.ShapeDtypeStruct((8, LANES), F32)],
        scratch_shapes=[
            pltpu.VMEM((1, slabs * count * LANES), BF16),
            pltpu.VMEM((1, slabs * GRID_Y), BF16),
            pltpu.SemaphoreType.DMA((slabs,)),
            pltpu.SemaphoreType.DMA((slabs,)),
            pltpu.SemaphoreType.DMA((2,)),
        ],
    )(row, *fields, *numbers, *earlier)


def join_body(lines, begin, slabs_ref, *refs):
    row_ref, held, sems = refs[-3:]
    slabs, count, _ = slabs_ref.shape
    size = count * LANES
    copies = []
    for slab in range(slabs):
        at = pl.ds(slab * size, size)
        held[:, at] = slabs_ref[slab].reshape(1, size)
        target = row_ref.at[:, pl.ds((slab * lines + begin) * LANES, size)]
        copies.append(pltpu.make_async_copy(held.at[:, at], target, sems.at[slab]))
        copies[-1].start()
    for copy in copies:
        copy.wait()


def join_row(slabs, lines, begin, row):
    total, count, _ = slabs.shape
    begun = [] if row is None else [row]
    return call(
        functools.partial(join_body, lines, begin),
        "join_row",
        moved=6 * slabs.size,
        in_specs=[IN_VMEM] + [IN_HBM] * len(begun),
        out_specs=IN_HBM,
        out_shape=jax.ShapeDtypeStruct((1, total * lines * LANES), BF16),
        input_output_aliases={1: 0} if begun else {},
        scratch_shapes=[pltpu.VMEM((1, slabs.size), BF16), pltpu.SemaphoreType.DMA((total,))],
    )(slabs, *begun)


def same_line(total):
    wide = total * TILE
    row = lax.broadcasted_iota(jnp.int32, (wide, wide), 0)
    col = lax.broadcasted_iota(jnp.int32, (wide, wide), 1)
    return row % TILE == col % TILE


def members(total, dtype):
    wide = total * TILE
    row = lax.broadcasted_iota(jnp.int32, (wide, total), 0)
    col = lax.broadcasted_iota(jnp.int32, (wide, total), 1)
    return (row // TILE == col).astype(dtype)


def gram_body(steps, tiles, parts, states_ref, *refs):
    out_ref, pairs = refs[-2:]
    total = states_ref.shape[0]
    wide = total * TILE
    pairs[...] = jnp.zeros_like(pairs)

    def step(i, carry):
        parts = [
            states_ref[:, pl.ds(pl.multiple_of((i * tiles + t) * TILE, TILE), TILE), :].reshape(wide, LANES)
            for t in range(tiles)
        ]
        block = jnp.concatenate(parts, axis=1)
        pairs[...] += lax.dot_general(block, block, (((1,), (1,)), ((), ())), preferred_element_type=F32)
        return carry

    lax.fori_loop(0, steps, step, 0)
    equal = jnp.where(same_line(total), pairs[...], 0.0)
    rows = jnp.sum(equal.reshape(total, TILE, wide), axis=1)
    gram = jnp.dot(rows, members(total, F32), precision=lax.Precision.HIGHEST, preferred_element_type=F32)
    gram = jnp.concatenate([gram, jnp.zeros((total, LANES - total), F32)], axis=1)
    for part_ref in refs[:parts]:
        gram += part_ref[0]
    out_ref[...] = jnp.broadcast_to(gram[None], out_ref.shape)


def slab_gram(states, lines, copies, parts, earlier):
    total = states.shape[0]
    wide = total * TILE
    tiles = min(8, lines // TILE)
    return call(
        functools.partial(gram_body, lines // TILE // tiles, tiles, len(parts)),
        "slab_gram",
        flops=2 * wide * wide * LANES * (lines // TILE),
        moved=2 * states.size,
        in_specs=[IN_VMEM] * (1 + len(parts)) + [IN_HBM] * len(earlier),
        out_specs=IN_VMEM,
        out_shape=jax.ShapeDtypeStruct((copies, total, LANES), F32),
        scratch_shapes=[pltpu.VMEM((wide, wide), F32)],
    )(states, *parts, *earlier)


def gradient_body(lines, begin, end, parts, *refs):
    observed, precision, out_ref, grads, sems = refs[parts:]
    total = grads.shape[0]
    first = refs[0].shape[1] - TILE
    rows = BLOCK // LINE
    group = 4
    shape = (rows, LINE, LANES)
    lane = lax.broadcasted_iota(jnp.int32, (1, LINE, LANES), 2)
    line = lax.broadcasted_iota(jnp.int32, (1, LINE, LANES), 1)

    def load(particle, at, count):
        ref, at = (refs[0], at) if at < first else (refs[1], at - first)
        return ref[particle, at : at + count, :].astype(F32)

    def rim(particle):
        return refs[0][particle, first:, :].astype(F32)

    stores = []
    for k, at in enumerate(range(begin, end, BLOCK)):
        mine = slice(at - begin, at - begin + BLOCK)
        obs = observed[at : at + BLOCK, :].astype(F32).reshape(shape)
        prec = precision[at : at + BLOCK, :].astype(F32).reshape(shape)

        def step(i, carry):
            for p in range(group):
                particle = i * group + p
                here = load(particle, at, BLOCK)
                before = load(particle, at - TILE, TILE) if at else rim(particle)
                after = load(particle, at + BLOCK, TILE) if at + BLOCK < lines else rim(particle)
                above = jnp.concatenate([before[LINE:], here[:-LINE]], axis=0).reshape(shape)
                below = jnp.concatenate([here[LINE:], after[:LINE]], axis=0).reshape(shape)
                field = here.reshape(shape)
                turned = pltpu.roll(field, 1, 2)
                carried = jnp.where(line == 0, 0.0, pltpu.roll(turned, 1, 1))
                left = jnp.where(lane == 0, carried, turned)
                turned = pltpu.roll(field, LANES - 1, 2)
                carried = jnp.where(line == LINE - 1, 0.0, pltpu.roll(turned, LINE - 1, 1))
                right = jnp.where(lane == LANES - 1, carried, turned)
                laplace = (4.0 + mass_term) * field - (below + above + right + left)
                squash = jnp.tanh(field)
                result = prec * (obs - squash) * (1.0 - squash * squash) - prior_scale * laplace
                grads[particle, mine, :] = result.reshape(BLOCK, LANES).astype(BF16)
            return carry

        lax.fori_loop(0, total // group, step, 0)
        stores.append(pltpu.make_async_copy(grads.at[:, mine, :], out_ref.at[:, mine, :], sems.at[k]))
        stores[-1].start()
    for store in stores:
        store.wait()


def slab_gradient(parts, observed, precision, lines, begin, end):
    total = parts[0].shape[0]
    count = end - begin
    out = jax.ShapeDtypeStruct((total, count, LANES), BF16)
    return call(
        functools.partial(gradient_body, lines, begin, end, len(parts)),
        "slab_gradient",
        flops=30 * out.size,
        moved=8 * out.size,
        in_specs=[IN_VMEM] * (len(parts) + 2),
        out_specs=IN_HBM,
        out_shape=out,
        scratch_shapes=[pltpu.VMEM(out.shape, BF16), pltpu.SemaphoreType.DMA((count // BLOCK,))],
    )(*parts, observed, precision)


def update_body(begin, end, parts, *refs):
    states_refs, refs = refs[:parts], refs[parts:]
    scalars_ref, grams_ref, grads_ref = refs[:3]
    out_ref, grads, mixer, own, sem = refs[-5:]
    total = out_ref.shape[0]
    wide = total * TILE
    fetch = pltpu.make_async_copy(grads_ref, grads, sem)
    fetch.start()
    gram = jnp.sum(grams_ref[...], axis=0)[:, :total]
    row = lax.broadcasted_iota(jnp.int32, (total, total), 0)
    col = lax.broadcasted_iota(jnp.int32, (total, total), 1)
    diagonal = jnp.where(row == col, gram, 0.0)
    down = jnp.sum(diagonal, axis=1, keepdims=True)
    across = jnp.sum(diagonal, axis=0, keepdims=True)
    member = members(total, BF16)
    spread, anneal, step_size = (scalars_ref[k : k + 1, :1] for k in range(3))
    rate = step_size / total
    coeff = 2.0 * anneal / spread
    kernel = jnp.exp(-(down + across - 2.0 * gram) / (spread * NCELL)).astype(BF16)
    ksum = jnp.sum(kernel.astype(F32), axis=1, keepdims=True)
    half = jnp.dot(member, kernel, preferred_element_type=F32).astype(BF16)
    full = lax.dot_general(half, member, (((1,), (1,)), ((), ())), preferred_element_type=F32)
    mixer[...] = jnp.where(same_line(total), full, 0.0).astype(BF16)
    gain = 1.0 + rate * coeff * ksum
    own[...] = jnp.broadcast_to(gain[:, :, None], (total, TILE, LANES)).reshape(wide, LANES)
    fetch.wait()

    done = 0
    for part, states_ref in enumerate(states_refs):
        have = states_ref.shape[1] - (0 if part else TILE)
        low = max(begin - done, 0)
        high = min(end - done, have)
        into = done - begin
        done += have

        def step(i, carry):
            for t in range(BLOCK // TILE):
                at = pl.multiple_of(i * BLOCK + t * TILE, TILE)
                there = pl.ds(pl.multiple_of(at + into, TILE), TILE)
                states = states_ref[:, pl.ds(at, TILE), :].reshape(wide, LANES)
                both = jnp.concatenate([grads[:, there, :].reshape(wide, LANES), states], axis=1)
                mixed = jnp.dot(mixer[...], both, preferred_element_type=F32)
                drive, pulled = mixed[:, :LANES], mixed[:, LANES:]
                new = states.astype(F32) * own[...] + rate * (drive - coeff * pulled)
                out_ref[:, there, :] = new.astype(BF16).reshape(total, TILE, LANES)
            return carry

        lax.fori_loop(low // BLOCK, high // BLOCK, step, 0)


def slab_update(scalars, grams, parts, grads, begin, end, earlier):
    total, count, _ = grads.shape
    wide = total * TILE
    return call(
        functools.partial(update_body, begin, end, len(parts)),
        "slab_update",
        flops=4 * wide * wide * LANES * (count // TILE),
        moved=6 * grads.size,
        in_specs=[IN_VMEM] * len(parts)
        + [IN_VMEM, IN_VMEM, IN_HBM]
        + [IN_HBM] * len(earlier),
        out_specs=IN_VMEM,
        out_shape=jax.ShapeDtypeStruct(grads.shape, BF16),
        scratch_shapes=[
            pltpu.VMEM(grads.shape, BF16),
            pltpu.VMEM((wide, wide), BF16),
            pltpu.VMEM((wide, LANES), F32),
            pltpu.SemaphoreType.DMA,
        ],
    )(*parts, scalars, grams, grads, *earlier)


def plain_update(spread, anneal, step_size, states, grads):
    total, lines, _ = grads.shape
    flat = states[:, :lines].reshape(total, -1)
    gram = lax.dot_general(flat, flat, (((1,), (1,)), ((), ())), preferred_element_type=F32)
    gram = lax.psum(gram, "slab")
    norms = jnp.diagonal(gram)
    kernel = jnp.exp(-(norms[:, None] + norms[None, :] - 2.0 * gram) / (spread[0] * NCELL)).astype(BF16)
    ksum = jnp.sum(kernel.astype(F32), axis=1)
    drive = jnp.dot(kernel, grads.reshape(total, -1), preferred_element_type=F32)
    pulled = jnp.dot(kernel, flat, preferred_element_type=F32)
    values = flat.astype(F32)
    repel = values * ksum[:, None] - pulled
    coeff = 2.0 * anneal[0] / spread[0]
    new = values + step_size[0] / total * (drive + coeff * repel)
    return new.astype(BF16).reshape(grads.shape)


def swap(slabs):
    return lax.all_to_all(slabs, "slab", split_axis=0, concat_axis=0, tiled=True)


def device_at(at, half):
    me = lax.axis_index("slab").astype(jnp.int32)
    return jnp.where(at < half, me - me % half + at, me ^ at)


def lines_of(start, count):
    return pl.ds(pl.multiple_of(start, TILE), count)


def split_pieces_body(slabs, raw, lines, fields, row_ref, *refs):
    half = slabs // 2
    field_refs, near_out, far_outs = refs[:fields], refs[fields], refs[fields + 1 : fields + 1 + half]
    slab_refs, helds, sems = refs[fields + 1 + half : -slabs - 1], refs[-slabs - 1 : -1], refs[-1]
    cells = lines * LANES
    end = row_ref.shape[1]
    started = []

    def fetch(source, target):
        started.append(pltpu.make_async_copy(source, target, sems.at[len(started)]))
        started[-1].start()
        return started[-1]

    copies = []
    for at, held in enumerate(helds):
        slab = device_at(at, half)
        parts = [
            (slab * cells, cells),
            (jnp.minimum((slab + 1) * cells, end - GRID_Y), GRID_Y),
            (jnp.maximum(slab * cells - GRID_Y, 0), GRID_Y),
        ]
        if at < half:
            other = slab ^ half
            parts += [(other * cells, raw * LANES + GRID_Y), (jnp.maximum(other * cells - GRID_Y, 0), GRID_Y)]
        mine, to = [], 0
        for start, size in parts:
            source = row_ref.at[:, pl.ds(pl.multiple_of(start, GRID_Y), size)]
            mine.append(fetch(source, held.at[:, pl.ds(to, size)]))
            to += size
        copies.append(mine)
    me = lax.axis_index("slab").astype(jnp.int32)
    fetches = []
    for n, target in enumerate(slab_refs):
        start = (me if n < fields else me ^ half) * lines
        fetches.append(fetch(field_refs[n % fields].at[lines_of(start, target.shape[0]), :], target))

    def grid_row(held, at):
        return held[:, pl.ds(at, GRID_Y)].astype(F32).reshape(LINE, LANES)

    for at, held in enumerate(helds):
        out_ref = near_out.at[at] if at < half else far_outs[at - half]
        for copy in copies[at]:
            copy.wait()
        slab = device_at(at, half)
        out_ref[:lines, :] = held[:, :cells].reshape(lines, LANES)
        below = jnp.where(slab == slabs - 1, 0.0, grid_row(held, cells))
        above = jnp.where(slab == 0, 0.0, grid_row(held, cells + GRID_Y))
        out_ref[lines : lines + TILE, :] = jnp.concatenate([below, above], axis=0).astype(BF16)
        if at < half:
            start = cells + 2 * GRID_Y
            to = lines + TILE
            out_ref[to : to + raw, :] = held[:, start : start + raw * LANES].reshape(raw, LANES)
            below = grid_row(held, start + raw * LANES)
            above = jnp.where(slab ^ half == 0, 0.0, grid_row(held, start + raw * LANES + GRID_Y))
            out_ref[to + raw :, :] = jnp.concatenate([below, above], axis=0).astype(BF16)
    for copy in fetches:
        copy.wait()


def split_pieces(row, slabs, raw, fields):
    lines = row.shape[1] // slabs // LANES
    half = slabs // 2
    rim = lines + TILE
    size = rim + raw + TILE
    out_shape = [jax.ShapeDtypeStruct((half, size, LANES), BF16)]
    out_shape += [jax.ShapeDtypeStruct((rim, LANES), BF16)] * half
    out_shape += [jax.ShapeDtypeStruct((lines, LANES), BF16)] * len(fields)
    out_shape += [jax.ShapeDtypeStruct((raw, LANES), BF16)] * len(fields)
    return call(
        functools.partial(split_pieces_body, slabs, raw, lines, len(fields)),
        "split_pieces",
        moved=6 * half * (rim + size) * LANES,
        in_specs=[IN_HBM] * (1 + len(fields)),
        out_specs=[IN_VMEM] * len(out_shape),
        out_shape=out_shape,
        scratch_shapes=[pltpu.VMEM((1, size * LANES), BF16)] * half
        + [pltpu.VMEM((1, rim * LANES), BF16)] * half
        + [pltpu.SemaphoreType.DMA((8 * slabs + 2 * len(fields),))],
    )(row, *fields)


def join_pieces_body(pieces, half, raw, lines, begun, arrays, *refs):
    row_ref, helds, sems = refs[begun + arrays], refs[begun + arrays + 1 : -1], refs[-1]
    cells = lines * LANES
    skip = raw * LANES
    copies = []
    for (array, lead, at), held in zip(pieces, helds):
        ref = refs[begun + array]
        piece = ref[...] if lead is None else ref[lead]
        held[...] = piece.reshape(held.shape)
        slab = device_at(at, half)
        if at < half:
            parts = [(0, cells, slab * cells), (cells, skip, (slab ^ half) * cells)]
        else:
            parts = [(0, cells - skip, slab * cells + skip)]
        for begin, size, start in parts:
            target = row_ref.at[:, pl.ds(pl.multiple_of(start, GRID_Y), size)]
            copies.append(pltpu.make_async_copy(held.at[:, pl.ds(begin, size)], target, sems.at[len(copies)]))
            copies[-1].start()
    for copy in copies:
        copy.wait()


def join_pieces(row, slabs, raw, arrays, pieces):
    sizes = [arrays[piece[0]].shape[-2] * LANES for piece in pieces]
    begun = [] if row is None else [row]
    return call(
        functools.partial(
            join_pieces_body, pieces, slabs // 2, raw, NCELL // slabs // LANES, len(begun), len(arrays)
        ),
        "join_pieces",
        moved=6 * sum(sizes),
        in_specs=[IN_HBM] * len(begun) + [IN_VMEM] * len(arrays),
        out_specs=IN_HBM,
        out_shape=jax.ShapeDtypeStruct((1, NCELL), BF16),
        input_output_aliases={0: 0} if begun else {},
        scratch_shapes=[pltpu.VMEM((1, size), BF16) for size in sizes]
        + [pltpu.SemaphoreType.DMA((2 * len(sizes),))],
    )(*begun, *arrays)


def owners(total, dtype):
    wide = total * TILE
    row = lax.broadcasted_iota(jnp.int32, (wide, total), 0)
    col = lax.broadcasted_iota(jnp.int32, (wide, total), 1)
    return (device_at(row // TILE, total // 2) == col).astype(dtype)


def gram_pieces_body(lines, total, near_ref, *refs):
    half = total // 2
    pieces, out_ref, pairs = refs[:half], refs[-2], refs[-1]
    wide = total * TILE
    tiles = 4
    pairs[...] = jnp.zeros_like(pairs)

    def step(i, carry):
        parts = []
        for t in range(tiles):
            at = lines_of((i * tiles + t) * TILE, TILE)
            near = near_ref[:, at, :].reshape(wide // 2, LANES)
            parts.append(jnp.concatenate([near] + [piece[at, :] for piece in pieces], axis=0))
        block = jnp.concatenate(parts, axis=1)
        pairs[...] += lax.dot_general(block, block, (((1,), (1,)), ((), ())), preferred_element_type=F32)
        return carry

    lax.fori_loop(0, lines // TILE // tiles, step, 0)
    equal = jnp.where(same_line(total), pairs[...], 0.0)
    exact = {"precision": lax.Precision.HIGHEST, "preferred_element_type": F32}
    rows = jnp.sum(equal.reshape(total, TILE, wide), axis=1)
    gram = jnp.dot(rows, owners(total, F32), **exact)
    row = lax.broadcasted_iota(jnp.int32, (total, total), 0)
    col = lax.broadcasted_iota(jnp.int32, (total, total), 1)
    gram = jnp.dot((row == device_at(col, half)).astype(F32), gram, **exact)
    gram = jnp.concatenate([gram, jnp.zeros((total, LANES - total), F32)], axis=1)
    out_ref[...] = jnp.broadcast_to(gram[None], out_ref.shape)


def gram_pieces(near, far, lines, gates, early):
    total = 2 * len(far)
    wide = total * TILE
    return call(
        functools.partial(gram_pieces_body, lines, total),
        "gram_pieces",
        flops=2 * wide * wide * LANES * (lines // TILE),
        moved=2 * total * lines * LANES,
        in_specs=[IN_VMEM] * (1 + len(far)) + [IN_HBM] * len(gates) + [IN_VMEM] * len(early),
        out_specs=IN_VMEM,
        out_shape=jax.ShapeDtypeStruct((total, total, LANES), F32),
        scratch_shapes=[pltpu.VMEM((wide, wide), F32)],
    )(near, *far, *gates, *early)


def block_gradient(load, i, count, observed, precision):
    start = i * BLOCK
    at = lines_of(start, BLOCK)
    shape = (BLOCK // LINE, LINE, LANES)
    lane = lax.broadcasted_iota(jnp.int32, (1, LINE, LANES), 2)
    line = lax.broadcasted_iota(jnp.int32, (1, LINE, LANES), 1)
    obs = observed[at, :].astype(F32).reshape(shape)
    prec = precision[at, :].astype(F32).reshape(shape)
    here = load(start, BLOCK).astype(F32)
    before = load(jnp.where(i == 0, count, start - TILE), TILE).astype(F32)
    after = load(start + BLOCK, TILE).astype(F32)
    above = jnp.concatenate([before[LINE:], here[:-LINE]], axis=0).reshape(shape)
    below = jnp.concatenate([here[LINE:], after[:LINE]], axis=0).reshape(shape)
    field = here.reshape(shape)
    turned = pltpu.roll(field, 1, 2)
    carried = jnp.where(line == 0, 0.0, pltpu.roll(turned, 1, 1))
    left = jnp.where(lane == 0, carried, turned)
    turned = pltpu.roll(field, LANES - 1, 2)
    carried = jnp.where(line == LINE - 1, 0.0, pltpu.roll(turned, LINE - 1, 1))
    right = jnp.where(lane == LANES - 1, carried, turned)
    laplace = (4.0 + mass_term) * field - (below + above + right + left)
    squash = jnp.tanh(field)
    result = prec * (obs - squash) * (1.0 - squash * squash) - prior_scale * laplace
    return result.reshape(BLOCK, LANES).astype(BF16)


def gradient_pieces_body(views, arrays, numbers, *refs):
    observed, precision, *number_refs = refs[arrays : arrays + 2 + numbers]
    out_ref, rows_ref, grads, sems = refs[-4:]
    for n, number_ref in enumerate(number_refs):
        rows_ref[n : n + 1, :] = jnp.full((1, LANES), number_ref[0], F32)
    count = observed.shape[0]
    steps = count // BLOCK

    def store(i):
        at = lines_of(i * BLOCK, BLOCK)
        return pltpu.make_async_copy(grads.at[:, at, :], out_ref.at[:, at, :], sems.at[i])

    def step(i, carry):
        for p, (array, lead) in enumerate(views):

            def load(start, size):
                part = lines_of(start, size)
                return refs[array][part, :] if lead is None else refs[array][lead, part, :]

            grads[p, lines_of(i * BLOCK, BLOCK), :] = block_gradient(load, i, count, observed, precision)
        store(i).start()
        return carry

    def finish(i, carry):
        store(i).wait()
        return carry

    lax.fori_loop(0, steps, step, 0)
    lax.fori_loop(0, steps, finish, 0)


def gradient_pieces(arrays, views, observed, precision, numbers):
    count = observed.shape[0]
    out = pltpu.HBM((len(views), count, LANES), BF16)
    size = len(views) * count * LANES
    return call(
        functools.partial(gradient_pieces_body, views, len(arrays), len(numbers)),
        "gradient_pieces",
        flops=30 * size,
        moved=8 * size,
        in_specs=[IN_VMEM] * (len(arrays) + 2)
        + [pl.BlockSpec(memory_space=pltpu.SMEM)] * len(numbers),
        out_specs=[IN_HBM, IN_VMEM],
        out_shape=[out, jax.ShapeDtypeStruct((8, LANES), F32)],
        scratch_shapes=[pltpu.VMEM(out.shape, BF16), pltpu.SemaphoreType.DMA((count // BLOCK,))],
    )(*arrays, observed, precision, *numbers)


def raw_body(raw, lines, near_ref, *refs):
    out_ref = refs[-1]
    for k in range(near_ref.shape[0]):
        out_ref[k, :raw, :] = near_ref[k, :raw, :]
        below = near_ref[k, raw : raw + TILE, :].astype(F32)[:LINE]
        above = near_ref[k, lines : lines + TILE, :].astype(F32)[LINE:]
        out_ref[k, raw:, :] = jnp.concatenate([below, above], axis=0).astype(BF16)


def raw_states(near, raw, lines, gates):
    out = jax.ShapeDtypeStruct((near.shape[0], raw + TILE, LANES), BF16)
    return call(
        functools.partial(raw_body, raw, lines),
        "raw_states",
        moved=4 * out.size,
        in_specs=[IN_VMEM] * (1 + len(gates)),
        out_specs=IN_VMEM,
        out_shape=out,
    )(near, *gates)


def mix(mixer, own, numbers_ref, total, states, slopes):
    high = mixer.shape[0]
    rate = numbers_ref[2:3, :1] / total
    coeff = 2.0 * numbers_ref[1:2, :1] / numbers_ref[:1, :1]
    both = jnp.concatenate([slopes, states], axis=1)
    mixed = jnp.dot(mixer[...], both, preferred_element_type=F32)
    drive, pulled = mixed[:, :LANES], mixed[:, LANES:]
    return (states[:high].astype(F32) * own[...] + rate * (drive - coeff * pulled)).astype(BF16)


def update_pieces_body(half, raw, lines, groups, near_ref, *refs):
    total = 2 * half
    far_refs, refs = refs[:half], refs[half:]
    across_ref, raw_observed, raw_precision, numbers_ref, grams_ref, *refs = refs
    group_refs, near_to, far_tos = refs[: len(groups)], refs[len(groups)], refs[len(groups) + 1 : -8]
    near_out, far_out, mixer, own, grads, raw_grads, sems, out_sems = refs[-8:]
    wide = total * TILE
    high = half * TILE
    fetches = []
    for group, group_ref in zip(groups, group_refs):
        for j, at in enumerate(group):
            fetches.append(pltpu.make_async_copy(group_ref.at[j], grads.at[at], sems.at[len(fetches)]))
    for fetch in fetches:
        fetch.start()

    def raw_gradient(i, carry):
        for k in range(total):

            def load(start, size):
                if k < half:
                    return near_ref[k, lines_of(lines + TILE + start, size), :]
                return across_ref[k - half, lines_of(start, size), :]

            part = lines_of(i * BLOCK, BLOCK)
            raw_grads[k, part, :] = block_gradient(load, i, raw, raw_observed, raw_precision)
        return carry

    lax.fori_loop(0, raw // BLOCK, raw_gradient, 0)
    gram = jnp.sum(grams_ref[...], axis=0)[:, :total]
    spread, anneal, step_size = (numbers_ref[k : k + 1, :1] for k in range(3))
    rate = step_size / total
    coeff = 2.0 * anneal / spread
    row = lax.broadcasted_iota(jnp.int32, (total, total), 0)
    col = lax.broadcasted_iota(jnp.int32, (total, total), 1)
    diagonal = jnp.where(row == col, gram, 0.0)
    down = jnp.sum(diagonal, axis=1, keepdims=True)
    across = jnp.sum(diagonal, axis=0, keepdims=True)
    kernel = jnp.exp(-(down + across - 2.0 * gram) / (spread * NCELL)).astype(BF16)
    owner = owners(total, BF16)
    half_way = jnp.dot(owner, kernel, preferred_element_type=F32).astype(BF16)
    full = lax.dot_general(half_way, owner, (((1,), (1,)), ((), ())), preferred_element_type=F32)
    full = jnp.where(same_line(total), full, 0.0)
    mixer[...] = full.astype(BF16)
    ksum = jnp.sum(full, axis=1, keepdims=True)
    own[...] = jnp.broadcast_to(1.0 + rate * coeff * ksum, (wide, LANES))
    for fetch in fetches:
        fetch.wait()

    def near_store(i):
        part = lines_of(i * BLOCK, BLOCK)
        return pltpu.make_async_copy(near_out.at[:, part, :], near_to.at[:, part, :], out_sems.at[i, 0])

    def far_store(x, i):
        part = lines_of(i * BLOCK - raw, BLOCK)
        return pltpu.make_async_copy(far_out.at[x, part, :], far_tos[x].at[part, :], out_sems.at[i, 1 + x])

    def slab_step(with_far, i, carry):
        rows = wide if with_far else high
        for t in range(BLOCK // TILE):
            at = i * BLOCK + t * TILE
            part = lines_of(at, TILE)
            states = [near_ref[:, part, :].reshape(high, LANES)] + [ref[part, :] for ref in far_refs]
            slopes = grads[:, part, :].reshape(wide, LANES)
            states = jnp.concatenate(states, axis=0)
            new = mix(mixer.at[:rows, :], own.at[:rows, :], numbers_ref, total, states, slopes)
            near_out[:, part, :] = new[:high].reshape(half, TILE, LANES)
            if with_far:
                far_out[:, lines_of(at - raw, TILE), :] = new[high:].reshape(half, TILE, LANES)
        near_store(i).start()
        if with_far:
            for x in range(half):
                far_store(x, i).start()
        return carry

    here = lax.axis_index("slab").astype(jnp.int32) % half

    def raw_step(i, carry):
        for t in range(BLOCK // TILE):
            at = i * BLOCK + t * TILE
            part = lines_of(at, TILE)
            states = [near_ref[:, lines_of(lines + TILE + at, TILE), :].reshape(high, LANES)]
            slopes = [raw_grads[:half, part, :].reshape(high, LANES)]
            for x in range(half):
                states += [across_ref[here ^ x, part, :]]
                slopes += [raw_grads[half + (here ^ x), part, :]]
            states, slopes = jnp.concatenate(states, axis=0), jnp.concatenate(slopes, axis=0)
            new = mix(mixer.at[:high, :], own.at[:high, :], numbers_ref, total, states, slopes)
            near_out[:, lines_of(lines + at, TILE), :] = new.reshape(half, TILE, LANES)
        near_store(lines // BLOCK + i).start()
        return carry

    def finish(i, carry):
        near_store(i).wait()
        return carry

    def finish_far(i, carry):
        for x in range(half):
            far_store(x, i).wait()
        return carry

    lax.fori_loop(0, raw // BLOCK, raw_step, 0)
    lax.fori_loop(0, raw // BLOCK, functools.partial(slab_step, False), 0)
    lax.fori_loop(raw // BLOCK, lines // BLOCK, functools.partial(slab_step, True), 0)
    lax.fori_loop(0, (lines + raw) // BLOCK, finish, 0)
    lax.fori_loop(raw // BLOCK, lines // BLOCK, finish_far, 0)


def update_pieces(numbers, grams, near, far, across, raw_fields, grads, groups, raw, lines):
    half = len(far)
    total = 2 * half
    wide = total * TILE
    out_shape = [pltpu.HBM((half, lines + raw, LANES), BF16)]
    out_shape += [pltpu.HBM((lines - raw, LANES), BF16)] * half
    return call(
        functools.partial(update_pieces_body, half, raw, lines, groups),
        "update_pieces",
        flops=4 * wide * wide * LANES * (lines // TILE),
        moved=6 * total * lines * LANES,
        in_specs=[IN_VMEM] * (half + 6) + [IN_HBM] * len(groups),
        out_specs=[IN_HBM] * len(out_shape),
        out_shape=out_shape,
        scratch_shapes=[
            pltpu.VMEM((half, lines + raw, LANES), BF16),
            pltpu.VMEM((half, lines - raw, LANES), BF16),
            pltpu.VMEM((wide, wide), BF16),
            pltpu.VMEM((wide, LANES), F32),
            pltpu.VMEM((total, lines, LANES), BF16),
            pltpu.VMEM((total, raw, LANES), BF16),
            pltpu.SemaphoreType.DMA((total,)),
            pltpu.SemaphoreType.DMA(((lines + raw) // BLOCK, 1 + half)),
        ],
    )(near, *far, across, *raw_fields, numbers, grams, *grads)


def exchange(piece, k, slabs):
    return lax.ppermute(piece, "slab", [(i, i ^ k) for i in range(slabs)])


def swap_near(pieces, slabs):
    groups = [list(range(slabs // 2)), list(range(slabs // 2, slabs))]
    return lax.all_to_all(pieces, "slab", 0, 0, axis_index_groups=groups, tiled=True)


RAW = 128
GRADIENTS = ((8, 9, 10, 11), (12, 13, 14, 15), (0, 1, 2, 3, 4, 5, 6, 7))


def by_halves(particles, observed, precision, spread, anneal, step_size):
    slabs = lax.axis_size("slab")
    half = slabs // 2
    lines = NCELL // slabs // LANES
    row = in_hbm(particles)
    fields = [in_hbm(field.reshape(-1, LANES)) for field in (observed, precision)]
    near, *far = split_pieces(row, slabs, RAW, fields)
    far, (obs, prec, *raw_fields) = far[:half], far[half:]
    near = swap_near(near, slabs)
    far = [exchange(piece, half + x, slabs) for x, piece in enumerate(far)]
    raw_near = raw_states(near, RAW, lines, far)
    across = exchange(raw_near, half, slabs)
    grads = []
    numbers = [spread, anneal, step_size]
    for group in GRADIENTS:
        if group[0] < half:
            arrays, views = [near], [(0, k) for k in group]
        else:
            arrays, views = [far[k - half] for k in group], [(j, None) for j in range(len(group))]
        slopes, rows = gradient_pieces(arrays, tuple(views), obs, prec, [] if grads else numbers)
        grads.append(in_hbm(slopes))
        numbers = numbers if len(grads) > 1 else rows
    grams = swap(gram_pieces(near, far, lines, grads[:1], [raw_near]))
    new_near, *new_far = update_pieces(
        numbers, grams, near, far, across, raw_fields, grads, GRADIENTS, RAW, lines
    )
    new_near = swap_near(new_near, slabs)
    new_far = [exchange(piece, half + x, slabs) for x, piece in enumerate(new_far)]
    row = join_pieces(None, slabs, RAW, [new_near], [(0, k, k) for k in range(half)])
    for group in ((0, 1, 2, 3), (4, 5)):
        pieces = [(n, None, half + x) for n, x in enumerate(group)]
        row = join_pieces(row, slabs, RAW, [new_far[x] for x in group], pieces)
    return join_pieces(row, slabs, RAW, new_far[6:], [(n, None, half + 6 + n) for n in range(half - 6)])


def on_device(particles, observed, precision, spread, anneal, step_size):
    slabs = lax.axis_size("slab")
    total = particles.shape[0] * slabs
    lines = NCELL // slabs // LANES
    if slabs == 16:
        return by_halves(particles, observed, precision, spread, anneal, step_size)
    sent, begun = cuts(lines)
    fields = [observed.reshape(-1, LANES), precision.reshape(-1, LANES)]
    numbers = [spread, anneal, step_size]
    first, obs, prec, scalars = split_row(particles, slabs, 0, sent, True, fields, numbers, [])
    parts = [swap(first)]
    if sent < lines:
        parts += [swap(split_row(particles, slabs, sent, lines, False, [], [], [scalars])[0])]
    if total * TILE > 256:
        grads = slab_gradient(parts, obs, prec, lines, 0, lines)
        states = jnp.concatenate([parts[0][:, :sent]] + parts[1:], axis=1)
        new = plain_update(spread, anneal, step_size, states, grads)
        return join_row(swap(new), lines, 0, None)
    if sent == lines:
        grads = slab_gradient(parts, obs, prec, lines, 0, lines)
        grams = swap(slab_gram(parts[0], lines, slabs, [], []))
        new = slab_update(scalars, grams, parts, grads, 0, lines, [])
        return join_row(swap(new), lines, 0, None)
    gram = slab_gram(parts[0], sent, 1, [], [])
    early = slab_gradient(parts[:1], obs, prec, lines, 0, begun)
    grams = swap(slab_gram(parts[1], lines - sent, slabs, [gram], [early]))
    late = slab_gradient(parts, obs, prec, lines, begun, lines)
    new = slab_update(scalars, grams, parts[:1], early, 0, begun, [])
    rest = slab_update(scalars, grams, parts, late, begun, lines, [new])
    row = join_row(swap(new), lines, 0, None)
    return join_row(swap(rest), lines, begun, row)


def solution(mesh):
    in_specs = (
        P(("groups", "slab"), None),
        P("groups"),
        P("groups"),
        P("groups"),
        P("groups"),
        P("groups"),
    )
    out_specs = P(("groups", "slab"), None)
    return jax.shard_map(
        on_device, mesh=mesh, in_specs=in_specs, out_specs=out_specs, check_vma=False
    )
```

```python
import functools

import jax
import jax.numpy as jnp
from jax import lax
from jax.experimental import pallas as pl
from jax.experimental.pallas import tpu as pltpu
from jax.sharding import PartitionSpec as P

GRID_X = 1024
GRID_Y = 1024
NCELL = 1048576
LANES = 128
LINE = GRID_Y // LANES
TILE = 16

prior_scale = 0.25
mass_term = 1.0

F32 = jnp.float32
BF16 = jnp.bfloat16
MIB = 1024 * 1024


def call(body, name, flops=0, moved=0, limit=16, **kwargs):
    return pl.pallas_call(
        body,
        name=name,
        compiler_params=pltpu.CompilerParams(vmem_limit_bytes=limit * MIB),
        cost_estimate=pl.CostEstimate(flops=flops, bytes_accessed=moved, transcendentals=0),
        **kwargs,
    )


IN_VMEM = pl.BlockSpec(memory_space=pltpu.VMEM)
IN_HBM = pl.BlockSpec(memory_space=pltpu.HBM)


def in_hbm(array):
    return pltpu.with_memory_space_constraint(array, pltpu.HBM)


BLOCK = 4 * TILE


def cuts(lines):
    if lines % (8 * BLOCK):
        return lines, lines
    return lines * 3 // 4, lines * 3 // 4 - BLOCK


def split_body(lines, begin, rim, fields, numbers, row_ref, *refs):
    field_refs, number_refs = refs[:fields], refs[fields : fields + numbers]
    out_ref, *slab_refs, rows_ref = refs[-7 - fields : -5]
    held, edges, sems, edge_sems, field_sems = refs[-5:]
    for k, number_ref in enumerate(number_refs):
        rows_ref[k : k + 1, :] = jnp.broadcast_to(number_ref[...].reshape(1, 1), (1, LANES))
    slabs, count, _ = out_ref.shape
    count -= TILE * rim
    size = count * LANES
    cells = lines * LANES

    def part(slab):
        source = row_ref.at[:, pl.ds(slab * cells + begin * LANES, size)]
        return pltpu.make_async_copy(source, held.at[:, pl.ds(slab * size, size)], sems.at[slab])

    def edge(slab):
        source = row_ref.at[:, pl.ds(slab * cells - GRID_Y, GRID_Y)]
        return pltpu.make_async_copy(source, edges.at[:, pl.ds(slab * GRID_Y, GRID_Y)], edge_sems.at[slab])

    def grid_row(ref, start):
        return ref[:, pl.ds(start, GRID_Y)].astype(F32).reshape(LINE, LANES)

    for slab in range(slabs):
        part(slab).start()
        if rim and slab:
            edge(slab).start()
    mine = pl.ds(pl.multiple_of(lax.axis_index("slab") * lines, TILE), lines)
    fetches = [
        pltpu.make_async_copy(source.at[mine, :], target, field_sems.at[k])
        for k, (source, target) in enumerate(zip(field_refs, slab_refs))
    ]
    for fetch in fetches:
        fetch.start()
    part(0).wait()
    outside = jnp.zeros((LINE, LANES), F32)
    for slab in range(slabs):
        if slab + 1 < slabs:
            part(slab + 1).wait()
        out_ref[slab, :count, :] = held[:, pl.ds(slab * size, size)].reshape(count, LANES)
        if rim:
            if slab:
                edge(slab).wait()
            below = grid_row(held, (slab + 1) * size) if slab + 1 < slabs else outside
            above = grid_row(edges, slab * GRID_Y) if slab else outside
            out_ref[slab, count:, :] = jnp.concatenate([below, above], axis=0).astype(BF16)
    for fetch in fetches:
        fetch.wait()


def split_row(row, slabs, begin, end, rim, fields, numbers, earlier):
    lines = row.shape[1] // slabs // LANES
    count = end - begin
    return call(
        functools.partial(split_body, lines, begin, rim, len(fields), len(numbers)),
        "split_row",
        moved=6 * slabs * count * LANES,
        in_specs=[IN_HBM] * (1 + len(fields)) + [IN_VMEM] * len(numbers) + [IN_HBM] * len(earlier),
        out_specs=[IN_VMEM] * (2 + len(fields)),
        out_shape=[jax.ShapeDtypeStruct((slabs, count + TILE * rim, LANES), BF16)]
        + [jax.ShapeDtypeStruct((lines, LANES), BF16)] * len(fields)
        + [jax.ShapeDtypeStruct((8, LANES), F32)],
        scratch_shapes=[
            pltpu.VMEM((1, slabs * count * LANES), BF16),
            pltpu.VMEM((1, slabs * GRID_Y), BF16),
            pltpu.SemaphoreType.DMA((slabs,)),
            pltpu.SemaphoreType.DMA((slabs,)),
            pltpu.SemaphoreType.DMA((2,)),
        ],
    )(row, *fields, *numbers, *earlier)


def join_body(lines, begin, slabs_ref, *refs):
    row_ref, held, sems = refs[-3:]
    slabs, count, _ = slabs_ref.shape
    size = count * LANES
    copies = []
    for slab in range(slabs):
        at = pl.ds(slab * size, size)
        held[:, at] = slabs_ref[slab].reshape(1, size)
        target = row_ref.at[:, pl.ds((slab * lines + begin) * LANES, size)]
        copies.append(pltpu.make_async_copy(held.at[:, at], target, sems.at[slab]))
        copies[-1].start()
    for copy in copies:
        copy.wait()


def join_row(slabs, lines, begin, row):
    total, count, _ = slabs.shape
    begun = [] if row is None else [row]
    return call(
        functools.partial(join_body, lines, begin),
        "join_row",
        moved=6 * slabs.size,
        in_specs=[IN_VMEM] + [IN_HBM] * len(begun),
        out_specs=IN_HBM,
        out_shape=jax.ShapeDtypeStruct((1, total * lines * LANES), BF16),
        input_output_aliases={1: 0} if begun else {},
        scratch_shapes=[pltpu.VMEM((1, slabs.size), BF16), pltpu.SemaphoreType.DMA((total,))],
    )(slabs, *begun)


def same_line(total):
    wide = total * TILE
    row = lax.broadcasted_iota(jnp.int32, (wide, wide), 0)
    col = lax.broadcasted_iota(jnp.int32, (wide, wide), 1)
    return row % TILE == col % TILE


def members(total, dtype):
    wide = total * TILE
    row = lax.broadcasted_iota(jnp.int32, (wide, total), 0)
    col = lax.broadcasted_iota(jnp.int32, (wide, total), 1)
    return (row // TILE == col).astype(dtype)


def gram_body(steps, tiles, parts, states_ref, *refs):
    out_ref, pairs = refs[-2:]
    total = states_ref.shape[0]
    wide = total * TILE
    pairs[...] = jnp.zeros_like(pairs)

    def step(i, carry):
        parts = [
            states_ref[:, pl.ds(pl.multiple_of((i * tiles + t) * TILE, TILE), TILE), :].reshape(wide, LANES)
            for t in range(tiles)
        ]
        block = jnp.concatenate(parts, axis=1)
        pairs[...] += lax.dot_general(block, block, (((1,), (1,)), ((), ())), preferred_element_type=F32)
        return carry

    lax.fori_loop(0, steps, step, 0)
    equal = jnp.where(same_line(total), pairs[...], 0.0)
    rows = jnp.sum(equal.reshape(total, TILE, wide), axis=1)
    gram = jnp.dot(rows, members(total, F32), precision=lax.Precision.HIGHEST, preferred_element_type=F32)
    gram = jnp.concatenate([gram, jnp.zeros((total, LANES - total), F32)], axis=1)
    for part_ref in refs[:parts]:
        gram += part_ref[0]
    out_ref[...] = jnp.broadcast_to(gram[None], out_ref.shape)


def slab_gram(states, lines, copies, parts, earlier):
    total = states.shape[0]
    wide = total * TILE
    tiles = min(8, lines // TILE)
    return call(
        functools.partial(gram_body, lines // TILE // tiles, tiles, len(parts)),
        "slab_gram",
        flops=2 * wide * wide * LANES * (lines // TILE),
        moved=2 * states.size,
        in_specs=[IN_VMEM] * (1 + len(parts)) + [IN_HBM] * len(earlier),
        out_specs=IN_VMEM,
        out_shape=jax.ShapeDtypeStruct((copies, total, LANES), F32),
        scratch_shapes=[pltpu.VMEM((wide, wide), F32)],
    )(states, *parts, *earlier)


def gradient_body(lines, begin, end, parts, *refs):
    observed, precision, out_ref, grads, sems = refs[parts:]
    total = grads.shape[0]
    first = refs[0].shape[1] - TILE
    rows = BLOCK // LINE
    group = 4
    shape = (rows, LINE, LANES)
    lane = lax.broadcasted_iota(jnp.int32, (1, LINE, LANES), 2)
    line = lax.broadcasted_iota(jnp.int32, (1, LINE, LANES), 1)

    def load(particle, at, count):
        ref, at = (refs[0], at) if at < first else (refs[1], at - first)
        return ref[particle, at : at + count, :].astype(F32)

    def rim(particle):
        return refs[0][particle, first:, :].astype(F32)

    stores = []
    for k, at in enumerate(range(begin, end, BLOCK)):
        mine = slice(at - begin, at - begin + BLOCK)
        obs = observed[at : at + BLOCK, :].astype(F32).reshape(shape)
        prec = precision[at : at + BLOCK, :].astype(F32).reshape(shape)

        def step(i, carry):
            for p in range(group):
                particle = i * group + p
                here = load(particle, at, BLOCK)
                before = load(particle, at - TILE, TILE) if at else rim(particle)
                after = load(particle, at + BLOCK, TILE) if at + BLOCK < lines else rim(particle)
                above = jnp.concatenate([before[LINE:], here[:-LINE]], axis=0).reshape(shape)
                below = jnp.concatenate([here[LINE:], after[:LINE]], axis=0).reshape(shape)
                field = here.reshape(shape)
                turned = pltpu.roll(field, 1, 2)
                carried = jnp.where(line == 0, 0.0, pltpu.roll(turned, 1, 1))
                left = jnp.where(lane == 0, carried, turned)
                turned = pltpu.roll(field, LANES - 1, 2)
                carried = jnp.where(line == LINE - 1, 0.0, pltpu.roll(turned, LINE - 1, 1))
                right = jnp.where(lane == LANES - 1, carried, turned)
                laplace = (4.0 + mass_term) * field - (below + above + right + left)
                squash = jnp.tanh(field)
                result = prec * (obs - squash) * (1.0 - squash * squash) - prior_scale * laplace
                grads[particle, mine, :] = result.reshape(BLOCK, LANES).astype(BF16)
            return carry

        lax.fori_loop(0, total // group, step, 0)
        stores.append(pltpu.make_async_copy(grads.at[:, mine, :], out_ref.at[:, mine, :], sems.at[k]))
        stores[-1].start()
    for store in stores:
        store.wait()


def slab_gradient(parts, observed, precision, lines, begin, end):
    total = parts[0].shape[0]
    count = end - begin
    out = jax.ShapeDtypeStruct((total, count, LANES), BF16)
    return call(
        functools.partial(gradient_body, lines, begin, end, len(parts)),
        "slab_gradient",
        flops=30 * out.size,
        moved=8 * out.size,
        in_specs=[IN_VMEM] * (len(parts) + 2),
        out_specs=IN_HBM,
        out_shape=out,
        scratch_shapes=[pltpu.VMEM(out.shape, BF16), pltpu.SemaphoreType.DMA((count // BLOCK,))],
    )(*parts, observed, precision)


def update_body(begin, end, parts, *refs):
    states_refs, refs = refs[:parts], refs[parts:]
    scalars_ref, grams_ref, grads_ref = refs[:3]
    out_ref, grads, mixer, own, sem = refs[-5:]
    total = out_ref.shape[0]
    wide = total * TILE
    fetch = pltpu.make_async_copy(grads_ref, grads, sem)
    fetch.start()
    gram = jnp.sum(grams_ref[...], axis=0)[:, :total]
    row = lax.broadcasted_iota(jnp.int32, (total, total), 0)
    col = lax.broadcasted_iota(jnp.int32, (total, total), 1)
    diagonal = jnp.where(row == col, gram, 0.0)
    down = jnp.sum(diagonal, axis=1, keepdims=True)
    across = jnp.sum(diagonal, axis=0, keepdims=True)
    member = members(total, BF16)
    spread, anneal, step_size = (scalars_ref[k : k + 1, :1] for k in range(3))
    rate = step_size / total
    coeff = 2.0 * anneal / spread
    kernel = jnp.exp(-(down + across - 2.0 * gram) / (spread * NCELL)).astype(BF16)
    ksum = jnp.sum(kernel.astype(F32), axis=1, keepdims=True)
    half = jnp.dot(member, kernel, preferred_element_type=F32).astype(BF16)
    full = lax.dot_general(half, member, (((1,), (1,)), ((), ())), preferred_element_type=F32)
    mixer[...] = jnp.where(same_line(total), full, 0.0).astype(BF16)
    gain = 1.0 + rate * coeff * ksum
    own[...] = jnp.broadcast_to(gain[:, :, None], (total, TILE, LANES)).reshape(wide, LANES)
    fetch.wait()

    done = 0
    for part, states_ref in enumerate(states_refs):
        have = states_ref.shape[1] - (0 if part else TILE)
        low = max(begin - done, 0)
        high = min(end - done, have)
        into = done - begin
        done += have

        def step(i, carry):
            for t in range(BLOCK // TILE):
                at = pl.multiple_of(i * BLOCK + t * TILE, TILE)
                there = pl.ds(pl.multiple_of(at + into, TILE), TILE)
                states = states_ref[:, pl.ds(at, TILE), :].reshape(wide, LANES)
                both = jnp.concatenate([grads[:, there, :].reshape(wide, LANES), states], axis=1)
                mixed = jnp.dot(mixer[...], both, preferred_element_type=F32)
                drive, pulled = mixed[:, :LANES], mixed[:, LANES:]
                new = states.astype(F32) * own[...] + rate * (drive - coeff * pulled)
                out_ref[:, there, :] = new.astype(BF16).reshape(total, TILE, LANES)
            return carry

        lax.fori_loop(low // BLOCK, high // BLOCK, step, 0)


def slab_update(scalars, grams, parts, grads, begin, end, earlier):
    total, count, _ = grads.shape
    wide = total * TILE
    return call(
        functools.partial(update_body, begin, end, len(parts)),
        "slab_update",
        flops=4 * wide * wide * LANES * (count // TILE),
        moved=6 * grads.size,
        in_specs=[IN_VMEM] * len(parts)
        + [IN_VMEM, IN_VMEM, IN_HBM]
        + [IN_HBM] * len(earlier),
        out_specs=IN_VMEM,
        out_shape=jax.ShapeDtypeStruct(grads.shape, BF16),
        scratch_shapes=[
            pltpu.VMEM(grads.shape, BF16),
            pltpu.VMEM((wide, wide), BF16),
            pltpu.VMEM((wide, LANES), F32),
            pltpu.SemaphoreType.DMA,
        ],
    )(*parts, scalars, grams, grads, *earlier)


def plain_update(spread, anneal, step_size, states, grads):
    total, lines, _ = grads.shape
    flat = states[:, :lines].reshape(total, -1)
    gram = lax.dot_general(flat, flat, (((1,), (1,)), ((), ())), preferred_element_type=F32)
    gram = lax.psum(gram, "slab")
    norms = jnp.diagonal(gram)
    kernel = jnp.exp(-(norms[:, None] + norms[None, :] - 2.0 * gram) / (spread[0] * NCELL)).astype(BF16)
    ksum = jnp.sum(kernel.astype(F32), axis=1)
    drive = jnp.dot(kernel, grads.reshape(total, -1), preferred_element_type=F32)
    pulled = jnp.dot(kernel, flat, preferred_element_type=F32)
    values = flat.astype(F32)
    repel = values * ksum[:, None] - pulled
    coeff = 2.0 * anneal[0] / spread[0]
    new = values + step_size[0] / total * (drive + coeff * repel)
    return new.astype(BF16).reshape(grads.shape)


def swap(slabs):
    return lax.all_to_all(slabs, "slab", split_axis=0, concat_axis=0, tiled=True)


def device_at(at, half):
    me = lax.axis_index("slab").astype(jnp.int32)
    return jnp.where(at < half, me - me % half + at, me ^ at)


def lines_of(start, count):
    return pl.ds(pl.multiple_of(start, TILE), count)


def split_pieces_body(slabs, raw, lines, fields, row_ref, *refs):
    half = slabs // 2
    field_refs, near_out, far_outs = refs[:fields], refs[fields], refs[fields + 1 : fields + 1 + half]
    slab_refs, helds, sems = refs[fields + 1 + half : -slabs - 1], refs[-slabs - 1 : -1], refs[-1]
    cells = lines * LANES
    end = row_ref.shape[1]
    started = []

    def fetch(source, target):
        started.append(pltpu.make_async_copy(source, target, sems.at[len(started)]))
        started[-1].start()
        return started[-1]

    copies = []
    for at, held in enumerate(helds):
        slab = device_at(at, half)
        parts = [
            (slab * cells, cells),
            (jnp.minimum((slab + 1) * cells, end - GRID_Y), GRID_Y),
            (jnp.maximum(slab * cells - GRID_Y, 0), GRID_Y),
        ]
        if at < half:
            other = slab ^ half
            parts += [(other * cells, raw * LANES + GRID_Y), (jnp.maximum(other * cells - GRID_Y, 0), GRID_Y)]
        mine, to = [], 0
        for start, size in parts:
            source = row_ref.at[:, pl.ds(pl.multiple_of(start, GRID_Y), size)]
            mine.append(fetch(source, held.at[:, pl.ds(to, size)]))
            to += size
        copies.append(mine)
    me = lax.axis_index("slab").astype(jnp.int32)
    fetches = []
    for n, target in enumerate(slab_refs):
        start = (me if n < fields else me ^ half) * lines
        fetches.append(fetch(field_refs[n % fields].at[lines_of(start, target.shape[0]), :], target))

    def grid_row(held, at):
        return held[:, pl.ds(at, GRID_Y)].astype(F32).reshape(LINE, LANES)

    for at, held in enumerate(helds):
        out_ref = near_out.at[at] if at < half else far_outs[at - half]
        for copy in copies[at]:
            copy.wait()
        slab = device_at(at, half)
        out_ref[:lines, :] = held[:, :cells].reshape(lines, LANES)
        below = jnp.where(slab == slabs - 1, 0.0, grid_row(held, cells))
        above = jnp.where(slab == 0, 0.0, grid_row(held, cells + GRID_Y))
        out_ref[lines : lines + TILE, :] = jnp.concatenate([below, above], axis=0).astype(BF16)
        if at < half:
            start = cells + 2 * GRID_Y
            to = lines + TILE
            out_ref[to : to + raw, :] = held[:, start : start + raw * LANES].reshape(raw, LANES)
            below = grid_row(held, start + raw * LANES)
            above = jnp.where(slab ^ half == 0, 0.0, grid_row(held, start + raw * LANES + GRID_Y))
            out_ref[to + raw :, :] = jnp.concatenate([below, above], axis=0).astype(BF16)
    for copy in fetches:
        copy.wait()


def split_pieces(row, slabs, raw, fields):
    lines = row.shape[1] // slabs // LANES
    half = slabs // 2
    rim = lines + TILE
    size = rim + raw + TILE
    out_shape = [jax.ShapeDtypeStruct((half, size, LANES), BF16)]
    out_shape += [jax.ShapeDtypeStruct((rim, LANES), BF16)] * half
    out_shape += [jax.ShapeDtypeStruct((lines, LANES), BF16)] * len(fields)
    out_shape += [jax.ShapeDtypeStruct((raw, LANES), BF16)] * len(fields)
    return call(
        functools.partial(split_pieces_body, slabs, raw, lines, len(fields)),
        "split_pieces",
        moved=6 * half * (rim + size) * LANES,
        in_specs=[IN_HBM] * (1 + len(fields)),
        out_specs=[IN_VMEM] * len(out_shape),
        out_shape=out_shape,
        scratch_shapes=[pltpu.VMEM((1, size * LANES), BF16)] * half
        + [pltpu.VMEM((1, rim * LANES), BF16)] * half
        + [pltpu.SemaphoreType.DMA((8 * slabs + 2 * len(fields),))],
    )(row, *fields)


def join_pieces_body(pieces, half, raw, lines, begun, arrays, *refs):
    row_ref, helds, sems = refs[begun + arrays], refs[begun + arrays + 1 : -1], refs[-1]
    cells = lines * LANES
    skip = raw * LANES
    copies = []
    for (array, lead, at), held in zip(pieces, helds):
        ref = refs[begun + array]
        piece = ref[...] if lead is None else ref[lead]
        held[...] = piece.reshape(held.shape)
        slab = device_at(at, half)
        if at < half:
            parts = [(0, cells, slab * cells), (cells, skip, (slab ^ half) * cells)]
        else:
            parts = [(0, cells - skip, slab * cells + skip)]
        for begin, size, start in parts:
            target = row_ref.at[:, pl.ds(pl.multiple_of(start, GRID_Y), size)]
            copies.append(pltpu.make_async_copy(held.at[:, pl.ds(begin, size)], target, sems.at[len(copies)]))
            copies[-1].start()
    for copy in copies:
        copy.wait()


def join_pieces(row, slabs, raw, arrays, pieces):
    sizes = [arrays[piece[0]].shape[-2] * LANES for piece in pieces]
    begun = [] if row is None else [row]
    return call(
        functools.partial(
            join_pieces_body, pieces, slabs // 2, raw, NCELL // slabs // LANES, len(begun), len(arrays)
        ),
        "join_pieces",
        moved=6 * sum(sizes),
        in_specs=[IN_HBM] * len(begun) + [IN_VMEM] * len(arrays),
        out_specs=IN_HBM,
        out_shape=jax.ShapeDtypeStruct((1, NCELL), BF16),
        input_output_aliases={0: 0} if begun else {},
        scratch_shapes=[pltpu.VMEM((1, size), BF16) for size in sizes]
        + [pltpu.SemaphoreType.DMA((2 * len(sizes),))],
    )(*begun, *arrays)


def owners(total, dtype):
    wide = total * TILE
    row = lax.broadcasted_iota(jnp.int32, (wide, total), 0)
    col = lax.broadcasted_iota(jnp.int32, (wide, total), 1)
    return (device_at(row // TILE, total // 2) == col).astype(dtype)


def gram_pieces_body(lines, total, near_ref, *refs):
    half = total // 2
    pieces, out_ref, pairs = refs[:half], refs[-2], refs[-1]
    wide = total * TILE
    tiles = 4
    pairs[...] = jnp.zeros_like(pairs)

    def step(i, carry):
        parts = []
        for t in range(tiles):
            at = lines_of((i * tiles + t) * TILE, TILE)
            near = near_ref[:, at, :].reshape(wide // 2, LANES)
            parts.append(jnp.concatenate([near] + [piece[at, :] for piece in pieces], axis=0))
        block = jnp.concatenate(parts, axis=1)
        pairs[...] += lax.dot_general(block, block, (((1,), (1,)), ((), ())), preferred_element_type=F32)
        return carry

    lax.fori_loop(0, lines // TILE // tiles, step, 0)
    equal = jnp.where(same_line(total), pairs[...], 0.0)
    exact = {"precision": lax.Precision.HIGHEST, "preferred_element_type": F32}
    rows = jnp.sum(equal.reshape(total, TILE, wide), axis=1)
    gram = jnp.dot(rows, owners(total, F32), **exact)
    row = lax.broadcasted_iota(jnp.int32, (total, total), 0)
    col = lax.broadcasted_iota(jnp.int32, (total, total), 1)
    gram = jnp.dot((row == device_at(col, half)).astype(F32), gram, **exact)
    gram = jnp.concatenate([gram, jnp.zeros((total, LANES - total), F32)], axis=1)
    out_ref[...] = jnp.broadcast_to(gram[None], out_ref.shape)


def gram_pieces(near, far, lines, gates, early):
    total = 2 * len(far)
    wide = total * TILE
    return call(
        functools.partial(gram_pieces_body, lines, total),
        "gram_pieces",
        flops=2 * wide * wide * LANES * (lines // TILE),
        moved=2 * total * lines * LANES,
        in_specs=[IN_VMEM] * (1 + len(far)) + [IN_HBM] * len(gates) + [IN_VMEM] * len(early),
        out_specs=IN_VMEM,
        out_shape=jax.ShapeDtypeStruct((total, total, LANES), F32),
        scratch_shapes=[pltpu.VMEM((wide, wide), F32)],
    )(near, *far, *gates, *early)


def block_gradient(load, i, count, observed, precision):
    start = i * BLOCK
    at = lines_of(start, BLOCK)
    shape = (BLOCK // LINE, LINE, LANES)
    lane = lax.broadcasted_iota(jnp.int32, (1, LINE, LANES), 2)
    line = lax.broadcasted_iota(jnp.int32, (1, LINE, LANES), 1)
    obs = observed[at, :].astype(F32).reshape(shape)
    prec = precision[at, :].astype(F32).reshape(shape)
    here = load(start, BLOCK).astype(F32)
    before = load(jnp.where(i == 0, count, start - TILE), TILE).astype(F32)
    after = load(start + BLOCK, TILE).astype(F32)
    above = jnp.concatenate([before[LINE:], here[:-LINE]], axis=0).reshape(shape)
    below = jnp.concatenate([here[LINE:], after[:LINE]], axis=0).reshape(shape)
    field = here.reshape(shape)
    turned = pltpu.roll(field, 1, 2)
    carried = jnp.where(line == 0, 0.0, pltpu.roll(turned, 1, 1))
    left = jnp.where(lane == 0, carried, turned)
    turned = pltpu.roll(field, LANES - 1, 2)
    carried = jnp.where(line == LINE - 1, 0.0, pltpu.roll(turned, LINE - 1, 1))
    right = jnp.where(lane == LANES - 1, carried, turned)
    laplace = (4.0 + mass_term) * field - (below + above + right + left)
    squash = jnp.tanh(field)
    result = prec * (obs - squash) * (1.0 - squash * squash) - prior_scale * laplace
    return result.reshape(BLOCK, LANES).astype(BF16)


def gradient_pieces_body(views, arrays, numbers, *refs):
    observed, precision, *number_refs = refs[arrays : arrays + 2 + numbers]
    out_ref, rows_ref, grads, sems = refs[-4:]
    for n, number_ref in enumerate(number_refs):
        rows_ref[n : n + 1, :] = jnp.full((1, LANES), number_ref[0], F32)
    count = observed.shape[0]
    steps = count // BLOCK

    def store(i):
        at = lines_of(i * BLOCK, BLOCK)
        return pltpu.make_async_copy(grads.at[:, at, :], out_ref.at[:, at, :], sems.at[i])

    def step(i, carry):
        for p, (array, lead) in enumerate(views):

            def load(start, size):
                part = lines_of(start, size)
                return refs[array][part, :] if lead is None else refs[array][lead, part, :]

            grads[p, lines_of(i * BLOCK, BLOCK), :] = block_gradient(load, i, count, observed, precision)
        store(i).start()
        return carry

    def finish(i, carry):
        store(i).wait()
        return carry

    lax.fori_loop(0, steps, step, 0)
    lax.fori_loop(0, steps, finish, 0)


def gradient_pieces(arrays, views, observed, precision, numbers):
    count = observed.shape[0]
    out = pltpu.HBM((len(views), count, LANES), BF16)
    size = len(views) * count * LANES
    return call(
        functools.partial(gradient_pieces_body, views, len(arrays), len(numbers)),
        "gradient_pieces",
        flops=30 * size,
        moved=8 * size,
        in_specs=[IN_VMEM] * (len(arrays) + 2)
        + [pl.BlockSpec(memory_space=pltpu.SMEM)] * len(numbers),
        out_specs=[IN_HBM, IN_VMEM],
        out_shape=[out, jax.ShapeDtypeStruct((8, LANES), F32)],
        scratch_shapes=[pltpu.VMEM(out.shape, BF16), pltpu.SemaphoreType.DMA((count // BLOCK,))],
    )(*arrays, observed, precision, *numbers)


def raw_body(raw, lines, near_ref, *refs):
    out_ref = refs[-1]
    for k in range(near_ref.shape[0]):
        out_ref[k, :raw, :] = near_ref[k, :raw, :]
        below = near_ref[k, raw : raw + TILE, :].astype(F32)[:LINE]
        above = near_ref[k, lines : lines + TILE, :].astype(F32)[LINE:]
        out_ref[k, raw:, :] = jnp.concatenate([below, above], axis=0).astype(BF16)


def raw_states(near, raw, lines, gates):
    out = jax.ShapeDtypeStruct((near.shape[0], raw + TILE, LANES), BF16)
    return call(
        functools.partial(raw_body, raw, lines),
        "raw_states",
        moved=4 * out.size,
        in_specs=[IN_VMEM] * (1 + len(gates)),
        out_specs=IN_VMEM,
        out_shape=out,
    )(near, *gates)


def mix(mixer, own, numbers_ref, total, states, slopes):
    high = mixer.shape[0]
    rate = numbers_ref[2:3, :1] / total
    coeff = 2.0 * numbers_ref[1:2, :1] / numbers_ref[:1, :1]
    both = jnp.concatenate([slopes, states], axis=1)
    mixed = jnp.dot(mixer[...], both, preferred_element_type=F32)
    drive, pulled = mixed[:, :LANES], mixed[:, LANES:]
    return (states[:high].astype(F32) * own[...] + rate * (drive - coeff * pulled)).astype(BF16)


def update_pieces_body(half, raw, lines, groups, near_ref, *refs):
    total = 2 * half
    far_refs, refs = refs[:half], refs[half:]
    across_ref, raw_observed, raw_precision, numbers_ref, grams_ref, *refs = refs
    group_refs, near_to, far_outs = refs[: len(groups)], refs[len(groups)], refs[len(groups) + 1 : -7]
    near_out, mixer, own, grads, raw_grads, sems, out_sems = refs[-7:]
    wide = total * TILE
    high = half * TILE
    fetches = []
    for group, group_ref in zip(groups, group_refs):
        for j, at in enumerate(group):
            fetches.append(pltpu.make_async_copy(group_ref.at[j], grads.at[at], sems.at[len(fetches)]))
    for fetch in fetches:
        fetch.start()

    def raw_gradient(i, carry):
        for k in range(total):

            def load(start, size):
                if k < half:
                    return near_ref[k, lines_of(lines + TILE + start, size), :]
                return across_ref[k - half, lines_of(start, size), :]

            part = lines_of(i * BLOCK, BLOCK)
            raw_grads[k, part, :] = block_gradient(load, i, raw, raw_observed, raw_precision)
        return carry

    lax.fori_loop(0, raw // BLOCK, raw_gradient, 0)
    gram = jnp.sum(grams_ref[...], axis=0)[:, :total]
    spread, anneal, step_size = (numbers_ref[k : k + 1, :1] for k in range(3))
    rate = step_size / total
    coeff = 2.0 * anneal / spread
    row = lax.broadcasted_iota(jnp.int32, (total, total), 0)
    col = lax.broadcasted_iota(jnp.int32, (total, total), 1)
    diagonal = jnp.where(row == col, gram, 0.0)
    down = jnp.sum(diagonal, axis=1, keepdims=True)
    across = jnp.sum(diagonal, axis=0, keepdims=True)
    kernel = jnp.exp(-(down + across - 2.0 * gram) / (spread * NCELL)).astype(BF16)
    owner = owners(total, BF16)
    half_way = jnp.dot(owner, kernel, preferred_element_type=F32).astype(BF16)
    full = lax.dot_general(half_way, owner, (((1,), (1,)), ((), ())), preferred_element_type=F32)
    full = jnp.where(same_line(total), full, 0.0)
    mixer[...] = full.astype(BF16)
    ksum = jnp.sum(full, axis=1, keepdims=True)
    own[...] = jnp.broadcast_to(1.0 + rate * coeff * ksum, (wide, LANES))
    for fetch in fetches:
        fetch.wait()

    def near_store(i):
        part = lines_of(i * BLOCK, BLOCK)
        return pltpu.make_async_copy(near_out.at[:, part, :], near_to.at[:, part, :], out_sems.at[i])

    def slab_step(with_far, i, carry):
        rows = wide if with_far else high
        for t in range(BLOCK // TILE):
            at = i * BLOCK + t * TILE
            part = lines_of(at, TILE)
            states = [near_ref[:, part, :].reshape(high, LANES)] + [ref[part, :] for ref in far_refs]
            slopes = grads[:, part, :].reshape(wide, LANES)
            states = jnp.concatenate(states, axis=0)
            new = mix(mixer.at[:rows, :], own.at[:rows, :], numbers_ref, total, states, slopes)
            near_out[:, part, :] = new[:high].reshape(half, TILE, LANES)
            if with_far:
                for x, far_out in enumerate(far_outs):
                    far_out[lines_of(at - raw, TILE), :] = new[high + x * TILE : high + (x + 1) * TILE]
        near_store(i).start()
        return carry

    here = lax.axis_index("slab").astype(jnp.int32) % half

    def raw_step(i, carry):
        for t in range(BLOCK // TILE):
            at = i * BLOCK + t * TILE
            part = lines_of(at, TILE)
            states = [near_ref[:, lines_of(lines + TILE + at, TILE), :].reshape(high, LANES)]
            slopes = [raw_grads[:half, part, :].reshape(high, LANES)]
            for x in range(half):
                states += [across_ref[here ^ x, part, :]]
                slopes += [raw_grads[half + (here ^ x), part, :]]
            states, slopes = jnp.concatenate(states, axis=0), jnp.concatenate(slopes, axis=0)
            new = mix(mixer.at[:high, :], own.at[:high, :], numbers_ref, total, states, slopes)
            near_out[:, lines_of(lines + at, TILE), :] = new.reshape(half, TILE, LANES)
        near_store(lines // BLOCK + i).start()
        return carry

    def finish(i, carry):
        near_store(i).wait()
        return carry

    lax.fori_loop(0, raw // BLOCK, raw_step, 0)
    lax.fori_loop(0, raw // BLOCK, functools.partial(slab_step, False), 0)
    lax.fori_loop(raw // BLOCK, lines // BLOCK, functools.partial(slab_step, True), 0)
    lax.fori_loop(0, (lines + raw) // BLOCK, finish, 0)


def update_pieces(numbers, grams, near, far, across, raw_fields, grads, groups, raw, lines):
    half = len(far)
    total = 2 * half
    wide = total * TILE
    out_shape = [pltpu.HBM((half, lines + raw, LANES), BF16)]
    out_shape += [jax.ShapeDtypeStruct((lines - raw, LANES), BF16)] * half
    return call(
        functools.partial(update_pieces_body, half, raw, lines, groups),
        "update_pieces",
        flops=4 * wide * wide * LANES * (lines // TILE),
        moved=6 * total * lines * LANES,
        in_specs=[IN_VMEM] * (half + 6) + [IN_HBM] * len(groups),
        out_specs=[IN_HBM] + [IN_VMEM] * half,
        out_shape=out_shape,
        scratch_shapes=[
            pltpu.VMEM((half, lines + raw, LANES), BF16),
            pltpu.VMEM((wide, wide), BF16),
            pltpu.VMEM((wide, LANES), F32),
            pltpu.VMEM((total, lines, LANES), BF16),
            pltpu.VMEM((total, raw, LANES), BF16),
            pltpu.SemaphoreType.DMA((total,)),
            pltpu.SemaphoreType.DMA(((lines + raw) // BLOCK,)),
        ],
    )(near, *far, across, *raw_fields, numbers, grams, *grads)


def exchange(piece, k, slabs):
    return lax.ppermute(piece, "slab", [(i, i ^ k) for i in range(slabs)])


def swap_near(pieces, slabs):
    groups = [list(range(slabs // 2)), list(range(slabs // 2, slabs))]
    return lax.all_to_all(pieces, "slab", 0, 0, axis_index_groups=groups, tiled=True)


RAW = 128
GRADIENTS = ((8, 9, 10, 11), (12, 13, 14, 15), (0, 1, 2, 3, 4, 5, 6, 7))


def by_halves(particles, observed, precision, spread, anneal, step_size):
    slabs = lax.axis_size("slab")
    half = slabs // 2
    lines = NCELL // slabs // LANES
    row = in_hbm(particles)
    fields = [in_hbm(field.reshape(-1, LANES)) for field in (observed, precision)]
    near, *far = split_pieces(row, slabs, RAW, fields)
    far, (obs, prec, *raw_fields) = far[:half], far[half:]
    near = swap_near(near, slabs)
    far = [exchange(piece, half + x, slabs) for x, piece in enumerate(far)]
    raw_near = raw_states(near, RAW, lines, far)
    across = exchange(raw_near, half, slabs)
    grads = []
    numbers = [spread, anneal, step_size]
    for group in GRADIENTS:
        if group[0] < half:
            arrays, views = [near], [(0, k) for k in group]
        else:
            arrays, views = [far[k - half] for k in group], [(j, None) for j in range(len(group))]
        slopes, rows = gradient_pieces(arrays, tuple(views), obs, prec, [] if grads else numbers)
        grads.append(in_hbm(slopes))
        numbers = numbers if len(grads) > 1 else rows
    grams = swap(gram_pieces(near, far, lines, grads[:1], [raw_near]))
    new_near, *new_far = update_pieces(
        numbers, grams, near, far, across, raw_fields, grads, GRADIENTS, RAW, lines
    )
    new_near = swap_near(new_near, slabs)
    new_far = [exchange(piece, half + x, slabs) for x, piece in enumerate(new_far)]
    row = join_pieces(None, slabs, RAW, [new_near], [(0, k, k) for k in range(half)])
    for group in ((0, 1, 2, 3), (4, 5)):
        pieces = [(n, None, half + x) for n, x in enumerate(group)]
        row = join_pieces(row, slabs, RAW, [new_far[x] for x in group], pieces)
    return join_pieces(row, slabs, RAW, new_far[6:], [(n, None, half + 6 + n) for n in range(half - 6)])


def on_device(particles, observed, precision, spread, anneal, step_size):
    slabs = lax.axis_size("slab")
    total = particles.shape[0] * slabs
    lines = NCELL // slabs // LANES
    if slabs == 16:
        return by_halves(particles, observed, precision, spread, anneal, step_size)
    sent, begun = cuts(lines)
    fields = [observed.reshape(-1, LANES), precision.reshape(-1, LANES)]
    numbers = [spread, anneal, step_size]
    first, obs, prec, scalars = split_row(particles, slabs, 0, sent, True, fields, numbers, [])
    parts = [swap(first)]
    if sent < lines:
        parts += [swap(split_row(particles, slabs, sent, lines, False, [], [], [scalars])[0])]
    if total * TILE > 256:
        grads = slab_gradient(parts, obs, prec, lines, 0, lines)
        states = jnp.concatenate([parts[0][:, :sent]] + parts[1:], axis=1)
        new = plain_update(spread, anneal, step_size, states, grads)
        return join_row(swap(new), lines, 0, None)
    if sent == lines:
        grads = slab_gradient(parts, obs, prec, lines, 0, lines)
        grams = swap(slab_gram(parts[0], lines, slabs, [], []))
        new = slab_update(scalars, grams, parts, grads, 0, lines, [])
        return join_row(swap(new), lines, 0, None)
    gram = slab_gram(parts[0], sent, 1, [], [])
    early = slab_gradient(parts[:1], obs, prec, lines, 0, begun)
    grams = swap(slab_gram(parts[1], lines - sent, slabs, [gram], [early]))
    late = slab_gradient(parts, obs, prec, lines, begun, lines)
    new = slab_update(scalars, grams, parts[:1], early, 0, begun, [])
    rest = slab_update(scalars, grams, parts, late, begun, lines, [new])
    row = join_row(swap(new), lines, 0, None)
    return join_row(swap(rest), lines, begun, row)


def solution(mesh):
    in_specs = (
        P(("groups", "slab"), None),
        P("groups"),
        P("groups"),
        P("groups"),
        P("groups"),
        P("groups"),
    )
    out_specs = P(("groups", "slab"), None)
    return jax.shard_map(
        on_device, mesh=mesh, in_specs=in_specs, out_specs=out_specs, check_vma=False
    )
```

```python
import functools

import jax
import jax.numpy as jnp
from jax import lax
from jax.experimental import pallas as pl
from jax.experimental.pallas import tpu as pltpu
from jax.sharding import PartitionSpec as P

GRID_X = 1024
GRID_Y = 1024
NCELL = 1048576
LANES = 128
LINE = GRID_Y // LANES
TILE = 16

prior_scale = 0.25
mass_term = 1.0

F32 = jnp.float32
BF16 = jnp.bfloat16
MIB = 1024 * 1024


def call(body, name, flops=0, moved=0, limit=16, **kwargs):
    return pl.pallas_call(
        body,
        name=name,
        compiler_params=pltpu.CompilerParams(vmem_limit_bytes=limit * MIB),
        cost_estimate=pl.CostEstimate(flops=flops, bytes_accessed=moved, transcendentals=0),
        **kwargs,
    )


IN_VMEM = pl.BlockSpec(memory_space=pltpu.VMEM)
IN_HBM = pl.BlockSpec(memory_space=pltpu.HBM)


def in_hbm(array):
    return pltpu.with_memory_space_constraint(array, pltpu.HBM)


BLOCK = 4 * TILE


def cuts(lines):
    if lines % (8 * BLOCK):
        return lines, lines
    return lines * 3 // 4, lines * 3 // 4 - BLOCK


def split_body(lines, begin, rim, fields, numbers, row_ref, *refs):
    field_refs, number_refs = refs[:fields], refs[fields : fields + numbers]
    out_ref, *slab_refs, rows_ref = refs[-7 - fields : -5]
    held, edges, sems, edge_sems, field_sems = refs[-5:]
    for k, number_ref in enumerate(number_refs):
        rows_ref[k : k + 1, :] = jnp.broadcast_to(number_ref[...].reshape(1, 1), (1, LANES))
    slabs, count, _ = out_ref.shape
    count -= TILE * rim
    size = count * LANES
    cells = lines * LANES

    def part(slab):
        source = row_ref.at[:, pl.ds(slab * cells + begin * LANES, size)]
        return pltpu.make_async_copy(source, held.at[:, pl.ds(slab * size, size)], sems.at[slab])

    def edge(slab):
        source = row_ref.at[:, pl.ds(slab * cells - GRID_Y, GRID_Y)]
        return pltpu.make_async_copy(source, edges.at[:, pl.ds(slab * GRID_Y, GRID_Y)], edge_sems.at[slab])

    def grid_row(ref, start):
        return ref[:, pl.ds(start, GRID_Y)].astype(F32).reshape(LINE, LANES)

    for slab in range(slabs):
        part(slab).start()
        if rim and slab:
            edge(slab).start()
    mine = pl.ds(pl.multiple_of(lax.axis_index("slab") * lines, TILE), lines)
    fetches = [
        pltpu.make_async_copy(source.at[mine, :], target, field_sems.at[k])
        for k, (source, target) in enumerate(zip(field_refs, slab_refs))
    ]
    for fetch in fetches:
        fetch.start()
    part(0).wait()
    outside = jnp.zeros((LINE, LANES), F32)
    for slab in range(slabs):
        if slab + 1 < slabs:
            part(slab + 1).wait()
        out_ref[slab, :count, :] = held[:, pl.ds(slab * size, size)].reshape(count, LANES)
        if rim:
            if slab:
                edge(slab).wait()
            below = grid_row(held, (slab + 1) * size) if slab + 1 < slabs else outside
            above = grid_row(edges, slab * GRID_Y) if slab else outside
            out_ref[slab, count:, :] = jnp.concatenate([below, above], axis=0).astype(BF16)
    for fetch in fetches:
        fetch.wait()


def split_row(row, slabs, begin, end, rim, fields, numbers, earlier):
    lines = row.shape[1] // slabs // LANES
    count = end - begin
    return call(
        functools.partial(split_body, lines, begin, rim, len(fields), len(numbers)),
        "split_row",
        moved=6 * slabs * count * LANES,
        in_specs=[IN_HBM] * (1 + len(fields)) + [IN_VMEM] * len(numbers) + [IN_HBM] * len(earlier),
        out_specs=[IN_VMEM] * (2 + len(fields)),
        out_shape=[jax.ShapeDtypeStruct((slabs, count + TILE * rim, LANES), BF16)]
        + [jax.ShapeDtypeStruct((lines, LANES), BF16)] * len(fields)
        + [jax.ShapeDtypeStruct((8, LANES), F32)],
        scratch_shapes=[
            pltpu.VMEM((1, slabs * count * LANES), BF16),
            pltpu.VMEM((1, slabs * GRID_Y), BF16),
            pltpu.SemaphoreType.DMA((slabs,)),
            pltpu.SemaphoreType.DMA((slabs,)),
            pltpu.SemaphoreType.DMA((2,)),
        ],
    )(row, *fields, *numbers, *earlier)


def join_body(lines, begin, slabs_ref, *refs):
    row_ref, held, sems = refs[-3:]
    slabs, count, _ = slabs_ref.shape
    size = count * LANES
    copies = []
    for slab in range(slabs):
        at = pl.ds(slab * size, size)
        held[:, at] = slabs_ref[slab].reshape(1, size)
        target = row_ref.at[:, pl.ds((slab * lines + begin) * LANES, size)]
        copies.append(pltpu.make_async_copy(held.at[:, at], target, sems.at[slab]))
        copies[-1].start()
    for copy in copies:
        copy.wait()


def join_row(slabs, lines, begin, row):
    total, count, _ = slabs.shape
    begun = [] if row is None else [row]
    return call(
        functools.partial(join_body, lines, begin),
        "join_row",
        moved=6 * slabs.size,
        in_specs=[IN_VMEM] + [IN_HBM] * len(begun),
        out_specs=IN_HBM,
        out_shape=jax.ShapeDtypeStruct((1, total * lines * LANES), BF16),
        input_output_aliases={1: 0} if begun else {},
        scratch_shapes=[pltpu.VMEM((1, slabs.size), BF16), pltpu.SemaphoreType.DMA((total,))],
    )(slabs, *begun)


def same_line(total):
    wide = total * TILE
    row = lax.broadcasted_iota(jnp.int32, (wide, wide), 0)
    col = lax.broadcasted_iota(jnp.int32, (wide, wide), 1)
    return row % TILE == col % TILE


def members(total, dtype):
    wide = total * TILE
    row = lax.broadcasted_iota(jnp.int32, (wide, total), 0)
    col = lax.broadcasted_iota(jnp.int32, (wide, total), 1)
    return (row // TILE == col).astype(dtype)


def gram_body(steps, tiles, parts, states_ref, *refs):
    out_ref, pairs = refs[-2:]
    total = states_ref.shape[0]
    wide = total * TILE
    pairs[...] = jnp.zeros_like(pairs)

    def step(i, carry):
        parts = [
            states_ref[:, pl.ds(pl.multiple_of((i * tiles + t) * TILE, TILE), TILE), :].reshape(wide, LANES)
            for t in range(tiles)
        ]
        block = jnp.concatenate(parts, axis=1)
        pairs[...] += lax.dot_general(block, block, (((1,), (1,)), ((), ())), preferred_element_type=F32)
        return carry

    lax.fori_loop(0, steps, step, 0)
    equal = jnp.where(same_line(total), pairs[...], 0.0)
    rows = jnp.sum(equal.reshape(total, TILE, wide), axis=1)
    gram = jnp.dot(rows, members(total, F32), precision=lax.Precision.HIGHEST, preferred_element_type=F32)
    gram = jnp.concatenate([gram, jnp.zeros((total, LANES - total), F32)], axis=1)
    for part_ref in refs[:parts]:
        gram += part_ref[0]
    out_ref[...] = jnp.broadcast_to(gram[None], out_ref.shape)


def slab_gram(states, lines, copies, parts, earlier):
    total = states.shape[0]
    wide = total * TILE
    tiles = min(8, lines // TILE)
    return call(
        functools.partial(gram_body, lines // TILE // tiles, tiles, len(parts)),
        "slab_gram",
        flops=2 * wide * wide * LANES * (lines // TILE),
        moved=2 * states.size,
        in_specs=[IN_VMEM] * (1 + len(parts)) + [IN_HBM] * len(earlier),
        out_specs=IN_VMEM,
        out_shape=jax.ShapeDtypeStruct((copies, total, LANES), F32),
        scratch_shapes=[pltpu.VMEM((wide, wide), F32)],
    )(states, *parts, *earlier)


def gradient_body(lines, begin, end, parts, *refs):
    observed, precision, out_ref, grads, sems = refs[parts:]
    total = grads.shape[0]
    first = refs[0].shape[1] - TILE
    rows = BLOCK // LINE
    group = 4
    shape = (rows, LINE, LANES)
    lane = lax.broadcasted_iota(jnp.int32, (1, LINE, LANES), 2)
    line = lax.broadcasted_iota(jnp.int32, (1, LINE, LANES), 1)

    def load(particle, at, count):
        ref, at = (refs[0], at) if at < first else (refs[1], at - first)
        return ref[particle, at : at + count, :].astype(F32)

    def rim(particle):
        return refs[0][particle, first:, :].astype(F32)

    stores = []
    for k, at in enumerate(range(begin, end, BLOCK)):
        mine = slice(at - begin, at - begin + BLOCK)
        obs = observed[at : at + BLOCK, :].astype(F32).reshape(shape)
        prec = precision[at : at + BLOCK, :].astype(F32).reshape(shape)

        def step(i, carry):
            for p in range(group):
                particle = i * group + p
                here = load(particle, at, BLOCK)
                before = load(particle, at - TILE, TILE) if at else rim(particle)
                after = load(particle, at + BLOCK, TILE) if at + BLOCK < lines else rim(particle)
                above = jnp.concatenate([before[LINE:], here[:-LINE]], axis=0).reshape(shape)
                below = jnp.concatenate([here[LINE:], after[:LINE]], axis=0).reshape(shape)
                field = here.reshape(shape)
                turned = pltpu.roll(field, 1, 2)
                carried = jnp.where(line == 0, 0.0, pltpu.roll(turned, 1, 1))
                left = jnp.where(lane == 0, carried, turned)
                turned = pltpu.roll(field, LANES - 1, 2)
                carried = jnp.where(line == LINE - 1, 0.0, pltpu.roll(turned, LINE - 1, 1))
                right = jnp.where(lane == LANES - 1, carried, turned)
                laplace = (4.0 + mass_term) * field - (below + above + right + left)
                squash = jnp.tanh(field)
                result = prec * (obs - squash) * (1.0 - squash * squash) - prior_scale * laplace
                grads[particle, mine, :] = result.reshape(BLOCK, LANES).astype(BF16)
            return carry

        lax.fori_loop(0, total // group, step, 0)
        stores.append(pltpu.make_async_copy(grads.at[:, mine, :], out_ref.at[:, mine, :], sems.at[k]))
        stores[-1].start()
    for store in stores:
        store.wait()


def slab_gradient(parts, observed, precision, lines, begin, end):
    total = parts[0].shape[0]
    count = end - begin
    out = jax.ShapeDtypeStruct((total, count, LANES), BF16)
    return call(
        functools.partial(gradient_body, lines, begin, end, len(parts)),
        "slab_gradient",
        flops=30 * out.size,
        moved=8 * out.size,
        in_specs=[IN_VMEM] * (len(parts) + 2),
        out_specs=IN_HBM,
        out_shape=out,
        scratch_shapes=[pltpu.VMEM(out.shape, BF16), pltpu.SemaphoreType.DMA((count // BLOCK,))],
    )(*parts, observed, precision)


def update_body(begin, end, parts, *refs):
    states_refs, refs = refs[:parts], refs[parts:]
    scalars_ref, grams_ref, grads_ref = refs[:3]
    out_ref, grads, mixer, own, sem = refs[-5:]
    total = out_ref.shape[0]
    wide = total * TILE
    fetch = pltpu.make_async_copy(grads_ref, grads, sem)
    fetch.start()
    gram = jnp.sum(grams_ref[...], axis=0)[:, :total]
    row = lax.broadcasted_iota(jnp.int32, (total, total), 0)
    col = lax.broadcasted_iota(jnp.int32, (total, total), 1)
    diagonal = jnp.where(row == col, gram, 0.0)
    down = jnp.sum(diagonal, axis=1, keepdims=True)
    across = jnp.sum(diagonal, axis=0, keepdims=True)
    member = members(total, BF16)
    spread, anneal, step_size = (scalars_ref[k : k + 1, :1] for k in range(3))
    rate = step_size / total
    coeff = 2.0 * anneal / spread
    kernel = jnp.exp(-(down + across - 2.0 * gram) / (spread * NCELL)).astype(BF16)
    ksum = jnp.sum(kernel.astype(F32), axis=1, keepdims=True)
    half = jnp.dot(member, kernel, preferred_element_type=F32).astype(BF16)
    full = lax.dot_general(half, member, (((1,), (1,)), ((), ())), preferred_element_type=F32)
    mixer[...] = jnp.where(same_line(total), full, 0.0).astype(BF16)
    gain = 1.0 + rate * coeff * ksum
    own[...] = jnp.broadcast_to(gain[:, :, None], (total, TILE, LANES)).reshape(wide, LANES)
    fetch.wait()

    done = 0
    for part, states_ref in enumerate(states_refs):
        have = states_ref.shape[1] - (0 if part else TILE)
        low = max(begin - done, 0)
        high = min(end - done, have)
        into = done - begin
        done += have

        def step(i, carry):
            for t in range(BLOCK // TILE):
                at = pl.multiple_of(i * BLOCK + t * TILE, TILE)
                there = pl.ds(pl.multiple_of(at + into, TILE), TILE)
                states = states_ref[:, pl.ds(at, TILE), :].reshape(wide, LANES)
                both = jnp.concatenate([grads[:, there, :].reshape(wide, LANES), states], axis=1)
                mixed = jnp.dot(mixer[...], both, preferred_element_type=F32)
                drive, pulled = mixed[:, :LANES], mixed[:, LANES:]
                new = states.astype(F32) * own[...] + rate * (drive - coeff * pulled)
                out_ref[:, there, :] = new.astype(BF16).reshape(total, TILE, LANES)
            return carry

        lax.fori_loop(low // BLOCK, high // BLOCK, step, 0)


def slab_update(scalars, grams, parts, grads, begin, end, earlier):
    total, count, _ = grads.shape
    wide = total * TILE
    return call(
        functools.partial(update_body, begin, end, len(parts)),
        "slab_update",
        flops=4 * wide * wide * LANES * (count // TILE),
        moved=6 * grads.size,
        in_specs=[IN_VMEM] * len(parts)
        + [IN_VMEM, IN_VMEM, IN_HBM]
        + [IN_HBM] * len(earlier),
        out_specs=IN_VMEM,
        out_shape=jax.ShapeDtypeStruct(grads.shape, BF16),
        scratch_shapes=[
            pltpu.VMEM(grads.shape, BF16),
            pltpu.VMEM((wide, wide), BF16),
            pltpu.VMEM((wide, LANES), F32),
            pltpu.SemaphoreType.DMA,
        ],
    )(*parts, scalars, grams, grads, *earlier)


def plain_update(spread, anneal, step_size, states, grads):
    total, lines, _ = grads.shape
    flat = states[:, :lines].reshape(total, -1)
    gram = lax.dot_general(flat, flat, (((1,), (1,)), ((), ())), preferred_element_type=F32)
    gram = lax.psum(gram, "slab")
    norms = jnp.diagonal(gram)
    kernel = jnp.exp(-(norms[:, None] + norms[None, :] - 2.0 * gram) / (spread[0] * NCELL)).astype(BF16)
    ksum = jnp.sum(kernel.astype(F32), axis=1)
    drive = jnp.dot(kernel, grads.reshape(total, -1), preferred_element_type=F32)
    pulled = jnp.dot(kernel, flat, preferred_element_type=F32)
    values = flat.astype(F32)
    repel = values * ksum[:, None] - pulled
    coeff = 2.0 * anneal[0] / spread[0]
    new = values + step_size[0] / total * (drive + coeff * repel)
    return new.astype(BF16).reshape(grads.shape)


def swap(slabs):
    return lax.all_to_all(slabs, "slab", split_axis=0, concat_axis=0, tiled=True)


def device_at(at, half):
    me = lax.axis_index("slab").astype(jnp.int32)
    return jnp.where(at < half, me - me % half + at, me ^ at)


def lines_of(start, count):
    return pl.ds(pl.multiple_of(start, TILE), count)


def split_pieces_body(slabs, raw, lines, fields, row_ref, *refs):
    half = slabs // 2
    field_refs, near_out, far_outs = refs[:fields], refs[fields], refs[fields + 1 : fields + 1 + half]
    slab_refs, helds, sems = refs[fields + 1 + half : -slabs - 1], refs[-slabs - 1 : -1], refs[-1]
    cells = lines * LANES
    end = row_ref.shape[1]
    started = []

    def fetch(source, target):
        started.append(pltpu.make_async_copy(source, target, sems.at[len(started)]))
        started[-1].start()
        return started[-1]

    copies = []
    for at, held in enumerate(helds):
        slab = device_at(at, half)
        parts = [
            (slab * cells, cells),
            (jnp.minimum((slab + 1) * cells, end - GRID_Y), GRID_Y),
            (jnp.maximum(slab * cells - GRID_Y, 0), GRID_Y),
        ]
        if at < half:
            other = slab ^ half
            parts += [(other * cells, raw * LANES + GRID_Y), (jnp.maximum(other * cells - GRID_Y, 0), GRID_Y)]
        mine, to = [], 0
        for start, size in parts:
            source = row_ref.at[:, pl.ds(pl.multiple_of(start, GRID_Y), size)]
            mine.append(fetch(source, held.at[:, pl.ds(to, size)]))
            to += size
        copies.append(mine)
    me = lax.axis_index("slab").astype(jnp.int32)
    fetches = []
    for n, target in enumerate(slab_refs):
        start = (me if n < fields else me ^ half) * lines
        fetches.append(fetch(field_refs[n % fields].at[lines_of(start, target.shape[0]), :], target))

    def grid_row(held, at):
        return held[:, pl.ds(at, GRID_Y)].astype(F32).reshape(LINE, LANES)

    for at, held in enumerate(helds):
        out_ref = near_out.at[at] if at < half else far_outs[at - half]
        for copy in copies[at]:
            copy.wait()
        slab = device_at(at, half)
        out_ref[:lines, :] = held[:, :cells].reshape(lines, LANES)
        below = jnp.where(slab == slabs - 1, 0.0, grid_row(held, cells))
        above = jnp.where(slab == 0, 0.0, grid_row(held, cells + GRID_Y))
        out_ref[lines : lines + TILE, :] = jnp.concatenate([below, above], axis=0).astype(BF16)
        if at < half:
            start = cells + 2 * GRID_Y
            to = lines + TILE
            out_ref[to : to + raw, :] = held[:, start : start + raw * LANES].reshape(raw, LANES)
            below = grid_row(held, start + raw * LANES)
            above = jnp.where(slab ^ half == 0, 0.0, grid_row(held, start + raw * LANES + GRID_Y))
            out_ref[to + raw :, :] = jnp.concatenate([below, above], axis=0).astype(BF16)
    for copy in fetches:
        copy.wait()


def split_pieces(row, slabs, raw, fields):
    lines = row.shape[1] // slabs // LANES
    half = slabs // 2
    rim = lines + TILE
    size = rim + raw + TILE
    out_shape = [jax.ShapeDtypeStruct((half, size, LANES), BF16)]
    out_shape += [jax.ShapeDtypeStruct((rim, LANES), BF16)] * half
    out_shape += [jax.ShapeDtypeStruct((lines, LANES), BF16)] * len(fields)
    out_shape += [jax.ShapeDtypeStruct((raw, LANES), BF16)] * len(fields)
    return call(
        functools.partial(split_pieces_body, slabs, raw, lines, len(fields)),
        "split_pieces",
        moved=6 * half * (rim + size) * LANES,
        in_specs=[IN_HBM] * (1 + len(fields)),
        out_specs=[IN_VMEM] * len(out_shape),
        out_shape=out_shape,
        scratch_shapes=[pltpu.VMEM((1, size * LANES), BF16)] * half
        + [pltpu.VMEM((1, rim * LANES), BF16)] * half
        + [pltpu.SemaphoreType.DMA((8 * slabs + 2 * len(fields),))],
    )(row, *fields)


def join_pieces_body(positions, half, raw, lines, begun, arrays, *refs):
    pieces, row_ref, held, sems = refs[begun : begun + arrays], refs[begun + arrays], refs[begun + arrays + 1], refs[-1]
    near = positions[0] < half
    size = held.shape[1] // len(positions)
    cells = lines * LANES
    skip = raw * LANES
    fetches = []
    if near:
        here = refs[-2]
        for n in range(len(positions)):
            fetches.append(pltpu.make_async_copy(pieces[0].at[n], here.at[n], sems.at[2 * len(positions) + n]))
            fetches[-1].start()
    copies = []
    for n, at in enumerate(positions):
        slab = device_at(at, half)
        if near:
            fetches[n].wait()
            piece = here[n]
            parts = [(0, cells, slab * cells), (cells, skip, (slab ^ half) * cells)]
        else:
            piece = pieces[n][...]
            parts = [(0, cells - skip, slab * cells + skip)]
        held[:, pl.ds(n * size, size)] = piece.reshape(1, size)
        for begin, count, start in parts:
            target = row_ref.at[:, pl.ds(pl.multiple_of(start, GRID_Y), count)]
            source = held.at[:, pl.ds(n * size + begin, count)]
            copies.append(pltpu.make_async_copy(source, target, sems.at[len(copies)]))
            copies[-1].start()
    for copy in copies:
        copy.wait()


def join_pieces(row, slabs, raw, pieces, positions):
    half = slabs // 2
    near = positions[0] < half
    shape = pieces[0].shape
    size = shape[-2] * LANES
    count = len(positions)
    begun = [] if row is None else [row]
    return call(
        functools.partial(
            join_pieces_body, positions, half, raw, NCELL // slabs // LANES, len(begun), len(pieces)
        ),
        "join_pieces",
        moved=6 * size * count,
        in_specs=[IN_HBM] * len(begun) + [IN_HBM if near else IN_VMEM] * len(pieces),
        out_specs=IN_HBM,
        out_shape=jax.ShapeDtypeStruct((1, NCELL), BF16),
        input_output_aliases={0: 0} if begun else {},
        scratch_shapes=[pltpu.VMEM((1, size * count), BF16)]
        + [pltpu.VMEM(shape, BF16)] * near
        + [pltpu.SemaphoreType.DMA((3 * count,))],
    )(*begun, *pieces)


def owners(total, dtype):
    wide = total * TILE
    row = lax.broadcasted_iota(jnp.int32, (wide, total), 0)
    col = lax.broadcasted_iota(jnp.int32, (wide, total), 1)
    return (device_at(row // TILE, total // 2) == col).astype(dtype)


def gram_pieces_body(lines, total, near_ref, *refs):
    half = total // 2
    pieces, out_ref, pairs = refs[:half], refs[-2], refs[-1]
    wide = total * TILE
    tiles = 4
    pairs[...] = jnp.zeros_like(pairs)

    def step(i, carry):
        parts = []
        for t in range(tiles):
            at = lines_of((i * tiles + t) * TILE, TILE)
            near = near_ref[:, at, :].reshape(wide // 2, LANES)
            parts.append(jnp.concatenate([near] + [piece[at, :] for piece in pieces], axis=0))
        block = jnp.concatenate(parts, axis=1)
        pairs[...] += lax.dot_general(block, block, (((1,), (1,)), ((), ())), preferred_element_type=F32)
        return carry

    lax.fori_loop(0, lines // TILE // tiles, step, 0)
    equal = jnp.where(same_line(total), pairs[...], 0.0)
    exact = {"precision": lax.Precision.HIGHEST, "preferred_element_type": F32}
    rows = jnp.sum(equal.reshape(total, TILE, wide), axis=1)
    gram = jnp.dot(rows, owners(total, F32), **exact)
    row = lax.broadcasted_iota(jnp.int32, (total, total), 0)
    col = lax.broadcasted_iota(jnp.int32, (total, total), 1)
    gram = jnp.dot((row == device_at(col, half)).astype(F32), gram, **exact)
    gram = jnp.concatenate([gram, jnp.zeros((total, LANES - total), F32)], axis=1)
    out_ref[...] = jnp.broadcast_to(gram[None], out_ref.shape)


def gram_pieces(near, far, lines, gates, early):
    total = 2 * len(far)
    wide = total * TILE
    return call(
        functools.partial(gram_pieces_body, lines, total),
        "gram_pieces",
        flops=2 * wide * wide * LANES * (lines // TILE),
        moved=2 * total * lines * LANES,
        in_specs=[IN_VMEM] * (1 + len(far)) + [IN_HBM] * len(gates) + [IN_VMEM] * len(early),
        out_specs=IN_VMEM,
        out_shape=jax.ShapeDtypeStruct((total, total, LANES), F32),
        scratch_shapes=[pltpu.VMEM((wide, wide), F32)],
    )(near, *far, *gates, *early)


def block_gradient(load, i, count, observed, precision):
    start = i * BLOCK
    at = lines_of(start, BLOCK)
    shape = (BLOCK // LINE, LINE, LANES)
    lane = lax.broadcasted_iota(jnp.int32, (1, LINE, LANES), 2)
    line = lax.broadcasted_iota(jnp.int32, (1, LINE, LANES), 1)
    obs = observed[at, :].astype(F32).reshape(shape)
    prec = precision[at, :].astype(F32).reshape(shape)
    here = load(start, BLOCK).astype(F32)
    before = load(jnp.where(i == 0, count, start - TILE), TILE).astype(F32)
    after = load(start + BLOCK, TILE).astype(F32)
    above = jnp.concatenate([before[LINE:], here[:-LINE]], axis=0).reshape(shape)
    below = jnp.concatenate([here[LINE:], after[:LINE]], axis=0).reshape(shape)
    field = here.reshape(shape)
    turned = pltpu.roll(field, 1, 2)
    carried = jnp.where(line == 0, 0.0, pltpu.roll(turned, 1, 1))
    left = jnp.where(lane == 0, carried, turned)
    turned = pltpu.roll(field, LANES - 1, 2)
    carried = jnp.where(line == LINE - 1, 0.0, pltpu.roll(turned, LINE - 1, 1))
    right = jnp.where(lane == LANES - 1, carried, turned)
    laplace = (4.0 + mass_term) * field - (below + above + right + left)
    squash = jnp.tanh(field)
    result = prec * (obs - squash) * (1.0 - squash * squash) - prior_scale * laplace
    return result.reshape(BLOCK, LANES).astype(BF16)


def gradient_pieces_body(views, arrays, numbers, *refs):
    observed, precision, *number_refs = refs[arrays : arrays + 2 + numbers]
    out_ref, rows_ref, grads, sems = refs[-4:]
    for n, number_ref in enumerate(number_refs):
        rows_ref[n : n + 1, :] = jnp.full((1, LANES), number_ref[0], F32)
    count = observed.shape[0]
    steps = count // BLOCK

    def store(i):
        at = lines_of(i * BLOCK, BLOCK)
        return pltpu.make_async_copy(grads.at[:, at, :], out_ref.at[:, at, :], sems.at[i])

    def step(i, carry):
        for p, (array, lead) in enumerate(views):

            def load(start, size):
                part = lines_of(start, size)
                return refs[array][part, :] if lead is None else refs[array][lead, part, :]

            grads[p, lines_of(i * BLOCK, BLOCK), :] = block_gradient(load, i, count, observed, precision)
        store(i).start()
        return carry

    def finish(i, carry):
        store(i).wait()
        return carry

    lax.fori_loop(0, steps, step, 0)
    lax.fori_loop(0, steps, finish, 0)


def gradient_pieces(arrays, views, observed, precision, numbers):
    count = observed.shape[0]
    out = pltpu.HBM((len(views), count, LANES), BF16)
    size = len(views) * count * LANES
    return call(
        functools.partial(gradient_pieces_body, views, len(arrays), len(numbers)),
        "gradient_pieces",
        flops=30 * size,
        moved=8 * size,
        in_specs=[IN_VMEM] * (len(arrays) + 2)
        + [pl.BlockSpec(memory_space=pltpu.SMEM)] * len(numbers),
        out_specs=[IN_HBM, IN_VMEM],
        out_shape=[out, jax.ShapeDtypeStruct((8, LANES), F32)],
        scratch_shapes=[pltpu.VMEM(out.shape, BF16), pltpu.SemaphoreType.DMA((count // BLOCK,))],
    )(*arrays, observed, precision, *numbers)


def raw_body(raw, lines, near_ref, *refs):
    out_ref = refs[-1]
    for k in range(near_ref.shape[0]):
        out_ref[k, :raw, :] = near_ref[k, :raw, :]
        below = near_ref[k, raw : raw + TILE, :].astype(F32)[:LINE]
        above = near_ref[k, lines : lines + TILE, :].astype(F32)[LINE:]
        out_ref[k, raw:, :] = jnp.concatenate([below, above], axis=0).astype(BF16)


def raw_states(near, raw, lines, gates):
    out = jax.ShapeDtypeStruct((near.shape[0], raw + TILE, LANES), BF16)
    return call(
        functools.partial(raw_body, raw, lines),
        "raw_states",
        moved=4 * out.size,
        in_specs=[IN_VMEM] * (1 + len(gates)),
        out_specs=IN_VMEM,
        out_shape=out,
    )(near, *gates)


def mix(mixer, own, numbers_ref, total, states, slopes):
    high = mixer.shape[0]
    rate = numbers_ref[2:3, :1] / total
    coeff = 2.0 * numbers_ref[1:2, :1] / numbers_ref[:1, :1]
    both = jnp.concatenate([slopes, states], axis=1)
    mixed = jnp.dot(mixer[...], both, preferred_element_type=F32)
    drive, pulled = mixed[:, :LANES], mixed[:, LANES:]
    return (states[:high].astype(F32) * own[...] + rate * (drive - coeff * pulled)).astype(BF16)


def update_pieces_body(half, raw, lines, groups, near_ref, *refs):
    total = 2 * half
    far_refs, refs = refs[:half], refs[half:]
    across_ref, raw_observed, raw_precision, numbers_ref, grams_ref, *refs = refs
    group_refs, near_out, far_outs = refs[: len(groups)], refs[len(groups)], refs[len(groups) + 1 : -5]
    mixer, own, grads, raw_grads, sems = refs[-5:]
    wide = total * TILE
    high = half * TILE
    fetches = []
    for group, group_ref in zip(groups, group_refs):
        for j, at in enumerate(group):
            fetches.append(pltpu.make_async_copy(group_ref.at[j], grads.at[at], sems.at[len(fetches)]))
    for fetch in fetches:
        fetch.start()

    def raw_gradient(i, carry):
        for k in range(total):

            def load(start, size):
                if k < half:
                    return near_ref[k, lines_of(lines + TILE + start, size), :]
                return across_ref[k - half, lines_of(start, size), :]

            part = lines_of(i * BLOCK, BLOCK)
            raw_grads[k, part, :] = block_gradient(load, i, raw, raw_observed, raw_precision)
        return carry

    lax.fori_loop(0, raw // BLOCK, raw_gradient, 0)
    gram = jnp.sum(grams_ref[...], axis=0)[:, :total]
    spread, anneal, step_size = (numbers_ref[k : k + 1, :1] for k in range(3))
    rate = step_size / total
    coeff = 2.0 * anneal / spread
    row = lax.broadcasted_iota(jnp.int32, (total, total), 0)
    col = lax.broadcasted_iota(jnp.int32, (total, total), 1)
    diagonal = jnp.where(row == col, gram, 0.0)
    down = jnp.sum(diagonal, axis=1, keepdims=True)
    across = jnp.sum(diagonal, axis=0, keepdims=True)
    kernel = jnp.exp(-(down + across - 2.0 * gram) / (spread * NCELL)).astype(BF16)
    owner = owners(total, BF16)
    half_way = jnp.dot(owner, kernel, preferred_element_type=F32).astype(BF16)
    full = lax.dot_general(half_way, owner, (((1,), (1,)), ((), ())), preferred_element_type=F32)
    full = jnp.where(same_line(total), full, 0.0)
    mixer[...] = full.astype(BF16)
    ksum = jnp.sum(full, axis=1, keepdims=True)
    own[...] = jnp.broadcast_to(1.0 + rate * coeff * ksum, (wide, LANES))
    for fetch in fetches:
        fetch.wait()

    def slab_step(with_far, i, carry):
        rows = wide if with_far else high
        for t in range(BLOCK // TILE):
            at = i * BLOCK + t * TILE
            part = lines_of(at, TILE)
            states = [near_ref[:, part, :].reshape(high, LANES)] + [ref[part, :] for ref in far_refs]
            slopes = grads[:, part, :].reshape(wide, LANES)
            states = jnp.concatenate(states, axis=0)
            new = mix(mixer.at[:rows, :], own.at[:rows, :], numbers_ref, total, states, slopes)
            near_out[:, part, :] = new[:high].reshape(half, TILE, LANES)
            if with_far:
                for x, far_out in enumerate(far_outs):
                    far_out[lines_of(at - raw, TILE), :] = new[high + x * TILE : high + (x + 1) * TILE]
        return carry

    here = lax.axis_index("slab").astype(jnp.int32) % half

    def raw_step(i, carry):
        for t in range(BLOCK // TILE):
            at = i * BLOCK + t * TILE
            part = lines_of(at, TILE)
            states = [near_ref[:, lines_of(lines + TILE + at, TILE), :].reshape(high, LANES)]
            slopes = [raw_grads[:half, part, :].reshape(high, LANES)]
            for x in range(half):
                states += [across_ref[here ^ x, part, :]]
                slopes += [raw_grads[half + (here ^ x), part, :]]
            states, slopes = jnp.concatenate(states, axis=0), jnp.concatenate(slopes, axis=0)
            new = mix(mixer.at[:high, :], own.at[:high, :], numbers_ref, total, states, slopes)
            near_out[:, lines_of(lines + at, TILE), :] = new.reshape(half, TILE, LANES)
        return carry

    lax.fori_loop(0, raw // BLOCK, raw_step, 0)
    lax.fori_loop(0, raw // BLOCK, functools.partial(slab_step, False), 0)
    lax.fori_loop(raw // BLOCK, lines // BLOCK, functools.partial(slab_step, True), 0)


def update_pieces(numbers, grams, near, far, across, raw_fields, grads, groups, raw, lines):
    half = len(far)
    total = 2 * half
    wide = total * TILE
    out_shape = [jax.ShapeDtypeStruct((half, lines + raw, LANES), BF16)]
    out_shape += [jax.ShapeDtypeStruct((lines - raw, LANES), BF16)] * half
    return call(
        functools.partial(update_pieces_body, half, raw, lines, groups),
        "update_pieces",
        flops=4 * wide * wide * LANES * (lines // TILE),
        moved=6 * total * lines * LANES,
        in_specs=[IN_VMEM] * (half + 6) + [IN_HBM] * len(groups),
        out_specs=[IN_VMEM] * len(out_shape),
        out_shape=out_shape,
        scratch_shapes=[
            pltpu.VMEM((wide, wide), BF16),
            pltpu.VMEM((wide, LANES), F32),
            pltpu.VMEM((total, lines, LANES), BF16),
            pltpu.VMEM((total, raw, LANES), BF16),
            pltpu.SemaphoreType.DMA((total,)),
        ],
    )(near, *far, across, *raw_fields, numbers, grams, *grads)


def exchange(piece, k, slabs):
    return lax.ppermute(piece, "slab", [(i, i ^ k) for i in range(slabs)])


def swap_near(pieces, slabs):
    groups = [list(range(slabs // 2)), list(range(slabs // 2, slabs))]
    return lax.all_to_all(pieces, "slab", 0, 0, axis_index_groups=groups, tiled=True)


RAW = 128
GRADIENTS = ((8, 9, 10, 11), (12, 13, 14, 15), (0, 1, 2, 3, 4, 5, 6, 7))


def by_halves(particles, observed, precision, spread, anneal, step_size):
    slabs = lax.axis_size("slab")
    half = slabs // 2
    lines = NCELL // slabs // LANES
    row = in_hbm(particles)
    fields = [in_hbm(field.reshape(-1, LANES)) for field in (observed, precision)]
    near, *far = split_pieces(row, slabs, RAW, fields)
    far, (obs, prec, *raw_fields) = far[:half], far[half:]
    near = swap_near(near, slabs)
    far = [exchange(piece, half + x, slabs) for x, piece in enumerate(far)]
    raw_near = raw_states(near, RAW, lines, far)
    across = exchange(raw_near, half, slabs)
    grads = []
    numbers = [spread, anneal, step_size]
    for group in GRADIENTS:
        if group[0] < half:
            arrays, views = [near], [(0, k) for k in group]
        else:
            arrays, views = [far[k - half] for k in group], [(j, None) for j in range(len(group))]
        slopes, rows = gradient_pieces(arrays, tuple(views), obs, prec, [] if grads else numbers)
        grads.append(in_hbm(slopes))
        numbers = numbers if len(grads) > 1 else rows
    grams = swap(gram_pieces(near, far, lines, grads[:1], [raw_near]))
    new_near, *new_far = update_pieces(
        numbers, grams, near, far, across, raw_fields, grads, GRADIENTS, RAW, lines
    )
    new_near = swap_near(new_near, slabs)
    new_far = [exchange(piece, half + x, slabs) for x, piece in enumerate(new_far)]
    row = join_pieces(None, slabs, RAW, [in_hbm(new_near)], tuple(range(half)))
    for group in ((0, 1, 2, 3), (4, 5), (6, 7)):
        row = join_pieces(row, slabs, RAW, [new_far[x] for x in group], tuple(half + x for x in group))
    return row


def on_device(particles, observed, precision, spread, anneal, step_size):
    slabs = lax.axis_size("slab")
    total = particles.shape[0] * slabs
    lines = NCELL // slabs // LANES
    if slabs == 16:
        return by_halves(particles, observed, precision, spread, anneal, step_size)
    sent, begun = cuts(lines)
    fields = [observed.reshape(-1, LANES), precision.reshape(-1, LANES)]
    numbers = [spread, anneal, step_size]
    first, obs, prec, scalars = split_row(particles, slabs, 0, sent, True, fields, numbers, [])
    parts = [swap(first)]
    if sent < lines:
        parts += [swap(split_row(particles, slabs, sent, lines, False, [], [], [scalars])[0])]
    if total * TILE > 256:
        grads = slab_gradient(parts, obs, prec, lines, 0, lines)
        states = jnp.concatenate([parts[0][:, :sent]] + parts[1:], axis=1)
        new = plain_update(spread, anneal, step_size, states, grads)
        return join_row(swap(new), lines, 0, None)
    if sent == lines:
        grads = slab_gradient(parts, obs, prec, lines, 0, lines)
        grams = swap(slab_gram(parts[0], lines, slabs, [], []))
        new = slab_update(scalars, grams, parts, grads, 0, lines, [])
        return join_row(swap(new), lines, 0, None)
    gram = slab_gram(parts[0], sent, 1, [], [])
    early = slab_gradient(parts[:1], obs, prec, lines, 0, begun)
    grams = swap(slab_gram(parts[1], lines - sent, slabs, [gram], [early]))
    late = slab_gradient(parts, obs, prec, lines, begun, lines)
    new = slab_update(scalars, grams, parts[:1], early, 0, begun, [])
    rest = slab_update(scalars, grams, parts, late, begun, lines, [new])
    row = join_row(swap(new), lines, 0, None)
    return join_row(swap(rest), lines, begun, row)


def solution(mesh):
    in_specs = (
        P(("groups", "slab"), None),
        P("groups"),
        P("groups"),
        P("groups"),
        P("groups"),
        P("groups"),
    )
    out_specs = P(("groups", "slab"), None)
    return jax.shard_map(
        on_device, mesh=mesh, in_specs=in_specs, out_specs=out_specs, check_vma=False
    )
```

```python
import functools

import jax
import jax.numpy as jnp
from jax import lax
from jax.experimental import pallas as pl
from jax.experimental.pallas import tpu as pltpu
from jax.sharding import PartitionSpec as P

GRID_X = 1024
GRID_Y = 1024
NCELL = 1048576
LANES = 128
LINE = GRID_Y // LANES
TILE = 16

prior_scale = 0.25
mass_term = 1.0

F32 = jnp.float32
BF16 = jnp.bfloat16
MIB = 1024 * 1024


def call(body, name, flops=0, moved=0, limit=16, **kwargs):
    return pl.pallas_call(
        body,
        name=name,
        compiler_params=pltpu.CompilerParams(vmem_limit_bytes=limit * MIB),
        cost_estimate=pl.CostEstimate(flops=flops, bytes_accessed=moved, transcendentals=0),
        **kwargs,
    )


IN_VMEM = pl.BlockSpec(memory_space=pltpu.VMEM)
IN_HBM = pl.BlockSpec(memory_space=pltpu.HBM)


def in_hbm(array):
    return pltpu.with_memory_space_constraint(array, pltpu.HBM)


BLOCK = 4 * TILE


def cuts(lines):
    if lines % (8 * BLOCK):
        return lines, lines
    return lines * 3 // 4, lines * 3 // 4 - BLOCK


def split_body(lines, begin, rim, fields, numbers, row_ref, *refs):
    field_refs, number_refs = refs[:fields], refs[fields : fields + numbers]
    out_ref, *slab_refs, rows_ref = refs[-7 - fields : -5]
    held, edges, sems, edge_sems, field_sems = refs[-5:]
    for k, number_ref in enumerate(number_refs):
        rows_ref[k : k + 1, :] = jnp.broadcast_to(number_ref[...].reshape(1, 1), (1, LANES))
    slabs, count, _ = out_ref.shape
    count -= TILE * rim
    size = count * LANES
    cells = lines * LANES

    def part(slab):
        source = row_ref.at[:, pl.ds(slab * cells + begin * LANES, size)]
        return pltpu.make_async_copy(source, held.at[:, pl.ds(slab * size, size)], sems.at[slab])

    def edge(slab):
        source = row_ref.at[:, pl.ds(slab * cells - GRID_Y, GRID_Y)]
        return pltpu.make_async_copy(source, edges.at[:, pl.ds(slab * GRID_Y, GRID_Y)], edge_sems.at[slab])

    def grid_row(ref, start):
        return ref[:, pl.ds(start, GRID_Y)].astype(F32).reshape(LINE, LANES)

    for slab in range(slabs):
        part(slab).start()
        if rim and slab:
            edge(slab).start()
    mine = pl.ds(pl.multiple_of(lax.axis_index("slab") * lines, TILE), lines)
    fetches = [
        pltpu.make_async_copy(source.at[mine, :], target, field_sems.at[k])
        for k, (source, target) in enumerate(zip(field_refs, slab_refs))
    ]
    for fetch in fetches:
        fetch.start()
    part(0).wait()
    outside = jnp.zeros((LINE, LANES), F32)
    for slab in range(slabs):
        if slab + 1 < slabs:
            part(slab + 1).wait()
        out_ref[slab, :count, :] = held[:, pl.ds(slab * size, size)].reshape(count, LANES)
        if rim:
            if slab:
                edge(slab).wait()
            below = grid_row(held, (slab + 1) * size) if slab + 1 < slabs else outside
            above = grid_row(edges, slab * GRID_Y) if slab else outside
            out_ref[slab, count:, :] = jnp.concatenate([below, above], axis=0).astype(BF16)
    for fetch in fetches:
        fetch.wait()


def split_row(row, slabs, begin, end, rim, fields, numbers, earlier):
    lines = row.shape[1] // slabs // LANES
    count = end - begin
    return call(
        functools.partial(split_body, lines, begin, rim, len(fields), len(numbers)),
        "split_row",
        moved=6 * slabs * count * LANES,
        in_specs=[IN_HBM] * (1 + len(fields)) + [IN_VMEM] * len(numbers) + [IN_HBM] * len(earlier),
        out_specs=[IN_VMEM] * (2 + len(fields)),
        out_shape=[jax.ShapeDtypeStruct((slabs, count + TILE * rim, LANES), BF16)]
        + [jax.ShapeDtypeStruct((lines, LANES), BF16)] * len(fields)
        + [jax.ShapeDtypeStruct((8, LANES), F32)],
        scratch_shapes=[
            pltpu.VMEM((1, slabs * count * LANES), BF16),
            pltpu.VMEM((1, slabs * GRID_Y), BF16),
            pltpu.SemaphoreType.DMA((slabs,)),
            pltpu.SemaphoreType.DMA((slabs,)),
            pltpu.SemaphoreType.DMA((2,)),
        ],
    )(row, *fields, *numbers, *earlier)


def join_body(lines, begin, slabs_ref, *refs):
    row_ref, held, sems = refs[-3:]
    slabs, count, _ = slabs_ref.shape
    size = count * LANES
    copies = []
    for slab in range(slabs):
        at = pl.ds(slab * size, size)
        held[:, at] = slabs_ref[slab].reshape(1, size)
        target = row_ref.at[:, pl.ds((slab * lines + begin) * LANES, size)]
        copies.append(pltpu.make_async_copy(held.at[:, at], target, sems.at[slab]))
        copies[-1].start()
    for copy in copies:
        copy.wait()


def join_row(slabs, lines, begin, row):
    total, count, _ = slabs.shape
    begun = [] if row is None else [row]
    return call(
        functools.partial(join_body, lines, begin),
        "join_row",
        moved=6 * slabs.size,
        in_specs=[IN_VMEM] + [IN_HBM] * len(begun),
        out_specs=IN_HBM,
        out_shape=jax.ShapeDtypeStruct((1, total * lines * LANES), BF16),
        input_output_aliases={1: 0} if begun else {},
        scratch_shapes=[pltpu.VMEM((1, slabs.size), BF16), pltpu.SemaphoreType.DMA((total,))],
    )(slabs, *begun)


def same_line(total):
    wide = total * TILE
    row = lax.broadcasted_iota(jnp.int32, (wide, wide), 0)
    col = lax.broadcasted_iota(jnp.int32, (wide, wide), 1)
    return row % TILE == col % TILE


def members(total, dtype):
    wide = total * TILE
    row = lax.broadcasted_iota(jnp.int32, (wide, total), 0)
    col = lax.broadcasted_iota(jnp.int32, (wide, total), 1)
    return (row // TILE == col).astype(dtype)


def gram_body(steps, tiles, parts, states_ref, *refs):
    out_ref, pairs = refs[-2:]
    total = states_ref.shape[0]
    wide = total * TILE
    pairs[...] = jnp.zeros_like(pairs)

    def step(i, carry):
        parts = [
            states_ref[:, pl.ds(pl.multiple_of((i * tiles + t) * TILE, TILE), TILE), :].reshape(wide, LANES)
            for t in range(tiles)
        ]
        block = jnp.concatenate(parts, axis=1)
        pairs[...] += lax.dot_general(block, block, (((1,), (1,)), ((), ())), preferred_element_type=F32)
        return carry

    lax.fori_loop(0, steps, step, 0)
    equal = jnp.where(same_line(total), pairs[...], 0.0)
    rows = jnp.sum(equal.reshape(total, TILE, wide), axis=1)
    gram = jnp.dot(rows, members(total, F32), precision=lax.Precision.HIGHEST, preferred_element_type=F32)
    gram = jnp.concatenate([gram, jnp.zeros((total, LANES - total), F32)], axis=1)
    for part_ref in refs[:parts]:
        gram += part_ref[0]
    out_ref[...] = jnp.broadcast_to(gram[None], out_ref.shape)


def slab_gram(states, lines, copies, parts, earlier):
    total = states.shape[0]
    wide = total * TILE
    tiles = min(8, lines // TILE)
    return call(
        functools.partial(gram_body, lines // TILE // tiles, tiles, len(parts)),
        "slab_gram",
        flops=2 * wide * wide * LANES * (lines // TILE),
        moved=2 * states.size,
        in_specs=[IN_VMEM] * (1 + len(parts)) + [IN_HBM] * len(earlier),
        out_specs=IN_VMEM,
        out_shape=jax.ShapeDtypeStruct((copies, total, LANES), F32),
        scratch_shapes=[pltpu.VMEM((wide, wide), F32)],
    )(states, *parts, *earlier)


def gradient_body(lines, begin, end, parts, *refs):
    observed, precision, out_ref, grads, sems = refs[parts:]
    total = grads.shape[0]
    first = refs[0].shape[1] - TILE
    rows = BLOCK // LINE
    group = 4
    shape = (rows, LINE, LANES)
    lane = lax.broadcasted_iota(jnp.int32, (1, LINE, LANES), 2)
    line = lax.broadcasted_iota(jnp.int32, (1, LINE, LANES), 1)

    def load(particle, at, count):
        ref, at = (refs[0], at) if at < first else (refs[1], at - first)
        return ref[particle, at : at + count, :].astype(F32)

    def rim(particle):
        return refs[0][particle, first:, :].astype(F32)

    stores = []
    for k, at in enumerate(range(begin, end, BLOCK)):
        mine = slice(at - begin, at - begin + BLOCK)
        obs = observed[at : at + BLOCK, :].astype(F32).reshape(shape)
        prec = precision[at : at + BLOCK, :].astype(F32).reshape(shape)

        def step(i, carry):
            for p in range(group):
                particle = i * group + p
                here = load(particle, at, BLOCK)
                before = load(particle, at - TILE, TILE) if at else rim(particle)
                after = load(particle, at + BLOCK, TILE) if at + BLOCK < lines else rim(particle)
                above = jnp.concatenate([before[LINE:], here[:-LINE]], axis=0).reshape(shape)
                below = jnp.concatenate([here[LINE:], after[:LINE]], axis=0).reshape(shape)
                field = here.reshape(shape)
                turned = pltpu.roll(field, 1, 2)
                carried = jnp.where(line == 0, 0.0, pltpu.roll(turned, 1, 1))
                left = jnp.where(lane == 0, carried, turned)
                turned = pltpu.roll(field, LANES - 1, 2)
                carried = jnp.where(line == LINE - 1, 0.0, pltpu.roll(turned, LINE - 1, 1))
                right = jnp.where(lane == LANES - 1, carried, turned)
                laplace = (4.0 + mass_term) * field - (below + above + right + left)
                squash = jnp.tanh(field)
                result = prec * (obs - squash) * (1.0 - squash * squash) - prior_scale * laplace
                grads[particle, mine, :] = result.reshape(BLOCK, LANES).astype(BF16)
            return carry

        lax.fori_loop(0, total // group, step, 0)
        stores.append(pltpu.make_async_copy(grads.at[:, mine, :], out_ref.at[:, mine, :], sems.at[k]))
        stores[-1].start()
    for store in stores:
        store.wait()


def slab_gradient(parts, observed, precision, lines, begin, end):
    total = parts[0].shape[0]
    count = end - begin
    out = jax.ShapeDtypeStruct((total, count, LANES), BF16)
    return call(
        functools.partial(gradient_body, lines, begin, end, len(parts)),
        "slab_gradient",
        flops=30 * out.size,
        moved=8 * out.size,
        in_specs=[IN_VMEM] * (len(parts) + 2),
        out_specs=IN_HBM,
        out_shape=out,
        scratch_shapes=[pltpu.VMEM(out.shape, BF16), pltpu.SemaphoreType.DMA((count // BLOCK,))],
    )(*parts, observed, precision)


def update_body(begin, end, parts, *refs):
    states_refs, refs = refs[:parts], refs[parts:]
    scalars_ref, grams_ref, grads_ref = refs[:3]
    out_ref, grads, mixer, own, sem = refs[-5:]
    total = out_ref.shape[0]
    wide = total * TILE
    fetch = pltpu.make_async_copy(grads_ref, grads, sem)
    fetch.start()
    gram = jnp.sum(grams_ref[...], axis=0)[:, :total]
    row = lax.broadcasted_iota(jnp.int32, (total, total), 0)
    col = lax.broadcasted_iota(jnp.int32, (total, total), 1)
    diagonal = jnp.where(row == col, gram, 0.0)
    down = jnp.sum(diagonal, axis=1, keepdims=True)
    across = jnp.sum(diagonal, axis=0, keepdims=True)
    member = members(total, BF16)
    spread, anneal, step_size = (scalars_ref[k : k + 1, :1] for k in range(3))
    rate = step_size / total
    coeff = 2.0 * anneal / spread
    kernel = jnp.exp(-(down + across - 2.0 * gram) / (spread * NCELL)).astype(BF16)
    ksum = jnp.sum(kernel.astype(F32), axis=1, keepdims=True)
    half = jnp.dot(member, kernel, preferred_element_type=F32).astype(BF16)
    full = lax.dot_general(half, member, (((1,), (1,)), ((), ())), preferred_element_type=F32)
    mixer[...] = jnp.where(same_line(total), full, 0.0).astype(BF16)
    gain = 1.0 + rate * coeff * ksum
    own[...] = jnp.broadcast_to(gain[:, :, None], (total, TILE, LANES)).reshape(wide, LANES)
    fetch.wait()

    done = 0
    for part, states_ref in enumerate(states_refs):
        have = states_ref.shape[1] - (0 if part else TILE)
        low = max(begin - done, 0)
        high = min(end - done, have)
        into = done - begin
        done += have

        def step(i, carry):
            for t in range(BLOCK // TILE):
                at = pl.multiple_of(i * BLOCK + t * TILE, TILE)
                there = pl.ds(pl.multiple_of(at + into, TILE), TILE)
                states = states_ref[:, pl.ds(at, TILE), :].reshape(wide, LANES)
                both = jnp.concatenate([grads[:, there, :].reshape(wide, LANES), states], axis=1)
                mixed = jnp.dot(mixer[...], both, preferred_element_type=F32)
                drive, pulled = mixed[:, :LANES], mixed[:, LANES:]
                new = states.astype(F32) * own[...] + rate * (drive - coeff * pulled)
                out_ref[:, there, :] = new.astype(BF16).reshape(total, TILE, LANES)
            return carry

        lax.fori_loop(low // BLOCK, high // BLOCK, step, 0)


def slab_update(scalars, grams, parts, grads, begin, end, earlier):
    total, count, _ = grads.shape
    wide = total * TILE
    return call(
        functools.partial(update_body, begin, end, len(parts)),
        "slab_update",
        flops=4 * wide * wide * LANES * (count // TILE),
        moved=6 * grads.size,
        in_specs=[IN_VMEM] * len(parts)
        + [IN_VMEM, IN_VMEM, IN_HBM]
        + [IN_HBM] * len(earlier),
        out_specs=IN_VMEM,
        out_shape=jax.ShapeDtypeStruct(grads.shape, BF16),
        scratch_shapes=[
            pltpu.VMEM(grads.shape, BF16),
            pltpu.VMEM((wide, wide), BF16),
            pltpu.VMEM((wide, LANES), F32),
            pltpu.SemaphoreType.DMA,
        ],
    )(*parts, scalars, grams, grads, *earlier)


def plain_update(spread, anneal, step_size, states, grads):
    total, lines, _ = grads.shape
    flat = states[:, :lines].reshape(total, -1)
    gram = lax.dot_general(flat, flat, (((1,), (1,)), ((), ())), preferred_element_type=F32)
    gram = lax.psum(gram, "slab")
    norms = jnp.diagonal(gram)
    kernel = jnp.exp(-(norms[:, None] + norms[None, :] - 2.0 * gram) / (spread[0] * NCELL)).astype(BF16)
    ksum = jnp.sum(kernel.astype(F32), axis=1)
    drive = jnp.dot(kernel, grads.reshape(total, -1), preferred_element_type=F32)
    pulled = jnp.dot(kernel, flat, preferred_element_type=F32)
    values = flat.astype(F32)
    repel = values * ksum[:, None] - pulled
    coeff = 2.0 * anneal[0] / spread[0]
    new = values + step_size[0] / total * (drive + coeff * repel)
    return new.astype(BF16).reshape(grads.shape)


def swap(slabs):
    return lax.all_to_all(slabs, "slab", split_axis=0, concat_axis=0, tiled=True)


def device_at(at, half):
    me = lax.axis_index("slab").astype(jnp.int32)
    return jnp.where(at < half, me - me % half + at, me ^ at)


def lines_of(start, count):
    return pl.ds(pl.multiple_of(start, TILE), count)


def split_pieces_body(slabs, raw, lines, fields, row_ref, *refs):
    half = slabs // 2
    field_refs, near_out, far_outs = refs[:fields], refs[fields], refs[fields + 1 : fields + 1 + half]
    slab_refs, helds, sems = refs[fields + 1 + half : -slabs - 1], refs[-slabs - 1 : -1], refs[-1]
    cells = lines * LANES
    end = row_ref.shape[1]
    started = []

    def fetch(source, target):
        started.append(pltpu.make_async_copy(source, target, sems.at[len(started)]))
        started[-1].start()
        return started[-1]

    copies = []
    for at, held in enumerate(helds):
        slab = device_at(at, half)
        parts = [
            (slab * cells, cells),
            (jnp.minimum((slab + 1) * cells, end - GRID_Y), GRID_Y),
            (jnp.maximum(slab * cells - GRID_Y, 0), GRID_Y),
        ]
        if at < half:
            other = slab ^ half
            parts += [(other * cells, raw * LANES + GRID_Y), (jnp.maximum(other * cells - GRID_Y, 0), GRID_Y)]
        mine, to = [], 0
        for start, size in parts:
            source = row_ref.at[:, pl.ds(pl.multiple_of(start, GRID_Y), size)]
            mine.append(fetch(source, held.at[:, pl.ds(to, size)]))
            to += size
        copies.append(mine)
    me = lax.axis_index("slab").astype(jnp.int32)
    fetches = []
    for n, target in enumerate(slab_refs):
        start = (me if n < fields else me ^ half) * lines
        fetches.append(fetch(field_refs[n % fields].at[lines_of(start, target.shape[0]), :], target))

    def grid_row(held, at):
        return held[:, pl.ds(at, GRID_Y)].astype(F32).reshape(LINE, LANES)

    for at, held in enumerate(helds):
        out_ref = near_out.at[at] if at < half else far_outs[at - half]
        for copy in copies[at]:
            copy.wait()
        slab = device_at(at, half)
        out_ref[:lines, :] = held[:, :cells].reshape(lines, LANES)
        below = jnp.where(slab == slabs - 1, 0.0, grid_row(held, cells))
        above = jnp.where(slab == 0, 0.0, grid_row(held, cells + GRID_Y))
        out_ref[lines : lines + TILE, :] = jnp.concatenate([below, above], axis=0).astype(BF16)
        if at < half:
            start = cells + 2 * GRID_Y
            to = lines + TILE
            out_ref[to : to + raw, :] = held[:, start : start + raw * LANES].reshape(raw, LANES)
            below = grid_row(held, start + raw * LANES)
            above = jnp.where(slab ^ half == 0, 0.0, grid_row(held, start + raw * LANES + GRID_Y))
            out_ref[to + raw :, :] = jnp.concatenate([below, above], axis=0).astype(BF16)
    for copy in fetches:
        copy.wait()


def split_pieces(row, slabs, raw, fields):
    lines = row.shape[1] // slabs // LANES
    half = slabs // 2
    rim = lines + TILE
    size = rim + raw + TILE
    out_shape = [jax.ShapeDtypeStruct((half, size, LANES), BF16)]
    out_shape += [jax.ShapeDtypeStruct((rim, LANES), BF16)] * half
    out_shape += [jax.ShapeDtypeStruct((lines, LANES), BF16)] * len(fields)
    out_shape += [jax.ShapeDtypeStruct((raw, LANES), BF16)] * len(fields)
    return call(
        functools.partial(split_pieces_body, slabs, raw, lines, len(fields)),
        "split_pieces",
        moved=6 * half * (rim + size) * LANES,
        in_specs=[IN_HBM] * (1 + len(fields)),
        out_specs=[IN_VMEM] * len(out_shape),
        out_shape=out_shape,
        scratch_shapes=[pltpu.VMEM((1, size * LANES), BF16)] * half
        + [pltpu.VMEM((1, rim * LANES), BF16)] * half
        + [pltpu.SemaphoreType.DMA((8 * slabs + 2 * len(fields),))],
    )(row, *fields)


def join_pieces_body(pieces, half, raw, lines, begun, arrays, *refs):
    row_ref, helds, sems = refs[begun + arrays], refs[begun + arrays + 1 : -1], refs[-1]
    cells = lines * LANES
    skip = raw * LANES
    copies = []
    for (array, lead, at), held in zip(pieces, helds):
        ref = refs[begun + array]
        piece = ref[...] if lead is None else ref[lead]
        held[...] = piece.reshape(held.shape)
        slab = device_at(at, half)
        if at < half:
            parts = [(0, cells, slab * cells), (cells, skip, (slab ^ half) * cells)]
        else:
            parts = [(0, cells - skip, slab * cells + skip)]
        for begin, size, start in parts:
            target = row_ref.at[:, pl.ds(pl.multiple_of(start, GRID_Y), size)]
            copies.append(pltpu.make_async_copy(held.at[:, pl.ds(begin, size)], target, sems.at[len(copies)]))
            copies[-1].start()
    for copy in copies:
        copy.wait()


def join_pieces(row, slabs, raw, arrays, pieces):
    sizes = [arrays[piece[0]].shape[-2] * LANES for piece in pieces]
    begun = [] if row is None else [row]
    return call(
        functools.partial(
            join_pieces_body, pieces, slabs // 2, raw, NCELL // slabs // LANES, len(begun), len(arrays)
        ),
        "join_pieces",
        moved=6 * sum(sizes),
        in_specs=[IN_HBM] * len(begun) + [IN_VMEM] * len(arrays),
        out_specs=IN_HBM,
        out_shape=jax.ShapeDtypeStruct((1, NCELL), BF16),
        input_output_aliases={0: 0} if begun else {},
        scratch_shapes=[pltpu.VMEM((1, size), BF16) for size in sizes]
        + [pltpu.SemaphoreType.DMA((2 * len(sizes),))],
    )(*begun, *arrays)


def owners(total, dtype):
    wide = total * TILE
    row = lax.broadcasted_iota(jnp.int32, (wide, total), 0)
    col = lax.broadcasted_iota(jnp.int32, (wide, total), 1)
    return (device_at(row // TILE, total // 2) == col).astype(dtype)


def gram_pieces_body(lines, total, near_ref, *refs):
    half = total // 2
    pieces, out_ref, pairs = refs[:half], refs[-2], refs[-1]
    wide = total * TILE
    tiles = 8
    pairs[...] = jnp.zeros_like(pairs)

    def step(i, carry):
        parts = []
        for t in range(tiles):
            at = lines_of((i * tiles + t) * TILE, TILE)
            near = near_ref[:, at, :].reshape(wide // 2, LANES)
            parts.append(jnp.concatenate([near] + [piece[at, :] for piece in pieces], axis=0))
        block = jnp.concatenate(parts, axis=1)
        pairs[...] += lax.dot_general(block, block, (((1,), (1,)), ((), ())), preferred_element_type=F32)
        return carry

    lax.fori_loop(0, lines // TILE // tiles, step, 0)
    equal = jnp.where(same_line(total), pairs[...], 0.0)
    exact = {"precision": lax.Precision.HIGHEST, "preferred_element_type": F32}
    rows = jnp.sum(equal.reshape(total, TILE, wide), axis=1)
    gram = jnp.dot(rows, owners(total, F32), **exact)
    row = lax.broadcasted_iota(jnp.int32, (total, total), 0)
    col = lax.broadcasted_iota(jnp.int32, (total, total), 1)
    gram = jnp.dot((row == device_at(col, half)).astype(F32), gram, **exact)
    gram = jnp.concatenate([gram, jnp.zeros((total, LANES - total), F32)], axis=1)
    out_ref[...] = jnp.broadcast_to(gram[None], out_ref.shape)


def gram_pieces(near, far, lines, gates, early):
    total = 2 * len(far)
    wide = total * TILE
    return call(
        functools.partial(gram_pieces_body, lines, total),
        "gram_pieces",
        flops=2 * wide * wide * LANES * (lines // TILE),
        moved=2 * total * lines * LANES,
        in_specs=[IN_VMEM] * (1 + len(far)) + [IN_HBM] * len(gates) + [IN_VMEM] * len(early),
        out_specs=IN_VMEM,
        out_shape=jax.ShapeDtypeStruct((total, total, LANES), F32),
        scratch_shapes=[pltpu.VMEM((wide, wide), F32)],
    )(near, *far, *gates, *early)


def block_gradient(load, i, count, observed, precision):
    start = i * BLOCK
    at = lines_of(start, BLOCK)
    shape = (BLOCK // LINE, LINE, LANES)
    lane = lax.broadcasted_iota(jnp.int32, (1, LINE, LANES), 2)
    line = lax.broadcasted_iota(jnp.int32, (1, LINE, LANES), 1)
    obs = observed[at, :].astype(F32).reshape(shape)
    prec = precision[at, :].astype(F32).reshape(shape)
    here = load(start, BLOCK).astype(F32)
    before = load(jnp.where(i == 0, count, start - TILE), TILE).astype(F32)
    after = load(start + BLOCK, TILE).astype(F32)
    above = jnp.concatenate([before[LINE:], here[:-LINE]], axis=0).reshape(shape)
    below = jnp.concatenate([here[LINE:], after[:LINE]], axis=0).reshape(shape)
    field = here.reshape(shape)
    turned = pltpu.roll(field, 1, 2)
    carried = jnp.where(line == 0, 0.0, pltpu.roll(turned, 1, 1))
    left = jnp.where(lane == 0, carried, turned)
    turned = pltpu.roll(field, LANES - 1, 2)
    carried = jnp.where(line == LINE - 1, 0.0, pltpu.roll(turned, LINE - 1, 1))
    right = jnp.where(lane == LANES - 1, carried, turned)
    laplace = (4.0 + mass_term) * field - (below + above + right + left)
    squash = jnp.tanh(field)
    result = prec * (obs - squash) * (1.0 - squash * squash) - prior_scale * laplace
    return result.reshape(BLOCK, LANES).astype(BF16)


def gradient_pieces_body(views, arrays, numbers, *refs):
    observed, precision, *number_refs = refs[arrays : arrays + 2 + numbers]
    out_ref, rows_ref, grads, sems = refs[-4:]
    for n, number_ref in enumerate(number_refs):
        rows_ref[n : n + 1, :] = jnp.full((1, LANES), number_ref[0], F32)
    count = observed.shape[0]
    steps = count // BLOCK

    def store(i):
        at = lines_of(i * BLOCK, BLOCK)
        return pltpu.make_async_copy(grads.at[:, at, :], out_ref.at[:, at, :], sems.at[i])

    def step(i, carry):
        for p, (array, lead) in enumerate(views):

            def load(start, size):
                part = lines_of(start, size)
                return refs[array][part, :] if lead is None else refs[array][lead, part, :]

            grads[p, lines_of(i * BLOCK, BLOCK), :] = block_gradient(load, i, count, observed, precision)
        store(i).start()
        return carry

    def finish(i, carry):
        store(i).wait()
        return carry

    lax.fori_loop(0, steps, step, 0)
    lax.fori_loop(0, steps, finish, 0)


def gradient_pieces(arrays, views, observed, precision, numbers):
    count = observed.shape[0]
    out = pltpu.HBM((len(views), count, LANES), BF16)
    size = len(views) * count * LANES
    return call(
        functools.partial(gradient_pieces_body, views, len(arrays), len(numbers)),
        "gradient_pieces",
        flops=30 * size,
        moved=8 * size,
        in_specs=[IN_VMEM] * (len(arrays) + 2)
        + [pl.BlockSpec(memory_space=pltpu.SMEM)] * len(numbers),
        out_specs=[IN_HBM, IN_VMEM],
        out_shape=[out, jax.ShapeDtypeStruct((8, LANES), F32)],
        scratch_shapes=[pltpu.VMEM(out.shape, BF16), pltpu.SemaphoreType.DMA((count // BLOCK,))],
    )(*arrays, observed, precision, *numbers)


def raw_body(raw, lines, near_ref, *refs):
    out_ref = refs[-1]
    for k in range(near_ref.shape[0]):
        out_ref[k, :raw, :] = near_ref[k, :raw, :]
        below = near_ref[k, raw : raw + TILE, :].astype(F32)[:LINE]
        above = near_ref[k, lines : lines + TILE, :].astype(F32)[LINE:]
        out_ref[k, raw:, :] = jnp.concatenate([below, above], axis=0).astype(BF16)


def raw_states(near, raw, lines, gates):
    out = jax.ShapeDtypeStruct((near.shape[0], raw + TILE, LANES), BF16)
    return call(
        functools.partial(raw_body, raw, lines),
        "raw_states",
        moved=4 * out.size,
        in_specs=[IN_VMEM] * (1 + len(gates)),
        out_specs=IN_VMEM,
        out_shape=out,
    )(near, *gates)


def mix(mixer, own, numbers_ref, total, states, slopes):
    high = mixer.shape[0]
    rate = numbers_ref[2:3, :1] / total
    coeff = 2.0 * numbers_ref[1:2, :1] / numbers_ref[:1, :1]
    both = jnp.concatenate([slopes, states], axis=1)
    mixed = jnp.dot(mixer[...], both, preferred_element_type=F32)
    drive, pulled = mixed[:, :LANES], mixed[:, LANES:]
    return (states[:high].astype(F32) * own[...] + rate * (drive - coeff * pulled)).astype(BF16)


def update_pieces_body(half, raw, lines, groups, near_ref, *refs):
    total = 2 * half
    far_refs, refs = refs[:half], refs[half:]
    across_ref, raw_observed, raw_precision, numbers_ref, grams_ref, *refs = refs
    group_refs, near_to, far_tos = refs[: len(groups)], refs[len(groups)], refs[len(groups) + 1 : -8]
    near_out, far_out, mixer, own, grads, raw_grads, sems, out_sems = refs[-8:]
    wide = total * TILE
    high = half * TILE
    fetches = []
    for group, group_ref in zip(groups, group_refs):
        for j, at in enumerate(group):
            fetches.append(pltpu.make_async_copy(group_ref.at[j], grads.at[at], sems.at[len(fetches)]))
    for fetch in fetches:
        fetch.start()

    def raw_gradient(i, carry):
        for k in range(total):

            def load(start, size):
                if k < half:
                    return near_ref[k, lines_of(lines + TILE + start, size), :]
                return across_ref[k - half, lines_of(start, size), :]

            part = lines_of(i * BLOCK, BLOCK)
            raw_grads[k, part, :] = block_gradient(load, i, raw, raw_observed, raw_precision)
        return carry

    lax.fori_loop(0, raw // BLOCK, raw_gradient, 0)
    gram = jnp.sum(grams_ref[...], axis=0)[:, :total]
    spread, anneal, step_size = (numbers_ref[k : k + 1, :1] for k in range(3))
    rate = step_size / total
    coeff = 2.0 * anneal / spread
    row = lax.broadcasted_iota(jnp.int32, (total, total), 0)
    col = lax.broadcasted_iota(jnp.int32, (total, total), 1)
    diagonal = jnp.where(row == col, gram, 0.0)
    down = jnp.sum(diagonal, axis=1, keepdims=True)
    across = jnp.sum(diagonal, axis=0, keepdims=True)
    kernel = jnp.exp(-(down + across - 2.0 * gram) / (spread * NCELL)).astype(BF16)
    owner = owners(total, BF16)
    half_way = jnp.dot(owner, kernel, preferred_element_type=F32).astype(BF16)
    full = lax.dot_general(half_way, owner, (((1,), (1,)), ((), ())), preferred_element_type=F32)
    full = jnp.where(same_line(total), full, 0.0)
    mixer[...] = full.astype(BF16)
    ksum = jnp.sum(full, axis=1, keepdims=True)
    own[...] = jnp.broadcast_to(1.0 + rate * coeff * ksum, (wide, LANES))
    for fetch in fetches:
        fetch.wait()

    stores = []

    def store(source, target, at):
        stores.append(pltpu.make_async_copy(source, target, out_sems.at[at]))
        stores[-1].start()

    def store_near(first, last, at):
        part = pl.ds(first, last - first)
        store(near_out.at[:, part, :], near_to.at[:, part, :], (half, at))

    def store_far(first, last, at):
        part = pl.ds(first - raw, last - first)
        for x, far_to in enumerate(far_tos):
            store(far_out.at[x, part, :], far_to.at[part, :], (x, at))

    def slab_step(with_far, i, carry):
        rows = wide if with_far else high
        for t in range(BLOCK // TILE):
            at = i * BLOCK + t * TILE
            part = lines_of(at, TILE)
            states = [near_ref[:, part, :].reshape(high, LANES)] + [ref[part, :] for ref in far_refs]
            slopes = grads[:, part, :].reshape(wide, LANES)
            states = jnp.concatenate(states, axis=0)
            new = mix(mixer.at[:rows, :], own.at[:rows, :], numbers_ref, total, states, slopes)
            near_out[:, part, :] = new[:high].reshape(half, TILE, LANES)
            if with_far:
                far_out[:, lines_of(at - raw, TILE), :] = new[high:].reshape(half, TILE, LANES)
        return carry

    here = lax.axis_index("slab").astype(jnp.int32) % half

    def raw_step(i, carry):
        for t in range(BLOCK // TILE):
            at = i * BLOCK + t * TILE
            part = lines_of(at, TILE)
            states = [near_ref[:, lines_of(lines + TILE + at, TILE), :].reshape(high, LANES)]
            slopes = [raw_grads[:half, part, :].reshape(high, LANES)]
            for x in range(half):
                states += [across_ref[here ^ x, part, :]]
                slopes += [raw_grads[half + (here ^ x), part, :]]
            states, slopes = jnp.concatenate(states, axis=0), jnp.concatenate(slopes, axis=0)
            new = mix(mixer.at[:high, :], own.at[:high, :], numbers_ref, total, states, slopes)
            near_out[:, lines_of(lines + at, TILE), :] = new.reshape(half, TILE, LANES)
        return carry

    lax.fori_loop(0, raw // BLOCK, raw_step, 0)
    store_near(lines, lines + raw, 0)
    lax.fori_loop(0, raw // BLOCK, functools.partial(slab_step, False), 0)
    middle = (raw + 2 * lines) // 3 // BLOCK * BLOCK
    lax.fori_loop(raw // BLOCK, middle // BLOCK, functools.partial(slab_step, True), 0)
    store_near(0, middle, 1)
    store_far(raw, middle, 0)
    lax.fori_loop(middle // BLOCK, lines // BLOCK, functools.partial(slab_step, True), 0)
    store_near(middle, lines, 2)
    store_far(middle, lines, 1)
    for copy in stores:
        copy.wait()


def update_pieces(numbers, grams, near, far, across, raw_fields, grads, groups, raw, lines):
    half = len(far)
    total = 2 * half
    wide = total * TILE
    out_shape = [pltpu.HBM((half, lines + raw, LANES), BF16)]
    out_shape += [pltpu.HBM((lines - raw, LANES), BF16)] * half
    return call(
        functools.partial(update_pieces_body, half, raw, lines, groups),
        "update_pieces",
        flops=4 * wide * wide * LANES * (lines // TILE),
        moved=6 * total * lines * LANES,
        in_specs=[IN_VMEM] * (half + 6) + [IN_HBM] * len(groups),
        out_specs=[IN_HBM] * len(out_shape),
        out_shape=out_shape,
        scratch_shapes=[
            pltpu.VMEM((half, lines + raw, LANES), BF16),
            pltpu.VMEM((half, lines - raw, LANES), BF16),
            pltpu.VMEM((wide, wide), BF16),
            pltpu.VMEM((wide, LANES), F32),
            pltpu.VMEM((total, lines, LANES), BF16),
            pltpu.VMEM((total, raw, LANES), BF16),
            pltpu.SemaphoreType.DMA((total,)),
            pltpu.SemaphoreType.DMA((half + 1, 3)),
        ],
    )(near, *far, across, *raw_fields, numbers, grams, *grads)


def exchange(piece, k, slabs):
    return lax.ppermute(piece, "slab", [(i, i ^ k) for i in range(slabs)])


def swap_near(pieces, slabs):
    groups = [list(range(slabs // 2)), list(range(slabs // 2, slabs))]
    return lax.all_to_all(pieces, "slab", 0, 0, axis_index_groups=groups, tiled=True)


RAW = 128
GRADIENTS = ((8, 9, 10, 11), (12, 13, 14, 15), (0, 1, 2, 3, 4, 5, 6, 7))


def by_halves(particles, observed, precision, spread, anneal, step_size):
    slabs = lax.axis_size("slab")
    half = slabs // 2
    lines = NCELL // slabs // LANES
    row = in_hbm(particles)
    fields = [in_hbm(field.reshape(-1, LANES)) for field in (observed, precision)]
    near, *far = split_pieces(row, slabs, RAW, fields)
    far, (obs, prec, *raw_fields) = far[:half], far[half:]
    near = swap_near(near, slabs)
    far = [exchange(piece, half + x, slabs) for x, piece in enumerate(far)]
    raw_near = raw_states(near, RAW, lines, far)
    across = exchange(raw_near, half, slabs)
    grads = []
    numbers = [spread, anneal, step_size]
    for group in GRADIENTS:
        if group[0] < half:
            arrays, views = [near], [(0, k) for k in group]
        else:
            arrays, views = [far[k - half] for k in group], [(j, None) for j in range(len(group))]
        slopes, rows = gradient_pieces(arrays, tuple(views), obs, prec, [] if grads else numbers)
        grads.append(in_hbm(slopes))
        numbers = numbers if len(grads) > 1 else rows
    grams = swap(gram_pieces(near, far, lines, grads[:1], [raw_near]))
    new_near, *new_far = update_pieces(
        numbers, grams, near, far, across, raw_fields, grads, GRADIENTS, RAW, lines
    )
    new_near = swap_near(new_near, slabs)
    new_far = [exchange(piece, half + x, slabs) for x, piece in enumerate(new_far)]
    row = join_pieces(None, slabs, RAW, [new_near], [(0, k, k) for k in range(half)])
    for group in ((0, 1, 2, 3), (4, 5)):
        pieces = [(n, None, half + x) for n, x in enumerate(group)]
        row = join_pieces(row, slabs, RAW, [new_far[x] for x in group], pieces)
    return join_pieces(row, slabs, RAW, new_far[6:], [(n, None, half + 6 + n) for n in range(half - 6)])


def on_device(particles, observed, precision, spread, anneal, step_size):
    slabs = lax.axis_size("slab")
    total = particles.shape[0] * slabs
    lines = NCELL // slabs // LANES
    if slabs == 16:
        return by_halves(particles, observed, precision, spread, anneal, step_size)
    sent, begun = cuts(lines)
    fields = [observed.reshape(-1, LANES), precision.reshape(-1, LANES)]
    numbers = [spread, anneal, step_size]
    first, obs, prec, scalars = split_row(particles, slabs, 0, sent, True, fields, numbers, [])
    parts = [swap(first)]
    if sent < lines:
        parts += [swap(split_row(particles, slabs, sent, lines, False, [], [], [scalars])[0])]
    if total * TILE > 256:
        grads = slab_gradient(parts, obs, prec, lines, 0, lines)
        states = jnp.concatenate([parts[0][:, :sent]] + parts[1:], axis=1)
        new = plain_update(spread, anneal, step_size, states, grads)
        return join_row(swap(new), lines, 0, None)
    if sent == lines:
        grads = slab_gradient(parts, obs, prec, lines, 0, lines)
        grams = swap(slab_gram(parts[0], lines, slabs, [], []))
        new = slab_update(scalars, grams, parts, grads, 0, lines, [])
        return join_row(swap(new), lines, 0, None)
    gram = slab_gram(parts[0], sent, 1, [], [])
    early = slab_gradient(parts[:1], obs, prec, lines, 0, begun)
    grams = swap(slab_gram(parts[1], lines - sent, slabs, [gram], [early]))
    late = slab_gradient(parts, obs, prec, lines, begun, lines)
    new = slab_update(scalars, grams, parts[:1], early, 0, begun, [])
    rest = slab_update(scalars, grams, parts, late, begun, lines, [new])
    row = join_row(swap(new), lines, 0, None)
    return join_row(swap(rest), lines, begun, row)


def solution(mesh):
    in_specs = (
        P(("groups", "slab"), None),
        P("groups"),
        P("groups"),
        P("groups"),
        P("groups"),
        P("groups"),
    )
    out_specs = P(("groups", "slab"), None)
    return jax.shard_map(
        on_device, mesh=mesh, in_specs=in_specs, out_specs=out_specs, check_vma=False
    )
```

```python
import functools

import jax
import jax.numpy as jnp
from jax import lax
from jax.experimental import pallas as pl
from jax.experimental.pallas import tpu as pltpu
from jax.sharding import PartitionSpec as P

GRID_X = 1024
GRID_Y = 1024
NCELL = 1048576
LANES = 128
LINE = GRID_Y // LANES
TILE = 16

prior_scale = 0.25
mass_term = 1.0

F32 = jnp.float32
BF16 = jnp.bfloat16
MIB = 1024 * 1024


def call(body, name, flops=0, moved=0, limit=16, **kwargs):
    return pl.pallas_call(
        body,
        name=name,
        compiler_params=pltpu.CompilerParams(vmem_limit_bytes=limit * MIB),
        cost_estimate=pl.CostEstimate(flops=flops, bytes_accessed=moved, transcendentals=0),
        **kwargs,
    )


IN_VMEM = pl.BlockSpec(memory_space=pltpu.VMEM)
IN_HBM = pl.BlockSpec(memory_space=pltpu.HBM)


def in_hbm(array):
    return pltpu.with_memory_space_constraint(array, pltpu.HBM)


BLOCK = 4 * TILE


def cuts(lines):
    if lines % (8 * BLOCK):
        return lines, lines
    return lines * 3 // 4, lines * 3 // 4 - BLOCK


def split_body(lines, begin, rim, fields, numbers, row_ref, *refs):
    field_refs, number_refs = refs[:fields], refs[fields : fields + numbers]
    out_ref, *slab_refs, rows_ref = refs[-7 - fields : -5]
    held, edges, sems, edge_sems, field_sems = refs[-5:]
    for k, number_ref in enumerate(number_refs):
        rows_ref[k : k + 1, :] = jnp.broadcast_to(number_ref[...].reshape(1, 1), (1, LANES))
    slabs, count, _ = out_ref.shape
    count -= TILE * rim
    size = count * LANES
    cells = lines * LANES

    def part(slab):
        source = row_ref.at[:, pl.ds(slab * cells + begin * LANES, size)]
        return pltpu.make_async_copy(source, held.at[:, pl.ds(slab * size, size)], sems.at[slab])

    def edge(slab):
        source = row_ref.at[:, pl.ds(slab * cells - GRID_Y, GRID_Y)]
        return pltpu.make_async_copy(source, edges.at[:, pl.ds(slab * GRID_Y, GRID_Y)], edge_sems.at[slab])

    def grid_row(ref, start):
        return ref[:, pl.ds(start, GRID_Y)].astype(F32).reshape(LINE, LANES)

    for slab in range(slabs):
        part(slab).start()
        if rim and slab:
            edge(slab).start()
    mine = pl.ds(pl.multiple_of(lax.axis_index("slab") * lines, TILE), lines)
    fetches = [
        pltpu.make_async_copy(source.at[mine, :], target, field_sems.at[k])
        for k, (source, target) in enumerate(zip(field_refs, slab_refs))
    ]
    for fetch in fetches:
        fetch.start()
    part(0).wait()
    outside = jnp.zeros((LINE, LANES), F32)
    for slab in range(slabs):
        if slab + 1 < slabs:
            part(slab + 1).wait()
        out_ref[slab, :count, :] = held[:, pl.ds(slab * size, size)].reshape(count, LANES)
        if rim:
            if slab:
                edge(slab).wait()
            below = grid_row(held, (slab + 1) * size) if slab + 1 < slabs else outside
            above = grid_row(edges, slab * GRID_Y) if slab else outside
            out_ref[slab, count:, :] = jnp.concatenate([below, above], axis=0).astype(BF16)
    for fetch in fetches:
        fetch.wait()


def split_row(row, slabs, begin, end, rim, fields, numbers, earlier):
    lines = row.shape[1] // slabs // LANES
    count = end - begin
    return call(
        functools.partial(split_body, lines, begin, rim, len(fields), len(numbers)),
        "split_row",
        moved=6 * slabs * count * LANES,
        in_specs=[IN_HBM] * (1 + len(fields)) + [IN_VMEM] * len(numbers) + [IN_HBM] * len(earlier),
        out_specs=[IN_VMEM] * (2 + len(fields)),
        out_shape=[jax.ShapeDtypeStruct((slabs, count + TILE * rim, LANES), BF16)]
        + [jax.ShapeDtypeStruct((lines, LANES), BF16)] * len(fields)
        + [jax.ShapeDtypeStruct((8, LANES), F32)],
        scratch_shapes=[
            pltpu.VMEM((1, slabs * count * LANES), BF16),
            pltpu.VMEM((1, slabs * GRID_Y), BF16),
            pltpu.SemaphoreType.DMA((slabs,)),
            pltpu.SemaphoreType.DMA((slabs,)),
            pltpu.SemaphoreType.DMA((2,)),
        ],
    )(row, *fields, *numbers, *earlier)


def join_body(lines, begin, slabs_ref, *refs):
    row_ref, held, sems = refs[-3:]
    slabs, count, _ = slabs_ref.shape
    size = count * LANES
    copies = []
    for slab in range(slabs):
        at = pl.ds(slab * size, size)
        held[:, at] = slabs_ref[slab].reshape(1, size)
        target = row_ref.at[:, pl.ds((slab * lines + begin) * LANES, size)]
        copies.append(pltpu.make_async_copy(held.at[:, at], target, sems.at[slab]))
        copies[-1].start()
    for copy in copies:
        copy.wait()


def join_row(slabs, lines, begin, row):
    total, count, _ = slabs.shape
    begun = [] if row is None else [row]
    return call(
        functools.partial(join_body, lines, begin),
        "join_row",
        moved=6 * slabs.size,
        in_specs=[IN_VMEM] + [IN_HBM] * len(begun),
        out_specs=IN_HBM,
        out_shape=jax.ShapeDtypeStruct((1, total * lines * LANES), BF16),
        input_output_aliases={1: 0} if begun else {},
        scratch_shapes=[pltpu.VMEM((1, slabs.size), BF16), pltpu.SemaphoreType.DMA((total,))],
    )(slabs, *begun)


def same_line(total):
    wide = total * TILE
    row = lax.broadcasted_iota(jnp.int32, (wide, wide), 0)
    col = lax.broadcasted_iota(jnp.int32, (wide, wide), 1)
    return row % TILE == col % TILE


def members(total, dtype):
    wide = total * TILE
    row = lax.broadcasted_iota(jnp.int32, (wide, total), 0)
    col = lax.broadcasted_iota(jnp.int32, (wide, total), 1)
    return (row // TILE == col).astype(dtype)


def gram_body(steps, tiles, parts, states_ref, *refs):
    out_ref, pairs = refs[-2:]
    total = states_ref.shape[0]
    wide = total * TILE
    pairs[...] = jnp.zeros_like(pairs)

    def step(i, carry):
        parts = [
            states_ref[:, pl.ds(pl.multiple_of((i * tiles + t) * TILE, TILE), TILE), :].reshape(wide, LANES)
            for t in range(tiles)
        ]
        block = jnp.concatenate(parts, axis=1)
        pairs[...] += lax.dot_general(block, block, (((1,), (1,)), ((), ())), preferred_element_type=F32)
        return carry

    lax.fori_loop(0, steps, step, 0)
    equal = jnp.where(same_line(total), pairs[...], 0.0)
    rows = jnp.sum(equal.reshape(total, TILE, wide), axis=1)
    gram = jnp.dot(rows, members(total, F32), precision=lax.Precision.HIGHEST, preferred_element_type=F32)
    gram = jnp.concatenate([gram, jnp.zeros((total, LANES - total), F32)], axis=1)
    for part_ref in refs[:parts]:
        gram += part_ref[0]
    out_ref[...] = jnp.broadcast_to(gram[None], out_ref.shape)


def slab_gram(states, lines, copies, parts, earlier):
    total = states.shape[0]
    wide = total * TILE
    tiles = min(8, lines // TILE)
    return call(
        functools.partial(gram_body, lines // TILE // tiles, tiles, len(parts)),
        "slab_gram",
        flops=2 * wide * wide * LANES * (lines // TILE),
        moved=2 * states.size,
        in_specs=[IN_VMEM] * (1 + len(parts)) + [IN_HBM] * len(earlier),
        out_specs=IN_VMEM,
        out_shape=jax.ShapeDtypeStruct((copies, total, LANES), F32),
        scratch_shapes=[pltpu.VMEM((wide, wide), F32)],
    )(states, *parts, *earlier)


def gradient_body(lines, begin, end, parts, *refs):
    observed, precision, out_ref, grads, sems = refs[parts:]
    total = grads.shape[0]
    first = refs[0].shape[1] - TILE
    rows = BLOCK // LINE
    group = 4
    shape = (rows, LINE, LANES)
    lane = lax.broadcasted_iota(jnp.int32, (1, LINE, LANES), 2)
    line = lax.broadcasted_iota(jnp.int32, (1, LINE, LANES), 1)

    def load(particle, at, count):
        ref, at = (refs[0], at) if at < first else (refs[1], at - first)
        return ref[particle, at : at + count, :].astype(F32)

    def rim(particle):
        return refs[0][particle, first:, :].astype(F32)

    stores = []
    for k, at in enumerate(range(begin, end, BLOCK)):
        mine = slice(at - begin, at - begin + BLOCK)
        obs = observed[at : at + BLOCK, :].astype(F32).reshape(shape)
        prec = precision[at : at + BLOCK, :].astype(F32).reshape(shape)

        def step(i, carry):
            for p in range(group):
                particle = i * group + p
                here = load(particle, at, BLOCK)
                before = load(particle, at - TILE, TILE) if at else rim(particle)
                after = load(particle, at + BLOCK, TILE) if at + BLOCK < lines else rim(particle)
                above = jnp.concatenate([before[LINE:], here[:-LINE]], axis=0).reshape(shape)
                below = jnp.concatenate([here[LINE:], after[:LINE]], axis=0).reshape(shape)
                field = here.reshape(shape)
                turned = pltpu.roll(field, 1, 2)
                carried = jnp.where(line == 0, 0.0, pltpu.roll(turned, 1, 1))
                left = jnp.where(lane == 0, carried, turned)
                turned = pltpu.roll(field, LANES - 1, 2)
                carried = jnp.where(line == LINE - 1, 0.0, pltpu.roll(turned, LINE - 1, 1))
                right = jnp.where(lane == LANES - 1, carried, turned)
                laplace = (4.0 + mass_term) * field - (below + above + right + left)
                squash = jnp.tanh(field)
                result = prec * (obs - squash) * (1.0 - squash * squash) - prior_scale * laplace
                grads[particle, mine, :] = result.reshape(BLOCK, LANES).astype(BF16)
            return carry

        lax.fori_loop(0, total // group, step, 0)
        stores.append(pltpu.make_async_copy(grads.at[:, mine, :], out_ref.at[:, mine, :], sems.at[k]))
        stores[-1].start()
    for store in stores:
        store.wait()


def slab_gradient(parts, observed, precision, lines, begin, end):
    total = parts[0].shape[0]
    count = end - begin
    out = jax.ShapeDtypeStruct((total, count, LANES), BF16)
    return call(
        functools.partial(gradient_body, lines, begin, end, len(parts)),
        "slab_gradient",
        flops=30 * out.size,
        moved=8 * out.size,
        in_specs=[IN_VMEM] * (len(parts) + 2),
        out_specs=IN_HBM,
        out_shape=out,
        scratch_shapes=[pltpu.VMEM(out.shape, BF16), pltpu.SemaphoreType.DMA((count // BLOCK,))],
    )(*parts, observed, precision)


def update_body(begin, end, parts, *refs):
    states_refs, refs = refs[:parts], refs[parts:]
    scalars_ref, grams_ref, grads_ref = refs[:3]
    out_ref, grads, mixer, own, sem = refs[-5:]
    total = out_ref.shape[0]
    wide = total * TILE
    fetch = pltpu.make_async_copy(grads_ref, grads, sem)
    fetch.start()
    gram = jnp.sum(grams_ref[...], axis=0)[:, :total]
    row = lax.broadcasted_iota(jnp.int32, (total, total), 0)
    col = lax.broadcasted_iota(jnp.int32, (total, total), 1)
    diagonal = jnp.where(row == col, gram, 0.0)
    down = jnp.sum(diagonal, axis=1, keepdims=True)
    across = jnp.sum(diagonal, axis=0, keepdims=True)
    member = members(total, BF16)
    spread, anneal, step_size = (scalars_ref[k : k + 1, :1] for k in range(3))
    rate = step_size / total
    coeff = 2.0 * anneal / spread
    kernel = jnp.exp(-(down + across - 2.0 * gram) / (spread * NCELL)).astype(BF16)
    ksum = jnp.sum(kernel.astype(F32), axis=1, keepdims=True)
    half = jnp.dot(member, kernel, preferred_element_type=F32).astype(BF16)
    full = lax.dot_general(half, member, (((1,), (1,)), ((), ())), preferred_element_type=F32)
    mixer[...] = jnp.where(same_line(total), full, 0.0).astype(BF16)
    gain = 1.0 + rate * coeff * ksum
    own[...] = jnp.broadcast_to(gain[:, :, None], (total, TILE, LANES)).reshape(wide, LANES)
    fetch.wait()

    done = 0
    for part, states_ref in enumerate(states_refs):
        have = states_ref.shape[1] - (0 if part else TILE)
        low = max(begin - done, 0)
        high = min(end - done, have)
        into = done - begin
        done += have

        def step(i, carry):
            for t in range(BLOCK // TILE):
                at = pl.multiple_of(i * BLOCK + t * TILE, TILE)
                there = pl.ds(pl.multiple_of(at + into, TILE), TILE)
                states = states_ref[:, pl.ds(at, TILE), :].reshape(wide, LANES)
                both = jnp.concatenate([grads[:, there, :].reshape(wide, LANES), states], axis=1)
                mixed = jnp.dot(mixer[...], both, preferred_element_type=F32)
                drive, pulled = mixed[:, :LANES], mixed[:, LANES:]
                new = states.astype(F32) * own[...] + rate * (drive - coeff * pulled)
                out_ref[:, there, :] = new.astype(BF16).reshape(total, TILE, LANES)
            return carry

        lax.fori_loop(low // BLOCK, high // BLOCK, step, 0)


def slab_update(scalars, grams, parts, grads, begin, end, earlier):
    total, count, _ = grads.shape
    wide = total * TILE
    return call(
        functools.partial(update_body, begin, end, len(parts)),
        "slab_update",
        flops=4 * wide * wide * LANES * (count // TILE),
        moved=6 * grads.size,
        in_specs=[IN_VMEM] * len(parts)
        + [IN_VMEM, IN_VMEM, IN_HBM]
        + [IN_HBM] * len(earlier),
        out_specs=IN_VMEM,
        out_shape=jax.ShapeDtypeStruct(grads.shape, BF16),
        scratch_shapes=[
            pltpu.VMEM(grads.shape, BF16),
            pltpu.VMEM((wide, wide), BF16),
            pltpu.VMEM((wide, LANES), F32),
            pltpu.SemaphoreType.DMA,
        ],
    )(*parts, scalars, grams, grads, *earlier)


def plain_update(spread, anneal, step_size, states, grads):
    total, lines, _ = grads.shape
    flat = states[:, :lines].reshape(total, -1)
    gram = lax.dot_general(flat, flat, (((1,), (1,)), ((), ())), preferred_element_type=F32)
    gram = lax.psum(gram, "slab")
    norms = jnp.diagonal(gram)
    kernel = jnp.exp(-(norms[:, None] + norms[None, :] - 2.0 * gram) / (spread[0] * NCELL)).astype(BF16)
    ksum = jnp.sum(kernel.astype(F32), axis=1)
    drive = jnp.dot(kernel, grads.reshape(total, -1), preferred_element_type=F32)
    pulled = jnp.dot(kernel, flat, preferred_element_type=F32)
    values = flat.astype(F32)
    repel = values * ksum[:, None] - pulled
    coeff = 2.0 * anneal[0] / spread[0]
    new = values + step_size[0] / total * (drive + coeff * repel)
    return new.astype(BF16).reshape(grads.shape)


def swap(slabs):
    return lax.all_to_all(slabs, "slab", split_axis=0, concat_axis=0, tiled=True)


def device_at(at, half):
    me = lax.axis_index("slab").astype(jnp.int32)
    return jnp.where(at < half, me - me % half + at, me ^ at)


def lines_of(start, count):
    return pl.ds(pl.multiple_of(start, TILE), count)


def split_pieces_body(slabs, raw, lines, fields, row_ref, *refs):
    half = slabs // 2
    field_refs, near_out, far_outs = refs[:fields], refs[fields], refs[fields + 1 : fields + 1 + half]
    slab_refs, helds, sems = refs[fields + 1 + half : -slabs - 1], refs[-slabs - 1 : -1], refs[-1]
    cells = lines * LANES
    end = row_ref.shape[1]
    started = []

    def fetch(source, target):
        started.append(pltpu.make_async_copy(source, target, sems.at[len(started)]))
        started[-1].start()
        return started[-1]

    copies = []
    for at, held in enumerate(helds):
        slab = device_at(at, half)
        parts = [
            (slab * cells, cells),
            (jnp.minimum((slab + 1) * cells, end - GRID_Y), GRID_Y),
            (jnp.maximum(slab * cells - GRID_Y, 0), GRID_Y),
        ]
        if at < half:
            other = slab ^ half
            parts += [(other * cells, raw * LANES + GRID_Y), (jnp.maximum(other * cells - GRID_Y, 0), GRID_Y)]
        mine, to = [], 0
        for start, size in parts:
            source = row_ref.at[:, pl.ds(pl.multiple_of(start, GRID_Y), size)]
            mine.append(fetch(source, held.at[:, pl.ds(to, size)]))
            to += size
        copies.append(mine)
    me = lax.axis_index("slab").astype(jnp.int32)
    fetches = []
    for n, target in enumerate(slab_refs):
        start = (me if n < fields else me ^ half) * lines
        fetches.append(fetch(field_refs[n % fields].at[lines_of(start, target.shape[0]), :], target))

    def grid_row(held, at):
        return held[:, pl.ds(at, GRID_Y)].astype(F32).reshape(LINE, LANES)

    for at, held in enumerate(helds):
        out_ref = near_out.at[at] if at < half else far_outs[at - half]
        for copy in copies[at]:
            copy.wait()
        slab = device_at(at, half)
        out_ref[:lines, :] = held[:, :cells].reshape(lines, LANES)
        below = jnp.where(slab == slabs - 1, 0.0, grid_row(held, cells))
        above = jnp.where(slab == 0, 0.0, grid_row(held, cells + GRID_Y))
        out_ref[lines : lines + TILE, :] = jnp.concatenate([below, above], axis=0).astype(BF16)
        if at < half:
            start = cells + 2 * GRID_Y
            to = lines + TILE
            out_ref[to : to + raw, :] = held[:, start : start + raw * LANES].reshape(raw, LANES)
            below = grid_row(held, start + raw * LANES)
            above = jnp.where(slab ^ half == 0, 0.0, grid_row(held, start + raw * LANES + GRID_Y))
            out_ref[to + raw :, :] = jnp.concatenate([below, above], axis=0).astype(BF16)
    for copy in fetches:
        copy.wait()


def split_pieces(row, slabs, raw, fields):
    lines = row.shape[1] // slabs // LANES
    half = slabs // 2
    rim = lines + TILE
    size = rim + raw + TILE
    out_shape = [jax.ShapeDtypeStruct((half, size, LANES), BF16)]
    out_shape += [jax.ShapeDtypeStruct((rim, LANES), BF16)] * half
    out_shape += [jax.ShapeDtypeStruct((lines, LANES), BF16)] * len(fields)
    out_shape += [jax.ShapeDtypeStruct((raw, LANES), BF16)] * len(fields)
    return call(
        functools.partial(split_pieces_body, slabs, raw, lines, len(fields)),
        "split_pieces",
        moved=6 * half * (rim + size) * LANES,
        in_specs=[IN_HBM] * (1 + len(fields)),
        out_specs=[IN_VMEM] * len(out_shape),
        out_shape=out_shape,
        scratch_shapes=[pltpu.VMEM((1, size * LANES), BF16)] * half
        + [pltpu.VMEM((1, rim * LANES), BF16)] * half
        + [pltpu.SemaphoreType.DMA((8 * slabs + 2 * len(fields),))],
    )(row, *fields)


def join_pieces_body(pieces, half, raw, lines, begun, arrays, *refs):
    row_ref, helds, sems = refs[begun + arrays], refs[begun + arrays + 1 : -1], refs[-1]
    cells = lines * LANES
    skip = raw * LANES
    copies = []
    for (array, lead, at), held in zip(pieces, helds):
        ref = refs[begun + array]
        piece = ref[...] if lead is None else ref[lead]
        held[...] = piece.reshape(held.shape)
        slab = device_at(at, half)
        if at < half:
            parts = [(0, cells, slab * cells), (cells, skip, (slab ^ half) * cells)]
        else:
            parts = [(0, cells - skip, slab * cells + skip)]
        for begin, size, start in parts:
            target = row_ref.at[:, pl.ds(pl.multiple_of(start, GRID_Y), size)]
            copies.append(pltpu.make_async_copy(held.at[:, pl.ds(begin, size)], target, sems.at[len(copies)]))
            copies[-1].start()
    for copy in copies:
        copy.wait()


def join_pieces(row, slabs, raw, arrays, pieces):
    sizes = [arrays[piece[0]].shape[-2] * LANES for piece in pieces]
    begun = [] if row is None else [row]
    return call(
        functools.partial(
            join_pieces_body, pieces, slabs // 2, raw, NCELL // slabs // LANES, len(begun), len(arrays)
        ),
        "join_pieces",
        moved=6 * sum(sizes),
        in_specs=[IN_HBM] * len(begun) + [IN_VMEM] * len(arrays),
        out_specs=IN_HBM,
        out_shape=jax.ShapeDtypeStruct((1, NCELL), BF16),
        input_output_aliases={0: 0} if begun else {},
        scratch_shapes=[pltpu.VMEM((1, size), BF16) for size in sizes]
        + [pltpu.SemaphoreType.DMA((2 * len(sizes),))],
    )(*begun, *arrays)


def owners(total, dtype):
    wide = total * TILE
    row = lax.broadcasted_iota(jnp.int32, (wide, total), 0)
    col = lax.broadcasted_iota(jnp.int32, (wide, total), 1)
    return (device_at(row // TILE, total // 2) == col).astype(dtype)


def gram_pieces_body(lines, total, near_ref, *refs):
    half = total // 2
    pieces, out_ref, pairs = refs[:half], refs[-2], refs[-1]
    wide = total * TILE
    tiles = 8
    pairs[...] = jnp.zeros_like(pairs)

    def step(i, carry):
        parts = []
        for t in range(tiles):
            at = lines_of((i * tiles + t) * TILE, TILE)
            near = near_ref[:, at, :].reshape(wide // 2, LANES)
            parts.append(jnp.concatenate([near] + [piece[at, :] for piece in pieces], axis=0))
        block = jnp.concatenate(parts, axis=1)
        pairs[...] += lax.dot_general(block, block, (((1,), (1,)), ((), ())), preferred_element_type=F32)
        return carry

    lax.fori_loop(0, lines // TILE // tiles, step, 0)
    equal = jnp.where(same_line(total), pairs[...], 0.0)
    exact = {"precision": lax.Precision.HIGHEST, "preferred_element_type": F32}
    rows = jnp.sum(equal.reshape(total, TILE, wide), axis=1)
    gram = jnp.dot(rows, owners(total, F32), **exact)
    row = lax.broadcasted_iota(jnp.int32, (total, total), 0)
    col = lax.broadcasted_iota(jnp.int32, (total, total), 1)
    gram = jnp.dot((row == device_at(col, half)).astype(F32), gram, **exact)
    gram = jnp.concatenate([gram, jnp.zeros((total, LANES - total), F32)], axis=1)
    out_ref[...] = jnp.broadcast_to(gram[None], out_ref.shape)


def gram_pieces(near, far, lines, gates, early):
    total = 2 * len(far)
    wide = total * TILE
    return call(
        functools.partial(gram_pieces_body, lines, total),
        "gram_pieces",
        flops=2 * wide * wide * LANES * (lines // TILE),
        moved=2 * total * lines * LANES,
        in_specs=[IN_VMEM] * (1 + len(far)) + [IN_HBM] * len(gates) + [IN_VMEM] * len(early),
        out_specs=IN_VMEM,
        out_shape=jax.ShapeDtypeStruct((total, total, LANES), F32),
        scratch_shapes=[pltpu.VMEM((wide, wide), F32)],
    )(near, *far, *gates, *early)


def block_gradient(load, i, count, observed, precision):
    start = i * BLOCK
    at = lines_of(start, BLOCK)
    shape = (BLOCK // LINE, LINE, LANES)
    lane = lax.broadcasted_iota(jnp.int32, (1, LINE, LANES), 2)
    line = lax.broadcasted_iota(jnp.int32, (1, LINE, LANES), 1)
    obs = observed[at, :].astype(F32).reshape(shape)
    prec = precision[at, :].astype(F32).reshape(shape)
    here = load(start, BLOCK).astype(F32)
    before = load(jnp.where(i == 0, count, start - TILE), TILE).astype(F32)
    after = load(start + BLOCK, TILE).astype(F32)
    above = jnp.concatenate([before[LINE:], here[:-LINE]], axis=0).reshape(shape)
    below = jnp.concatenate([here[LINE:], after[:LINE]], axis=0).reshape(shape)
    field = here.reshape(shape)
    turned = pltpu.roll(field, 1, 2)
    carried = jnp.where(line == 0, 0.0, pltpu.roll(turned, 1, 1))
    left = jnp.where(lane == 0, carried, turned)
    turned = pltpu.roll(field, LANES - 1, 2)
    carried = jnp.where(line == LINE - 1, 0.0, pltpu.roll(turned, LINE - 1, 1))
    right = jnp.where(lane == LANES - 1, carried, turned)
    laplace = (4.0 + mass_term) * field - (below + above + right + left)
    squash = jnp.tanh(field)
    result = prec * (obs - squash) * (1.0 - squash * squash) - prior_scale * laplace
    return result.reshape(BLOCK, LANES).astype(BF16)


def gradient_pieces_body(views, arrays, numbers, *refs):
    observed, precision, *number_refs = refs[arrays : arrays + 2 + numbers]
    out_ref, rows_ref, grads, sems = refs[-4:]
    for n, number_ref in enumerate(number_refs):
        rows_ref[n : n + 1, :] = jnp.full((1, LANES), number_ref[0], F32)
    count = observed.shape[0]
    steps = count // BLOCK

    def store(i):
        at = lines_of(i * BLOCK, BLOCK)
        return pltpu.make_async_copy(grads.at[:, at, :], out_ref.at[:, at, :], sems.at[i])

    def step(i, carry):
        for p, (array, lead) in enumerate(views):

            def load(start, size):
                part = lines_of(start, size)
                return refs[array][part, :] if lead is None else refs[array][lead, part, :]

            grads[p, lines_of(i * BLOCK, BLOCK), :] = block_gradient(load, i, count, observed, precision)
        store(i).start()
        return carry

    def finish(i, carry):
        store(i).wait()
        return carry

    lax.fori_loop(0, steps, step, 0)
    lax.fori_loop(0, steps, finish, 0)


def gradient_pieces(arrays, views, observed, precision, numbers):
    count = observed.shape[0]
    out = pltpu.HBM((len(views), count, LANES), BF16)
    size = len(views) * count * LANES
    return call(
        functools.partial(gradient_pieces_body, views, len(arrays), len(numbers)),
        "gradient_pieces",
        flops=30 * size,
        moved=8 * size,
        in_specs=[IN_VMEM] * (len(arrays) + 2)
        + [pl.BlockSpec(memory_space=pltpu.SMEM)] * len(numbers),
        out_specs=[IN_HBM, IN_VMEM],
        out_shape=[out, jax.ShapeDtypeStruct((8, LANES), F32)],
        scratch_shapes=[pltpu.VMEM(out.shape, BF16), pltpu.SemaphoreType.DMA((count // BLOCK,))],
    )(*arrays, observed, precision, *numbers)


def raw_body(raw, lines, near_ref, *refs):
    out_ref = refs[-1]
    for k in range(near_ref.shape[0]):
        out_ref[k, :raw, :] = near_ref[k, :raw, :]
        below = near_ref[k, raw : raw + TILE, :].astype(F32)[:LINE]
        above = near_ref[k, lines : lines + TILE, :].astype(F32)[LINE:]
        out_ref[k, raw:, :] = jnp.concatenate([below, above], axis=0).astype(BF16)


def raw_states(near, raw, lines, gates):
    out = jax.ShapeDtypeStruct((near.shape[0], raw + TILE, LANES), BF16)
    return call(
        functools.partial(raw_body, raw, lines),
        "raw_states",
        moved=4 * out.size,
        in_specs=[IN_VMEM] * (1 + len(gates)),
        out_specs=IN_VMEM,
        out_shape=out,
    )(near, *gates)


def mix(mixer, own, numbers_ref, total, states, slopes):
    high = mixer.shape[0]
    rate = numbers_ref[2:3, :1] / total
    coeff = 2.0 * numbers_ref[1:2, :1] / numbers_ref[:1, :1]
    both = jnp.concatenate([slopes, states], axis=1)
    mixed = jnp.dot(mixer[...], both, preferred_element_type=F32)
    drive, pulled = mixed[:, :LANES], mixed[:, LANES:]
    return (states[:high].astype(F32) * own[...] + rate * (drive - coeff * pulled)).astype(BF16)


def update_pieces_body(half, raw, lines, groups, near_ref, *refs):
    total = 2 * half
    far_refs, refs = refs[:half], refs[half:]
    across_ref, raw_observed, raw_precision, numbers_ref, grams_ref, *refs = refs
    group_refs, near_to, far_tos = refs[: len(groups)], refs[len(groups)], refs[len(groups) + 1 : -8]
    near_out, far_out, mixer, own, grads, raw_grads, sems, out_sems = refs[-8:]
    wide = total * TILE
    high = half * TILE
    fetches = []
    for group, group_ref in zip(groups, group_refs):
        for j, at in enumerate(group):
            fetches.append(pltpu.make_async_copy(group_ref.at[j], grads.at[at], sems.at[len(fetches)]))
    for fetch in fetches:
        fetch.start()

    def raw_gradient(i, carry):
        for k in range(total):

            def load(start, size):
                if k < half:
                    return near_ref[k, lines_of(lines + TILE + start, size), :]
                return across_ref[k - half, lines_of(start, size), :]

            part = lines_of(i * BLOCK, BLOCK)
            raw_grads[k, part, :] = block_gradient(load, i, raw, raw_observed, raw_precision)
        return carry

    lax.fori_loop(0, raw // BLOCK, raw_gradient, 0)
    gram = jnp.sum(grams_ref[...], axis=0)[:, :total]
    spread, anneal, step_size = (numbers_ref[k : k + 1, :1] for k in range(3))
    rate = step_size / total
    coeff = 2.0 * anneal / spread
    row = lax.broadcasted_iota(jnp.int32, (total, total), 0)
    col = lax.broadcasted_iota(jnp.int32, (total, total), 1)
    diagonal = jnp.where(row == col, gram, 0.0)
    down = jnp.sum(diagonal, axis=1, keepdims=True)
    across = jnp.sum(diagonal, axis=0, keepdims=True)
    kernel = jnp.exp(-(down + across - 2.0 * gram) / (spread * NCELL)).astype(BF16)
    owner = owners(total, BF16)
    half_way = jnp.dot(owner, kernel, preferred_element_type=F32).astype(BF16)
    full = lax.dot_general(half_way, owner, (((1,), (1,)), ((), ())), preferred_element_type=F32)
    full = jnp.where(same_line(total), full, 0.0)
    mixer[...] = full.astype(BF16)
    ksum = jnp.sum(full, axis=1, keepdims=True)
    own[...] = jnp.broadcast_to(1.0 + rate * coeff * ksum, (wide, LANES))
    for fetch in fetches:
        fetch.wait()

    stores = []

    def store(source, target, at):
        stores.append(pltpu.make_async_copy(source, target, out_sems.at[at]))
        stores[-1].start()

    def store_near(first, last, at):
        part = pl.ds(first, last - first)
        store(near_out.at[:, part, :], near_to.at[:, part, :], (half, at))

    def store_far(first, last, at):
        part = pl.ds(first - raw, last - first)
        for x, far_to in enumerate(far_tos):
            store(far_out.at[x, part, :], far_to.at[part, :], (x, at))

    def slab_step(with_far, i, carry):
        rows = wide if with_far else high
        for t in range(BLOCK // TILE):
            at = i * BLOCK + t * TILE
            part = lines_of(at, TILE)
            states = [near_ref[:, part, :].reshape(high, LANES)] + [ref[part, :] for ref in far_refs]
            slopes = grads[:, part, :].reshape(wide, LANES)
            states = jnp.concatenate(states, axis=0)
            new = mix(mixer.at[:rows, :], own.at[:rows, :], numbers_ref, total, states, slopes)
            near_out[:, part, :] = new[:high].reshape(half, TILE, LANES)
            if with_far:
                far_out[:, lines_of(at - raw, TILE), :] = new[high:].reshape(half, TILE, LANES)
        return carry

    here = lax.axis_index("slab").astype(jnp.int32) % half

    def raw_step(i, carry):
        for t in range(BLOCK // TILE):
            at = i * BLOCK + t * TILE
            part = lines_of(at, TILE)
            states = [near_ref[:, lines_of(lines + TILE + at, TILE), :].reshape(high, LANES)]
            slopes = [raw_grads[:half, part, :].reshape(high, LANES)]
            for x in range(half):
                states += [across_ref[here ^ x, part, :]]
                slopes += [raw_grads[half + (here ^ x), part, :]]
            states, slopes = jnp.concatenate(states, axis=0), jnp.concatenate(slopes, axis=0)
            new = mix(mixer.at[:high, :], own.at[:high, :], numbers_ref, total, states, slopes)
            near_out[:, lines_of(lines + at, TILE), :] = new.reshape(half, TILE, LANES)
        return carry

    lax.fori_loop(0, raw // BLOCK, raw_step, 0)
    store_near(lines, lines + raw, 0)
    lax.fori_loop(0, raw // BLOCK, functools.partial(slab_step, False), 0)
    middle = (raw + 2 * lines) // 3 // BLOCK * BLOCK
    lax.fori_loop(raw // BLOCK, middle // BLOCK, functools.partial(slab_step, True), 0)
    store_near(0, middle, 1)
    store_far(raw, middle, 0)
    lax.fori_loop(middle // BLOCK, lines // BLOCK, functools.partial(slab_step, True), 0)
    store_near(middle, lines, 2)
    store_far(middle, lines, 1)
    for copy in stores:
        copy.wait()


def update_pieces(numbers, grams, near, far, across, raw_fields, grads, groups, raw, lines):
    half = len(far)
    total = 2 * half
    wide = total * TILE
    out_shape = [pltpu.HBM((half, lines + raw, LANES), BF16)]
    out_shape += [pltpu.HBM((lines - raw, LANES), BF16)] * half
    return call(
        functools.partial(update_pieces_body, half, raw, lines, groups),
        "update_pieces",
        flops=4 * wide * wide * LANES * (lines // TILE),
        moved=6 * total * lines * LANES,
        in_specs=[IN_VMEM] * (half + 6) + [IN_HBM] * len(groups),
        out_specs=[IN_HBM] * len(out_shape),
        out_shape=out_shape,
        scratch_shapes=[
            pltpu.VMEM((half, lines + raw, LANES), BF16),
            pltpu.VMEM((half, lines - raw, LANES), BF16),
            pltpu.VMEM((wide, wide), BF16),
            pltpu.VMEM((wide, LANES), F32),
            pltpu.VMEM((total, lines, LANES), BF16),
            pltpu.VMEM((total, raw, LANES), BF16),
            pltpu.SemaphoreType.DMA((total,)),
            pltpu.SemaphoreType.DMA((half + 1, 3)),
        ],
    )(near, *far, across, *raw_fields, numbers, grams, *grads)


def exchange(piece, k, slabs):
    return lax.ppermute(piece, "slab", [(i, i ^ k) for i in range(slabs)])


def swap_near(pieces, slabs):
    groups = [list(range(slabs // 2)), list(range(slabs // 2, slabs))]
    return lax.all_to_all(pieces, "slab", 0, 0, axis_index_groups=groups, tiled=True)


RAW = 64
GRADIENTS = ((8, 9, 10, 11), (12, 13, 14, 15), (0, 1, 2, 3, 4, 5, 6, 7))


def by_halves(particles, observed, precision, spread, anneal, step_size):
    slabs = lax.axis_size("slab")
    half = slabs // 2
    lines = NCELL // slabs // LANES
    row = in_hbm(particles)
    fields = [in_hbm(field.reshape(-1, LANES)) for field in (observed, precision)]
    near, *far = split_pieces(row, slabs, RAW, fields)
    far, (obs, prec, *raw_fields) = far[:half], far[half:]
    near = swap_near(near, slabs)
    far = [exchange(piece, half + x, slabs) for x, piece in enumerate(far)]
    raw_near = raw_states(near, RAW, lines, far)
    across = exchange(raw_near, half, slabs)
    grads = []
    numbers = [spread, anneal, step_size]
    for group in GRADIENTS:
        if group[0] < half:
            arrays, views = [near], [(0, k) for k in group]
        else:
            arrays, views = [far[k - half] for k in group], [(j, None) for j in range(len(group))]
        slopes, rows = gradient_pieces(arrays, tuple(views), obs, prec, [] if grads else numbers)
        grads.append(in_hbm(slopes))
        numbers = numbers if len(grads) > 1 else rows
    grams = swap(gram_pieces(near, far, lines, grads[:1], [raw_near]))
    new_near, *new_far = update_pieces(
        numbers, grams, near, far, across, raw_fields, grads, GRADIENTS, RAW, lines
    )
    new_near = swap_near(new_near, slabs)
    new_far = [exchange(piece, half + x, slabs) for x, piece in enumerate(new_far)]
    row = join_pieces(None, slabs, RAW, [new_near], [(0, k, k) for k in range(half)])
    for group in ((0, 1, 2, 3), (4, 5)):
        pieces = [(n, None, half + x) for n, x in enumerate(group)]
        row = join_pieces(row, slabs, RAW, [new_far[x] for x in group], pieces)
    return join_pieces(row, slabs, RAW, new_far[6:], [(n, None, half + 6 + n) for n in range(half - 6)])


def on_device(particles, observed, precision, spread, anneal, step_size):
    slabs = lax.axis_size("slab")
    total = particles.shape[0] * slabs
    lines = NCELL // slabs // LANES
    if slabs == 16:
        return by_halves(particles, observed, precision, spread, anneal, step_size)
    sent, begun = cuts(lines)
    fields = [observed.reshape(-1, LANES), precision.reshape(-1, LANES)]
    numbers = [spread, anneal, step_size]
    first, obs, prec, scalars = split_row(particles, slabs, 0, sent, True, fields, numbers, [])
    parts = [swap(first)]
    if sent < lines:
        parts += [swap(split_row(particles, slabs, sent, lines, False, [], [], [scalars])[0])]
    if total * TILE > 256:
        grads = slab_gradient(parts, obs, prec, lines, 0, lines)
        states = jnp.concatenate([parts[0][:, :sent]] + parts[1:], axis=1)
        new = plain_update(spread, anneal, step_size, states, grads)
        return join_row(swap(new), lines, 0, None)
    if sent == lines:
        grads = slab_gradient(parts, obs, prec, lines, 0, lines)
        grams = swap(slab_gram(parts[0], lines, slabs, [], []))
        new = slab_update(scalars, grams, parts, grads, 0, lines, [])
        return join_row(swap(new), lines, 0, None)
    gram = slab_gram(parts[0], sent, 1, [], [])
    early = slab_gradient(parts[:1], obs, prec, lines, 0, begun)
    grams = swap(slab_gram(parts[1], lines - sent, slabs, [gram], [early]))
    late = slab_gradient(parts, obs, prec, lines, begun, lines)
    new = slab_update(scalars, grams, parts[:1], early, 0, begun, [])
    rest = slab_update(scalars, grams, parts, late, begun, lines, [new])
    row = join_row(swap(new), lines, 0, None)
    return join_row(swap(rest), lines, begun, row)


def solution(mesh):
    in_specs = (
        P(("groups", "slab"), None),
        P("groups"),
        P("groups"),
        P("groups"),
        P("groups"),
        P("groups"),
    )
    out_specs = P(("groups", "slab"), None)
    return jax.shard_map(
        on_device, mesh=mesh, in_specs=in_specs, out_specs=out_specs, check_vma=False
    )
```

```python
import functools

import jax
import jax.numpy as jnp
from jax import lax
from jax.experimental import pallas as pl
from jax.experimental.pallas import tpu as pltpu
from jax.sharding import PartitionSpec as P

GRID_X = 1024
GRID_Y = 1024
NCELL = 1048576
LANES = 128
LINE = GRID_Y // LANES
TILE = 16

prior_scale = 0.25
mass_term = 1.0

F32 = jnp.float32
BF16 = jnp.bfloat16
MIB = 1024 * 1024


def call(body, name, flops=0, moved=0, limit=16, **kwargs):
    return pl.pallas_call(
        body,
        name=name,
        compiler_params=pltpu.CompilerParams(vmem_limit_bytes=limit * MIB),
        cost_estimate=pl.CostEstimate(flops=flops, bytes_accessed=moved, transcendentals=0),
        **kwargs,
    )


IN_VMEM = pl.BlockSpec(memory_space=pltpu.VMEM)
IN_HBM = pl.BlockSpec(memory_space=pltpu.HBM)


def in_hbm(array):
    return pltpu.with_memory_space_constraint(array, pltpu.HBM)


BLOCK = 4 * TILE


def cuts(lines):
    if lines % (8 * BLOCK):
        return lines, lines
    return lines * 3 // 4, lines * 3 // 4 - BLOCK


def split_body(lines, begin, rim, fields, numbers, row_ref, *refs):
    field_refs, number_refs = refs[:fields], refs[fields : fields + numbers]
    out_ref, *slab_refs, rows_ref = refs[-7 - fields : -5]
    held, edges, sems, edge_sems, field_sems = refs[-5:]
    for k, number_ref in enumerate(number_refs):
        rows_ref[k : k + 1, :] = jnp.broadcast_to(number_ref[...].reshape(1, 1), (1, LANES))
    slabs, count, _ = out_ref.shape
    count -= TILE * rim
    size = count * LANES
    cells = lines * LANES

    def part(slab):
        source = row_ref.at[:, pl.ds(slab * cells + begin * LANES, size)]
        return pltpu.make_async_copy(source, held.at[:, pl.ds(slab * size, size)], sems.at[slab])

    def edge(slab):
        source = row_ref.at[:, pl.ds(slab * cells - GRID_Y, GRID_Y)]
        return pltpu.make_async_copy(source, edges.at[:, pl.ds(slab * GRID_Y, GRID_Y)], edge_sems.at[slab])

    def grid_row(ref, start):
        return ref[:, pl.ds(start, GRID_Y)].astype(F32).reshape(LINE, LANES)

    for slab in range(slabs):
        part(slab).start()
        if rim and slab:
            edge(slab).start()
    mine = pl.ds(pl.multiple_of(lax.axis_index("slab") * lines, TILE), lines)
    fetches = [
        pltpu.make_async_copy(source.at[mine, :], target, field_sems.at[k])
        for k, (source, target) in enumerate(zip(field_refs, slab_refs))
    ]
    for fetch in fetches:
        fetch.start()
    part(0).wait()
    outside = jnp.zeros((LINE, LANES), F32)
    for slab in range(slabs):
        if slab + 1 < slabs:
            part(slab + 1).wait()
        out_ref[slab, :count, :] = held[:, pl.ds(slab * size, size)].reshape(count, LANES)
        if rim:
            if slab:
                edge(slab).wait()
            below = grid_row(held, (slab + 1) * size) if slab + 1 < slabs else outside
            above = grid_row(edges, slab * GRID_Y) if slab else outside
            out_ref[slab, count:, :] = jnp.concatenate([below, above], axis=0).astype(BF16)
    for fetch in fetches:
        fetch.wait()


def split_row(row, slabs, begin, end, rim, fields, numbers, earlier):
    lines = row.shape[1] // slabs // LANES
    count = end - begin
    return call(
        functools.partial(split_body, lines, begin, rim, len(fields), len(numbers)),
        "split_row",
        moved=6 * slabs * count * LANES,
        in_specs=[IN_HBM] * (1 + len(fields)) + [IN_VMEM] * len(numbers) + [IN_HBM] * len(earlier),
        out_specs=[IN_VMEM] * (2 + len(fields)),
        out_shape=[jax.ShapeDtypeStruct((slabs, count + TILE * rim, LANES), BF16)]
        + [jax.ShapeDtypeStruct((lines, LANES), BF16)] * len(fields)
        + [jax.ShapeDtypeStruct((8, LANES), F32)],
        scratch_shapes=[
            pltpu.VMEM((1, slabs * count * LANES), BF16),
            pltpu.VMEM((1, slabs * GRID_Y), BF16),
            pltpu.SemaphoreType.DMA((slabs,)),
            pltpu.SemaphoreType.DMA((slabs,)),
            pltpu.SemaphoreType.DMA((2,)),
        ],
    )(row, *fields, *numbers, *earlier)


def join_body(lines, begin, slabs_ref, *refs):
    row_ref, held, sems = refs[-3:]
    slabs, count, _ = slabs_ref.shape
    size = count * LANES
    copies = []
    for slab in range(slabs):
        at = pl.ds(slab * size, size)
        held[:, at] = slabs_ref[slab].reshape(1, size)
        target = row_ref.at[:, pl.ds((slab * lines + begin) * LANES, size)]
        copies.append(pltpu.make_async_copy(held.at[:, at], target, sems.at[slab]))
        copies[-1].start()
    for copy in copies:
        copy.wait()


def join_row(slabs, lines, begin, row):
    total, count, _ = slabs.shape
    begun = [] if row is None else [row]
    return call(
        functools.partial(join_body, lines, begin),
        "join_row",
        moved=6 * slabs.size,
        in_specs=[IN_VMEM] + [IN_HBM] * len(begun),
        out_specs=IN_HBM,
        out_shape=jax.ShapeDtypeStruct((1, total * lines * LANES), BF16),
        input_output_aliases={1: 0} if begun else {},
        scratch_shapes=[pltpu.VMEM((1, slabs.size), BF16), pltpu.SemaphoreType.DMA((total,))],
    )(slabs, *begun)


def same_line(total):
    wide = total * TILE
    row = lax.broadcasted_iota(jnp.int32, (wide, wide), 0)
    col = lax.broadcasted_iota(jnp.int32, (wide, wide), 1)
    return row % TILE == col % TILE


def members(total, dtype):
    wide = total * TILE
    row = lax.broadcasted_iota(jnp.int32, (wide, total), 0)
    col = lax.broadcasted_iota(jnp.int32, (wide, total), 1)
    return (row // TILE == col).astype(dtype)


def gram_body(steps, tiles, parts, states_ref, *refs):
    out_ref, pairs = refs[-2:]
    total = states_ref.shape[0]
    wide = total * TILE
    pairs[...] = jnp.zeros_like(pairs)

    def step(i, carry):
        parts = [
            states_ref[:, pl.ds(pl.multiple_of((i * tiles + t) * TILE, TILE), TILE), :].reshape(wide, LANES)
            for t in range(tiles)
        ]
        block = jnp.concatenate(parts, axis=1)
        pairs[...] += lax.dot_general(block, block, (((1,), (1,)), ((), ())), preferred_element_type=F32)
        return carry

    lax.fori_loop(0, steps, step, 0)
    equal = jnp.where(same_line(total), pairs[...], 0.0)
    rows = jnp.sum(equal.reshape(total, TILE, wide), axis=1)
    gram = jnp.dot(rows, members(total, F32), precision=lax.Precision.HIGHEST, preferred_element_type=F32)
    gram = jnp.concatenate([gram, jnp.zeros((total, LANES - total), F32)], axis=1)
    for part_ref in refs[:parts]:
        gram += part_ref[0]
    out_ref[...] = jnp.broadcast_to(gram[None], out_ref.shape)


def slab_gram(states, lines, copies, parts, earlier):
    total = states.shape[0]
    wide = total * TILE
    tiles = min(8, lines // TILE)
    return call(
        functools.partial(gram_body, lines // TILE // tiles, tiles, len(parts)),
        "slab_gram",
        flops=2 * wide * wide * LANES * (lines // TILE),
        moved=2 * states.size,
        in_specs=[IN_VMEM] * (1 + len(parts)) + [IN_HBM] * len(earlier),
        out_specs=IN_VMEM,
        out_shape=jax.ShapeDtypeStruct((copies, total, LANES), F32),
        scratch_shapes=[pltpu.VMEM((wide, wide), F32)],
    )(states, *parts, *earlier)


def gradient_body(lines, begin, end, parts, *refs):
    observed, precision, out_ref, grads, sems = refs[parts:]
    total = grads.shape[0]
    first = refs[0].shape[1] - TILE
    rows = BLOCK // LINE
    group = 4
    shape = (rows, LINE, LANES)
    lane = lax.broadcasted_iota(jnp.int32, (1, LINE, LANES), 2)
    line = lax.broadcasted_iota(jnp.int32, (1, LINE, LANES), 1)

    def load(particle, at, count):
        ref, at = (refs[0], at) if at < first else (refs[1], at - first)
        return ref[particle, at : at + count, :].astype(F32)

    def rim(particle):
        return refs[0][particle, first:, :].astype(F32)

    stores = []
    for k, at in enumerate(range(begin, end, BLOCK)):
        mine = slice(at - begin, at - begin + BLOCK)
        obs = observed[at : at + BLOCK, :].astype(F32).reshape(shape)
        prec = precision[at : at + BLOCK, :].astype(F32).reshape(shape)

        def step(i, carry):
            for p in range(group):
                particle = i * group + p
                here = load(particle, at, BLOCK)
                before = load(particle, at - TILE, TILE) if at else rim(particle)
                after = load(particle, at + BLOCK, TILE) if at + BLOCK < lines else rim(particle)
                above = jnp.concatenate([before[LINE:], here[:-LINE]], axis=0).reshape(shape)
                below = jnp.concatenate([here[LINE:], after[:LINE]], axis=0).reshape(shape)
                field = here.reshape(shape)
                turned = pltpu.roll(field, 1, 2)
                carried = jnp.where(line == 0, 0.0, pltpu.roll(turned, 1, 1))
                left = jnp.where(lane == 0, carried, turned)
                turned = pltpu.roll(field, LANES - 1, 2)
                carried = jnp.where(line == LINE - 1, 0.0, pltpu.roll(turned, LINE - 1, 1))
                right = jnp.where(lane == LANES - 1, carried, turned)
                laplace = (4.0 + mass_term) * field - (below + above + right + left)
                squash = jnp.tanh(field)
                result = prec * (obs - squash) * (1.0 - squash * squash) - prior_scale * laplace
                grads[particle, mine, :] = result.reshape(BLOCK, LANES).astype(BF16)
            return carry

        lax.fori_loop(0, total // group, step, 0)
        stores.append(pltpu.make_async_copy(grads.at[:, mine, :], out_ref.at[:, mine, :], sems.at[k]))
        stores[-1].start()
    for store in stores:
        store.wait()


def slab_gradient(parts, observed, precision, lines, begin, end):
    total = parts[0].shape[0]
    count = end - begin
    out = jax.ShapeDtypeStruct((total, count, LANES), BF16)
    return call(
        functools.partial(gradient_body, lines, begin, end, len(parts)),
        "slab_gradient",
        flops=30 * out.size,
        moved=8 * out.size,
        in_specs=[IN_VMEM] * (len(parts) + 2),
        out_specs=IN_HBM,
        out_shape=out,
        scratch_shapes=[pltpu.VMEM(out.shape, BF16), pltpu.SemaphoreType.DMA((count // BLOCK,))],
    )(*parts, observed, precision)


def update_body(begin, end, parts, *refs):
    states_refs, refs = refs[:parts], refs[parts:]
    scalars_ref, grams_ref, grads_ref = refs[:3]
    out_ref, grads, mixer, own, sem = refs[-5:]
    total = out_ref.shape[0]
    wide = total * TILE
    fetch = pltpu.make_async_copy(grads_ref, grads, sem)
    fetch.start()
    gram = jnp.sum(grams_ref[...], axis=0)[:, :total]
    row = lax.broadcasted_iota(jnp.int32, (total, total), 0)
    col = lax.broadcasted_iota(jnp.int32, (total, total), 1)
    diagonal = jnp.where(row == col, gram, 0.0)
    down = jnp.sum(diagonal, axis=1, keepdims=True)
    across = jnp.sum(diagonal, axis=0, keepdims=True)
    member = members(total, BF16)
    spread, anneal, step_size = (scalars_ref[k : k + 1, :1] for k in range(3))
    rate = step_size / total
    coeff = 2.0 * anneal / spread
    kernel = jnp.exp(-(down + across - 2.0 * gram) / (spread * NCELL)).astype(BF16)
    ksum = jnp.sum(kernel.astype(F32), axis=1, keepdims=True)
    half = jnp.dot(member, kernel, preferred_element_type=F32).astype(BF16)
    full = lax.dot_general(half, member, (((1,), (1,)), ((), ())), preferred_element_type=F32)
    mixer[...] = jnp.where(same_line(total), full, 0.0).astype(BF16)
    gain = 1.0 + rate * coeff * ksum
    own[...] = jnp.broadcast_to(gain[:, :, None], (total, TILE, LANES)).reshape(wide, LANES)
    fetch.wait()

    done = 0
    for part, states_ref in enumerate(states_refs):
        have = states_ref.shape[1] - (0 if part else TILE)
        low = max(begin - done, 0)
        high = min(end - done, have)
        into = done - begin
        done += have

        def step(i, carry):
            for t in range(BLOCK // TILE):
                at = pl.multiple_of(i * BLOCK + t * TILE, TILE)
                there = pl.ds(pl.multiple_of(at + into, TILE), TILE)
                states = states_ref[:, pl.ds(at, TILE), :].reshape(wide, LANES)
                both = jnp.concatenate([grads[:, there, :].reshape(wide, LANES), states], axis=1)
                mixed = jnp.dot(mixer[...], both, preferred_element_type=F32)
                drive, pulled = mixed[:, :LANES], mixed[:, LANES:]
                new = states.astype(F32) * own[...] + rate * (drive - coeff * pulled)
                out_ref[:, there, :] = new.astype(BF16).reshape(total, TILE, LANES)
            return carry

        lax.fori_loop(low // BLOCK, high // BLOCK, step, 0)


def slab_update(scalars, grams, parts, grads, begin, end, earlier):
    total, count, _ = grads.shape
    wide = total * TILE
    return call(
        functools.partial(update_body, begin, end, len(parts)),
        "slab_update",
        flops=4 * wide * wide * LANES * (count // TILE),
        moved=6 * grads.size,
        in_specs=[IN_VMEM] * len(parts)
        + [IN_VMEM, IN_VMEM, IN_HBM]
        + [IN_HBM] * len(earlier),
        out_specs=IN_VMEM,
        out_shape=jax.ShapeDtypeStruct(grads.shape, BF16),
        scratch_shapes=[
            pltpu.VMEM(grads.shape, BF16),
            pltpu.VMEM((wide, wide), BF16),
            pltpu.VMEM((wide, LANES), F32),
            pltpu.SemaphoreType.DMA,
        ],
    )(*parts, scalars, grams, grads, *earlier)


def plain_update(spread, anneal, step_size, states, grads):
    total, lines, _ = grads.shape
    flat = states[:, :lines].reshape(total, -1)
    gram = lax.dot_general(flat, flat, (((1,), (1,)), ((), ())), preferred_element_type=F32)
    gram = lax.psum(gram, "slab")
    norms = jnp.diagonal(gram)
    kernel = jnp.exp(-(norms[:, None] + norms[None, :] - 2.0 * gram) / (spread[0] * NCELL)).astype(BF16)
    ksum = jnp.sum(kernel.astype(F32), axis=1)
    drive = jnp.dot(kernel, grads.reshape(total, -1), preferred_element_type=F32)
    pulled = jnp.dot(kernel, flat, preferred_element_type=F32)
    values = flat.astype(F32)
    repel = values * ksum[:, None] - pulled
    coeff = 2.0 * anneal[0] / spread[0]
    new = values + step_size[0] / total * (drive + coeff * repel)
    return new.astype(BF16).reshape(grads.shape)


def swap(slabs):
    return lax.all_to_all(slabs, "slab", split_axis=0, concat_axis=0, tiled=True)


def device_at(at, half):
    me = lax.axis_index("slab").astype(jnp.int32)
    return jnp.where(at < half, me - me % half + at, me ^ at)


def lines_of(start, count):
    return pl.ds(pl.multiple_of(start, TILE), count)


def split_pieces_body(slabs, raw, lines, fields, row_ref, *refs):
    half = slabs // 2
    field_refs, near_out, far_outs = refs[:fields], refs[fields], refs[fields + 1 : fields + 1 + half]
    slab_refs, held, sems = refs[fields + 1 + half : -2], refs[-2], refs[-1]
    cells = lines * LANES
    end = row_ref.shape[1]
    me = lax.axis_index("slab").astype(jnp.int32)
    copies = []
    for slab in range(slabs):
        part = pl.ds(slab * cells, cells)
        copies.append(pltpu.make_async_copy(row_ref.at[:, part], held.at[:, part], sems.at[slab]))
    for n, target in enumerate(slab_refs):
        start = (me if n < fields else me ^ half) * lines
        source = field_refs[n % fields].at[lines_of(start, target.shape[0]), :]
        copies.append(pltpu.make_async_copy(source, target, sems.at[slabs + n]))
    for copy in copies:
        copy.start()
    for copy in copies[:slabs]:
        copy.wait()

    def part(start, size):
        return held[:, pl.ds(pl.multiple_of(start, GRID_Y), size)]

    def grid_row(start):
        return part(start, GRID_Y).astype(F32).reshape(LINE, LANES)

    for at in range(slabs):
        out_ref = near_out.at[at] if at < half else far_outs[at - half]
        slab = device_at(at, half)
        start = slab * cells
        out_ref[:lines, :] = part(start, cells).reshape(lines, LANES)
        below = jnp.where(slab == slabs - 1, 0.0, grid_row(jnp.minimum(start + cells, end - GRID_Y)))
        above = jnp.where(slab == 0, 0.0, grid_row(jnp.maximum(start - GRID_Y, 0)))
        out_ref[lines : lines + TILE, :] = jnp.concatenate([below, above], axis=0).astype(BF16)
        if at < half:
            start = (slab ^ half) * cells
            to = lines + TILE
            out_ref[to : to + raw, :] = part(start, raw * LANES).reshape(raw, LANES)
            below = grid_row(start + raw * LANES)
            above = jnp.where(slab ^ half == 0, 0.0, grid_row(jnp.maximum(start - GRID_Y, 0)))
            out_ref[to + raw :, :] = jnp.concatenate([below, above], axis=0).astype(BF16)
    for copy in copies[slabs:]:
        copy.wait()


def split_pieces(row, slabs, raw, fields):
    lines = row.shape[1] // slabs // LANES
    half = slabs // 2
    rim = lines + TILE
    size = rim + raw + TILE
    out_shape = [jax.ShapeDtypeStruct((half, size, LANES), BF16)]
    out_shape += [jax.ShapeDtypeStruct((rim, LANES), BF16)] * half
    out_shape += [jax.ShapeDtypeStruct((lines, LANES), BF16)] * len(fields)
    out_shape += [jax.ShapeDtypeStruct((raw, LANES), BF16)] * len(fields)
    return call(
        functools.partial(split_pieces_body, slabs, raw, lines, len(fields)),
        "split_pieces",
        moved=6 * half * (rim + size) * LANES,
        in_specs=[IN_HBM] * (1 + len(fields)),
        out_specs=[IN_VMEM] * len(out_shape),
        out_shape=out_shape,
        scratch_shapes=[pltpu.VMEM(row.shape, BF16), pltpu.SemaphoreType.DMA((slabs + 2 * len(fields),))],
    )(row, *fields)


def join_pieces_body(pieces, half, raw, lines, begun, arrays, *refs):
    row_ref, helds, sems = refs[begun + arrays], refs[begun + arrays + 1 : -1], refs[-1]
    cells = lines * LANES
    skip = raw * LANES
    copies = []
    for (array, lead, at), held in zip(pieces, helds):
        ref = refs[begun + array]
        piece = ref[...] if lead is None else ref[lead]
        held[...] = piece.reshape(held.shape)
        slab = device_at(at, half)
        if at < half:
            parts = [(0, cells, slab * cells), (cells, skip, (slab ^ half) * cells)]
        else:
            parts = [(0, cells - skip, slab * cells + skip)]
        for begin, size, start in parts:
            target = row_ref.at[:, pl.ds(pl.multiple_of(start, GRID_Y), size)]
            copies.append(pltpu.make_async_copy(held.at[:, pl.ds(begin, size)], target, sems.at[len(copies)]))
            copies[-1].start()
    for copy in copies:
        copy.wait()


def join_pieces(row, slabs, raw, arrays, pieces):
    sizes = [arrays[piece[0]].shape[-2] * LANES for piece in pieces]
    begun = [] if row is None else [row]
    return call(
        functools.partial(
            join_pieces_body, pieces, slabs // 2, raw, NCELL // slabs // LANES, len(begun), len(arrays)
        ),
        "join_pieces",
        moved=6 * sum(sizes),
        in_specs=[IN_HBM] * len(begun) + [IN_VMEM] * len(arrays),
        out_specs=IN_HBM,
        out_shape=jax.ShapeDtypeStruct((1, NCELL), BF16),
        input_output_aliases={0: 0} if begun else {},
        scratch_shapes=[pltpu.VMEM((1, size), BF16) for size in sizes]
        + [pltpu.SemaphoreType.DMA((2 * len(sizes),))],
    )(*begun, *arrays)


def owners(total, dtype):
    wide = total * TILE
    row = lax.broadcasted_iota(jnp.int32, (wide, total), 0)
    col = lax.broadcasted_iota(jnp.int32, (wide, total), 1)
    return (device_at(row // TILE, total // 2) == col).astype(dtype)


def gram_pieces_body(lines, total, near_ref, *refs):
    half = total // 2
    pieces, out_ref, pairs = refs[:half], refs[-2], refs[-1]
    wide = total * TILE
    tiles = 8
    pairs[...] = jnp.zeros_like(pairs)

    def step(i, carry):
        parts = []
        for t in range(tiles):
            at = lines_of((i * tiles + t) * TILE, TILE)
            near = near_ref[:, at, :].reshape(wide // 2, LANES)
            parts.append(jnp.concatenate([near] + [piece[at, :] for piece in pieces], axis=0))
        block = jnp.concatenate(parts, axis=1)
        pairs[...] += lax.dot_general(block, block, (((1,), (1,)), ((), ())), preferred_element_type=F32)
        return carry

    lax.fori_loop(0, lines // TILE // tiles, step, 0)
    equal = jnp.where(same_line(total), pairs[...], 0.0)
    exact = {"precision": lax.Precision.HIGHEST, "preferred_element_type": F32}
    rows = jnp.sum(equal.reshape(total, TILE, wide), axis=1)
    gram = jnp.dot(rows, owners(total, F32), **exact)
    row = lax.broadcasted_iota(jnp.int32, (total, total), 0)
    col = lax.broadcasted_iota(jnp.int32, (total, total), 1)
    gram = jnp.dot((row == device_at(col, half)).astype(F32), gram, **exact)
    gram = jnp.concatenate([gram, jnp.zeros((total, LANES - total), F32)], axis=1)
    out_ref[...] = jnp.broadcast_to(gram[None], out_ref.shape)


def gram_pieces(near, far, lines, gates, early):
    total = 2 * len(far)
    wide = total * TILE
    return call(
        functools.partial(gram_pieces_body, lines, total),
        "gram_pieces",
        flops=2 * wide * wide * LANES * (lines // TILE),
        moved=2 * total * lines * LANES,
        in_specs=[IN_VMEM] * (1 + len(far)) + [IN_HBM] * len(gates) + [IN_VMEM] * len(early),
        out_specs=IN_VMEM,
        out_shape=jax.ShapeDtypeStruct((total, total, LANES), F32),
        scratch_shapes=[pltpu.VMEM((wide, wide), F32)],
    )(near, *far, *gates, *early)


def block_gradient(load, i, count, observed, precision):
    start = i * BLOCK
    at = lines_of(start, BLOCK)
    shape = (BLOCK // LINE, LINE, LANES)
    lane = lax.broadcasted_iota(jnp.int32, (1, LINE, LANES), 2)
    line = lax.broadcasted_iota(jnp.int32, (1, LINE, LANES), 1)
    obs = observed[at, :].astype(F32).reshape(shape)
    prec = precision[at, :].astype(F32).reshape(shape)
    here = load(start, BLOCK).astype(F32)
    before = load(jnp.where(i == 0, count, start - TILE), TILE).astype(F32)
    after = load(start + BLOCK, TILE).astype(F32)
    above = jnp.concatenate([before[LINE:], here[:-LINE]], axis=0).reshape(shape)
    below = jnp.concatenate([here[LINE:], after[:LINE]], axis=0).reshape(shape)
    field = here.reshape(shape)
    turned = pltpu.roll(field, 1, 2)
    carried = jnp.where(line == 0, 0.0, pltpu.roll(turned, 1, 1))
    left = jnp.where(lane == 0, carried, turned)
    turned = pltpu.roll(field, LANES - 1, 2)
    carried = jnp.where(line == LINE - 1, 0.0, pltpu.roll(turned, LINE - 1, 1))
    right = jnp.where(lane == LANES - 1, carried, turned)
    laplace = (4.0 + mass_term) * field - (below + above + right + left)
    squash = jnp.tanh(field)
    result = prec * (obs - squash) * (1.0 - squash * squash) - prior_scale * laplace
    return result.reshape(BLOCK, LANES).astype(BF16)


def gradient_pieces_body(views, arrays, numbers, *refs):
    observed, precision, *number_refs = refs[arrays : arrays + 2 + numbers]
    out_ref, rows_ref, grads, sems = refs[-4:]
    for n, number_ref in enumerate(number_refs):
        rows_ref[n : n + 1, :] = jnp.full((1, LANES), number_ref[0], F32)
    count = observed.shape[0]
    steps = count // BLOCK

    def store(i):
        at = lines_of(i * BLOCK, BLOCK)
        return pltpu.make_async_copy(grads.at[:, at, :], out_ref.at[:, at, :], sems.at[i])

    def step(i, carry):
        for p, (array, lead, base) in enumerate(views):

            def load(start, size):
                part = lines_of(base + start, size)
                return refs[array][part, :] if lead is None else refs[array][lead, part, :]

            grads[p, lines_of(i * BLOCK, BLOCK), :] = block_gradient(load, i, count, observed, precision)
        store(i).start()
        return carry

    def finish(i, carry):
        store(i).wait()
        return carry

    lax.fori_loop(0, steps, step, 0)
    lax.fori_loop(0, steps, finish, 0)


def gradient_pieces(arrays, views, observed, precision, numbers):
    count = observed.shape[0]
    out = pltpu.HBM((len(views), count, LANES), BF16)
    size = len(views) * count * LANES
    return call(
        functools.partial(gradient_pieces_body, views, len(arrays), len(numbers)),
        "gradient_pieces",
        flops=30 * size,
        moved=8 * size,
        in_specs=[IN_VMEM] * (len(arrays) + 2)
        + [pl.BlockSpec(memory_space=pltpu.SMEM)] * len(numbers),
        out_specs=[IN_HBM, IN_VMEM],
        out_shape=[out, jax.ShapeDtypeStruct((8, LANES), F32)],
        scratch_shapes=[pltpu.VMEM(out.shape, BF16), pltpu.SemaphoreType.DMA((count // BLOCK,))],
    )(*arrays, observed, precision, *numbers)


def raw_body(raw, lines, near_ref, *refs):
    out_ref = refs[-1]
    for k in range(near_ref.shape[0]):
        out_ref[k, :raw, :] = near_ref[k, :raw, :]
        below = near_ref[k, raw : raw + TILE, :].astype(F32)[:LINE]
        above = near_ref[k, lines : lines + TILE, :].astype(F32)[LINE:]
        out_ref[k, raw:, :] = jnp.concatenate([below, above], axis=0).astype(BF16)


def raw_states(near, raw, lines, gates):
    out = jax.ShapeDtypeStruct((near.shape[0], raw + TILE, LANES), BF16)
    return call(
        functools.partial(raw_body, raw, lines),
        "raw_states",
        moved=4 * out.size,
        in_specs=[IN_VMEM] * (1 + len(gates)),
        out_specs=IN_VMEM,
        out_shape=out,
    )(near, *gates)


def mix(mixer, own, numbers_ref, total, states, slopes):
    high = mixer.shape[0]
    rate = numbers_ref[2:3, :1] / total
    coeff = 2.0 * numbers_ref[1:2, :1] / numbers_ref[:1, :1]
    both = jnp.concatenate([slopes, states], axis=1)
    mixed = jnp.dot(mixer[...], both, preferred_element_type=F32)
    drive, pulled = mixed[:, :LANES], mixed[:, LANES:]
    return (states[:high].astype(F32) * own[...] + rate * (drive - coeff * pulled)).astype(BF16)


def update_pieces_body(half, raw, lines, groups, near_ref, *refs):
    total = 2 * half
    far_refs, refs = refs[:half], refs[half:]
    across_ref, numbers_ref, grams_ref, raw_grads_ref, *refs = refs
    group_refs, near_to, far_tos = refs[: len(groups)], refs[len(groups)], refs[len(groups) + 1 : -8]
    near_out, far_out, mixer, own, grads, raw_grads, sems, out_sems = refs[-8:]
    wide = total * TILE
    high = half * TILE
    fetches = []
    for group, group_ref in zip(groups, group_refs):
        for j, at in enumerate(group):
            fetches.append(pltpu.make_async_copy(group_ref.at[j], grads.at[at], sems.at[len(fetches)]))
    fetches.append(pltpu.make_async_copy(raw_grads_ref, raw_grads, sems.at[total]))
    for fetch in fetches:
        fetch.start()
    gram = jnp.sum(grams_ref[...], axis=0)[:, :total]
    spread, anneal, step_size = (numbers_ref[k : k + 1, :1] for k in range(3))
    rate = step_size / total
    coeff = 2.0 * anneal / spread
    row = lax.broadcasted_iota(jnp.int32, (total, total), 0)
    col = lax.broadcasted_iota(jnp.int32, (total, total), 1)
    diagonal = jnp.where(row == col, gram, 0.0)
    down = jnp.sum(diagonal, axis=1, keepdims=True)
    across = jnp.sum(diagonal, axis=0, keepdims=True)
    kernel = jnp.exp(-(down + across - 2.0 * gram) / (spread * NCELL)).astype(BF16)
    owner = owners(total, BF16)
    half_way = jnp.dot(owner, kernel, preferred_element_type=F32).astype(BF16)
    full = lax.dot_general(half_way, owner, (((1,), (1,)), ((), ())), preferred_element_type=F32)
    full = jnp.where(same_line(total), full, 0.0)
    mixer[...] = full.astype(BF16)
    ksum = jnp.sum(full, axis=1, keepdims=True)
    own[...] = jnp.broadcast_to(1.0 + rate * coeff * ksum, (wide, LANES))
    for fetch in fetches:
        fetch.wait()

    stores = []

    def store(source, target, at):
        stores.append(pltpu.make_async_copy(source, target, out_sems.at[at]))
        stores[-1].start()

    def store_near(first, last, at):
        part = pl.ds(first, last - first)
        store(near_out.at[:, part, :], near_to.at[:, part, :], (half, at))

    def store_far(first, last, at):
        part = pl.ds(first - raw, last - first)
        for x, far_to in enumerate(far_tos):
            store(far_out.at[x, part, :], far_to.at[part, :], (x, at))

    def slab_step(with_far, i, carry):
        rows = wide if with_far else high
        for t in range(BLOCK // TILE):
            at = i * BLOCK + t * TILE
            part = lines_of(at, TILE)
            states = [near_ref[:, part, :].reshape(high, LANES)] + [ref[part, :] for ref in far_refs]
            slopes = grads[:, part, :].reshape(wide, LANES)
            states = jnp.concatenate(states, axis=0)
            new = mix(mixer.at[:rows, :], own.at[:rows, :], numbers_ref, total, states, slopes)
            near_out[:, part, :] = new[:high].reshape(half, TILE, LANES)
            if with_far:
                far_out[:, lines_of(at - raw, TILE), :] = new[high:].reshape(half, TILE, LANES)
        return carry

    here = lax.axis_index("slab").astype(jnp.int32) % half

    def raw_step(i, carry):
        for t in range(BLOCK // TILE):
            at = i * BLOCK + t * TILE
            part = lines_of(at, TILE)
            states = [near_ref[:, lines_of(lines + TILE + at, TILE), :].reshape(high, LANES)]
            slopes = [raw_grads[:half, part, :].reshape(high, LANES)]
            for x in range(half):
                states += [across_ref[here ^ x, part, :]]
                slopes += [raw_grads[half + (here ^ x), part, :]]
            states, slopes = jnp.concatenate(states, axis=0), jnp.concatenate(slopes, axis=0)
            new = mix(mixer.at[:high, :], own.at[:high, :], numbers_ref, total, states, slopes)
            near_out[:, lines_of(lines + at, TILE), :] = new.reshape(half, TILE, LANES)
        return carry

    lax.fori_loop(0, raw // BLOCK, raw_step, 0)
    store_near(lines, lines + raw, 0)
    lax.fori_loop(0, raw // BLOCK, functools.partial(slab_step, False), 0)
    middle = (raw + 2 * lines) // 3 // BLOCK * BLOCK
    lax.fori_loop(raw // BLOCK, middle // BLOCK, functools.partial(slab_step, True), 0)
    store_near(0, middle, 1)
    store_far(raw, middle, 0)
    lax.fori_loop(middle // BLOCK, lines // BLOCK, functools.partial(slab_step, True), 0)
    store_near(middle, lines, 2)
    store_far(middle, lines, 1)
    for copy in stores:
        copy.wait()


def update_pieces(numbers, grams, near, far, across, raw_grads, grads, groups, raw, lines):
    half = len(far)
    total = 2 * half
    wide = total * TILE
    out_shape = [pltpu.HBM((half, lines + raw, LANES), BF16)]
    out_shape += [pltpu.HBM((lines - raw, LANES), BF16)] * half
    return call(
        functools.partial(update_pieces_body, half, raw, lines, groups),
        "update_pieces",
        flops=4 * wide * wide * LANES * (lines // TILE),
        moved=6 * total * lines * LANES,
        in_specs=[IN_VMEM] * (half + 4) + [IN_HBM] * (1 + len(groups)),
        out_specs=[IN_HBM] * len(out_shape),
        out_shape=out_shape,
        scratch_shapes=[
            pltpu.VMEM((half, lines + raw, LANES), BF16),
            pltpu.VMEM((half, lines - raw, LANES), BF16),
            pltpu.VMEM((wide, wide), BF16),
            pltpu.VMEM((wide, LANES), F32),
            pltpu.VMEM((total, lines, LANES), BF16),
            pltpu.VMEM((total, raw, LANES), BF16),
            pltpu.SemaphoreType.DMA((total + 1,)),
            pltpu.SemaphoreType.DMA((half + 1, 3)),
        ],
    )(near, *far, across, numbers, grams, raw_grads, *grads)


def exchange(piece, k, slabs):
    return lax.ppermute(piece, "slab", [(i, i ^ k) for i in range(slabs)])


def swap_near(pieces, slabs):
    groups = [list(range(slabs // 2)), list(range(slabs // 2, slabs))]
    return lax.all_to_all(pieces, "slab", 0, 0, axis_index_groups=groups, tiled=True)


RAW = 128
GRADIENTS = ((8, 9, 10, 11), (12, 13, 14, 15), (0, 1, 2, 3, 4, 5, 6, 7))


def by_halves(particles, observed, precision, spread, anneal, step_size):
    slabs = lax.axis_size("slab")
    half = slabs // 2
    lines = NCELL // slabs // LANES
    row = in_hbm(particles)
    fields = [in_hbm(field.reshape(-1, LANES)) for field in (observed, precision)]
    near, *far = split_pieces(row, slabs, RAW, fields)
    far, (obs, prec, *raw_fields) = far[:half], far[half:]
    near = swap_near(near, slabs)
    far = [exchange(piece, half + x, slabs) for x, piece in enumerate(far)]
    raw_near = raw_states(near, RAW, lines, far)
    across = exchange(raw_near, half, slabs)
    grads = []
    numbers = [spread, anneal, step_size]
    for group in GRADIENTS:
        if group[0] < half:
            arrays, views = [near], [(0, k, 0) for k in group]
        else:
            arrays, views = [far[k - half] for k in group], [(j, None, 0) for j in range(len(group))]
        slopes, rows = gradient_pieces(arrays, tuple(views), obs, prec, [] if grads else numbers)
        grads.append(in_hbm(slopes))
        numbers = numbers if len(grads) > 1 else rows
    grams = swap(gram_pieces(near, far, lines, grads[:1], [raw_near]))
    views = [(0, k, lines + TILE) for k in range(half)] + [(1, k, 0) for k in range(half)]
    raw_grads, _ = gradient_pieces([near, across], tuple(views), *raw_fields, [])
    new_near, *new_far = update_pieces(
        numbers, grams, near, far, across, in_hbm(raw_grads), grads, GRADIENTS, RAW, lines
    )
    new_near = swap_near(new_near, slabs)
    new_far = [exchange(piece, half + x, slabs) for x, piece in enumerate(new_far)]
    row = join_pieces(None, slabs, RAW, [new_near], [(0, k, k) for k in range(half)])
    for group in ((0, 1, 2, 3), (4, 5)):
        pieces = [(n, None, half + x) for n, x in enumerate(group)]
        row = join_pieces(row, slabs, RAW, [new_far[x] for x in group], pieces)
    return join_pieces(row, slabs, RAW, new_far[6:], [(n, None, half + 6 + n) for n in range(half - 6)])


def on_device(particles, observed, precision, spread, anneal, step_size):
    slabs = lax.axis_size("slab")
    total = particles.shape[0] * slabs
    lines = NCELL // slabs // LANES
    if slabs == 16:
        return by_halves(particles, observed, precision, spread, anneal, step_size)
    sent, begun = cuts(lines)
    fields = [observed.reshape(-1, LANES), precision.reshape(-1, LANES)]
    numbers = [spread, anneal, step_size]
    first, obs, prec, scalars = split_row(particles, slabs, 0, sent, True, fields, numbers, [])
    parts = [swap(first)]
    if sent < lines:
        parts += [swap(split_row(particles, slabs, sent, lines, False, [], [], [scalars])[0])]
    if total * TILE > 256:
        grads = slab_gradient(parts, obs, prec, lines, 0, lines)
        states = jnp.concatenate([parts[0][:, :sent]] + parts[1:], axis=1)
        new = plain_update(spread, anneal, step_size, states, grads)
        return join_row(swap(new), lines, 0, None)
    if sent == lines:
        grads = slab_gradient(parts, obs, prec, lines, 0, lines)
        grams = swap(slab_gram(parts[0], lines, slabs, [], []))
        new = slab_update(scalars, grams, parts, grads, 0, lines, [])
        return join_row(swap(new), lines, 0, None)
    gram = slab_gram(parts[0], sent, 1, [], [])
    early = slab_gradient(parts[:1], obs, prec, lines, 0, begun)
    grams = swap(slab_gram(parts[1], lines - sent, slabs, [gram], [early]))
    late = slab_gradient(parts, obs, prec, lines, begun, lines)
    new = slab_update(scalars, grams, parts[:1], early, 0, begun, [])
    rest = slab_update(scalars, grams, parts, late, begun, lines, [new])
    row = join_row(swap(new), lines, 0, None)
    return join_row(swap(rest), lines, begun, row)


def solution(mesh):
    in_specs = (
        P(("groups", "slab"), None),
        P("groups"),
        P("groups"),
        P("groups"),
        P("groups"),
        P("groups"),
    )
    out_specs = P(("groups", "slab"), None)
    return jax.shard_map(
        on_device, mesh=mesh, in_specs=in_specs, out_specs=out_specs, check_vma=False
    )
```

```python
import functools

import jax
import jax.numpy as jnp
from jax import lax
from jax.experimental import pallas as pl
from jax.experimental.pallas import tpu as pltpu
from jax.sharding import PartitionSpec as P

GRID_X = 1024
GRID_Y = 1024
NCELL = 1048576
LANES = 128
LINE = GRID_Y // LANES
TILE = 16

prior_scale = 0.25
mass_term = 1.0

F32 = jnp.float32
BF16 = jnp.bfloat16
MIB = 1024 * 1024


def call(body, name, flops=0, moved=0, limit=16, **kwargs):
    return pl.pallas_call(
        body,
        name=name,
        compiler_params=pltpu.CompilerParams(vmem_limit_bytes=limit * MIB),
        cost_estimate=pl.CostEstimate(flops=flops, bytes_accessed=moved, transcendentals=0),
        **kwargs,
    )


IN_VMEM = pl.BlockSpec(memory_space=pltpu.VMEM)
IN_HBM = pl.BlockSpec(memory_space=pltpu.HBM)


def in_hbm(array):
    return pltpu.with_memory_space_constraint(array, pltpu.HBM)


BLOCK = 4 * TILE


def cuts(lines):
    if lines % (8 * BLOCK):
        return lines, lines
    return lines * 3 // 4, lines * 3 // 4 - BLOCK


def split_body(lines, begin, rim, fields, numbers, row_ref, *refs):
    field_refs, number_refs = refs[:fields], refs[fields : fields + numbers]
    out_ref, *slab_refs, rows_ref = refs[-7 - fields : -5]
    held, edges, sems, edge_sems, field_sems = refs[-5:]
    for k, number_ref in enumerate(number_refs):
        rows_ref[k : k + 1, :] = jnp.broadcast_to(number_ref[...].reshape(1, 1), (1, LANES))
    slabs, count, _ = out_ref.shape
    count -= TILE * rim
    size = count * LANES
    cells = lines * LANES

    def part(slab):
        source = row_ref.at[:, pl.ds(slab * cells + begin * LANES, size)]
        return pltpu.make_async_copy(source, held.at[:, pl.ds(slab * size, size)], sems.at[slab])

    def edge(slab):
        source = row_ref.at[:, pl.ds(slab * cells - GRID_Y, GRID_Y)]
        return pltpu.make_async_copy(source, edges.at[:, pl.ds(slab * GRID_Y, GRID_Y)], edge_sems.at[slab])

    def grid_row(ref, start):
        return ref[:, pl.ds(start, GRID_Y)].astype(F32).reshape(LINE, LANES)

    for slab in range(slabs):
        part(slab).start()
        if rim and slab:
            edge(slab).start()
    mine = pl.ds(pl.multiple_of(lax.axis_index("slab") * lines, TILE), lines)
    fetches = [
        pltpu.make_async_copy(source.at[mine, :], target, field_sems.at[k])
        for k, (source, target) in enumerate(zip(field_refs, slab_refs))
    ]
    for fetch in fetches:
        fetch.start()
    part(0).wait()
    outside = jnp.zeros((LINE, LANES), F32)
    for slab in range(slabs):
        if slab + 1 < slabs:
            part(slab + 1).wait()
        out_ref[slab, :count, :] = held[:, pl.ds(slab * size, size)].reshape(count, LANES)
        if rim:
            if slab:
                edge(slab).wait()
            below = grid_row(held, (slab + 1) * size) if slab + 1 < slabs else outside
            above = grid_row(edges, slab * GRID_Y) if slab else outside
            out_ref[slab, count:, :] = jnp.concatenate([below, above], axis=0).astype(BF16)
    for fetch in fetches:
        fetch.wait()


def split_row(row, slabs, begin, end, rim, fields, numbers, earlier):
    lines = row.shape[1] // slabs // LANES
    count = end - begin
    return call(
        functools.partial(split_body, lines, begin, rim, len(fields), len(numbers)),
        "split_row",
        moved=6 * slabs * count * LANES,
        in_specs=[IN_HBM] * (1 + len(fields)) + [IN_VMEM] * len(numbers) + [IN_HBM] * len(earlier),
        out_specs=[IN_VMEM] * (2 + len(fields)),
        out_shape=[jax.ShapeDtypeStruct((slabs, count + TILE * rim, LANES), BF16)]
        + [jax.ShapeDtypeStruct((lines, LANES), BF16)] * len(fields)
        + [jax.ShapeDtypeStruct((8, LANES), F32)],
        scratch_shapes=[
            pltpu.VMEM((1, slabs * count * LANES), BF16),
            pltpu.VMEM((1, slabs * GRID_Y), BF16),
            pltpu.SemaphoreType.DMA((slabs,)),
            pltpu.SemaphoreType.DMA((slabs,)),
            pltpu.SemaphoreType.DMA((2,)),
        ],
    )(row, *fields, *numbers, *earlier)


def join_body(lines, begin, slabs_ref, *refs):
    row_ref, held, sems = refs[-3:]
    slabs, count, _ = slabs_ref.shape
    size = count * LANES
    copies = []
    for slab in range(slabs):
        at = pl.ds(slab * size, size)
        held[:, at] = slabs_ref[slab].reshape(1, size)
        target = row_ref.at[:, pl.ds((slab * lines + begin) * LANES, size)]
        copies.append(pltpu.make_async_copy(held.at[:, at], target, sems.at[slab]))
        copies[-1].start()
    for copy in copies:
        copy.wait()


def join_row(slabs, lines, begin, row):
    total, count, _ = slabs.shape
    begun = [] if row is None else [row]
    return call(
        functools.partial(join_body, lines, begin),
        "join_row",
        moved=6 * slabs.size,
        in_specs=[IN_VMEM] + [IN_HBM] * len(begun),
        out_specs=IN_HBM,
        out_shape=jax.ShapeDtypeStruct((1, total * lines * LANES), BF16),
        input_output_aliases={1: 0} if begun else {},
        scratch_shapes=[pltpu.VMEM((1, slabs.size), BF16), pltpu.SemaphoreType.DMA((total,))],
    )(slabs, *begun)


def same_line(total):
    wide = total * TILE
    row = lax.broadcasted_iota(jnp.int32, (wide, wide), 0)
    col = lax.broadcasted_iota(jnp.int32, (wide, wide), 1)
    return row % TILE == col % TILE


def members(total, dtype):
    wide = total * TILE
    row = lax.broadcasted_iota(jnp.int32, (wide, total), 0)
    col = lax.broadcasted_iota(jnp.int32, (wide, total), 1)
    return (row // TILE == col).astype(dtype)


def gram_body(steps, tiles, parts, states_ref, *refs):
    out_ref, pairs = refs[-2:]
    total = states_ref.shape[0]
    wide = total * TILE
    pairs[...] = jnp.zeros_like(pairs)

    def step(i, carry):
        parts = [
            states_ref[:, pl.ds(pl.multiple_of((i * tiles + t) * TILE, TILE), TILE), :].reshape(wide, LANES)
            for t in range(tiles)
        ]
        block = jnp.concatenate(parts, axis=1)
        pairs[...] += lax.dot_general(block, block, (((1,), (1,)), ((), ())), preferred_element_type=F32)
        return carry

    lax.fori_loop(0, steps, step, 0)
    equal = jnp.where(same_line(total), pairs[...], 0.0)
    rows = jnp.sum(equal.reshape(total, TILE, wide), axis=1)
    gram = jnp.dot(rows, members(total, F32), precision=lax.Precision.HIGHEST, preferred_element_type=F32)
    gram = jnp.concatenate([gram, jnp.zeros((total, LANES - total), F32)], axis=1)
    for part_ref in refs[:parts]:
        gram += part_ref[0]
    out_ref[...] = jnp.broadcast_to(gram[None], out_ref.shape)


def slab_gram(states, lines, copies, parts, earlier):
    total = states.shape[0]
    wide = total * TILE
    tiles = min(8, lines // TILE)
    return call(
        functools.partial(gram_body, lines // TILE // tiles, tiles, len(parts)),
        "slab_gram",
        flops=2 * wide * wide * LANES * (lines // TILE),
        moved=2 * states.size,
        in_specs=[IN_VMEM] * (1 + len(parts)) + [IN_HBM] * len(earlier),
        out_specs=IN_VMEM,
        out_shape=jax.ShapeDtypeStruct((copies, total, LANES), F32),
        scratch_shapes=[pltpu.VMEM((wide, wide), F32)],
    )(states, *parts, *earlier)


def gradient_body(lines, begin, end, parts, *refs):
    observed, precision, out_ref, grads, sems = refs[parts:]
    total = grads.shape[0]
    first = refs[0].shape[1] - TILE
    rows = BLOCK // LINE
    group = 4
    shape = (rows, LINE, LANES)
    lane = lax.broadcasted_iota(jnp.int32, (1, LINE, LANES), 2)
    line = lax.broadcasted_iota(jnp.int32, (1, LINE, LANES), 1)

    def load(particle, at, count):
        ref, at = (refs[0], at) if at < first else (refs[1], at - first)
        return ref[particle, at : at + count, :].astype(F32)

    def rim(particle):
        return refs[0][particle, first:, :].astype(F32)

    stores = []
    for k, at in enumerate(range(begin, end, BLOCK)):
        mine = slice(at - begin, at - begin + BLOCK)
        obs = observed[at : at + BLOCK, :].astype(F32).reshape(shape)
        prec = precision[at : at + BLOCK, :].astype(F32).reshape(shape)

        def step(i, carry):
            for p in range(group):
                particle = i * group + p
                here = load(particle, at, BLOCK)
                before = load(particle, at - TILE, TILE) if at else rim(particle)
                after = load(particle, at + BLOCK, TILE) if at + BLOCK < lines else rim(particle)
                above = jnp.concatenate([before[LINE:], here[:-LINE]], axis=0).reshape(shape)
                below = jnp.concatenate([here[LINE:], after[:LINE]], axis=0).reshape(shape)
                field = here.reshape(shape)
                turned = pltpu.roll(field, 1, 2)
                carried = jnp.where(line == 0, 0.0, pltpu.roll(turned, 1, 1))
                left = jnp.where(lane == 0, carried, turned)
                turned = pltpu.roll(field, LANES - 1, 2)
                carried = jnp.where(line == LINE - 1, 0.0, pltpu.roll(turned, LINE - 1, 1))
                right = jnp.where(lane == LANES - 1, carried, turned)
                laplace = (4.0 + mass_term) * field - (below + above + right + left)
                squash = jnp.tanh(field)
                result = prec * (obs - squash) * (1.0 - squash * squash) - prior_scale * laplace
                grads[particle, mine, :] = result.reshape(BLOCK, LANES).astype(BF16)
            return carry

        lax.fori_loop(0, total // group, step, 0)
        stores.append(pltpu.make_async_copy(grads.at[:, mine, :], out_ref.at[:, mine, :], sems.at[k]))
        stores[-1].start()
    for store in stores:
        store.wait()


def slab_gradient(parts, observed, precision, lines, begin, end):
    total = parts[0].shape[0]
    count = end - begin
    out = jax.ShapeDtypeStruct((total, count, LANES), BF16)
    return call(
        functools.partial(gradient_body, lines, begin, end, len(parts)),
        "slab_gradient",
        flops=30 * out.size,
        moved=8 * out.size,
        in_specs=[IN_VMEM] * (len(parts) + 2),
        out_specs=IN_HBM,
        out_shape=out,
        scratch_shapes=[pltpu.VMEM(out.shape, BF16), pltpu.SemaphoreType.DMA((count // BLOCK,))],
    )(*parts, observed, precision)


def update_body(begin, end, parts, *refs):
    states_refs, refs = refs[:parts], refs[parts:]
    scalars_ref, grams_ref, grads_ref = refs[:3]
    out_ref, grads, mixer, own, sem = refs[-5:]
    total = out_ref.shape[0]
    wide = total * TILE
    fetch = pltpu.make_async_copy(grads_ref, grads, sem)
    fetch.start()
    gram = jnp.sum(grams_ref[...], axis=0)[:, :total]
    row = lax.broadcasted_iota(jnp.int32, (total, total), 0)
    col = lax.broadcasted_iota(jnp.int32, (total, total), 1)
    diagonal = jnp.where(row == col, gram, 0.0)
    down = jnp.sum(diagonal, axis=1, keepdims=True)
    across = jnp.sum(diagonal, axis=0, keepdims=True)
    member = members(total, BF16)
    spread, anneal, step_size = (scalars_ref[k : k + 1, :1] for k in range(3))
    rate = step_size / total
    coeff = 2.0 * anneal / spread
    kernel = jnp.exp(-(down + across - 2.0 * gram) / (spread * NCELL)).astype(BF16)
    ksum = jnp.sum(kernel.astype(F32), axis=1, keepdims=True)
    half = jnp.dot(member, kernel, preferred_element_type=F32).astype(BF16)
    full = lax.dot_general(half, member, (((1,), (1,)), ((), ())), preferred_element_type=F32)
    mixer[...] = jnp.where(same_line(total), full, 0.0).astype(BF16)
    gain = 1.0 + rate * coeff * ksum
    own[...] = jnp.broadcast_to(gain[:, :, None], (total, TILE, LANES)).reshape(wide, LANES)
    fetch.wait()

    done = 0
    for part, states_ref in enumerate(states_refs):
        have = states_ref.shape[1] - (0 if part else TILE)
        low = max(begin - done, 0)
        high = min(end - done, have)
        into = done - begin
        done += have

        def step(i, carry):
            for t in range(BLOCK // TILE):
                at = pl.multiple_of(i * BLOCK + t * TILE, TILE)
                there = pl.ds(pl.multiple_of(at + into, TILE), TILE)
                states = states_ref[:, pl.ds(at, TILE), :].reshape(wide, LANES)
                both = jnp.concatenate([grads[:, there, :].reshape(wide, LANES), states], axis=1)
                mixed = jnp.dot(mixer[...], both, preferred_element_type=F32)
                drive, pulled = mixed[:, :LANES], mixed[:, LANES:]
                new = states.astype(F32) * own[...] + rate * (drive - coeff * pulled)
                out_ref[:, there, :] = new.astype(BF16).reshape(total, TILE, LANES)
            return carry

        lax.fori_loop(low // BLOCK, high // BLOCK, step, 0)


def slab_update(scalars, grams, parts, grads, begin, end, earlier):
    total, count, _ = grads.shape
    wide = total * TILE
    return call(
        functools.partial(update_body, begin, end, len(parts)),
        "slab_update",
        flops=4 * wide * wide * LANES * (count // TILE),
        moved=6 * grads.size,
        in_specs=[IN_VMEM] * len(parts)
        + [IN_VMEM, IN_VMEM, IN_HBM]
        + [IN_HBM] * len(earlier),
        out_specs=IN_VMEM,
        out_shape=jax.ShapeDtypeStruct(grads.shape, BF16),
        scratch_shapes=[
            pltpu.VMEM(grads.shape, BF16),
            pltpu.VMEM((wide, wide), BF16),
            pltpu.VMEM((wide, LANES), F32),
            pltpu.SemaphoreType.DMA,
        ],
    )(*parts, scalars, grams, grads, *earlier)


def plain_update(spread, anneal, step_size, states, grads):
    total, lines, _ = grads.shape
    flat = states[:, :lines].reshape(total, -1)
    gram = lax.dot_general(flat, flat, (((1,), (1,)), ((), ())), preferred_element_type=F32)
    gram = lax.psum(gram, "slab")
    norms = jnp.diagonal(gram)
    kernel = jnp.exp(-(norms[:, None] + norms[None, :] - 2.0 * gram) / (spread[0] * NCELL)).astype(BF16)
    ksum = jnp.sum(kernel.astype(F32), axis=1)
    drive = jnp.dot(kernel, grads.reshape(total, -1), preferred_element_type=F32)
    pulled = jnp.dot(kernel, flat, preferred_element_type=F32)
    values = flat.astype(F32)
    repel = values * ksum[:, None] - pulled
    coeff = 2.0 * anneal[0] / spread[0]
    new = values + step_size[0] / total * (drive + coeff * repel)
    return new.astype(BF16).reshape(grads.shape)


def swap(slabs):
    return lax.all_to_all(slabs, "slab", split_axis=0, concat_axis=0, tiled=True)


def device_at(at, half):
    me = lax.axis_index("slab").astype(jnp.int32)
    return jnp.where(at < half, me - me % half + at, me ^ at)


def lines_of(start, count):
    return pl.ds(pl.multiple_of(start, TILE), count)


def split_pieces_body(slabs, raw, lines, fields, row_ref, *refs):
    half = slabs // 2
    field_refs, near_out, far_outs = refs[:fields], refs[fields], refs[fields + 1 : fields + 1 + half]
    slab_refs, held, sems = refs[fields + 1 + half : -2], refs[-2], refs[-1]
    cells = lines * LANES
    end = row_ref.shape[1]
    me = lax.axis_index("slab").astype(jnp.int32)
    copies = []
    for slab in range(slabs):
        part = pl.ds(slab * cells, cells)
        copies.append(pltpu.make_async_copy(row_ref.at[:, part], held.at[:, part], sems.at[slab]))
    for n, target in enumerate(slab_refs):
        start = (me if n < fields else me ^ half) * lines
        source = field_refs[n % fields].at[lines_of(start, target.shape[0]), :]
        copies.append(pltpu.make_async_copy(source, target, sems.at[slabs + n]))
    for copy in copies:
        copy.start()
    for copy in copies[:slabs]:
        copy.wait()

    def part(start, size):
        return held[:, pl.ds(pl.multiple_of(start, GRID_Y), size)]

    def grid_row(start):
        return part(start, GRID_Y).astype(F32).reshape(LINE, LANES)

    for at in range(slabs):
        out_ref = near_out.at[at] if at < half else far_outs[at - half]
        slab = device_at(at, half)
        start = slab * cells
        out_ref[:lines, :] = part(start, cells).reshape(lines, LANES)
        below = jnp.where(slab == slabs - 1, 0.0, grid_row(jnp.minimum(start + cells, end - GRID_Y)))
        above = jnp.where(slab == 0, 0.0, grid_row(jnp.maximum(start - GRID_Y, 0)))
        out_ref[lines : lines + TILE, :] = jnp.concatenate([below, above], axis=0).astype(BF16)
        if at < half:
            start = (slab ^ half) * cells
            to = lines + TILE
            out_ref[to : to + raw, :] = part(start, raw * LANES).reshape(raw, LANES)
            below = grid_row(start + raw * LANES)
            above = jnp.where(slab ^ half == 0, 0.0, grid_row(jnp.maximum(start - GRID_Y, 0)))
            out_ref[to + raw :, :] = jnp.concatenate([below, above], axis=0).astype(BF16)
    for copy in copies[slabs:]:
        copy.wait()


def split_pieces(row, slabs, raw, fields):
    lines = row.shape[1] // slabs // LANES
    half = slabs // 2
    rim = lines + TILE
    size = rim + raw + TILE
    out_shape = [jax.ShapeDtypeStruct((half, size, LANES), BF16)]
    out_shape += [jax.ShapeDtypeStruct((rim, LANES), BF16)] * half
    out_shape += [jax.ShapeDtypeStruct((lines, LANES), BF16)] * len(fields)
    out_shape += [jax.ShapeDtypeStruct((raw, LANES), BF16)] * len(fields)
    return call(
        functools.partial(split_pieces_body, slabs, raw, lines, len(fields)),
        "split_pieces",
        moved=6 * half * (rim + size) * LANES,
        in_specs=[IN_HBM] * (1 + len(fields)),
        out_specs=[IN_VMEM] * len(out_shape),
        out_shape=out_shape,
        scratch_shapes=[pltpu.VMEM(row.shape, BF16), pltpu.SemaphoreType.DMA((slabs + 2 * len(fields),))],
    )(row, *fields)


def join_pieces_body(pieces, half, raw, lines, begun, arrays, *refs):
    row_ref, helds, sems = refs[begun + arrays], refs[begun + arrays + 1 : -1], refs[-1]
    cells = lines * LANES
    skip = raw * LANES
    copies = []
    for (array, lead, at), held in zip(pieces, helds):
        ref = refs[begun + array]
        piece = ref[...] if lead is None else ref[lead]
        held[...] = piece.reshape(held.shape)
        slab = device_at(at, half)
        if at < half:
            parts = [(0, cells, slab * cells), (cells, skip, (slab ^ half) * cells)]
        else:
            parts = [(0, cells - skip, slab * cells + skip)]
        for begin, size, start in parts:
            target = row_ref.at[:, pl.ds(pl.multiple_of(start, GRID_Y), size)]
            copies.append(pltpu.make_async_copy(held.at[:, pl.ds(begin, size)], target, sems.at[len(copies)]))
            copies[-1].start()
    for copy in copies:
        copy.wait()


def join_pieces(row, slabs, raw, arrays, pieces):
    sizes = [arrays[piece[0]].shape[-2] * LANES for piece in pieces]
    begun = [] if row is None else [row]
    return call(
        functools.partial(
            join_pieces_body, pieces, slabs // 2, raw, NCELL // slabs // LANES, len(begun), len(arrays)
        ),
        "join_pieces",
        moved=6 * sum(sizes),
        in_specs=[IN_HBM] * len(begun) + [IN_VMEM] * len(arrays),
        out_specs=IN_HBM,
        out_shape=jax.ShapeDtypeStruct((1, NCELL), BF16),
        input_output_aliases={0: 0} if begun else {},
        scratch_shapes=[pltpu.VMEM((1, size), BF16) for size in sizes]
        + [pltpu.SemaphoreType.DMA((2 * len(sizes),))],
    )(*begun, *arrays)


def owners(total, dtype):
    wide = total * TILE
    row = lax.broadcasted_iota(jnp.int32, (wide, total), 0)
    col = lax.broadcasted_iota(jnp.int32, (wide, total), 1)
    return (device_at(row // TILE, total // 2) == col).astype(dtype)


def gram_pieces_body(lines, total, near_ref, *refs):
    half = total // 2
    pieces, out_ref, pairs = refs[:half], refs[-2], refs[-1]
    wide = total * TILE
    tiles = 8
    pairs[...] = jnp.zeros_like(pairs)

    def step(i, carry):
        parts = []
        for t in range(tiles):
            at = lines_of((i * tiles + t) * TILE, TILE)
            near = near_ref[:, at, :].reshape(wide // 2, LANES)
            parts.append(jnp.concatenate([near] + [piece[at, :] for piece in pieces], axis=0))
        block = jnp.concatenate(parts, axis=1)
        pairs[...] += lax.dot_general(block, block, (((1,), (1,)), ((), ())), preferred_element_type=F32)
        return carry

    lax.fori_loop(0, lines // TILE // tiles, step, 0)
    equal = jnp.where(same_line(total), pairs[...], 0.0)
    exact = {"precision": lax.Precision.HIGHEST, "preferred_element_type": F32}
    rows = jnp.sum(equal.reshape(total, TILE, wide), axis=1)
    gram = jnp.dot(rows, owners(total, F32), **exact)
    row = lax.broadcasted_iota(jnp.int32, (total, total), 0)
    col = lax.broadcasted_iota(jnp.int32, (total, total), 1)
    gram = jnp.dot((row == device_at(col, half)).astype(F32), gram, **exact)
    gram = jnp.concatenate([gram, jnp.zeros((total, LANES - total), F32)], axis=1)
    out_ref[...] = jnp.broadcast_to(gram[None], out_ref.shape)


def gram_pieces(near, far, lines, gates, early):
    total = 2 * len(far)
    wide = total * TILE
    return call(
        functools.partial(gram_pieces_body, lines, total),
        "gram_pieces",
        flops=2 * wide * wide * LANES * (lines // TILE),
        moved=2 * total * lines * LANES,
        in_specs=[IN_VMEM] * (1 + len(far)) + [IN_HBM] * len(gates) + [IN_VMEM] * len(early),
        out_specs=IN_VMEM,
        out_shape=jax.ShapeDtypeStruct((total, total, LANES), F32),
        scratch_shapes=[pltpu.VMEM((wide, wide), F32)],
    )(near, *far, *gates, *early)


def block_gradient(load, i, count, observed, precision):
    start = i * BLOCK
    at = lines_of(start, BLOCK)
    shape = (BLOCK // LINE, LINE, LANES)
    lane = lax.broadcasted_iota(jnp.int32, (1, LINE, LANES), 2)
    line = lax.broadcasted_iota(jnp.int32, (1, LINE, LANES), 1)
    obs = observed[at, :].astype(F32).reshape(shape)
    prec = precision[at, :].astype(F32).reshape(shape)
    here = load(start, BLOCK).astype(F32)
    before = load(jnp.where(i == 0, count, start - TILE), TILE).astype(F32)
    after = load(start + BLOCK, TILE).astype(F32)
    above = jnp.concatenate([before[LINE:], here[:-LINE]], axis=0).reshape(shape)
    below = jnp.concatenate([here[LINE:], after[:LINE]], axis=0).reshape(shape)
    field = here.reshape(shape)
    turned = pltpu.roll(field, 1, 2)
    carried = jnp.where(line == 0, 0.0, pltpu.roll(turned, 1, 1))
    left = jnp.where(lane == 0, carried, turned)
    turned = pltpu.roll(field, LANES - 1, 2)
    carried = jnp.where(line == LINE - 1, 0.0, pltpu.roll(turned, LINE - 1, 1))
    right = jnp.where(lane == LANES - 1, carried, turned)
    laplace = (4.0 + mass_term) * field - (below + above + right + left)
    squash = jnp.tanh(field)
    result = prec * (obs - squash) * (1.0 - squash * squash) - prior_scale * laplace
    return result.reshape(BLOCK, LANES).astype(BF16)


def gradient_pieces_body(views, arrays, numbers, *refs):
    observed, precision, *number_refs = refs[arrays : arrays + 2 + numbers]
    out_ref, rows_ref, grads, sems = refs[-4:]
    for n, number_ref in enumerate(number_refs):
        rows_ref[n : n + 1, :] = jnp.full((1, LANES), number_ref[0], F32)
    count = observed.shape[0]
    steps = count // BLOCK

    def store(i):
        at = lines_of(i * BLOCK, BLOCK)
        return pltpu.make_async_copy(grads.at[:, at, :], out_ref.at[:, at, :], sems.at[i])

    def step(i, carry):
        for p, (array, lead, base) in enumerate(views):

            def load(start, size):
                part = lines_of(base + start, size)
                return refs[array][part, :] if lead is None else refs[array][lead, part, :]

            grads[p, lines_of(i * BLOCK, BLOCK), :] = block_gradient(load, i, count, observed, precision)
        store(i).start()
        return carry

    def finish(i, carry):
        store(i).wait()
        return carry

    lax.fori_loop(0, steps, step, 0)
    lax.fori_loop(0, steps, finish, 0)


def gradient_pieces(arrays, views, observed, precision, numbers):
    count = observed.shape[0]
    out = pltpu.HBM((len(views), count, LANES), BF16)
    size = len(views) * count * LANES
    return call(
        functools.partial(gradient_pieces_body, views, len(arrays), len(numbers)),
        "gradient_pieces",
        flops=30 * size,
        moved=8 * size,
        in_specs=[IN_VMEM] * (len(arrays) + 2)
        + [pl.BlockSpec(memory_space=pltpu.SMEM)] * len(numbers),
        out_specs=[IN_HBM, IN_VMEM],
        out_shape=[out, jax.ShapeDtypeStruct((8, LANES), F32)],
        scratch_shapes=[pltpu.VMEM(out.shape, BF16), pltpu.SemaphoreType.DMA((count // BLOCK,))],
    )(*arrays, observed, precision, *numbers)


def raw_body(raw, lines, near_ref, *refs):
    out_ref = refs[-1]
    for k in range(near_ref.shape[0]):
        out_ref[k, :raw, :] = near_ref[k, :raw, :]
        below = near_ref[k, raw : raw + TILE, :].astype(F32)[:LINE]
        above = near_ref[k, lines : lines + TILE, :].astype(F32)[LINE:]
        out_ref[k, raw:, :] = jnp.concatenate([below, above], axis=0).astype(BF16)


def raw_states(near, raw, lines, gates):
    out = jax.ShapeDtypeStruct((near.shape[0], raw + TILE, LANES), BF16)
    return call(
        functools.partial(raw_body, raw, lines),
        "raw_states",
        moved=4 * out.size,
        in_specs=[IN_VMEM] * (1 + len(gates)),
        out_specs=IN_VMEM,
        out_shape=out,
    )(near, *gates)


def mix(mixer, own, numbers_ref, total, states, slopes):
    high = mixer.shape[0]
    rate = numbers_ref[2:3, :1] / total
    coeff = 2.0 * numbers_ref[1:2, :1] / numbers_ref[:1, :1]
    both = jnp.concatenate([slopes, states], axis=1)
    mixed = jnp.dot(mixer[...], both, preferred_element_type=F32)
    drive, pulled = mixed[:, :LANES], mixed[:, LANES:]
    return (states[:high].astype(F32) * own[...] + rate * (drive - coeff * pulled)).astype(BF16)


def update_pieces_body(half, raw, lines, groups, near_ref, *refs):
    total = 2 * half
    far_refs, refs = refs[:half], refs[half:]
    across_ref, numbers_ref, grams_ref, raw_grads_ref, *refs = refs
    group_refs, near_to, far_tos = refs[: len(groups)], refs[len(groups)], refs[len(groups) + 1 : -8]
    near_out, far_out, mixer, own, grads, raw_grads, sems, out_sems = refs[-8:]
    wide = total * TILE
    high = half * TILE
    raw_fetch = pltpu.make_async_copy(raw_grads_ref, raw_grads, sems.at[len(groups), 0])
    raw_fetch.start()
    middle = (raw + 2 * lines) // 3 // BLOCK * BLOCK
    parts = ((0, raw), (raw, middle), (middle, lines))
    fetches = []
    for n, (first, last) in enumerate(parts):
        part = pl.ds(first, last - first)
        fetches.append([])
        for g, (group, group_ref) in enumerate(zip(groups, group_refs)):
            target = grads.at[pl.ds(group[0], len(group)), part, :]
            fetches[n].append(pltpu.make_async_copy(group_ref.at[:, part, :], target, sems.at[g, n]))
            fetches[n][-1].start()
    gram = jnp.sum(grams_ref[...], axis=0)[:, :total]
    spread, anneal, step_size = (numbers_ref[k : k + 1, :1] for k in range(3))
    rate = step_size / total
    coeff = 2.0 * anneal / spread
    row = lax.broadcasted_iota(jnp.int32, (total, total), 0)
    col = lax.broadcasted_iota(jnp.int32, (total, total), 1)
    diagonal = jnp.where(row == col, gram, 0.0)
    down = jnp.sum(diagonal, axis=1, keepdims=True)
    across = jnp.sum(diagonal, axis=0, keepdims=True)
    kernel = jnp.exp(-(down + across - 2.0 * gram) / (spread * NCELL)).astype(BF16)
    owner = owners(total, BF16)
    half_way = jnp.dot(owner, kernel, preferred_element_type=F32).astype(BF16)
    full = lax.dot_general(half_way, owner, (((1,), (1,)), ((), ())), preferred_element_type=F32)
    full = jnp.where(same_line(total), full, 0.0)
    mixer[...] = full.astype(BF16)
    ksum = jnp.sum(full, axis=1, keepdims=True)
    own[...] = jnp.broadcast_to(1.0 + rate * coeff * ksum, (wide, LANES))

    stores = []

    def store(source, target, at):
        stores.append(pltpu.make_async_copy(source, target, out_sems.at[at]))
        stores[-1].start()

    def store_near(first, last, at):
        part = pl.ds(first, last - first)
        store(near_out.at[:, part, :], near_to.at[:, part, :], (half, at))

    def store_far(first, last, at):
        part = pl.ds(first - raw, last - first)
        for x, far_to in enumerate(far_tos):
            store(far_out.at[x, part, :], far_to.at[part, :], (x, at))

    def slab_step(with_far, i, carry):
        rows = wide if with_far else high
        for t in range(BLOCK // TILE):
            at = i * BLOCK + t * TILE
            part = lines_of(at, TILE)
            states = [near_ref[:, part, :].reshape(high, LANES)] + [ref[part, :] for ref in far_refs]
            slopes = grads[:, part, :].reshape(wide, LANES)
            states = jnp.concatenate(states, axis=0)
            new = mix(mixer.at[:rows, :], own.at[:rows, :], numbers_ref, total, states, slopes)
            near_out[:, part, :] = new[:high].reshape(half, TILE, LANES)
            if with_far:
                far_out[:, lines_of(at - raw, TILE), :] = new[high:].reshape(half, TILE, LANES)
        return carry

    here = lax.axis_index("slab").astype(jnp.int32) % half

    def raw_step(i, carry):
        for t in range(BLOCK // TILE):
            at = i * BLOCK + t * TILE
            part = lines_of(at, TILE)
            states = [near_ref[:, lines_of(lines + TILE + at, TILE), :].reshape(high, LANES)]
            slopes = [raw_grads[:half, part, :].reshape(high, LANES)]
            for x in range(half):
                states += [across_ref[here ^ x, part, :]]
                slopes += [raw_grads[half + (here ^ x), part, :]]
            states, slopes = jnp.concatenate(states, axis=0), jnp.concatenate(slopes, axis=0)
            new = mix(mixer.at[:high, :], own.at[:high, :], numbers_ref, total, states, slopes)
            near_out[:, lines_of(lines + at, TILE), :] = new.reshape(half, TILE, LANES)
        return carry

    raw_fetch.wait()
    lax.fori_loop(0, raw // BLOCK, raw_step, 0)
    store_near(lines, lines + raw, 0)
    for n, (first, last) in enumerate(parts):
        for fetch in fetches[n]:
            fetch.wait()
        lax.fori_loop(first // BLOCK, last // BLOCK, functools.partial(slab_step, n > 0), 0)
        store_near(first, last, 1 + n)
        if n:
            store_far(first, last, n - 1)
    for copy in stores:
        copy.wait()


def update_pieces(numbers, grams, near, far, across, raw_grads, grads, groups, raw, lines):
    half = len(far)
    total = 2 * half
    wide = total * TILE
    out_shape = [pltpu.HBM((half, lines + raw, LANES), BF16)]
    out_shape += [pltpu.HBM((lines - raw, LANES), BF16)] * half
    return call(
        functools.partial(update_pieces_body, half, raw, lines, groups),
        "update_pieces",
        flops=4 * wide * wide * LANES * (lines // TILE),
        moved=6 * total * lines * LANES,
        in_specs=[IN_VMEM] * (half + 4) + [IN_HBM] * (1 + len(groups)),
        out_specs=[IN_HBM] * len(out_shape),
        out_shape=out_shape,
        scratch_shapes=[
            pltpu.VMEM((half, lines + raw, LANES), BF16),
            pltpu.VMEM((half, lines - raw, LANES), BF16),
            pltpu.VMEM((wide, wide), BF16),
            pltpu.VMEM((wide, LANES), F32),
            pltpu.VMEM((total, lines, LANES), BF16),
            pltpu.VMEM((total, raw, LANES), BF16),
            pltpu.SemaphoreType.DMA((len(groups) + 1, 3)),
            pltpu.SemaphoreType.DMA((half + 1, 4)),
        ],
    )(near, *far, across, numbers, grams, raw_grads, *grads)


def exchange(piece, k, slabs):
    return lax.ppermute(piece, "slab", [(i, i ^ k) for i in range(slabs)])


def swap_near(pieces, slabs):
    groups = [list(range(slabs // 2)), list(range(slabs // 2, slabs))]
    return lax.all_to_all(pieces, "slab", 0, 0, axis_index_groups=groups, tiled=True)


RAW = 128
GRADIENTS = ((8, 9, 10, 11), (12, 13, 14, 15), (0, 1, 2, 3, 4, 5, 6, 7))


def by_halves(particles, observed, precision, spread, anneal, step_size):
    slabs = lax.axis_size("slab")
    half = slabs // 2
    lines = NCELL // slabs // LANES
    row = in_hbm(particles)
    fields = [in_hbm(field.reshape(-1, LANES)) for field in (observed, precision)]
    near, *far = split_pieces(row, slabs, RAW, fields)
    far, (obs, prec, *raw_fields) = far[:half], far[half:]
    near = swap_near(near, slabs)
    far = [exchange(piece, half + x, slabs) for x, piece in enumerate(far)]
    raw_near = raw_states(near, RAW, lines, far)
    across = exchange(raw_near, half, slabs)
    grads = []
    numbers = [spread, anneal, step_size]
    for group in GRADIENTS:
        if group[0] < half:
            arrays, views = [near], [(0, k, 0) for k in group]
        else:
            arrays, views = [far[k - half] for k in group], [(j, None, 0) for j in range(len(group))]
        slopes, rows = gradient_pieces(arrays, tuple(views), obs, prec, [] if grads else numbers)
        grads.append(in_hbm(slopes))
        numbers = numbers if len(grads) > 1 else rows
    grams = swap(gram_pieces(near, far, lines, grads[:1], [raw_near]))
    views = [(0, k, lines + TILE) for k in range(half)] + [(1, k, 0) for k in range(half)]
    raw_grads, _ = gradient_pieces([near, across], tuple(views), *raw_fields, [])
    new_near, *new_far = update_pieces(
        numbers, grams, near, far, across, in_hbm(raw_grads), grads, GRADIENTS, RAW, lines
    )
    new_near = swap_near(new_near, slabs)
    new_far = [exchange(piece, half + x, slabs) for x, piece in enumerate(new_far)]
    row = join_pieces(None, slabs, RAW, [new_near], [(0, k, k) for k in range(half)])
    for group in ((0, 1, 2, 3), (4, 5)):
        pieces = [(n, None, half + x) for n, x in enumerate(group)]
        row = join_pieces(row, slabs, RAW, [new_far[x] for x in group], pieces)
    return join_pieces(row, slabs, RAW, new_far[6:], [(n, None, half + 6 + n) for n in range(half - 6)])


def on_device(particles, observed, precision, spread, anneal, step_size):
    slabs = lax.axis_size("slab")
    total = particles.shape[0] * slabs
    lines = NCELL // slabs // LANES
    if slabs == 16:
        return by_halves(particles, observed, precision, spread, anneal, step_size)
    sent, begun = cuts(lines)
    fields = [observed.reshape(-1, LANES), precision.reshape(-1, LANES)]
    numbers = [spread, anneal, step_size]
    first, obs, prec, scalars = split_row(particles, slabs, 0, sent, True, fields, numbers, [])
    parts = [swap(first)]
    if sent < lines:
        parts += [swap(split_row(particles, slabs, sent, lines, False, [], [], [scalars])[0])]
    if total * TILE > 256:
        grads = slab_gradient(parts, obs, prec, lines, 0, lines)
        states = jnp.concatenate([parts[0][:, :sent]] + parts[1:], axis=1)
        new = plain_update(spread, anneal, step_size, states, grads)
        return join_row(swap(new), lines, 0, None)
    if sent == lines:
        grads = slab_gradient(parts, obs, prec, lines, 0, lines)
        grams = swap(slab_gram(parts[0], lines, slabs, [], []))
        new = slab_update(scalars, grams, parts, grads, 0, lines, [])
        return join_row(swap(new), lines, 0, None)
    gram = slab_gram(parts[0], sent, 1, [], [])
    early = slab_gradient(parts[:1], obs, prec, lines, 0, begun)
    grams = swap(slab_gram(parts[1], lines - sent, slabs, [gram], [early]))
    late = slab_gradient(parts, obs, prec, lines, begun, lines)
    new = slab_update(scalars, grams, parts[:1], early, 0, begun, [])
    rest = slab_update(scalars, grams, parts, late, begun, lines, [new])
    row = join_row(swap(new), lines, 0, None)
    return join_row(swap(rest), lines, begun, row)


def solution(mesh):
    in_specs = (
        P(("groups", "slab"), None),
        P("groups"),
        P("groups"),
        P("groups"),
        P("groups"),
        P("groups"),
    )
    out_specs = P(("groups", "slab"), None)
    return jax.shard_map(
        on_device, mesh=mesh, in_specs=in_specs, out_specs=out_specs, check_vma=False
    )
```

```python
import functools

import jax
import jax.numpy as jnp
from jax import lax
from jax.experimental import pallas as pl
from jax.experimental.pallas import tpu as pltpu
from jax.sharding import PartitionSpec as P

GRID_X = 1024
GRID_Y = 1024
NCELL = 1048576
LANES = 128
LINE = GRID_Y // LANES
TILE = 16

prior_scale = 0.25
mass_term = 1.0

F32 = jnp.float32
BF16 = jnp.bfloat16
MIB = 1024 * 1024


def call(body, name, flops=0, moved=0, limit=16, **kwargs):
    return pl.pallas_call(
        body,
        name=name,
        compiler_params=pltpu.CompilerParams(vmem_limit_bytes=limit * MIB),
        cost_estimate=pl.CostEstimate(flops=flops, bytes_accessed=moved, transcendentals=0),
        **kwargs,
    )


IN_VMEM = pl.BlockSpec(memory_space=pltpu.VMEM)
IN_HBM = pl.BlockSpec(memory_space=pltpu.HBM)


def in_hbm(array):
    return pltpu.with_memory_space_constraint(array, pltpu.HBM)


BLOCK = 4 * TILE


def cuts(lines):
    if lines % (8 * BLOCK):
        return lines, lines
    return lines * 3 // 4, lines * 3 // 4 - BLOCK


def split_body(lines, begin, rim, fields, numbers, row_ref, *refs):
    field_refs, number_refs = refs[:fields], refs[fields : fields + numbers]
    out_ref, *slab_refs, rows_ref = refs[-7 - fields : -5]
    held, edges, sems, edge_sems, field_sems = refs[-5:]
    for k, number_ref in enumerate(number_refs):
        rows_ref[k : k + 1, :] = jnp.broadcast_to(number_ref[...].reshape(1, 1), (1, LANES))
    slabs, count, _ = out_ref.shape
    count -= TILE * rim
    size = count * LANES
    cells = lines * LANES

    def part(slab):
        source = row_ref.at[:, pl.ds(slab * cells + begin * LANES, size)]
        return pltpu.make_async_copy(source, held.at[:, pl.ds(slab * size, size)], sems.at[slab])

    def edge(slab):
        source = row_ref.at[:, pl.ds(slab * cells - GRID_Y, GRID_Y)]
        return pltpu.make_async_copy(source, edges.at[:, pl.ds(slab * GRID_Y, GRID_Y)], edge_sems.at[slab])

    def grid_row(ref, start):
        return ref[:, pl.ds(start, GRID_Y)].astype(F32).reshape(LINE, LANES)

    for slab in range(slabs):
        part(slab).start()
        if rim and slab:
            edge(slab).start()
    mine = pl.ds(pl.multiple_of(lax.axis_index("slab") * lines, TILE), lines)
    fetches = [
        pltpu.make_async_copy(source.at[mine, :], target, field_sems.at[k])
        for k, (source, target) in enumerate(zip(field_refs, slab_refs))
    ]
    for fetch in fetches:
        fetch.start()
    part(0).wait()
    outside = jnp.zeros((LINE, LANES), F32)
    for slab in range(slabs):
        if slab + 1 < slabs:
            part(slab + 1).wait()
        out_ref[slab, :count, :] = held[:, pl.ds(slab * size, size)].reshape(count, LANES)
        if rim:
            if slab:
                edge(slab).wait()
            below = grid_row(held, (slab + 1) * size) if slab + 1 < slabs else outside
            above = grid_row(edges, slab * GRID_Y) if slab else outside
            out_ref[slab, count:, :] = jnp.concatenate([below, above], axis=0).astype(BF16)
    for fetch in fetches:
        fetch.wait()


def split_row(row, slabs, begin, end, rim, fields, numbers, earlier):
    lines = row.shape[1] // slabs // LANES
    count = end - begin
    return call(
        functools.partial(split_body, lines, begin, rim, len(fields), len(numbers)),
        "split_row",
        moved=6 * slabs * count * LANES,
        in_specs=[IN_HBM] * (1 + len(fields)) + [IN_VMEM] * len(numbers) + [IN_HBM] * len(earlier),
        out_specs=[IN_VMEM] * (2 + len(fields)),
        out_shape=[jax.ShapeDtypeStruct((slabs, count + TILE * rim, LANES), BF16)]
        + [jax.ShapeDtypeStruct((lines, LANES), BF16)] * len(fields)
        + [jax.ShapeDtypeStruct((8, LANES), F32)],
        scratch_shapes=[
            pltpu.VMEM((1, slabs * count * LANES), BF16),
            pltpu.VMEM((1, slabs * GRID_Y), BF16),
            pltpu.SemaphoreType.DMA((slabs,)),
            pltpu.SemaphoreType.DMA((slabs,)),
            pltpu.SemaphoreType.DMA((2,)),
        ],
    )(row, *fields, *numbers, *earlier)


def join_body(lines, begin, slabs_ref, *refs):
    row_ref, held, sems = refs[-3:]
    slabs, count, _ = slabs_ref.shape
    size = count * LANES
    copies = []
    for slab in range(slabs):
        at = pl.ds(slab * size, size)
        held[:, at] = slabs_ref[slab].reshape(1, size)
        target = row_ref.at[:, pl.ds((slab * lines + begin) * LANES, size)]
        copies.append(pltpu.make_async_copy(held.at[:, at], target, sems.at[slab]))
        copies[-1].start()
    for copy in copies:
        copy.wait()


def join_row(slabs, lines, begin, row):
    total, count, _ = slabs.shape
    begun = [] if row is None else [row]
    return call(
        functools.partial(join_body, lines, begin),
        "join_row",
        moved=6 * slabs.size,
        in_specs=[IN_VMEM] + [IN_HBM] * len(begun),
        out_specs=IN_HBM,
        out_shape=jax.ShapeDtypeStruct((1, total * lines * LANES), BF16),
        input_output_aliases={1: 0} if begun else {},
        scratch_shapes=[pltpu.VMEM((1, slabs.size), BF16), pltpu.SemaphoreType.DMA((total,))],
    )(slabs, *begun)


def same_line(total):
    wide = total * TILE
    row = lax.broadcasted_iota(jnp.int32, (wide, wide), 0)
    col = lax.broadcasted_iota(jnp.int32, (wide, wide), 1)
    return row % TILE == col % TILE


def members(total, dtype):
    wide = total * TILE
    row = lax.broadcasted_iota(jnp.int32, (wide, total), 0)
    col = lax.broadcasted_iota(jnp.int32, (wide, total), 1)
    return (row // TILE == col).astype(dtype)


def gram_body(steps, tiles, parts, states_ref, *refs):
    out_ref, pairs = refs[-2:]
    total = states_ref.shape[0]
    wide = total * TILE
    pairs[...] = jnp.zeros_like(pairs)

    def step(i, carry):
        parts = [
            states_ref[:, pl.ds(pl.multiple_of((i * tiles + t) * TILE, TILE), TILE), :].reshape(wide, LANES)
            for t in range(tiles)
        ]
        block = jnp.concatenate(parts, axis=1)
        pairs[...] += lax.dot_general(block, block, (((1,), (1,)), ((), ())), preferred_element_type=F32)
        return carry

    lax.fori_loop(0, steps, step, 0)
    equal = jnp.where(same_line(total), pairs[...], 0.0)
    rows = jnp.sum(equal.reshape(total, TILE, wide), axis=1)
    gram = jnp.dot(rows, members(total, F32), precision=lax.Precision.HIGHEST, preferred_element_type=F32)
    gram = jnp.concatenate([gram, jnp.zeros((total, LANES - total), F32)], axis=1)
    for part_ref in refs[:parts]:
        gram += part_ref[0]
    out_ref[...] = jnp.broadcast_to(gram[None], out_ref.shape)


def slab_gram(states, lines, copies, parts, earlier):
    total = states.shape[0]
    wide = total * TILE
    tiles = min(8, lines // TILE)
    return call(
        functools.partial(gram_body, lines // TILE // tiles, tiles, len(parts)),
        "slab_gram",
        flops=2 * wide * wide * LANES * (lines // TILE),
        moved=2 * states.size,
        in_specs=[IN_VMEM] * (1 + len(parts)) + [IN_HBM] * len(earlier),
        out_specs=IN_VMEM,
        out_shape=jax.ShapeDtypeStruct((copies, total, LANES), F32),
        scratch_shapes=[pltpu.VMEM((wide, wide), F32)],
    )(states, *parts, *earlier)


def gradient_body(lines, begin, end, parts, *refs):
    observed, precision, out_ref, grads, sems = refs[parts:]
    total = grads.shape[0]
    first = refs[0].shape[1] - TILE
    rows = BLOCK // LINE
    group = 4
    shape = (rows, LINE, LANES)
    lane = lax.broadcasted_iota(jnp.int32, (1, LINE, LANES), 2)
    line = lax.broadcasted_iota(jnp.int32, (1, LINE, LANES), 1)

    def load(particle, at, count):
        ref, at = (refs[0], at) if at < first else (refs[1], at - first)
        return ref[particle, at : at + count, :].astype(F32)

    def rim(particle):
        return refs[0][particle, first:, :].astype(F32)

    stores = []
    for k, at in enumerate(range(begin, end, BLOCK)):
        mine = slice(at - begin, at - begin + BLOCK)
        obs = observed[at : at + BLOCK, :].astype(F32).reshape(shape)
        prec = precision[at : at + BLOCK, :].astype(F32).reshape(shape)

        def step(i, carry):
            for p in range(group):
                particle = i * group + p
                here = load(particle, at, BLOCK)
                before = load(particle, at - TILE, TILE) if at else rim(particle)
                after = load(particle, at + BLOCK, TILE) if at + BLOCK < lines else rim(particle)
                above = jnp.concatenate([before[LINE:], here[:-LINE]], axis=0).reshape(shape)
                below = jnp.concatenate([here[LINE:], after[:LINE]], axis=0).reshape(shape)
                field = here.reshape(shape)
                turned = pltpu.roll(field, 1, 2)
                carried = jnp.where(line == 0, 0.0, pltpu.roll(turned, 1, 1))
                left = jnp.where(lane == 0, carried, turned)
                turned = pltpu.roll(field, LANES - 1, 2)
                carried = jnp.where(line == LINE - 1, 0.0, pltpu.roll(turned, LINE - 1, 1))
                right = jnp.where(lane == LANES - 1, carried, turned)
                laplace = (4.0 + mass_term) * field - (below + above + right + left)
                squash = jnp.tanh(field)
                result = prec * (obs - squash) * (1.0 - squash * squash) - prior_scale * laplace
                grads[particle, mine, :] = result.reshape(BLOCK, LANES).astype(BF16)
            return carry

        lax.fori_loop(0, total // group, step, 0)
        stores.append(pltpu.make_async_copy(grads.at[:, mine, :], out_ref.at[:, mine, :], sems.at[k]))
        stores[-1].start()
    for store in stores:
        store.wait()


def slab_gradient(parts, observed, precision, lines, begin, end):
    total = parts[0].shape[0]
    count = end - begin
    out = jax.ShapeDtypeStruct((total, count, LANES), BF16)
    return call(
        functools.partial(gradient_body, lines, begin, end, len(parts)),
        "slab_gradient",
        flops=30 * out.size,
        moved=8 * out.size,
        in_specs=[IN_VMEM] * (len(parts) + 2),
        out_specs=IN_HBM,
        out_shape=out,
        scratch_shapes=[pltpu.VMEM(out.shape, BF16), pltpu.SemaphoreType.DMA((count // BLOCK,))],
    )(*parts, observed, precision)


def update_body(begin, end, parts, *refs):
    states_refs, refs = refs[:parts], refs[parts:]
    scalars_ref, grams_ref, grads_ref = refs[:3]
    out_ref, grads, mixer, own, sem = refs[-5:]
    total = out_ref.shape[0]
    wide = total * TILE
    fetch = pltpu.make_async_copy(grads_ref, grads, sem)
    fetch.start()
    gram = jnp.sum(grams_ref[...], axis=0)[:, :total]
    row = lax.broadcasted_iota(jnp.int32, (total, total), 0)
    col = lax.broadcasted_iota(jnp.int32, (total, total), 1)
    diagonal = jnp.where(row == col, gram, 0.0)
    down = jnp.sum(diagonal, axis=1, keepdims=True)
    across = jnp.sum(diagonal, axis=0, keepdims=True)
    member = members(total, BF16)
    spread, anneal, step_size = (scalars_ref[k : k + 1, :1] for k in range(3))
    rate = step_size / total
    coeff = 2.0 * anneal / spread
    kernel = jnp.exp(-(down + across - 2.0 * gram) / (spread * NCELL)).astype(BF16)
    ksum = jnp.sum(kernel.astype(F32), axis=1, keepdims=True)
    half = jnp.dot(member, kernel, preferred_element_type=F32).astype(BF16)
    full = lax.dot_general(half, member, (((1,), (1,)), ((), ())), preferred_element_type=F32)
    mixer[...] = jnp.where(same_line(total), full, 0.0).astype(BF16)
    gain = 1.0 + rate * coeff * ksum
    own[...] = jnp.broadcast_to(gain[:, :, None], (total, TILE, LANES)).reshape(wide, LANES)
    fetch.wait()

    done = 0
    for part, states_ref in enumerate(states_refs):
        have = states_ref.shape[1] - (0 if part else TILE)
        low = max(begin - done, 0)
        high = min(end - done, have)
        into = done - begin
        done += have

        def step(i, carry):
            for t in range(BLOCK // TILE):
                at = pl.multiple_of(i * BLOCK + t * TILE, TILE)
                there = pl.ds(pl.multiple_of(at + into, TILE), TILE)
                states = states_ref[:, pl.ds(at, TILE), :].reshape(wide, LANES)
                both = jnp.concatenate([grads[:, there, :].reshape(wide, LANES), states], axis=1)
                mixed = jnp.dot(mixer[...], both, preferred_element_type=F32)
                drive, pulled = mixed[:, :LANES], mixed[:, LANES:]
                new = states.astype(F32) * own[...] + rate * (drive - coeff * pulled)
                out_ref[:, there, :] = new.astype(BF16).reshape(total, TILE, LANES)
            return carry

        lax.fori_loop(low // BLOCK, high // BLOCK, step, 0)


def slab_update(scalars, grams, parts, grads, begin, end, earlier):
    total, count, _ = grads.shape
    wide = total * TILE
    return call(
        functools.partial(update_body, begin, end, len(parts)),
        "slab_update",
        flops=4 * wide * wide * LANES * (count // TILE),
        moved=6 * grads.size,
        in_specs=[IN_VMEM] * len(parts)
        + [IN_VMEM, IN_VMEM, IN_HBM]
        + [IN_HBM] * len(earlier),
        out_specs=IN_VMEM,
        out_shape=jax.ShapeDtypeStruct(grads.shape, BF16),
        scratch_shapes=[
            pltpu.VMEM(grads.shape, BF16),
            pltpu.VMEM((wide, wide), BF16),
            pltpu.VMEM((wide, LANES), F32),
            pltpu.SemaphoreType.DMA,
        ],
    )(*parts, scalars, grams, grads, *earlier)


def plain_update(spread, anneal, step_size, states, grads):
    total, lines, _ = grads.shape
    flat = states[:, :lines].reshape(total, -1)
    gram = lax.dot_general(flat, flat, (((1,), (1,)), ((), ())), preferred_element_type=F32)
    gram = lax.psum(gram, "slab")
    norms = jnp.diagonal(gram)
    kernel = jnp.exp(-(norms[:, None] + norms[None, :] - 2.0 * gram) / (spread[0] * NCELL)).astype(BF16)
    ksum = jnp.sum(kernel.astype(F32), axis=1)
    drive = jnp.dot(kernel, grads.reshape(total, -1), preferred_element_type=F32)
    pulled = jnp.dot(kernel, flat, preferred_element_type=F32)
    values = flat.astype(F32)
    repel = values * ksum[:, None] - pulled
    coeff = 2.0 * anneal[0] / spread[0]
    new = values + step_size[0] / total * (drive + coeff * repel)
    return new.astype(BF16).reshape(grads.shape)


def swap(slabs):
    return lax.all_to_all(slabs, "slab", split_axis=0, concat_axis=0, tiled=True)


def device_at(at, half):
    me = lax.axis_index("slab").astype(jnp.int32)
    return jnp.where(at < half, me - me % half + at, me ^ at)


def lines_of(start, count):
    return pl.ds(pl.multiple_of(start, TILE), count)


def split_pieces_body(slabs, raw, lines, fields, row_ref, *refs):
    half = slabs // 2
    field_refs, near_out, far_outs = refs[:fields], refs[fields], refs[fields + 1 : fields + 1 + half]
    slab_refs, held, sems = refs[fields + 1 + half : -2], refs[-2], refs[-1]
    cells = lines * LANES
    end = row_ref.shape[1]
    me = lax.axis_index("slab").astype(jnp.int32)
    copies = []
    for slab in range(slabs):
        part = pl.ds(slab * cells, cells)
        copies.append(pltpu.make_async_copy(row_ref.at[:, part], held.at[:, part], sems.at[slab]))
    for n, target in enumerate(slab_refs):
        start = (me if n < fields else me ^ half) * lines
        source = field_refs[n % fields].at[lines_of(start, target.shape[0]), :]
        copies.append(pltpu.make_async_copy(source, target, sems.at[slabs + n]))
    for copy in copies:
        copy.start()
    for copy in copies[:slabs]:
        copy.wait()

    def part(start, size):
        return held[:, pl.ds(pl.multiple_of(start, GRID_Y), size)]

    def grid_row(start):
        return part(start, GRID_Y).astype(F32).reshape(LINE, LANES)

    for at in range(slabs):
        out_ref = near_out.at[at] if at < half else far_outs[at - half]
        slab = device_at(at, half)
        start = slab * cells
        out_ref[:lines, :] = part(start, cells).reshape(lines, LANES)
        below = jnp.where(slab == slabs - 1, 0.0, grid_row(jnp.minimum(start + cells, end - GRID_Y)))
        above = jnp.where(slab == 0, 0.0, grid_row(jnp.maximum(start - GRID_Y, 0)))
        out_ref[lines : lines + TILE, :] = jnp.concatenate([below, above], axis=0).astype(BF16)
        if at < half:
            start = (slab ^ half) * cells
            to = lines + TILE
            out_ref[to : to + raw, :] = part(start, raw * LANES).reshape(raw, LANES)
            below = grid_row(start + raw * LANES)
            above = jnp.where(slab ^ half == 0, 0.0, grid_row(jnp.maximum(start - GRID_Y, 0)))
            out_ref[to + raw :, :] = jnp.concatenate([below, above], axis=0).astype(BF16)
    for copy in copies[slabs:]:
        copy.wait()


def split_pieces(row, slabs, raw, fields):
    lines = row.shape[1] // slabs // LANES
    half = slabs // 2
    rim = lines + TILE
    size = rim + raw + TILE
    out_shape = [jax.ShapeDtypeStruct((half, size, LANES), BF16)]
    out_shape += [jax.ShapeDtypeStruct((rim, LANES), BF16)] * half
    out_shape += [jax.ShapeDtypeStruct((lines, LANES), BF16)] * len(fields)
    out_shape += [jax.ShapeDtypeStruct((raw, LANES), BF16)] * len(fields)
    return call(
        functools.partial(split_pieces_body, slabs, raw, lines, len(fields)),
        "split_pieces",
        moved=6 * half * (rim + size) * LANES,
        in_specs=[IN_HBM] * (1 + len(fields)),
        out_specs=[IN_VMEM] * len(out_shape),
        out_shape=out_shape,
        scratch_shapes=[pltpu.VMEM(row.shape, BF16), pltpu.SemaphoreType.DMA((slabs + 2 * len(fields),))],
    )(row, *fields)


def copy_body(piece_ref, *refs):
    refs[-1][...] = piece_ref[...]


def copy_after(piece, gates):
    return call(
        copy_body,
        "copy_after",
        moved=4 * piece.size,
        in_specs=[IN_VMEM] * (1 + len(gates)),
        out_specs=IN_VMEM,
        out_shape=jax.ShapeDtypeStruct(piece.shape, piece.dtype),
    )(piece, *gates)


def join_pieces_body(pieces, half, raw, lines, begun, arrays, *refs):
    row_ref, helds, sems = refs[begun + arrays], refs[begun + arrays + 1 : -1], refs[-1]
    cells = lines * LANES
    skip = raw * LANES
    copies = []
    for (array, lead, at), held in zip(pieces, helds):
        ref = refs[begun + array]
        piece = ref[...] if lead is None else ref[lead]
        held[...] = piece.reshape(held.shape)
        slab = device_at(at, half)
        if at < half:
            parts = [(0, cells, slab * cells), (cells, skip, (slab ^ half) * cells)]
        else:
            parts = [(0, cells - skip, slab * cells + skip)]
        for begin, size, start in parts:
            target = row_ref.at[:, pl.ds(pl.multiple_of(start, GRID_Y), size)]
            copies.append(pltpu.make_async_copy(held.at[:, pl.ds(begin, size)], target, sems.at[len(copies)]))
            copies[-1].start()
    for copy in copies:
        copy.wait()


def join_pieces(row, slabs, raw, arrays, pieces):
    sizes = [arrays[piece[0]].shape[-2] * LANES for piece in pieces]
    begun = [] if row is None else [row]
    return call(
        functools.partial(
            join_pieces_body, pieces, slabs // 2, raw, NCELL // slabs // LANES, len(begun), len(arrays)
        ),
        "join_pieces",
        moved=6 * sum(sizes),
        in_specs=[IN_HBM] * len(begun) + [IN_VMEM] * len(arrays),
        out_specs=IN_HBM,
        out_shape=jax.ShapeDtypeStruct((1, NCELL), BF16),
        input_output_aliases={0: 0} if begun else {},
        scratch_shapes=[pltpu.VMEM((1, size), BF16) for size in sizes]
        + [pltpu.SemaphoreType.DMA((2 * len(sizes),))],
    )(*begun, *arrays)


def owners(total, dtype):
    wide = total * TILE
    row = lax.broadcasted_iota(jnp.int32, (wide, total), 0)
    col = lax.broadcasted_iota(jnp.int32, (wide, total), 1)
    return (device_at(row // TILE, total // 2) == col).astype(dtype)


def gram_pieces_body(lines, total, near_ref, *refs):
    half = total // 2
    pieces, out_ref, pairs = refs[:half], refs[-2], refs[-1]
    wide = total * TILE
    tiles = 8
    pairs[...] = jnp.zeros_like(pairs)

    def step(i, carry):
        parts = []
        for t in range(tiles):
            at = lines_of((i * tiles + t) * TILE, TILE)
            near = near_ref[:, at, :].reshape(wide // 2, LANES)
            parts.append(jnp.concatenate([near] + [piece[at, :] for piece in pieces], axis=0))
        block = jnp.concatenate(parts, axis=1)
        pairs[...] += lax.dot_general(block, block, (((1,), (1,)), ((), ())), preferred_element_type=F32)
        return carry

    lax.fori_loop(0, lines // TILE // tiles, step, 0)
    equal = jnp.where(same_line(total), pairs[...], 0.0)
    exact = {"precision": lax.Precision.HIGHEST, "preferred_element_type": F32}
    rows = jnp.sum(equal.reshape(total, TILE, wide), axis=1)
    gram = jnp.dot(rows, owners(total, F32), **exact)
    row = lax.broadcasted_iota(jnp.int32, (total, total), 0)
    col = lax.broadcasted_iota(jnp.int32, (total, total), 1)
    gram = jnp.dot((row == device_at(col, half)).astype(F32), gram, **exact)
    gram = jnp.concatenate([gram, jnp.zeros((total, LANES - total), F32)], axis=1)
    out_ref[...] = jnp.broadcast_to(gram[None], out_ref.shape)


def gram_pieces(near, far, lines, gates, early):
    total = 2 * len(far)
    wide = total * TILE
    return call(
        functools.partial(gram_pieces_body, lines, total),
        "gram_pieces",
        flops=2 * wide * wide * LANES * (lines // TILE),
        moved=2 * total * lines * LANES,
        in_specs=[IN_VMEM] * (1 + len(far)) + [IN_HBM] * len(gates) + [IN_VMEM] * len(early),
        out_specs=IN_VMEM,
        out_shape=jax.ShapeDtypeStruct((total, total, LANES), F32),
        scratch_shapes=[pltpu.VMEM((wide, wide), F32)],
    )(near, *far, *gates, *early)


def block_gradient(load, i, count, observed, precision):
    start = i * BLOCK
    at = lines_of(start, BLOCK)
    shape = (BLOCK // LINE, LINE, LANES)
    lane = lax.broadcasted_iota(jnp.int32, (1, LINE, LANES), 2)
    line = lax.broadcasted_iota(jnp.int32, (1, LINE, LANES), 1)
    obs = observed[at, :].astype(F32).reshape(shape)
    prec = precision[at, :].astype(F32).reshape(shape)
    here = load(start, BLOCK).astype(F32)
    before = load(jnp.where(i == 0, count, start - TILE), TILE).astype(F32)
    after = load(start + BLOCK, TILE).astype(F32)
    above = jnp.concatenate([before[LINE:], here[:-LINE]], axis=0).reshape(shape)
    below = jnp.concatenate([here[LINE:], after[:LINE]], axis=0).reshape(shape)
    field = here.reshape(shape)
    turned = pltpu.roll(field, 1, 2)
    carried = jnp.where(line == 0, 0.0, pltpu.roll(turned, 1, 1))
    left = jnp.where(lane == 0, carried, turned)
    turned = pltpu.roll(field, LANES - 1, 2)
    carried = jnp.where(line == LINE - 1, 0.0, pltpu.roll(turned, LINE - 1, 1))
    right = jnp.where(lane == LANES - 1, carried, turned)
    laplace = (4.0 + mass_term) * field - (below + above + right + left)
    squash = jnp.tanh(field)
    result = prec * (obs - squash) * (1.0 - squash * squash) - prior_scale * laplace
    return result.reshape(BLOCK, LANES).astype(BF16)


def gradient_pieces_body(views, arrays, numbers, *refs):
    observed, precision, *number_refs = refs[arrays : arrays + 2 + numbers]
    out_ref, rows_ref, grads, sems = refs[-4:]
    for n, number_ref in enumerate(number_refs):
        rows_ref[n : n + 1, :] = jnp.full((1, LANES), number_ref[0], F32)
    count = observed.shape[0]
    steps = count // BLOCK

    def store(i):
        at = lines_of(i * BLOCK, BLOCK)
        return pltpu.make_async_copy(grads.at[:, at, :], out_ref.at[:, at, :], sems.at[i])

    def step(i, carry):
        for p, (array, lead, base) in enumerate(views):

            def load(start, size):
                part = lines_of(base + start, size)
                return refs[array][part, :] if lead is None else refs[array][lead, part, :]

            grads[p, lines_of(i * BLOCK, BLOCK), :] = block_gradient(load, i, count, observed, precision)
        store(i).start()
        return carry

    def finish(i, carry):
        store(i).wait()
        return carry

    lax.fori_loop(0, steps, step, 0)
    lax.fori_loop(0, steps, finish, 0)


def gradient_pieces(arrays, views, observed, precision, numbers):
    count = observed.shape[0]
    out = pltpu.HBM((len(views), count, LANES), BF16)
    size = len(views) * count * LANES
    return call(
        functools.partial(gradient_pieces_body, views, len(arrays), len(numbers)),
        "gradient_pieces",
        flops=30 * size,
        moved=8 * size,
        in_specs=[IN_VMEM] * (len(arrays) + 2)
        + [pl.BlockSpec(memory_space=pltpu.SMEM)] * len(numbers),
        out_specs=[IN_HBM, IN_VMEM],
        out_shape=[out, jax.ShapeDtypeStruct((8, LANES), F32)],
        scratch_shapes=[pltpu.VMEM(out.shape, BF16), pltpu.SemaphoreType.DMA((count // BLOCK,))],
    )(*arrays, observed, precision, *numbers)


def raw_body(raw, lines, near_ref, *refs):
    out_ref = refs[-1]
    for k in range(near_ref.shape[0]):
        out_ref[k, :raw, :] = near_ref[k, :raw, :]
        below = near_ref[k, raw : raw + TILE, :].astype(F32)[:LINE]
        above = near_ref[k, lines : lines + TILE, :].astype(F32)[LINE:]
        out_ref[k, raw:, :] = jnp.concatenate([below, above], axis=0).astype(BF16)


def raw_states(near, raw, lines, gates):
    out = jax.ShapeDtypeStruct((near.shape[0], raw + TILE, LANES), BF16)
    return call(
        functools.partial(raw_body, raw, lines),
        "raw_states",
        moved=4 * out.size,
        in_specs=[IN_VMEM] * (1 + len(gates)),
        out_specs=IN_VMEM,
        out_shape=out,
    )(near, *gates)


def mix(mixer, own, numbers_ref, total, states, slopes):
    high = mixer.shape[0]
    rate = numbers_ref[2:3, :1] / total
    coeff = 2.0 * numbers_ref[1:2, :1] / numbers_ref[:1, :1]
    both = jnp.concatenate([slopes, states], axis=1)
    mixed = jnp.dot(mixer[...], both, preferred_element_type=F32)
    drive, pulled = mixed[:, :LANES], mixed[:, LANES:]
    return (states[:high].astype(F32) * own[...] + rate * (drive - coeff * pulled)).astype(BF16)


def update_pieces_body(half, raw, lines, groups, near_ref, *refs):
    total = 2 * half
    far_refs, refs = refs[:half], refs[half:]
    across_ref, numbers_ref, grams_ref, raw_grads_ref, *refs = refs
    group_refs, near_to, far_tos = refs[: len(groups)], refs[len(groups)], refs[len(groups) + 1 : -8]
    near_out, far_out, mixer, own, grads, raw_grads, sems, out_sems = refs[-8:]
    wide = total * TILE
    high = half * TILE
    raw_fetch = pltpu.make_async_copy(raw_grads_ref, raw_grads, sems.at[len(groups), 0])
    raw_fetch.start()
    middle = (raw + 2 * lines) // 3 // BLOCK * BLOCK
    parts = ((0, raw), (raw, middle), (middle, lines))
    fetches = []
    for n, (first, last) in enumerate(parts):
        part = pl.ds(first, last - first)
        fetches.append([])
        for g, (group, group_ref) in enumerate(zip(groups, group_refs)):
            target = grads.at[pl.ds(group[0], len(group)), part, :]
            fetches[n].append(pltpu.make_async_copy(group_ref.at[:, part, :], target, sems.at[g, n]))
            fetches[n][-1].start()
    gram = jnp.sum(grams_ref[...], axis=0)[:, :total]
    spread, anneal, step_size = (numbers_ref[k : k + 1, :1] for k in range(3))
    rate = step_size / total
    coeff = 2.0 * anneal / spread
    row = lax.broadcasted_iota(jnp.int32, (total, total), 0)
    col = lax.broadcasted_iota(jnp.int32, (total, total), 1)
    diagonal = jnp.where(row == col, gram, 0.0)
    down = jnp.sum(diagonal, axis=1, keepdims=True)
    across = jnp.sum(diagonal, axis=0, keepdims=True)
    kernel = jnp.exp(-(down + across - 2.0 * gram) / (spread * NCELL)).astype(BF16)
    owner = owners(total, BF16)
    half_way = jnp.dot(owner, kernel, preferred_element_type=F32).astype(BF16)
    full = lax.dot_general(half_way, owner, (((1,), (1,)), ((), ())), preferred_element_type=F32)
    full = jnp.where(same_line(total), full, 0.0)
    mixer[...] = full.astype(BF16)
    ksum = jnp.sum(full, axis=1, keepdims=True)
    own[...] = jnp.broadcast_to(1.0 + rate * coeff * ksum, (wide, LANES))

    stores = []

    def store(source, target, at):
        stores.append(pltpu.make_async_copy(source, target, out_sems.at[at]))
        stores[-1].start()

    def store_near(first, last, at):
        part = pl.ds(first, last - first)
        store(near_out.at[:, part, :], near_to.at[:, part, :], (half, at))

    def store_far(first, last, at):
        part = pl.ds(first - raw, last - first)
        for x, far_to in enumerate(far_tos):
            store(far_out.at[x, part, :], far_to.at[part, :], (x, at))

    def slab_step(with_far, i, carry):
        rows = wide if with_far else high
        for t in range(BLOCK // TILE):
            at = i * BLOCK + t * TILE
            part = lines_of(at, TILE)
            states = [near_ref[:, part, :].reshape(high, LANES)] + [ref[part, :] for ref in far_refs]
            slopes = grads[:, part, :].reshape(wide, LANES)
            states = jnp.concatenate(states, axis=0)
            new = mix(mixer.at[:rows, :], own.at[:rows, :], numbers_ref, total, states, slopes)
            near_out[:, part, :] = new[:high].reshape(half, TILE, LANES)
            if with_far:
                far_out[:, lines_of(at - raw, TILE), :] = new[high:].reshape(half, TILE, LANES)
        return carry

    here = lax.axis_index("slab").astype(jnp.int32) % half

    def raw_step(i, carry):
        for t in range(BLOCK // TILE):
            at = i * BLOCK + t * TILE
            part = lines_of(at, TILE)
            states = [near_ref[:, lines_of(lines + TILE + at, TILE), :].reshape(high, LANES)]
            slopes = [raw_grads[:half, part, :].reshape(high, LANES)]
            for x in range(half):
                states += [across_ref[here ^ x, part, :]]
                slopes += [raw_grads[half + (here ^ x), part, :]]
            states, slopes = jnp.concatenate(states, axis=0), jnp.concatenate(slopes, axis=0)
            new = mix(mixer.at[:high, :], own.at[:high, :], numbers_ref, total, states, slopes)
            near_out[:, lines_of(lines + at, TILE), :] = new.reshape(half, TILE, LANES)
        return carry

    raw_fetch.wait()
    lax.fori_loop(0, raw // BLOCK, raw_step, 0)
    store_near(lines, lines + raw, 0)
    for n, (first, last) in enumerate(parts):
        for fetch in fetches[n]:
            fetch.wait()
        lax.fori_loop(first // BLOCK, last // BLOCK, functools.partial(slab_step, n > 0), 0)
        store_near(first, last, 1 + n)
        if n:
            store_far(first, last, n - 1)
    for copy in stores:
        copy.wait()


def update_pieces(numbers, grams, near, far, across, raw_grads, grads, groups, raw, lines):
    half = len(far)
    total = 2 * half
    wide = total * TILE
    out_shape = [pltpu.HBM((half, lines + raw, LANES), BF16)]
    out_shape += [pltpu.HBM((lines - raw, LANES), BF16)] * half
    return call(
        functools.partial(update_pieces_body, half, raw, lines, groups),
        "update_pieces",
        flops=4 * wide * wide * LANES * (lines // TILE),
        moved=6 * total * lines * LANES,
        in_specs=[IN_VMEM] * (half + 4) + [IN_HBM] * (1 + len(groups)),
        out_specs=[IN_HBM] * len(out_shape),
        out_shape=out_shape,
        scratch_shapes=[
            pltpu.VMEM((half, lines + raw, LANES), BF16),
            pltpu.VMEM((half, lines - raw, LANES), BF16),
            pltpu.VMEM((wide, wide), BF16),
            pltpu.VMEM((wide, LANES), F32),
            pltpu.VMEM((total, lines, LANES), BF16),
            pltpu.VMEM((total, raw, LANES), BF16),
            pltpu.SemaphoreType.DMA((len(groups) + 1, 3)),
            pltpu.SemaphoreType.DMA((half + 1, 4)),
        ],
    )(near, *far, across, numbers, grams, raw_grads, *grads)


def exchange(piece, k, slabs):
    return lax.ppermute(piece, "slab", [(i, i ^ k) for i in range(slabs)])


def swap_near(pieces, slabs):
    groups = [list(range(slabs // 2)), list(range(slabs // 2, slabs))]
    return lax.all_to_all(pieces, "slab", 0, 0, axis_index_groups=groups, tiled=True)


RAW = 128
GRADIENTS = ((8, 9, 10, 11), (12, 13, 14, 15), (0, 1, 2, 3, 4, 5, 6, 7))


def by_halves(particles, observed, precision, spread, anneal, step_size):
    slabs = lax.axis_size("slab")
    half = slabs // 2
    lines = NCELL // slabs // LANES
    row = in_hbm(particles)
    fields = [in_hbm(field.reshape(-1, LANES)) for field in (observed, precision)]
    near, *far = split_pieces(row, slabs, RAW, fields)
    far, (obs, prec, *raw_fields) = far[:half], far[half:]
    near = swap_near(near, slabs)
    views = tuple((0, k, 0) for k in range(half))
    near_grads, rows = gradient_pieces([near], views, obs, prec, [])
    far[-1] = copy_after(far[-1], [rows])
    far = [exchange(piece, half + x, slabs) for x, piece in enumerate(far)]
    raw_near = raw_states(near, RAW, lines, far)
    across = exchange(raw_near, half, slabs)
    grads = []
    numbers = [spread, anneal, step_size]
    for group in GRADIENTS[:-1]:
        arrays, views = [far[k - half] for k in group], [(j, None, 0) for j in range(len(group))]
        slopes, rows = gradient_pieces(arrays, tuple(views), obs, prec, [] if grads else numbers)
        grads.append(in_hbm(slopes))
        numbers = numbers if len(grads) > 1 else rows
    grads.append(in_hbm(near_grads))
    grams = swap(gram_pieces(near, far, lines, grads[:1], [raw_near]))
    views = [(0, k, lines + TILE) for k in range(half)] + [(1, k, 0) for k in range(half)]
    raw_grads, _ = gradient_pieces([near, across], tuple(views), *raw_fields, [])
    new_near, *new_far = update_pieces(
        numbers, grams, near, far, across, in_hbm(raw_grads), grads, GRADIENTS, RAW, lines
    )
    new_near = swap_near(new_near, slabs)
    new_far = [exchange(piece, half + x, slabs) for x, piece in enumerate(new_far)]
    row = join_pieces(None, slabs, RAW, [new_near], [(0, k, k) for k in range(half)])
    for group in ((0, 1, 2, 3), (4, 5)):
        pieces = [(n, None, half + x) for n, x in enumerate(group)]
        row = join_pieces(row, slabs, RAW, [new_far[x] for x in group], pieces)
    return join_pieces(row, slabs, RAW, new_far[6:], [(n, None, half + 6 + n) for n in range(half - 6)])


def on_device(particles, observed, precision, spread, anneal, step_size):
    slabs = lax.axis_size("slab")
    total = particles.shape[0] * slabs
    lines = NCELL // slabs // LANES
    if slabs == 16:
        return by_halves(particles, observed, precision, spread, anneal, step_size)
    sent, begun = cuts(lines)
    fields = [observed.reshape(-1, LANES), precision.reshape(-1, LANES)]
    numbers = [spread, anneal, step_size]
    first, obs, prec, scalars = split_row(particles, slabs, 0, sent, True, fields, numbers, [])
    parts = [swap(first)]
    if sent < lines:
        parts += [swap(split_row(particles, slabs, sent, lines, False, [], [], [scalars])[0])]
    if total * TILE > 256:
        grads = slab_gradient(parts, obs, prec, lines, 0, lines)
        states = jnp.concatenate([parts[0][:, :sent]] + parts[1:], axis=1)
        new = plain_update(spread, anneal, step_size, states, grads)
        return join_row(swap(new), lines, 0, None)
    if sent == lines:
        grads = slab_gradient(parts, obs, prec, lines, 0, lines)
        grams = swap(slab_gram(parts[0], lines, slabs, [], []))
        new = slab_update(scalars, grams, parts, grads, 0, lines, [])
        return join_row(swap(new), lines, 0, None)
    gram = slab_gram(parts[0], sent, 1, [], [])
    early = slab_gradient(parts[:1], obs, prec, lines, 0, begun)
    grams = swap(slab_gram(parts[1], lines - sent, slabs, [gram], [early]))
    late = slab_gradient(parts, obs, prec, lines, begun, lines)
    new = slab_update(scalars, grams, parts[:1], early, 0, begun, [])
    rest = slab_update(scalars, grams, parts, late, begun, lines, [new])
    row = join_row(swap(new), lines, 0, None)
    return join_row(swap(rest), lines, begun, row)


def solution(mesh):
    in_specs = (
        P(("groups", "slab"), None),
        P("groups"),
        P("groups"),
        P("groups"),
        P("groups"),
        P("groups"),
    )
    out_specs = P(("groups", "slab"), None)
    return jax.shard_map(
        on_device, mesh=mesh, in_specs=in_specs, out_specs=out_specs, check_vma=False
    )
```

```python
import functools

import jax
import jax.numpy as jnp
from jax import lax
from jax.experimental import pallas as pl
from jax.experimental.pallas import tpu as pltpu
from jax.sharding import PartitionSpec as P

GRID_X = 1024
GRID_Y = 1024
NCELL = 1048576
LANES = 128
LINE = GRID_Y // LANES
TILE = 16

prior_scale = 0.25
mass_term = 1.0

F32 = jnp.float32
BF16 = jnp.bfloat16
MIB = 1024 * 1024


def call(body, name, flops=0, moved=0, limit=16, **kwargs):
    return pl.pallas_call(
        body,
        name=name,
        compiler_params=pltpu.CompilerParams(vmem_limit_bytes=limit * MIB),
        cost_estimate=pl.CostEstimate(flops=flops, bytes_accessed=moved, transcendentals=0),
        **kwargs,
    )


IN_VMEM = pl.BlockSpec(memory_space=pltpu.VMEM)
IN_HBM = pl.BlockSpec(memory_space=pltpu.HBM)


def in_hbm(array):
    return pltpu.with_memory_space_constraint(array, pltpu.HBM)


BLOCK = 4 * TILE


def cuts(lines):
    if lines % (8 * BLOCK):
        return lines, lines
    return lines * 3 // 4, lines * 3 // 4 - BLOCK


def split_body(lines, begin, rim, fields, numbers, row_ref, *refs):
    field_refs, number_refs = refs[:fields], refs[fields : fields + numbers]
    out_ref, *slab_refs, rows_ref = refs[-7 - fields : -5]
    held, edges, sems, edge_sems, field_sems = refs[-5:]
    for k, number_ref in enumerate(number_refs):
        rows_ref[k : k + 1, :] = jnp.broadcast_to(number_ref[...].reshape(1, 1), (1, LANES))
    slabs, count, _ = out_ref.shape
    count -= TILE * rim
    size = count * LANES
    cells = lines * LANES

    def part(slab):
        source = row_ref.at[:, pl.ds(slab * cells + begin * LANES, size)]
        return pltpu.make_async_copy(source, held.at[:, pl.ds(slab * size, size)], sems.at[slab])

    def edge(slab):
        source = row_ref.at[:, pl.ds(slab * cells - GRID_Y, GRID_Y)]
        return pltpu.make_async_copy(source, edges.at[:, pl.ds(slab * GRID_Y, GRID_Y)], edge_sems.at[slab])

    def grid_row(ref, start):
        return ref[:, pl.ds(start, GRID_Y)].astype(F32).reshape(LINE, LANES)

    for slab in range(slabs):
        part(slab).start()
        if rim and slab:
            edge(slab).start()
    mine = pl.ds(pl.multiple_of(lax.axis_index("slab") * lines, TILE), lines)
    fetches = [
        pltpu.make_async_copy(source.at[mine, :], target, field_sems.at[k])
        for k, (source, target) in enumerate(zip(field_refs, slab_refs))
    ]
    for fetch in fetches:
        fetch.start()
    part(0).wait()
    outside = jnp.zeros((LINE, LANES), F32)
    for slab in range(slabs):
        if slab + 1 < slabs:
            part(slab + 1).wait()
        out_ref[slab, :count, :] = held[:, pl.ds(slab * size, size)].reshape(count, LANES)
        if rim:
            if slab:
                edge(slab).wait()
            below = grid_row(held, (slab + 1) * size) if slab + 1 < slabs else outside
            above = grid_row(edges, slab * GRID_Y) if slab else outside
            out_ref[slab, count:, :] = jnp.concatenate([below, above], axis=0).astype(BF16)
    for fetch in fetches:
        fetch.wait()


def split_row(row, slabs, begin, end, rim, fields, numbers, earlier):
    lines = row.shape[1] // slabs // LANES
    count = end - begin
    return call(
        functools.partial(split_body, lines, begin, rim, len(fields), len(numbers)),
        "split_row",
        moved=6 * slabs * count * LANES,
        in_specs=[IN_HBM] * (1 + len(fields)) + [IN_VMEM] * len(numbers) + [IN_HBM] * len(earlier),
        out_specs=[IN_VMEM] * (2 + len(fields)),
        out_shape=[jax.ShapeDtypeStruct((slabs, count + TILE * rim, LANES), BF16)]
        + [jax.ShapeDtypeStruct((lines, LANES), BF16)] * len(fields)
        + [jax.ShapeDtypeStruct((8, LANES), F32)],
        scratch_shapes=[
            pltpu.VMEM((1, slabs * count * LANES), BF16),
            pltpu.VMEM((1, slabs * GRID_Y), BF16),
            pltpu.SemaphoreType.DMA((slabs,)),
            pltpu.SemaphoreType.DMA((slabs,)),
            pltpu.SemaphoreType.DMA((2,)),
        ],
    )(row, *fields, *numbers, *earlier)


def join_body(lines, begin, slabs_ref, *refs):
    row_ref, held, sems = refs[-3:]
    slabs, count, _ = slabs_ref.shape
    size = count * LANES
    copies = []
    for slab in range(slabs):
        at = pl.ds(slab * size, size)
        held[:, at] = slabs_ref[slab].reshape(1, size)
        target = row_ref.at[:, pl.ds((slab * lines + begin) * LANES, size)]
        copies.append(pltpu.make_async_copy(held.at[:, at], target, sems.at[slab]))
        copies[-1].start()
    for copy in copies:
        copy.wait()


def join_row(slabs, lines, begin, row):
    total, count, _ = slabs.shape
    begun = [] if row is None else [row]
    return call(
        functools.partial(join_body, lines, begin),
        "join_row",
        moved=6 * slabs.size,
        in_specs=[IN_VMEM] + [IN_HBM] * len(begun),
        out_specs=IN_HBM,
        out_shape=jax.ShapeDtypeStruct((1, total * lines * LANES), BF16),
        input_output_aliases={1: 0} if begun else {},
        scratch_shapes=[pltpu.VMEM((1, slabs.size), BF16), pltpu.SemaphoreType.DMA((total,))],
    )(slabs, *begun)


def same_line(total):
    wide = total * TILE
    row = lax.broadcasted_iota(jnp.int32, (wide, wide), 0)
    col = lax.broadcasted_iota(jnp.int32, (wide, wide), 1)
    return row % TILE == col % TILE


def members(total, dtype):
    wide = total * TILE
    row = lax.broadcasted_iota(jnp.int32, (wide, total), 0)
    col = lax.broadcasted_iota(jnp.int32, (wide, total), 1)
    return (row // TILE == col).astype(dtype)


def gram_body(steps, tiles, parts, states_ref, *refs):
    out_ref, pairs = refs[-2:]
    total = states_ref.shape[0]
    wide = total * TILE
    pairs[...] = jnp.zeros_like(pairs)

    def step(i, carry):
        parts = [
            states_ref[:, pl.ds(pl.multiple_of((i * tiles + t) * TILE, TILE), TILE), :].reshape(wide, LANES)
            for t in range(tiles)
        ]
        block = jnp.concatenate(parts, axis=1)
        pairs[...] += lax.dot_general(block, block, (((1,), (1,)), ((), ())), preferred_element_type=F32)
        return carry

    lax.fori_loop(0, steps, step, 0)
    equal = jnp.where(same_line(total), pairs[...], 0.0)
    rows = jnp.sum(equal.reshape(total, TILE, wide), axis=1)
    gram = jnp.dot(rows, members(total, F32), precision=lax.Precision.HIGHEST, preferred_element_type=F32)
    gram = jnp.concatenate([gram, jnp.zeros((total, LANES - total), F32)], axis=1)
    for part_ref in refs[:parts]:
        gram += part_ref[0]
    out_ref[...] = jnp.broadcast_to(gram[None], out_ref.shape)


def slab_gram(states, lines, copies, parts, earlier):
    total = states.shape[0]
    wide = total * TILE
    tiles = min(8, lines // TILE)
    return call(
        functools.partial(gram_body, lines // TILE // tiles, tiles, len(parts)),
        "slab_gram",
        flops=2 * wide * wide * LANES * (lines // TILE),
        moved=2 * states.size,
        in_specs=[IN_VMEM] * (1 + len(parts)) + [IN_HBM] * len(earlier),
        out_specs=IN_VMEM,
        out_shape=jax.ShapeDtypeStruct((copies, total, LANES), F32),
        scratch_shapes=[pltpu.VMEM((wide, wide), F32)],
    )(states, *parts, *earlier)


def gradient_body(lines, begin, end, parts, *refs):
    observed, precision, out_ref, grads, sems = refs[parts:]
    total = grads.shape[0]
    first = refs[0].shape[1] - TILE
    rows = BLOCK // LINE
    group = 4
    shape = (rows, LINE, LANES)
    lane = lax.broadcasted_iota(jnp.int32, (1, LINE, LANES), 2)
    line = lax.broadcasted_iota(jnp.int32, (1, LINE, LANES), 1)

    def load(particle, at, count):
        ref, at = (refs[0], at) if at < first else (refs[1], at - first)
        return ref[particle, at : at + count, :].astype(F32)

    def rim(particle):
        return refs[0][particle, first:, :].astype(F32)

    stores = []
    for k, at in enumerate(range(begin, end, BLOCK)):
        mine = slice(at - begin, at - begin + BLOCK)
        obs = observed[at : at + BLOCK, :].astype(F32).reshape(shape)
        prec = precision[at : at + BLOCK, :].astype(F32).reshape(shape)

        def step(i, carry):
            for p in range(group):
                particle = i * group + p
                here = load(particle, at, BLOCK)
                before = load(particle, at - TILE, TILE) if at else rim(particle)
                after = load(particle, at + BLOCK, TILE) if at + BLOCK < lines else rim(particle)
                above = jnp.concatenate([before[LINE:], here[:-LINE]], axis=0).reshape(shape)
                below = jnp.concatenate([here[LINE:], after[:LINE]], axis=0).reshape(shape)
                field = here.reshape(shape)
                turned = pltpu.roll(field, 1, 2)
                carried = jnp.where(line == 0, 0.0, pltpu.roll(turned, 1, 1))
                left = jnp.where(lane == 0, carried, turned)
                turned = pltpu.roll(field, LANES - 1, 2)
                carried = jnp.where(line == LINE - 1, 0.0, pltpu.roll(turned, LINE - 1, 1))
                right = jnp.where(lane == LANES - 1, carried, turned)
                laplace = (4.0 + mass_term) * field - (below + above + right + left)
                squash = jnp.tanh(field)
                result = prec * (obs - squash) * (1.0 - squash * squash) - prior_scale * laplace
                grads[particle, mine, :] = result.reshape(BLOCK, LANES).astype(BF16)
            return carry

        lax.fori_loop(0, total // group, step, 0)
        stores.append(pltpu.make_async_copy(grads.at[:, mine, :], out_ref.at[:, mine, :], sems.at[k]))
        stores[-1].start()
    for store in stores:
        store.wait()


def slab_gradient(parts, observed, precision, lines, begin, end):
    total = parts[0].shape[0]
    count = end - begin
    out = jax.ShapeDtypeStruct((total, count, LANES), BF16)
    return call(
        functools.partial(gradient_body, lines, begin, end, len(parts)),
        "slab_gradient",
        flops=30 * out.size,
        moved=8 * out.size,
        in_specs=[IN_VMEM] * (len(parts) + 2),
        out_specs=IN_HBM,
        out_shape=out,
        scratch_shapes=[pltpu.VMEM(out.shape, BF16), pltpu.SemaphoreType.DMA((count // BLOCK,))],
    )(*parts, observed, precision)


def update_body(begin, end, parts, *refs):
    states_refs, refs = refs[:parts], refs[parts:]
    scalars_ref, grams_ref, grads_ref = refs[:3]
    out_ref, grads, mixer, own, sem = refs[-5:]
    total = out_ref.shape[0]
    wide = total * TILE
    fetch = pltpu.make_async_copy(grads_ref, grads, sem)
    fetch.start()
    gram = jnp.sum(grams_ref[...], axis=0)[:, :total]
    row = lax.broadcasted_iota(jnp.int32, (total, total), 0)
    col = lax.broadcasted_iota(jnp.int32, (total, total), 1)
    diagonal = jnp.where(row == col, gram, 0.0)
    down = jnp.sum(diagonal, axis=1, keepdims=True)
    across = jnp.sum(diagonal, axis=0, keepdims=True)
    member = members(total, BF16)
    spread, anneal, step_size = (scalars_ref[k : k + 1, :1] for k in range(3))
    rate = step_size / total
    coeff = 2.0 * anneal / spread
    kernel = jnp.exp(-(down + across - 2.0 * gram) / (spread * NCELL)).astype(BF16)
    ksum = jnp.sum(kernel.astype(F32), axis=1, keepdims=True)
    half = jnp.dot(member, kernel, preferred_element_type=F32).astype(BF16)
    full = lax.dot_general(half, member, (((1,), (1,)), ((), ())), preferred_element_type=F32)
    mixer[...] = jnp.where(same_line(total), full, 0.0).astype(BF16)
    gain = 1.0 + rate * coeff * ksum
    own[...] = jnp.broadcast_to(gain[:, :, None], (total, TILE, LANES)).reshape(wide, LANES)
    fetch.wait()

    done = 0
    for part, states_ref in enumerate(states_refs):
        have = states_ref.shape[1] - (0 if part else TILE)
        low = max(begin - done, 0)
        high = min(end - done, have)
        into = done - begin
        done += have

        def step(i, carry):
            for t in range(BLOCK // TILE):
                at = pl.multiple_of(i * BLOCK + t * TILE, TILE)
                there = pl.ds(pl.multiple_of(at + into, TILE), TILE)
                states = states_ref[:, pl.ds(at, TILE), :].reshape(wide, LANES)
                both = jnp.concatenate([grads[:, there, :].reshape(wide, LANES), states], axis=1)
                mixed = jnp.dot(mixer[...], both, preferred_element_type=F32)
                drive, pulled = mixed[:, :LANES], mixed[:, LANES:]
                new = states.astype(F32) * own[...] + rate * (drive - coeff * pulled)
                out_ref[:, there, :] = new.astype(BF16).reshape(total, TILE, LANES)
            return carry

        lax.fori_loop(low // BLOCK, high // BLOCK, step, 0)


def slab_update(scalars, grams, parts, grads, begin, end, earlier):
    total, count, _ = grads.shape
    wide = total * TILE
    return call(
        functools.partial(update_body, begin, end, len(parts)),
        "slab_update",
        flops=4 * wide * wide * LANES * (count // TILE),
        moved=6 * grads.size,
        in_specs=[IN_VMEM] * len(parts)
        + [IN_VMEM, IN_VMEM, IN_HBM]
        + [IN_HBM] * len(earlier),
        out_specs=IN_VMEM,
        out_shape=jax.ShapeDtypeStruct(grads.shape, BF16),
        scratch_shapes=[
            pltpu.VMEM(grads.shape, BF16),
            pltpu.VMEM((wide, wide), BF16),
            pltpu.VMEM((wide, LANES), F32),
            pltpu.SemaphoreType.DMA,
        ],
    )(*parts, scalars, grams, grads, *earlier)


def plain_update(spread, anneal, step_size, states, grads):
    total, lines, _ = grads.shape
    flat = states[:, :lines].reshape(total, -1)
    gram = lax.dot_general(flat, flat, (((1,), (1,)), ((), ())), preferred_element_type=F32)
    gram = lax.psum(gram, "slab")
    norms = jnp.diagonal(gram)
    kernel = jnp.exp(-(norms[:, None] + norms[None, :] - 2.0 * gram) / (spread[0] * NCELL)).astype(BF16)
    ksum = jnp.sum(kernel.astype(F32), axis=1)
    drive = jnp.dot(kernel, grads.reshape(total, -1), preferred_element_type=F32)
    pulled = jnp.dot(kernel, flat, preferred_element_type=F32)
    values = flat.astype(F32)
    repel = values * ksum[:, None] - pulled
    coeff = 2.0 * anneal[0] / spread[0]
    new = values + step_size[0] / total * (drive + coeff * repel)
    return new.astype(BF16).reshape(grads.shape)


def swap(slabs):
    return lax.all_to_all(slabs, "slab", split_axis=0, concat_axis=0, tiled=True)


def device_at(at, half):
    me = lax.axis_index("slab").astype(jnp.int32)
    return jnp.where(at < half, me - me % half + at, me ^ at)


def lines_of(start, count):
    return pl.ds(pl.multiple_of(start, TILE), count)


def split_pieces_body(slabs, raw, lines, fields, row_ref, *refs):
    half = slabs // 2
    field_refs, near_out, far_outs = refs[:fields], refs[fields], refs[fields + 1 : fields + 1 + half]
    slab_refs, held, sems = refs[fields + 1 + half : -2], refs[-2], refs[-1]
    cells = lines * LANES
    end = row_ref.shape[1]
    me = lax.axis_index("slab").astype(jnp.int32)
    copies = []
    for slab in range(slabs):
        part = pl.ds(slab * cells, cells)
        copies.append(pltpu.make_async_copy(row_ref.at[:, part], held.at[:, part], sems.at[slab]))
    for n, target in enumerate(slab_refs):
        start = (me if n < fields else me ^ half) * lines
        source = field_refs[n % fields].at[lines_of(start, target.shape[0]), :]
        copies.append(pltpu.make_async_copy(source, target, sems.at[slabs + n]))
    for copy in copies:
        copy.start()
    for copy in copies[:slabs]:
        copy.wait()

    def part(start, size):
        return held[:, pl.ds(pl.multiple_of(start, GRID_Y), size)]

    def grid_row(start):
        return part(start, GRID_Y).astype(F32).reshape(LINE, LANES)

    for at in range(slabs):
        out_ref = near_out.at[at] if at < half else far_outs[at - half]
        slab = device_at(at, half)
        start = slab * cells
        out_ref[:lines, :] = part(start, cells).reshape(lines, LANES)
        below = jnp.where(slab == slabs - 1, 0.0, grid_row(jnp.minimum(start + cells, end - GRID_Y)))
        above = jnp.where(slab == 0, 0.0, grid_row(jnp.maximum(start - GRID_Y, 0)))
        out_ref[lines : lines + TILE, :] = jnp.concatenate([below, above], axis=0).astype(BF16)
        if at < half:
            start = (slab ^ half) * cells
            to = lines + TILE
            out_ref[to : to + raw, :] = part(start, raw * LANES).reshape(raw, LANES)
            below = grid_row(start + raw * LANES)
            above = jnp.where(slab ^ half == 0, 0.0, grid_row(jnp.maximum(start - GRID_Y, 0)))
            out_ref[to + raw :, :] = jnp.concatenate([below, above], axis=0).astype(BF16)
    for copy in copies[slabs:]:
        copy.wait()


def split_pieces(row, slabs, raw, fields):
    lines = row.shape[1] // slabs // LANES
    half = slabs // 2
    rim = lines + TILE
    size = rim + raw + TILE
    out_shape = [jax.ShapeDtypeStruct((half, size, LANES), BF16)]
    out_shape += [jax.ShapeDtypeStruct((rim, LANES), BF16)] * half
    out_shape += [jax.ShapeDtypeStruct((lines, LANES), BF16)] * len(fields)
    out_shape += [jax.ShapeDtypeStruct((raw, LANES), BF16)] * len(fields)
    return call(
        functools.partial(split_pieces_body, slabs, raw, lines, len(fields)),
        "split_pieces",
        moved=6 * half * (rim + size) * LANES,
        in_specs=[IN_HBM] * (1 + len(fields)),
        out_specs=[IN_VMEM] * len(out_shape),
        out_shape=out_shape,
        scratch_shapes=[pltpu.VMEM(row.shape, BF16), pltpu.SemaphoreType.DMA((slabs + 2 * len(fields),))],
    )(row, *fields)


def join_pieces_body(pieces, half, raw, lines, begun, arrays, *refs):
    row_ref, helds, sems = refs[begun + arrays], refs[begun + arrays + 1 : -1], refs[-1]
    cells = lines * LANES
    skip = raw * LANES
    copies = []
    for (array, lead, at), held in zip(pieces, helds):
        ref = refs[begun + array]
        piece = ref[...] if lead is None else ref[lead]
        held[...] = piece.reshape(held.shape)
        slab = device_at(at, half)
        if at < half:
            parts = [(0, cells, slab * cells), (cells, skip, (slab ^ half) * cells)]
        else:
            parts = [(0, cells - skip, slab * cells + skip)]
        for begin, size, start in parts:
            target = row_ref.at[:, pl.ds(pl.multiple_of(start, GRID_Y), size)]
            copies.append(pltpu.make_async_copy(held.at[:, pl.ds(begin, size)], target, sems.at[len(copies)]))
            copies[-1].start()
    for copy in copies:
        copy.wait()


def join_pieces(row, slabs, raw, arrays, pieces):
    sizes = [arrays[piece[0]].shape[-2] * LANES for piece in pieces]
    begun = [] if row is None else [row]
    return call(
        functools.partial(
            join_pieces_body, pieces, slabs // 2, raw, NCELL // slabs // LANES, len(begun), len(arrays)
        ),
        "join_pieces",
        moved=6 * sum(sizes),
        in_specs=[IN_HBM] * len(begun) + [IN_VMEM] * len(arrays),
        out_specs=IN_HBM,
        out_shape=jax.ShapeDtypeStruct((1, NCELL), BF16),
        input_output_aliases={0: 0} if begun else {},
        scratch_shapes=[pltpu.VMEM((1, size), BF16) for size in sizes]
        + [pltpu.SemaphoreType.DMA((2 * len(sizes),))],
    )(*begun, *arrays)


def owners(total, dtype):
    wide = total * TILE
    row = lax.broadcasted_iota(jnp.int32, (wide, total), 0)
    col = lax.broadcasted_iota(jnp.int32, (wide, total), 1)
    return (device_at(row // TILE, total // 2) == col).astype(dtype)


def gram_pieces_body(lines, total, near_ref, *refs):
    half = total // 2
    pieces, out_ref, pairs = refs[:half], refs[-2], refs[-1]
    wide = total * TILE
    tiles = 8
    pairs[...] = jnp.zeros_like(pairs)

    def step(i, carry):
        parts = []
        for t in range(tiles):
            at = lines_of((i * tiles + t) * TILE, TILE)
            near = near_ref[:, at, :].reshape(wide // 2, LANES)
            parts.append(jnp.concatenate([near] + [piece[at, :] for piece in pieces], axis=0))
        block = jnp.concatenate(parts, axis=1)
        pairs[...] += lax.dot_general(block, block, (((1,), (1,)), ((), ())), preferred_element_type=F32)
        return carry

    lax.fori_loop(0, lines // TILE // tiles, step, 0)
    equal = jnp.where(same_line(total), pairs[...], 0.0)
    exact = {"precision": lax.Precision.HIGHEST, "preferred_element_type": F32}
    rows = jnp.sum(equal.reshape(total, TILE, wide), axis=1)
    gram = jnp.dot(rows, owners(total, F32), **exact)
    row = lax.broadcasted_iota(jnp.int32, (total, total), 0)
    col = lax.broadcasted_iota(jnp.int32, (total, total), 1)
    gram = jnp.dot((row == device_at(col, half)).astype(F32), gram, **exact)
    gram = jnp.concatenate([gram, jnp.zeros((total, LANES - total), F32)], axis=1)
    out_ref[...] = jnp.broadcast_to(gram[None], out_ref.shape)


def gram_pieces(near, far, lines, gates, early):
    total = 2 * len(far)
    wide = total * TILE
    return call(
        functools.partial(gram_pieces_body, lines, total),
        "gram_pieces",
        flops=2 * wide * wide * LANES * (lines // TILE),
        moved=2 * total * lines * LANES,
        in_specs=[IN_VMEM] * (1 + len(far)) + [IN_HBM] * len(gates) + [IN_VMEM] * len(early),
        out_specs=IN_VMEM,
        out_shape=jax.ShapeDtypeStruct((total, total, LANES), F32),
        scratch_shapes=[pltpu.VMEM((wide, wide), F32)],
    )(near, *far, *gates, *early)


def block_gradient(load, i, count, observed, precision):
    start = i * BLOCK
    at = lines_of(start, BLOCK)
    shape = (BLOCK // LINE, LINE, LANES)
    lane = lax.broadcasted_iota(jnp.int32, (1, LINE, LANES), 2)
    line = lax.broadcasted_iota(jnp.int32, (1, LINE, LANES), 1)
    obs = observed[at, :].astype(F32).reshape(shape)
    prec = precision[at, :].astype(F32).reshape(shape)
    here = load(start, BLOCK).astype(F32)
    before = load(jnp.where(i == 0, count, start - TILE), TILE).astype(F32)
    after = load(start + BLOCK, TILE).astype(F32)
    above = jnp.concatenate([before[LINE:], here[:-LINE]], axis=0).reshape(shape)
    below = jnp.concatenate([here[LINE:], after[:LINE]], axis=0).reshape(shape)
    field = here.reshape(shape)
    turned = pltpu.roll(field, 1, 2)
    carried = jnp.where(line == 0, 0.0, pltpu.roll(turned, 1, 1))
    left = jnp.where(lane == 0, carried, turned)
    turned = pltpu.roll(field, LANES - 1, 2)
    carried = jnp.where(line == LINE - 1, 0.0, pltpu.roll(turned, LINE - 1, 1))
    right = jnp.where(lane == LANES - 1, carried, turned)
    laplace = (4.0 + mass_term) * field - (below + above + right + left)
    squash = jnp.tanh(field)
    result = prec * (obs - squash) * (1.0 - squash * squash) - prior_scale * laplace
    return result.reshape(BLOCK, LANES).astype(BF16)


def gradient_pieces_body(views, arrays, numbers, *refs):
    observed, precision, *number_refs = refs[arrays : arrays + 2 + numbers]
    out_ref, rows_ref, grads, sems = refs[-4:]
    for n, number_ref in enumerate(number_refs):
        rows_ref[n : n + 1, :] = jnp.full((1, LANES), number_ref[0], F32)
    count = observed.shape[0]
    steps = count // BLOCK

    def store(i):
        at = lines_of(i * BLOCK, BLOCK)
        return pltpu.make_async_copy(grads.at[:, at, :], out_ref.at[:, at, :], sems.at[i])

    def step(i, carry):
        for p, (array, lead, base) in enumerate(views):

            def load(start, size):
                part = lines_of(base + start, size)
                return refs[array][part, :] if lead is None else refs[array][lead, part, :]

            grads[p, lines_of(i * BLOCK, BLOCK), :] = block_gradient(load, i, count, observed, precision)
        store(i).start()
        return carry

    def finish(i, carry):
        store(i).wait()
        return carry

    lax.fori_loop(0, steps, step, 0)
    lax.fori_loop(0, steps, finish, 0)


def gradient_pieces(arrays, views, observed, precision, numbers):
    count = observed.shape[0]
    out = pltpu.HBM((len(views), count, LANES), BF16)
    size = len(views) * count * LANES
    return call(
        functools.partial(gradient_pieces_body, views, len(arrays), len(numbers)),
        "gradient_pieces",
        flops=30 * size,
        moved=8 * size,
        in_specs=[IN_VMEM] * (len(arrays) + 2)
        + [pl.BlockSpec(memory_space=pltpu.SMEM)] * len(numbers),
        out_specs=[IN_HBM, IN_VMEM],
        out_shape=[out, jax.ShapeDtypeStruct((8, LANES), F32)],
        scratch_shapes=[pltpu.VMEM(out.shape, BF16), pltpu.SemaphoreType.DMA((count // BLOCK,))],
    )(*arrays, observed, precision, *numbers)


def raw_body(raw, lines, near_ref, *refs):
    out_ref = refs[-1]
    for k in range(near_ref.shape[0]):
        out_ref[k, :raw, :] = near_ref[k, :raw, :]
        below = near_ref[k, raw : raw + TILE, :].astype(F32)[:LINE]
        above = near_ref[k, lines : lines + TILE, :].astype(F32)[LINE:]
        out_ref[k, raw:, :] = jnp.concatenate([below, above], axis=0).astype(BF16)


def raw_states(near, raw, lines, gates):
    out = jax.ShapeDtypeStruct((near.shape[0], raw + TILE, LANES), BF16)
    return call(
        functools.partial(raw_body, raw, lines),
        "raw_states",
        moved=4 * out.size,
        in_specs=[IN_VMEM] * (1 + len(gates)),
        out_specs=IN_VMEM,
        out_shape=out,
    )(near, *gates)


def mix(mixer, own, numbers_ref, total, states, slopes):
    high = mixer.shape[0]
    rate = numbers_ref[2:3, :1] / total
    coeff = 2.0 * numbers_ref[1:2, :1] / numbers_ref[:1, :1]
    both = jnp.concatenate([slopes, states], axis=1)
    mixed = jnp.dot(mixer[...], both, preferred_element_type=F32)
    drive, pulled = mixed[:, :LANES], mixed[:, LANES:]
    return (states[:high].astype(F32) * own[...] + rate * (drive - coeff * pulled)).astype(BF16)


def update_pieces_body(half, raw, lines, groups, near_ref, *refs):
    total = 2 * half
    far_refs, refs = refs[:half], refs[half:]
    across_ref, raw_observed, raw_precision, numbers_ref, grams_ref, *refs = refs
    group_refs, near_to, far_tos = refs[: len(groups)], refs[len(groups)], refs[len(groups) + 1 : -8]
    near_out, far_out, mixer, own, grads, raw_grads, sems, out_sems = refs[-8:]
    wide = total * TILE
    high = half * TILE
    middle = (raw + 2 * lines) // 3 // BLOCK * BLOCK
    parts = ((0, raw), (raw, middle), (middle, lines))
    fetches = []
    for n, (first, last) in enumerate(parts):
        part = pl.ds(first, last - first)
        fetches.append([])
        for g, (group, group_ref) in enumerate(zip(groups, group_refs)):
            target = grads.at[pl.ds(group[0], len(group)), part, :]
            fetches[n].append(pltpu.make_async_copy(group_ref.at[:, part, :], target, sems.at[g, n]))
            fetches[n][-1].start()

    def raw_gradient(i, carry):
        for k in range(total):

            def load(start, size):
                if k < half:
                    return near_ref[k, lines_of(lines + TILE + start, size), :]
                return across_ref[k - half, lines_of(start, size), :]

            part = lines_of(i * BLOCK, BLOCK)
            raw_grads[k, part, :] = block_gradient(load, i, raw, raw_observed, raw_precision)
        return carry

    lax.fori_loop(0, raw // BLOCK, raw_gradient, 0)
    gram = jnp.sum(grams_ref[...], axis=0)[:, :total]
    spread, anneal, step_size = (numbers_ref[k : k + 1, :1] for k in range(3))
    rate = step_size / total
    coeff = 2.0 * anneal / spread
    row = lax.broadcasted_iota(jnp.int32, (total, total), 0)
    col = lax.broadcasted_iota(jnp.int32, (total, total), 1)
    diagonal = jnp.where(row == col, gram, 0.0)
    down = jnp.sum(diagonal, axis=1, keepdims=True)
    across = jnp.sum(diagonal, axis=0, keepdims=True)
    kernel = jnp.exp(-(down + across - 2.0 * gram) / (spread * NCELL)).astype(BF16)
    owner = owners(total, BF16)
    half_way = jnp.dot(owner, kernel, preferred_element_type=F32).astype(BF16)
    full = lax.dot_general(half_way, owner, (((1,), (1,)), ((), ())), preferred_element_type=F32)
    full = jnp.where(same_line(total), full, 0.0)
    mixer[...] = full.astype(BF16)
    ksum = jnp.sum(full, axis=1, keepdims=True)
    own[...] = jnp.broadcast_to(1.0 + rate * coeff * ksum, (wide, LANES))

    stores = []

    def store(source, target, at):
        stores.append(pltpu.make_async_copy(source, target, out_sems.at[at]))
        stores[-1].start()

    def store_near(first, last, at):
        part = pl.ds(first, last - first)
        store(near_out.at[:, part, :], near_to.at[:, part, :], (half, at))

    def store_far(first, last, at):
        part = pl.ds(first - raw, last - first)
        for x, far_to in enumerate(far_tos):
            store(far_out.at[x, part, :], far_to.at[part, :], (x, at))

    def slab_step(with_far, i, carry):
        rows = wide if with_far else high
        for t in range(BLOCK // TILE):
            at = i * BLOCK + t * TILE
            part = lines_of(at, TILE)
            states = [near_ref[:, part, :].reshape(high, LANES)] + [ref[part, :] for ref in far_refs]
            slopes = grads[:, part, :].reshape(wide, LANES)
            states = jnp.concatenate(states, axis=0)
            new = mix(mixer.at[:rows, :], own.at[:rows, :], numbers_ref, total, states, slopes)
            near_out[:, part, :] = new[:high].reshape(half, TILE, LANES)
            if with_far:
                far_out[:, lines_of(at - raw, TILE), :] = new[high:].reshape(half, TILE, LANES)
        return carry

    here = lax.axis_index("slab").astype(jnp.int32) % half

    def raw_step(i, carry):
        for t in range(BLOCK // TILE):
            at = i * BLOCK + t * TILE
            part = lines_of(at, TILE)
            states = [near_ref[:, lines_of(lines + TILE + at, TILE), :].reshape(high, LANES)]
            slopes = [raw_grads[:half, part, :].reshape(high, LANES)]
            for x in range(half):
                states += [across_ref[here ^ x, part, :]]
                slopes += [raw_grads[half + (here ^ x), part, :]]
            states, slopes = jnp.concatenate(states, axis=0), jnp.concatenate(slopes, axis=0)
            new = mix(mixer.at[:high, :], own.at[:high, :], numbers_ref, total, states, slopes)
            near_out[:, lines_of(lines + at, TILE), :] = new.reshape(half, TILE, LANES)
        return carry

    lax.fori_loop(0, raw // BLOCK, raw_step, 0)
    store_near(lines, lines + raw, 0)
    for n, (first, last) in enumerate(parts):
        for fetch in fetches[n]:
            fetch.wait()
        lax.fori_loop(first // BLOCK, last // BLOCK, functools.partial(slab_step, n > 0), 0)
        store_near(first, last, 1 + n)
        if n:
            store_far(first, last, n - 1)
    for copy in stores:
        copy.wait()


def update_pieces(numbers, grams, near, far, across, raw_fields, grads, groups, raw, lines):
    half = len(far)
    total = 2 * half
    wide = total * TILE
    out_shape = [pltpu.HBM((half, lines + raw, LANES), BF16)]
    out_shape += [pltpu.HBM((lines - raw, LANES), BF16)] * half
    return call(
        functools.partial(update_pieces_body, half, raw, lines, groups),
        "update_pieces",
        flops=4 * wide * wide * LANES * (lines // TILE),
        moved=6 * total * lines * LANES,
        in_specs=[IN_VMEM] * (half + 6) + [IN_HBM] * len(groups),
        out_specs=[IN_HBM] * len(out_shape),
        out_shape=out_shape,
        scratch_shapes=[
            pltpu.VMEM((half, lines + raw, LANES), BF16),
            pltpu.VMEM((half, lines - raw, LANES), BF16),
            pltpu.VMEM((wide, wide), BF16),
            pltpu.VMEM((wide, LANES), F32),
            pltpu.VMEM((total, lines, LANES), BF16),
            pltpu.VMEM((total, raw, LANES), BF16),
            pltpu.SemaphoreType.DMA((len(groups), 3)),
            pltpu.SemaphoreType.DMA((half + 1, 4)),
        ],
    )(near, *far, across, *raw_fields, numbers, grams, *grads)


def exchange(piece, k, slabs):
    return lax.ppermute(piece, "slab", [(i, i ^ k) for i in range(slabs)])


def swap_near(pieces, slabs):
    groups = [list(range(slabs // 2)), list(range(slabs // 2, slabs))]
    return lax.all_to_all(pieces, "slab", 0, 0, axis_index_groups=groups, tiled=True)


RAW = 128
GRADIENTS = ((8, 9, 10, 11), (12, 13, 14, 15), (0, 1, 2, 3, 4, 5, 6, 7))


def by_halves(particles, observed, precision, spread, anneal, step_size):
    slabs = lax.axis_size("slab")
    half = slabs // 2
    lines = NCELL // slabs // LANES
    row = in_hbm(particles)
    fields = [in_hbm(field.reshape(-1, LANES)) for field in (observed, precision)]
    near, *far = split_pieces(row, slabs, RAW, fields)
    far, (obs, prec, *raw_fields) = far[:half], far[half:]
    near = swap_near(near, slabs)
    far = [exchange(piece, half + x, slabs) for x, piece in enumerate(far)]
    raw_near = raw_states(near, RAW, lines, far)
    across = exchange(raw_near, half, slabs)
    grads = []
    numbers = [spread, anneal, step_size]
    for group in GRADIENTS:
        if group[0] < half:
            arrays, views = [near], [(0, k, 0) for k in group]
        else:
            arrays, views = [far[k - half] for k in group], [(j, None, 0) for j in range(len(group))]
        slopes, rows = gradient_pieces(arrays, tuple(views), obs, prec, [] if grads else numbers)
        grads.append(in_hbm(slopes))
        numbers = numbers if len(grads) > 1 else rows
    grams = swap(gram_pieces(near, far, lines, grads[:1], [raw_near]))
    new_near, *new_far = update_pieces(
        numbers, grams, near, far, across, raw_fields, grads, GRADIENTS, RAW, lines
    )
    new_near = swap_near(new_near, slabs)
    new_far = [exchange(piece, half + x, slabs) for x, piece in enumerate(new_far)]
    row = join_pieces(None, slabs, RAW, [new_near], [(0, k, k) for k in range(half)])
    for group in ((0, 1, 2, 3), (4, 5)):
        pieces = [(n, None, half + x) for n, x in enumerate(group)]
        row = join_pieces(row, slabs, RAW, [new_far[x] for x in group], pieces)
    return join_pieces(row, slabs, RAW, new_far[6:], [(n, None, half + 6 + n) for n in range(half - 6)])


def on_device(particles, observed, precision, spread, anneal, step_size):
    slabs = lax.axis_size("slab")
    total = particles.shape[0] * slabs
    lines = NCELL // slabs // LANES
    if slabs == 16:
        return by_halves(particles, observed, precision, spread, anneal, step_size)
    sent, begun = cuts(lines)
    fields = [observed.reshape(-1, LANES), precision.reshape(-1, LANES)]
    numbers = [spread, anneal, step_size]
    first, obs, prec, scalars = split_row(particles, slabs, 0, sent, True, fields, numbers, [])
    parts = [swap(first)]
    if sent < lines:
        parts += [swap(split_row(particles, slabs, sent, lines, False, [], [], [scalars])[0])]
    if total * TILE > 256:
        grads = slab_gradient(parts, obs, prec, lines, 0, lines)
        states = jnp.concatenate([parts[0][:, :sent]] + parts[1:], axis=1)
        new = plain_update(spread, anneal, step_size, states, grads)
        return join_row(swap(new), lines, 0, None)
    if sent == lines:
        grads = slab_gradient(parts, obs, prec, lines, 0, lines)
        grams = swap(slab_gram(parts[0], lines, slabs, [], []))
        new = slab_update(scalars, grams, parts, grads, 0, lines, [])
        return join_row(swap(new), lines, 0, None)
    gram = slab_gram(parts[0], sent, 1, [], [])
    early = slab_gradient(parts[:1], obs, prec, lines, 0, begun)
    grams = swap(slab_gram(parts[1], lines - sent, slabs, [gram], [early]))
    late = slab_gradient(parts, obs, prec, lines, begun, lines)
    new = slab_update(scalars, grams, parts[:1], early, 0, begun, [])
    rest = slab_update(scalars, grams, parts, late, begun, lines, [new])
    row = join_row(swap(new), lines, 0, None)
    return join_row(swap(rest), lines, begun, row)


def solution(mesh):
    in_specs = (
        P(("groups", "slab"), None),
        P("groups"),
        P("groups"),
        P("groups"),
        P("groups"),
        P("groups"),
    )
    out_specs = P(("groups", "slab"), None)
    return jax.shard_map(
        on_device, mesh=mesh, in_specs=in_specs, out_specs=out_specs, check_vma=False
    )
```

```python
import functools

import jax
import jax.numpy as jnp
from jax import lax
from jax.experimental import pallas as pl
from jax.experimental.pallas import tpu as pltpu
from jax.sharding import PartitionSpec as P

GRID_X = 1024
GRID_Y = 1024
NCELL = 1048576
LANES = 128
LINE = GRID_Y // LANES
TILE = 16

prior_scale = 0.25
mass_term = 1.0

F32 = jnp.float32
BF16 = jnp.bfloat16
MIB = 1024 * 1024


def call(body, name, flops=0, moved=0, limit=16, **kwargs):
    return pl.pallas_call(
        body,
        name=name,
        compiler_params=pltpu.CompilerParams(vmem_limit_bytes=limit * MIB),
        cost_estimate=pl.CostEstimate(flops=flops, bytes_accessed=moved, transcendentals=0),
        **kwargs,
    )


IN_VMEM = pl.BlockSpec(memory_space=pltpu.VMEM)
IN_HBM = pl.BlockSpec(memory_space=pltpu.HBM)


def in_hbm(array):
    return pltpu.with_memory_space_constraint(array, pltpu.HBM)


BLOCK = 4 * TILE


def cuts(lines):
    if lines % (8 * BLOCK):
        return lines, lines
    return lines * 3 // 4, lines * 3 // 4 - BLOCK


def split_body(lines, begin, rim, fields, numbers, row_ref, *refs):
    field_refs, number_refs = refs[:fields], refs[fields : fields + numbers]
    out_ref, *slab_refs, rows_ref = refs[-7 - fields : -5]
    held, edges, sems, edge_sems, field_sems = refs[-5:]
    for k, number_ref in enumerate(number_refs):
        rows_ref[k : k + 1, :] = jnp.broadcast_to(number_ref[...].reshape(1, 1), (1, LANES))
    slabs, count, _ = out_ref.shape
    count -= TILE * rim
    size = count * LANES
    cells = lines * LANES

    def part(slab):
        source = row_ref.at[:, pl.ds(slab * cells + begin * LANES, size)]
        return pltpu.make_async_copy(source, held.at[:, pl.ds(slab * size, size)], sems.at[slab])

    def edge(slab):
        source = row_ref.at[:, pl.ds(slab * cells - GRID_Y, GRID_Y)]
        return pltpu.make_async_copy(source, edges.at[:, pl.ds(slab * GRID_Y, GRID_Y)], edge_sems.at[slab])

    def grid_row(ref, start):
        return ref[:, pl.ds(start, GRID_Y)].astype(F32).reshape(LINE, LANES)

    for slab in range(slabs):
        part(slab).start()
        if rim and slab:
            edge(slab).start()
    mine = pl.ds(pl.multiple_of(lax.axis_index("slab") * lines, TILE), lines)
    fetches = [
        pltpu.make_async_copy(source.at[mine, :], target, field_sems.at[k])
        for k, (source, target) in enumerate(zip(field_refs, slab_refs))
    ]
    for fetch in fetches:
        fetch.start()
    part(0).wait()
    outside = jnp.zeros((LINE, LANES), F32)
    for slab in range(slabs):
        if slab + 1 < slabs:
            part(slab + 1).wait()
        out_ref[slab, :count, :] = held[:, pl.ds(slab * size, size)].reshape(count, LANES)
        if rim:
            if slab:
                edge(slab).wait()
            below = grid_row(held, (slab + 1) * size) if slab + 1 < slabs else outside
            above = grid_row(edges, slab * GRID_Y) if slab else outside
            out_ref[slab, count:, :] = jnp.concatenate([below, above], axis=0).astype(BF16)
    for fetch in fetches:
        fetch.wait()


def split_row(row, slabs, begin, end, rim, fields, numbers, earlier):
    lines = row.shape[1] // slabs // LANES
    count = end - begin
    return call(
        functools.partial(split_body, lines, begin, rim, len(fields), len(numbers)),
        "split_row",
        moved=6 * slabs * count * LANES,
        in_specs=[IN_HBM] * (1 + len(fields)) + [IN_VMEM] * len(numbers) + [IN_HBM] * len(earlier),
        out_specs=[IN_VMEM] * (2 + len(fields)),
        out_shape=[jax.ShapeDtypeStruct((slabs, count + TILE * rim, LANES), BF16)]
        + [jax.ShapeDtypeStruct((lines, LANES), BF16)] * len(fields)
        + [jax.ShapeDtypeStruct((8, LANES), F32)],
        scratch_shapes=[
            pltpu.VMEM((1, slabs * count * LANES), BF16),
            pltpu.VMEM((1, slabs * GRID_Y), BF16),
            pltpu.SemaphoreType.DMA((slabs,)),
            pltpu.SemaphoreType.DMA((slabs,)),
            pltpu.SemaphoreType.DMA((2,)),
        ],
    )(row, *fields, *numbers, *earlier)


def join_body(lines, begin, slabs_ref, *refs):
    row_ref, held, sems = refs[-3:]
    slabs, count, _ = slabs_ref.shape
    size = count * LANES
    copies = []
    for slab in range(slabs):
        at = pl.ds(slab * size, size)
        held[:, at] = slabs_ref[slab].reshape(1, size)
        target = row_ref.at[:, pl.ds((slab * lines + begin) * LANES, size)]
        copies.append(pltpu.make_async_copy(held.at[:, at], target, sems.at[slab]))
        copies[-1].start()
    for copy in copies:
        copy.wait()


def join_row(slabs, lines, begin, row):
    total, count, _ = slabs.shape
    begun = [] if row is None else [row]
    return call(
        functools.partial(join_body, lines, begin),
        "join_row",
        moved=6 * slabs.size,
        in_specs=[IN_VMEM] + [IN_HBM] * len(begun),
        out_specs=IN_HBM,
        out_shape=jax.ShapeDtypeStruct((1, total * lines * LANES), BF16),
        input_output_aliases={1: 0} if begun else {},
        scratch_shapes=[pltpu.VMEM((1, slabs.size), BF16), pltpu.SemaphoreType.DMA((total,))],
    )(slabs, *begun)


def same_line(total):
    wide = total * TILE
    row = lax.broadcasted_iota(jnp.int32, (wide, wide), 0)
    col = lax.broadcasted_iota(jnp.int32, (wide, wide), 1)
    return row % TILE == col % TILE


def members(total, dtype):
    wide = total * TILE
    row = lax.broadcasted_iota(jnp.int32, (wide, total), 0)
    col = lax.broadcasted_iota(jnp.int32, (wide, total), 1)
    return (row // TILE == col).astype(dtype)


def gram_body(steps, tiles, parts, states_ref, *refs):
    out_ref, pairs = refs[-2:]
    total = states_ref.shape[0]
    wide = total * TILE
    pairs[...] = jnp.zeros_like(pairs)

    def step(i, carry):
        parts = [
            states_ref[:, pl.ds(pl.multiple_of((i * tiles + t) * TILE, TILE), TILE), :].reshape(wide, LANES)
            for t in range(tiles)
        ]
        block = jnp.concatenate(parts, axis=1)
        pairs[...] += lax.dot_general(block, block, (((1,), (1,)), ((), ())), preferred_element_type=F32)
        return carry

    lax.fori_loop(0, steps, step, 0)
    equal = jnp.where(same_line(total), pairs[...], 0.0)
    rows = jnp.sum(equal.reshape(total, TILE, wide), axis=1)
    gram = jnp.dot(rows, members(total, F32), precision=lax.Precision.HIGHEST, preferred_element_type=F32)
    gram = jnp.concatenate([gram, jnp.zeros((total, LANES - total), F32)], axis=1)
    for part_ref in refs[:parts]:
        gram += part_ref[0]
    out_ref[...] = jnp.broadcast_to(gram[None], out_ref.shape)


def slab_gram(states, lines, copies, parts, earlier):
    total = states.shape[0]
    wide = total * TILE
    tiles = min(8, lines // TILE)
    return call(
        functools.partial(gram_body, lines // TILE // tiles, tiles, len(parts)),
        "slab_gram",
        flops=2 * wide * wide * LANES * (lines // TILE),
        moved=2 * states.size,
        in_specs=[IN_VMEM] * (1 + len(parts)) + [IN_HBM] * len(earlier),
        out_specs=IN_VMEM,
        out_shape=jax.ShapeDtypeStruct((copies, total, LANES), F32),
        scratch_shapes=[pltpu.VMEM((wide, wide), F32)],
    )(states, *parts, *earlier)


def gradient_body(lines, begin, end, parts, *refs):
    observed, precision, out_ref, grads, sems = refs[parts:]
    total = grads.shape[0]
    first = refs[0].shape[1] - TILE
    rows = BLOCK // LINE
    group = 4
    shape = (rows, LINE, LANES)
    lane = lax.broadcasted_iota(jnp.int32, (1, LINE, LANES), 2)
    line = lax.broadcasted_iota(jnp.int32, (1, LINE, LANES), 1)

    def load(particle, at, count):
        ref, at = (refs[0], at) if at < first else (refs[1], at - first)
        return ref[particle, at : at + count, :].astype(F32)

    def rim(particle):
        return refs[0][particle, first:, :].astype(F32)

    stores = []
    for k, at in enumerate(range(begin, end, BLOCK)):
        mine = slice(at - begin, at - begin + BLOCK)
        obs = observed[at : at + BLOCK, :].astype(F32).reshape(shape)
        prec = precision[at : at + BLOCK, :].astype(F32).reshape(shape)

        def step(i, carry):
            for p in range(group):
                particle = i * group + p
                here = load(particle, at, BLOCK)
                before = load(particle, at - TILE, TILE) if at else rim(particle)
                after = load(particle, at + BLOCK, TILE) if at + BLOCK < lines else rim(particle)
                above = jnp.concatenate([before[LINE:], here[:-LINE]], axis=0).reshape(shape)
                below = jnp.concatenate([here[LINE:], after[:LINE]], axis=0).reshape(shape)
                field = here.reshape(shape)
                turned = pltpu.roll(field, 1, 2)
                carried = jnp.where(line == 0, 0.0, pltpu.roll(turned, 1, 1))
                left = jnp.where(lane == 0, carried, turned)
                turned = pltpu.roll(field, LANES - 1, 2)
                carried = jnp.where(line == LINE - 1, 0.0, pltpu.roll(turned, LINE - 1, 1))
                right = jnp.where(lane == LANES - 1, carried, turned)
                laplace = (4.0 + mass_term) * field - (below + above + right + left)
                squash = jnp.tanh(field)
                result = prec * (obs - squash) * (1.0 - squash * squash) - prior_scale * laplace
                grads[particle, mine, :] = result.reshape(BLOCK, LANES).astype(BF16)
            return carry

        lax.fori_loop(0, total // group, step, 0)
        stores.append(pltpu.make_async_copy(grads.at[:, mine, :], out_ref.at[:, mine, :], sems.at[k]))
        stores[-1].start()
    for store in stores:
        store.wait()


def slab_gradient(parts, observed, precision, lines, begin, end):
    total = parts[0].shape[0]
    count = end - begin
    out = jax.ShapeDtypeStruct((total, count, LANES), BF16)
    return call(
        functools.partial(gradient_body, lines, begin, end, len(parts)),
        "slab_gradient",
        flops=30 * out.size,
        moved=8 * out.size,
        in_specs=[IN_VMEM] * (len(parts) + 2),
        out_specs=IN_HBM,
        out_shape=out,
        scratch_shapes=[pltpu.VMEM(out.shape, BF16), pltpu.SemaphoreType.DMA((count // BLOCK,))],
    )(*parts, observed, precision)


def update_body(begin, end, parts, *refs):
    states_refs, refs = refs[:parts], refs[parts:]
    scalars_ref, grams_ref, grads_ref = refs[:3]
    out_ref, grads, mixer, own, sem = refs[-5:]
    total = out_ref.shape[0]
    wide = total * TILE
    fetch = pltpu.make_async_copy(grads_ref, grads, sem)
    fetch.start()
    gram = jnp.sum(grams_ref[...], axis=0)[:, :total]
    row = lax.broadcasted_iota(jnp.int32, (total, total), 0)
    col = lax.broadcasted_iota(jnp.int32, (total, total), 1)
    diagonal = jnp.where(row == col, gram, 0.0)
    down = jnp.sum(diagonal, axis=1, keepdims=True)
    across = jnp.sum(diagonal, axis=0, keepdims=True)
    member = members(total, BF16)
    spread, anneal, step_size = (scalars_ref[k : k + 1, :1] for k in range(3))
    rate = step_size / total
    coeff = 2.0 * anneal / spread
    kernel = jnp.exp(-(down + across - 2.0 * gram) / (spread * NCELL)).astype(BF16)
    ksum = jnp.sum(kernel.astype(F32), axis=1, keepdims=True)
    half = jnp.dot(member, kernel, preferred_element_type=F32).astype(BF16)
    full = lax.dot_general(half, member, (((1,), (1,)), ((), ())), preferred_element_type=F32)
    mixer[...] = jnp.where(same_line(total), full, 0.0).astype(BF16)
    gain = 1.0 + rate * coeff * ksum
    own[...] = jnp.broadcast_to(gain[:, :, None], (total, TILE, LANES)).reshape(wide, LANES)
    fetch.wait()

    done = 0
    for part, states_ref in enumerate(states_refs):
        have = states_ref.shape[1] - (0 if part else TILE)
        low = max(begin - done, 0)
        high = min(end - done, have)
        into = done - begin
        done += have

        def step(i, carry):
            for t in range(BLOCK // TILE):
                at = pl.multiple_of(i * BLOCK + t * TILE, TILE)
                there = pl.ds(pl.multiple_of(at + into, TILE), TILE)
                states = states_ref[:, pl.ds(at, TILE), :].reshape(wide, LANES)
                both = jnp.concatenate([grads[:, there, :].reshape(wide, LANES), states], axis=1)
                mixed = jnp.dot(mixer[...], both, preferred_element_type=F32)
                drive, pulled = mixed[:, :LANES], mixed[:, LANES:]
                new = states.astype(F32) * own[...] + rate * (drive - coeff * pulled)
                out_ref[:, there, :] = new.astype(BF16).reshape(total, TILE, LANES)
            return carry

        lax.fori_loop(low // BLOCK, high // BLOCK, step, 0)


def slab_update(scalars, grams, parts, grads, begin, end, earlier):
    total, count, _ = grads.shape
    wide = total * TILE
    return call(
        functools.partial(update_body, begin, end, len(parts)),
        "slab_update",
        flops=4 * wide * wide * LANES * (count // TILE),
        moved=6 * grads.size,
        in_specs=[IN_VMEM] * len(parts)
        + [IN_VMEM, IN_VMEM, IN_HBM]
        + [IN_HBM] * len(earlier),
        out_specs=IN_VMEM,
        out_shape=jax.ShapeDtypeStruct(grads.shape, BF16),
        scratch_shapes=[
            pltpu.VMEM(grads.shape, BF16),
            pltpu.VMEM((wide, wide), BF16),
            pltpu.VMEM((wide, LANES), F32),
            pltpu.SemaphoreType.DMA,
        ],
    )(*parts, scalars, grams, grads, *earlier)


def plain_update(spread, anneal, step_size, states, grads):
    total, lines, _ = grads.shape
    flat = states[:, :lines].reshape(total, -1)
    gram = lax.dot_general(flat, flat, (((1,), (1,)), ((), ())), preferred_element_type=F32)
    gram = lax.psum(gram, "slab")
    norms = jnp.diagonal(gram)
    kernel = jnp.exp(-(norms[:, None] + norms[None, :] - 2.0 * gram) / (spread[0] * NCELL)).astype(BF16)
    ksum = jnp.sum(kernel.astype(F32), axis=1)
    drive = jnp.dot(kernel, grads.reshape(total, -1), preferred_element_type=F32)
    pulled = jnp.dot(kernel, flat, preferred_element_type=F32)
    values = flat.astype(F32)
    repel = values * ksum[:, None] - pulled
    coeff = 2.0 * anneal[0] / spread[0]
    new = values + step_size[0] / total * (drive + coeff * repel)
    return new.astype(BF16).reshape(grads.shape)


def swap(slabs):
    return lax.all_to_all(slabs, "slab", split_axis=0, concat_axis=0, tiled=True)


def device_at(at, half):
    me = lax.axis_index("slab").astype(jnp.int32)
    return jnp.where(at < half, me - me % half + at, me ^ at)


def lines_of(start, count):
    return pl.ds(pl.multiple_of(start, TILE), count)


def split_pieces_body(slabs, raw, lines, fields, row_ref, *refs):
    half = slabs // 2
    field_refs, near_out, far_outs = refs[:fields], refs[fields], refs[fields + 1 : fields + 1 + half]
    slab_refs, held, sems = refs[fields + 1 + half : -2], refs[-2], refs[-1]
    cells = lines * LANES
    end = row_ref.shape[1]
    me = lax.axis_index("slab").astype(jnp.int32)
    copies = []
    for slab in range(slabs):
        part = pl.ds(slab * cells, cells)
        copies.append(pltpu.make_async_copy(row_ref.at[:, part], held.at[:, part], sems.at[slab]))
    for n, target in enumerate(slab_refs):
        start = (me if n < fields else me ^ half) * lines
        source = field_refs[n % fields].at[lines_of(start, target.shape[0]), :]
        copies.append(pltpu.make_async_copy(source, target, sems.at[slabs + n]))
    for copy in copies:
        copy.start()
    for copy in copies[:slabs]:
        copy.wait()

    def part(start, size):
        return held[:, pl.ds(pl.multiple_of(start, GRID_Y), size)]

    def grid_row(start):
        return part(start, GRID_Y).astype(F32).reshape(LINE, LANES)

    for at in range(slabs):
        out_ref = near_out.at[at] if at < half else far_outs[at - half]
        slab = device_at(at, half)
        start = slab * cells
        out_ref[:lines, :] = part(start, cells).reshape(lines, LANES)
        below = jnp.where(slab == slabs - 1, 0.0, grid_row(jnp.minimum(start + cells, end - GRID_Y)))
        above = jnp.where(slab == 0, 0.0, grid_row(jnp.maximum(start - GRID_Y, 0)))
        out_ref[lines : lines + TILE, :] = jnp.concatenate([below, above], axis=0).astype(BF16)
        if at < half:
            start = (slab ^ half) * cells
            to = lines + TILE
            out_ref[to : to + raw, :] = part(start, raw * LANES).reshape(raw, LANES)
            below = grid_row(start + raw * LANES)
            above = jnp.where(slab ^ half == 0, 0.0, grid_row(jnp.maximum(start - GRID_Y, 0)))
            out_ref[to + raw :, :] = jnp.concatenate([below, above], axis=0).astype(BF16)
    for copy in copies[slabs:]:
        copy.wait()


def split_pieces(row, slabs, raw, fields):
    lines = row.shape[1] // slabs // LANES
    half = slabs // 2
    rim = lines + TILE
    size = rim + raw + TILE
    out_shape = [jax.ShapeDtypeStruct((half, size, LANES), BF16)]
    out_shape += [jax.ShapeDtypeStruct((rim, LANES), BF16)] * half
    out_shape += [jax.ShapeDtypeStruct((lines, LANES), BF16)] * len(fields)
    out_shape += [jax.ShapeDtypeStruct((raw, LANES), BF16)] * len(fields)
    return call(
        functools.partial(split_pieces_body, slabs, raw, lines, len(fields)),
        "split_pieces",
        moved=6 * half * (rim + size) * LANES,
        in_specs=[IN_HBM] * (1 + len(fields)),
        out_specs=[IN_VMEM] * len(out_shape),
        out_shape=out_shape,
        scratch_shapes=[pltpu.VMEM(row.shape, BF16), pltpu.SemaphoreType.DMA((slabs + 2 * len(fields),))],
    )(row, *fields)


def join_pieces_body(pieces, half, raw, lines, begun, arrays, *refs):
    row_ref, helds, sems = refs[begun + arrays], refs[begun + arrays + 1 : -1], refs[-1]
    cells = lines * LANES
    skip = raw * LANES
    copies = []
    for (array, lead, at), held in zip(pieces, helds):
        ref = refs[begun + array]
        piece = ref[...] if lead is None else ref[lead]
        held[...] = piece.reshape(held.shape)
        slab = device_at(at, half)
        if at < half:
            parts = [(0, cells, slab * cells), (cells, skip, (slab ^ half) * cells)]
        else:
            parts = [(0, cells - skip, slab * cells + skip)]
        for begin, size, start in parts:
            target = row_ref.at[:, pl.ds(pl.multiple_of(start, GRID_Y), size)]
            copies.append(pltpu.make_async_copy(held.at[:, pl.ds(begin, size)], target, sems.at[len(copies)]))
            copies[-1].start()
    for copy in copies:
        copy.wait()


def join_pieces(row, slabs, raw, arrays, pieces):
    sizes = [arrays[piece[0]].shape[-2] * LANES for piece in pieces]
    begun = [] if row is None else [row]
    return call(
        functools.partial(
            join_pieces_body, pieces, slabs // 2, raw, NCELL // slabs // LANES, len(begun), len(arrays)
        ),
        "join_pieces",
        moved=6 * sum(sizes),
        in_specs=[IN_HBM] * len(begun) + [IN_VMEM] * len(arrays),
        out_specs=IN_HBM,
        out_shape=jax.ShapeDtypeStruct((1, NCELL), BF16),
        input_output_aliases={0: 0} if begun else {},
        scratch_shapes=[pltpu.VMEM((1, size), BF16) for size in sizes]
        + [pltpu.SemaphoreType.DMA((2 * len(sizes),))],
    )(*begun, *arrays)


def owners(total, dtype):
    wide = total * TILE
    row = lax.broadcasted_iota(jnp.int32, (wide, total), 0)
    col = lax.broadcasted_iota(jnp.int32, (wide, total), 1)
    return (device_at(row // TILE, total // 2) == col).astype(dtype)


def gram_pieces_body(lines, total, near_ref, *refs):
    half = total // 2
    pieces, out_ref, pairs = refs[:half], refs[-2], refs[-1]
    wide = total * TILE
    tiles = 8
    pairs[...] = jnp.zeros_like(pairs)

    def step(i, carry):
        parts = []
        for t in range(tiles):
            at = lines_of((i * tiles + t) * TILE, TILE)
            near = near_ref[:, at, :].reshape(wide // 2, LANES)
            parts.append(jnp.concatenate([near] + [piece[at, :] for piece in pieces], axis=0))
        block = jnp.concatenate(parts, axis=1)
        pairs[...] += lax.dot_general(block, block, (((1,), (1,)), ((), ())), preferred_element_type=F32)
        return carry

    lax.fori_loop(0, lines // TILE // tiles, step, 0)
    equal = jnp.where(same_line(total), pairs[...], 0.0)
    exact = {"precision": lax.Precision.HIGHEST, "preferred_element_type": F32}
    rows = jnp.sum(equal.reshape(total, TILE, wide), axis=1)
    gram = jnp.dot(rows, owners(total, F32), **exact)
    row = lax.broadcasted_iota(jnp.int32, (total, total), 0)
    col = lax.broadcasted_iota(jnp.int32, (total, total), 1)
    gram = jnp.dot((row == device_at(col, half)).astype(F32), gram, **exact)
    gram = jnp.concatenate([gram, jnp.zeros((total, LANES - total), F32)], axis=1)
    out_ref[...] = jnp.broadcast_to(gram[None], out_ref.shape)


def gram_pieces(near, far, lines, gates, early):
    total = 2 * len(far)
    wide = total * TILE
    return call(
        functools.partial(gram_pieces_body, lines, total),
        "gram_pieces",
        flops=2 * wide * wide * LANES * (lines // TILE),
        moved=2 * total * lines * LANES,
        in_specs=[IN_VMEM] * (1 + len(far)) + [IN_HBM] * len(gates) + [IN_VMEM] * len(early),
        out_specs=IN_VMEM,
        out_shape=jax.ShapeDtypeStruct((total, total, LANES), F32),
        scratch_shapes=[pltpu.VMEM((wide, wide), F32)],
    )(near, *far, *gates, *early)


def block_gradient(load, i, count, observed, precision):
    start = i * BLOCK
    at = lines_of(start, BLOCK)
    shape = (BLOCK // LINE, LINE, LANES)
    lane = lax.broadcasted_iota(jnp.int32, (1, LINE, LANES), 2)
    line = lax.broadcasted_iota(jnp.int32, (1, LINE, LANES), 1)
    obs = observed[at, :].astype(F32).reshape(shape)
    prec = precision[at, :].astype(F32).reshape(shape)
    here = load(start, BLOCK).astype(F32)
    before = load(jnp.where(i == 0, count, start - TILE), TILE).astype(F32)
    after = load(start + BLOCK, TILE).astype(F32)
    above = jnp.concatenate([before[LINE:], here[:-LINE]], axis=0).reshape(shape)
    below = jnp.concatenate([here[LINE:], after[:LINE]], axis=0).reshape(shape)
    field = here.reshape(shape)
    turned = pltpu.roll(field, 1, 2)
    carried = jnp.where(line == 0, 0.0, pltpu.roll(turned, 1, 1))
    left = jnp.where(lane == 0, carried, turned)
    turned = pltpu.roll(field, LANES - 1, 2)
    carried = jnp.where(line == LINE - 1, 0.0, pltpu.roll(turned, LINE - 1, 1))
    right = jnp.where(lane == LANES - 1, carried, turned)
    laplace = (4.0 + mass_term) * field - (below + above + right + left)
    squash = jnp.tanh(field)
    result = prec * (obs - squash) * (1.0 - squash * squash) - prior_scale * laplace
    return result.reshape(BLOCK, LANES).astype(BF16)


def gradient_pieces_body(views, arrays, numbers, *refs):
    observed, precision, *number_refs = refs[arrays : arrays + 2 + numbers]
    out_ref, rows_ref, grads, sems = refs[-4:]
    for n, number_ref in enumerate(number_refs):
        rows_ref[n : n + 1, :] = jnp.full((1, LANES), number_ref[0], F32)
    count = observed.shape[0]
    steps = count // BLOCK

    def store(i):
        at = lines_of(i * BLOCK, BLOCK)
        return pltpu.make_async_copy(grads.at[:, at, :], out_ref.at[:, at, :], sems.at[i])

    def step(i, carry):
        for p, (array, lead, base) in enumerate(views):

            def load(start, size):
                part = lines_of(base + start, size)
                return refs[array][part, :] if lead is None else refs[array][lead, part, :]

            grads[p, lines_of(i * BLOCK, BLOCK), :] = block_gradient(load, i, count, observed, precision)
        store(i).start()
        return carry

    def finish(i, carry):
        store(i).wait()
        return carry

    lax.fori_loop(0, steps, step, 0)
    lax.fori_loop(0, steps, finish, 0)


def gradient_pieces(arrays, views, observed, precision, numbers):
    count = observed.shape[0]
    out = pltpu.HBM((len(views), count, LANES), BF16)
    size = len(views) * count * LANES
    return call(
        functools.partial(gradient_pieces_body, views, len(arrays), len(numbers)),
        "gradient_pieces",
        flops=30 * size,
        moved=8 * size,
        in_specs=[IN_VMEM] * (len(arrays) + 2)
        + [pl.BlockSpec(memory_space=pltpu.SMEM)] * len(numbers),
        out_specs=[IN_HBM, IN_VMEM],
        out_shape=[out, jax.ShapeDtypeStruct((8, LANES), F32)],
        scratch_shapes=[pltpu.VMEM(out.shape, BF16), pltpu.SemaphoreType.DMA((count // BLOCK,))],
    )(*arrays, observed, precision, *numbers)


def raw_body(raw, lines, near_ref, *refs):
    out_ref = refs[-1]
    for k in range(near_ref.shape[0]):
        out_ref[k, :raw, :] = near_ref[k, :raw, :]
        below = near_ref[k, raw : raw + TILE, :].astype(F32)[:LINE]
        above = near_ref[k, lines : lines + TILE, :].astype(F32)[LINE:]
        out_ref[k, raw:, :] = jnp.concatenate([below, above], axis=0).astype(BF16)


def raw_states(near, raw, lines, gates):
    out = jax.ShapeDtypeStruct((near.shape[0], raw + TILE, LANES), BF16)
    return call(
        functools.partial(raw_body, raw, lines),
        "raw_states",
        moved=4 * out.size,
        in_specs=[IN_VMEM] * (1 + len(gates)),
        out_specs=IN_VMEM,
        out_shape=out,
    )(near, *gates)


def mix(mixer, own, numbers_ref, total, states, slopes):
    high = mixer.shape[0]
    rate = numbers_ref[2:3, :1] / total
    coeff = 2.0 * numbers_ref[1:2, :1] / numbers_ref[:1, :1]
    both = jnp.concatenate([slopes, states], axis=1)
    mixed = jnp.dot(mixer[...], both, preferred_element_type=F32)
    drive, pulled = mixed[:, :LANES], mixed[:, LANES:]
    return (states[:high].astype(F32) * own[...] + rate * (drive - coeff * pulled)).astype(BF16)


def update_pieces_body(half, raw, lines, groups, near_ref, *refs):
    total = 2 * half
    far_refs, refs = refs[:half], refs[half:]
    across_ref, raw_observed, raw_precision, numbers_ref, grams_ref, *refs = refs
    group_refs, near_to, far_tos = refs[: len(groups)], refs[len(groups)], refs[len(groups) + 1 : -8]
    near_out, far_out, mixer, own, grads, raw_grads, sems, out_sems = refs[-8:]
    wide = total * TILE
    high = half * TILE
    middle = (raw + 2 * lines) // 3 // BLOCK * BLOCK
    parts = ((0, raw), (raw, middle), (middle, lines))
    fetches = []
    for n, (first, last) in enumerate(parts):
        part = pl.ds(first, last - first)
        fetches.append([])
        for g, (group, group_ref) in enumerate(zip(groups, group_refs)):
            target = grads.at[pl.ds(group[0], len(group)), part, :]
            fetches[n].append(pltpu.make_async_copy(group_ref.at[:, part, :], target, sems.at[g, n]))
            fetches[n][-1].start()

    def raw_gradient(i, carry):
        for k in range(total):

            def load(start, size):
                if k < half:
                    return near_ref[k, lines_of(lines + TILE + start, size), :]
                return across_ref[k - half, lines_of(start, size), :]

            part = lines_of(i * BLOCK, BLOCK)
            raw_grads[k, part, :] = block_gradient(load, i, raw, raw_observed, raw_precision)
        return carry

    lax.fori_loop(0, raw // BLOCK, raw_gradient, 0)
    gram = jnp.sum(grams_ref[...], axis=0)[:, :total]
    spread, anneal, step_size = (numbers_ref[k : k + 1, :1] for k in range(3))
    rate = step_size / total
    coeff = 2.0 * anneal / spread
    row = lax.broadcasted_iota(jnp.int32, (total, total), 0)
    col = lax.broadcasted_iota(jnp.int32, (total, total), 1)
    diagonal = jnp.where(row == col, gram, 0.0)
    down = jnp.sum(diagonal, axis=1, keepdims=True)
    across = jnp.sum(diagonal, axis=0, keepdims=True)
    kernel = jnp.exp(-(down + across - 2.0 * gram) / (spread * NCELL)).astype(BF16)
    owner = owners(total, BF16)
    half_way = jnp.dot(owner, kernel, preferred_element_type=F32).astype(BF16)
    full = lax.dot_general(half_way, owner, (((1,), (1,)), ((), ())), preferred_element_type=F32)
    full = jnp.where(same_line(total), full, 0.0)
    mixer[...] = full.astype(BF16)
    ksum = jnp.sum(full, axis=1, keepdims=True)
    own[...] = jnp.broadcast_to(1.0 + rate * coeff * ksum, (wide, LANES))

    stores = []

    def store(source, target, at):
        stores.append(pltpu.make_async_copy(source, target, out_sems.at[at]))
        stores[-1].start()

    def store_near(first, last, at):
        part = pl.ds(first, last - first)
        store(near_out.at[:, part, :], near_to.at[:, part, :], (half, at))

    def store_far(first, last, at):
        part = pl.ds(first - raw, last - first)
        for x, far_to in enumerate(far_tos):
            store(far_out.at[x, part, :], far_to.at[part, :], (x, at))

    def slab_step(with_far, i, carry):
        rows = wide if with_far else high
        for t in range(BLOCK // TILE):
            at = i * BLOCK + t * TILE
            part = lines_of(at, TILE)
            states = [near_ref[:, part, :].reshape(high, LANES)] + [ref[part, :] for ref in far_refs]
            slopes = grads[:, part, :].reshape(wide, LANES)
            states = jnp.concatenate(states, axis=0)
            new = mix(mixer.at[:rows, :], own.at[:rows, :], numbers_ref, total, states, slopes)
            near_out[:, part, :] = new[:high].reshape(half, TILE, LANES)
            if with_far:
                far_out[:, lines_of(at - raw, TILE), :] = new[high:].reshape(half, TILE, LANES)
        return carry

    here = lax.axis_index("slab").astype(jnp.int32) % half

    def raw_step(i, carry):
        for t in range(BLOCK // TILE):
            at = i * BLOCK + t * TILE
            part = lines_of(at, TILE)
            states = [near_ref[:, lines_of(lines + TILE + at, TILE), :].reshape(high, LANES)]
            slopes = [raw_grads[:half, part, :].reshape(high, LANES)]
            for x in range(half):
                states += [across_ref[here ^ x, part, :]]
                slopes += [raw_grads[half + (here ^ x), part, :]]
            states, slopes = jnp.concatenate(states, axis=0), jnp.concatenate(slopes, axis=0)
            new = mix(mixer.at[:high, :], own.at[:high, :], numbers_ref, total, states, slopes)
            near_out[:, lines_of(lines + at, TILE), :] = new.reshape(half, TILE, LANES)
        return carry

    lax.fori_loop(0, raw // BLOCK, raw_step, 0)
    store_near(lines, lines + raw, 0)
    for n, (first, last) in enumerate(parts):
        for fetch in fetches[n]:
            fetch.wait()
        lax.fori_loop(first // BLOCK, last // BLOCK, functools.partial(slab_step, n > 0), 0)
        store_near(first, last, 1 + n)
        if n:
            store_far(first, last, n - 1)
    for copy in stores:
        copy.wait()


def update_pieces(numbers, grams, near, far, across, raw_fields, grads, groups, raw, lines):
    half = len(far)
    total = 2 * half
    wide = total * TILE
    out_shape = [pltpu.HBM((half, lines + raw, LANES), BF16)]
    out_shape += [pltpu.HBM((lines - raw, LANES), BF16)] * half
    return call(
        functools.partial(update_pieces_body, half, raw, lines, groups),
        "update_pieces",
        flops=4 * wide * wide * LANES * (lines // TILE),
        moved=6 * total * lines * LANES,
        in_specs=[IN_VMEM] * (half + 6) + [IN_HBM] * len(groups),
        out_specs=[IN_HBM] * len(out_shape),
        out_shape=out_shape,
        scratch_shapes=[
            pltpu.VMEM((half, lines + raw, LANES), BF16),
            pltpu.VMEM((half, lines - raw, LANES), BF16),
            pltpu.VMEM((wide, wide), BF16),
            pltpu.VMEM((wide, LANES), F32),
            pltpu.VMEM((total, lines, LANES), BF16),
            pltpu.VMEM((total, raw, LANES), BF16),
            pltpu.SemaphoreType.DMA((len(groups), 3)),
            pltpu.SemaphoreType.DMA((half + 1, 4)),
        ],
    )(near, *far, across, *raw_fields, numbers, grams, *grads)


def exchange(piece, k, slabs):
    return lax.ppermute(piece, "slab", [(i, i ^ k) for i in range(slabs)])


def swap_near(pieces, slabs):
    groups = [list(range(slabs // 2)), list(range(slabs // 2, slabs))]
    return lax.all_to_all(pieces, "slab", 0, 0, axis_index_groups=groups, tiled=True)


RAW = 128
GRADIENTS = ((8, 9, 10, 11), (12, 13, 14, 15), (0, 1, 2, 3, 4, 5, 6, 7))


def by_halves(particles, observed, precision, spread, anneal, step_size):
    slabs = lax.axis_size("slab")
    half = slabs // 2
    lines = NCELL // slabs // LANES
    row = in_hbm(particles)
    fields = [in_hbm(field.reshape(-1, LANES)) for field in (observed, precision)]
    near, *far = split_pieces(row, slabs, RAW, fields)
    far, (obs, prec, *raw_fields) = far[:half], far[half:]
    near = swap_near(near, slabs)
    far = [exchange(piece, half + x, slabs) for x, piece in enumerate(far)]
    raw_near = raw_states(near, RAW, lines, far[:-1])
    across = exchange(raw_near, half, slabs)
    grads = []
    numbers = [spread, anneal, step_size]
    for group in GRADIENTS:
        if group[0] < half:
            arrays, views = [near], [(0, k, 0) for k in group]
        else:
            arrays, views = [far[k - half] for k in group], [(j, None, 0) for j in range(len(group))]
        slopes, rows = gradient_pieces(arrays, tuple(views), obs, prec, [] if grads else numbers)
        grads.append(in_hbm(slopes))
        numbers = numbers if len(grads) > 1 else rows
    grams = swap(gram_pieces(near, far, lines, grads[:1], [raw_near]))
    new_near, *new_far = update_pieces(
        numbers, grams, near, far, across, raw_fields, grads, GRADIENTS, RAW, lines
    )
    new_near = swap_near(new_near, slabs)
    new_far = [exchange(piece, half + x, slabs) for x, piece in enumerate(new_far)]
    row = join_pieces(None, slabs, RAW, [new_near], [(0, k, k) for k in range(half)])
    for group in ((0, 1, 2, 3), (4, 5)):
        pieces = [(n, None, half + x) for n, x in enumerate(group)]
        row = join_pieces(row, slabs, RAW, [new_far[x] for x in group], pieces)
    return join_pieces(row, slabs, RAW, new_far[6:], [(n, None, half + 6 + n) for n in range(half - 6)])


def on_device(particles, observed, precision, spread, anneal, step_size):
    slabs = lax.axis_size("slab")
    total = particles.shape[0] * slabs
    lines = NCELL // slabs // LANES
    if slabs == 16:
        return by_halves(particles, observed, precision, spread, anneal, step_size)
    sent, begun = cuts(lines)
    fields = [observed.reshape(-1, LANES), precision.reshape(-1, LANES)]
    numbers = [spread, anneal, step_size]
    first, obs, prec, scalars = split_row(particles, slabs, 0, sent, True, fields, numbers, [])
    parts = [swap(first)]
    if sent < lines:
        parts += [swap(split_row(particles, slabs, sent, lines, False, [], [], [scalars])[0])]
    if total * TILE > 256:
        grads = slab_gradient(parts, obs, prec, lines, 0, lines)
        states = jnp.concatenate([parts[0][:, :sent]] + parts[1:], axis=1)
        new = plain_update(spread, anneal, step_size, states, grads)
        return join_row(swap(new), lines, 0, None)
    if sent == lines:
        grads = slab_gradient(parts, obs, prec, lines, 0, lines)
        grams = swap(slab_gram(parts[0], lines, slabs, [], []))
        new = slab_update(scalars, grams, parts, grads, 0, lines, [])
        return join_row(swap(new), lines, 0, None)
    gram = slab_gram(parts[0], sent, 1, [], [])
    early = slab_gradient(parts[:1], obs, prec, lines, 0, begun)
    grams = swap(slab_gram(parts[1], lines - sent, slabs, [gram], [early]))
    late = slab_gradient(parts, obs, prec, lines, begun, lines)
    new = slab_update(scalars, grams, parts[:1], early, 0, begun, [])
    rest = slab_update(scalars, grams, parts, late, begun, lines, [new])
    row = join_row(swap(new), lines, 0, None)
    return join_row(swap(rest), lines, begun, row)


def solution(mesh):
    in_specs = (
        P(("groups", "slab"), None),
        P("groups"),
        P("groups"),
        P("groups"),
        P("groups"),
        P("groups"),
    )
    out_specs = P(("groups", "slab"), None)
    return jax.shard_map(
        on_device, mesh=mesh, in_specs=in_specs, out_specs=out_specs, check_vma=False
    )
```

```python
import functools

import jax
import jax.numpy as jnp
from jax import lax
from jax.experimental import pallas as pl
from jax.experimental.pallas import tpu as pltpu
from jax.sharding import PartitionSpec as P

GRID_X = 1024
GRID_Y = 1024
NCELL = 1048576
LANES = 128
LINE = GRID_Y // LANES
TILE = 16

prior_scale = 0.25
mass_term = 1.0

F32 = jnp.float32
BF16 = jnp.bfloat16
MIB = 1024 * 1024


def call(body, name, flops=0, moved=0, limit=16, **kwargs):
    return pl.pallas_call(
        body,
        name=name,
        compiler_params=pltpu.CompilerParams(vmem_limit_bytes=limit * MIB),
        cost_estimate=pl.CostEstimate(flops=flops, bytes_accessed=moved, transcendentals=0),
        **kwargs,
    )


IN_VMEM = pl.BlockSpec(memory_space=pltpu.VMEM)
IN_HBM = pl.BlockSpec(memory_space=pltpu.HBM)


def in_hbm(array):
    return pltpu.with_memory_space_constraint(array, pltpu.HBM)


BLOCK = 4 * TILE


def cuts(lines):
    if lines % (8 * BLOCK):
        return lines, lines
    return lines * 3 // 4, lines * 3 // 4 - BLOCK


def split_body(lines, begin, rim, fields, numbers, row_ref, *refs):
    field_refs, number_refs = refs[:fields], refs[fields : fields + numbers]
    out_ref, *slab_refs, rows_ref = refs[-7 - fields : -5]
    held, edges, sems, edge_sems, field_sems = refs[-5:]
    for k, number_ref in enumerate(number_refs):
        rows_ref[k : k + 1, :] = jnp.broadcast_to(number_ref[...].reshape(1, 1), (1, LANES))
    slabs, count, _ = out_ref.shape
    count -= TILE * rim
    size = count * LANES
    cells = lines * LANES

    def part(slab):
        source = row_ref.at[:, pl.ds(slab * cells + begin * LANES, size)]
        return pltpu.make_async_copy(source, held.at[:, pl.ds(slab * size, size)], sems.at[slab])

    def edge(slab):
        source = row_ref.at[:, pl.ds(slab * cells - GRID_Y, GRID_Y)]
        return pltpu.make_async_copy(source, edges.at[:, pl.ds(slab * GRID_Y, GRID_Y)], edge_sems.at[slab])

    def grid_row(ref, start):
        return ref[:, pl.ds(start, GRID_Y)].astype(F32).reshape(LINE, LANES)

    for slab in range(slabs):
        part(slab).start()
        if rim and slab:
            edge(slab).start()
    mine = pl.ds(pl.multiple_of(lax.axis_index("slab") * lines, TILE), lines)
    fetches = [
        pltpu.make_async_copy(source.at[mine, :], target, field_sems.at[k])
        for k, (source, target) in enumerate(zip(field_refs, slab_refs))
    ]
    for fetch in fetches:
        fetch.start()
    part(0).wait()
    outside = jnp.zeros((LINE, LANES), F32)
    for slab in range(slabs):
        if slab + 1 < slabs:
            part(slab + 1).wait()
        out_ref[slab, :count, :] = held[:, pl.ds(slab * size, size)].reshape(count, LANES)
        if rim:
            if slab:
                edge(slab).wait()
            below = grid_row(held, (slab + 1) * size) if slab + 1 < slabs else outside
            above = grid_row(edges, slab * GRID_Y) if slab else outside
            out_ref[slab, count:, :] = jnp.concatenate([below, above], axis=0).astype(BF16)
    for fetch in fetches:
        fetch.wait()


def split_row(row, slabs, begin, end, rim, fields, numbers, earlier):
    lines = row.shape[1] // slabs // LANES
    count = end - begin
    return call(
        functools.partial(split_body, lines, begin, rim, len(fields), len(numbers)),
        "split_row",
        moved=6 * slabs * count * LANES,
        in_specs=[IN_HBM] * (1 + len(fields)) + [IN_VMEM] * len(numbers) + [IN_HBM] * len(earlier),
        out_specs=[IN_VMEM] * (2 + len(fields)),
        out_shape=[jax.ShapeDtypeStruct((slabs, count + TILE * rim, LANES), BF16)]
        + [jax.ShapeDtypeStruct((lines, LANES), BF16)] * len(fields)
        + [jax.ShapeDtypeStruct((8, LANES), F32)],
        scratch_shapes=[
            pltpu.VMEM((1, slabs * count * LANES), BF16),
            pltpu.VMEM((1, slabs * GRID_Y), BF16),
            pltpu.SemaphoreType.DMA((slabs,)),
            pltpu.SemaphoreType.DMA((slabs,)),
            pltpu.SemaphoreType.DMA((2,)),
        ],
    )(row, *fields, *numbers, *earlier)


def join_body(lines, begin, slabs_ref, *refs):
    row_ref, held, sems = refs[-3:]
    slabs, count, _ = slabs_ref.shape
    size = count * LANES
    copies = []
    for slab in range(slabs):
        at = pl.ds(slab * size, size)
        held[:, at] = slabs_ref[slab].reshape(1, size)
        target = row_ref.at[:, pl.ds((slab * lines + begin) * LANES, size)]
        copies.append(pltpu.make_async_copy(held.at[:, at], target, sems.at[slab]))
        copies[-1].start()
    for copy in copies:
        copy.wait()


def join_row(slabs, lines, begin, row):
    total, count, _ = slabs.shape
    begun = [] if row is None else [row]
    return call(
        functools.partial(join_body, lines, begin),
        "join_row",
        moved=6 * slabs.size,
        in_specs=[IN_VMEM] + [IN_HBM] * len(begun),
        out_specs=IN_HBM,
        out_shape=jax.ShapeDtypeStruct((1, total * lines * LANES), BF16),
        input_output_aliases={1: 0} if begun else {},
        scratch_shapes=[pltpu.VMEM((1, slabs.size), BF16), pltpu.SemaphoreType.DMA((total,))],
    )(slabs, *begun)


def same_line(total):
    wide = total * TILE
    row = lax.broadcasted_iota(jnp.int32, (wide, wide), 0)
    col = lax.broadcasted_iota(jnp.int32, (wide, wide), 1)
    return (row ^ col) & (TILE - 1) == 0


def members(total, dtype):
    wide = total * TILE
    row = lax.broadcasted_iota(jnp.int32, (wide, total), 0)
    col = lax.broadcasted_iota(jnp.int32, (wide, total), 1)
    return (row // TILE == col).astype(dtype)


def gram_body(steps, tiles, parts, states_ref, *refs):
    out_ref, pairs = refs[-2:]
    total = states_ref.shape[0]
    wide = total * TILE
    pairs[...] = jnp.zeros_like(pairs)

    def step(i, carry):
        parts = [
            states_ref[:, pl.ds(pl.multiple_of((i * tiles + t) * TILE, TILE), TILE), :].reshape(wide, LANES)
            for t in range(tiles)
        ]
        block = jnp.concatenate(parts, axis=1)
        pairs[...] += lax.dot_general(block, block, (((1,), (1,)), ((), ())), preferred_element_type=F32)
        return carry

    lax.fori_loop(0, steps, step, 0)
    equal = jnp.where(same_line(total), pairs[...], 0.0)
    rows = jnp.sum(equal.reshape(total, TILE, wide), axis=1)
    gram = jnp.dot(rows, members(total, F32), precision=lax.Precision.HIGHEST, preferred_element_type=F32)
    gram = jnp.concatenate([gram, jnp.zeros((total, LANES - total), F32)], axis=1)
    for part_ref in refs[:parts]:
        gram += part_ref[0]
    out_ref[...] = jnp.broadcast_to(gram[None], out_ref.shape)


def slab_gram(states, lines, copies, parts, earlier):
    total = states.shape[0]
    wide = total * TILE
    tiles = min(8, lines // TILE)
    return call(
        functools.partial(gram_body, lines // TILE // tiles, tiles, len(parts)),
        "slab_gram",
        flops=2 * wide * wide * LANES * (lines // TILE),
        moved=2 * states.size,
        in_specs=[IN_VMEM] * (1 + len(parts)) + [IN_HBM] * len(earlier),
        out_specs=IN_VMEM,
        out_shape=jax.ShapeDtypeStruct((copies, total, LANES), F32),
        scratch_shapes=[pltpu.VMEM((wide, wide), F32)],
    )(states, *parts, *earlier)


def gradient_body(lines, begin, end, parts, *refs):
    observed, precision, out_ref, grads, sems = refs[parts:]
    total = grads.shape[0]
    first = refs[0].shape[1] - TILE
    rows = BLOCK // LINE
    group = 4
    shape = (rows, LINE, LANES)
    lane = lax.broadcasted_iota(jnp.int32, (1, LINE, LANES), 2)
    line = lax.broadcasted_iota(jnp.int32, (1, LINE, LANES), 1)

    def load(particle, at, count):
        ref, at = (refs[0], at) if at < first else (refs[1], at - first)
        return ref[particle, at : at + count, :].astype(F32)

    def rim(particle):
        return refs[0][particle, first:, :].astype(F32)

    stores = []
    for k, at in enumerate(range(begin, end, BLOCK)):
        mine = slice(at - begin, at - begin + BLOCK)
        obs = observed[at : at + BLOCK, :].astype(F32).reshape(shape)
        prec = precision[at : at + BLOCK, :].astype(F32).reshape(shape)

        def step(i, carry):
            for p in range(group):
                particle = i * group + p
                here = load(particle, at, BLOCK)
                before = load(particle, at - TILE, TILE) if at else rim(particle)
                after = load(particle, at + BLOCK, TILE) if at + BLOCK < lines else rim(particle)
                above = jnp.concatenate([before[LINE:], here[:-LINE]], axis=0).reshape(shape)
                below = jnp.concatenate([here[LINE:], after[:LINE]], axis=0).reshape(shape)
                field = here.reshape(shape)
                turned = pltpu.roll(field, 1, 2)
                carried = jnp.where(line == 0, 0.0, pltpu.roll(turned, 1, 1))
                left = jnp.where(lane == 0, carried, turned)
                turned = pltpu.roll(field, LANES - 1, 2)
                carried = jnp.where(line == LINE - 1, 0.0, pltpu.roll(turned, LINE - 1, 1))
                right = jnp.where(lane == LANES - 1, carried, turned)
                laplace = (4.0 + mass_term) * field - (below + above + right + left)
                squash = jnp.tanh(field)
                result = prec * (obs - squash) * (1.0 - squash * squash) - prior_scale * laplace
                grads[particle, mine, :] = result.reshape(BLOCK, LANES).astype(BF16)
            return carry

        lax.fori_loop(0, total // group, step, 0)
        stores.append(pltpu.make_async_copy(grads.at[:, mine, :], out_ref.at[:, mine, :], sems.at[k]))
        stores[-1].start()
    for store in stores:
        store.wait()


def slab_gradient(parts, observed, precision, lines, begin, end):
    total = parts[0].shape[0]
    count = end - begin
    out = jax.ShapeDtypeStruct((total, count, LANES), BF16)
    return call(
        functools.partial(gradient_body, lines, begin, end, len(parts)),
        "slab_gradient",
        flops=30 * out.size,
        moved=8 * out.size,
        in_specs=[IN_VMEM] * (len(parts) + 2),
        out_specs=IN_HBM,
        out_shape=out,
        scratch_shapes=[pltpu.VMEM(out.shape, BF16), pltpu.SemaphoreType.DMA((count // BLOCK,))],
    )(*parts, observed, precision)


def update_body(begin, end, parts, *refs):
    states_refs, refs = refs[:parts], refs[parts:]
    scalars_ref, grams_ref, grads_ref = refs[:3]
    out_ref, grads, mixer, own, sem = refs[-5:]
    total = out_ref.shape[0]
    wide = total * TILE
    fetch = pltpu.make_async_copy(grads_ref, grads, sem)
    fetch.start()
    gram = jnp.sum(grams_ref[...], axis=0)[:, :total]
    row = lax.broadcasted_iota(jnp.int32, (total, total), 0)
    col = lax.broadcasted_iota(jnp.int32, (total, total), 1)
    diagonal = jnp.where(row == col, gram, 0.0)
    down = jnp.sum(diagonal, axis=1, keepdims=True)
    across = jnp.sum(diagonal, axis=0, keepdims=True)
    member = members(total, BF16)
    spread, anneal, step_size = (scalars_ref[k : k + 1, :1] for k in range(3))
    rate = step_size / total
    coeff = 2.0 * anneal / spread
    kernel = jnp.exp(-(down + across - 2.0 * gram) / (spread * NCELL)).astype(BF16)
    ksum = jnp.sum(kernel.astype(F32), axis=1, keepdims=True)
    half = jnp.dot(member, kernel, preferred_element_type=F32).astype(BF16)
    full = lax.dot_general(half, member, (((1,), (1,)), ((), ())), preferred_element_type=F32)
    mixer[...] = jnp.where(same_line(total), full, 0.0).astype(BF16)
    gain = 1.0 + rate * coeff * ksum
    own[...] = jnp.broadcast_to(gain[:, :, None], (total, TILE, LANES)).reshape(wide, LANES)
    fetch.wait()

    done = 0
    for part, states_ref in enumerate(states_refs):
        have = states_ref.shape[1] - (0 if part else TILE)
        low = max(begin - done, 0)
        high = min(end - done, have)
        into = done - begin
        done += have

        def step(i, carry):
            for t in range(BLOCK // TILE):
                at = pl.multiple_of(i * BLOCK + t * TILE, TILE)
                there = pl.ds(pl.multiple_of(at + into, TILE), TILE)
                states = states_ref[:, pl.ds(at, TILE), :].reshape(wide, LANES)
                both = jnp.concatenate([grads[:, there, :].reshape(wide, LANES), states], axis=1)
                mixed = jnp.dot(mixer[...], both, preferred_element_type=F32)
                drive, pulled = mixed[:, :LANES], mixed[:, LANES:]
                new = states.astype(F32) * own[...] + rate * (drive - coeff * pulled)
                out_ref[:, there, :] = new.astype(BF16).reshape(total, TILE, LANES)
            return carry

        lax.fori_loop(low // BLOCK, high // BLOCK, step, 0)


def slab_update(scalars, grams, parts, grads, begin, end, earlier):
    total, count, _ = grads.shape
    wide = total * TILE
    return call(
        functools.partial(update_body, begin, end, len(parts)),
        "slab_update",
        flops=4 * wide * wide * LANES * (count // TILE),
        moved=6 * grads.size,
        in_specs=[IN_VMEM] * len(parts)
        + [IN_VMEM, IN_VMEM, IN_HBM]
        + [IN_HBM] * len(earlier),
        out_specs=IN_VMEM,
        out_shape=jax.ShapeDtypeStruct(grads.shape, BF16),
        scratch_shapes=[
            pltpu.VMEM(grads.shape, BF16),
            pltpu.VMEM((wide, wide), BF16),
            pltpu.VMEM((wide, LANES), F32),
            pltpu.SemaphoreType.DMA,
        ],
    )(*parts, scalars, grams, grads, *earlier)


def plain_update(spread, anneal, step_size, states, grads):
    total, lines, _ = grads.shape
    flat = states[:, :lines].reshape(total, -1)
    gram = lax.dot_general(flat, flat, (((1,), (1,)), ((), ())), preferred_element_type=F32)
    gram = lax.psum(gram, "slab")
    norms = jnp.diagonal(gram)
    kernel = jnp.exp(-(norms[:, None] + norms[None, :] - 2.0 * gram) / (spread[0] * NCELL)).astype(BF16)
    ksum = jnp.sum(kernel.astype(F32), axis=1)
    drive = jnp.dot(kernel, grads.reshape(total, -1), preferred_element_type=F32)
    pulled = jnp.dot(kernel, flat, preferred_element_type=F32)
    values = flat.astype(F32)
    repel = values * ksum[:, None] - pulled
    coeff = 2.0 * anneal[0] / spread[0]
    new = values + step_size[0] / total * (drive + coeff * repel)
    return new.astype(BF16).reshape(grads.shape)


def swap(slabs):
    return lax.all_to_all(slabs, "slab", split_axis=0, concat_axis=0, tiled=True)


def device_at(at, half):
    me = lax.axis_index("slab").astype(jnp.int32)
    return jnp.where(at < half, me - me % half + at, me ^ at)


def lines_of(start, count):
    return pl.ds(pl.multiple_of(start, TILE), count)


def split_pieces_body(slabs, raw, lines, fields, row_ref, *refs):
    half = slabs // 2
    field_refs, near_out, far_outs = refs[:fields], refs[fields], refs[fields + 1 : fields + 1 + half]
    slab_refs, held, sems = refs[fields + 1 + half : -2], refs[-2], refs[-1]
    cells = lines * LANES
    end = row_ref.shape[1]
    me = lax.axis_index("slab").astype(jnp.int32)
    copies = []
    for slab in range(slabs):
        part = pl.ds(slab * cells, cells)
        copies.append(pltpu.make_async_copy(row_ref.at[:, part], held.at[:, part], sems.at[slab]))
    for n, target in enumerate(slab_refs):
        start = (me if n < fields else me ^ half) * lines
        source = field_refs[n % fields].at[lines_of(start, target.shape[0]), :]
        copies.append(pltpu.make_async_copy(source, target, sems.at[slabs + n]))
    for copy in copies:
        copy.start()
    for copy in copies[:slabs]:
        copy.wait()

    def part(start, size):
        return held[:, pl.ds(pl.multiple_of(start, GRID_Y), size)]

    def grid_row(start):
        return part(start, GRID_Y).astype(F32).reshape(LINE, LANES)

    for at in range(slabs):
        out_ref = near_out.at[at] if at < half else far_outs[at - half]
        slab = device_at(at, half)
        start = slab * cells
        out_ref[:lines, :] = part(start, cells).reshape(lines, LANES)
        below = jnp.where(slab == slabs - 1, 0.0, grid_row(jnp.minimum(start + cells, end - GRID_Y)))
        above = jnp.where(slab == 0, 0.0, grid_row(jnp.maximum(start - GRID_Y, 0)))
        out_ref[lines : lines + TILE, :] = jnp.concatenate([below, above], axis=0).astype(BF16)
        if at < half:
            start = (slab ^ half) * cells
            to = lines + TILE
            out_ref[to : to + raw, :] = part(start, raw * LANES).reshape(raw, LANES)
            below = grid_row(start + raw * LANES)
            above = jnp.where(slab ^ half == 0, 0.0, grid_row(jnp.maximum(start - GRID_Y, 0)))
            out_ref[to + raw :, :] = jnp.concatenate([below, above], axis=0).astype(BF16)
    for copy in copies[slabs:]:
        copy.wait()


def split_pieces(row, slabs, raw, fields):
    lines = row.shape[1] // slabs // LANES
    half = slabs // 2
    rim = lines + TILE
    size = rim + raw + TILE
    out_shape = [jax.ShapeDtypeStruct((half, size, LANES), BF16)]
    out_shape += [jax.ShapeDtypeStruct((rim, LANES), BF16)] * half
    out_shape += [jax.ShapeDtypeStruct((lines, LANES), BF16)] * len(fields)
    out_shape += [jax.ShapeDtypeStruct((raw, LANES), BF16)] * len(fields)
    return call(
        functools.partial(split_pieces_body, slabs, raw, lines, len(fields)),
        "split_pieces",
        moved=6 * half * (rim + size) * LANES,
        in_specs=[IN_HBM] * (1 + len(fields)),
        out_specs=[IN_VMEM] * len(out_shape),
        out_shape=out_shape,
        scratch_shapes=[pltpu.VMEM(row.shape, BF16), pltpu.SemaphoreType.DMA((slabs + 2 * len(fields),))],
    )(row, *fields)


def join_pieces_body(pieces, half, raw, lines, begun, arrays, *refs):
    row_ref, helds, sems = refs[begun + arrays], refs[begun + arrays + 1 : -1], refs[-1]
    cells = lines * LANES
    skip = raw * LANES
    copies = []
    for (array, lead, at), held in zip(pieces, helds):
        ref = refs[begun + array]
        piece = ref[...] if lead is None else ref[lead]
        held[...] = piece.reshape(held.shape)
        slab = device_at(at, half)
        if at < half:
            parts = [(0, cells, slab * cells), (cells, skip, (slab ^ half) * cells)]
        else:
            parts = [(0, cells - skip, slab * cells + skip)]
        for begin, size, start in parts:
            target = row_ref.at[:, pl.ds(pl.multiple_of(start, GRID_Y), size)]
            copies.append(pltpu.make_async_copy(held.at[:, pl.ds(begin, size)], target, sems.at[len(copies)]))
            copies[-1].start()
    for copy in copies:
        copy.wait()


def join_pieces(row, slabs, raw, arrays, pieces):
    sizes = [arrays[piece[0]].shape[-2] * LANES for piece in pieces]
    begun = [] if row is None else [row]
    return call(
        functools.partial(
            join_pieces_body, pieces, slabs // 2, raw, NCELL // slabs // LANES, len(begun), len(arrays)
        ),
        "join_pieces",
        moved=6 * sum(sizes),
        in_specs=[IN_HBM] * len(begun) + [IN_VMEM] * len(arrays),
        out_specs=IN_HBM,
        out_shape=jax.ShapeDtypeStruct((1, NCELL), BF16),
        input_output_aliases={0: 0} if begun else {},
        scratch_shapes=[pltpu.VMEM((1, size), BF16) for size in sizes]
        + [pltpu.SemaphoreType.DMA((2 * len(sizes),))],
    )(*begun, *arrays)


def owners(total, dtype):
    wide = total * TILE
    row = lax.broadcasted_iota(jnp.int32, (wide, total), 0)
    col = lax.broadcasted_iota(jnp.int32, (wide, total), 1)
    return (device_at(row // TILE, total // 2) == col).astype(dtype)


def gram_pieces_body(lines, total, near_ref, *refs):
    half = total // 2
    pieces, out_ref, pairs = refs[:half], refs[-2], refs[-1]
    wide = total * TILE
    tiles = 8
    pairs[...] = jnp.zeros_like(pairs)

    def step(i, carry):
        parts = []
        for t in range(tiles):
            at = lines_of((i * tiles + t) * TILE, TILE)
            near = near_ref[:, at, :].reshape(wide // 2, LANES)
            parts.append(jnp.concatenate([near] + [piece[at, :] for piece in pieces], axis=0))
        block = jnp.concatenate(parts, axis=1)
        pairs[...] += lax.dot_general(block, block, (((1,), (1,)), ((), ())), preferred_element_type=F32)
        return carry

    lax.fori_loop(0, lines // TILE // tiles, step, 0)
    equal = jnp.where(same_line(total), pairs[...], 0.0)
    exact = {"precision": lax.Precision.HIGHEST, "preferred_element_type": F32}
    rows = jnp.sum(equal.reshape(total, TILE, wide), axis=1)
    gram = jnp.dot(rows, owners(total, F32), **exact)
    row = lax.broadcasted_iota(jnp.int32, (total, total), 0)
    col = lax.broadcasted_iota(jnp.int32, (total, total), 1)
    gram = jnp.dot((row == device_at(col, half)).astype(F32), gram, **exact)
    gram = jnp.concatenate([gram, jnp.zeros((total, LANES - total), F32)], axis=1)
    out_ref[...] = jnp.broadcast_to(gram[None], out_ref.shape)


def gram_pieces(near, far, lines, gates, early):
    total = 2 * len(far)
    wide = total * TILE
    return call(
        functools.partial(gram_pieces_body, lines, total),
        "gram_pieces",
        flops=2 * wide * wide * LANES * (lines // TILE),
        moved=2 * total * lines * LANES,
        in_specs=[IN_VMEM] * (1 + len(far)) + [IN_HBM] * len(gates) + [IN_VMEM] * len(early),
        out_specs=IN_VMEM,
        out_shape=jax.ShapeDtypeStruct((total, total, LANES), F32),
        scratch_shapes=[pltpu.VMEM((wide, wide), F32)],
    )(near, *far, *gates, *early)


def block_gradient(load, i, count, observed, precision):
    start = i * BLOCK
    at = lines_of(start, BLOCK)
    shape = (BLOCK // LINE, LINE, LANES)
    lane = lax.broadcasted_iota(jnp.int32, (1, LINE, LANES), 2)
    line = lax.broadcasted_iota(jnp.int32, (1, LINE, LANES), 1)
    obs = observed[at, :].astype(F32).reshape(shape)
    prec = precision[at, :].astype(F32).reshape(shape)
    here = load(start, BLOCK).astype(F32)
    before = load(jnp.where(i == 0, count, start - TILE), TILE).astype(F32)
    after = load(start + BLOCK, TILE).astype(F32)
    above = jnp.concatenate([before[LINE:], here[:-LINE]], axis=0).reshape(shape)
    below = jnp.concatenate([here[LINE:], after[:LINE]], axis=0).reshape(shape)
    field = here.reshape(shape)
    turned = pltpu.roll(field, 1, 2)
    carried = jnp.where(line == 0, 0.0, pltpu.roll(turned, 1, 1))
    left = jnp.where(lane == 0, carried, turned)
    turned = pltpu.roll(field, LANES - 1, 2)
    carried = jnp.where(line == LINE - 1, 0.0, pltpu.roll(turned, LINE - 1, 1))
    right = jnp.where(lane == LANES - 1, carried, turned)
    laplace = (4.0 + mass_term) * field - (below + above + right + left)
    squash = jnp.tanh(field)
    result = prec * (obs - squash) * (1.0 - squash * squash) - prior_scale * laplace
    return result.reshape(BLOCK, LANES).astype(BF16)


def gradient_pieces_body(views, arrays, numbers, *refs):
    observed, precision, *number_refs = refs[arrays : arrays + 2 + numbers]
    out_ref, rows_ref, grads, sems = refs[-4:]
    for n, number_ref in enumerate(number_refs):
        rows_ref[n : n + 1, :] = jnp.full((1, LANES), number_ref[0], F32)
    count = observed.shape[0]
    steps = count // BLOCK

    def store(i):
        at = lines_of(i * BLOCK, BLOCK)
        return pltpu.make_async_copy(grads.at[:, at, :], out_ref.at[:, at, :], sems.at[i])

    def step(i, carry):
        for p, (array, lead, base) in enumerate(views):

            def load(start, size):
                part = lines_of(base + start, size)
                return refs[array][part, :] if lead is None else refs[array][lead, part, :]

            grads[p, lines_of(i * BLOCK, BLOCK), :] = block_gradient(load, i, count, observed, precision)
        store(i).start()
        return carry

    def finish(i, carry):
        store(i).wait()
        return carry

    lax.fori_loop(0, steps, step, 0)
    lax.fori_loop(0, steps, finish, 0)


def gradient_pieces(arrays, views, observed, precision, numbers):
    count = observed.shape[0]
    out = pltpu.HBM((len(views), count, LANES), BF16)
    size = len(views) * count * LANES
    return call(
        functools.partial(gradient_pieces_body, views, len(arrays), len(numbers)),
        "gradient_pieces",
        flops=30 * size,
        moved=8 * size,
        in_specs=[IN_VMEM] * (len(arrays) + 2)
        + [pl.BlockSpec(memory_space=pltpu.SMEM)] * len(numbers),
        out_specs=[IN_HBM, IN_VMEM],
        out_shape=[out, jax.ShapeDtypeStruct((8, LANES), F32)],
        scratch_shapes=[pltpu.VMEM(out.shape, BF16), pltpu.SemaphoreType.DMA((count // BLOCK,))],
    )(*arrays, observed, precision, *numbers)


def raw_body(raw, lines, near_ref, *refs):
    out_ref = refs[-1]
    for k in range(near_ref.shape[0]):
        out_ref[k, :raw, :] = near_ref[k, :raw, :]
        below = near_ref[k, raw : raw + TILE, :].astype(F32)[:LINE]
        above = near_ref[k, lines : lines + TILE, :].astype(F32)[LINE:]
        out_ref[k, raw:, :] = jnp.concatenate([below, above], axis=0).astype(BF16)


def raw_states(near, raw, lines, gates):
    out = jax.ShapeDtypeStruct((near.shape[0], raw + TILE, LANES), BF16)
    return call(
        functools.partial(raw_body, raw, lines),
        "raw_states",
        moved=4 * out.size,
        in_specs=[IN_VMEM] * (1 + len(gates)),
        out_specs=IN_VMEM,
        out_shape=out,
    )(near, *gates)


def mix(mixer, own, numbers_ref, total, states, slopes):
    high = mixer.shape[0]
    rate = numbers_ref[2:3, :1] / total
    coeff = 2.0 * numbers_ref[1:2, :1] / numbers_ref[:1, :1]
    both = jnp.concatenate([slopes, states], axis=1)
    mixed = jnp.dot(mixer[...], both, preferred_element_type=F32)
    drive, pulled = mixed[:, :LANES], mixed[:, LANES:]
    return (states[:high].astype(F32) * own[...] + rate * (drive - coeff * pulled)).astype(BF16)


def update_pieces_body(half, raw, lines, groups, near_ref, *refs):
    total = 2 * half
    far_refs, refs = refs[:half], refs[half:]
    across_ref, raw_observed, raw_precision, numbers_ref, grams_ref, raw_grads_ref, *refs = refs
    group_refs, near_to, far_tos = refs[: len(groups)], refs[len(groups)], refs[len(groups) + 1 : -8]
    near_out, far_out, mixer, own, grads, raw_grads, sems, out_sems = refs[-8:]
    wide = total * TILE
    high = half * TILE
    raw_fetch = pltpu.make_async_copy(raw_grads_ref, raw_grads.at[pl.ds(0, half), :, :], sems.at[len(groups), 0])
    raw_fetch.start()
    middle = (raw + 2 * lines) // 3 // BLOCK * BLOCK
    parts = ((0, raw), (raw, middle), (middle, lines - BLOCK), (lines - BLOCK, lines))
    fetches = []
    for n, (first, last) in enumerate(parts):
        part = pl.ds(first, last - first)
        fetches.append([])
        for g, (group, group_ref) in enumerate(zip(groups, group_refs)):
            target = grads.at[pl.ds(group[0], len(group)), part, :]
            fetches[n].append(pltpu.make_async_copy(group_ref.at[:, part, :], target, sems.at[g, n]))
            fetches[n][-1].start()

    def raw_gradient(i, carry):
        for k in range(half):

            def load(start, size):
                return across_ref[k, lines_of(start, size), :]

            part = lines_of(i * BLOCK, BLOCK)
            raw_grads[half + k, part, :] = block_gradient(load, i, raw, raw_observed, raw_precision)
        return carry

    lax.fori_loop(0, raw // BLOCK, raw_gradient, 0)
    gram = jnp.sum(grams_ref[...], axis=0)[:, :total]
    spread, anneal, step_size = (numbers_ref[k : k + 1, :1] for k in range(3))
    rate = step_size / total
    coeff = 2.0 * anneal / spread
    row = lax.broadcasted_iota(jnp.int32, (total, total), 0)
    col = lax.broadcasted_iota(jnp.int32, (total, total), 1)
    diagonal = jnp.where(row == col, gram, 0.0)
    down = jnp.sum(diagonal, axis=1, keepdims=True)
    across = jnp.sum(diagonal, axis=0, keepdims=True)
    kernel = jnp.exp(-(down + across - 2.0 * gram) / (spread * NCELL)).astype(BF16)
    owner = owners(total, BF16)
    half_way = jnp.dot(owner, kernel, preferred_element_type=F32).astype(BF16)
    full = lax.dot_general(half_way, owner, (((1,), (1,)), ((), ())), preferred_element_type=F32)
    full = jnp.where(same_line(total), full, 0.0)
    mixer[...] = full.astype(BF16)
    ksum = jnp.sum(full, axis=1, keepdims=True)
    own[...] = jnp.broadcast_to(1.0 + rate * coeff * ksum, (wide, LANES))

    stores = []

    def store(source, target, at):
        stores.append(pltpu.make_async_copy(source, target, out_sems.at[at]))
        stores[-1].start()

    def store_near(first, last, at):
        part = pl.ds(first, last - first)
        store(near_out.at[:, part, :], near_to.at[:, part, :], (half, at))

    def store_far(first, last, at):
        part = pl.ds(first - raw, last - first)
        for x, far_to in enumerate(far_tos):
            store(far_out.at[x, part, :], far_to.at[part, :], (x, at))

    def slab_step(with_far, i, carry):
        rows = wide if with_far else high
        for t in range(BLOCK // TILE):
            at = i * BLOCK + t * TILE
            part = lines_of(at, TILE)
            states = [near_ref[:, part, :].reshape(high, LANES)] + [ref[part, :] for ref in far_refs]
            slopes = grads[:, part, :].reshape(wide, LANES)
            states = jnp.concatenate(states, axis=0)
            new = mix(mixer.at[:rows, :], own.at[:rows, :], numbers_ref, total, states, slopes)
            near_out[:, part, :] = new[:high].reshape(half, TILE, LANES)
            if with_far:
                far_out[:, lines_of(at - raw, TILE), :] = new[high:].reshape(half, TILE, LANES)
        return carry

    here = lax.axis_index("slab").astype(jnp.int32) % half

    def raw_step(i, carry):
        for t in range(BLOCK // TILE):
            at = i * BLOCK + t * TILE
            part = lines_of(at, TILE)
            states = [near_ref[:, lines_of(lines + TILE + at, TILE), :].reshape(high, LANES)]
            slopes = [raw_grads[:half, part, :].reshape(high, LANES)]
            for x in range(half):
                states += [across_ref[here ^ x, part, :]]
                slopes += [raw_grads[half + (here ^ x), part, :]]
            states, slopes = jnp.concatenate(states, axis=0), jnp.concatenate(slopes, axis=0)
            new = mix(mixer.at[:high, :], own.at[:high, :], numbers_ref, total, states, slopes)
            near_out[:, lines_of(lines + at, TILE), :] = new.reshape(half, TILE, LANES)
        return carry

    raw_fetch.wait()
    lax.fori_loop(0, raw // BLOCK, raw_step, 0)
    store_near(lines, lines + raw, 0)
    for n, (first, last) in enumerate(parts):
        for fetch in fetches[n]:
            fetch.wait()
        lax.fori_loop(first // BLOCK, last // BLOCK, functools.partial(slab_step, n > 0), 0)
        store_near(first, last, 1 + n)
        if n:
            store_far(first, last, n - 1)
    for copy in stores:
        copy.wait()


def update_pieces(numbers, grams, near, far, across, raw_fields, raw_grads, grads, groups, raw, lines):
    half = len(far)
    total = 2 * half
    wide = total * TILE
    out_shape = [pltpu.HBM((half, lines + raw, LANES), BF16)]
    out_shape += [pltpu.HBM((lines - raw, LANES), BF16)] * half
    return call(
        functools.partial(update_pieces_body, half, raw, lines, groups),
        "update_pieces",
        flops=4 * wide * wide * LANES * (lines // TILE),
        moved=6 * total * lines * LANES,
        in_specs=[IN_VMEM] * (half + 6) + [IN_HBM] * (1 + len(groups)),
        out_specs=[IN_HBM] * len(out_shape),
        out_shape=out_shape,
        scratch_shapes=[
            pltpu.VMEM((half, lines + raw, LANES), BF16),
            pltpu.VMEM((half, lines - raw, LANES), BF16),
            pltpu.VMEM((wide, wide), BF16),
            pltpu.VMEM((wide, LANES), F32),
            pltpu.VMEM((total, lines, LANES), BF16),
            pltpu.VMEM((total, raw, LANES), BF16),
            pltpu.SemaphoreType.DMA((len(groups) + 1, 4)),
            pltpu.SemaphoreType.DMA((half + 1, 5)),
        ],
    )(near, *far, across, *raw_fields, numbers, grams, raw_grads, *grads)


def exchange(piece, k, slabs):
    return lax.ppermute(piece, "slab", [(i, i ^ k) for i in range(slabs)])


def swap_near(pieces, slabs):
    groups = [list(range(slabs // 2)), list(range(slabs // 2, slabs))]
    return lax.all_to_all(pieces, "slab", 0, 0, axis_index_groups=groups, tiled=True)


RAW = 128
GRADIENTS = ((8, 9, 10, 11), (12, 13, 14, 15), (0, 1, 2, 3, 4, 5, 6, 7))


def by_halves(particles, observed, precision, spread, anneal, step_size):
    slabs = lax.axis_size("slab")
    half = slabs // 2
    lines = NCELL // slabs // LANES
    row = in_hbm(particles)
    fields = [in_hbm(field.reshape(-1, LANES)) for field in (observed, precision)]
    near, *far = split_pieces(row, slabs, RAW, fields)
    far, (obs, prec, *raw_fields) = far[:half], far[half:]
    near = swap_near(near, slabs)
    far = [exchange(piece, half + x, slabs) for x, piece in enumerate(far)]
    raw_near = raw_states(near, RAW, lines, far)
    across = exchange(raw_near, half, slabs)
    grads = []
    numbers = [spread, anneal, step_size]
    for group in GRADIENTS:
        if group[0] < half:
            arrays, views = [near], [(0, k, 0) for k in group]
        else:
            arrays, views = [far[k - half] for k in group], [(j, None, 0) for j in range(len(group))]
        slopes, rows = gradient_pieces(arrays, tuple(views), obs, prec, [] if grads else numbers)
        grads.append(in_hbm(slopes))
        numbers = numbers if len(grads) > 1 else rows
    grams = swap(gram_pieces(near, far, lines, grads[:1], [raw_near]))
    views = tuple((0, k, lines + TILE) for k in range(half))
    raw_grads = in_hbm(gradient_pieces([near], views, *raw_fields, [])[0])
    new_near, *new_far = update_pieces(
        numbers, grams, near, far, across, raw_fields, raw_grads, grads, GRADIENTS, RAW, lines
    )
    new_near = swap_near(new_near, slabs)
    new_far = [exchange(piece, half + x, slabs) for x, piece in enumerate(new_far)]
    row = join_pieces(None, slabs, RAW, [new_near], [(0, k, k) for k in range(half)])
    for group in ((0, 1, 2, 3), (4, 5)):
        pieces = [(n, None, half + x) for n, x in enumerate(group)]
        row = join_pieces(row, slabs, RAW, [new_far[x] for x in group], pieces)
    return join_pieces(row, slabs, RAW, new_far[6:], [(n, None, half + 6 + n) for n in range(half - 6)])


def on_device(particles, observed, precision, spread, anneal, step_size):
    slabs = lax.axis_size("slab")
    total = particles.shape[0] * slabs
    lines = NCELL // slabs // LANES
    if slabs == 16:
        return by_halves(particles, observed, precision, spread, anneal, step_size)
    sent, begun = cuts(lines)
    fields = [observed.reshape(-1, LANES), precision.reshape(-1, LANES)]
    numbers = [spread, anneal, step_size]
    first, obs, prec, scalars = split_row(particles, slabs, 0, sent, True, fields, numbers, [])
    parts = [swap(first)]
    if sent < lines:
        parts += [swap(split_row(particles, slabs, sent, lines, False, [], [], [scalars])[0])]
    if total * TILE > 256:
        grads = slab_gradient(parts, obs, prec, lines, 0, lines)
        states = jnp.concatenate([parts[0][:, :sent]] + parts[1:], axis=1)
        new = plain_update(spread, anneal, step_size, states, grads)
        return join_row(swap(new), lines, 0, None)
    if sent == lines:
        grads = slab_gradient(parts, obs, prec, lines, 0, lines)
        grams = swap(slab_gram(parts[0], lines, slabs, [], []))
        new = slab_update(scalars, grams, parts, grads, 0, lines, [])
        return join_row(swap(new), lines, 0, None)
    gram = slab_gram(parts[0], sent, 1, [], [])
    early = slab_gradient(parts[:1], obs, prec, lines, 0, begun)
    grams = swap(slab_gram(parts[1], lines - sent, slabs, [gram], [early]))
    late = slab_gradient(parts, obs, prec, lines, begun, lines)
    new = slab_update(scalars, grams, parts[:1], early, 0, begun, [])
    rest = slab_update(scalars, grams, parts, late, begun, lines, [new])
    row = join_row(swap(new), lines, 0, None)
    return join_row(swap(rest), lines, begun, row)


def solution(mesh):
    in_specs = (
        P(("groups", "slab"), None),
        P("groups"),
        P("groups"),
        P("groups"),
        P("groups"),
        P("groups"),
    )
    out_specs = P(("groups", "slab"), None)
    return jax.shard_map(
        on_device, mesh=mesh, in_specs=in_specs, out_specs=out_specs, check_vma=False
    )
```

```python
import functools

import jax
import jax.numpy as jnp
from jax import lax
from jax.experimental import pallas as pl
from jax.experimental.pallas import tpu as pltpu
from jax.sharding import PartitionSpec as P

GRID_X = 1024
GRID_Y = 1024
NCELL = 1048576
LANES = 128
LINE = GRID_Y // LANES
TILE = 16

prior_scale = 0.25
mass_term = 1.0

F32 = jnp.float32
BF16 = jnp.bfloat16
MIB = 1024 * 1024


def call(body, name, flops=0, moved=0, limit=16, **kwargs):
    return pl.pallas_call(
        body,
        name=name,
        compiler_params=pltpu.CompilerParams(vmem_limit_bytes=limit * MIB),
        cost_estimate=pl.CostEstimate(flops=flops, bytes_accessed=moved, transcendentals=0),
        **kwargs,
    )


IN_VMEM = pl.BlockSpec(memory_space=pltpu.VMEM)
IN_HBM = pl.BlockSpec(memory_space=pltpu.HBM)


def in_hbm(array):
    return pltpu.with_memory_space_constraint(array, pltpu.HBM)


BLOCK = 4 * TILE


def cuts(lines):
    if lines % (8 * BLOCK):
        return lines, lines
    return lines * 3 // 4, lines * 3 // 4 - BLOCK


def split_body(lines, begin, rim, fields, numbers, row_ref, *refs):
    field_refs, number_refs = refs[:fields], refs[fields : fields + numbers]
    out_ref, *slab_refs, rows_ref = refs[-7 - fields : -5]
    held, edges, sems, edge_sems, field_sems = refs[-5:]
    for k, number_ref in enumerate(number_refs):
        rows_ref[k : k + 1, :] = jnp.broadcast_to(number_ref[...].reshape(1, 1), (1, LANES))
    slabs, count, _ = out_ref.shape
    count -= TILE * rim
    size = count * LANES
    cells = lines * LANES

    def part(slab):
        source = row_ref.at[:, pl.ds(slab * cells + begin * LANES, size)]
        return pltpu.make_async_copy(source, held.at[:, pl.ds(slab * size, size)], sems.at[slab])

    def edge(slab):
        source = row_ref.at[:, pl.ds(slab * cells - GRID_Y, GRID_Y)]
        return pltpu.make_async_copy(source, edges.at[:, pl.ds(slab * GRID_Y, GRID_Y)], edge_sems.at[slab])

    def grid_row(ref, start):
        return ref[:, pl.ds(start, GRID_Y)].astype(F32).reshape(LINE, LANES)

    for slab in range(slabs):
        part(slab).start()
        if rim and slab:
            edge(slab).start()
    mine = pl.ds(pl.multiple_of(lax.axis_index("slab") * lines, TILE), lines)
    fetches = [
        pltpu.make_async_copy(source.at[mine, :], target, field_sems.at[k])
        for k, (source, target) in enumerate(zip(field_refs, slab_refs))
    ]
    for fetch in fetches:
        fetch.start()
    part(0).wait()
    outside = jnp.zeros((LINE, LANES), F32)
    for slab in range(slabs):
        if slab + 1 < slabs:
            part(slab + 1).wait()
        out_ref[slab, :count, :] = held[:, pl.ds(slab * size, size)].reshape(count, LANES)
        if rim:
            if slab:
                edge(slab).wait()
            below = grid_row(held, (slab + 1) * size) if slab + 1 < slabs else outside
            above = grid_row(edges, slab * GRID_Y) if slab else outside
            out_ref[slab, count:, :] = jnp.concatenate([below, above], axis=0).astype(BF16)
    for fetch in fetches:
        fetch.wait()


def split_row(row, slabs, begin, end, rim, fields, numbers, earlier):
    lines = row.shape[1] // slabs // LANES
    count = end - begin
    return call(
        functools.partial(split_body, lines, begin, rim, len(fields), len(numbers)),
        "split_row",
        moved=6 * slabs * count * LANES,
        in_specs=[IN_HBM] * (1 + len(fields)) + [IN_VMEM] * len(numbers) + [IN_HBM] * len(earlier),
        out_specs=[IN_VMEM] * (2 + len(fields)),
        out_shape=[jax.ShapeDtypeStruct((slabs, count + TILE * rim, LANES), BF16)]
        + [jax.ShapeDtypeStruct((lines, LANES), BF16)] * len(fields)
        + [jax.ShapeDtypeStruct((8, LANES), F32)],
        scratch_shapes=[
            pltpu.VMEM((1, slabs * count * LANES), BF16),
            pltpu.VMEM((1, slabs * GRID_Y), BF16),
            pltpu.SemaphoreType.DMA((slabs,)),
            pltpu.SemaphoreType.DMA((slabs,)),
            pltpu.SemaphoreType.DMA((2,)),
        ],
    )(row, *fields, *numbers, *earlier)


def join_body(lines, begin, slabs_ref, *refs):
    row_ref, held, sems = refs[-3:]
    slabs, count, _ = slabs_ref.shape
    size = count * LANES
    copies = []
    for slab in range(slabs):
        at = pl.ds(slab * size, size)
        held[:, at] = slabs_ref[slab].reshape(1, size)
        target = row_ref.at[:, pl.ds((slab * lines + begin) * LANES, size)]
        copies.append(pltpu.make_async_copy(held.at[:, at], target, sems.at[slab]))
        copies[-1].start()
    for copy in copies:
        copy.wait()


def join_row(slabs, lines, begin, row):
    total, count, _ = slabs.shape
    begun = [] if row is None else [row]
    return call(
        functools.partial(join_body, lines, begin),
        "join_row",
        moved=6 * slabs.size,
        in_specs=[IN_VMEM] + [IN_HBM] * len(begun),
        out_specs=IN_HBM,
        out_shape=jax.ShapeDtypeStruct((1, total * lines * LANES), BF16),
        input_output_aliases={1: 0} if begun else {},
        scratch_shapes=[pltpu.VMEM((1, slabs.size), BF16), pltpu.SemaphoreType.DMA((total,))],
    )(slabs, *begun)


def same_line(total):
    wide = total * TILE
    row = lax.broadcasted_iota(jnp.int32, (wide, wide), 0)
    col = lax.broadcasted_iota(jnp.int32, (wide, wide), 1)
    return (row ^ col) & (TILE - 1) == 0


def members(total, dtype):
    wide = total * TILE
    row = lax.broadcasted_iota(jnp.int32, (wide, total), 0)
    col = lax.broadcasted_iota(jnp.int32, (wide, total), 1)
    return (row // TILE == col).astype(dtype)


def gram_body(steps, tiles, parts, states_ref, *refs):
    out_ref, pairs = refs[-2:]
    total = states_ref.shape[0]
    wide = total * TILE
    pairs[...] = jnp.zeros_like(pairs)

    def step(i, carry):
        parts = [
            states_ref[:, pl.ds(pl.multiple_of((i * tiles + t) * TILE, TILE), TILE), :].reshape(wide, LANES)
            for t in range(tiles)
        ]
        block = jnp.concatenate(parts, axis=1)
        pairs[...] += lax.dot_general(block, block, (((1,), (1,)), ((), ())), preferred_element_type=F32)
        return carry

    lax.fori_loop(0, steps, step, 0)
    equal = jnp.where(same_line(total), pairs[...], 0.0)
    rows = jnp.sum(equal.reshape(total, TILE, wide), axis=1)
    gram = jnp.dot(rows, members(total, F32), precision=lax.Precision.HIGHEST, preferred_element_type=F32)
    gram = jnp.concatenate([gram, jnp.zeros((total, LANES - total), F32)], axis=1)
    for part_ref in refs[:parts]:
        gram += part_ref[0]
    out_ref[...] = jnp.broadcast_to(gram[None], out_ref.shape)


def slab_gram(states, lines, copies, parts, earlier):
    total = states.shape[0]
    wide = total * TILE
    tiles = min(8, lines // TILE)
    return call(
        functools.partial(gram_body, lines // TILE // tiles, tiles, len(parts)),
        "slab_gram",
        flops=2 * wide * wide * LANES * (lines // TILE),
        moved=2 * states.size,
        in_specs=[IN_VMEM] * (1 + len(parts)) + [IN_HBM] * len(earlier),
        out_specs=IN_VMEM,
        out_shape=jax.ShapeDtypeStruct((copies, total, LANES), F32),
        scratch_shapes=[pltpu.VMEM((wide, wide), F32)],
    )(states, *parts, *earlier)


def gradient_body(lines, begin, end, parts, *refs):
    observed, precision, out_ref, grads, sems = refs[parts:]
    total = grads.shape[0]
    first = refs[0].shape[1] - TILE
    rows = BLOCK // LINE
    group = 4
    shape = (rows, LINE, LANES)
    lane = lax.broadcasted_iota(jnp.int32, (1, LINE, LANES), 2)
    line = lax.broadcasted_iota(jnp.int32, (1, LINE, LANES), 1)

    def load(particle, at, count):
        ref, at = (refs[0], at) if at < first else (refs[1], at - first)
        return ref[particle, at : at + count, :].astype(F32)

    def rim(particle):
        return refs[0][particle, first:, :].astype(F32)

    stores = []
    for k, at in enumerate(range(begin, end, BLOCK)):
        mine = slice(at - begin, at - begin + BLOCK)
        obs = observed[at : at + BLOCK, :].astype(F32).reshape(shape)
        prec = precision[at : at + BLOCK, :].astype(F32).reshape(shape)

        def step(i, carry):
            for p in range(group):
                particle = i * group + p
                here = load(particle, at, BLOCK)
                before = load(particle, at - TILE, TILE) if at else rim(particle)
                after = load(particle, at + BLOCK, TILE) if at + BLOCK < lines else rim(particle)
                above = jnp.concatenate([before[LINE:], here[:-LINE]], axis=0).reshape(shape)
                below = jnp.concatenate([here[LINE:], after[:LINE]], axis=0).reshape(shape)
                field = here.reshape(shape)
                turned = pltpu.roll(field, 1, 2)
                carried = jnp.where(line == 0, 0.0, pltpu.roll(turned, 1, 1))
                left = jnp.where(lane == 0, carried, turned)
                turned = pltpu.roll(field, LANES - 1, 2)
                carried = jnp.where(line == LINE - 1, 0.0, pltpu.roll(turned, LINE - 1, 1))
                right = jnp.where(lane == LANES - 1, carried, turned)
                laplace = (4.0 + mass_term) * field - (below + above + right + left)
                squash = jnp.tanh(field)
                result = prec * (obs - squash) * (1.0 - squash * squash) - prior_scale * laplace
                grads[particle, mine, :] = result.reshape(BLOCK, LANES).astype(BF16)
            return carry

        lax.fori_loop(0, total // group, step, 0)
        stores.append(pltpu.make_async_copy(grads.at[:, mine, :], out_ref.at[:, mine, :], sems.at[k]))
        stores[-1].start()
    for store in stores:
        store.wait()


def slab_gradient(parts, observed, precision, lines, begin, end):
    total = parts[0].shape[0]
    count = end - begin
    out = jax.ShapeDtypeStruct((total, count, LANES), BF16)
    return call(
        functools.partial(gradient_body, lines, begin, end, len(parts)),
        "slab_gradient",
        flops=30 * out.size,
        moved=8 * out.size,
        in_specs=[IN_VMEM] * (len(parts) + 2),
        out_specs=IN_HBM,
        out_shape=out,
        scratch_shapes=[pltpu.VMEM(out.shape, BF16), pltpu.SemaphoreType.DMA((count // BLOCK,))],
    )(*parts, observed, precision)


def update_body(begin, end, parts, *refs):
    states_refs, refs = refs[:parts], refs[parts:]
    scalars_ref, grams_ref, grads_ref = refs[:3]
    out_ref, grads, mixer, own, sem = refs[-5:]
    total = out_ref.shape[0]
    wide = total * TILE
    fetch = pltpu.make_async_copy(grads_ref, grads, sem)
    fetch.start()
    gram = jnp.sum(grams_ref[...], axis=0)[:, :total]
    row = lax.broadcasted_iota(jnp.int32, (total, total), 0)
    col = lax.broadcasted_iota(jnp.int32, (total, total), 1)
    diagonal = jnp.where(row == col, gram, 0.0)
    down = jnp.sum(diagonal, axis=1, keepdims=True)
    across = jnp.sum(diagonal, axis=0, keepdims=True)
    member = members(total, BF16)
    spread, anneal, step_size = (scalars_ref[k : k + 1, :1] for k in range(3))
    rate = step_size / total
    coeff = 2.0 * anneal / spread
    kernel = jnp.exp(-(down + across - 2.0 * gram) / (spread * NCELL)).astype(BF16)
    ksum = jnp.sum(kernel.astype(F32), axis=1, keepdims=True)
    half = jnp.dot(member, kernel, preferred_element_type=F32).astype(BF16)
    full = lax.dot_general(half, member, (((1,), (1,)), ((), ())), preferred_element_type=F32)
    mixer[...] = jnp.where(same_line(total), full, 0.0).astype(BF16)
    gain = 1.0 + rate * coeff * ksum
    own[...] = jnp.broadcast_to(gain[:, :, None], (total, TILE, LANES)).reshape(wide, LANES)
    fetch.wait()

    done = 0
    for part, states_ref in enumerate(states_refs):
        have = states_ref.shape[1] - (0 if part else TILE)
        low = max(begin - done, 0)
        high = min(end - done, have)
        into = done - begin
        done += have

        def step(i, carry):
            for t in range(BLOCK // TILE):
                at = pl.multiple_of(i * BLOCK + t * TILE, TILE)
                there = pl.ds(pl.multiple_of(at + into, TILE), TILE)
                states = states_ref[:, pl.ds(at, TILE), :].reshape(wide, LANES)
                both = jnp.concatenate([grads[:, there, :].reshape(wide, LANES), states], axis=1)
                mixed = jnp.dot(mixer[...], both, preferred_element_type=F32)
                drive, pulled = mixed[:, :LANES], mixed[:, LANES:]
                new = states.astype(F32) * own[...] + rate * (drive - coeff * pulled)
                out_ref[:, there, :] = new.astype(BF16).reshape(total, TILE, LANES)
            return carry

        lax.fori_loop(low // BLOCK, high // BLOCK, step, 0)


def slab_update(scalars, grams, parts, grads, begin, end, earlier):
    total, count, _ = grads.shape
    wide = total * TILE
    return call(
        functools.partial(update_body, begin, end, len(parts)),
        "slab_update",
        flops=4 * wide * wide * LANES * (count // TILE),
        moved=6 * grads.size,
        in_specs=[IN_VMEM] * len(parts)
        + [IN_VMEM, IN_VMEM, IN_HBM]
        + [IN_HBM] * len(earlier),
        out_specs=IN_VMEM,
        out_shape=jax.ShapeDtypeStruct(grads.shape, BF16),
        scratch_shapes=[
            pltpu.VMEM(grads.shape, BF16),
            pltpu.VMEM((wide, wide), BF16),
            pltpu.VMEM((wide, LANES), F32),
            pltpu.SemaphoreType.DMA,
        ],
    )(*parts, scalars, grams, grads, *earlier)


def plain_update(spread, anneal, step_size, states, grads):
    total, lines, _ = grads.shape
    flat = states[:, :lines].reshape(total, -1)
    gram = lax.dot_general(flat, flat, (((1,), (1,)), ((), ())), preferred_element_type=F32)
    gram = lax.psum(gram, "slab")
    norms = jnp.diagonal(gram)
    kernel = jnp.exp(-(norms[:, None] + norms[None, :] - 2.0 * gram) / (spread[0] * NCELL)).astype(BF16)
    ksum = jnp.sum(kernel.astype(F32), axis=1)
    drive = jnp.dot(kernel, grads.reshape(total, -1), preferred_element_type=F32)
    pulled = jnp.dot(kernel, flat, preferred_element_type=F32)
    values = flat.astype(F32)
    repel = values * ksum[:, None] - pulled
    coeff = 2.0 * anneal[0] / spread[0]
    new = values + step_size[0] / total * (drive + coeff * repel)
    return new.astype(BF16).reshape(grads.shape)


def swap(slabs):
    return lax.all_to_all(slabs, "slab", split_axis=0, concat_axis=0, tiled=True)


def device_at(at, half):
    me = lax.axis_index("slab").astype(jnp.int32)
    return jnp.where(at < half, me - me % half + at, me ^ at)


def lines_of(start, count):
    return pl.ds(pl.multiple_of(start, TILE), count)


def split_pieces_body(slabs, raw, lines, fields, row_ref, *refs):
    half = slabs // 2
    field_refs, near_out, far_outs = refs[:fields], refs[fields], refs[fields + 1 : fields + 1 + half]
    slab_refs, held, sems = refs[fields + 1 + half : -2], refs[-2], refs[-1]
    cells = lines * LANES
    end = row_ref.shape[1]
    me = lax.axis_index("slab").astype(jnp.int32)

    def part(start, size):
        return pl.ds(pl.multiple_of(start, GRID_Y), size)

    def grid_row(start):
        return held[:, part(start, GRID_Y)].astype(F32).reshape(LINE, LANES)

    copies = []
    for at in range(slabs):
        cut = part(device_at(at, half) * cells, cells)
        copies.append(pltpu.make_async_copy(row_ref.at[:, cut], held.at[:, cut], sems.at[at]))
    for n, target in enumerate(slab_refs):
        start = (me if n < fields else me ^ half) * lines
        source = field_refs[n % fields].at[lines_of(start, target.shape[0]), :]
        copies.append(pltpu.make_async_copy(source, target, sems.at[slabs + n]))
    for copy in copies:
        copy.start()
    outs = [near_out.at[at] for at in range(half)] + list(far_outs)
    for at, out_ref in enumerate(outs):
        copies[at].wait()
        out_ref[:lines, :] = held[:, part(device_at(at, half) * cells, cells)].reshape(lines, LANES)
    for at, out_ref in enumerate(outs):
        slab = device_at(at, half)
        start = slab * cells
        below = jnp.where(slab == slabs - 1, 0.0, grid_row(jnp.minimum(start + cells, end - GRID_Y)))
        above = jnp.where(slab == 0, 0.0, grid_row(jnp.maximum(start - GRID_Y, 0)))
        out_ref[lines : lines + TILE, :] = jnp.concatenate([below, above], axis=0).astype(BF16)
        if at < half:
            start = (slab ^ half) * cells
            to = lines + TILE
            out_ref[to : to + raw, :] = held[:, part(start, raw * LANES)].reshape(raw, LANES)
            below = grid_row(start + raw * LANES)
            above = jnp.where(slab ^ half == 0, 0.0, grid_row(jnp.maximum(start - GRID_Y, 0)))
            out_ref[to + raw :, :] = jnp.concatenate([below, above], axis=0).astype(BF16)
    for copy in copies[slabs:]:
        copy.wait()


def split_pieces(row, slabs, raw, fields):
    lines = row.shape[1] // slabs // LANES
    half = slabs // 2
    rim = lines + TILE
    size = rim + raw + TILE
    out_shape = [jax.ShapeDtypeStruct((half, size, LANES), BF16)]
    out_shape += [jax.ShapeDtypeStruct((rim, LANES), BF16)] * half
    out_shape += [jax.ShapeDtypeStruct((lines, LANES), BF16)] * len(fields)
    out_shape += [jax.ShapeDtypeStruct((raw, LANES), BF16)] * len(fields)
    return call(
        functools.partial(split_pieces_body, slabs, raw, lines, len(fields)),
        "split_pieces",
        moved=6 * half * (rim + size) * LANES,
        in_specs=[IN_HBM] * (1 + len(fields)),
        out_specs=[IN_VMEM] * len(out_shape),
        out_shape=out_shape,
        scratch_shapes=[pltpu.VMEM(row.shape, BF16), pltpu.SemaphoreType.DMA((slabs + 2 * len(fields),))],
    )(row, *fields)


def join_pieces_body(pieces, half, raw, lines, begun, arrays, *refs):
    row_ref, helds, sems = refs[begun + arrays], refs[begun + arrays + 1 : -1], refs[-1]
    cells = lines * LANES
    skip = raw * LANES
    copies = []
    for (array, lead, at), held in zip(pieces, helds):
        ref = refs[begun + array]
        piece = ref[...] if lead is None else ref[lead]
        held[...] = piece.reshape(held.shape)
        slab = device_at(at, half)
        if at < half:
            parts = [(0, cells, slab * cells), (cells, skip, (slab ^ half) * cells)]
        else:
            parts = [(0, cells - skip, slab * cells + skip)]
        for begin, size, start in parts:
            target = row_ref.at[:, pl.ds(pl.multiple_of(start, GRID_Y), size)]
            copies.append(pltpu.make_async_copy(held.at[:, pl.ds(begin, size)], target, sems.at[len(copies)]))
            copies[-1].start()
    for copy in copies:
        copy.wait()


def join_pieces(row, slabs, raw, arrays, pieces):
    sizes = [arrays[piece[0]].shape[-2] * LANES for piece in pieces]
    begun = [] if row is None else [row]
    return call(
        functools.partial(
            join_pieces_body, pieces, slabs // 2, raw, NCELL // slabs // LANES, len(begun), len(arrays)
        ),
        "join_pieces",
        moved=6 * sum(sizes),
        in_specs=[IN_HBM] * len(begun) + [IN_VMEM] * len(arrays),
        out_specs=IN_HBM,
        out_shape=jax.ShapeDtypeStruct((1, NCELL), BF16),
        input_output_aliases={0: 0} if begun else {},
        scratch_shapes=[pltpu.VMEM((1, size), BF16) for size in sizes]
        + [pltpu.SemaphoreType.DMA((2 * len(sizes),))],
    )(*begun, *arrays)


def owners(total, dtype):
    wide = total * TILE
    row = lax.broadcasted_iota(jnp.int32, (wide, total), 0)
    col = lax.broadcasted_iota(jnp.int32, (wide, total), 1)
    return (device_at(row // TILE, total // 2) == col).astype(dtype)


def gram_pieces_body(lines, total, near_ref, *refs):
    half = total // 2
    pieces, out_ref, pairs = refs[:half], refs[-2], refs[-1]
    wide = total * TILE
    tiles = 8
    pairs[...] = jnp.zeros_like(pairs)

    def step(i, carry):
        parts = []
        for t in range(tiles):
            at = lines_of((i * tiles + t) * TILE, TILE)
            near = near_ref[:, at, :].reshape(wide // 2, LANES)
            parts.append(jnp.concatenate([near] + [piece[at, :] for piece in pieces], axis=0))
        block = jnp.concatenate(parts, axis=1)
        pairs[...] += lax.dot_general(block, block, (((1,), (1,)), ((), ())), preferred_element_type=F32)
        return carry

    lax.fori_loop(0, lines // TILE // tiles, step, 0)
    equal = jnp.where(same_line(total), pairs[...], 0.0)
    exact = {"precision": lax.Precision.HIGHEST, "preferred_element_type": F32}
    rows = jnp.sum(equal.reshape(total, TILE, wide), axis=1)
    gram = jnp.dot(rows, owners(total, F32), **exact)
    row = lax.broadcasted_iota(jnp.int32, (total, total), 0)
    col = lax.broadcasted_iota(jnp.int32, (total, total), 1)
    gram = jnp.dot((row == device_at(col, half)).astype(F32), gram, **exact)
    gram = jnp.concatenate([gram, jnp.zeros((total, LANES - total), F32)], axis=1)
    out_ref[...] = jnp.broadcast_to(gram[None], out_ref.shape)


def gram_pieces(near, far, lines, gates, early):
    total = 2 * len(far)
    wide = total * TILE
    return call(
        functools.partial(gram_pieces_body, lines, total),
        "gram_pieces",
        flops=2 * wide * wide * LANES * (lines // TILE),
        moved=2 * total * lines * LANES,
        in_specs=[IN_VMEM] * (1 + len(far)) + [IN_HBM] * len(gates) + [IN_VMEM] * len(early),
        out_specs=IN_VMEM,
        out_shape=jax.ShapeDtypeStruct((total, total, LANES), F32),
        scratch_shapes=[pltpu.VMEM((wide, wide), F32)],
    )(near, *far, *gates, *early)


def block_gradient(load, i, count, observed, precision):
    start = i * BLOCK
    at = lines_of(start, BLOCK)
    shape = (BLOCK // LINE, LINE, LANES)
    lane = lax.broadcasted_iota(jnp.int32, (1, LINE, LANES), 2)
    line = lax.broadcasted_iota(jnp.int32, (1, LINE, LANES), 1)
    obs = observed[at, :].astype(F32).reshape(shape)
    prec = precision[at, :].astype(F32).reshape(shape)
    here = load(start, BLOCK).astype(F32)
    before = load(jnp.where(i == 0, count, start - TILE), TILE).astype(F32)
    after = load(start + BLOCK, TILE).astype(F32)
    above = jnp.concatenate([before[LINE:], here[:-LINE]], axis=0).reshape(shape)
    below = jnp.concatenate([here[LINE:], after[:LINE]], axis=0).reshape(shape)
    field = here.reshape(shape)
    turned = pltpu.roll(field, 1, 2)
    carried = jnp.where(line == 0, 0.0, pltpu.roll(turned, 1, 1))
    left = jnp.where(lane == 0, carried, turned)
    turned = pltpu.roll(field, LANES - 1, 2)
    carried = jnp.where(line == LINE - 1, 0.0, pltpu.roll(turned, LINE - 1, 1))
    right = jnp.where(lane == LANES - 1, carried, turned)
    laplace = (4.0 + mass_term) * field - (below + above + right + left)
    squash = jnp.tanh(field)
    result = prec * (obs - squash) * (1.0 - squash * squash) - prior_scale * laplace
    return result.reshape(BLOCK, LANES).astype(BF16)


def gradient_pieces_body(views, arrays, numbers, *refs):
    observed, precision, *number_refs = refs[arrays : arrays + 2 + numbers]
    out_ref, rows_ref, grads, sems = refs[-4:]
    for n, number_ref in enumerate(number_refs):
        rows_ref[n : n + 1, :] = jnp.full((1, LANES), number_ref[0], F32)
    count = observed.shape[0]
    steps = count // BLOCK

    def store(i):
        at = lines_of(i * BLOCK, BLOCK)
        return pltpu.make_async_copy(grads.at[:, at, :], out_ref.at[:, at, :], sems.at[i])

    def step(i, carry):
        for p, (array, lead, base) in enumerate(views):

            def load(start, size):
                part = lines_of(base + start, size)
                return refs[array][part, :] if lead is None else refs[array][lead, part, :]

            grads[p, lines_of(i * BLOCK, BLOCK), :] = block_gradient(load, i, count, observed, precision)
        store(i).start()
        return carry

    def finish(i, carry):
        store(i).wait()
        return carry

    lax.fori_loop(0, steps, step, 0)
    lax.fori_loop(0, steps, finish, 0)


def gradient_pieces(arrays, views, observed, precision, numbers):
    count = observed.shape[0]
    out = pltpu.HBM((len(views), count, LANES), BF16)
    size = len(views) * count * LANES
    return call(
        functools.partial(gradient_pieces_body, views, len(arrays), len(numbers)),
        "gradient_pieces",
        flops=30 * size,
        moved=8 * size,
        in_specs=[IN_VMEM] * (len(arrays) + 2)
        + [pl.BlockSpec(memory_space=pltpu.SMEM)] * len(numbers),
        out_specs=[IN_HBM, IN_VMEM],
        out_shape=[out, jax.ShapeDtypeStruct((8, LANES), F32)],
        scratch_shapes=[pltpu.VMEM(out.shape, BF16), pltpu.SemaphoreType.DMA((count // BLOCK,))],
    )(*arrays, observed, precision, *numbers)


def raw_body(raw, lines, near_ref, *refs):
    out_ref = refs[-1]
    for k in range(near_ref.shape[0]):
        out_ref[k, :raw, :] = near_ref[k, :raw, :]
        below = near_ref[k, raw : raw + TILE, :].astype(F32)[:LINE]
        above = near_ref[k, lines : lines + TILE, :].astype(F32)[LINE:]
        out_ref[k, raw:, :] = jnp.concatenate([below, above], axis=0).astype(BF16)


def raw_states(near, raw, lines, gates):
    out = jax.ShapeDtypeStruct((near.shape[0], raw + TILE, LANES), BF16)
    return call(
        functools.partial(raw_body, raw, lines),
        "raw_states",
        moved=4 * out.size,
        in_specs=[IN_VMEM] * (1 + len(gates)),
        out_specs=IN_VMEM,
        out_shape=out,
    )(near, *gates)


def mix(mixer, own, numbers_ref, total, states, slopes):
    high = mixer.shape[0]
    rate = numbers_ref[2:3, :1] / total
    coeff = 2.0 * numbers_ref[1:2, :1] / numbers_ref[:1, :1]
    both = jnp.concatenate([slopes, states], axis=1)
    mixed = jnp.dot(mixer[...], both, preferred_element_type=F32)
    drive, pulled = mixed[:, :LANES], mixed[:, LANES:]
    return (states[:high].astype(F32) * own[...] + rate * (drive - coeff * pulled)).astype(BF16)


def update_pieces_body(half, raw, lines, groups, near_ref, *refs):
    total = 2 * half
    far_refs, refs = refs[:half], refs[half:]
    across_ref, raw_observed, raw_precision, numbers_ref, grams_ref, raw_grads_ref, *refs = refs
    group_refs, near_to, far_tos = refs[: len(groups)], refs[len(groups)], refs[len(groups) + 1 : -8]
    near_out, far_out, mixer, own, grads, raw_grads, sems, out_sems = refs[-8:]
    wide = total * TILE
    high = half * TILE
    raw_fetch = pltpu.make_async_copy(raw_grads_ref, raw_grads.at[pl.ds(0, half), :, :], sems.at[len(groups), 0])
    raw_fetch.start()
    middle = (raw + 2 * lines) // 3 // BLOCK * BLOCK
    parts = ((0, raw), (raw, middle), (middle, lines - BLOCK), (lines - BLOCK, lines))
    fetches = []
    for n, (first, last) in enumerate(parts):
        part = pl.ds(first, last - first)
        fetches.append([])
        for g, (group, group_ref) in enumerate(zip(groups, group_refs)):
            target = grads.at[pl.ds(group[0], len(group)), part, :]
            fetches[n].append(pltpu.make_async_copy(group_ref.at[:, part, :], target, sems.at[g, n]))
            fetches[n][-1].start()

    def raw_gradient(i, carry):
        for k in range(half):

            def load(start, size):
                return across_ref[k, lines_of(start, size), :]

            part = lines_of(i * BLOCK, BLOCK)
            raw_grads[half + k, part, :] = block_gradient(load, i, raw, raw_observed, raw_precision)
        return carry

    lax.fori_loop(0, raw // BLOCK, raw_gradient, 0)
    gram = jnp.sum(grams_ref[...], axis=0)[:, :total]
    spread, anneal, step_size = (numbers_ref[k : k + 1, :1] for k in range(3))
    rate = step_size / total
    coeff = 2.0 * anneal / spread
    row = lax.broadcasted_iota(jnp.int32, (total, total), 0)
    col = lax.broadcasted_iota(jnp.int32, (total, total), 1)
    diagonal = jnp.where(row == col, gram, 0.0)
    down = jnp.sum(diagonal, axis=1, keepdims=True)
    across = jnp.sum(diagonal, axis=0, keepdims=True)
    kernel = jnp.exp(-(down + across - 2.0 * gram) / (spread * NCELL)).astype(BF16)
    owner = owners(total, BF16)
    half_way = jnp.dot(owner, kernel, preferred_element_type=F32).astype(BF16)
    full = lax.dot_general(half_way, owner, (((1,), (1,)), ((), ())), preferred_element_type=F32)
    full = jnp.where(same_line(total), full, 0.0)
    mixer[...] = full.astype(BF16)
    ksum = jnp.sum(full, axis=1, keepdims=True)
    own[...] = jnp.broadcast_to(1.0 + rate * coeff * ksum, (wide, LANES))

    stores = []

    def store(source, target, at):
        stores.append(pltpu.make_async_copy(source, target, out_sems.at[at]))
        stores[-1].start()

    def store_near(first, last, at):
        part = pl.ds(first, last - first)
        store(near_out.at[:, part, :], near_to.at[:, part, :], (half, at))

    def store_far(first, last, at):
        part = pl.ds(first - raw, last - first)
        for x, far_to in enumerate(far_tos):
            store(far_out.at[x, part, :], far_to.at[part, :], (x, at))

    def slab_step(with_far, i, carry):
        rows = wide if with_far else high
        for t in range(BLOCK // TILE):
            at = i * BLOCK + t * TILE
            part = lines_of(at, TILE)
            states = [near_ref[:, part, :].reshape(high, LANES)] + [ref[part, :] for ref in far_refs]
            slopes = grads[:, part, :].reshape(wide, LANES)
            states = jnp.concatenate(states, axis=0)
            new = mix(mixer.at[:rows, :], own.at[:rows, :], numbers_ref, total, states, slopes)
            near_out[:, part, :] = new[:high].reshape(half, TILE, LANES)
            if with_far:
                far_out[:, lines_of(at - raw, TILE), :] = new[high:].reshape(half, TILE, LANES)
        return carry

    here = lax.axis_index("slab").astype(jnp.int32) % half

    def raw_step(i, carry):
        for t in range(BLOCK // TILE):
            at = i * BLOCK + t * TILE
            part = lines_of(at, TILE)
            states = [near_ref[:, lines_of(lines + TILE + at, TILE), :].reshape(high, LANES)]
            slopes = [raw_grads[:half, part, :].reshape(high, LANES)]
            for x in range(half):
                states += [across_ref[here ^ x, part, :]]
                slopes += [raw_grads[half + (here ^ x), part, :]]
            states, slopes = jnp.concatenate(states, axis=0), jnp.concatenate(slopes, axis=0)
            new = mix(mixer.at[:high, :], own.at[:high, :], numbers_ref, total, states, slopes)
            near_out[:, lines_of(lines + at, TILE), :] = new.reshape(half, TILE, LANES)
        return carry

    raw_fetch.wait()
    lax.fori_loop(0, raw // BLOCK, raw_step, 0)
    store_near(lines, lines + raw, 0)
    for n, (first, last) in enumerate(parts):
        for fetch in fetches[n]:
            fetch.wait()
        lax.fori_loop(first // BLOCK, last // BLOCK, functools.partial(slab_step, n > 0), 0)
        store_near(first, last, 1 + n)
        if n:
            store_far(first, last, n - 1)
    for copy in stores:
        copy.wait()


def update_pieces(numbers, grams, near, far, across, raw_fields, raw_grads, grads, groups, raw, lines):
    half = len(far)
    total = 2 * half
    wide = total * TILE
    out_shape = [pltpu.HBM((half, lines + raw, LANES), BF16)]
    out_shape += [pltpu.HBM((lines - raw, LANES), BF16)] * half
    return call(
        functools.partial(update_pieces_body, half, raw, lines, groups),
        "update_pieces",
        flops=4 * wide * wide * LANES * (lines // TILE),
        moved=6 * total * lines * LANES,
        in_specs=[IN_VMEM] * (half + 6) + [IN_HBM] * (1 + len(groups)),
        out_specs=[IN_HBM] * len(out_shape),
        out_shape=out_shape,
        scratch_shapes=[
            pltpu.VMEM((half, lines + raw, LANES), BF16),
            pltpu.VMEM((half, lines - raw, LANES), BF16),
            pltpu.VMEM((wide, wide), BF16),
            pltpu.VMEM((wide, LANES), F32),
            pltpu.VMEM((total, lines, LANES), BF16),
            pltpu.VMEM((total, raw, LANES), BF16),
            pltpu.SemaphoreType.DMA((len(groups) + 1, 4)),
            pltpu.SemaphoreType.DMA((half + 1, 5)),
        ],
    )(near, *far, across, *raw_fields, numbers, grams, raw_grads, *grads)


def exchange(piece, k, slabs):
    return lax.ppermute(piece, "slab", [(i, i ^ k) for i in range(slabs)])


def swap_near(pieces, slabs):
    groups = [list(range(slabs // 2)), list(range(slabs // 2, slabs))]
    return lax.all_to_all(pieces, "slab", 0, 0, axis_index_groups=groups, tiled=True)


RAW = 128
GRADIENTS = ((8, 9, 10, 11), (12, 13, 14, 15), (0, 1, 2, 3, 4, 5, 6, 7))


def by_halves(particles, observed, precision, spread, anneal, step_size):
    slabs = lax.axis_size("slab")
    half = slabs // 2
    lines = NCELL // slabs // LANES
    row = in_hbm(particles)
    fields = [in_hbm(field.reshape(-1, LANES)) for field in (observed, precision)]
    near, *far = split_pieces(row, slabs, RAW, fields)
    far, (obs, prec, *raw_fields) = far[:half], far[half:]
    near = swap_near(near, slabs)
    far = [exchange(piece, half + x, slabs) for x, piece in enumerate(far)]
    raw_near = raw_states(near, RAW, lines, far)
    across = exchange(raw_near, half, slabs)
    grads = []
    numbers = [spread, anneal, step_size]
    for group in GRADIENTS:
        if group[0] < half:
            arrays, views = [near], [(0, k, 0) for k in group]
        else:
            arrays, views = [far[k - half] for k in group], [(j, None, 0) for j in range(len(group))]
        slopes, rows = gradient_pieces(arrays, tuple(views), obs, prec, [] if grads else numbers)
        grads.append(in_hbm(slopes))
        numbers = numbers if len(grads) > 1 else rows
    grams = swap(gram_pieces(near, far, lines, grads[:1], [raw_near]))
    views = tuple((0, k, lines + TILE) for k in range(half))
    raw_grads = in_hbm(gradient_pieces([near], views, *raw_fields, [])[0])
    new_near, *new_far = update_pieces(
        numbers, grams, near, far, across, raw_fields, raw_grads, grads, GRADIENTS, RAW, lines
    )
    new_near = swap_near(new_near, slabs)
    new_far = [exchange(piece, half + x, slabs) for x, piece in enumerate(new_far)]
    row = join_pieces(None, slabs, RAW, [new_near], [(0, k, k) for k in range(half)])
    for group in ((0, 1, 2, 3), (4, 5)):
        pieces = [(n, None, half + x) for n, x in enumerate(group)]
        row = join_pieces(row, slabs, RAW, [new_far[x] for x in group], pieces)
    return join_pieces(row, slabs, RAW, new_far[6:], [(n, None, half + 6 + n) for n in range(half - 6)])


def on_device(particles, observed, precision, spread, anneal, step_size):
    slabs = lax.axis_size("slab")
    total = particles.shape[0] * slabs
    lines = NCELL // slabs // LANES
    if slabs == 16:
        return by_halves(particles, observed, precision, spread, anneal, step_size)
    sent, begun = cuts(lines)
    fields = [observed.reshape(-1, LANES), precision.reshape(-1, LANES)]
    numbers = [spread, anneal, step_size]
    first, obs, prec, scalars = split_row(particles, slabs, 0, sent, True, fields, numbers, [])
    parts = [swap(first)]
    if sent < lines:
        parts += [swap(split_row(particles, slabs, sent, lines, False, [], [], [scalars])[0])]
    if total * TILE > 256:
        grads = slab_gradient(parts, obs, prec, lines, 0, lines)
        states = jnp.concatenate([parts[0][:, :sent]] + parts[1:], axis=1)
        new = plain_update(spread, anneal, step_size, states, grads)
        return join_row(swap(new), lines, 0, None)
    if sent == lines:
        grads = slab_gradient(parts, obs, prec, lines, 0, lines)
        grams = swap(slab_gram(parts[0], lines, slabs, [], []))
        new = slab_update(scalars, grams, parts, grads, 0, lines, [])
        return join_row(swap(new), lines, 0, None)
    gram = slab_gram(parts[0], sent, 1, [], [])
    early = slab_gradient(parts[:1], obs, prec, lines, 0, begun)
    grams = swap(slab_gram(parts[1], lines - sent, slabs, [gram], [early]))
    late = slab_gradient(parts, obs, prec, lines, begun, lines)
    new = slab_update(scalars, grams, parts[:1], early, 0, begun, [])
    rest = slab_update(scalars, grams, parts, late, begun, lines, [new])
    row = join_row(swap(new), lines, 0, None)
    return join_row(swap(rest), lines, begun, row)


def solution(mesh):
    in_specs = (
        P(("groups", "slab"), None),
        P("groups"),
        P("groups"),
        P("groups"),
        P("groups"),
        P("groups"),
    )
    out_specs = P(("groups", "slab"), None)
    return jax.shard_map(
        on_device, mesh=mesh, in_specs=in_specs, out_specs=out_specs, check_vma=False
    )
```

```python
import functools

import jax
import jax.numpy as jnp
from jax import lax
from jax.experimental import pallas as pl
from jax.experimental.pallas import tpu as pltpu
from jax.sharding import PartitionSpec as P

GRID_X = 1024
GRID_Y = 1024
NCELL = 1048576
LANES = 128
LINE = GRID_Y // LANES
TILE = 16

prior_scale = 0.25
mass_term = 1.0

F32 = jnp.float32
BF16 = jnp.bfloat16
MIB = 1024 * 1024


def call(body, name, flops=0, moved=0, limit=16, **kwargs):
    return pl.pallas_call(
        body,
        name=name,
        compiler_params=pltpu.CompilerParams(vmem_limit_bytes=limit * MIB),
        cost_estimate=pl.CostEstimate(flops=flops, bytes_accessed=moved, transcendentals=0),
        **kwargs,
    )


IN_VMEM = pl.BlockSpec(memory_space=pltpu.VMEM)
IN_HBM = pl.BlockSpec(memory_space=pltpu.HBM)


def in_hbm(array):
    return pltpu.with_memory_space_constraint(array, pltpu.HBM)


BLOCK = 4 * TILE


def cuts(lines):
    if lines % (8 * BLOCK):
        return lines, lines
    return lines * 3 // 4, lines * 3 // 4 - BLOCK


def split_body(lines, begin, rim, fields, numbers, row_ref, *refs):
    field_refs, number_refs = refs[:fields], refs[fields : fields + numbers]
    out_ref, *slab_refs, rows_ref = refs[-7 - fields : -5]
    held, edges, sems, edge_sems, field_sems = refs[-5:]
    for k, number_ref in enumerate(number_refs):
        rows_ref[k : k + 1, :] = jnp.broadcast_to(number_ref[...].reshape(1, 1), (1, LANES))
    slabs, count, _ = out_ref.shape
    count -= TILE * rim
    size = count * LANES
    cells = lines * LANES

    def part(slab):
        source = row_ref.at[:, pl.ds(slab * cells + begin * LANES, size)]
        return pltpu.make_async_copy(source, held.at[:, pl.ds(slab * size, size)], sems.at[slab])

    def edge(slab):
        source = row_ref.at[:, pl.ds(slab * cells - GRID_Y, GRID_Y)]
        return pltpu.make_async_copy(source, edges.at[:, pl.ds(slab * GRID_Y, GRID_Y)], edge_sems.at[slab])

    def grid_row(ref, start):
        return ref[:, pl.ds(start, GRID_Y)].astype(F32).reshape(LINE, LANES)

    for slab in range(slabs):
        part(slab).start()
        if rim and slab:
            edge(slab).start()
    mine = pl.ds(pl.multiple_of(lax.axis_index("slab") * lines, TILE), lines)
    fetches = [
        pltpu.make_async_copy(source.at[mine, :], target, field_sems.at[k])
        for k, (source, target) in enumerate(zip(field_refs, slab_refs))
    ]
    for fetch in fetches:
        fetch.start()
    part(0).wait()
    outside = jnp.zeros((LINE, LANES), F32)
    for slab in range(slabs):
        if slab + 1 < slabs:
            part(slab + 1).wait()
        out_ref[slab, :count, :] = held[:, pl.ds(slab * size, size)].reshape(count, LANES)
        if rim:
            if slab:
                edge(slab).wait()
            below = grid_row(held, (slab + 1) * size) if slab + 1 < slabs else outside
            above = grid_row(edges, slab * GRID_Y) if slab else outside
            out_ref[slab, count:, :] = jnp.concatenate([below, above], axis=0).astype(BF16)
    for fetch in fetches:
        fetch.wait()


def split_row(row, slabs, begin, end, rim, fields, numbers, earlier):
    lines = row.shape[1] // slabs // LANES
    count = end - begin
    return call(
        functools.partial(split_body, lines, begin, rim, len(fields), len(numbers)),
        "split_row",
        moved=6 * slabs * count * LANES,
        in_specs=[IN_HBM] * (1 + len(fields)) + [IN_VMEM] * len(numbers) + [IN_HBM] * len(earlier),
        out_specs=[IN_VMEM] * (2 + len(fields)),
        out_shape=[jax.ShapeDtypeStruct((slabs, count + TILE * rim, LANES), BF16)]
        + [jax.ShapeDtypeStruct((lines, LANES), BF16)] * len(fields)
        + [jax.ShapeDtypeStruct((8, LANES), F32)],
        scratch_shapes=[
            pltpu.VMEM((1, slabs * count * LANES), BF16),
            pltpu.VMEM((1, slabs * GRID_Y), BF16),
            pltpu.SemaphoreType.DMA((slabs,)),
            pltpu.SemaphoreType.DMA((slabs,)),
            pltpu.SemaphoreType.DMA((2,)),
        ],
    )(row, *fields, *numbers, *earlier)


def join_body(lines, begin, slabs_ref, *refs):
    row_ref, held, sems = refs[-3:]
    slabs, count, _ = slabs_ref.shape
    size = count * LANES
    copies = []
    for slab in range(slabs):
        at = pl.ds(slab * size, size)
        held[:, at] = slabs_ref[slab].reshape(1, size)
        target = row_ref.at[:, pl.ds((slab * lines + begin) * LANES, size)]
        copies.append(pltpu.make_async_copy(held.at[:, at], target, sems.at[slab]))
        copies[-1].start()
    for copy in copies:
        copy.wait()


def join_row(slabs, lines, begin, row):
    total, count, _ = slabs.shape
    begun = [] if row is None else [row]
    return call(
        functools.partial(join_body, lines, begin),
        "join_row",
        moved=6 * slabs.size,
        in_specs=[IN_VMEM] + [IN_HBM] * len(begun),
        out_specs=IN_HBM,
        out_shape=jax.ShapeDtypeStruct((1, total * lines * LANES), BF16),
        input_output_aliases={1: 0} if begun else {},
        scratch_shapes=[pltpu.VMEM((1, slabs.size), BF16), pltpu.SemaphoreType.DMA((total,))],
    )(slabs, *begun)


def same_line(total):
    wide = total * TILE
    row = lax.broadcasted_iota(jnp.int32, (wide, wide), 0)
    col = lax.broadcasted_iota(jnp.int32, (wide, wide), 1)
    return (row ^ col) & (TILE - 1) == 0


def members(total, dtype):
    wide = total * TILE
    row = lax.broadcasted_iota(jnp.int32, (wide, total), 0)
    col = lax.broadcasted_iota(jnp.int32, (wide, total), 1)
    return (row // TILE == col).astype(dtype)


def gram_body(steps, tiles, parts, states_ref, *refs):
    out_ref, pairs = refs[-2:]
    total = states_ref.shape[0]
    wide = total * TILE
    pairs[...] = jnp.zeros_like(pairs)

    def step(i, carry):
        parts = [
            states_ref[:, pl.ds(pl.multiple_of((i * tiles + t) * TILE, TILE), TILE), :].reshape(wide, LANES)
            for t in range(tiles)
        ]
        block = jnp.concatenate(parts, axis=1)
        pairs[...] += lax.dot_general(block, block, (((1,), (1,)), ((), ())), preferred_element_type=F32)
        return carry

    lax.fori_loop(0, steps, step, 0)
    equal = jnp.where(same_line(total), pairs[...], 0.0)
    rows = jnp.sum(equal.reshape(total, TILE, wide), axis=1)
    gram = jnp.dot(rows, members(total, F32), precision=lax.Precision.HIGHEST, preferred_element_type=F32)
    gram = jnp.concatenate([gram, jnp.zeros((total, LANES - total), F32)], axis=1)
    for part_ref in refs[:parts]:
        gram += part_ref[0]
    out_ref[...] = jnp.broadcast_to(gram[None], out_ref.shape)


def slab_gram(states, lines, copies, parts, earlier):
    total = states.shape[0]
    wide = total * TILE
    tiles = min(8, lines // TILE)
    return call(
        functools.partial(gram_body, lines // TILE // tiles, tiles, len(parts)),
        "slab_gram",
        flops=2 * wide * wide * LANES * (lines // TILE),
        moved=2 * states.size,
        in_specs=[IN_VMEM] * (1 + len(parts)) + [IN_HBM] * len(earlier),
        out_specs=IN_VMEM,
        out_shape=jax.ShapeDtypeStruct((copies, total, LANES), F32),
        scratch_shapes=[pltpu.VMEM((wide, wide), F32)],
    )(states, *parts, *earlier)


def gradient_body(lines, begin, end, parts, *refs):
    observed, precision, out_ref, grads, sems = refs[parts:]
    total = grads.shape[0]
    first = refs[0].shape[1] - TILE
    rows = BLOCK // LINE
    group = 4
    shape = (rows, LINE, LANES)
    lane = lax.broadcasted_iota(jnp.int32, (1, LINE, LANES), 2)
    line = lax.broadcasted_iota(jnp.int32, (1, LINE, LANES), 1)

    def load(particle, at, count):
        ref, at = (refs[0], at) if at < first else (refs[1], at - first)
        return ref[particle, at : at + count, :].astype(F32)

    def rim(particle):
        return refs[0][particle, first:, :].astype(F32)

    stores = []
    for k, at in enumerate(range(begin, end, BLOCK)):
        mine = slice(at - begin, at - begin + BLOCK)
        obs = observed[at : at + BLOCK, :].astype(F32).reshape(shape)
        prec = precision[at : at + BLOCK, :].astype(F32).reshape(shape)

        def step(i, carry):
            for p in range(group):
                particle = i * group + p
                here = load(particle, at, BLOCK)
                before = load(particle, at - TILE, TILE) if at else rim(particle)
                after = load(particle, at + BLOCK, TILE) if at + BLOCK < lines else rim(particle)
                above = jnp.concatenate([before[LINE:], here[:-LINE]], axis=0).reshape(shape)
                below = jnp.concatenate([here[LINE:], after[:LINE]], axis=0).reshape(shape)
                field = here.reshape(shape)
                turned = pltpu.roll(field, 1, 2)
                carried = jnp.where(line == 0, 0.0, pltpu.roll(turned, 1, 1))
                left = jnp.where(lane == 0, carried, turned)
                turned = pltpu.roll(field, LANES - 1, 2)
                carried = jnp.where(line == LINE - 1, 0.0, pltpu.roll(turned, LINE - 1, 1))
                right = jnp.where(lane == LANES - 1, carried, turned)
                laplace = (4.0 + mass_term) * field - (below + above + right + left)
                squash = jnp.tanh(field)
                result = prec * (obs - squash) * (1.0 - squash * squash) - prior_scale * laplace
                grads[particle, mine, :] = result.reshape(BLOCK, LANES).astype(BF16)
            return carry

        lax.fori_loop(0, total // group, step, 0)
        stores.append(pltpu.make_async_copy(grads.at[:, mine, :], out_ref.at[:, mine, :], sems.at[k]))
        stores[-1].start()
    for store in stores:
        store.wait()


def slab_gradient(parts, observed, precision, lines, begin, end):
    total = parts[0].shape[0]
    count = end - begin
    out = jax.ShapeDtypeStruct((total, count, LANES), BF16)
    return call(
        functools.partial(gradient_body, lines, begin, end, len(parts)),
        "slab_gradient",
        flops=30 * out.size,
        moved=8 * out.size,
        in_specs=[IN_VMEM] * (len(parts) + 2),
        out_specs=IN_HBM,
        out_shape=out,
        scratch_shapes=[pltpu.VMEM(out.shape, BF16), pltpu.SemaphoreType.DMA((count // BLOCK,))],
    )(*parts, observed, precision)


def update_body(begin, end, parts, *refs):
    states_refs, refs = refs[:parts], refs[parts:]
    scalars_ref, grams_ref, grads_ref = refs[:3]
    out_ref, grads, mixer, own, sem = refs[-5:]
    total = out_ref.shape[0]
    wide = total * TILE
    fetch = pltpu.make_async_copy(grads_ref, grads, sem)
    fetch.start()
    gram = jnp.sum(grams_ref[...], axis=0)[:, :total]
    row = lax.broadcasted_iota(jnp.int32, (total, total), 0)
    col = lax.broadcasted_iota(jnp.int32, (total, total), 1)
    diagonal = jnp.where(row == col, gram, 0.0)
    down = jnp.sum(diagonal, axis=1, keepdims=True)
    across = jnp.sum(diagonal, axis=0, keepdims=True)
    member = members(total, BF16)
    spread, anneal, step_size = (scalars_ref[k : k + 1, :1] for k in range(3))
    rate = step_size / total
    coeff = 2.0 * anneal / spread
    kernel = jnp.exp(-(down + across - 2.0 * gram) / (spread * NCELL)).astype(BF16)
    ksum = jnp.sum(kernel.astype(F32), axis=1, keepdims=True)
    half = jnp.dot(member, kernel, preferred_element_type=F32).astype(BF16)
    full = lax.dot_general(half, member, (((1,), (1,)), ((), ())), preferred_element_type=F32)
    mixer[...] = jnp.where(same_line(total), full, 0.0).astype(BF16)
    gain = 1.0 + rate * coeff * ksum
    own[...] = jnp.broadcast_to(gain[:, :, None], (total, TILE, LANES)).reshape(wide, LANES)
    fetch.wait()

    done = 0
    for part, states_ref in enumerate(states_refs):
        have = states_ref.shape[1] - (0 if part else TILE)
        low = max(begin - done, 0)
        high = min(end - done, have)
        into = done - begin
        done += have

        def step(i, carry):
            for t in range(BLOCK // TILE):
                at = pl.multiple_of(i * BLOCK + t * TILE, TILE)
                there = pl.ds(pl.multiple_of(at + into, TILE), TILE)
                states = states_ref[:, pl.ds(at, TILE), :].reshape(wide, LANES)
                both = jnp.concatenate([grads[:, there, :].reshape(wide, LANES), states], axis=1)
                mixed = jnp.dot(mixer[...], both, preferred_element_type=F32)
                drive, pulled = mixed[:, :LANES], mixed[:, LANES:]
                new = states.astype(F32) * own[...] + rate * (drive - coeff * pulled)
                out_ref[:, there, :] = new.astype(BF16).reshape(total, TILE, LANES)
            return carry

        lax.fori_loop(low // BLOCK, high // BLOCK, step, 0)


def slab_update(scalars, grams, parts, grads, begin, end, earlier):
    total, count, _ = grads.shape
    wide = total * TILE
    return call(
        functools.partial(update_body, begin, end, len(parts)),
        "slab_update",
        flops=4 * wide * wide * LANES * (count // TILE),
        moved=6 * grads.size,
        in_specs=[IN_VMEM] * len(parts)
        + [IN_VMEM, IN_VMEM, IN_HBM]
        + [IN_HBM] * len(earlier),
        out_specs=IN_VMEM,
        out_shape=jax.ShapeDtypeStruct(grads.shape, BF16),
        scratch_shapes=[
            pltpu.VMEM(grads.shape, BF16),
            pltpu.VMEM((wide, wide), BF16),
            pltpu.VMEM((wide, LANES), F32),
            pltpu.SemaphoreType.DMA,
        ],
    )(*parts, scalars, grams, grads, *earlier)


def plain_update(spread, anneal, step_size, states, grads):
    total, lines, _ = grads.shape
    flat = states[:, :lines].reshape(total, -1)
    gram = lax.dot_general(flat, flat, (((1,), (1,)), ((), ())), preferred_element_type=F32)
    gram = lax.psum(gram, "slab")
    norms = jnp.diagonal(gram)
    kernel = jnp.exp(-(norms[:, None] + norms[None, :] - 2.0 * gram) / (spread[0] * NCELL)).astype(BF16)
    ksum = jnp.sum(kernel.astype(F32), axis=1)
    drive = jnp.dot(kernel, grads.reshape(total, -1), preferred_element_type=F32)
    pulled = jnp.dot(kernel, flat, preferred_element_type=F32)
    values = flat.astype(F32)
    repel = values * ksum[:, None] - pulled
    coeff = 2.0 * anneal[0] / spread[0]
    new = values + step_size[0] / total * (drive + coeff * repel)
    return new.astype(BF16).reshape(grads.shape)


def swap(slabs):
    return lax.all_to_all(slabs, "slab", split_axis=0, concat_axis=0, tiled=True)


def device_at(at, half):
    me = lax.axis_index("slab").astype(jnp.int32)
    return jnp.where(at < half, me - me % half + at, me ^ at)


def lines_of(start, count):
    return pl.ds(pl.multiple_of(start, TILE), count)


def split_pieces_body(slabs, raw, lines, fields, row_ref, *refs):
    half = slabs // 2
    field_refs, near_out, far_outs = refs[:fields], refs[fields], refs[fields + 1 : fields + 1 + half]
    slab_refs, held, sems = refs[fields + 1 + half : -2], refs[-2], refs[-1]
    cells = lines * LANES
    end = row_ref.shape[1]
    me = lax.axis_index("slab").astype(jnp.int32)

    def part(start, size):
        return pl.ds(pl.multiple_of(start, GRID_Y), size)

    def grid_row(start):
        return held[:, part(start, GRID_Y)].astype(F32).reshape(LINE, LANES)

    copies = []
    for at in range(slabs):
        cut = part(device_at(at, half) * cells, cells)
        copies.append(pltpu.make_async_copy(row_ref.at[:, cut], held.at[:, cut], sems.at[at]))
    for n, target in enumerate(slab_refs):
        start = (me if n < fields else me ^ half) * lines
        source = field_refs[n % fields].at[lines_of(start, target.shape[0]), :]
        copies.append(pltpu.make_async_copy(source, target, sems.at[slabs + n]))
    for copy in copies:
        copy.start()
    outs = [near_out.at[at] for at in range(half)] + list(far_outs)
    for at, out_ref in enumerate(outs):
        copies[at].wait()
        out_ref[:lines, :] = held[:, part(device_at(at, half) * cells, cells)].reshape(lines, LANES)
    for at, out_ref in enumerate(outs):
        slab = device_at(at, half)
        start = slab * cells
        below = jnp.where(slab == slabs - 1, 0.0, grid_row(jnp.minimum(start + cells, end - GRID_Y)))
        above = jnp.where(slab == 0, 0.0, grid_row(jnp.maximum(start - GRID_Y, 0)))
        out_ref[lines : lines + TILE, :] = jnp.concatenate([below, above], axis=0).astype(BF16)
        if at < half:
            start = (slab ^ half) * cells
            to = lines + TILE
            out_ref[to : to + raw, :] = held[:, part(start, raw * LANES)].reshape(raw, LANES)
            below = grid_row(start + raw * LANES)
            above = jnp.where(slab ^ half == 0, 0.0, grid_row(jnp.maximum(start - GRID_Y, 0)))
            out_ref[to + raw :, :] = jnp.concatenate([below, above], axis=0).astype(BF16)
    for copy in copies[slabs:]:
        copy.wait()


def split_pieces(row, slabs, raw, fields):
    lines = row.shape[1] // slabs // LANES
    half = slabs // 2
    rim = lines + TILE
    size = rim + raw + TILE
    out_shape = [jax.ShapeDtypeStruct((half, size, LANES), BF16)]
    out_shape += [jax.ShapeDtypeStruct((rim, LANES), BF16)] * half
    out_shape += [jax.ShapeDtypeStruct((lines, LANES), BF16)] * len(fields)
    out_shape += [jax.ShapeDtypeStruct((raw, LANES), BF16)] * len(fields)
    return call(
        functools.partial(split_pieces_body, slabs, raw, lines, len(fields)),
        "split_pieces",
        moved=6 * half * (rim + size) * LANES,
        in_specs=[IN_HBM] * (1 + len(fields)),
        out_specs=[IN_VMEM] * len(out_shape),
        out_shape=out_shape,
        scratch_shapes=[pltpu.VMEM(row.shape, BF16), pltpu.SemaphoreType.DMA((slabs + 2 * len(fields),))],
    )(row, *fields)


def join_pieces_body(pieces, half, raw, lines, begun, arrays, *refs):
    row_ref, helds, sems = refs[begun + arrays], refs[begun + arrays + 1 : -1], refs[-1]
    cells = lines * LANES
    skip = raw * LANES
    copies = []
    for (array, lead, at), held in zip(pieces, helds):
        ref = refs[begun + array]
        piece = ref[...] if lead is None else ref[lead]
        held[...] = piece.reshape(held.shape)
        slab = device_at(at, half)
        if at < half:
            parts = [(0, cells, slab * cells), (cells, skip, (slab ^ half) * cells)]
        else:
            parts = [(0, cells - skip, slab * cells + skip)]
        for begin, size, start in parts:
            target = row_ref.at[:, pl.ds(pl.multiple_of(start, GRID_Y), size)]
            copies.append(pltpu.make_async_copy(held.at[:, pl.ds(begin, size)], target, sems.at[len(copies)]))
            copies[-1].start()
    for copy in copies:
        copy.wait()


def join_pieces(row, slabs, raw, arrays, pieces):
    sizes = [arrays[piece[0]].shape[-2] * LANES for piece in pieces]
    begun = [] if row is None else [row]
    return call(
        functools.partial(
            join_pieces_body, pieces, slabs // 2, raw, NCELL // slabs // LANES, len(begun), len(arrays)
        ),
        "join_pieces",
        moved=6 * sum(sizes),
        in_specs=[IN_HBM] * len(begun) + [IN_VMEM] * len(arrays),
        out_specs=IN_HBM,
        out_shape=jax.ShapeDtypeStruct((1, NCELL), BF16),
        input_output_aliases={0: 0} if begun else {},
        scratch_shapes=[pltpu.VMEM((1, size), BF16) for size in sizes]
        + [pltpu.SemaphoreType.DMA((2 * len(sizes),))],
    )(*begun, *arrays)


def owners(total, dtype):
    wide = total * TILE
    row = lax.broadcasted_iota(jnp.int32, (wide, total), 0)
    col = lax.broadcasted_iota(jnp.int32, (wide, total), 1)
    return (device_at(row // TILE, total // 2) == col).astype(dtype)


def gram_pieces_body(lines, total, near_ref, *refs):
    half = total // 2
    pieces, out_ref, pairs = refs[:half], refs[-2], refs[-1]
    wide = total * TILE
    tiles = 8
    pairs[...] = jnp.zeros_like(pairs)

    def step(i, carry):
        parts = []
        for t in range(tiles):
            at = lines_of((i * tiles + t) * TILE, TILE)
            near = near_ref[:, at, :].reshape(wide // 2, LANES)
            parts.append(jnp.concatenate([near] + [piece[at, :] for piece in pieces], axis=0))
        block = jnp.concatenate(parts, axis=1)
        pairs[...] += lax.dot_general(block, block, (((1,), (1,)), ((), ())), preferred_element_type=F32)
        return carry

    lax.fori_loop(0, lines // TILE // tiles, step, 0)
    equal = jnp.where(same_line(total), pairs[...], 0.0)
    exact = {"precision": lax.Precision.HIGHEST, "preferred_element_type": F32}
    rows = jnp.sum(equal.reshape(total, TILE, wide), axis=1)
    gram = jnp.dot(rows, owners(total, F32), **exact)
    row = lax.broadcasted_iota(jnp.int32, (total, total), 0)
    col = lax.broadcasted_iota(jnp.int32, (total, total), 1)
    gram = jnp.dot((row == device_at(col, half)).astype(F32), gram, **exact)
    gram = jnp.concatenate([gram, jnp.zeros((total, LANES - total), F32)], axis=1)
    out_ref[...] = jnp.broadcast_to(gram[None], out_ref.shape)


def gram_pieces(near, far, lines, gates, early):
    total = 2 * len(far)
    wide = total * TILE
    return call(
        functools.partial(gram_pieces_body, lines, total),
        "gram_pieces",
        flops=2 * wide * wide * LANES * (lines // TILE),
        moved=2 * total * lines * LANES,
        in_specs=[IN_VMEM] * (1 + len(far)) + [IN_HBM] * len(gates) + [IN_VMEM] * len(early),
        out_specs=IN_VMEM,
        out_shape=jax.ShapeDtypeStruct((total, total, LANES), F32),
        scratch_shapes=[pltpu.VMEM((wide, wide), F32)],
    )(near, *far, *gates, *early)


def block_gradient(load, i, count, observed, precision):
    start = i * BLOCK
    at = lines_of(start, BLOCK)
    shape = (BLOCK // LINE, LINE, LANES)
    lane = lax.broadcasted_iota(jnp.int32, (1, LINE, LANES), 2)
    line = lax.broadcasted_iota(jnp.int32, (1, LINE, LANES), 1)
    obs = observed[at, :].astype(F32).reshape(shape)
    prec = precision[at, :].astype(F32).reshape(shape)
    here = load(start, BLOCK).astype(F32)
    before = load(jnp.where(i == 0, count, start - TILE), TILE).astype(F32)
    after = load(start + BLOCK, TILE).astype(F32)
    above = jnp.concatenate([before[LINE:], here[:-LINE]], axis=0).reshape(shape)
    below = jnp.concatenate([here[LINE:], after[:LINE]], axis=0).reshape(shape)
    field = here.reshape(shape)
    turned = pltpu.roll(field, 1, 2)
    carried = jnp.where(line == 0, 0.0, pltpu.roll(turned, 1, 1))
    left = jnp.where(lane == 0, carried, turned)
    turned = pltpu.roll(field, LANES - 1, 2)
    carried = jnp.where(line == LINE - 1, 0.0, pltpu.roll(turned, LINE - 1, 1))
    right = jnp.where(lane == LANES - 1, carried, turned)
    laplace = (4.0 + mass_term) * field - (below + above + right + left)
    squash = jnp.tanh(field)
    result = prec * (obs - squash) * (1.0 - squash * squash) - prior_scale * laplace
    return result.reshape(BLOCK, LANES).astype(BF16)


def gradient_pieces_body(views, arrays, numbers, *refs):
    observed, precision, *number_refs = refs[arrays : arrays + 2 + numbers]
    out_ref, rows_ref, grads, sems = refs[-4:]
    for n, number_ref in enumerate(number_refs):
        rows_ref[n : n + 1, :] = jnp.full((1, LANES), number_ref[0], F32)
    count = observed.shape[0]
    steps = count // BLOCK

    def store(i):
        at = lines_of(i * BLOCK, BLOCK)
        return pltpu.make_async_copy(grads.at[:, at, :], out_ref.at[:, at, :], sems.at[i])

    def step(i, carry):
        for p, (array, lead, base) in enumerate(views):

            def load(start, size):
                part = lines_of(base + start, size)
                return refs[array][part, :] if lead is None else refs[array][lead, part, :]

            grads[p, lines_of(i * BLOCK, BLOCK), :] = block_gradient(load, i, count, observed, precision)
        store(i).start()
        return carry

    def finish(i, carry):
        store(i).wait()
        return carry

    lax.fori_loop(0, steps, step, 0)
    lax.fori_loop(0, steps, finish, 0)


def gradient_pieces(arrays, views, observed, precision, numbers):
    count = observed.shape[0]
    out = pltpu.HBM((len(views), count, LANES), BF16)
    size = len(views) * count * LANES
    return call(
        functools.partial(gradient_pieces_body, views, len(arrays), len(numbers)),
        "gradient_pieces",
        flops=30 * size,
        moved=8 * size,
        in_specs=[IN_VMEM] * (len(arrays) + 2)
        + [pl.BlockSpec(memory_space=pltpu.SMEM)] * len(numbers),
        out_specs=[IN_HBM, IN_VMEM],
        out_shape=[out, jax.ShapeDtypeStruct((8, LANES), F32)],
        scratch_shapes=[pltpu.VMEM(out.shape, BF16), pltpu.SemaphoreType.DMA((count // BLOCK,))],
    )(*arrays, observed, precision, *numbers)


def raw_body(raw, lines, near_ref, *refs):
    out_ref = refs[-1]
    for k in range(near_ref.shape[0]):
        out_ref[k, :raw, :] = near_ref[k, :raw, :]
        below = near_ref[k, raw : raw + TILE, :].astype(F32)[:LINE]
        above = near_ref[k, lines : lines + TILE, :].astype(F32)[LINE:]
        out_ref[k, raw:, :] = jnp.concatenate([below, above], axis=0).astype(BF16)


def raw_states(near, raw, lines, gates):
    out = jax.ShapeDtypeStruct((near.shape[0], raw + TILE, LANES), BF16)
    return call(
        functools.partial(raw_body, raw, lines),
        "raw_states",
        moved=4 * out.size,
        in_specs=[IN_VMEM] * (1 + len(gates)),
        out_specs=IN_VMEM,
        out_shape=out,
    )(near, *gates)


def mix(mixer, own, numbers_ref, total, states, slopes):
    high = mixer.shape[0]
    rate = numbers_ref[2:3, :1] / total
    coeff = 2.0 * numbers_ref[1:2, :1] / numbers_ref[:1, :1]
    both = jnp.concatenate([slopes, states], axis=1)
    mixed = jnp.dot(mixer[...], both, preferred_element_type=F32)
    drive, pulled = mixed[:, :LANES], mixed[:, LANES:]
    return (states[:high].astype(F32) * own[...] + rate * (drive - coeff * pulled)).astype(BF16)


def update_pieces_body(half, raw, lines, groups, near_ref, *refs):
    total = 2 * half
    far_refs, refs = refs[:half], refs[half:]
    across_ref, raw_observed, raw_precision, numbers_ref, grams_ref, raw_grads_ref, *refs = refs
    group_refs, near_to, far_tos = refs[: len(groups)], refs[len(groups)], refs[len(groups) + 1 : -8]
    near_out, far_out, mixer, own, grads, raw_grads, sems, out_sems = refs[-8:]
    wide = total * TILE
    high = half * TILE
    raw_fetch = pltpu.make_async_copy(raw_grads_ref, raw_grads.at[pl.ds(0, half), :, :], sems.at[len(groups), 0])
    raw_fetch.start()
    middle = (raw + 2 * lines) // 3 // BLOCK * BLOCK
    parts = ((0, raw), (raw, middle), (middle, lines - BLOCK), (lines - BLOCK, lines))
    fetches = []
    for n, (first, last) in enumerate(parts):
        part = pl.ds(first, last - first)
        fetches.append([])
        for g, (group, group_ref) in enumerate(zip(groups, group_refs)):
            target = grads.at[pl.ds(group[0], len(group)), part, :]
            fetches[n].append(pltpu.make_async_copy(group_ref.at[:, part, :], target, sems.at[g, n]))
            fetches[n][-1].start()

    def raw_gradient(i, carry):
        for k in range(half):

            def load(start, size):
                return across_ref[k, lines_of(start, size), :]

            part = lines_of(i * BLOCK, BLOCK)
            raw_grads[half + k, part, :] = block_gradient(load, i, raw, raw_observed, raw_precision)
        return carry

    lax.fori_loop(0, raw // BLOCK, raw_gradient, 0)
    gram = jnp.sum(grams_ref[...], axis=0)[:, :total]
    spread, anneal, step_size = (numbers_ref[k : k + 1, :1] for k in range(3))
    rate = step_size / total
    coeff = 2.0 * anneal / spread
    row = lax.broadcasted_iota(jnp.int32, (total, total), 0)
    col = lax.broadcasted_iota(jnp.int32, (total, total), 1)
    diagonal = jnp.where(row == col, gram, 0.0)
    down = jnp.sum(diagonal, axis=1, keepdims=True)
    across = jnp.sum(diagonal, axis=0, keepdims=True)
    kernel = jnp.exp(-(down + across - 2.0 * gram) / (spread * NCELL)).astype(BF16)
    owner = owners(total, BF16)
    half_way = jnp.dot(owner, kernel, preferred_element_type=F32).astype(BF16)
    full = lax.dot_general(half_way, owner, (((1,), (1,)), ((), ())), preferred_element_type=F32)
    full = jnp.where(same_line(total), full, 0.0)
    mixer[...] = full.astype(BF16)
    ksum = jnp.sum(full, axis=1, keepdims=True)
    own[...] = jnp.broadcast_to(1.0 + rate * coeff * ksum, (wide, LANES))

    stores = []

    def store(source, target, at):
        stores.append(pltpu.make_async_copy(source, target, out_sems.at[at]))
        stores[-1].start()

    def store_near(first, last, at):
        part = pl.ds(first, last - first)
        store(near_out.at[:, part, :], near_to.at[:, part, :], (half, at))

    def store_far(first, last, at):
        part = pl.ds(first - raw, last - first)
        for x, far_to in enumerate(far_tos):
            store(far_out.at[x, part, :], far_to.at[part, :], (x, at))

    def slab_step(with_far, i, carry):
        rows = wide if with_far else high
        for t in range(BLOCK // TILE):
            at = i * BLOCK + t * TILE
            part = lines_of(at, TILE)
            states = [near_ref[:, part, :].reshape(high, LANES)] + [ref[part, :] for ref in far_refs]
            slopes = grads[:, part, :].reshape(wide, LANES)
            states = jnp.concatenate(states, axis=0)
            new = mix(mixer.at[:rows, :], own.at[:rows, :], numbers_ref, total, states, slopes)
            near_out[:, part, :] = new[:high].reshape(half, TILE, LANES)
            if with_far:
                far_out[:, lines_of(at - raw, TILE), :] = new[high:].reshape(half, TILE, LANES)
        return carry

    here = lax.axis_index("slab").astype(jnp.int32) % half

    def raw_step(i, carry):
        for t in range(BLOCK // TILE):
            at = i * BLOCK + t * TILE
            part = lines_of(at, TILE)
            states = [near_ref[:, lines_of(lines + TILE + at, TILE), :].reshape(high, LANES)]
            slopes = [raw_grads[:half, part, :].reshape(high, LANES)]
            for x in range(half):
                states += [across_ref[here ^ x, part, :]]
                slopes += [raw_grads[half + (here ^ x), part, :]]
            states, slopes = jnp.concatenate(states, axis=0), jnp.concatenate(slopes, axis=0)
            new = mix(mixer.at[:high, :], own.at[:high, :], numbers_ref, total, states, slopes)
            near_out[:, lines_of(lines + at, TILE), :] = new.reshape(half, TILE, LANES)
        return carry

    raw_fetch.wait()
    lax.fori_loop(0, raw // BLOCK, raw_step, 0)
    store_near(lines, lines + raw, 0)
    for n, (first, last) in enumerate(parts):
        for fetch in fetches[n]:
            fetch.wait()
        lax.fori_loop(first // BLOCK, last // BLOCK, functools.partial(slab_step, n > 0), 0)
        store_near(first, last, 1 + n)
        if n:
            store_far(first, last, n - 1)
    for copy in stores:
        copy.wait()


def update_pieces(numbers, grams, near, far, across, raw_fields, raw_grads, grads, groups, raw, lines):
    half = len(far)
    total = 2 * half
    wide = total * TILE
    out_shape = [pltpu.HBM((half, lines + raw, LANES), BF16)]
    out_shape += [pltpu.HBM((lines - raw, LANES), BF16)] * half
    return call(
        functools.partial(update_pieces_body, half, raw, lines, groups),
        "update_pieces",
        flops=4 * wide * wide * LANES * (lines // TILE),
        moved=6 * total * lines * LANES,
        in_specs=[IN_VMEM] * (half + 6) + [IN_HBM] * (1 + len(groups)),
        out_specs=[IN_HBM] * len(out_shape),
        out_shape=out_shape,
        scratch_shapes=[
            pltpu.VMEM((half, lines + raw, LANES), BF16),
            pltpu.VMEM((half, lines - raw, LANES), BF16),
            pltpu.VMEM((wide, wide), BF16),
            pltpu.VMEM((wide, LANES), F32),
            pltpu.VMEM((total, lines, LANES), BF16),
            pltpu.VMEM((total, raw, LANES), BF16),
            pltpu.SemaphoreType.DMA((len(groups) + 1, 4)),
            pltpu.SemaphoreType.DMA((half + 1, 5)),
        ],
    )(near, *far, across, *raw_fields, numbers, grams, raw_grads, *grads)


def exchange(piece, k, slabs):
    return lax.ppermute(piece, "slab", [(i, i ^ k) for i in range(slabs)])


def swap_near(pieces, slabs):
    groups = [list(range(slabs // 2)), list(range(slabs // 2, slabs))]
    return lax.all_to_all(pieces, "slab", 0, 0, axis_index_groups=groups, tiled=True)


RAW = 192
GRADIENTS = ((8, 9, 10, 11), (12, 13, 14, 15), (0, 1, 2, 3, 4, 5, 6, 7))


def by_halves(particles, observed, precision, spread, anneal, step_size):
    slabs = lax.axis_size("slab")
    half = slabs // 2
    lines = NCELL // slabs // LANES
    row = in_hbm(particles)
    fields = [in_hbm(field.reshape(-1, LANES)) for field in (observed, precision)]
    near, *far = split_pieces(row, slabs, RAW, fields)
    far, (obs, prec, *raw_fields) = far[:half], far[half:]
    near = swap_near(near, slabs)
    far = [exchange(piece, half + x, slabs) for x, piece in enumerate(far)]
    raw_near = raw_states(near, RAW, lines, far)
    across = exchange(raw_near, half, slabs)
    grads = []
    numbers = [spread, anneal, step_size]
    for group in GRADIENTS:
        if group[0] < half:
            arrays, views = [near], [(0, k, 0) for k in group]
        else:
            arrays, views = [far[k - half] for k in group], [(j, None, 0) for j in range(len(group))]
        slopes, rows = gradient_pieces(arrays, tuple(views), obs, prec, [] if grads else numbers)
        grads.append(in_hbm(slopes))
        numbers = numbers if len(grads) > 1 else rows
    grams = swap(gram_pieces(near, far, lines, grads[:1], [raw_near]))
    views = tuple((0, k, lines + TILE) for k in range(half))
    raw_grads = in_hbm(gradient_pieces([near], views, *raw_fields, [])[0])
    new_near, *new_far = update_pieces(
        numbers, grams, near, far, across, raw_fields, raw_grads, grads, GRADIENTS, RAW, lines
    )
    new_near = swap_near(new_near, slabs)
    new_far = [exchange(piece, half + x, slabs) for x, piece in enumerate(new_far)]
    row = join_pieces(None, slabs, RAW, [new_near], [(0, k, k) for k in range(half)])
    for group in ((0, 1, 2, 3), (4, 5)):
        pieces = [(n, None, half + x) for n, x in enumerate(group)]
        row = join_pieces(row, slabs, RAW, [new_far[x] for x in group], pieces)
    return join_pieces(row, slabs, RAW, new_far[6:], [(n, None, half + 6 + n) for n in range(half - 6)])


def on_device(particles, observed, precision, spread, anneal, step_size):
    slabs = lax.axis_size("slab")
    total = particles.shape[0] * slabs
    lines = NCELL // slabs // LANES
    if slabs == 16:
        return by_halves(particles, observed, precision, spread, anneal, step_size)
    sent, begun = cuts(lines)
    fields = [observed.reshape(-1, LANES), precision.reshape(-1, LANES)]
    numbers = [spread, anneal, step_size]
    first, obs, prec, scalars = split_row(particles, slabs, 0, sent, True, fields, numbers, [])
    parts = [swap(first)]
    if sent < lines:
        parts += [swap(split_row(particles, slabs, sent, lines, False, [], [], [scalars])[0])]
    if total * TILE > 256:
        grads = slab_gradient(parts, obs, prec, lines, 0, lines)
        states = jnp.concatenate([parts[0][:, :sent]] + parts[1:], axis=1)
        new = plain_update(spread, anneal, step_size, states, grads)
        return join_row(swap(new), lines, 0, None)
    if sent == lines:
        grads = slab_gradient(parts, obs, prec, lines, 0, lines)
        grams = swap(slab_gram(parts[0], lines, slabs, [], []))
        new = slab_update(scalars, grams, parts, grads, 0, lines, [])
        return join_row(swap(new), lines, 0, None)
    gram = slab_gram(parts[0], sent, 1, [], [])
    early = slab_gradient(parts[:1], obs, prec, lines, 0, begun)
    grams = swap(slab_gram(parts[1], lines - sent, slabs, [gram], [early]))
    late = slab_gradient(parts, obs, prec, lines, begun, lines)
    new = slab_update(scalars, grams, parts[:1], early, 0, begun, [])
    rest = slab_update(scalars, grams, parts, late, begun, lines, [new])
    row = join_row(swap(new), lines, 0, None)
    return join_row(swap(rest), lines, begun, row)


def solution(mesh):
    in_specs = (
        P(("groups", "slab"), None),
        P("groups"),
        P("groups"),
        P("groups"),
        P("groups"),
        P("groups"),
    )
    out_specs = P(("groups", "slab"), None)
    return jax.shard_map(
        on_device, mesh=mesh, in_specs=in_specs, out_specs=out_specs, check_vma=False
    )
```

```python
import functools

import jax
import jax.numpy as jnp
from jax import lax
from jax.experimental import pallas as pl
from jax.experimental.pallas import tpu as pltpu
from jax.sharding import PartitionSpec as P

GRID_X = 1024
GRID_Y = 1024
NCELL = 1048576
LANES = 128
LINE = GRID_Y // LANES
TILE = 16

prior_scale = 0.25
mass_term = 1.0

F32 = jnp.float32
BF16 = jnp.bfloat16
MIB = 1024 * 1024


def call(body, name, flops=0, moved=0, limit=16, **kwargs):
    return pl.pallas_call(
        body,
        name=name,
        compiler_params=pltpu.CompilerParams(vmem_limit_bytes=limit * MIB),
        cost_estimate=pl.CostEstimate(flops=flops, bytes_accessed=moved, transcendentals=0),
        **kwargs,
    )


IN_VMEM = pl.BlockSpec(memory_space=pltpu.VMEM)
IN_HBM = pl.BlockSpec(memory_space=pltpu.HBM)


def in_hbm(array):
    return pltpu.with_memory_space_constraint(array, pltpu.HBM)


BLOCK = 4 * TILE


def cuts(lines):
    if lines % (8 * BLOCK):
        return lines, lines
    return lines * 3 // 4, lines * 3 // 4 - BLOCK


def split_body(lines, begin, rim, fields, numbers, row_ref, *refs):
    field_refs, number_refs = refs[:fields], refs[fields : fields + numbers]
    out_ref, *slab_refs, rows_ref = refs[-7 - fields : -5]
    held, edges, sems, edge_sems, field_sems = refs[-5:]
    for k, number_ref in enumerate(number_refs):
        rows_ref[k : k + 1, :] = jnp.broadcast_to(number_ref[...].reshape(1, 1), (1, LANES))
    slabs, count, _ = out_ref.shape
    count -= TILE * rim
    size = count * LANES
    cells = lines * LANES

    def part(slab):
        source = row_ref.at[:, pl.ds(slab * cells + begin * LANES, size)]
        return pltpu.make_async_copy(source, held.at[:, pl.ds(slab * size, size)], sems.at[slab])

    def edge(slab):
        source = row_ref.at[:, pl.ds(slab * cells - GRID_Y, GRID_Y)]
        return pltpu.make_async_copy(source, edges.at[:, pl.ds(slab * GRID_Y, GRID_Y)], edge_sems.at[slab])

    def grid_row(ref, start):
        return ref[:, pl.ds(start, GRID_Y)].astype(F32).reshape(LINE, LANES)

    for slab in range(slabs):
        part(slab).start()
        if rim and slab:
            edge(slab).start()
    mine = pl.ds(pl.multiple_of(lax.axis_index("slab") * lines, TILE), lines)
    fetches = [
        pltpu.make_async_copy(source.at[mine, :], target, field_sems.at[k])
        for k, (source, target) in enumerate(zip(field_refs, slab_refs))
    ]
    for fetch in fetches:
        fetch.start()
    part(0).wait()
    outside = jnp.zeros((LINE, LANES), F32)
    for slab in range(slabs):
        if slab + 1 < slabs:
            part(slab + 1).wait()
        out_ref[slab, :count, :] = held[:, pl.ds(slab * size, size)].reshape(count, LANES)
        if rim:
            if slab:
                edge(slab).wait()
            below = grid_row(held, (slab + 1) * size) if slab + 1 < slabs else outside
            above = grid_row(edges, slab * GRID_Y) if slab else outside
            out_ref[slab, count:, :] = jnp.concatenate([below, above], axis=0).astype(BF16)
    for fetch in fetches:
        fetch.wait()


def split_row(row, slabs, begin, end, rim, fields, numbers, earlier):
    lines = row.shape[1] // slabs // LANES
    count = end - begin
    return call(
        functools.partial(split_body, lines, begin, rim, len(fields), len(numbers)),
        "split_row",
        moved=6 * slabs * count * LANES,
        in_specs=[IN_HBM] * (1 + len(fields)) + [IN_VMEM] * len(numbers) + [IN_HBM] * len(earlier),
        out_specs=[IN_VMEM] * (2 + len(fields)),
        out_shape=[jax.ShapeDtypeStruct((slabs, count + TILE * rim, LANES), BF16)]
        + [jax.ShapeDtypeStruct((lines, LANES), BF16)] * len(fields)
        + [jax.ShapeDtypeStruct((8, LANES), F32)],
        scratch_shapes=[
            pltpu.VMEM((1, slabs * count * LANES), BF16),
            pltpu.VMEM((1, slabs * GRID_Y), BF16),
            pltpu.SemaphoreType.DMA((slabs,)),
            pltpu.SemaphoreType.DMA((slabs,)),
            pltpu.SemaphoreType.DMA((2,)),
        ],
    )(row, *fields, *numbers, *earlier)


def join_body(lines, begin, slabs_ref, *refs):
    row_ref, held, sems = refs[-3:]
    slabs, count, _ = slabs_ref.shape
    size = count * LANES
    copies = []
    for slab in range(slabs):
        at = pl.ds(slab * size, size)
        held[:, at] = slabs_ref[slab].reshape(1, size)
        target = row_ref.at[:, pl.ds((slab * lines + begin) * LANES, size)]
        copies.append(pltpu.make_async_copy(held.at[:, at], target, sems.at[slab]))
        copies[-1].start()
    for copy in copies:
        copy.wait()


def join_row(slabs, lines, begin, row):
    total, count, _ = slabs.shape
    begun = [] if row is None else [row]
    return call(
        functools.partial(join_body, lines, begin),
        "join_row",
        moved=6 * slabs.size,
        in_specs=[IN_VMEM] + [IN_HBM] * len(begun),
        out_specs=IN_HBM,
        out_shape=jax.ShapeDtypeStruct((1, total * lines * LANES), BF16),
        input_output_aliases={1: 0} if begun else {},
        scratch_shapes=[pltpu.VMEM((1, slabs.size), BF16), pltpu.SemaphoreType.DMA((total,))],
    )(slabs, *begun)


def same_line(total):
    wide = total * TILE
    row = lax.broadcasted_iota(jnp.int32, (wide, wide), 0)
    col = lax.broadcasted_iota(jnp.int32, (wide, wide), 1)
    return (row ^ col) & (TILE - 1) == 0


def members(total, dtype):
    wide = total * TILE
    row = lax.broadcasted_iota(jnp.int32, (wide, total), 0)
    col = lax.broadcasted_iota(jnp.int32, (wide, total), 1)
    return (row // TILE == col).astype(dtype)


def gram_body(steps, tiles, parts, states_ref, *refs):
    out_ref, pairs = refs[-2:]
    total = states_ref.shape[0]
    wide = total * TILE
    pairs[...] = jnp.zeros_like(pairs)

    def step(i, carry):
        parts = [
            states_ref[:, pl.ds(pl.multiple_of((i * tiles + t) * TILE, TILE), TILE), :].reshape(wide, LANES)
            for t in range(tiles)
        ]
        block = jnp.concatenate(parts, axis=1)
        pairs[...] += lax.dot_general(block, block, (((1,), (1,)), ((), ())), preferred_element_type=F32)
        return carry

    lax.fori_loop(0, steps, step, 0)
    equal = jnp.where(same_line(total), pairs[...], 0.0)
    rows = jnp.sum(equal.reshape(total, TILE, wide), axis=1)
    gram = jnp.dot(rows, members(total, F32), precision=lax.Precision.HIGHEST, preferred_element_type=F32)
    gram = jnp.concatenate([gram, jnp.zeros((total, LANES - total), F32)], axis=1)
    for part_ref in refs[:parts]:
        gram += part_ref[0]
    out_ref[...] = jnp.broadcast_to(gram[None], out_ref.shape)


def slab_gram(states, lines, copies, parts, earlier):
    total = states.shape[0]
    wide = total * TILE
    tiles = min(8, lines // TILE)
    return call(
        functools.partial(gram_body, lines // TILE // tiles, tiles, len(parts)),
        "slab_gram",
        flops=2 * wide * wide * LANES * (lines // TILE),
        moved=2 * states.size,
        in_specs=[IN_VMEM] * (1 + len(parts)) + [IN_HBM] * len(earlier),
        out_specs=IN_VMEM,
        out_shape=jax.ShapeDtypeStruct((copies, total, LANES), F32),
        scratch_shapes=[pltpu.VMEM((wide, wide), F32)],
    )(states, *parts, *earlier)


def gradient_body(lines, begin, end, parts, *refs):
    observed, precision, out_ref, grads, sems = refs[parts:]
    total = grads.shape[0]
    first = refs[0].shape[1] - TILE
    rows = BLOCK // LINE
    group = 4
    shape = (rows, LINE, LANES)
    lane = lax.broadcasted_iota(jnp.int32, (1, LINE, LANES), 2)
    line = lax.broadcasted_iota(jnp.int32, (1, LINE, LANES), 1)

    def load(particle, at, count):
        ref, at = (refs[0], at) if at < first else (refs[1], at - first)
        return ref[particle, at : at + count, :].astype(F32)

    def rim(particle):
        return refs[0][particle, first:, :].astype(F32)

    stores = []
    for k, at in enumerate(range(begin, end, BLOCK)):
        mine = slice(at - begin, at - begin + BLOCK)
        obs = observed[at : at + BLOCK, :].astype(F32).reshape(shape)
        prec = precision[at : at + BLOCK, :].astype(F32).reshape(shape)

        def step(i, carry):
            for p in range(group):
                particle = i * group + p
                here = load(particle, at, BLOCK)
                before = load(particle, at - TILE, TILE) if at else rim(particle)
                after = load(particle, at + BLOCK, TILE) if at + BLOCK < lines else rim(particle)
                above = jnp.concatenate([before[LINE:], here[:-LINE]], axis=0).reshape(shape)
                below = jnp.concatenate([here[LINE:], after[:LINE]], axis=0).reshape(shape)
                field = here.reshape(shape)
                turned = pltpu.roll(field, 1, 2)
                carried = jnp.where(line == 0, 0.0, pltpu.roll(turned, 1, 1))
                left = jnp.where(lane == 0, carried, turned)
                turned = pltpu.roll(field, LANES - 1, 2)
                carried = jnp.where(line == LINE - 1, 0.0, pltpu.roll(turned, LINE - 1, 1))
                right = jnp.where(lane == LANES - 1, carried, turned)
                laplace = (4.0 + mass_term) * field - (below + above + right + left)
                squash = jnp.tanh(field)
                result = prec * (obs - squash) * (1.0 - squash * squash) - prior_scale * laplace
                grads[particle, mine, :] = result.reshape(BLOCK, LANES).astype(BF16)
            return carry

        lax.fori_loop(0, total // group, step, 0)
        stores.append(pltpu.make_async_copy(grads.at[:, mine, :], out_ref.at[:, mine, :], sems.at[k]))
        stores[-1].start()
    for store in stores:
        store.wait()


def slab_gradient(parts, observed, precision, lines, begin, end):
    total = parts[0].shape[0]
    count = end - begin
    out = jax.ShapeDtypeStruct((total, count, LANES), BF16)
    return call(
        functools.partial(gradient_body, lines, begin, end, len(parts)),
        "slab_gradient",
        flops=30 * out.size,
        moved=8 * out.size,
        in_specs=[IN_VMEM] * (len(parts) + 2),
        out_specs=IN_HBM,
        out_shape=out,
        scratch_shapes=[pltpu.VMEM(out.shape, BF16), pltpu.SemaphoreType.DMA((count // BLOCK,))],
    )(*parts, observed, precision)


def update_body(begin, end, parts, *refs):
    states_refs, refs = refs[:parts], refs[parts:]
    scalars_ref, grams_ref, grads_ref = refs[:3]
    out_ref, grads, mixer, own, sem = refs[-5:]
    total = out_ref.shape[0]
    wide = total * TILE
    fetch = pltpu.make_async_copy(grads_ref, grads, sem)
    fetch.start()
    gram = jnp.sum(grams_ref[...], axis=0)[:, :total]
    row = lax.broadcasted_iota(jnp.int32, (total, total), 0)
    col = lax.broadcasted_iota(jnp.int32, (total, total), 1)
    diagonal = jnp.where(row == col, gram, 0.0)
    down = jnp.sum(diagonal, axis=1, keepdims=True)
    across = jnp.sum(diagonal, axis=0, keepdims=True)
    member = members(total, BF16)
    spread, anneal, step_size = (scalars_ref[k : k + 1, :1] for k in range(3))
    rate = step_size / total
    coeff = 2.0 * anneal / spread
    kernel = jnp.exp(-(down + across - 2.0 * gram) / (spread * NCELL)).astype(BF16)
    ksum = jnp.sum(kernel.astype(F32), axis=1, keepdims=True)
    half = jnp.dot(member, kernel, preferred_element_type=F32).astype(BF16)
    full = lax.dot_general(half, member, (((1,), (1,)), ((), ())), preferred_element_type=F32)
    mixer[...] = jnp.where(same_line(total), full, 0.0).astype(BF16)
    gain = 1.0 + rate * coeff * ksum
    own[...] = jnp.broadcast_to(gain[:, :, None], (total, TILE, LANES)).reshape(wide, LANES)
    fetch.wait()

    done = 0
    for part, states_ref in enumerate(states_refs):
        have = states_ref.shape[1] - (0 if part else TILE)
        low = max(begin - done, 0)
        high = min(end - done, have)
        into = done - begin
        done += have

        def step(i, carry):
            for t in range(BLOCK // TILE):
                at = pl.multiple_of(i * BLOCK + t * TILE, TILE)
                there = pl.ds(pl.multiple_of(at + into, TILE), TILE)
                states = states_ref[:, pl.ds(at, TILE), :].reshape(wide, LANES)
                both = jnp.concatenate([grads[:, there, :].reshape(wide, LANES), states], axis=1)
                mixed = jnp.dot(mixer[...], both, preferred_element_type=F32)
                drive, pulled = mixed[:, :LANES], mixed[:, LANES:]
                new = states.astype(F32) * own[...] + rate * (drive - coeff * pulled)
                out_ref[:, there, :] = new.astype(BF16).reshape(total, TILE, LANES)
            return carry

        lax.fori_loop(low // BLOCK, high // BLOCK, step, 0)


def slab_update(scalars, grams, parts, grads, begin, end, earlier):
    total, count, _ = grads.shape
    wide = total * TILE
    return call(
        functools.partial(update_body, begin, end, len(parts)),
        "slab_update",
        flops=4 * wide * wide * LANES * (count // TILE),
        moved=6 * grads.size,
        in_specs=[IN_VMEM] * len(parts)
        + [IN_VMEM, IN_VMEM, IN_HBM]
        + [IN_HBM] * len(earlier),
        out_specs=IN_VMEM,
        out_shape=jax.ShapeDtypeStruct(grads.shape, BF16),
        scratch_shapes=[
            pltpu.VMEM(grads.shape, BF16),
            pltpu.VMEM((wide, wide), BF16),
            pltpu.VMEM((wide, LANES), F32),
            pltpu.SemaphoreType.DMA,
        ],
    )(*parts, scalars, grams, grads, *earlier)


def plain_update(spread, anneal, step_size, states, grads):
    total, lines, _ = grads.shape
    flat = states[:, :lines].reshape(total, -1)
    gram = lax.dot_general(flat, flat, (((1,), (1,)), ((), ())), preferred_element_type=F32)
    gram = lax.psum(gram, "slab")
    norms = jnp.diagonal(gram)
    kernel = jnp.exp(-(norms[:, None] + norms[None, :] - 2.0 * gram) / (spread[0] * NCELL)).astype(BF16)
    ksum = jnp.sum(kernel.astype(F32), axis=1)
    drive = jnp.dot(kernel, grads.reshape(total, -1), preferred_element_type=F32)
    pulled = jnp.dot(kernel, flat, preferred_element_type=F32)
    values = flat.astype(F32)
    repel = values * ksum[:, None] - pulled
    coeff = 2.0 * anneal[0] / spread[0]
    new = values + step_size[0] / total * (drive + coeff * repel)
    return new.astype(BF16).reshape(grads.shape)


def swap(slabs):
    return lax.all_to_all(slabs, "slab", split_axis=0, concat_axis=0, tiled=True)


def device_at(at, half):
    me = lax.axis_index("slab").astype(jnp.int32)
    return jnp.where(at < half, me - me % half + at, me ^ at)


def lines_of(start, count):
    return pl.ds(pl.multiple_of(start, TILE), count)


def split_pieces_body(slabs, raw, lines, fields, row_ref, *refs):
    half = slabs // 2
    field_refs, near_out, far_outs = refs[:fields], refs[fields], refs[fields + 1 : fields + 1 + half]
    slab_refs, held, sems = refs[fields + 1 + half : -2], refs[-2], refs[-1]
    cells = lines * LANES
    end = row_ref.shape[1]
    me = lax.axis_index("slab").astype(jnp.int32)

    def part(start, size):
        return pl.ds(pl.multiple_of(start, GRID_Y), size)

    def grid_row(start):
        return held[:, part(start, GRID_Y)].astype(F32).reshape(LINE, LANES)

    copies = []
    for at in range(slabs):
        cut = part(device_at(at, half) * cells, cells)
        copies.append(pltpu.make_async_copy(row_ref.at[:, cut], held.at[:, cut], sems.at[at]))
    for n, target in enumerate(slab_refs):
        start = (me if n < fields else me ^ half) * lines
        source = field_refs[n % fields].at[lines_of(start, target.shape[0]), :]
        copies.append(pltpu.make_async_copy(source, target, sems.at[slabs + n]))
    for copy in copies:
        copy.start()
    outs = [near_out.at[at] for at in range(half)] + list(far_outs)
    for at, out_ref in enumerate(outs):
        copies[at].wait()
        out_ref[:lines, :] = held[:, part(device_at(at, half) * cells, cells)].reshape(lines, LANES)
    for at, out_ref in enumerate(outs):
        slab = device_at(at, half)
        start = slab * cells
        below = jnp.where(slab == slabs - 1, 0.0, grid_row(jnp.minimum(start + cells, end - GRID_Y)))
        above = jnp.where(slab == 0, 0.0, grid_row(jnp.maximum(start - GRID_Y, 0)))
        out_ref[lines : lines + TILE, :] = jnp.concatenate([below, above], axis=0).astype(BF16)
        if at < half:
            start = (slab ^ half) * cells
            to = lines + TILE
            out_ref[to : to + raw, :] = held[:, part(start, raw * LANES)].reshape(raw, LANES)
            below = grid_row(start + raw * LANES)
            above = jnp.where(slab ^ half == 0, 0.0, grid_row(jnp.maximum(start - GRID_Y, 0)))
            out_ref[to + raw :, :] = jnp.concatenate([below, above], axis=0).astype(BF16)
    for copy in copies[slabs:]:
        copy.wait()


def split_pieces(row, slabs, raw, fields):
    lines = row.shape[1] // slabs // LANES
    half = slabs // 2
    rim = lines + TILE
    size = rim + raw + TILE
    out_shape = [jax.ShapeDtypeStruct((half, size, LANES), BF16)]
    out_shape += [jax.ShapeDtypeStruct((rim, LANES), BF16)] * half
    out_shape += [jax.ShapeDtypeStruct((lines, LANES), BF16)] * len(fields)
    out_shape += [jax.ShapeDtypeStruct((raw, LANES), BF16)] * len(fields)
    return call(
        functools.partial(split_pieces_body, slabs, raw, lines, len(fields)),
        "split_pieces",
        moved=6 * half * (rim + size) * LANES,
        in_specs=[IN_HBM] * (1 + len(fields)),
        out_specs=[IN_VMEM] * len(out_shape),
        out_shape=out_shape,
        scratch_shapes=[pltpu.VMEM(row.shape, BF16), pltpu.SemaphoreType.DMA((slabs + 2 * len(fields),))],
    )(row, *fields)


def join_pieces_body(pieces, half, raw, lines, begun, arrays, *refs):
    row_ref, helds, sems = refs[begun + arrays], refs[begun + arrays + 1 : -1], refs[-1]
    cells = lines * LANES
    skip = raw * LANES
    copies = []
    for (array, lead, at), held in zip(pieces, helds):
        ref = refs[begun + array]
        piece = ref[...] if lead is None else ref[lead]
        held[...] = piece.reshape(held.shape)
        slab = device_at(at, half)
        if at < half:
            parts = [(0, cells, slab * cells), (cells, skip, (slab ^ half) * cells)]
        else:
            parts = [(0, cells - skip, slab * cells + skip)]
        for begin, size, start in parts:
            target = row_ref.at[:, pl.ds(pl.multiple_of(start, GRID_Y), size)]
            copies.append(pltpu.make_async_copy(held.at[:, pl.ds(begin, size)], target, sems.at[len(copies)]))
            copies[-1].start()
    for copy in copies:
        copy.wait()


def join_pieces(row, slabs, raw, arrays, pieces):
    sizes = [arrays[piece[0]].shape[-2] * LANES for piece in pieces]
    begun = [] if row is None else [row]
    return call(
        functools.partial(
            join_pieces_body, pieces, slabs // 2, raw, NCELL // slabs // LANES, len(begun), len(arrays)
        ),
        "join_pieces",
        moved=6 * sum(sizes),
        in_specs=[IN_HBM] * len(begun) + [IN_VMEM] * len(arrays),
        out_specs=IN_HBM,
        out_shape=jax.ShapeDtypeStruct((1, NCELL), BF16),
        input_output_aliases={0: 0} if begun else {},
        scratch_shapes=[pltpu.VMEM((1, size), BF16) for size in sizes]
        + [pltpu.SemaphoreType.DMA((2 * len(sizes),))],
    )(*begun, *arrays)


def owners(total, dtype):
    wide = total * TILE
    row = lax.broadcasted_iota(jnp.int32, (wide, total), 0)
    col = lax.broadcasted_iota(jnp.int32, (wide, total), 1)
    return (device_at(row // TILE, total // 2) == col).astype(dtype)


def gram_pieces_body(lines, total, near_ref, *refs):
    half = total // 2
    pieces, out_ref, pairs = refs[:half], refs[-2], refs[-1]
    wide = total * TILE
    tiles = 8
    pairs[...] = jnp.zeros_like(pairs)

    def step(i, carry):
        parts = []
        for t in range(tiles):
            at = lines_of((i * tiles + t) * TILE, TILE)
            near = near_ref[:, at, :].reshape(wide // 2, LANES)
            parts.append(jnp.concatenate([near] + [piece[at, :] for piece in pieces], axis=0))
        block = jnp.concatenate(parts, axis=1)
        pairs[...] += lax.dot_general(block, block, (((1,), (1,)), ((), ())), preferred_element_type=F32)
        return carry

    lax.fori_loop(0, lines // TILE // tiles, step, 0)
    equal = jnp.where(same_line(total), pairs[...], 0.0)
    exact = {"precision": lax.Precision.HIGHEST, "preferred_element_type": F32}
    rows = jnp.sum(equal.reshape(total, TILE, wide), axis=1)
    gram = jnp.dot(rows, owners(total, F32), **exact)
    row = lax.broadcasted_iota(jnp.int32, (total, total), 0)
    col = lax.broadcasted_iota(jnp.int32, (total, total), 1)
    gram = jnp.dot((row == device_at(col, half)).astype(F32), gram, **exact)
    filler = jnp.zeros((half, LANES - 2 * total), F32)
    gram = jnp.concatenate([gram[:half], gram[half:], filler], axis=1)
    out_ref[...] = jnp.broadcast_to(gram[None], out_ref.shape)


def gram_pieces(near, far, lines, gates, early):
    total = 2 * len(far)
    wide = total * TILE
    return call(
        functools.partial(gram_pieces_body, lines, total),
        "gram_pieces",
        flops=2 * wide * wide * LANES * (lines // TILE),
        moved=2 * total * lines * LANES,
        in_specs=[IN_VMEM] * (1 + len(far)) + [IN_HBM] * len(gates) + [IN_VMEM] * len(early),
        out_specs=IN_VMEM,
        out_shape=jax.ShapeDtypeStruct((total, total // 2, LANES), F32),
        scratch_shapes=[pltpu.VMEM((wide, wide), F32)],
    )(near, *far, *gates, *early)


def block_gradient(load, i, count, observed, precision):
    start = i * BLOCK
    at = lines_of(start, BLOCK)
    shape = (BLOCK // LINE, LINE, LANES)
    lane = lax.broadcasted_iota(jnp.int32, (1, LINE, LANES), 2)
    line = lax.broadcasted_iota(jnp.int32, (1, LINE, LANES), 1)
    obs = observed[at, :].astype(F32).reshape(shape)
    prec = precision[at, :].astype(F32).reshape(shape)
    here = load(start, BLOCK).astype(F32)
    before = load(jnp.where(i == 0, count, start - TILE), TILE).astype(F32)
    after = load(start + BLOCK, TILE).astype(F32)
    above = jnp.concatenate([before[LINE:], here[:-LINE]], axis=0).reshape(shape)
    below = jnp.concatenate([here[LINE:], after[:LINE]], axis=0).reshape(shape)
    field = here.reshape(shape)
    turned = pltpu.roll(field, 1, 2)
    carried = jnp.where(line == 0, 0.0, pltpu.roll(turned, 1, 1))
    left = jnp.where(lane == 0, carried, turned)
    turned = pltpu.roll(field, LANES - 1, 2)
    carried = jnp.where(line == LINE - 1, 0.0, pltpu.roll(turned, LINE - 1, 1))
    right = jnp.where(lane == LANES - 1, carried, turned)
    laplace = (4.0 + mass_term) * field - (below + above + right + left)
    squash = jnp.tanh(field)
    result = prec * (obs - squash) * (1.0 - squash * squash) - prior_scale * laplace
    return result.reshape(BLOCK, LANES).astype(BF16)


def gradient_pieces_body(views, arrays, numbers, *refs):
    observed, precision, *number_refs = refs[arrays : arrays + 2 + numbers]
    out_ref, rows_ref, grads, sems = refs[-4:]
    for n, number_ref in enumerate(number_refs):
        rows_ref[n : n + 1, :] = jnp.full((1, LANES), number_ref[0], F32)
    count = observed.shape[0]
    steps = count // BLOCK

    def store(i):
        at = lines_of(i * BLOCK, BLOCK)
        return pltpu.make_async_copy(grads.at[:, at, :], out_ref.at[:, at, :], sems.at[i])

    def step(i, carry):
        for p, (array, lead, base) in enumerate(views):

            def load(start, size):
                part = lines_of(base + start, size)
                return refs[array][part, :] if lead is None else refs[array][lead, part, :]

            grads[p, lines_of(i * BLOCK, BLOCK), :] = block_gradient(load, i, count, observed, precision)
        store(i).start()
        return carry

    def finish(i, carry):
        store(i).wait()
        return carry

    lax.fori_loop(0, steps, step, 0)
    lax.fori_loop(0, steps, finish, 0)


def gradient_pieces(arrays, views, observed, precision, numbers):
    count = observed.shape[0]
    out = pltpu.HBM((len(views), count, LANES), BF16)
    size = len(views) * count * LANES
    return call(
        functools.partial(gradient_pieces_body, views, len(arrays), len(numbers)),
        "gradient_pieces",
        flops=30 * size,
        moved=8 * size,
        in_specs=[IN_VMEM] * (len(arrays) + 2)
        + [pl.BlockSpec(memory_space=pltpu.SMEM)] * len(numbers),
        out_specs=[IN_HBM, IN_VMEM],
        out_shape=[out, jax.ShapeDtypeStruct((8, LANES), F32)],
        scratch_shapes=[pltpu.VMEM(out.shape, BF16), pltpu.SemaphoreType.DMA((count // BLOCK,))],
    )(*arrays, observed, precision, *numbers)


def raw_body(raw, lines, near_ref, *refs):
    out_ref = refs[-1]
    for k in range(near_ref.shape[0]):
        out_ref[k, :raw, :] = near_ref[k, :raw, :]
        below = near_ref[k, raw : raw + TILE, :].astype(F32)[:LINE]
        above = near_ref[k, lines : lines + TILE, :].astype(F32)[LINE:]
        out_ref[k, raw:, :] = jnp.concatenate([below, above], axis=0).astype(BF16)


def raw_states(near, raw, lines, gates):
    out = jax.ShapeDtypeStruct((near.shape[0], raw + TILE, LANES), BF16)
    return call(
        functools.partial(raw_body, raw, lines),
        "raw_states",
        moved=4 * out.size,
        in_specs=[IN_VMEM] * (1 + len(gates)),
        out_specs=IN_VMEM,
        out_shape=out,
    )(near, *gates)


def mix(mixer, own, numbers_ref, total, states, slopes):
    high = mixer.shape[0]
    rate = numbers_ref[2:3, :1] / total
    coeff = 2.0 * numbers_ref[1:2, :1] / numbers_ref[:1, :1]
    both = jnp.concatenate([slopes, states], axis=1)
    mixed = jnp.dot(mixer[...], both, preferred_element_type=F32)
    drive, pulled = mixed[:, :LANES], mixed[:, LANES:]
    return (states[:high].astype(F32) * own[...] + rate * (drive - coeff * pulled)).astype(BF16)


def update_pieces_body(half, raw, lines, groups, near_ref, *refs):
    total = 2 * half
    far_refs, refs = refs[:half], refs[half:]
    across_ref, raw_observed, raw_precision, numbers_ref, grams_ref, raw_grads_ref, *refs = refs
    group_refs, near_to, far_tos = refs[: len(groups)], refs[len(groups)], refs[len(groups) + 1 : -8]
    near_out, far_out, mixer, own, grads, raw_grads, sems, out_sems = refs[-8:]
    wide = total * TILE
    high = half * TILE
    raw_fetch = pltpu.make_async_copy(raw_grads_ref, raw_grads.at[pl.ds(0, half), :, :], sems.at[len(groups), 0])
    raw_fetch.start()
    middle = (raw + 2 * lines) // 3 // BLOCK * BLOCK
    parts = ((0, raw), (raw, middle), (middle, lines - BLOCK), (lines - BLOCK, lines))
    fetches = []
    for n, (first, last) in enumerate(parts):
        part = pl.ds(first, last - first)
        fetches.append([])
        for g, (group, group_ref) in enumerate(zip(groups, group_refs)):
            target = grads.at[pl.ds(group[0], len(group)), part, :]
            fetches[n].append(pltpu.make_async_copy(group_ref.at[:, part, :], target, sems.at[g, n]))
            fetches[n][-1].start()

    def raw_gradient(i, carry):
        for k in range(half):

            def load(start, size):
                return across_ref[k, lines_of(start, size), :]

            part = lines_of(i * BLOCK, BLOCK)
            raw_grads[half + k, part, :] = block_gradient(load, i, raw, raw_observed, raw_precision)
        return carry

    lax.fori_loop(0, raw // BLOCK, raw_gradient, 0)
    gram = jnp.sum(grams_ref[...], axis=0)
    gram = jnp.concatenate([gram[:, :total], gram[:, total : 2 * total]], axis=0)
    spread, anneal, step_size = (numbers_ref[k : k + 1, :1] for k in range(3))
    rate = step_size / total
    coeff = 2.0 * anneal / spread
    row = lax.broadcasted_iota(jnp.int32, (total, total), 0)
    col = lax.broadcasted_iota(jnp.int32, (total, total), 1)
    diagonal = jnp.where(row == col, gram, 0.0)
    down = jnp.sum(diagonal, axis=1, keepdims=True)
    across = jnp.sum(diagonal, axis=0, keepdims=True)
    kernel = jnp.exp(-(down + across - 2.0 * gram) / (spread * NCELL)).astype(BF16)
    owner = owners(total, BF16)
    half_way = jnp.dot(owner, kernel, preferred_element_type=F32).astype(BF16)
    full = lax.dot_general(half_way, owner, (((1,), (1,)), ((), ())), preferred_element_type=F32)
    full = jnp.where(same_line(total), full, 0.0)
    mixer[...] = full.astype(BF16)
    ksum = jnp.sum(full, axis=1, keepdims=True)
    own[...] = jnp.broadcast_to(1.0 + rate * coeff * ksum, (wide, LANES))

    stores = []

    def store(source, target, at):
        stores.append(pltpu.make_async_copy(source, target, out_sems.at[at]))
        stores[-1].start()

    def store_near(first, last, at):
        part = pl.ds(first, last - first)
        store(near_out.at[:, part, :], near_to.at[:, part, :], (half, at))

    def store_far(first, last, at):
        part = pl.ds(first - raw, last - first)
        for x, far_to in enumerate(far_tos):
            store(far_out.at[x, part, :], far_to.at[part, :], (x, at))

    def slab_step(with_far, i, carry):
        rows = wide if with_far else high
        for t in range(BLOCK // TILE):
            at = i * BLOCK + t * TILE
            part = lines_of(at, TILE)
            states = [near_ref[:, part, :].reshape(high, LANES)] + [ref[part, :] for ref in far_refs]
            slopes = grads[:, part, :].reshape(wide, LANES)
            states = jnp.concatenate(states, axis=0)
            new = mix(mixer.at[:rows, :], own.at[:rows, :], numbers_ref, total, states, slopes)
            near_out[:, part, :] = new[:high].reshape(half, TILE, LANES)
            if with_far:
                far_out[:, lines_of(at - raw, TILE), :] = new[high:].reshape(half, TILE, LANES)
        return carry

    here = lax.axis_index("slab").astype(jnp.int32) % half

    def raw_step(i, carry):
        for t in range(BLOCK // TILE):
            at = i * BLOCK + t * TILE
            part = lines_of(at, TILE)
            states = [near_ref[:, lines_of(lines + TILE + at, TILE), :].reshape(high, LANES)]
            slopes = [raw_grads[:half, part, :].reshape(high, LANES)]
            for x in range(half):
                states += [across_ref[here ^ x, part, :]]
                slopes += [raw_grads[half + (here ^ x), part, :]]
            states, slopes = jnp.concatenate(states, axis=0), jnp.concatenate(slopes, axis=0)
            new = mix(mixer.at[:high, :], own.at[:high, :], numbers_ref, total, states, slopes)
            near_out[:, lines_of(lines + at, TILE), :] = new.reshape(half, TILE, LANES)
        return carry

    raw_fetch.wait()
    lax.fori_loop(0, raw // BLOCK, raw_step, 0)
    store_near(lines, lines + raw, 0)
    for n, (first, last) in enumerate(parts):
        for fetch in fetches[n]:
            fetch.wait()
        lax.fori_loop(first // BLOCK, last // BLOCK, functools.partial(slab_step, n > 0), 0)
        store_near(first, last, 1 + n)
        if n:
            store_far(first, last, n - 1)
    for copy in stores:
        copy.wait()


def update_pieces(numbers, grams, near, far, across, raw_fields, raw_grads, grads, groups, raw, lines):
    half = len(far)
    total = 2 * half
    wide = total * TILE
    out_shape = [pltpu.HBM((half, lines + raw, LANES), BF16)]
    out_shape += [pltpu.HBM((lines - raw, LANES), BF16)] * half
    return call(
        functools.partial(update_pieces_body, half, raw, lines, groups),
        "update_pieces",
        flops=4 * wide * wide * LANES * (lines // TILE),
        moved=6 * total * lines * LANES,
        in_specs=[IN_VMEM] * (half + 6) + [IN_HBM] * (1 + len(groups)),
        out_specs=[IN_HBM] * len(out_shape),
        out_shape=out_shape,
        scratch_shapes=[
            pltpu.VMEM((half, lines + raw, LANES), BF16),
            pltpu.VMEM((half, lines - raw, LANES), BF16),
            pltpu.VMEM((wide, wide), BF16),
            pltpu.VMEM((wide, LANES), F32),
            pltpu.VMEM((total, lines, LANES), BF16),
            pltpu.VMEM((total, raw, LANES), BF16),
            pltpu.SemaphoreType.DMA((len(groups) + 1, 4)),
            pltpu.SemaphoreType.DMA((half + 1, 5)),
        ],
    )(near, *far, across, *raw_fields, numbers, grams, raw_grads, *grads)


def exchange(piece, k, slabs):
    return lax.ppermute(piece, "slab", [(i, i ^ k) for i in range(slabs)])


def swap_near(pieces, slabs):
    groups = [list(range(slabs // 2)), list(range(slabs // 2, slabs))]
    return lax.all_to_all(pieces, "slab", 0, 0, axis_index_groups=groups, tiled=True)


RAW = 128
GRADIENTS = ((8, 9, 10, 11), (12, 13, 14, 15), (0, 1, 2, 3, 4, 5, 6, 7))


def by_halves(particles, observed, precision, spread, anneal, step_size):
    slabs = lax.axis_size("slab")
    half = slabs // 2
    lines = NCELL // slabs // LANES
    row = in_hbm(particles)
    fields = [in_hbm(field.reshape(-1, LANES)) for field in (observed, precision)]
    near, *far = split_pieces(row, slabs, RAW, fields)
    far, (obs, prec, *raw_fields) = far[:half], far[half:]
    near = swap_near(near, slabs)
    far = [exchange(piece, half + x, slabs) for x, piece in enumerate(far)]
    raw_near = raw_states(near, RAW, lines, far)
    across = exchange(raw_near, half, slabs)
    grads = []
    numbers = [spread, anneal, step_size]
    for group in GRADIENTS:
        if group[0] < half:
            arrays, views = [near], [(0, k, 0) for k in group]
        else:
            arrays, views = [far[k - half] for k in group], [(j, None, 0) for j in range(len(group))]
        slopes, rows = gradient_pieces(arrays, tuple(views), obs, prec, [] if grads else numbers)
        grads.append(in_hbm(slopes))
        numbers = numbers if len(grads) > 1 else rows
    grams = swap(gram_pieces(near, far, lines, grads[:1], [raw_near]))
    views = tuple((0, k, lines + TILE) for k in range(half))
    raw_grads = in_hbm(gradient_pieces([near], views, *raw_fields, [])[0])
    new_near, *new_far = update_pieces(
        numbers, grams, near, far, across, raw_fields, raw_grads, grads, GRADIENTS, RAW, lines
    )
    new_near = swap_near(new_near, slabs)
    new_far = [exchange(piece, half + x, slabs) for x, piece in enumerate(new_far)]
    row = join_pieces(None, slabs, RAW, [new_near], [(0, k, k) for k in range(half)])
    for group in ((0, 1, 2, 3), (4, 5)):
        pieces = [(n, None, half + x) for n, x in enumerate(group)]
        row = join_pieces(row, slabs, RAW, [new_far[x] for x in group], pieces)
    return join_pieces(row, slabs, RAW, new_far[6:], [(n, None, half + 6 + n) for n in range(half - 6)])


def on_device(particles, observed, precision, spread, anneal, step_size):
    slabs = lax.axis_size("slab")
    total = particles.shape[0] * slabs
    lines = NCELL // slabs // LANES
    if slabs == 16:
        return by_halves(particles, observed, precision, spread, anneal, step_size)
    sent, begun = cuts(lines)
    fields = [observed.reshape(-1, LANES), precision.reshape(-1, LANES)]
    numbers = [spread, anneal, step_size]
    first, obs, prec, scalars = split_row(particles, slabs, 0, sent, True, fields, numbers, [])
    parts = [swap(first)]
    if sent < lines:
        parts += [swap(split_row(particles, slabs, sent, lines, False, [], [], [scalars])[0])]
    if total * TILE > 256:
        grads = slab_gradient(parts, obs, prec, lines, 0, lines)
        states = jnp.concatenate([parts[0][:, :sent]] + parts[1:], axis=1)
        new = plain_update(spread, anneal, step_size, states, grads)
        return join_row(swap(new), lines, 0, None)
    if sent == lines:
        grads = slab_gradient(parts, obs, prec, lines, 0, lines)
        grams = swap(slab_gram(parts[0], lines, slabs, [], []))
        new = slab_update(scalars, grams, parts, grads, 0, lines, [])
        return join_row(swap(new), lines, 0, None)
    gram = slab_gram(parts[0], sent, 1, [], [])
    early = slab_gradient(parts[:1], obs, prec, lines, 0, begun)
    grams = swap(slab_gram(parts[1], lines - sent, slabs, [gram], [early]))
    late = slab_gradient(parts, obs, prec, lines, begun, lines)
    new = slab_update(scalars, grams, parts[:1], early, 0, begun, [])
    rest = slab_update(scalars, grams, parts, late, begun, lines, [new])
    row = join_row(swap(new), lines, 0, None)
    return join_row(swap(rest), lines, begun, row)


def solution(mesh):
    in_specs = (
        P(("groups", "slab"), None),
        P("groups"),
        P("groups"),
        P("groups"),
        P("groups"),
        P("groups"),
    )
    out_specs = P(("groups", "slab"), None)
    return jax.shard_map(
        on_device, mesh=mesh, in_specs=in_specs, out_specs=out_specs, check_vma=False
    )
```

```python
import functools

import jax
import jax.numpy as jnp
from jax import lax
from jax.experimental import pallas as pl
from jax.experimental.pallas import tpu as pltpu
from jax.sharding import PartitionSpec as P

GRID_X = 1024
GRID_Y = 1024
NCELL = 1048576
LANES = 128
LINE = GRID_Y // LANES
TILE = 16

prior_scale = 0.25
mass_term = 1.0

F32 = jnp.float32
BF16 = jnp.bfloat16
MIB = 1024 * 1024


def call(body, name, flops=0, moved=0, limit=16, **kwargs):
    return pl.pallas_call(
        body,
        name=name,
        compiler_params=pltpu.CompilerParams(vmem_limit_bytes=limit * MIB),
        cost_estimate=pl.CostEstimate(flops=flops, bytes_accessed=moved, transcendentals=0),
        **kwargs,
    )


IN_VMEM = pl.BlockSpec(memory_space=pltpu.VMEM)
IN_HBM = pl.BlockSpec(memory_space=pltpu.HBM)


def in_hbm(array):
    return pltpu.with_memory_space_constraint(array, pltpu.HBM)


BLOCK = 4 * TILE


def cuts(lines):
    if lines % (8 * BLOCK):
        return lines, lines
    return lines * 3 // 4, lines * 3 // 4 - BLOCK


def split_body(lines, begin, rim, fields, numbers, row_ref, *refs):
    field_refs, number_refs = refs[:fields], refs[fields : fields + numbers]
    out_ref, *slab_refs, rows_ref = refs[-7 - fields : -5]
    held, edges, sems, edge_sems, field_sems = refs[-5:]
    for k, number_ref in enumerate(number_refs):
        rows_ref[k : k + 1, :] = jnp.broadcast_to(number_ref[...].reshape(1, 1), (1, LANES))
    slabs, count, _ = out_ref.shape
    count -= TILE * rim
    size = count * LANES
    cells = lines * LANES

    def part(slab):
        source = row_ref.at[:, pl.ds(slab * cells + begin * LANES, size)]
        return pltpu.make_async_copy(source, held.at[:, pl.ds(slab * size, size)], sems.at[slab])

    def edge(slab):
        source = row_ref.at[:, pl.ds(slab * cells - GRID_Y, GRID_Y)]
        return pltpu.make_async_copy(source, edges.at[:, pl.ds(slab * GRID_Y, GRID_Y)], edge_sems.at[slab])

    def grid_row(ref, start):
        return ref[:, pl.ds(start, GRID_Y)].astype(F32).reshape(LINE, LANES)

    for slab in range(slabs):
        part(slab).start()
        if rim and slab:
            edge(slab).start()
    mine = pl.ds(pl.multiple_of(lax.axis_index("slab") * lines, TILE), lines)
    fetches = [
        pltpu.make_async_copy(source.at[mine, :], target, field_sems.at[k])
        for k, (source, target) in enumerate(zip(field_refs, slab_refs))
    ]
    for fetch in fetches:
        fetch.start()
    part(0).wait()
    outside = jnp.zeros((LINE, LANES), F32)
    for slab in range(slabs):
        if slab + 1 < slabs:
            part(slab + 1).wait()
        out_ref[slab, :count, :] = held[:, pl.ds(slab * size, size)].reshape(count, LANES)
        if rim:
            if slab:
                edge(slab).wait()
            below = grid_row(held, (slab + 1) * size) if slab + 1 < slabs else outside
            above = grid_row(edges, slab * GRID_Y) if slab else outside
            out_ref[slab, count:, :] = jnp.concatenate([below, above], axis=0).astype(BF16)
    for fetch in fetches:
        fetch.wait()


def split_row(row, slabs, begin, end, rim, fields, numbers, earlier):
    lines = row.shape[1] // slabs // LANES
    count = end - begin
    return call(
        functools.partial(split_body, lines, begin, rim, len(fields), len(numbers)),
        "split_row",
        moved=6 * slabs * count * LANES,
        in_specs=[IN_HBM] * (1 + len(fields)) + [IN_VMEM] * len(numbers) + [IN_HBM] * len(earlier),
        out_specs=[IN_VMEM] * (2 + len(fields)),
        out_shape=[jax.ShapeDtypeStruct((slabs, count + TILE * rim, LANES), BF16)]
        + [jax.ShapeDtypeStruct((lines, LANES), BF16)] * len(fields)
        + [jax.ShapeDtypeStruct((8, LANES), F32)],
        scratch_shapes=[
            pltpu.VMEM((1, slabs * count * LANES), BF16),
            pltpu.VMEM((1, slabs * GRID_Y), BF16),
            pltpu.SemaphoreType.DMA((slabs,)),
            pltpu.SemaphoreType.DMA((slabs,)),
            pltpu.SemaphoreType.DMA((2,)),
        ],
    )(row, *fields, *numbers, *earlier)


def join_body(lines, begin, slabs_ref, *refs):
    row_ref, held, sems = refs[-3:]
    slabs, count, _ = slabs_ref.shape
    size = count * LANES
    copies = []
    for slab in range(slabs):
        at = pl.ds(slab * size, size)
        held[:, at] = slabs_ref[slab].reshape(1, size)
        target = row_ref.at[:, pl.ds((slab * lines + begin) * LANES, size)]
        copies.append(pltpu.make_async_copy(held.at[:, at], target, sems.at[slab]))
        copies[-1].start()
    for copy in copies:
        copy.wait()


def join_row(slabs, lines, begin, row):
    total, count, _ = slabs.shape
    begun = [] if row is None else [row]
    return call(
        functools.partial(join_body, lines, begin),
        "join_row",
        moved=6 * slabs.size,
        in_specs=[IN_VMEM] + [IN_HBM] * len(begun),
        out_specs=IN_HBM,
        out_shape=jax.ShapeDtypeStruct((1, total * lines * LANES), BF16),
        input_output_aliases={1: 0} if begun else {},
        scratch_shapes=[pltpu.VMEM((1, slabs.size), BF16), pltpu.SemaphoreType.DMA((total,))],
    )(slabs, *begun)


def same_line(total):
    wide = total * TILE
    row = lax.broadcasted_iota(jnp.int32, (wide, wide), 0)
    col = lax.broadcasted_iota(jnp.int32, (wide, wide), 1)
    return (row ^ col) & (TILE - 1) == 0


def members(total, dtype):
    wide = total * TILE
    row = lax.broadcasted_iota(jnp.int32, (wide, total), 0)
    col = lax.broadcasted_iota(jnp.int32, (wide, total), 1)
    return (row // TILE == col).astype(dtype)


def gram_body(steps, tiles, parts, states_ref, *refs):
    out_ref, pairs = refs[-2:]
    total = states_ref.shape[0]
    wide = total * TILE
    pairs[...] = jnp.zeros_like(pairs)

    def step(i, carry):
        parts = [
            states_ref[:, pl.ds(pl.multiple_of((i * tiles + t) * TILE, TILE), TILE), :].reshape(wide, LANES)
            for t in range(tiles)
        ]
        block = jnp.concatenate(parts, axis=1)
        pairs[...] += lax.dot_general(block, block, (((1,), (1,)), ((), ())), preferred_element_type=F32)
        return carry

    lax.fori_loop(0, steps, step, 0)
    equal = jnp.where(same_line(total), pairs[...], 0.0)
    rows = jnp.sum(equal.reshape(total, TILE, wide), axis=1)
    gram = jnp.dot(rows, members(total, F32), precision=lax.Precision.HIGHEST, preferred_element_type=F32)
    gram = jnp.concatenate([gram, jnp.zeros((total, LANES - total), F32)], axis=1)
    for part_ref in refs[:parts]:
        gram += part_ref[0]
    out_ref[...] = jnp.broadcast_to(gram[None], out_ref.shape)


def slab_gram(states, lines, copies, parts, earlier):
    total = states.shape[0]
    wide = total * TILE
    tiles = min(8, lines // TILE)
    return call(
        functools.partial(gram_body, lines // TILE // tiles, tiles, len(parts)),
        "slab_gram",
        flops=2 * wide * wide * LANES * (lines // TILE),
        moved=2 * states.size,
        in_specs=[IN_VMEM] * (1 + len(parts)) + [IN_HBM] * len(earlier),
        out_specs=IN_VMEM,
        out_shape=jax.ShapeDtypeStruct((copies, total, LANES), F32),
        scratch_shapes=[pltpu.VMEM((wide, wide), F32)],
    )(states, *parts, *earlier)


def gradient_body(lines, begin, end, parts, *refs):
    observed, precision, out_ref, grads, sems = refs[parts:]
    total = grads.shape[0]
    first = refs[0].shape[1] - TILE
    rows = BLOCK // LINE
    group = 4
    shape = (rows, LINE, LANES)
    lane = lax.broadcasted_iota(jnp.int32, (1, LINE, LANES), 2)
    line = lax.broadcasted_iota(jnp.int32, (1, LINE, LANES), 1)

    def load(particle, at, count):
        ref, at = (refs[0], at) if at < first else (refs[1], at - first)
        return ref[particle, at : at + count, :].astype(F32)

    def rim(particle):
        return refs[0][particle, first:, :].astype(F32)

    stores = []
    for k, at in enumerate(range(begin, end, BLOCK)):
        mine = slice(at - begin, at - begin + BLOCK)
        obs = observed[at : at + BLOCK, :].astype(F32).reshape(shape)
        prec = precision[at : at + BLOCK, :].astype(F32).reshape(shape)

        def step(i, carry):
            for p in range(group):
                particle = i * group + p
                here = load(particle, at, BLOCK)
                before = load(particle, at - TILE, TILE) if at else rim(particle)
                after = load(particle, at + BLOCK, TILE) if at + BLOCK < lines else rim(particle)
                above = jnp.concatenate([before[LINE:], here[:-LINE]], axis=0).reshape(shape)
                below = jnp.concatenate([here[LINE:], after[:LINE]], axis=0).reshape(shape)
                field = here.reshape(shape)
                turned = pltpu.roll(field, 1, 2)
                carried = jnp.where(line == 0, 0.0, pltpu.roll(turned, 1, 1))
                left = jnp.where(lane == 0, carried, turned)
                turned = pltpu.roll(field, LANES - 1, 2)
                carried = jnp.where(line == LINE - 1, 0.0, pltpu.roll(turned, LINE - 1, 1))
                right = jnp.where(lane == LANES - 1, carried, turned)
                laplace = (4.0 + mass_term) * field - (below + above + right + left)
                squash = jnp.tanh(field)
                result = prec * (obs - squash) * (1.0 - squash * squash) - prior_scale * laplace
                grads[particle, mine, :] = result.reshape(BLOCK, LANES).astype(BF16)
            return carry

        lax.fori_loop(0, total // group, step, 0)
        stores.append(pltpu.make_async_copy(grads.at[:, mine, :], out_ref.at[:, mine, :], sems.at[k]))
        stores[-1].start()
    for store in stores:
        store.wait()


def slab_gradient(parts, observed, precision, lines, begin, end):
    total = parts[0].shape[0]
    count = end - begin
    out = jax.ShapeDtypeStruct((total, count, LANES), BF16)
    return call(
        functools.partial(gradient_body, lines, begin, end, len(parts)),
        "slab_gradient",
        flops=30 * out.size,
        moved=8 * out.size,
        in_specs=[IN_VMEM] * (len(parts) + 2),
        out_specs=IN_HBM,
        out_shape=out,
        scratch_shapes=[pltpu.VMEM(out.shape, BF16), pltpu.SemaphoreType.DMA((count // BLOCK,))],
    )(*parts, observed, precision)


def update_body(begin, end, parts, *refs):
    states_refs, refs = refs[:parts], refs[parts:]
    scalars_ref, grams_ref, grads_ref = refs[:3]
    out_ref, grads, mixer, own, sem = refs[-5:]
    total = out_ref.shape[0]
    wide = total * TILE
    fetch = pltpu.make_async_copy(grads_ref, grads, sem)
    fetch.start()
    gram = jnp.sum(grams_ref[...], axis=0)[:, :total]
    row = lax.broadcasted_iota(jnp.int32, (total, total), 0)
    col = lax.broadcasted_iota(jnp.int32, (total, total), 1)
    diagonal = jnp.where(row == col, gram, 0.0)
    down = jnp.sum(diagonal, axis=1, keepdims=True)
    across = jnp.sum(diagonal, axis=0, keepdims=True)
    member = members(total, BF16)
    spread, anneal, step_size = (scalars_ref[k : k + 1, :1] for k in range(3))
    rate = step_size / total
    coeff = 2.0 * anneal / spread
    kernel = jnp.exp(-(down + across - 2.0 * gram) / (spread * NCELL)).astype(BF16)
    ksum = jnp.sum(kernel.astype(F32), axis=1, keepdims=True)
    half = jnp.dot(member, kernel, preferred_element_type=F32).astype(BF16)
    full = lax.dot_general(half, member, (((1,), (1,)), ((), ())), preferred_element_type=F32)
    mixer[...] = jnp.where(same_line(total), full, 0.0).astype(BF16)
    gain = 1.0 + rate * coeff * ksum
    own[...] = jnp.broadcast_to(gain[:, :, None], (total, TILE, LANES)).reshape(wide, LANES)
    fetch.wait()

    done = 0
    for part, states_ref in enumerate(states_refs):
        have = states_ref.shape[1] - (0 if part else TILE)
        low = max(begin - done, 0)
        high = min(end - done, have)
        into = done - begin
        done += have

        def step(i, carry):
            for t in range(BLOCK // TILE):
                at = pl.multiple_of(i * BLOCK + t * TILE, TILE)
                there = pl.ds(pl.multiple_of(at + into, TILE), TILE)
                states = states_ref[:, pl.ds(at, TILE), :].reshape(wide, LANES)
                both = jnp.concatenate([grads[:, there, :].reshape(wide, LANES), states], axis=1)
                mixed = jnp.dot(mixer[...], both, preferred_element_type=F32)
                drive, pulled = mixed[:, :LANES], mixed[:, LANES:]
                new = states.astype(F32) * own[...] + rate * (drive - coeff * pulled)
                out_ref[:, there, :] = new.astype(BF16).reshape(total, TILE, LANES)
            return carry

        lax.fori_loop(low // BLOCK, high // BLOCK, step, 0)


def slab_update(scalars, grams, parts, grads, begin, end, earlier):
    total, count, _ = grads.shape
    wide = total * TILE
    return call(
        functools.partial(update_body, begin, end, len(parts)),
        "slab_update",
        flops=4 * wide * wide * LANES * (count // TILE),
        moved=6 * grads.size,
        in_specs=[IN_VMEM] * len(parts)
        + [IN_VMEM, IN_VMEM, IN_HBM]
        + [IN_HBM] * len(earlier),
        out_specs=IN_VMEM,
        out_shape=jax.ShapeDtypeStruct(grads.shape, BF16),
        scratch_shapes=[
            pltpu.VMEM(grads.shape, BF16),
            pltpu.VMEM((wide, wide), BF16),
            pltpu.VMEM((wide, LANES), F32),
            pltpu.SemaphoreType.DMA,
        ],
    )(*parts, scalars, grams, grads, *earlier)


def plain_update(spread, anneal, step_size, states, grads):
    total, lines, _ = grads.shape
    flat = states[:, :lines].reshape(total, -1)
    gram = lax.dot_general(flat, flat, (((1,), (1,)), ((), ())), preferred_element_type=F32)
    gram = lax.psum(gram, "slab")
    norms = jnp.diagonal(gram)
    kernel = jnp.exp(-(norms[:, None] + norms[None, :] - 2.0 * gram) / (spread[0] * NCELL)).astype(BF16)
    ksum = jnp.sum(kernel.astype(F32), axis=1)
    drive = jnp.dot(kernel, grads.reshape(total, -1), preferred_element_type=F32)
    pulled = jnp.dot(kernel, flat, preferred_element_type=F32)
    values = flat.astype(F32)
    repel = values * ksum[:, None] - pulled
    coeff = 2.0 * anneal[0] / spread[0]
    new = values + step_size[0] / total * (drive + coeff * repel)
    return new.astype(BF16).reshape(grads.shape)


def swap(slabs):
    return lax.all_to_all(slabs, "slab", split_axis=0, concat_axis=0, tiled=True)


def device_at(at, half):
    me = lax.axis_index("slab").astype(jnp.int32)
    return jnp.where(at < half, me - me % half + at, me ^ at)


def lines_of(start, count):
    return pl.ds(pl.multiple_of(start, TILE), count)


def split_pieces_body(slabs, raw, lines, fields, row_ref, *refs):
    half = slabs // 2
    field_refs, near_out, far_outs = refs[:fields], refs[fields], refs[fields + 1 : fields + 1 + half]
    slab_refs, held, sems = refs[fields + 1 + half : -2], refs[-2], refs[-1]
    cells = lines * LANES
    end = row_ref.shape[1]
    me = lax.axis_index("slab").astype(jnp.int32)

    def part(start, size):
        return pl.ds(pl.multiple_of(start, GRID_Y), size)

    def grid_row(start):
        return held[:, part(start, GRID_Y)].astype(F32).reshape(LINE, LANES)

    copies = []
    for at in range(slabs):
        cut = part(device_at(at, half) * cells, cells)
        copies.append(pltpu.make_async_copy(row_ref.at[:, cut], held.at[:, cut], sems.at[at]))
    for n, target in enumerate(slab_refs):
        start = (me if n < fields else me ^ half) * lines
        source = field_refs[n % fields].at[lines_of(start, target.shape[0]), :]
        copies.append(pltpu.make_async_copy(source, target, sems.at[slabs + n]))
    for copy in copies:
        copy.start()
    outs = [near_out.at[at] for at in range(half)] + list(far_outs)
    for at, out_ref in enumerate(outs):
        copies[at].wait()
        out_ref[:lines, :] = held[:, part(device_at(at, half) * cells, cells)].reshape(lines, LANES)
    for at, out_ref in enumerate(outs):
        slab = device_at(at, half)
        start = slab * cells
        below = jnp.where(slab == slabs - 1, 0.0, grid_row(jnp.minimum(start + cells, end - GRID_Y)))
        above = jnp.where(slab == 0, 0.0, grid_row(jnp.maximum(start - GRID_Y, 0)))
        out_ref[lines : lines + TILE, :] = jnp.concatenate([below, above], axis=0).astype(BF16)
        if at < half:
            start = (slab ^ half) * cells
            to = lines + TILE
            out_ref[to : to + raw, :] = held[:, part(start, raw * LANES)].reshape(raw, LANES)
            below = grid_row(start + raw * LANES)
            above = jnp.where(slab ^ half == 0, 0.0, grid_row(jnp.maximum(start - GRID_Y, 0)))
            out_ref[to + raw :, :] = jnp.concatenate([below, above], axis=0).astype(BF16)
    for copy in copies[slabs:]:
        copy.wait()


def split_pieces(row, slabs, raw, fields):
    lines = row.shape[1] // slabs // LANES
    half = slabs // 2
    rim = lines + TILE
    size = rim + raw + TILE
    out_shape = [jax.ShapeDtypeStruct((half, size, LANES), BF16)]
    out_shape += [jax.ShapeDtypeStruct((rim, LANES), BF16)] * half
    out_shape += [jax.ShapeDtypeStruct((lines, LANES), BF16)] * len(fields)
    out_shape += [jax.ShapeDtypeStruct((raw, LANES), BF16)] * len(fields)
    return call(
        functools.partial(split_pieces_body, slabs, raw, lines, len(fields)),
        "split_pieces",
        moved=6 * half * (rim + size) * LANES,
        in_specs=[IN_HBM] * (1 + len(fields)),
        out_specs=[IN_VMEM] * len(out_shape),
        out_shape=out_shape,
        scratch_shapes=[pltpu.VMEM(row.shape, BF16), pltpu.SemaphoreType.DMA((slabs + 2 * len(fields),))],
    )(row, *fields)


def join_pieces_body(pieces, half, raw, lines, begun, arrays, *refs):
    row_ref, helds, sems = refs[begun + arrays], refs[begun + arrays + 1 : -1], refs[-1]
    cells = lines * LANES
    skip = raw * LANES
    copies = []
    for (array, lead, at), held in zip(pieces, helds):
        ref = refs[begun + array]
        piece = ref[...] if lead is None else ref[lead]
        held[...] = piece.reshape(held.shape)
        slab = device_at(at, half)
        if at < half:
            parts = [(0, cells, slab * cells), (cells, skip, (slab ^ half) * cells)]
        else:
            parts = [(0, cells - skip, slab * cells + skip)]
        for begin, size, start in parts:
            target = row_ref.at[:, pl.ds(pl.multiple_of(start, GRID_Y), size)]
            copies.append(pltpu.make_async_copy(held.at[:, pl.ds(begin, size)], target, sems.at[len(copies)]))
            copies[-1].start()
    for copy in copies:
        copy.wait()


def join_pieces(row, slabs, raw, arrays, pieces):
    sizes = [arrays[piece[0]].shape[-2] * LANES for piece in pieces]
    begun = [] if row is None else [row]
    return call(
        functools.partial(
            join_pieces_body, pieces, slabs // 2, raw, NCELL // slabs // LANES, len(begun), len(arrays)
        ),
        "join_pieces",
        moved=6 * sum(sizes),
        in_specs=[IN_HBM] * len(begun) + [IN_VMEM] * len(arrays),
        out_specs=IN_HBM,
        out_shape=jax.ShapeDtypeStruct((1, NCELL), BF16),
        input_output_aliases={0: 0} if begun else {},
        scratch_shapes=[pltpu.VMEM((1, size), BF16) for size in sizes]
        + [pltpu.SemaphoreType.DMA((2 * len(sizes),))],
    )(*begun, *arrays)


def owners(total, dtype):
    wide = total * TILE
    row = lax.broadcasted_iota(jnp.int32, (wide, total), 0)
    col = lax.broadcasted_iota(jnp.int32, (wide, total), 1)
    return (device_at(row // TILE, total // 2) == col).astype(dtype)


def gram_pieces_body(lines, total, near_ref, *refs):
    half = total // 2
    pieces, out_ref, pairs = refs[:half], refs[-2], refs[-1]
    wide = total * TILE
    tiles = 8
    pairs[...] = jnp.zeros_like(pairs)

    def step(i, carry):
        parts = []
        for t in range(tiles):
            at = lines_of((i * tiles + t) * TILE, TILE)
            near = near_ref[:, at, :].reshape(wide // 2, LANES)
            parts.append(jnp.concatenate([near] + [piece[at, :] for piece in pieces], axis=0))
        block = jnp.concatenate(parts, axis=1)
        pairs[...] += lax.dot_general(block, block, (((1,), (1,)), ((), ())), preferred_element_type=F32)
        return carry

    lax.fori_loop(0, lines // TILE // tiles, step, 0)
    equal = jnp.where(same_line(total), pairs[...], 0.0)
    exact = {"precision": lax.Precision.HIGHEST, "preferred_element_type": F32}
    rows = jnp.sum(equal.reshape(total, TILE, wide), axis=1)
    gram = jnp.dot(rows, owners(total, F32), **exact)
    row = lax.broadcasted_iota(jnp.int32, (total, total), 0)
    col = lax.broadcasted_iota(jnp.int32, (total, total), 1)
    gram = jnp.dot((row == device_at(col, half)).astype(F32), gram, **exact)
    filler = jnp.zeros((half, LANES - 2 * total), F32)
    gram = jnp.concatenate([gram[:half], gram[half:], filler], axis=1)
    out_ref[...] = jnp.broadcast_to(gram[None], out_ref.shape)


def gram_pieces(near, far, lines, gates, early):
    total = 2 * len(far)
    wide = total * TILE
    return call(
        functools.partial(gram_pieces_body, lines, total),
        "gram_pieces",
        flops=2 * wide * wide * LANES * (lines // TILE),
        moved=2 * total * lines * LANES,
        in_specs=[IN_VMEM] * (1 + len(far)) + [IN_HBM] * len(gates) + [IN_VMEM] * len(early),
        out_specs=IN_VMEM,
        out_shape=jax.ShapeDtypeStruct((total, total // 2, LANES), F32),
        scratch_shapes=[pltpu.VMEM((wide, wide), F32)],
    )(near, *far, *gates, *early)


def block_gradient(load, i, count, observed, precision):
    start = i * BLOCK
    at = lines_of(start, BLOCK)
    shape = (BLOCK // LINE, LINE, LANES)
    lane = lax.broadcasted_iota(jnp.int32, (1, LINE, LANES), 2)
    line = lax.broadcasted_iota(jnp.int32, (1, LINE, LANES), 1)
    obs = observed[at, :].astype(F32).reshape(shape)
    prec = precision[at, :].astype(F32).reshape(shape)
    here = load(start, BLOCK).astype(F32)
    before = load(jnp.where(i == 0, count, start - TILE), TILE).astype(F32)
    after = load(start + BLOCK, TILE).astype(F32)
    above = jnp.concatenate([before[LINE:], here[:-LINE]], axis=0).reshape(shape)
    below = jnp.concatenate([here[LINE:], after[:LINE]], axis=0).reshape(shape)
    field = here.reshape(shape)
    turned = pltpu.roll(field, 1, 2)
    carried = jnp.where(line == 0, 0.0, pltpu.roll(turned, 1, 1))
    left = jnp.where(lane == 0, carried, turned)
    turned = pltpu.roll(field, LANES - 1, 2)
    carried = jnp.where(line == LINE - 1, 0.0, pltpu.roll(turned, LINE - 1, 1))
    right = jnp.where(lane == LANES - 1, carried, turned)
    laplace = (4.0 + mass_term) * field - (below + above + right + left)
    squash = jnp.tanh(field)
    result = prec * (obs - squash) * (1.0 - squash * squash) - prior_scale * laplace
    return result.reshape(BLOCK, LANES).astype(BF16)


def gradient_pieces_body(views, arrays, numbers, *refs):
    observed, precision, *number_refs = refs[arrays : arrays + 2 + numbers]
    out_ref, rows_ref, grads, sems = refs[-4:]
    for n, number_ref in enumerate(number_refs):
        rows_ref[n : n + 1, :] = jnp.full((1, LANES), number_ref[0], F32)
    count = observed.shape[0]
    steps = count // BLOCK

    def store(i):
        at = lines_of(i * BLOCK, BLOCK)
        return pltpu.make_async_copy(grads.at[:, at, :], out_ref.at[:, at, :], sems.at[i])

    def step(i, carry):
        for p, (array, lead, base) in enumerate(views):

            def load(start, size):
                part = lines_of(base + start, size)
                return refs[array][part, :] if lead is None else refs[array][lead, part, :]

            grads[p, lines_of(i * BLOCK, BLOCK), :] = block_gradient(load, i, count, observed, precision)
        store(i).start()
        return carry

    def finish(i, carry):
        store(i).wait()
        return carry

    lax.fori_loop(0, steps, step, 0)
    lax.fori_loop(0, steps, finish, 0)


def gradient_pieces(arrays, views, observed, precision, numbers):
    count = observed.shape[0]
    out = pltpu.HBM((len(views), count, LANES), BF16)
    size = len(views) * count * LANES
    return call(
        functools.partial(gradient_pieces_body, views, len(arrays), len(numbers)),
        "gradient_pieces",
        flops=30 * size,
        moved=8 * size,
        in_specs=[IN_VMEM] * (len(arrays) + 2)
        + [pl.BlockSpec(memory_space=pltpu.SMEM)] * len(numbers),
        out_specs=[IN_HBM, IN_VMEM],
        out_shape=[out, jax.ShapeDtypeStruct((8, LANES), F32)],
        scratch_shapes=[pltpu.VMEM(out.shape, BF16), pltpu.SemaphoreType.DMA((count // BLOCK,))],
    )(*arrays, observed, precision, *numbers)


def raw_body(raw, lines, near_ref, *refs):
    out_ref = refs[-1]
    for k in range(near_ref.shape[0]):
        out_ref[k, :raw, :] = near_ref[k, :raw, :]
        below = near_ref[k, raw : raw + TILE, :].astype(F32)[:LINE]
        above = near_ref[k, lines : lines + TILE, :].astype(F32)[LINE:]
        out_ref[k, raw:, :] = jnp.concatenate([below, above], axis=0).astype(BF16)


def raw_states(near, raw, lines, gates):
    out = jax.ShapeDtypeStruct((near.shape[0], raw + TILE, LANES), BF16)
    return call(
        functools.partial(raw_body, raw, lines),
        "raw_states",
        moved=4 * out.size,
        in_specs=[IN_VMEM] * (1 + len(gates)),
        out_specs=IN_VMEM,
        out_shape=out,
    )(near, *gates)


def mix(mixer, own, numbers_ref, total, states, slopes):
    high = mixer.shape[0]
    rate = numbers_ref[2:3, :1] / total
    coeff = 2.0 * numbers_ref[1:2, :1] / numbers_ref[:1, :1]
    both = jnp.concatenate([slopes, states], axis=1)
    mixed = jnp.dot(mixer[...], both, preferred_element_type=F32)
    drive, pulled = mixed[:, :LANES], mixed[:, LANES:]
    return (states[:high].astype(F32) * own[...] + rate * (drive - coeff * pulled)).astype(BF16)


def update_pieces_body(half, raw, lines, groups, near_ref, *refs):
    total = 2 * half
    far_refs, refs = refs[:half], refs[half:]
    across_ref, raw_observed, raw_precision, numbers_ref, grams_ref, raw_grads_ref, *refs = refs
    group_refs, near_to, far_tos = refs[: len(groups)], refs[len(groups)], refs[len(groups) + 1 : -8]
    near_out, far_out, mixer, own, grads, raw_grads, sems, out_sems = refs[-8:]
    wide = total * TILE
    high = half * TILE
    raw_fetch = pltpu.make_async_copy(raw_grads_ref, raw_grads.at[pl.ds(0, half), :, :], sems.at[len(groups), 0])
    raw_fetch.start()
    middle = (raw + 2 * lines) // 3 // BLOCK * BLOCK
    parts = ((0, raw), (raw, middle), (middle, lines - BLOCK), (lines - BLOCK, lines))
    fetches = []
    for n, (first, last) in enumerate(parts):
        part = pl.ds(first, last - first)
        fetches.append([])
        for g, (group, group_ref) in enumerate(zip(groups, group_refs)):
            target = grads.at[pl.ds(group[0], len(group)), part, :]
            fetches[n].append(pltpu.make_async_copy(group_ref.at[:, part, :], target, sems.at[g, n]))
            fetches[n][-1].start()

    def raw_gradient(i, carry):
        for k in range(half):

            def load(start, size):
                return across_ref[k, lines_of(start, size), :]

            part = lines_of(i * BLOCK, BLOCK)
            raw_grads[half + k, part, :] = block_gradient(load, i, raw, raw_observed, raw_precision)
        return carry

    lax.fori_loop(0, raw // BLOCK, raw_gradient, 0)
    gram = jnp.sum(grams_ref[...], axis=0)
    gram = jnp.concatenate([gram[:, :total], gram[:, total : 2 * total]], axis=0)
    spread, anneal, step_size = (numbers_ref[k : k + 1, :1] for k in range(3))
    rate = step_size / total
    coeff = 2.0 * anneal / spread
    row = lax.broadcasted_iota(jnp.int32, (total, total), 0)
    col = lax.broadcasted_iota(jnp.int32, (total, total), 1)
    diagonal = jnp.where(row == col, gram, 0.0)
    down = jnp.sum(diagonal, axis=1, keepdims=True)
    across = jnp.sum(diagonal, axis=0, keepdims=True)
    kernel = jnp.exp(-(down + across - 2.0 * gram) / (spread * NCELL)).astype(BF16)
    owner = owners(total, BF16)
    half_way = jnp.dot(owner, kernel, preferred_element_type=F32).astype(BF16)
    full = lax.dot_general(half_way, owner, (((1,), (1,)), ((), ())), preferred_element_type=F32)
    full = jnp.where(same_line(total), full, 0.0)
    mixer[...] = full.astype(BF16)
    ksum = jnp.sum(full, axis=1, keepdims=True)
    own[...] = jnp.broadcast_to(1.0 + rate * coeff * ksum, (wide, LANES))

    stores = []

    def store(source, target, at):
        stores.append(pltpu.make_async_copy(source, target, out_sems.at[at]))
        stores[-1].start()

    def store_near(first, last, at):
        part = pl.ds(first, last - first)
        store(near_out.at[:, part, :], near_to.at[:, part, :], (half, at))

    def store_far(first, last, at):
        part = pl.ds(first - raw, last - first)
        for x, far_to in enumerate(far_tos):
            store(far_out.at[x, part, :], far_to.at[part, :], (x, at))

    def slab_step(with_far, i, carry):
        rows = wide if with_far else high
        for t in range(BLOCK // TILE):
            at = i * BLOCK + t * TILE
            part = lines_of(at, TILE)
            states = [near_ref[:, part, :].reshape(high, LANES)] + [ref[part, :] for ref in far_refs]
            slopes = grads[:, part, :].reshape(wide, LANES)
            states = jnp.concatenate(states, axis=0)
            new = mix(mixer.at[:rows, :], own.at[:rows, :], numbers_ref, total, states, slopes)
            near_out[:, part, :] = new[:high].reshape(half, TILE, LANES)
            if with_far:
                far_out[:, lines_of(at - raw, TILE), :] = new[high:].reshape(half, TILE, LANES)
        return carry

    here = lax.axis_index("slab").astype(jnp.int32) % half

    def raw_step(i, carry):
        for t in range(BLOCK // TILE):
            at = i * BLOCK + t * TILE
            part = lines_of(at, TILE)
            states = [near_ref[:, lines_of(lines + TILE + at, TILE), :].reshape(high, LANES)]
            slopes = [raw_grads[:half, part, :].reshape(high, LANES)]
            for x in range(half):
                states += [across_ref[here ^ x, part, :]]
                slopes += [raw_grads[half + (here ^ x), part, :]]
            states, slopes = jnp.concatenate(states, axis=0), jnp.concatenate(slopes, axis=0)
            new = mix(mixer.at[:high, :], own.at[:high, :], numbers_ref, total, states, slopes)
            near_out[:, lines_of(lines + at, TILE), :] = new.reshape(half, TILE, LANES)
        return carry

    raw_fetch.wait()
    lax.fori_loop(0, raw // BLOCK, raw_step, 0)
    store_near(lines, lines + raw, 0)
    for n, (first, last) in enumerate(parts):
        for fetch in fetches[n]:
            fetch.wait()
        lax.fori_loop(first // BLOCK, last // BLOCK, functools.partial(slab_step, n > 0), 0)
        store_near(first, last, 1 + n)
        if n:
            store_far(first, last, n - 1)
    for copy in stores:
        copy.wait()


def update_pieces(numbers, grams, near, far, across, raw_fields, raw_grads, grads, groups, raw, lines):
    half = len(far)
    total = 2 * half
    wide = total * TILE
    out_shape = [pltpu.HBM((half, lines + raw, LANES), BF16)]
    out_shape += [pltpu.HBM((lines - raw, LANES), BF16)] * half
    return call(
        functools.partial(update_pieces_body, half, raw, lines, groups),
        "update_pieces",
        flops=4 * wide * wide * LANES * (lines // TILE),
        moved=6 * total * lines * LANES,
        in_specs=[IN_VMEM] * (half + 6) + [IN_HBM] * (1 + len(groups)),
        out_specs=[IN_HBM] * len(out_shape),
        out_shape=out_shape,
        scratch_shapes=[
            pltpu.VMEM((half, lines + raw, LANES), BF16),
            pltpu.VMEM((half, lines - raw, LANES), BF16),
            pltpu.VMEM((wide, wide), BF16),
            pltpu.VMEM((wide, LANES), F32),
            pltpu.VMEM((total, lines, LANES), BF16),
            pltpu.VMEM((total, raw, LANES), BF16),
            pltpu.SemaphoreType.DMA((len(groups) + 1, 4)),
            pltpu.SemaphoreType.DMA((half + 1, 5)),
        ],
    )(near, *far, across, *raw_fields, numbers, grams, raw_grads, *grads)


def exchange(piece, k, slabs):
    return lax.ppermute(piece, "slab", [(i, i ^ k) for i in range(slabs)])


def swap_near(pieces, slabs):
    groups = [list(range(slabs // 2)), list(range(slabs // 2, slabs))]
    return lax.all_to_all(pieces, "slab", 0, 0, axis_index_groups=groups, tiled=True)


RAW = 128
GRADIENTS = ((8, 9, 10, 11), (12, 13, 14, 15), (0, 1, 2, 3, 4, 5, 6, 7))


def by_halves(particles, observed, precision, spread, anneal, step_size):
    slabs = lax.axis_size("slab")
    half = slabs // 2
    lines = NCELL // slabs // LANES
    row = in_hbm(particles)
    fields = [in_hbm(field.reshape(-1, LANES)) for field in (observed, precision)]
    near, *far = split_pieces(row, slabs, RAW, fields)
    far, (obs, prec, *raw_fields) = far[:half], far[half:]
    near = swap_near(near, slabs)
    far = [exchange(piece, half + x, slabs) for x, piece in enumerate(far)]
    grads = []
    numbers = [spread, anneal, step_size]
    for group in GRADIENTS:
        if group[0] < half:
            arrays, views = [near], [(0, k, 0) for k in group]
        else:
            arrays, views = [far[k - half] for k in group], [(j, None, 0) for j in range(len(group))]
        slopes, rows = gradient_pieces(arrays, tuple(views), obs, prec, [] if grads else numbers)
        grads.append(in_hbm(slopes))
        numbers = numbers if len(grads) > 1 else rows
    raw_near = raw_states(near, RAW, lines, [*far, numbers])
    across = exchange(raw_near, half, slabs)
    grams = swap(gram_pieces(near, far, lines, grads[:1], [raw_near]))
    views = tuple((0, k, lines + TILE) for k in range(half))
    raw_grads = in_hbm(gradient_pieces([near], views, *raw_fields, [])[0])
    new_near, *new_far = update_pieces(
        numbers, grams, near, far, across, raw_fields, raw_grads, grads, GRADIENTS, RAW, lines
    )
    new_near = swap_near(new_near, slabs)
    new_far = [exchange(piece, half + x, slabs) for x, piece in enumerate(new_far)]
    row = join_pieces(None, slabs, RAW, [new_near], [(0, k, k) for k in range(half)])
    for group in ((0, 1, 2, 3), (4, 5)):
        pieces = [(n, None, half + x) for n, x in enumerate(group)]
        row = join_pieces(row, slabs, RAW, [new_far[x] for x in group], pieces)
    return join_pieces(row, slabs, RAW, new_far[6:], [(n, None, half + 6 + n) for n in range(half - 6)])


def on_device(particles, observed, precision, spread, anneal, step_size):
    slabs = lax.axis_size("slab")
    total = particles.shape[0] * slabs
    lines = NCELL // slabs // LANES
    if slabs == 16:
        return by_halves(particles, observed, precision, spread, anneal, step_size)
    sent, begun = cuts(lines)
    fields = [observed.reshape(-1, LANES), precision.reshape(-1, LANES)]
    numbers = [spread, anneal, step_size]
    first, obs, prec, scalars = split_row(particles, slabs, 0, sent, True, fields, numbers, [])
    parts = [swap(first)]
    if sent < lines:
        parts += [swap(split_row(particles, slabs, sent, lines, False, [], [], [scalars])[0])]
    if total * TILE > 256:
        grads = slab_gradient(parts, obs, prec, lines, 0, lines)
        states = jnp.concatenate([parts[0][:, :sent]] + parts[1:], axis=1)
        new = plain_update(spread, anneal, step_size, states, grads)
        return join_row(swap(new), lines, 0, None)
    if sent == lines:
        grads = slab_gradient(parts, obs, prec, lines, 0, lines)
        grams = swap(slab_gram(parts[0], lines, slabs, [], []))
        new = slab_update(scalars, grams, parts, grads, 0, lines, [])
        return join_row(swap(new), lines, 0, None)
    gram = slab_gram(parts[0], sent, 1, [], [])
    early = slab_gradient(parts[:1], obs, prec, lines, 0, begun)
    grams = swap(slab_gram(parts[1], lines - sent, slabs, [gram], [early]))
    late = slab_gradient(parts, obs, prec, lines, begun, lines)
    new = slab_update(scalars, grams, parts[:1], early, 0, begun, [])
    rest = slab_update(scalars, grams, parts, late, begun, lines, [new])
    row = join_row(swap(new), lines, 0, None)
    return join_row(swap(rest), lines, begun, row)


def solution(mesh):
    in_specs = (
        P(("groups", "slab"), None),
        P("groups"),
        P("groups"),
        P("groups"),
        P("groups"),
        P("groups"),
    )
    out_specs = P(("groups", "slab"), None)
    return jax.shard_map(
        on_device, mesh=mesh, in_specs=in_specs, out_specs=out_specs, check_vma=False
    )
```
